32 devices in a mesh: batch: 2 (over x), blk: 4 (over z), uly: 4 (over y, core).
Axes of the slice: x: 2, y: 2, z: 4, core: 2. Of those that a mesh axis runs over, the one named last changes fastest.
Arguments:
- tokens: bfloat16 [2, 2048, 2048], P('batch', ('blk', 'uly')), may hold values from -6 to 6
- segments: int32 [2, 2048], P('batch'), may hold values from 0 to 18, as said below
- routes: int32 [2, 2048, 8], P('batch', ('blk', 'uly')), may hold values from 0 to 15, all different within a row; in each aligned block of 128 rows (0 to 127, 128 to 255, ..., all dimensions but the last counted through in order) at most 96 rows name the same one
- w_qkv: bfloat16 [2048, 6144], P(('batch', 'blk', 'uly')), may hold values from -0.125 to 0.125
- w_out: bfloat16 [2048, 2048], P(('batch', 'blk', 'uly')), may hold values from -4 to 4
- attn_gain: bfloat16 [2048], P(('batch', 'blk', 'uly')), may hold values from 0.5 to 1.5
- ffn_gain: bfloat16 [2048], P(('batch', 'blk', 'uly')), may hold values from 0.5 to 1.5
- qk_gain: bfloat16 [2, 128], replicated, may hold values from 1 to 2
- router: bfloat16 [2048, 16], P(('batch', 'blk', 'uly')), may hold values from -0.0625 to 0.0625
- w_gate_up: bfloat16 [16, 2048, 2048], P('blk', ('batch', 'uly')), may hold values from -0.125 to 0.125
- w_down: bfloat16 [16, 2048, 1024], P('blk', ('batch', 'uly')), may hold values from -1.5 to 1.5
- cotangent: bfloat16 [2, 2048, 2048], P('batch', ('blk', 'uly')), may hold values from -6 to 6
Outputs:
- output: bfloat16 [2, 2048, 2048], P('batch', ('blk', 'uly'))
- grad_tokens: float32 [2, 2048, 2048], P('batch', ('blk', 'uly'))
- grad_qkv: float32 [2048, 6144], P(('batch', 'blk', 'uly'))
- grad_out: float32 [2048, 2048], P(('batch', 'blk', 'uly'))
- grad_attn_gain: float32 [2048], P(('batch', 'blk', 'uly'))
- grad_ffn_gain: float32 [2048], P(('batch', 'blk', 'uly'))
- grad_qk_gain: float32 [2, 128], replicated
- grad_router: float32 [2048, 16], P(('batch', 'blk', 'uly'))
- grad_gate_up: float32 [16, 2048, 2048], P('blk', ('batch', 'uly'))
- grad_down: float32 [16, 2048, 1024], P('blk', ('batch', 'uly'))
- clipped_qkv: float32 [2048, 6144], P(('batch', 'blk', 'uly'))
The draws below stay inside these ranges and needn't reach their ends.
Inputs may be any that keep to these rules, and one draw needn't show every extreme that they name: `routes`: within the tokens of one device (aligned blocks of 128 tokens) no expert is named more than 96 times, a bound that some block reaches; a token names 8 different experts. `segments`: numbers never fall along a sequence; equal numbers mark one document.
All inputs are finite; a program needn't handle non-finite values.
Results may differ from the reference program's by a relative error of at most 0.025.
Values may be sent and summed in bfloat16 or wider, within the bound.
A program may use at most 384 MiB of HBM per device.

```python
import math
import jax
import jax.numpy as jnp
import numpy as np
from jax import lax

D = 2048
HEADS = 16
HEAD_SIZE = 128
F = 1024
TOP = 8
EXPERTS = 16
TOK_DEV = 128
CAP = 96
SEQS = 2
LEN = 2048
N_ULY = 4


cut_count = 8


def draw_segments(key, part):
    key = jax.random.fold_in(key, 7)
    shard_len = TOK_DEV * N_ULY

    def one_sequence(seq_key):
        keys_four = jax.random.split(seq_key, 4)
        doc_begin = jax.random.randint(keys_four[0], (), 1, shard_len)
        doc_finish = jax.random.randint(keys_four[1], (), LEN - shard_len + 1, LEN - 1)
        early_cuts = jax.random.randint(keys_four[2], (cut_count,), 1, doc_begin + 1)
        late_cuts = jax.random.randint(keys_four[3], (cut_count,), doc_finish + 1, LEN)
        cuts = jnp.concatenate([doc_begin[None], doc_finish[None], early_cuts, late_cuts])
        positions = jnp.arange(LEN, dtype=jnp.int32)
        return jnp.sum((positions[:, None] >= cuts[None, :]).astype(jnp.int32), axis=1).astype(jnp.int32)
    return jax.vmap(one_sequence)(jax.random.split(key, SEQS))


def shard_levels(own_key, extent, pieces, smallest, high):
    level, own = 1.0, jax.random.fold_in(own_key, 6)
    for axis_at, blocks in pieces:
        draws = jnp.exp(jax.random.uniform(jax.random.fold_in(own, axis_at), (blocks,), jnp.float32, smallest / len(pieces), high / len(pieces)))
        level = level * jnp.repeat(draws, extent[axis_at] // blocks).reshape([-1 if axis == axis_at else 1 for axis in range(len(extent))])
    return level


def assign_block(key, own, number, rows, number_of, top, most, lean):
    sequence = jax.random.permutation(key, number_of)
    crowded, common = shares(number_of, rows * top, most, lean, True), shares(number_of, rows * top, most, lean, False)
    places = jnp.arange(number_of)

    def named(tallies, offset_by):
        used = int((tallies > 0).sum())
        fixed = max(1, used // 4)
        passed = fixed + (places - fixed + offset_by * (used - fixed)) % max(1, number_of - fixed)
        return jnp.zeros((number_of,), jnp.int32).at[sequence[jnp.where(places < fixed, places, passed)]].set(jnp.asarray(tallies, jnp.int32))

    tallies = jnp.where(number % 4 == 0, named(crowded, number // 4), named(common, number - number // 4 - 1))
    mixed = jax.random.permutation(jax.random.fold_in(own, 3), number_of)
    source_of, sink = mixed[0:number_of // 2 * 2:2], mixed[1:number_of // 2 * 2:2]
    slack = jnp.minimum(tallies[source_of] - 1, most - tallies[sink]) // 2
    slack = jnp.where((source_of == sequence[0]) | (sink == sequence[0]) | (tallies[sink] == 0), 0, jnp.maximum(slack, 0))
    passed = jax.random.randint(jax.random.fold_in(own, 4), (number_of // 2,), 0, 1 << 20) % (slack + 1)
    tallies = tallies.at[source_of].add(-passed).at[sink].add(passed)
    members = jnp.searchsorted(jnp.cumsum(tallies), jnp.arange(rows * top), side="right").astype(jnp.int32)
    listing = members.reshape(top, rows).T
    listing = listing[jax.random.permutation(jax.random.fold_in(own, 1), rows)]
    offset_by = jax.random.randint(jax.random.fold_in(own, 2), (rows, 1), 0, top)
    return jnp.take_along_axis(listing, (jnp.arange(top)[None, :] + offset_by) % top, axis=1)


def shares(count, total, bound, skew, full):
    portions = [(1 << 20) // math.isqrt(rank ** skew) + 1 for rank in range(1, count + 1)]
    largest = bound if full else min(bound, max(-(-total // count), total * portions[0] // sum(portions)))
    least = 1 if total - largest >= count - 1 else 0
    holding, spare = [largest] + [least] * (count - 1), total - largest - least * (count - 1)
    while spare > 0:
        candidates = [i for i in range(1, count) if holding[i] < largest] or [i for i in range(1, count) if holding[i] < bound]
        pool, remaining = sum([portions[i] for i in candidates]), spare
        for i in candidates:
            more = min(bound - holding[i], max(1, remaining * portions[i] // pool), spare)
            holding[i] = holding[i] + more
            spare = spare - more
    return np.array(holding)


def bell_draw(key, dims, deviation, limit, cuts=(), kind=jnp.bfloat16):
    entries = jax.random.normal(key, dims, jnp.float32) * deviation
    if len(cuts) > 0:
        entries = shard_levels(key, dims, cuts, -0.22, 0.18) * entries
    return jnp.clip(entries, min=-limit, max=limit).astype(kind)


def setup_inputs(seed: int = 0) -> dict:
    key_list = jax.random.split(jax.random.key(seed), 13)
    tokens = bell_draw(key_list[0], (SEQS, LEN, D), 1.0, 6.0, ((0, 2), (1, 16)))
    segments = draw_segments(jax.random.fold_in(key_list[12], 71), 0)
    routes_keys = jax.random.split(jax.random.fold_in(key_list[2], 1), SEQS * LEN // TOK_DEV)
    routes_turns = jax.random.permutation(jax.random.fold_in(key_list[2], 3), SEQS * LEN // TOK_DEV)
    routes = jax.vmap(lambda own, number: assign_block(jax.random.fold_in(key_list[2], 2), own, number, TOK_DEV, EXPERTS, TOP, CAP, 2))(routes_keys, routes_turns).reshape((SEQS, LEN, TOP))
    w_qkv = bell_draw(key_list[3], (D, 3 * D), D ** -0.5, 0.125, ((0, 32),))
    w_out = bell_draw(key_list[4], (D, D), (max(1, D // 1024)) ** -0.5, 4.0, ((0, 32),))
    attn_gain = jnp.clip(1.0 + 0.1 * jax.random.normal(key_list[5], (D,), jnp.float32), 0.5, 1.5).astype(jnp.bfloat16)
    ffn_gain = jnp.clip(1.0 + 0.1 * jax.random.normal(key_list[6], (D,), jnp.float32), 0.5, 1.5).astype(jnp.bfloat16)
    qk_gain = jnp.clip(jnp.exp(jax.random.uniform(key_list[7], (2, HEAD_SIZE), jnp.float32, math.log(1.0), math.log(2.0))), 1.0, 2.0).astype(jnp.bfloat16)
    router = bell_draw(key_list[8], (D, EXPERTS), (4 * D) ** -0.5, 0.0625, ((0, 32),))
    w_gate_up = bell_draw(key_list[9], (EXPERTS, D, 2 * F), D ** -0.5, 0.125, ((0, 4), (1, 8)))
    w_down = bell_draw(key_list[10], (EXPERTS, D, F), (max(1, F // 64)) ** -0.5, 1.5, ((0, 4), (1, 8)))
    cotangent = bell_draw(key_list[11], (SEQS, LEN, D), 1.0, 6.0, ((0, 2), (1, 16)))
    return {"tokens": tokens, "segments": segments, "routes": routes, "w_qkv": w_qkv, "w_out": w_out, "attn_gain": attn_gain, "ffn_gain": ffn_gain, "qk_gain": qk_gain, "router": router, "w_gate_up": w_gate_up, "w_down": w_down, "cotangent": cotangent}


EPS = 1e-06
THETA = 50000.0
TAU = 4.0
NEG = -1e+30
HIGH_ACCURACY = lax.Precision.HIGHEST

@jax.custom_vjp
def lower_accuracy(v):
    return lax.optimization_barrier(v.astype(jnp.bfloat16)).astype(jnp.float32)

@jax.custom_vjp
def lower_accuracy_reverse(v):
    return v

def low_keep(v):
    return (lower_accuracy(v), None)

def low_pass(kept, grad):
    return (grad,)

def back_keep(v):
    return (v, None)

def back_low(kept, grad):
    return (lower_accuracy(grad),)
lower_accuracy.defvjp(low_keep, low_pass)
lower_accuracy_reverse.defvjp(back_keep, back_low)

def matmul_hi(left_side, right_side):
    return jnp.dot(left_side, right_side, precision=HIGH_ACCURACY, preferred_element_type=jnp.float32)

def rms_scale(values):
    return lax.rsqrt(lax.optimization_barrier(jnp.mean(values * values, axis=-1, keepdims=True)) + EPS)

def rope_tables(length):
    half_dim = HEAD_SIZE // 2
    frequency = THETA ** (-jnp.arange(half_dim, dtype=jnp.float32) * 2.0 / HEAD_SIZE)
    positions = jnp.arange(length, dtype=jnp.int32).astype(jnp.float32)
    angles = positions[:, None] * frequency[None, :]
    return (jnp.cos(angles)[:, None, :], jnp.sin(angles)[:, None, :])

def rotate(values, cos_table, sin_table):
    half_dim = values.shape[-1] // 2
    first_half = values[..., :half_dim]
    second_half = values[..., half_dim:]
    return jnp.concatenate([first_half * cos_table - second_half * sin_table, second_half * cos_table + first_half * sin_table], axis=-1)

def slot_table(route_blk):
    flat_routes = route_blk.reshape(-1).astype(jnp.int32)
    onehot = (flat_routes[:, None] == jnp.arange(EXPERTS, dtype=jnp.int32)[None, :]).astype(jnp.int32)
    slot_rank = lax.optimization_barrier(jnp.sum((jnp.cumsum(onehot, axis=0) - 1) * onehot, axis=1)).astype(jnp.int32)
    pair_slots = (flat_routes * CAP + slot_rank).astype(jnp.int32)
    pair_tokens = (jnp.arange(flat_routes.shape[0], dtype=jnp.int32) // route_blk.shape[1]).astype(jnp.int32)
    slot_owner = jnp.full((EXPERTS * CAP,), route_blk.shape[0], jnp.int32).at[pair_slots].set(pair_tokens)
    return (pair_slots, slot_owner)

def attention(queries, every_key, every_value, seg_row):
    length = queries.shape[0]
    block_size = min(512, length)
    block_count = length // block_size

    def one_block(inputs):
        query_tile, seg_blk = inputs
        logit_matrix = lower_accuracy_reverse(jnp.einsum('puw,quw->upq', query_tile, every_key, precision=HIGH_ACCURACY) * HEAD_SIZE ** (-0.5))
        allowed = (seg_blk[:, None] == seg_row[None, :])[None, :, :]
        masked = jnp.where(allowed, logit_matrix, NEG)
        row_top = lax.optimization_barrier(jnp.max(masked, axis=2, keepdims=True))
        attention_weights = jnp.where(allowed, jnp.exp(masked - row_top), 0.0)
        attention_weights = attention_weights / lax.optimization_barrier(jnp.sum(attention_weights, axis=2, keepdims=True))
        blended_heads = jnp.einsum('cqy,ycu->qcu', lower_accuracy(attention_weights), every_value, precision=HIGH_ACCURACY)
        return (blended_heads, lax.optimization_barrier(jnp.max(row_top[:, :, 0], axis=1)))
    blended_heads, largest = lax.map(jax.checkpoint(one_block), (queries.reshape(block_count, block_size, HEADS, HEAD_SIZE), seg_row.reshape(block_count, block_size)))
    return (blended_heads.reshape(length, HEADS * HEAD_SIZE), lax.optimization_barrier(jnp.max(largest, axis=0)))

def moe_block(inputs, w_gate_up, w_down):
    hidden_blk, route_blk, gate_blk = inputs
    pair_slots, slot_owner = slot_table(route_blk)
    padded = jnp.concatenate([hidden_blk, jnp.zeros((1, D), hidden_blk.dtype)], axis=0)
    rows_in = lower_accuracy_reverse(padded[slot_owner].reshape(EXPERTS, CAP, D))
    pre_act = lower_accuracy_reverse(jnp.einsum('ecd,edf->ecf', rows_in, w_gate_up, precision=HIGH_ACCURACY))
    activation = lower_accuracy(jax.nn.silu(pre_act[..., :F]) * pre_act[..., F:])
    result = lower_accuracy(lower_accuracy_reverse(jnp.einsum('ecf,edf->ecd', activation, w_down, precision=HIGH_ACCURACY)))
    paired = result.reshape(EXPERTS * CAP, D)[pair_slots].reshape(route_blk.shape[0], TOP, D)
    return lax.optimization_barrier(jnp.sum(gate_blk[:, :, None] * paired, axis=1))

def layer(x_seq, seg_row, route_seq, w_qkv, w_out, attn_gain, ffn_gain, qk_gain, router, w_gate_up, w_down):
    length = x_seq.shape[0]
    hidden_one = lower_accuracy(x_seq * rms_scale(x_seq) * attn_gain)
    projected = lower_accuracy_reverse(matmul_hi(hidden_one, w_qkv))
    query_raw = projected[:, :D].reshape(length, HEADS, HEAD_SIZE)
    key_raw = projected[:, D:2 * D].reshape(length, HEADS, HEAD_SIZE)
    value_raw = projected[:, 2 * D:].reshape(length, HEADS, HEAD_SIZE)
    cos_table, sin_table = rope_tables(length)
    queries = lower_accuracy(lower_accuracy_reverse(rotate(query_raw * rms_scale(query_raw) * qk_gain[0], cos_table, sin_table)))
    every_key = lower_accuracy(lower_accuracy_reverse(rotate(key_raw * rms_scale(key_raw) * qk_gain[1], cos_table, sin_table)))
    every_value = lower_accuracy(value_raw)
    blended_heads, largest = attention(queries, every_key, every_value, seg_row)
    attn_tok = lower_accuracy(lower_accuracy_reverse(blended_heads))
    residual_mid = x_seq + lower_accuracy_reverse(matmul_hi(attn_tok, w_out))
    hidden_two = lower_accuracy(residual_mid * rms_scale(residual_mid) * ffn_gain)
    router_probs = jax.nn.softmax(lower_accuracy_reverse(matmul_hi(hidden_two, router)), axis=1)
    chosen = (route_seq[:, :, None] == jnp.arange(EXPERTS, dtype=jnp.int32)[None, None, :]).astype(jnp.float32)
    gate_values = lax.optimization_barrier(jnp.sum(chosen * router_probs[:, None, :], axis=2))
    block_count = length // TOK_DEV
    expert_mix = lax.map(jax.checkpoint(lambda inputs: moe_block(inputs, w_gate_up, w_down)), (hidden_two.reshape(block_count, TOK_DEV, D), route_seq.reshape(block_count, TOK_DEV, TOP), gate_values.reshape(block_count, TOK_DEV, TOP)))
    return (residual_mid + expert_mix.reshape(length, D), largest)

def reference(tokens, segments, routes, w_qkv, w_out, attn_gain, ffn_gain, qk_gain, router, w_gate_up, w_down, cotangent):
    floats = tuple((value_in.astype(jnp.float32) for value_in in (tokens, w_qkv, w_out, attn_gain, ffn_gain, qk_gain, router, w_gate_up, w_down)))

    def forward(inputs, w_qkv, w_out, attn_gain, ffn_gain, qk_gain, router, w_gate_up, w_down):
        results = []
        largest = []
        for seq_index in range(SEQS):
            result, row_top = layer(inputs[seq_index], segments[seq_index], routes[seq_index], w_qkv, w_out, attn_gain, ffn_gain, qk_gain, router, w_gate_up, w_down)
            results.append(result)
            largest.append(row_top)
        return (jnp.stack(results), lax.optimization_barrier(jnp.max(jnp.stack(largest), axis=0)))
    output, pullback, head_max = jax.vjp(forward, *floats, has_aux=True)
    gradients = pullback(cotangent.astype(jnp.float32))
    clip_gamma = TAU / jnp.maximum(head_max, TAU)
    factor = jnp.repeat(jnp.sqrt(clip_gamma), HEAD_SIZE)
    column_scale = jnp.concatenate([factor, factor, jnp.ones((D,), jnp.float32)])
    clipped = floats[1] * column_scale[None, :]
    return (output.astype(jnp.bfloat16), gradients[0], gradients[1], gradients[2], gradients[3], gradients[4], gradients[5], gradients[6], gradients[7], gradients[8], clipped)
```

```python
import functools

import jax
import jax.numpy as jnp
from jax import lax
from jax.experimental import pallas as pl
from jax.experimental.pallas import tpu as pltpu
from jax.sharding import PartitionSpec as P

EPS = 1e-06
THETA = 50000.0
TAU = 4.0
NEG = -1e30
LOG2E = 1.4426950408889634
LANES = 128
MOST_TOKENS = 512
VMEM_LIMIT = 60 * 1024 * 1024

ALL = ("batch", "blk", "uly")
ROWS = ("batch", "blk")
PLANE = ("batch", "uly")

BF16 = jnp.bfloat16
F32 = jnp.float32


def rms_scale(values):
    return lax.rsqrt(jnp.mean(values * values, axis=-1, keepdims=True) + EPS)


def norm_back(grad_normed, values, scale):
    normed = values * scale
    return scale * (grad_normed - normed * jnp.mean(grad_normed * normed, axis=-1, keepdims=True))


def rope_tables(offset, length, head_dim):
    half_dim = head_dim // 2
    frequency = THETA ** (-jnp.arange(half_dim, dtype=F32) * 2.0 / head_dim)
    positions = (offset + jnp.arange(length, dtype=jnp.int32)).astype(F32)
    angles = positions[:, None] * frequency[None, :]
    return (jnp.cos(angles)[:, None, :], jnp.sin(angles)[:, None, :])


def rotate(values, cos_table, sin_table):
    half_dim = values.shape[-1] // 2
    first = values[..., :half_dim]
    second = values[..., half_dim:]
    return jnp.concatenate(
        [first * cos_table - second * sin_table, second * cos_table + first * sin_table], axis=-1
    )


def dot_nn(a, b):
    return lax.dot_general(a, b, (((1,), (0,)), ((), ())), preferred_element_type=F32)


def dot_nt(a, b):
    return lax.dot_general(a, b, (((1,), (1,)), ((), ())), preferred_element_type=F32)


def dot_tn(a, b):
    return lax.dot_general(a, b, (((0,), (0,)), ((), ())), preferred_element_type=F32)


def key_chunks(length):
    size = min(512, length)
    return size, length // size


def attn_fwd_kernel(factor, q_ref, k_ref, v_ref, sq_ref, sk_ref, o_ref, of_ref, lse_ref, top_ref, vt_ref):
    length = k_ref.shape[1]
    size, count = key_chunks(length)
    tile, head_dim = q_ref.shape[1:]

    @pl.when(pl.program_id(1) == 0)
    def _():
        vt_ref[...] = v_ref[0].astype(F32).T.astype(BF16)

    q = q_ref[0]
    seg_q = sq_ref[...]

    def step(j, carried):
        total, top, acc = carried
        at = pl.multiple_of(j * size, size)
        scores = dot_nt(k_ref[0, pl.ds(at, size), :], q)
        scores = jnp.where(sk_ref[pl.ds(at, size), :] == seg_q, scores, NEG)
        top = jnp.maximum(top, jnp.max(scores, axis=0, keepdims=True))
        weights = jnp.exp2(scores * factor)
        total = total + jnp.sum(weights, axis=0, keepdims=True)
        acc = acc + dot_nn(vt_ref[:, pl.ds(at, size)], weights.astype(BF16))
        return total, top, acc

    start = (
        jnp.zeros((1, tile), F32),
        jnp.full((1, tile), NEG, F32),
        jnp.zeros((head_dim, tile), F32),
    )
    total, top, acc = lax.fori_loop(0, count, step, start, unroll=count <= 4)
    out = (acc * (1.0 / total)).T
    o_ref[0] = out.astype(BF16)
    of_ref[0] = out
    lse_ref[0] = jnp.log2(total)
    top_ref[0] = top


def attn_bwd_kernel(
    factor, scale, q_ref, k_ref, v_ref, do_ref, of_ref, lse_ref, sq_ref, sk_ref,
    dq_ref, dk_ref, dv_ref, kt_ref, dk_acc, dv_acc,
):
    length = k_ref.shape[1]
    size, count = key_chunks(length)
    tile, head_dim = q_ref.shape[1:]

    @pl.when(pl.program_id(1) == 0)
    def _():
        kt_ref[...] = k_ref[0].astype(F32).T.astype(BF16)
        dk_acc[...] = jnp.zeros_like(dk_acc)
        dv_acc[...] = jnp.zeros_like(dv_acc)

    q = q_ref[0]
    grad = do_ref[0]
    seg_q = sq_ref[...]
    lse = lse_ref[0]
    row_dot = jnp.sum((grad.astype(F32) * of_ref[0]).T, axis=0, keepdims=True)

    def step(j, dq_t):
        at = pl.multiple_of(j * size, size)
        rows = pl.ds(at, size)
        scores = dot_nt(k_ref[0, rows, :], q)
        scores = jnp.where(sk_ref[rows, :] == seg_q, scores, NEG)
        weights = jnp.exp2(scores * factor - lse)
        grad_weights = dot_nt(v_ref[0, rows, :], grad)
        grad_scores = (weights * (grad_weights - row_dot)).astype(BF16)
        dk_acc[rows, :] += dot_nn(grad_scores, q)
        dv_acc[rows, :] += dot_nn(weights.astype(BF16), grad)
        return dq_t + dot_nn(kt_ref[:, rows], grad_scores)

    dq_t = lax.fori_loop(0, count, step, jnp.zeros((head_dim, tile), F32), unroll=count <= 4)
    dq_ref[0] = (dq_t * scale).T.astype(BF16)

    @pl.when(pl.program_id(1) == pl.num_programs(1) - 1)
    def _():
        dk_ref[0] = (dk_acc[...] * scale).astype(BF16)
        dv_ref[0] = dv_acc[...].astype(BF16)


def attention_tile(queries, length):
    return min(queries, 256 if length <= 4096 else 128)


def attention_forward(q_src, kv_src, cols, seg_q, seg_k, head_dim):
    heads, queries = q_src.shape[:2]
    length = kv_src.shape[1]
    tile = attention_tile(queries, length)
    q_col, k_col, v_col = cols
    factor = head_dim**-0.5 * LOG2E
    row = pl.BlockSpec((1, 1, tile), lambda h, i: (h, 0, i))
    block = pl.BlockSpec((1, tile, head_dim), lambda h, i: (h, i, 0))
    return pl.pallas_call(
        functools.partial(attn_fwd_kernel, factor),
        grid=(heads, queries // tile),
        in_specs=[
            pl.BlockSpec((1, tile, head_dim), lambda h, i: (h, i, q_col)),
            pl.BlockSpec((1, length, head_dim), lambda h, i: (h, 0, k_col)),
            pl.BlockSpec((1, length, head_dim), lambda h, i: (h, 0, v_col)),
            pl.BlockSpec((1, tile), lambda h, i: (0, i)),
            pl.BlockSpec((length, 1), lambda h, i: (0, 0)),
        ],
        out_specs=[block, block, row, row],
        out_shape=[
            jax.ShapeDtypeStruct((heads, queries, head_dim), BF16),
            jax.ShapeDtypeStruct((heads, queries, head_dim), F32),
            jax.ShapeDtypeStruct((heads, 1, queries), F32),
            jax.ShapeDtypeStruct((heads, 1, queries), F32),
        ],
        scratch_shapes=[pltpu.VMEM((head_dim, length), BF16)],
        compiler_params=pltpu.CompilerParams(vmem_limit_bytes=VMEM_LIMIT),
        cost_estimate=pl.CostEstimate(
            flops=4 * heads * queries * length * head_dim,
            bytes_accessed=heads * (queries + length) * head_dim * 8,
            transcendentals=heads * queries * length,
        ),
        name="attend",
    )(q_src, kv_src, kv_src, seg_q.reshape(1, -1), seg_k.reshape(-1, 1))


def attention_backward(q_src, kv_src, cols, grad, out_f32, lse, seg_q, seg_k, head_dim):
    heads, queries = q_src.shape[:2]
    length = kv_src.shape[1]
    tile = attention_tile(queries, length)
    q_col, k_col, v_col = cols
    scale = head_dim**-0.5
    row = pl.BlockSpec((1, 1, tile), lambda h, i: (h, 0, i))
    block = pl.BlockSpec((1, tile, head_dim), lambda h, i: (h, i, 0))
    whole = pl.BlockSpec((1, length, head_dim), lambda h, i: (h, 0, 0))
    return pl.pallas_call(
        functools.partial(attn_bwd_kernel, scale * LOG2E, scale),
        grid=(heads, queries // tile),
        in_specs=[
            pl.BlockSpec((1, tile, head_dim), lambda h, i: (h, i, q_col)),
            pl.BlockSpec((1, length, head_dim), lambda h, i: (h, 0, k_col)),
            pl.BlockSpec((1, length, head_dim), lambda h, i: (h, 0, v_col)),
            block,
            block,
            row,
            pl.BlockSpec((1, tile), lambda h, i: (0, i)),
            pl.BlockSpec((length, 1), lambda h, i: (0, 0)),
        ],
        out_specs=[block, whole, whole],
        out_shape=[
            jax.ShapeDtypeStruct((heads, queries, head_dim), BF16),
            jax.ShapeDtypeStruct((heads, length, head_dim), BF16),
            jax.ShapeDtypeStruct((heads, length, head_dim), BF16),
        ],
        scratch_shapes=[
            pltpu.VMEM((head_dim, length), BF16),
            pltpu.VMEM((length, head_dim), F32),
            pltpu.VMEM((length, head_dim), F32),
        ],
        compiler_params=pltpu.CompilerParams(vmem_limit_bytes=VMEM_LIMIT),
        cost_estimate=pl.CostEstimate(
            flops=10 * heads * queries * length * head_dim,
            bytes_accessed=heads * (queries + length) * head_dim * 12,
            transcendentals=heads * queries * length,
        ),
        name="attend_back",
    )(q_src, kv_src, kv_src, grad, out_f32, lse, seg_q.reshape(1, -1), seg_k.reshape(-1, 1))


def expert_kernel(
    h_ref, dy_ref, gate_ref, wg_ref, wu_ref, wd_ref,
    out_ref, dx_ref, dg_ref, gr_ref, ht_ref, dyt_ref, out_acc, dx_acc,
):
    expert, chunk = pl.program_id(0), pl.program_id(1)
    first = (expert == 0) & (chunk == 0)
    last = (expert == pl.num_programs(0) - 1) & (chunk == pl.num_programs(1) - 1)
    width = h_ref.shape[1]
    parts, _, part_rows, cols = wg_ref.shape

    @pl.when(first)
    def _():
        ht_ref[...] = h_ref[...].T
        dyt_ref[...] = dy_ref[...].T
        out_acc[...] = jnp.zeros_like(out_acc)
        dx_acc[...] = jnp.zeros_like(dx_acc)

    @pl.when(chunk == 0)
    def _():
        dg_ref[...] = jnp.zeros_like(dg_ref)

    w_gate = wg_ref[...].reshape(width, cols)
    w_up = wu_ref[...].reshape(width, cols)
    w_down = wd_ref[...].reshape(width, cols)
    gate = gate_ref[0]
    a_gate = dot_nn(h_ref[...], w_gate)
    a_up = dot_nn(h_ref[...], w_up)
    raw = dot_nn(dy_ref[...], w_down)
    sigma = 1.0 / (1.0 + jnp.exp2(a_gate * -LOG2E))
    swish = a_gate * sigma
    act = swish * a_up
    dg_ref[0] += jnp.sum(raw * act, axis=1, keepdims=True)
    gated = (gate * act).astype(BF16)
    d_act = gate * raw
    d_gate = (d_act * a_up * (sigma + swish * (1.0 - sigma))).astype(BF16)
    d_up = (d_act * swish).astype(BF16)
    out_acc[...] += dot_nt(gated, w_down)
    dx_acc[...] += dot_nt(d_gate, w_gate) + dot_nt(d_up, w_up)
    gr_ref[:, 0, 0] = dot_nn(ht_ref[...], d_gate).astype(BF16).reshape(parts, part_rows, cols)
    gr_ref[:, 1, 0] = dot_nn(ht_ref[...], d_up).astype(BF16).reshape(parts, part_rows, cols)
    gr_ref[:, 2, 0] = dot_nn(dyt_ref[...], gated).astype(BF16).reshape(parts, part_rows, cols)

    @pl.when(last)
    def _():
        out_ref[...] = out_acc[...].astype(BF16)
        dx_ref[...] = dx_acc[...].astype(BF16)


def experts(hidden, grad, gates, gate_up, down):
    tokens, width = hidden.shape
    parts, local, part_rows, units = down.shape
    cols = min(256, units)
    chunks = units // cols
    whole = pl.BlockSpec((tokens, width), lambda e, f: (0, 0))
    column = pl.BlockSpec((1, tokens, 1), lambda e, f: (e, 0, 0))
    weight = (parts, 1, part_rows, cols)
    return pl.pallas_call(
        expert_kernel,
        grid=(local, chunks),
        in_specs=[
            whole,
            whole,
            column,
            pl.BlockSpec(weight, lambda e, f: (0, e, 0, f)),
            pl.BlockSpec(weight, lambda e, f: (0, e, 0, chunks + f)),
            pl.BlockSpec(weight, lambda e, f: (0, e, 0, f)),
        ],
        out_specs=[
            whole,
            whole,
            column,
            pl.BlockSpec((parts, 3, 1, part_rows, cols), lambda e, f: (0, 0, e, 0, f)),
        ],
        out_shape=[
            jax.ShapeDtypeStruct((tokens, width), BF16),
            jax.ShapeDtypeStruct((tokens, width), BF16),
            jax.ShapeDtypeStruct((local, tokens, 1), F32),
            jax.ShapeDtypeStruct((parts, 3, local, part_rows, units), BF16),
        ],
        scratch_shapes=[
            pltpu.VMEM((width, tokens), BF16),
            pltpu.VMEM((width, tokens), BF16),
            pltpu.VMEM((tokens, width), F32),
            pltpu.VMEM((tokens, width), F32),
        ],
        compiler_params=pltpu.CompilerParams(vmem_limit_bytes=VMEM_LIMIT),
        cost_estimate=pl.CostEstimate(
            flops=18 * local * tokens * width * units,
            bytes_accessed=12 * local * width * units,
            transcendentals=local * tokens * units,
        ),
        name="experts",
    )(hidden, grad, gates, gate_up, gate_up, down)


def swap(values, axis):
    return lax.all_to_all(values, axis, split_axis=0, concat_axis=0, tiled=True)


def sum_scatter(values, axis):
    count = lax.axis_size(axis)
    rows, width = values.shape
    parts = swap(values.astype(BF16).reshape(count, rows // count, width), axis)
    return jnp.sum(parts.astype(F32), axis=0)


def per_device(
    tokens, segments, routes, w_qkv, w_out, attn_gain, ffn_gain, qk_gain, router, w_gate_up, w_down, cotangent
):
    own_tokens = tokens[0]
    own_grad = cotangent[0]
    count_tok, width = own_tokens.shape
    head_dim = qk_gain.shape[1]
    heads = width // head_dim
    uly, blk, batch = lax.axis_size("uly"), lax.axis_size("blk"), lax.axis_size("batch")
    blk_at, uly_at = lax.axis_index("blk"), lax.axis_index("uly")
    group = batch * blk
    local_heads = heads // uly
    local_width = local_heads * head_dim
    rows = count_tok * uly
    seg_row = segments[0]
    length = seg_row.shape[0]
    number = router.shape[1]
    local_experts, _, units = w_down.shape
    shard_rows = w_qkv.shape[0]

    extra = jnp.concatenate([attn_gain[:, None], ffn_gain[:, None], router], axis=1)
    extra = jnp.pad(extra, ((0, 0), (0, LANES - extra.shape[1])))
    columns = w_qkv.reshape(shard_rows, 3, uly, local_width).transpose(2, 0, 1, 3)
    packed = jnp.concatenate(
        [
            columns.reshape(uly, shard_rows, 3 * local_width),
            jnp.broadcast_to(extra[None], (uly, shard_rows, LANES)),
        ],
        axis=2,
    )
    packed = swap(packed, "uly").reshape(uly * shard_rows, 3 * local_width + LANES)
    packed = lax.all_gather(packed, ROWS, axis=0, tiled=True)
    own_qkv = packed[:, : 3 * local_width]
    gain_attn = packed[:, 3 * local_width].astype(F32)
    gain_ffn = packed[:, 3 * local_width + 1].astype(F32)
    whole_router = packed[:, 3 * local_width + 2 : 3 * local_width + 2 + number]
    tokens_all = lax.all_gather(own_tokens, "uly", axis=0, tiled=True)
    to_rows = [(u * group + g, g * uly + u) for g in range(group) for u in range(uly)]
    own_out = lax.all_gather(lax.ppermute(w_out, ALL, to_rows), ROWS, axis=0, tiled=True)
    whole_gate_up = lax.all_gather(w_gate_up, PLANE, axis=0, tiled=False)
    whole_down = lax.all_gather(w_down, PLANE, axis=0, tiled=False)
    grad_blk = lax.all_gather(own_grad, "blk", axis=0, tiled=True)
    routes_blk = lax.all_gather(routes[0], "blk", axis=0, tiled=True)

    gain_query = qk_gain[0].astype(F32)
    gain_key = qk_gain[1].astype(F32)
    inputs_all = tokens_all.astype(F32)
    normed_one = inputs_all * rms_scale(inputs_all)
    hidden_one = (normed_one * gain_attn).astype(BF16)
    projected = dot_nn(hidden_one, own_qkv)
    query_raw = projected[:, :local_width].reshape(rows, local_heads, head_dim)
    key_raw = projected[:, local_width : 2 * local_width].reshape(rows, local_heads, head_dim)
    value_raw = projected[:, 2 * local_width :].reshape(rows, local_heads, head_dim)
    cos_table, sin_table = rope_tables(blk_at * rows, rows, head_dim)
    query_scale = rms_scale(query_raw)
    key_scale = rms_scale(key_raw)
    qkv = jnp.concatenate(
        [
            rotate(query_raw * query_scale * gain_query, cos_table, sin_table),
            rotate(key_raw * key_scale * gain_key, cos_table, sin_table),
            value_raw,
        ],
        axis=2,
    ).astype(BF16)
    qkv = qkv.transpose(1, 0, 2)

    by_heads = local_heads % blk == 0
    if by_heads:
        per = local_heads // blk

        def to_heads(values):
            columns = values.shape[2]
            moved = swap(values.reshape(blk, per, rows, columns), "blk")
            return moved.transpose(1, 0, 2, 3).reshape(per, length, columns)

        def to_rows_back(values):
            columns = values.shape[2]
            parts = values.reshape(per, blk, rows, columns).transpose(1, 0, 2, 3)
            return swap(parts, "blk").reshape(local_heads, rows, columns)

        q_src = kv_src = to_heads(qkv)
        cols = (0, 1, 2)
        seg_q = seg_row
        first_head = uly_at * local_heads + blk_at * per
    else:

        def to_heads(values):
            return values

        def to_rows_back(values):
            return values

        q_src = qkv
        kv_src = lax.all_gather(qkv[:, :, head_dim:], "blk", axis=1, tiled=True)
        cols = (0, 0, 1)
        seg_q = lax.dynamic_slice_in_dim(seg_row, blk_at * rows, rows)
        first_head = uly_at * local_heads
    attn_low, attn_f32, lse, top = attention_forward(q_src, kv_src, cols, seg_q, seg_row, head_dim)
    head_vector = lax.dynamic_update_slice_in_dim(
        jnp.full((heads,), NEG, F32), jnp.max(top, axis=(1, 2)) * head_dim**-0.5, first_head, 0
    )
    head_max = lax.pmax(head_vector, ALL)
    attn_rows = to_rows_back(attn_low)
    out_heads = own_out.reshape(local_heads, head_dim, width)
    branch = jnp.einsum("htc,hcd->td", attn_rows, out_heads, preferred_element_type=F32)
    inputs = own_tokens.astype(F32)
    mid = inputs + sum_scatter(branch, "uly")

    scale_two = rms_scale(mid)
    normed_two = mid * scale_two
    hidden_two = (normed_two * gain_ffn).astype(BF16)
    hidden_blk = lax.all_gather(hidden_two, "blk", axis=0, tiled=True)
    probs_blk = jax.nn.softmax(dot_nn(hidden_blk, whole_router), axis=1)
    names = jnp.arange(number, dtype=jnp.int32)
    chosen_blk = jnp.any(routes_blk[:, :, None] == names, axis=1).astype(F32)
    own_names = blk_at * local_experts
    gates = lax.dynamic_slice_in_dim(probs_blk * chosen_blk, own_names, local_experts, axis=1)
    gate_columns = gates.T[:, :, None]
    most = min(MOST_TOKENS, hidden_blk.shape[0])
    made = [
        experts(
            hidden_blk[at : at + most],
            grad_blk[at : at + most],
            gate_columns[:, at : at + most],
            whole_gate_up,
            whole_down,
        )
        for at in range(0, hidden_blk.shape[0], most)
    ]
    out_part = jnp.concatenate([m[0] for m in made], axis=0)
    dx_part = jnp.concatenate([m[1] for m in made], axis=0)
    dg_part = jnp.concatenate([m[2] for m in made], axis=1)
    expert_grads = made[0][3]
    for m in made[1:]:
        expert_grads = (expert_grads.astype(F32) + m[3].astype(F32)).astype(BF16)
    expert_sums = lax.psum_scatter(expert_grads, PLANE, scatter_dimension=0, tiled=False).astype(F32)
    grad_gate_up = jnp.concatenate([expert_sums[0], expert_sums[1]], axis=2)
    grad_down = expert_sums[2]
    dg_parts = swap(dg_part.reshape(local_experts, blk, count_tok).transpose(1, 2, 0), "blk")
    grad_gates = dg_parts.transpose(1, 0, 2).reshape(count_tok, number)
    dx_sum = sum_scatter(dx_part, "blk")
    output = (mid + sum_scatter(out_part, "blk")).astype(BF16)
    router_probs = lax.dynamic_slice_in_dim(probs_blk, blk_at * count_tok, count_tok)
    chosen = lax.dynamic_slice_in_dim(chosen_blk, blk_at * count_tok, count_tok)
    grad_probs = chosen * grad_gates
    grad_logits = (
        router_probs * (grad_probs - jnp.sum(router_probs * grad_probs, axis=1, keepdims=True))
    ).astype(BF16)
    grad_hidden_two = dx_sum + dot_nt(grad_logits, whole_router)
    grad_router_part = dot_tn(hidden_two, grad_logits)
    grad_gain_ffn = jnp.sum(grad_hidden_two * normed_two, axis=0)
    grad_mid = own_grad.astype(F32) + norm_back(grad_hidden_two * gain_ffn, mid, scale_two)

    branch_grad = lax.all_gather(grad_mid.astype(BF16), "uly", axis=0, tiled=True)
    grad_attn = dot_nt(branch_grad, own_out).astype(BF16)
    grad_attn = to_heads(grad_attn.reshape(rows, local_heads, head_dim).transpose(1, 0, 2))
    grad_out_part = jnp.einsum("htc,td->hcd", attn_rows, branch_grad, preferred_element_type=F32)
    dq, dk, dv = attention_backward(
        q_src, kv_src, cols, grad_attn, attn_f32, lse, seg_q, seg_row, head_dim
    )
    if by_heads:
        dqkv = to_rows_back(jnp.concatenate([dq, dk, dv], axis=2))
        dq, dk, dv = jnp.split(dqkv, 3, axis=2)
    else:
        dk, dv = (lax.psum_scatter(g, "blk", scatter_dimension=1, tiled=True) for g in (dk, dv))
    dq, dk, dv = (g.transpose(1, 0, 2) for g in (dq, dk, dv))
    grad_query_norm = rotate(dq.astype(F32), cos_table, -sin_table)
    grad_key_norm = rotate(dk.astype(F32), cos_table, -sin_table)
    grad_gain_query = jnp.sum(grad_query_norm * (query_raw * query_scale), axis=(0, 1))
    grad_gain_key = jnp.sum(grad_key_norm * (key_raw * key_scale), axis=(0, 1))
    grad_projected = jnp.concatenate(
        [
            norm_back(grad_query_norm * gain_query, query_raw, query_scale)
            .reshape(rows, local_width)
            .astype(BF16),
            norm_back(grad_key_norm * gain_key, key_raw, key_scale)
            .reshape(rows, local_width)
            .astype(BF16),
            dv.reshape(rows, local_width),
        ],
        axis=1,
    )
    grad_hidden_part = dot_nt(grad_projected, own_qkv)
    grad_hidden_one = sum_scatter(grad_hidden_part, "uly")
    grad_gain_attn = jnp.sum(grad_hidden_part * normed_one, axis=0)
    grad_inputs = grad_mid + norm_back(grad_hidden_one * gain_attn, inputs, rms_scale(inputs))

    grad_qkv_part = dot_tn(hidden_one, grad_projected).astype(BF16)
    grad_qkv_rows = lax.psum_scatter(grad_qkv_part, ROWS, scatter_dimension=0, tiled=True)
    grad_qkv_rows = swap(grad_qkv_rows.reshape(uly, shard_rows, 3 * local_width), "uly")
    grad_qkv = (
        grad_qkv_rows.reshape(uly, shard_rows, 3, local_width)
        .transpose(1, 2, 0, 3)
        .reshape(shard_rows, 3 * width)
        .astype(F32)
    )
    grad_out_rows = lax.psum_scatter(
        grad_out_part.reshape(local_width, width).astype(BF16), ROWS, scatter_dimension=0, tiled=True
    )
    grad_out = lax.ppermute(grad_out_rows, ALL, [(b, a) for a, b in to_rows]).astype(F32)
    small = jnp.concatenate([grad_gain_attn[:, None], grad_gain_ffn[:, None], grad_router_part], axis=1)
    small = lax.psum_scatter(small, ALL, scatter_dimension=0, tiled=True)
    grad_qk_gain = lax.psum(jnp.stack([grad_gain_query, grad_gain_key]), ALL)

    clip_gamma = TAU / jnp.maximum(head_max, TAU)
    factor = jnp.repeat(jnp.sqrt(clip_gamma), head_dim)
    column_scale = jnp.concatenate([factor, factor, jnp.ones((width,), F32)])
    clipped = w_qkv.astype(F32) * column_scale[None, :]
    return (
        output[None],
        grad_inputs[None],
        grad_qkv,
        grad_out,
        small[:, 0],
        small[:, 1],
        grad_qk_gain,
        small[:, 2:],
        grad_gate_up,
        grad_down,
        clipped,
    )


def solution(mesh):
    in_specs = (
        P("batch", ("blk", "uly"), None),
        P("batch", None),
        P("batch", ("blk", "uly"), None),
        P(ALL, None),
        P(ALL, None),
        P(ALL),
        P(ALL),
        P(),
        P(ALL, None),
        P("blk", PLANE, None),
        P("blk", PLANE, None),
        P("batch", ("blk", "uly"), None),
    )
    out_specs = (
        P("batch", ("blk", "uly"), None),
        P("batch", ("blk", "uly"), None),
        P(ALL, None),
        P(ALL, None),
        P(ALL),
        P(ALL),
        P(),
        P(ALL, None),
        P("blk", PLANE, None),
        P("blk", PLANE, None),
        P(ALL, None),
    )
    return jax.shard_map(
        per_device, mesh=mesh, in_specs=in_specs, out_specs=out_specs, check_vma=False
    )
```

```python
import functools
import math

import jax
import jax.numpy as jnp
from jax import lax
from jax.experimental import pallas as pl
from jax.experimental.pallas import tpu as pltpu
from jax.sharding import PartitionSpec as P

EPS = 1e-06
THETA = 50000.0
TAU = 4.0
NEG = -1e30
LOG2E = 1.4426950408889634
LANES = 128
MOST_TOKENS = 512
VMEM_LIMIT = 60 * 1024 * 1024

ALL = ("batch", "blk", "uly")
ROWS = ("batch", "blk")
PLANE = ("batch", "uly")

MESH = pl.DeviceIdType.MESH
BF16 = jnp.bfloat16
F32 = jnp.float32


def rms_scale(values):
    return lax.rsqrt(jnp.mean(values * values, axis=-1, keepdims=True) + EPS)


def norm_back(grad_normed, values, scale):
    normed = values * scale
    return scale * (grad_normed - normed * jnp.mean(grad_normed * normed, axis=-1, keepdims=True))


def rope_tables(offset, length, head_dim):
    half_dim = head_dim // 2
    frequency = THETA ** (-jnp.arange(half_dim, dtype=F32) * 2.0 / head_dim)
    positions = (offset + jnp.arange(length, dtype=jnp.int32)).astype(F32)
    angles = positions[:, None] * frequency[None, :]
    return (jnp.cos(angles)[:, None, :], jnp.sin(angles)[:, None, :])


def rotate(values, cos_table, sin_table):
    half_dim = values.shape[-1] // 2
    first = values[..., :half_dim]
    second = values[..., half_dim:]
    return jnp.concatenate(
        [first * cos_table - second * sin_table, second * cos_table + first * sin_table], axis=-1
    )


def dot_nn(a, b):
    return lax.dot_general(a, b, (((1,), (0,)), ((), ())), preferred_element_type=F32)


def dot_nt(a, b):
    return lax.dot_general(a, b, (((1,), (1,)), ((), ())), preferred_element_type=F32)


def dot_tn(a, b):
    return lax.dot_general(a, b, (((0,), (0,)), ((), ())), preferred_element_type=F32)


def key_chunks(length):
    size = min(512, length)
    return size, length // size


def attn_fwd_kernel(factor, q_ref, k_ref, v_ref, sq_ref, sk_ref, o_ref, of_ref, lse_ref, top_ref, vt_ref):
    length = k_ref.shape[1]
    size, count = key_chunks(length)
    tile, head_dim = q_ref.shape[1:]

    @pl.when(pl.program_id(1) == 0)
    def _():
        vt_ref[...] = v_ref[0].astype(F32).T.astype(BF16)

    q = q_ref[0]
    seg_q = sq_ref[...]

    def step(j, carried):
        total, top, acc = carried
        at = pl.multiple_of(j * size, size)
        scores = dot_nt(k_ref[0, pl.ds(at, size), :], q)
        scores = jnp.where(sk_ref[pl.ds(at, size), :] == seg_q, scores, NEG)
        top = jnp.maximum(top, jnp.max(scores, axis=0, keepdims=True))
        weights = jnp.exp2(scores * factor)
        total = total + jnp.sum(weights, axis=0, keepdims=True)
        acc = acc + dot_nn(vt_ref[:, pl.ds(at, size)], weights.astype(BF16))
        return total, top, acc

    start = (
        jnp.zeros((1, tile), F32),
        jnp.full((1, tile), NEG, F32),
        jnp.zeros((head_dim, tile), F32),
    )
    total, top, acc = lax.fori_loop(0, count, step, start, unroll=count <= 4)
    out = (acc * (1.0 / total)).T
    o_ref[0] = out.astype(BF16)
    of_ref[0] = out
    lse_ref[0] = jnp.log2(total)
    top_ref[0] = top


def attn_bwd_kernel(
    factor, scale, q_ref, k_ref, v_ref, do_ref, of_ref, lse_ref, sq_ref, sk_ref,
    dq_ref, dk_ref, dv_ref, kt_ref, dk_acc, dv_acc,
):
    length = k_ref.shape[1]
    size, count = key_chunks(length)
    tile, head_dim = q_ref.shape[1:]

    @pl.when(pl.program_id(1) == 0)
    def _():
        kt_ref[...] = k_ref[0].astype(F32).T.astype(BF16)
        dk_acc[...] = jnp.zeros_like(dk_acc)
        dv_acc[...] = jnp.zeros_like(dv_acc)

    q = q_ref[0]
    grad = do_ref[0]
    seg_q = sq_ref[...]
    lse = lse_ref[0]
    row_dot = jnp.sum((grad.astype(F32) * of_ref[0]).T, axis=0, keepdims=True)

    def step(j, dq_t):
        at = pl.multiple_of(j * size, size)
        rows = pl.ds(at, size)
        scores = dot_nt(k_ref[0, rows, :], q)
        scores = jnp.where(sk_ref[rows, :] == seg_q, scores, NEG)
        weights = jnp.exp2(scores * factor - lse)
        grad_weights = dot_nt(v_ref[0, rows, :], grad)
        grad_scores = (weights * (grad_weights - row_dot)).astype(BF16)
        dk_acc[rows, :] += dot_nn(grad_scores, q)
        dv_acc[rows, :] += dot_nn(weights.astype(BF16), grad)
        return dq_t + dot_nn(kt_ref[:, rows], grad_scores)

    dq_t = lax.fori_loop(0, count, step, jnp.zeros((head_dim, tile), F32), unroll=count <= 4)
    dq_ref[0] = (dq_t * scale).T.astype(BF16)

    @pl.when(pl.program_id(1) == pl.num_programs(1) - 1)
    def _():
        dk_ref[0] = (dk_acc[...] * scale).astype(BF16)
        dv_ref[0] = dv_acc[...].astype(BF16)


def attention_tile(queries, length):
    return min(queries, 256 if length <= 4096 else 128)


def attention_forward(q_src, kv_src, cols, seg_q, seg_k, head_dim):
    heads, queries = q_src.shape[:2]
    length = kv_src.shape[1]
    tile = attention_tile(queries, length)
    q_col, k_col, v_col = cols
    factor = head_dim**-0.5 * LOG2E
    row = pl.BlockSpec((1, 1, tile), lambda h, i: (h, 0, i))
    block = pl.BlockSpec((1, tile, head_dim), lambda h, i: (h, i, 0))
    return pl.pallas_call(
        functools.partial(attn_fwd_kernel, factor),
        grid=(heads, queries // tile),
        in_specs=[
            pl.BlockSpec((1, tile, head_dim), lambda h, i: (h, i, q_col)),
            pl.BlockSpec((1, length, head_dim), lambda h, i: (h, 0, k_col)),
            pl.BlockSpec((1, length, head_dim), lambda h, i: (h, 0, v_col)),
            pl.BlockSpec((1, tile), lambda h, i: (0, i)),
            pl.BlockSpec((length, 1), lambda h, i: (0, 0)),
        ],
        out_specs=[block, block, row, row],
        out_shape=[
            jax.ShapeDtypeStruct((heads, queries, head_dim), BF16),
            jax.ShapeDtypeStruct((heads, queries, head_dim), F32),
            jax.ShapeDtypeStruct((heads, 1, queries), F32),
            jax.ShapeDtypeStruct((heads, 1, queries), F32),
        ],
        scratch_shapes=[pltpu.VMEM((head_dim, length), BF16)],
        compiler_params=pltpu.CompilerParams(vmem_limit_bytes=VMEM_LIMIT),
        cost_estimate=pl.CostEstimate(
            flops=4 * heads * queries * length * head_dim,
            bytes_accessed=heads * (queries + length) * head_dim * 8,
            transcendentals=heads * queries * length,
        ),
        name="attend",
    )(q_src, kv_src, kv_src, seg_q.reshape(1, -1), seg_k.reshape(-1, 1))


def attention_backward(q_src, kv_src, cols, grad, out_f32, lse, seg_q, seg_k, head_dim):
    heads, queries = q_src.shape[:2]
    length = kv_src.shape[1]
    tile = attention_tile(queries, length)
    q_col, k_col, v_col = cols
    scale = head_dim**-0.5
    row = pl.BlockSpec((1, 1, tile), lambda h, i: (h, 0, i))
    block = pl.BlockSpec((1, tile, head_dim), lambda h, i: (h, i, 0))
    whole = pl.BlockSpec((1, length, head_dim), lambda h, i: (h, 0, 0))
    return pl.pallas_call(
        functools.partial(attn_bwd_kernel, scale * LOG2E, scale),
        grid=(heads, queries // tile),
        in_specs=[
            pl.BlockSpec((1, tile, head_dim), lambda h, i: (h, i, q_col)),
            pl.BlockSpec((1, length, head_dim), lambda h, i: (h, 0, k_col)),
            pl.BlockSpec((1, length, head_dim), lambda h, i: (h, 0, v_col)),
            block,
            block,
            row,
            pl.BlockSpec((1, tile), lambda h, i: (0, i)),
            pl.BlockSpec((length, 1), lambda h, i: (0, 0)),
        ],
        out_specs=[block, whole, whole],
        out_shape=[
            jax.ShapeDtypeStruct((heads, queries, head_dim), BF16),
            jax.ShapeDtypeStruct((heads, length, head_dim), BF16),
            jax.ShapeDtypeStruct((heads, length, head_dim), BF16),
        ],
        scratch_shapes=[
            pltpu.VMEM((head_dim, length), BF16),
            pltpu.VMEM((length, head_dim), F32),
            pltpu.VMEM((length, head_dim), F32),
        ],
        compiler_params=pltpu.CompilerParams(vmem_limit_bytes=VMEM_LIMIT),
        cost_estimate=pl.CostEstimate(
            flops=10 * heads * queries * length * head_dim,
            bytes_accessed=heads * (queries + length) * head_dim * 12,
            transcendentals=heads * queries * length,
        ),
        name="attend_back",
    )(q_src, kv_src, kv_src, grad, out_f32, lse, seg_q.reshape(1, -1), seg_k.reshape(-1, 1))


def expert_kernel(
    h_ref, ht_ref, dy_ref, dyt_ref, gate_ref, wg_ref, wu_ref, wd_ref,
    out_ref, dx_ref, dg_ref, gr_ref, out_acc, dx_acc,
):
    chunk = pl.program_id(0)
    width = h_ref.shape[1]
    parts, part_rows, cols = wg_ref.shape

    @pl.when(chunk == 0)
    def _():
        out_acc[...] = jnp.zeros_like(out_acc)
        dx_acc[...] = jnp.zeros_like(dx_acc)
        dg_ref[...] = jnp.zeros_like(dg_ref)

    w_gate = wg_ref[...].reshape(width, cols)
    w_up = wu_ref[...].reshape(width, cols)
    w_down = wd_ref[...].reshape(width, cols)
    gate = gate_ref[...]
    a_gate = dot_nn(h_ref[...], w_gate)
    a_up = dot_nn(h_ref[...], w_up)
    raw = dot_nn(dy_ref[...], w_down)
    sigma = 1.0 / (1.0 + jnp.exp2(a_gate * -LOG2E))
    swish = a_gate * sigma
    act = swish * a_up
    dg_ref[...] += jnp.sum(raw * act, axis=1, keepdims=True)
    gated = (gate * act).astype(BF16)
    d_act = gate * raw
    d_gate = (d_act * a_up * (sigma + swish * (1.0 - sigma))).astype(BF16)
    d_up = (d_act * swish).astype(BF16)
    out_acc[...] += dot_nt(gated, w_down)
    dx_acc[...] += dot_nt(d_gate, w_gate) + dot_nt(d_up, w_up)
    gr_ref[:, 0] = dot_nn(ht_ref[...], d_gate).astype(BF16).reshape(parts, part_rows, cols)
    gr_ref[:, 1] = dot_nn(ht_ref[...], d_up).astype(BF16).reshape(parts, part_rows, cols)
    gr_ref[:, 2] = dot_nn(dyt_ref[...], gated).astype(BF16).reshape(parts, part_rows, cols)

    @pl.when(chunk == pl.num_programs(0) - 1)
    def _():
        out_ref[...] = out_acc[...].astype(BF16)
        dx_ref[...] = dx_acc[...].astype(BF16)


def one_expert(hidden, hidden_t, grad, grad_t, gate, gate_up, down):
    tokens, width = hidden.shape
    parts, part_rows, units = down.shape
    cols = min(256, units)
    chunks = units // cols
    once = pl.Buffered(1)
    whole = pl.BlockSpec((tokens, width), lambda f: (0, 0), pipeline_mode=once)
    whole_t = pl.BlockSpec((width, tokens), lambda f: (0, 0), pipeline_mode=once)
    column = pl.BlockSpec((tokens, 1), lambda f: (0, 0))
    result = pl.BlockSpec((tokens, width), lambda f: (0, 0))
    weight = (parts, part_rows, cols)
    return pl.pallas_call(
        expert_kernel,
        grid=(chunks,),
        in_specs=[
            whole,
            whole_t,
            whole,
            whole_t,
            column,
            pl.BlockSpec(weight, lambda f: (0, 0, f)),
            pl.BlockSpec(weight, lambda f: (0, 0, chunks + f)),
            pl.BlockSpec(weight, lambda f: (0, 0, f)),
        ],
        out_specs=[
            result,
            result,
            column,
            pl.BlockSpec((parts, 3, part_rows, cols), lambda f: (0, 0, 0, f)),
        ],
        out_shape=[
            jax.ShapeDtypeStruct((tokens, width), BF16),
            jax.ShapeDtypeStruct((tokens, width), BF16),
            jax.ShapeDtypeStruct((tokens, 1), F32),
            jax.ShapeDtypeStruct((parts, 3, part_rows, units), BF16),
        ],
        scratch_shapes=[
            pltpu.VMEM((tokens, width), F32),
            pltpu.VMEM((tokens, width), F32),
        ],
        compiler_params=pltpu.CompilerParams(vmem_limit_bytes=VMEM_LIMIT),
        cost_estimate=pl.CostEstimate(
            flops=18 * tokens * width * units,
            bytes_accessed=12 * width * units,
            transcendentals=tokens * units,
        ),
        name="expert",
    )(hidden, hidden_t, grad, grad_t, gate, gate_up, gate_up, down)


def swap(values, axis):
    return lax.all_to_all(values, axis, split_axis=0, concat_axis=0, tiled=True)


def sum_scatter(values, axis):
    count = lax.axis_size(axis)
    rows, width = values.shape
    parts = swap(values.astype(BF16).reshape(count, rows // count, width), axis)
    return jnp.sum(parts.astype(F32), axis=0)


def place(axes, index):
    found = {}
    for axis in reversed(axes):
        size = lax.axis_size(axis)
        found[axis] = lax.rem(index, size)
        index = index // size
    return found


def spread(axes):
    return math.prod(lax.axis_size(axis) for axis in axes)


def each(count, body):
    if count <= 4:
        for step in range(1, count):
            body(step)
    else:

        def looped(step, carried):
            body(step)
            return carried

        lax.fori_loop(1, count, looped, 0)


def ahead(index, step, size):
    return lax.rem(index + step, size)


def exchange(items, collective_id, after=()):
    count = len(items)
    sizes = [spread(axes) for _, axes, _ in items]
    groups = list(dict.fromkeys(axes for _, axes, _ in items))
    bases = [sum(sizes[:i]) for i in range(count)]

    def kernel(*refs):
        ins = refs[:count]
        outs = refs[count + len(after) : 2 * count + len(after)]
        send, recv, local = refs[-3:]
        barrier = pltpu.get_barrier_semaphore()
        for axes in groups:
            size, me = spread(axes), lax.axis_index(axes)

            def greet(step, axes=axes, size=size, me=me):
                pl.semaphore_signal(
                    barrier, inc=1, device_id=place(axes, ahead(me, step, size)), device_id_type=MESH
                )

            each(size, greet)
        pl.semaphore_wait(barrier, sum(spread(axes) - 1 for axes in groups))

        def remote(i, step):
            _, axes, kind = items[i]
            me = lax.axis_index(axes)
            peer = ahead(me, step, sizes[i])
            return pltpu.make_async_remote_copy(
                src_ref=ins[i] if kind == "gather" else ins[i].at[peer],
                dst_ref=outs[i].at[me],
                send_sem=send.at[bases[i] + step],
                recv_sem=recv.at[bases[i] + step],
                device_id=place(axes, peer),
                device_id_type=MESH,
            )

        def own(i):
            _, axes, kind = items[i]
            me = lax.axis_index(axes)
            return pltpu.make_async_copy(
                ins[i] if kind == "gather" else ins[i].at[me], outs[i].at[me], local.at[i]
            )

        for i in range(count):
            each(sizes[i], lambda step, i=i: remote(i, step).start())
        for i in range(count):
            own(i).start()
        for i in range(count):
            own(i).wait()
        for i in range(count):
            each(sizes[i], lambda step, i=i: remote(i, step).wait())

    shapes = [
        (size, *(array.shape if kind == "gather" else array.shape[1:]))
        for size, (array, _, kind) in zip(sizes, items)
    ]
    anywhere = pl.BlockSpec(memory_space=pl.ANY)
    return pl.pallas_call(
        kernel,
        in_specs=[anywhere] * (count + len(after)),
        out_specs=[anywhere] * count,
        out_shape=[jax.ShapeDtypeStruct(shape, item[0].dtype) for shape, item in zip(shapes, items)],
        scratch_shapes=[
            pltpu.SemaphoreType.DMA((sum(sizes),)),
            pltpu.SemaphoreType.DMA((sum(sizes),)),
            pltpu.SemaphoreType.DMA((count,)),
        ],
        compiler_params=pltpu.CompilerParams(collective_id=collective_id, has_side_effects=True),
        name="exchange",
    )(*[item[0] for item in items], *after)


def startup_kernel(
    head_ref, extra_ref, tok_ref, out_ref, heads_ref, extras_ref, toks_ref, outs_ref,
    head_send, head_recv, extra_send, extra_recv, out_send, out_recv,
    z_send, z_recv, y_send, y_recv, c_send, c_recv, local,
):
    batch, blk, uly = (lax.axis_size(axis) for axis in ALL)
    b, z, u = (lax.axis_index(axis) for axis in ALL)
    total, group = batch * blk * uly, batch * blk
    me = lax.axis_index(ALL)
    far = lax.rem(u + 2, uly)
    near = u + 1 - 2 * lax.rem(u, 2)

    barrier = pltpu.get_barrier_semaphore()

    def greet(step):
        pl.semaphore_signal(
            barrier, inc=1, device_id=place(ALL, ahead(me, step, total)), device_id_type=MESH
        )

    each(total, greet)
    pl.semaphore_wait(barrier, total - 1)

    def send(src, dst, sent, got, to):
        return pltpu.make_async_remote_copy(
            src_ref=src, dst_ref=dst, send_sem=sent, recv_sem=got, device_id=to, device_id_type=MESH
        )

    def along_z(step):
        to = (b, ahead(z, step, blk), u)
        return send(tok_ref, toks_ref.at[z, u], z_send.at[step], z_recv.at[step], to)

    def along_y(step):
        at = ahead(z, step, blk)
        src = tok_ref if step == 0 else toks_ref.at[at, u]
        return send(src, toks_ref.at[at, u], y_send.at[step], y_recv.at[step], (b, z, far))

    def to_near(step, place_from):
        at = ahead(z, step, blk)
        if place_from == 0:
            src = tok_ref if step == 0 else toks_ref.at[at, u]
            dst = toks_ref.at[at, u]
        else:
            src = dst = toks_ref.at[at, far]
        sem = 2 * step + place_from
        return send(src, dst, c_send.at[sem], c_recv.at[sem], (b, z, near))

    def head(step):
        to = place(ALL, ahead(me, step, total))
        src = head_ref.at[to["uly"] * blk + to["blk"]]
        return send(src, heads_ref.at[me], head_send.at[step], head_recv.at[step], to)

    def extra(step):
        to = place(ALL, ahead(me, step, total))
        return send(extra_ref, extras_ref.at[me], extra_send.at[step], extra_recv.at[step], to)

    keeper = me // group
    slot = lax.rem(me, group)

    def out_to(j):
        to = (j // blk, j % blk, keeper)
        return send(out_ref, outs_ref.at[slot], out_send.at[j], out_recv.at[slot], to)

    def out_from(j):
        sender = place(ALL, u * group + j)
        return send(out_ref, outs_ref.at[j], out_send.at[j], out_recv.at[j], sender)

    def out_is_own(j):
        return (keeper == u) & (b * blk + z == j)

    own = [
        pltpu.make_async_copy(tok_ref, toks_ref.at[z, u], local.at[0]),
        pltpu.make_async_copy(head_ref.at[u * blk + z], heads_ref.at[me], local.at[1]),
        pltpu.make_async_copy(extra_ref, extras_ref.at[me], local.at[2]),
    ]
    own_out = pltpu.make_async_copy(out_ref, outs_ref.at[slot], local.at[3])

    for step in range(1, blk):
        along_z(step).start()
    along_y(0).start()
    to_near(0, 0).start()

    def start_head(step):
        extra(step).start()
        head(step).start()

    each(total, start_head)
    for copy in own:
        copy.start()

    @pl.when(keeper == u)
    def _():
        own_out.start()

    for j in range(group):

        @pl.when(jnp.logical_not(out_is_own(j)))
        def _(j=j):
            out_to(j).start()

    for step in range(1, blk):
        along_z(step).wait_recv()
        along_y(blk - step).start()
        to_near(blk - step, 0).start()
    for step in [0, *reversed(range(1, blk))]:
        along_y(step).wait_recv()
        to_near(step, 1).start()
    for step in range(blk):
        to_near(step, 0).wait_recv()
        to_near(step, 1).wait_recv()

    def wait_head(step):
        extra(step).wait()
        head(step).wait()

    each(total, wait_head)
    for j in range(group):

        @pl.when(u * group + j != me)
        def _(j=j):
            out_from(j).wait_recv()

        @pl.when(jnp.logical_not(out_is_own(j)))
        def _(j=j):
            out_to(j).wait_send()

    @pl.when(keeper == u)
    def _():
        own_out.wait()

    for copy in own:
        copy.wait()
    for step in range(1, blk):
        along_z(step).wait_send()
    for step in range(blk):
        along_y(step).wait_send()
        to_near(step, 0).wait_send()
        to_near(step, 1).wait_send()


def startup(heads, extra, tok, out_rows, collective_id):
    batch, blk, uly = (lax.axis_size(axis) for axis in ALL)
    total, group = batch * blk * uly, batch * blk
    anywhere = pl.BlockSpec(memory_space=pl.ANY)
    dma = pltpu.SemaphoreType.DMA
    return pl.pallas_call(
        startup_kernel,
        in_specs=[anywhere] * 4,
        out_specs=[anywhere] * 4,
        out_shape=[
            jax.ShapeDtypeStruct((total, *heads.shape[1:]), BF16),
            jax.ShapeDtypeStruct((total, *extra.shape), BF16),
            jax.ShapeDtypeStruct((blk, uly, *tok.shape), BF16),
            jax.ShapeDtypeStruct((group, *out_rows.shape), BF16),
        ],
        scratch_shapes=[
            *[dma((total,))] * 4,
            *[dma((group,))] * 2,
            *[dma((blk,))] * 4,
            *[dma((2 * blk,))] * 2,
            dma((4,)),
        ],
        compiler_params=pltpu.CompilerParams(collective_id=collective_id, has_side_effects=True),
        name="startup",
    )(heads, extra, tok, out_rows)


def per_device_general(
    tokens, segments, routes, w_qkv, w_out, attn_gain, ffn_gain, qk_gain, router, w_gate_up, w_down, cotangent
):
    own_tokens = tokens[0]
    own_grad = cotangent[0]
    count_tok, width = own_tokens.shape
    head_dim = qk_gain.shape[1]
    heads = width // head_dim
    uly, blk, batch = lax.axis_size("uly"), lax.axis_size("blk"), lax.axis_size("batch")
    blk_at, uly_at = lax.axis_index("blk"), lax.axis_index("uly")
    group = batch * blk
    local_heads = heads // uly
    local_width = local_heads * head_dim
    rows = count_tok * uly
    seg_row = segments[0]
    length = seg_row.shape[0]
    number = router.shape[1]
    local_experts, _, units = w_down.shape
    shard_rows = w_qkv.shape[0]

    extra = jnp.concatenate([attn_gain[:, None], ffn_gain[:, None], router], axis=1)
    extra = jnp.pad(extra, ((0, 0), (0, LANES - extra.shape[1])))
    columns = w_qkv.reshape(shard_rows, 3, uly, local_width).transpose(2, 0, 1, 3)
    packed = jnp.concatenate(
        [
            columns.reshape(uly, shard_rows, 3 * local_width),
            jnp.broadcast_to(extra[None], (uly, shard_rows, LANES)),
        ],
        axis=2,
    )
    packed = swap(packed, "uly").reshape(uly * shard_rows, 3 * local_width + LANES)
    packed = lax.all_gather(packed, ROWS, axis=0, tiled=True)
    own_qkv = packed[:, : 3 * local_width]
    gain_attn = packed[:, 3 * local_width].astype(F32)
    gain_ffn = packed[:, 3 * local_width + 1].astype(F32)
    whole_router = packed[:, 3 * local_width + 2 : 3 * local_width + 2 + number]
    tokens_all = lax.all_gather(own_tokens, "uly", axis=0, tiled=True)
    to_rows = [(u * group + g, g * uly + u) for g in range(group) for u in range(uly)]
    own_out = lax.all_gather(lax.ppermute(w_out, ALL, to_rows), ROWS, axis=0, tiled=True)
    whole_gate_up = lax.all_gather(w_gate_up, PLANE, axis=0, tiled=False)
    whole_down = lax.all_gather(w_down, PLANE, axis=0, tiled=False)
    grad_blk = lax.all_gather(own_grad, "blk", axis=0, tiled=True)
    routes_blk = lax.all_gather(routes[0], "blk", axis=0, tiled=True)

    gain_query = qk_gain[0].astype(F32)
    gain_key = qk_gain[1].astype(F32)
    inputs_all = tokens_all.astype(F32)
    normed_one = inputs_all * rms_scale(inputs_all)
    hidden_one = (normed_one * gain_attn).astype(BF16)
    projected = dot_nn(hidden_one, own_qkv)
    query_raw = projected[:, :local_width].reshape(rows, local_heads, head_dim)
    key_raw = projected[:, local_width : 2 * local_width].reshape(rows, local_heads, head_dim)
    value_raw = projected[:, 2 * local_width :].reshape(rows, local_heads, head_dim)
    cos_table, sin_table = rope_tables(blk_at * rows, rows, head_dim)
    query_scale = rms_scale(query_raw)
    key_scale = rms_scale(key_raw)
    qkv = jnp.concatenate(
        [
            rotate(query_raw * query_scale * gain_query, cos_table, sin_table),
            rotate(key_raw * key_scale * gain_key, cos_table, sin_table),
            value_raw,
        ],
        axis=2,
    ).astype(BF16)
    qkv = qkv.transpose(1, 0, 2)

    by_heads = local_heads % blk == 0
    if by_heads:
        per = local_heads // blk

        def to_heads(values):
            columns = values.shape[2]
            moved = swap(values.reshape(blk, per, rows, columns), "blk")
            return moved.transpose(1, 0, 2, 3).reshape(per, length, columns)

        def to_rows_back(values):
            columns = values.shape[2]
            parts = values.reshape(per, blk, rows, columns).transpose(1, 0, 2, 3)
            return swap(parts, "blk").reshape(local_heads, rows, columns)

        q_src = kv_src = to_heads(qkv)
        cols = (0, 1, 2)
        seg_q = seg_row
        first_head = uly_at * local_heads + blk_at * per
    else:

        def to_heads(values):
            return values

        def to_rows_back(values):
            return values

        q_src = qkv
        kv_src = lax.all_gather(qkv[:, :, head_dim:], "blk", axis=1, tiled=True)
        cols = (0, 0, 1)
        seg_q = lax.dynamic_slice_in_dim(seg_row, blk_at * rows, rows)
        first_head = uly_at * local_heads
    attn_low, attn_f32, lse, top = attention_forward(q_src, kv_src, cols, seg_q, seg_row, head_dim)
    head_vector = lax.dynamic_update_slice_in_dim(
        jnp.full((heads,), NEG, F32), jnp.max(top, axis=(1, 2)) * head_dim**-0.5, first_head, 0
    )
    head_max = lax.pmax(head_vector, ALL)
    attn_rows = to_rows_back(attn_low)
    out_heads = own_out.reshape(local_heads, head_dim, width)
    branch = jnp.einsum("htc,hcd->td", attn_rows, out_heads, preferred_element_type=F32)
    inputs = own_tokens.astype(F32)
    mid = inputs + sum_scatter(branch, "uly")

    scale_two = rms_scale(mid)
    normed_two = mid * scale_two
    hidden_two = (normed_two * gain_ffn).astype(BF16)
    hidden_blk = lax.all_gather(hidden_two, "blk", axis=0, tiled=True)
    probs_blk = jax.nn.softmax(dot_nn(hidden_blk, whole_router), axis=1)
    names = jnp.arange(number, dtype=jnp.int32)
    chosen_blk = jnp.any(routes_blk[:, :, None] == names, axis=1).astype(F32)
    own_names = blk_at * local_experts
    gates = lax.dynamic_slice_in_dim(probs_blk * chosen_blk, own_names, local_experts, axis=1)
    gate_columns = gates.T[:, :, None]
    most = min(MOST_TOKENS, hidden_blk.shape[0])
    made = [
        [
            one_expert(
                hidden_blk[at : at + most],
                hidden_blk[at : at + most].T,
                grad_blk[at : at + most],
                grad_blk[at : at + most].T,
                gate_columns[e, at : at + most],
                whole_gate_up[:, e],
                whole_down[:, e],
            )
            for e in range(local_experts)
        ]
        for at in range(0, hidden_blk.shape[0], most)
    ]
    out_part = jnp.concatenate([sum(m[0].astype(F32) for m in group) for group in made], axis=0)
    dx_part = jnp.concatenate([sum(m[1].astype(F32) for m in group) for group in made], axis=0)
    dg_part = jnp.concatenate([jnp.stack([m[2] for m in group]) for group in made], axis=1)
    expert_grads = jnp.stack(
        [
            sum(group[e][3].astype(F32) for group in made).astype(BF16)
            for e in range(local_experts)
        ],
        axis=2,
    )
    expert_sums = lax.psum_scatter(expert_grads, PLANE, scatter_dimension=0, tiled=False).astype(F32)
    grad_gate_up = jnp.concatenate([expert_sums[0], expert_sums[1]], axis=2)
    grad_down = expert_sums[2]
    dg_parts = swap(dg_part.reshape(local_experts, blk, count_tok).transpose(1, 2, 0), "blk")
    grad_gates = dg_parts.transpose(1, 0, 2).reshape(count_tok, number)
    dx_sum = sum_scatter(dx_part, "blk")
    output = (mid + sum_scatter(out_part, "blk")).astype(BF16)
    router_probs = lax.dynamic_slice_in_dim(probs_blk, blk_at * count_tok, count_tok)
    chosen = lax.dynamic_slice_in_dim(chosen_blk, blk_at * count_tok, count_tok)
    grad_probs = chosen * grad_gates
    grad_logits = (
        router_probs * (grad_probs - jnp.sum(router_probs * grad_probs, axis=1, keepdims=True))
    ).astype(BF16)
    grad_hidden_two = dx_sum + dot_nt(grad_logits, whole_router)
    grad_router_part = dot_tn(hidden_two, grad_logits)
    grad_gain_ffn = jnp.sum(grad_hidden_two * normed_two, axis=0)
    grad_mid = own_grad.astype(F32) + norm_back(grad_hidden_two * gain_ffn, mid, scale_two)

    branch_grad = lax.all_gather(grad_mid.astype(BF16), "uly", axis=0, tiled=True)
    grad_attn = dot_nt(branch_grad, own_out).astype(BF16)
    grad_attn = to_heads(grad_attn.reshape(rows, local_heads, head_dim).transpose(1, 0, 2))
    grad_out_part = jnp.einsum("htc,td->hcd", attn_rows, branch_grad, preferred_element_type=F32)
    dq, dk, dv = attention_backward(
        q_src, kv_src, cols, grad_attn, attn_f32, lse, seg_q, seg_row, head_dim
    )
    if by_heads:
        dqkv = to_rows_back(jnp.concatenate([dq, dk, dv], axis=2))
        dq, dk, dv = jnp.split(dqkv, 3, axis=2)
    else:
        dk, dv = (lax.psum_scatter(g, "blk", scatter_dimension=1, tiled=True) for g in (dk, dv))
    dq, dk, dv = (g.transpose(1, 0, 2) for g in (dq, dk, dv))
    grad_query_norm = rotate(dq.astype(F32), cos_table, -sin_table)
    grad_key_norm = rotate(dk.astype(F32), cos_table, -sin_table)
    grad_gain_query = jnp.sum(grad_query_norm * (query_raw * query_scale), axis=(0, 1))
    grad_gain_key = jnp.sum(grad_key_norm * (key_raw * key_scale), axis=(0, 1))
    grad_projected = jnp.concatenate(
        [
            norm_back(grad_query_norm * gain_query, query_raw, query_scale)
            .reshape(rows, local_width)
            .astype(BF16),
            norm_back(grad_key_norm * gain_key, key_raw, key_scale)
            .reshape(rows, local_width)
            .astype(BF16),
            dv.reshape(rows, local_width),
        ],
        axis=1,
    )
    grad_hidden_part = dot_nt(grad_projected, own_qkv)
    grad_hidden_one = sum_scatter(grad_hidden_part, "uly")
    grad_gain_attn = jnp.sum(grad_hidden_part * normed_one, axis=0)
    grad_inputs = grad_mid + norm_back(grad_hidden_one * gain_attn, inputs, rms_scale(inputs))

    grad_qkv_part = dot_tn(hidden_one, grad_projected).astype(BF16)
    grad_qkv_rows = lax.psum_scatter(grad_qkv_part, ROWS, scatter_dimension=0, tiled=True)
    grad_qkv_rows = swap(grad_qkv_rows.reshape(uly, shard_rows, 3 * local_width), "uly")
    grad_qkv = (
        grad_qkv_rows.reshape(uly, shard_rows, 3, local_width)
        .transpose(1, 2, 0, 3)
        .reshape(shard_rows, 3 * width)
        .astype(F32)
    )
    grad_out_rows = lax.psum_scatter(
        grad_out_part.reshape(local_width, width).astype(BF16), ROWS, scatter_dimension=0, tiled=True
    )
    grad_out = lax.ppermute(grad_out_rows, ALL, [(b, a) for a, b in to_rows]).astype(F32)
    small = jnp.concatenate([grad_gain_attn[:, None], grad_gain_ffn[:, None], grad_router_part], axis=1)
    small = lax.psum_scatter(small, ALL, scatter_dimension=0, tiled=True)
    grad_qk_gain = lax.psum(jnp.stack([grad_gain_query, grad_gain_key]), ALL)

    clip_gamma = TAU / jnp.maximum(head_max, TAU)
    factor = jnp.repeat(jnp.sqrt(clip_gamma), head_dim)
    column_scale = jnp.concatenate([factor, factor, jnp.ones((width,), F32)])
    clipped = w_qkv.astype(F32) * column_scale[None, :]
    return (
        output[None],
        grad_inputs[None],
        grad_qkv,
        grad_out,
        small[:, 0],
        small[:, 1],
        grad_qk_gain,
        small[:, 2:],
        grad_gate_up,
        grad_down,
        clipped,
    )


def per_device(
    tokens, segments, routes, w_qkv, w_out, attn_gain, ffn_gain, qk_gain, router, w_gate_up, w_down, cotangent
):
    own_tokens = tokens[0]
    own_grad = cotangent[0]
    count_tok, width = own_tokens.shape
    head_dim = qk_gain.shape[1]
    heads = width // head_dim
    batch, blk, uly = (lax.axis_size(axis) for axis in ALL)
    total, group = batch * blk * uly, batch * blk
    if uly != 4 or heads != blk * uly:
        return per_device_general(
            tokens, segments, routes, w_qkv, w_out, attn_gain, ffn_gain, qk_gain, router, w_gate_up, w_down, cotangent
        )
    blk_at, uly_at = lax.axis_index("blk"), lax.axis_index("uly")
    rows = count_tok * uly
    seg_row = segments[0]
    length = seg_row.shape[0]
    number = router.shape[1]
    local_experts, _, units = w_down.shape
    shard_rows = w_qkv.shape[0]

    extra = jnp.concatenate([attn_gain[None], ffn_gain[None], router.T], axis=0)
    kept = extra.shape[0]
    extra = jnp.pad(extra, ((0, -kept % 16), (0, -shard_rows % LANES)))
    by_head = w_qkv.reshape(shard_rows, 3, heads, head_dim).transpose(2, 0, 1, 3)
    own_qkv, extras, toks, own_out = startup(
        by_head.reshape(heads, shard_rows, 3 * head_dim), extra, own_tokens, w_out, 0
    )
    own_qkv = own_qkv.reshape(width, 3 * head_dim)
    own_out = own_out.reshape(blk, head_dim, width)
    extras = extras[:, :kept, :shard_rows].transpose(1, 0, 2).reshape(kept, width)
    gain_attn = extras[0].astype(F32)
    gain_ffn = extras[1].astype(F32)
    router_t = extras[2:]
    whole_gate_up = [
        lax.all_gather(w_gate_up[e], PLANE, axis=0, tiled=False) for e in range(local_experts)
    ]
    whole_down = [lax.all_gather(w_down[e], PLANE, axis=0, tiled=False) for e in range(local_experts)]

    gain_query = qk_gain[0].astype(F32)
    gain_key = qk_gain[1].astype(F32)
    inputs_all = toks.reshape(length, width).astype(F32)
    hidden_one = (inputs_all * rms_scale(inputs_all) * gain_attn).astype(BF16)
    projected = dot_nn(hidden_one, own_qkv)
    query_raw = projected[:, :head_dim]
    key_raw = projected[:, head_dim : 2 * head_dim]
    cos_table, sin_table = (table[:, 0] for table in rope_tables(0, length, head_dim))
    query_scale = rms_scale(query_raw)
    key_scale = rms_scale(key_raw)
    qkv = jnp.concatenate(
        [
            rotate(query_raw * query_scale * gain_query, cos_table, sin_table),
            rotate(key_raw * key_scale * gain_key, cos_table, sin_table),
            projected[:, 2 * head_dim :],
        ],
        axis=1,
    ).astype(BF16)[None]
    cols = (0, 1, 2)
    attn_low, attn_f32, lse, top = attention_forward(qkv, qkv, cols, seg_row, seg_row, head_dim)
    (attn_rows,) = exchange([(attn_low.reshape(blk, rows, head_dim), ("blk",), "swap")], 1)
    branch = jnp.einsum("htc,hcd->td", attn_rows, own_out, preferred_element_type=F32)
    branch, grad_blk, routes_blk = exchange(
        [
            (branch.astype(BF16).reshape(uly, count_tok, width), ("uly",), "swap"),
            (own_grad, ("blk",), "gather"),
            (routes[0].T, ("blk",), "gather"),
        ],
        2,
        after=[whole_gate_up[0], whole_down[0]],
    )
    inputs = own_tokens.astype(F32)
    mid = inputs + jnp.sum(branch.astype(F32), axis=0)

    scale_two = rms_scale(mid)
    normed_two = mid * scale_two
    hidden_two = (normed_two * gain_ffn).astype(BF16)
    (hidden_blk,) = exchange(
        [(hidden_two, ("blk",), "gather")], 3, after=[whole_gate_up[1], whole_down[1]]
    )
    tokens_blk = blk * count_tok
    hidden_blk = hidden_blk.reshape(tokens_blk, width)
    grad_blk = grad_blk.reshape(tokens_blk, width)
    probs_blk = jax.nn.softmax(dot_nt(hidden_blk, router_t), axis=1)
    names = jnp.arange(number, dtype=jnp.int32)
    chosen_blk = jnp.any(routes_blk[:, :, :, None] == names, axis=1).astype(F32)
    chosen_blk = chosen_blk.reshape(tokens_blk, number)
    gates = lax.dynamic_slice_in_dim(
        probs_blk * chosen_blk, blk_at * local_experts, local_experts, axis=1
    )
    hidden_t, grad_t = hidden_blk.T, grad_blk.T
    made = [
        one_expert(
            hidden_blk, hidden_t, grad_blk, grad_t, gates[:, e : e + 1], whole_gate_up[e], whole_down[e]
        )
        for e in range(local_experts)
    ]
    expert_sums = [
        lax.psum_scatter(m[3], PLANE, scatter_dimension=0, tiled=False).astype(F32) for m in made
    ]
    grad_gate_up = jnp.stack([jnp.concatenate([g[0], g[1]], axis=1) for g in expert_sums])
    grad_down = jnp.stack([g[2] for g in expert_sums])
    dx_part = sum(m[1].astype(F32) for m in made).astype(BF16)
    dg_part = jnp.stack([m[2].reshape(blk, count_tok) for m in made], axis=1)
    dx_parts, dg_parts = exchange(
        [
            (dx_part.reshape(blk, count_tok, width), ("blk",), "swap"),
            (dg_part, ("blk",), "swap"),
        ],
        4,
    )
    out_part = sum(m[0].astype(F32) for m in made).astype(BF16).reshape(blk, count_tok, width)
    out_part, dx_parts = lax.optimization_barrier((out_part, dx_parts))
    out_parts = lax.all_to_all(out_part, "blk", split_axis=0, concat_axis=0, tiled=True)
    output = (mid + jnp.sum(out_parts.astype(F32), axis=0)).astype(BF16)
    router_probs = lax.dynamic_slice_in_dim(probs_blk, blk_at * count_tok, count_tok)
    chosen = lax.dynamic_slice_in_dim(chosen_blk, blk_at * count_tok, count_tok)
    grad_probs = chosen * dg_parts.reshape(number, count_tok).T
    grad_logits = (
        router_probs * (grad_probs - jnp.sum(router_probs * grad_probs, axis=1, keepdims=True))
    ).astype(BF16)
    grad_hidden_two = jnp.sum(dx_parts.astype(F32), axis=0) + dot_nn(grad_logits, router_t)
    grad_router_t = dot_tn(grad_logits, hidden_two)
    grad_gain_ffn = jnp.sum(grad_hidden_two * normed_two, axis=0)
    grad_mid = own_grad.astype(F32) + norm_back(grad_hidden_two * gain_ffn, mid, scale_two)

    (branch_grad,) = exchange([(grad_mid.astype(BF16), ("uly",), "gather")], 5)
    branch_grad = branch_grad.reshape(rows, width)
    grad_attn = dot_nt(branch_grad, own_out.reshape(blk * head_dim, width)).astype(BF16)
    (grad_attn,) = exchange(
        [(grad_attn.reshape(rows, blk, head_dim).transpose(1, 0, 2), ("blk",), "swap")], 6
    )
    grad_out_part = jnp.einsum("htc,td->hcd", attn_rows, branch_grad, preferred_element_type=F32)
    grad_out_parts = lax.all_to_all(
        grad_out_part.astype(BF16).reshape(group, shard_rows, width),
        ROWS,
        split_axis=0,
        concat_axis=0,
        tiled=True,
    )
    to_rows = [(u * group + g, g * uly + u) for g in range(group) for u in range(uly)]
    grad_out = lax.ppermute(
        jnp.sum(grad_out_parts.astype(F32), axis=0).astype(BF16), ALL, [(b, a) for a, b in to_rows]
    ).astype(F32)
    dq, dk, dv = attention_backward(
        qkv, qkv, cols, grad_attn.reshape(1, length, head_dim), attn_f32, lse, seg_row, seg_row, head_dim
    )
    grad_query_norm = rotate(dq[0].astype(F32), cos_table, -sin_table)
    grad_key_norm = rotate(dk[0].astype(F32), cos_table, -sin_table)
    grad_gain_query = jnp.sum(grad_query_norm * (query_raw * query_scale), axis=0)
    grad_gain_key = jnp.sum(grad_key_norm * (key_raw * key_scale), axis=0)
    grad_projected = jnp.concatenate(
        [
            norm_back(grad_query_norm * gain_query, query_raw, query_scale).astype(BF16),
            norm_back(grad_key_norm * gain_key, key_raw, key_scale).astype(BF16),
            dv[0],
        ],
        axis=1,
    )
    grad_qkv_part = dot_tn(hidden_one, grad_projected).astype(BF16)
    by_uly = grad_projected.reshape(blk, uly, count_tok, 3 * head_dim).transpose(1, 0, 2, 3)
    grad_projected, grad_qkv_parts = exchange(
        [
            (by_uly.reshape(uly, tokens_blk, 3 * head_dim), ("uly",), "swap"),
            (grad_qkv_part.reshape(total, shard_rows, 3 * head_dim), ALL, "swap"),
        ],
        7,
    )
    grad_qkv = jnp.sum(grad_qkv_parts.astype(F32).reshape(batch, blk, uly, shard_rows, 3, head_dim), axis=0)
    grad_qkv = grad_qkv.transpose(2, 3, 1, 0, 4).reshape(shard_rows, 3 * width)

    grad_hidden_part = jnp.zeros((tokens_blk, width), F32)
    for step in range(uly):
        weights = own_qkv
        if step:
            weights = lax.ppermute(own_qkv, "uly", [(u, (u + step) % uly) for u in range(uly)])
        sender = lax.rem(uly_at + uly - step, uly)
        own_part = lax.dynamic_index_in_dim(grad_projected, sender, 0, keepdims=False)
        grad_hidden_part = grad_hidden_part + dot_nt(own_part, weights)
    inputs_blk = lax.dynamic_index_in_dim(toks, uly_at, 1, keepdims=False)
    inputs_blk = inputs_blk.reshape(tokens_blk, width).astype(F32)
    grad_gain_attn = jnp.sum(grad_hidden_part * (inputs_blk * rms_scale(inputs_blk)), axis=0)

    small = jnp.concatenate([grad_gain_attn[None], grad_gain_ffn[None], grad_router_t], axis=0)
    small = small.reshape(kept, total, shard_rows).transpose(1, 0, 2)
    small = jnp.pad(small, ((0, 0), (0, 0), (0, LANES - shard_rows)))
    head_row = jnp.where(
        jnp.arange(LANES) == uly_at * blk + blk_at, jnp.max(top) * head_dim**-0.5, NEG
    )
    shared = jnp.stack([grad_gain_query, grad_gain_key, head_row])
    small = jnp.concatenate([small, jnp.broadcast_to(shared[None], (total, 3, LANES))], axis=1)
    small = jnp.pad(small, ((0, 0), (0, -small.shape[1] % 8), (0, 0)))
    grad_hidden_parts, small = exchange(
        [
            (grad_hidden_part.astype(BF16).reshape(blk, count_tok, width), ("blk",), "swap"),
            (small, ALL, "swap"),
        ],
        8,
    )
    grad_hidden_one = jnp.sum(grad_hidden_parts.astype(F32), axis=0)
    grad_inputs = grad_mid + norm_back(grad_hidden_one * gain_attn, inputs, rms_scale(inputs))
    sums = jnp.sum(small, axis=0)
    head_max = jnp.max(small[:, kept + 2, :heads], axis=0)
    factor = jnp.repeat(jnp.sqrt(TAU / jnp.maximum(head_max, TAU)), head_dim)
    column_scale = jnp.concatenate([factor, factor, jnp.ones((width,), F32)])
    clipped = w_qkv.astype(F32) * column_scale[None, :]
    return (
        output[None],
        grad_inputs[None],
        grad_qkv,
        grad_out,
        sums[0, :shard_rows],
        sums[1, :shard_rows],
        sums[kept : kept + 2],
        sums[2:kept, :shard_rows].T,
        grad_gate_up,
        grad_down,
        clipped,
    )


def solution(mesh):
    in_specs = (
        P("batch", ("blk", "uly"), None),
        P("batch", None),
        P("batch", ("blk", "uly"), None),
        P(ALL, None),
        P(ALL, None),
        P(ALL),
        P(ALL),
        P(),
        P(ALL, None),
        P("blk", PLANE, None),
        P("blk", PLANE, None),
        P("batch", ("blk", "uly"), None),
    )
    out_specs = (
        P("batch", ("blk", "uly"), None),
        P("batch", ("blk", "uly"), None),
        P(ALL, None),
        P(ALL, None),
        P(ALL),
        P(ALL),
        P(),
        P(ALL, None),
        P("blk", PLANE, None),
        P("blk", PLANE, None),
        P(ALL, None),
    )
    return jax.shard_map(
        per_device, mesh=mesh, in_specs=in_specs, out_specs=out_specs, check_vma=False
    )
```

```python
import functools
import math

import jax
import jax.numpy as jnp
from jax import lax
from jax.experimental import pallas as pl
from jax.experimental.pallas import tpu as pltpu
from jax.sharding import PartitionSpec as P

EPS = 1e-06
THETA = 50000.0
TAU = 4.0
NEG = -1e30
LOG2E = 1.4426950408889634
LANES = 128
MOST_TOKENS = 512
VMEM_LIMIT = 60 * 1024 * 1024

ALL = ("batch", "blk", "uly")
ROWS = ("batch", "blk")
PLANE = ("batch", "uly")

MESH = pl.DeviceIdType.MESH
BF16 = jnp.bfloat16
F32 = jnp.float32


def rms_scale(values):
    return lax.rsqrt(jnp.mean(values * values, axis=-1, keepdims=True) + EPS)


def norm_back(grad_normed, values, scale):
    normed = values * scale
    return scale * (grad_normed - normed * jnp.mean(grad_normed * normed, axis=-1, keepdims=True))


def rope_tables(offset, length, head_dim):
    half_dim = head_dim // 2
    frequency = THETA ** (-jnp.arange(half_dim, dtype=F32) * 2.0 / head_dim)
    positions = (offset + jnp.arange(length, dtype=jnp.int32)).astype(F32)
    angles = positions[:, None] * frequency[None, :]
    return (jnp.cos(angles)[:, None, :], jnp.sin(angles)[:, None, :])


def rotate(values, cos_table, sin_table):
    half_dim = values.shape[-1] // 2
    first = values[..., :half_dim]
    second = values[..., half_dim:]
    return jnp.concatenate(
        [first * cos_table - second * sin_table, second * cos_table + first * sin_table], axis=-1
    )


def dot_nn(a, b):
    return lax.dot_general(a, b, (((1,), (0,)), ((), ())), preferred_element_type=F32)


def dot_nt(a, b):
    return lax.dot_general(a, b, (((1,), (1,)), ((), ())), preferred_element_type=F32)


def dot_tn(a, b):
    return lax.dot_general(a, b, (((0,), (0,)), ((), ())), preferred_element_type=F32)


def key_chunks(length):
    size = min(512, length)
    return size, length // size


def attn_fwd_kernel(factor, q_ref, k_ref, v_ref, sq_ref, sk_ref, o_ref, of_ref, lse_ref, top_ref, vt_ref):
    length = k_ref.shape[1]
    size, count = key_chunks(length)
    tile, head_dim = q_ref.shape[1:]

    @pl.when(pl.program_id(1) == 0)
    def _():
        vt_ref[...] = v_ref[0].astype(F32).T.astype(BF16)

    q = q_ref[0]
    seg_q = sq_ref[...]

    def step(j, carried):
        total, top, acc = carried
        at = pl.multiple_of(j * size, size)
        scores = dot_nt(k_ref[0, pl.ds(at, size), :], q)
        scores = jnp.where(sk_ref[pl.ds(at, size), :] == seg_q, scores, NEG)
        top = jnp.maximum(top, jnp.max(scores, axis=0, keepdims=True))
        weights = jnp.exp2(scores * factor)
        total = total + jnp.sum(weights, axis=0, keepdims=True)
        acc = acc + dot_nn(vt_ref[:, pl.ds(at, size)], weights.astype(BF16))
        return total, top, acc

    start = (
        jnp.zeros((1, tile), F32),
        jnp.full((1, tile), NEG, F32),
        jnp.zeros((head_dim, tile), F32),
    )
    total, top, acc = lax.fori_loop(0, count, step, start, unroll=count <= 4)
    out = (acc * (1.0 / total)).T
    o_ref[0] = out.astype(BF16)
    of_ref[0] = out
    lse_ref[0] = jnp.log2(total)
    top_ref[0] = top


def attn_bwd_kernel(
    factor, scale, q_ref, k_ref, v_ref, do_ref, of_ref, lse_ref, sq_ref, sk_ref,
    dq_ref, dk_ref, dv_ref, kt_ref, dk_acc, dv_acc,
):
    length = k_ref.shape[1]
    size, count = key_chunks(length)
    tile, head_dim = q_ref.shape[1:]

    @pl.when(pl.program_id(1) == 0)
    def _():
        kt_ref[...] = k_ref[0].astype(F32).T.astype(BF16)
        dk_acc[...] = jnp.zeros_like(dk_acc)
        dv_acc[...] = jnp.zeros_like(dv_acc)

    q = q_ref[0]
    grad = do_ref[0]
    seg_q = sq_ref[...]
    lse = lse_ref[0]
    row_dot = jnp.sum((grad.astype(F32) * of_ref[0]).T, axis=0, keepdims=True)

    def step(j, dq_t):
        at = pl.multiple_of(j * size, size)
        rows = pl.ds(at, size)
        scores = dot_nt(k_ref[0, rows, :], q)
        scores = jnp.where(sk_ref[rows, :] == seg_q, scores, NEG)
        weights = jnp.exp2(scores * factor - lse)
        grad_weights = dot_nt(v_ref[0, rows, :], grad)
        grad_scores = (weights * (grad_weights - row_dot)).astype(BF16)
        dk_acc[rows, :] += dot_nn(grad_scores, q)
        dv_acc[rows, :] += dot_nn(weights.astype(BF16), grad)
        return dq_t + dot_nn(kt_ref[:, rows], grad_scores)

    dq_t = lax.fori_loop(0, count, step, jnp.zeros((head_dim, tile), F32), unroll=count <= 4)
    dq_ref[0] = (dq_t * scale).T.astype(BF16)

    @pl.when(pl.program_id(1) == pl.num_programs(1) - 1)
    def _():
        dk_ref[0] = (dk_acc[...] * scale).astype(BF16)
        dv_ref[0] = dv_acc[...].astype(BF16)


def attention_tile(queries, length):
    return min(queries, 256 if length <= 4096 else 128)


def attention_forward(q_src, kv_src, cols, seg_q, seg_k, head_dim):
    heads, queries = q_src.shape[:2]
    length = kv_src.shape[1]
    tile = attention_tile(queries, length)
    q_col, k_col, v_col = cols
    factor = head_dim**-0.5 * LOG2E
    row = pl.BlockSpec((1, 1, tile), lambda h, i: (h, 0, i))
    block = pl.BlockSpec((1, tile, head_dim), lambda h, i: (h, i, 0))
    return pl.pallas_call(
        functools.partial(attn_fwd_kernel, factor),
        grid=(heads, queries // tile),
        in_specs=[
            pl.BlockSpec((1, tile, head_dim), lambda h, i: (h, i, q_col)),
            pl.BlockSpec((1, length, head_dim), lambda h, i: (h, 0, k_col)),
            pl.BlockSpec((1, length, head_dim), lambda h, i: (h, 0, v_col)),
            pl.BlockSpec((1, tile), lambda h, i: (0, i)),
            pl.BlockSpec((length, 1), lambda h, i: (0, 0)),
        ],
        out_specs=[block, block, row, row],
        out_shape=[
            jax.ShapeDtypeStruct((heads, queries, head_dim), BF16),
            jax.ShapeDtypeStruct((heads, queries, head_dim), F32),
            jax.ShapeDtypeStruct((heads, 1, queries), F32),
            jax.ShapeDtypeStruct((heads, 1, queries), F32),
        ],
        scratch_shapes=[pltpu.VMEM((head_dim, length), BF16)],
        compiler_params=pltpu.CompilerParams(vmem_limit_bytes=VMEM_LIMIT),
        cost_estimate=pl.CostEstimate(
            flops=4 * heads * queries * length * head_dim,
            bytes_accessed=heads * (queries + length) * head_dim * 8,
            transcendentals=heads * queries * length,
        ),
        name="attend",
    )(q_src, kv_src, kv_src, seg_q.reshape(1, -1), seg_k.reshape(-1, 1))


def attention_backward(q_src, kv_src, cols, grad, out_f32, lse, seg_q, seg_k, head_dim):
    heads, queries = q_src.shape[:2]
    length = kv_src.shape[1]
    tile = attention_tile(queries, length)
    q_col, k_col, v_col = cols
    scale = head_dim**-0.5
    row = pl.BlockSpec((1, 1, tile), lambda h, i: (h, 0, i))
    block = pl.BlockSpec((1, tile, head_dim), lambda h, i: (h, i, 0))
    whole = pl.BlockSpec((1, length, head_dim), lambda h, i: (h, 0, 0))
    return pl.pallas_call(
        functools.partial(attn_bwd_kernel, scale * LOG2E, scale),
        grid=(heads, queries // tile),
        in_specs=[
            pl.BlockSpec((1, tile, head_dim), lambda h, i: (h, i, q_col)),
            pl.BlockSpec((1, length, head_dim), lambda h, i: (h, 0, k_col)),
            pl.BlockSpec((1, length, head_dim), lambda h, i: (h, 0, v_col)),
            block,
            block,
            row,
            pl.BlockSpec((1, tile), lambda h, i: (0, i)),
            pl.BlockSpec((length, 1), lambda h, i: (0, 0)),
        ],
        out_specs=[block, whole, whole],
        out_shape=[
            jax.ShapeDtypeStruct((heads, queries, head_dim), BF16),
            jax.ShapeDtypeStruct((heads, length, head_dim), BF16),
            jax.ShapeDtypeStruct((heads, length, head_dim), BF16),
        ],
        scratch_shapes=[
            pltpu.VMEM((head_dim, length), BF16),
            pltpu.VMEM((length, head_dim), F32),
            pltpu.VMEM((length, head_dim), F32),
        ],
        compiler_params=pltpu.CompilerParams(vmem_limit_bytes=VMEM_LIMIT),
        cost_estimate=pl.CostEstimate(
            flops=10 * heads * queries * length * head_dim,
            bytes_accessed=heads * (queries + length) * head_dim * 12,
            transcendentals=heads * queries * length,
        ),
        name="attend_back",
    )(q_src, kv_src, kv_src, grad, out_f32, lse, seg_q.reshape(1, -1), seg_k.reshape(-1, 1))


def expert_kernel(
    first, h_ref, ht_ref, dy_ref, dyt_ref, gate_ref, out0_ref, dx0_ref, wg_ref, wu_ref, wd_ref,
    out_ref, dx_ref, dg_ref, gr_ref, out_acc, dx_acc,
):
    expert, chunk = pl.program_id(0), pl.program_id(1)
    width = h_ref.shape[1]
    parts, _, part_rows, cols = wg_ref.shape

    @pl.when((expert == 0) & (chunk == 0))
    def _():
        out_acc[...] = out0_ref[...].astype(F32)
        dx_acc[...] = dx0_ref[...].astype(F32)

    @pl.when(chunk == 0)
    def _():
        dg_ref[...] = jnp.zeros_like(dg_ref)

    w_gate = wg_ref[...].reshape(width, cols)
    w_up = wu_ref[...].reshape(width, cols)
    w_down = wd_ref[...].reshape(width, cols)
    gates = gate_ref[...]
    mine = lax.broadcasted_iota(jnp.int32, gates.shape, 1) == first + expert
    gate = jnp.sum(jnp.where(mine, gates, 0.0), axis=1, keepdims=True)
    a_gate = dot_nn(h_ref[...], w_gate)
    a_up = dot_nn(h_ref[...], w_up)
    raw = dot_nn(dy_ref[...], w_down)
    sigma = 1.0 / (1.0 + jnp.exp2(a_gate * -LOG2E))
    swish = a_gate * sigma
    act = swish * a_up
    dg_ref[0] += jnp.sum(raw * act, axis=1, keepdims=True)
    gated = (gate * act).astype(BF16)
    d_act = gate * raw
    d_gate = (d_act * a_up * (sigma + swish * (1.0 - sigma))).astype(BF16)
    d_up = (d_act * swish).astype(BF16)
    out_acc[...] += dot_nt(gated, w_down)
    dx_acc[...] += dot_nt(d_gate, w_gate) + dot_nt(d_up, w_up)
    gr_ref[:, 0, 0] = dot_nn(ht_ref[...], d_gate).astype(BF16).reshape(parts, part_rows, cols)
    gr_ref[:, 1, 0] = dot_nn(ht_ref[...], d_up).astype(BF16).reshape(parts, part_rows, cols)
    gr_ref[:, 2, 0] = dot_nn(dyt_ref[...], gated).astype(BF16).reshape(parts, part_rows, cols)

    @pl.when((expert == pl.num_programs(0) - 1) & (chunk == pl.num_programs(1) - 1))
    def _():
        out_ref[...] = out_acc[...].astype(BF16)
        dx_ref[...] = dx_acc[...].astype(BF16)


def experts(first, count, hidden, hidden_t, grad, grad_t, gates, out, dx, gate_up, down):
    tokens, width = hidden.shape
    parts, _, part_rows, units = down.shape
    cols = min(256, units)
    chunks = units // cols
    once = pl.Buffered(1)
    whole = pl.BlockSpec((tokens, width), lambda e, f: (0, 0), pipeline_mode=once)
    whole_t = pl.BlockSpec((width, tokens), lambda e, f: (0, 0), pipeline_mode=once)
    result = pl.BlockSpec((tokens, width), lambda e, f: (0, 0))
    weight = (parts, 1, part_rows, cols)
    return pl.pallas_call(
        functools.partial(expert_kernel, first),
        grid=(count, chunks),
        in_specs=[
            whole,
            whole_t,
            whole,
            whole_t,
            pl.BlockSpec(gates.shape, lambda e, f: (0, 0), pipeline_mode=once),
            whole,
            whole,
            pl.BlockSpec(weight, lambda e, f: (0, first + e, 0, f)),
            pl.BlockSpec(weight, lambda e, f: (0, first + e, 0, chunks + f)),
            pl.BlockSpec(weight, lambda e, f: (0, first + e, 0, f)),
        ],
        out_specs=[
            result,
            result,
            pl.BlockSpec((1, tokens, 1), lambda e, f: (e, 0, 0)),
            pl.BlockSpec((parts, 3, 1, part_rows, cols), lambda e, f: (0, 0, e, 0, f)),
        ],
        out_shape=[
            jax.ShapeDtypeStruct((tokens, width), BF16),
            jax.ShapeDtypeStruct((tokens, width), BF16),
            jax.ShapeDtypeStruct((count, tokens, 1), F32),
            jax.ShapeDtypeStruct((parts, 3, count, part_rows, units), BF16),
        ],
        scratch_shapes=[
            pltpu.VMEM((tokens, width), F32),
            pltpu.VMEM((tokens, width), F32),
        ],
        compiler_params=pltpu.CompilerParams(vmem_limit_bytes=VMEM_LIMIT),
        cost_estimate=pl.CostEstimate(
            flops=18 * count * tokens * width * units,
            bytes_accessed=12 * count * width * units,
            transcendentals=count * tokens * units,
        ),
        name="experts",
    )(hidden, hidden_t, grad, grad_t, gates, out, dx, gate_up, gate_up, down)


def finish_experts_kernel(a_ref, b_ref, gate_up_ref, down_ref):
    units = down_ref.shape[2]

    def write(src):
        gate_up_ref[0, :, :units] = src[0, 0].astype(F32)
        gate_up_ref[0, :, units:] = src[1, 0].astype(F32)
        down_ref[0] = src[2, 0].astype(F32)

    @pl.when(pl.program_id(0) == 0)
    def _():
        write(a_ref)

    @pl.when(pl.program_id(0) > 0)
    def _():
        write(b_ref)


def finish_experts(first, others):
    _, count, rows, units = others.shape
    block = (3, 1, rows, units)
    return pl.pallas_call(
        finish_experts_kernel,
        grid=(count + 1,),
        in_specs=[
            pl.BlockSpec(block, lambda e: (0, 0, 0, 0)),
            pl.BlockSpec(block, lambda e: (0, jnp.maximum(e - 1, 0), 0, 0)),
        ],
        out_specs=[
            pl.BlockSpec((1, rows, 2 * units), lambda e: (e, 0, 0)),
            pl.BlockSpec((1, rows, units), lambda e: (e, 0, 0)),
        ],
        out_shape=[
            jax.ShapeDtypeStruct((count + 1, rows, 2 * units), F32),
            jax.ShapeDtypeStruct((count + 1, rows, units), F32),
        ],
        compiler_params=pltpu.CompilerParams(vmem_limit_bytes=VMEM_LIMIT),
        name="finish_experts",
    )(first, others)


def turn(values, cos, sin):
    return values * cos + pltpu.roll(values, values.shape[1] // 2, 1) * sin


def project_kernel(
    tok_ref, gain_ref, w_ref, cos_ref, sin_ref, gains_ref, hidden_ref, qkv_ref, raw_ref
):
    head_dim = cos_ref.shape[1]
    values = tok_ref[...].astype(F32)
    hidden = (values * rms_scale(values) * gain_ref[...]).astype(BF16)
    hidden_ref[...] = hidden
    projected = dot_nn(hidden, w_ref[...])
    raw_ref[...] = projected[:, : 2 * head_dim]
    for part in range(2):
        at = slice(part * head_dim, (part + 1) * head_dim)
        raw = projected[:, at]
        normed = raw * rms_scale(raw) * gains_ref[part : part + 1, :]
        qkv_ref[:, at] = turn(normed, cos_ref[...], sin_ref[...]).astype(BF16)
    qkv_ref[:, 2 * head_dim :] = projected[:, 2 * head_dim :].astype(BF16)


def project(toks, gain, weights, cos, sin, gains):
    length, width = toks.shape
    head_dim = cos.shape[1]
    tile = min(256, length)

    def rows(columns):
        return pl.BlockSpec((tile, columns), lambda i: (i, 0))

    def fixed(shape):
        return pl.BlockSpec(shape, lambda i: (0, 0))

    return pl.pallas_call(
        project_kernel,
        grid=(length // tile,),
        in_specs=[
            rows(width),
            fixed((1, width)),
            fixed(weights.shape),
            rows(head_dim),
            rows(head_dim),
            fixed(gains.shape),
        ],
        out_specs=[rows(width), rows(3 * head_dim), rows(2 * head_dim)],
        out_shape=[
            jax.ShapeDtypeStruct((length, width), BF16),
            jax.ShapeDtypeStruct((length, 3 * head_dim), BF16),
            jax.ShapeDtypeStruct((length, 2 * head_dim), F32),
        ],
        compiler_params=pltpu.CompilerParams(vmem_limit_bytes=VMEM_LIMIT),
        name="project",
    )(toks, gain, weights, cos, sin, gains)


def project_back_kernel(
    factor, scale, q_ref, k_ref, v_ref, do_ref, of_ref, lse_ref, sq_ref, sk_ref,
    raw_q_ref, raw_k_ref, cos_q_ref, sin_q_ref, cos_ref, sin_ref, gains_ref,
    dp_ref, dgain_ref, kt_ref, dk_acc, dv_acc,
):
    length, head_dim = k_ref.shape
    size, count = key_chunks(length)
    tile = q_ref.shape[0]
    step_at = pl.program_id(0)

    @pl.when(step_at == 0)
    def _():
        kt_ref[...] = k_ref[...].astype(F32).T.astype(BF16)
        dk_acc[...] = jnp.zeros_like(dk_acc)
        dv_acc[...] = jnp.zeros_like(dv_acc)
        dgain_ref[...] = jnp.zeros_like(dgain_ref)

    def to_raw(part, grad, raw, cos, sin):
        grad = turn(grad.astype(BF16).astype(F32), cos, -sin)
        raw_scale = rms_scale(raw)
        dgain_ref[part : part + 1, :] += jnp.sum(grad * (raw * raw_scale), axis=0, keepdims=True)
        return norm_back(grad * gains_ref[part : part + 1, :], raw, raw_scale).astype(BF16)

    q = q_ref[...]
    grad = do_ref[...]
    seg_q = sq_ref[...]
    lse = lse_ref[0]
    row_dot = jnp.sum((grad.astype(F32) * of_ref[0]).T, axis=0, keepdims=True)
    dq_t = jnp.zeros((head_dim, tile), F32)
    for j in range(count):
        rows = slice(j * size, (j + 1) * size)
        scores = dot_nt(k_ref[rows, :], q)
        scores = jnp.where(sk_ref[rows, :] == seg_q, scores, NEG)
        weights = jnp.exp2(scores * factor - lse)
        grad_weights = dot_nt(v_ref[rows, :], grad)
        grad_scores = (weights * (grad_weights - row_dot)).astype(BF16)
        dk_acc[rows, :] += dot_nn(grad_scores, q)
        dv_acc[rows, :] += dot_nn(weights.astype(BF16), grad)
        dq_t = dq_t + dot_nn(kt_ref[:, rows], grad_scores)
    own = pl.ds(pl.multiple_of(step_at * tile, tile), tile)
    dp_ref[own, :head_dim] = to_raw(
        0, (dq_t * scale).T, raw_q_ref[...], cos_q_ref[...], sin_q_ref[...]
    )

    @pl.when(step_at == pl.num_programs(0) - 1)
    def _():
        dp_ref[:, head_dim : 2 * head_dim] = to_raw(
            1, dk_acc[...] * scale, raw_k_ref[...], cos_ref[...], sin_ref[...]
        )
        dp_ref[:, 2 * head_dim :] = dv_acc[...].astype(BF16)


def project_back(qkv, grad, out_f32, lse, segments, raw, cos, sin, gains):
    length, head_dim = grad.shape
    tile = min(256, length)

    def rows(column):
        return pl.BlockSpec((tile, head_dim), lambda i: (i, column))

    def whole(column):
        return pl.BlockSpec((length, head_dim), lambda i: (0, column))

    return pl.pallas_call(
        functools.partial(project_back_kernel, head_dim**-0.5 * LOG2E, head_dim**-0.5),
        grid=(length // tile,),
        in_specs=[
            rows(0),
            whole(1),
            whole(2),
            rows(0),
            pl.BlockSpec((1, tile, head_dim), lambda i: (0, i, 0)),
            pl.BlockSpec((1, 1, tile), lambda i: (0, 0, i)),
            pl.BlockSpec((1, tile), lambda i: (0, i)),
            pl.BlockSpec((length, 1), lambda i: (0, 0)),
            rows(0),
            whole(1),
            rows(0),
            rows(0),
            whole(0),
            whole(0),
            pl.BlockSpec(gains.shape, lambda i: (0, 0)),
        ],
        out_specs=[
            pl.BlockSpec((length, 3 * head_dim), lambda i: (0, 0)),
            pl.BlockSpec((2, head_dim), lambda i: (0, 0)),
        ],
        out_shape=[
            jax.ShapeDtypeStruct((length, 3 * head_dim), BF16),
            jax.ShapeDtypeStruct((2, head_dim), F32),
        ],
        scratch_shapes=[
            pltpu.VMEM((head_dim, length), BF16),
            pltpu.VMEM((length, head_dim), F32),
            pltpu.VMEM((length, head_dim), F32),
        ],
        compiler_params=pltpu.CompilerParams(vmem_limit_bytes=VMEM_LIMIT),
        cost_estimate=pl.CostEstimate(
            flops=10 * length * length * head_dim,
            bytes_accessed=length * head_dim * 40,
            transcendentals=length * length,
        ),
        name="project_back",
    )(
        qkv, qkv, qkv, grad, out_f32, lse, segments.reshape(1, -1), segments.reshape(-1, 1),
        raw, raw, cos, sin, cos, sin, gains,
    )


def merge_heads_kernel(parts_ref, out_ref):
    batch, blk, uly, _, columns = parts_ref.shape
    head_dim = columns // 3
    heads = blk * uly
    for z in range(blk):
        for u in range(uly):
            total = parts_ref[0, z, u].astype(F32)
            for b in range(1, batch):
                total = total + parts_ref[b, z, u].astype(F32)
            for part in range(3):
                at = (part * heads + u * blk + z) * head_dim
                out_ref[:, at : at + head_dim] = total[:, part * head_dim : (part + 1) * head_dim]


def merge_heads(parts):
    _, blk, uly, rows, columns = parts.shape
    return pl.pallas_call(
        merge_heads_kernel,
        out_shape=jax.ShapeDtypeStruct((rows, blk * uly * columns), F32),
        compiler_params=pltpu.CompilerParams(vmem_limit_bytes=VMEM_LIMIT),
        name="merge_heads",
    )(parts)


def swap(values, axis):
    return lax.all_to_all(values, axis, split_axis=0, concat_axis=0, tiled=True)


def sum_scatter(values, axis):
    count = lax.axis_size(axis)
    rows, width = values.shape
    parts = swap(values.astype(BF16).reshape(count, rows // count, width), axis)
    return jnp.sum(parts.astype(F32), axis=0)


def place(axes, index):
    found = {}
    for axis in reversed(axes):
        size = lax.axis_size(axis)
        found[axis] = lax.rem(index, size)
        index = index // size
    return found


def spread(axes):
    return math.prod(lax.axis_size(axis) for axis in axes)


def each(count, body):
    if count <= 4:
        for step in range(1, count):
            body(step)
    else:

        def looped(step, carried):
            body(step)
            return carried

        lax.fori_loop(1, count, looped, 0)


def ahead(index, step, size):
    return lax.rem(index + step, size)


def exchange(items, collective_id, after=()):
    count = len(items)
    sizes = [spread(axes) for _, axes, _ in items]
    groups = list(dict.fromkeys(axes for _, axes, _ in items))
    bases = [sum(sizes[:i]) for i in range(count)]

    def kernel(*refs):
        ins = refs[:count]
        outs = refs[count + len(after) : 2 * count + len(after)]
        send, recv, local = refs[-3:]
        barrier = pltpu.get_barrier_semaphore()
        for axes in groups:
            size, me = spread(axes), lax.axis_index(axes)

            def greet(step, axes=axes, size=size, me=me):
                pl.semaphore_signal(
                    barrier, inc=1, device_id=place(axes, ahead(me, step, size)), device_id_type=MESH
                )

            each(size, greet)
        pl.semaphore_wait(barrier, sum(spread(axes) - 1 for axes in groups))

        def remote(i, step):
            _, axes, kind = items[i]
            me = lax.axis_index(axes)
            if kind == "relay":
                far, near = lax.rem(me + 2, 4), me + 1 - 2 * lax.rem(me, 2)
                held = far if step == 3 else me
                return pltpu.make_async_remote_copy(
                    src_ref=outs[i].at[far] if step == 3 else ins[i],
                    dst_ref=outs[i].at[held],
                    send_sem=send.at[bases[i] + step],
                    recv_sem=recv.at[bases[i] + step],
                    device_id=place(axes, far if step == 1 else near),
                    device_id_type=MESH,
                )
            peer = ahead(me, step, sizes[i])
            return pltpu.make_async_remote_copy(
                src_ref=ins[i].at[peer] if kind == "swap" else ins[i],
                dst_ref=outs[i].at[me],
                send_sem=send.at[bases[i] + step],
                recv_sem=recv.at[bases[i] + step],
                device_id=place(axes, peer),
                device_id_type=MESH,
            )

        def own(i):
            _, axes, kind = items[i]
            me = lax.axis_index(axes)
            return pltpu.make_async_copy(
                ins[i].at[me] if kind == "swap" else ins[i], outs[i].at[me], local.at[i]
            )

        relays = [i for i in range(count) if items[i][2] == "relay"]
        for i in range(count):
            each(3 if i in relays else sizes[i], lambda step, i=i: remote(i, step).start())
        for i in range(count):
            own(i).start()
        for i in relays:
            remote(i, 1).wait_recv()
            remote(i, 3).start()
            remote(i, 1).wait_send()
            for step in (2, 3):
                remote(i, step).wait()
        for i in range(count):
            if i not in relays:
                each(sizes[i], lambda step, i=i: remote(i, step).wait())
        for i in range(count):
            own(i).wait()

    shapes = [
        (size, *(array.shape[1:] if kind == "swap" else array.shape))
        for size, (array, _, kind) in zip(sizes, items)
    ]
    anywhere = pl.BlockSpec(memory_space=pl.ANY)
    return pl.pallas_call(
        kernel,
        in_specs=[anywhere] * (count + len(after)),
        out_specs=[anywhere] * count,
        out_shape=[jax.ShapeDtypeStruct(shape, item[0].dtype) for shape, item in zip(shapes, items)],
        scratch_shapes=[
            pltpu.SemaphoreType.DMA((sum(sizes),)),
            pltpu.SemaphoreType.DMA((sum(sizes),)),
            pltpu.SemaphoreType.DMA((count,)),
        ],
        compiler_params=pltpu.CompilerParams(collective_id=collective_id, has_side_effects=True),
        name="exchange",
    )(*[item[0] for item in items], *after)


def startup_kernel(
    head_ref, extra_ref, tok_ref, heads_ref, extras_ref, toks_ref,
    head_send, head_recv, extra_send, extra_recv,
    z_send, z_recv, y_send, y_recv, c_send, c_recv, local,
):
    batch, blk, uly = (lax.axis_size(axis) for axis in ALL)
    b, z, u = (lax.axis_index(axis) for axis in ALL)
    total = batch * blk * uly
    me = lax.axis_index(ALL)
    far = lax.rem(u + 2, uly)
    near = u + 1 - 2 * lax.rem(u, 2)

    barrier = pltpu.get_barrier_semaphore()

    def greet(step):
        pl.semaphore_signal(
            barrier, inc=1, device_id=place(ALL, ahead(me, step, total)), device_id_type=MESH
        )

    each(total, greet)
    pl.semaphore_wait(barrier, total - 1)

    def send(src, dst, sent, got, to):
        return pltpu.make_async_remote_copy(
            src_ref=src, dst_ref=dst, send_sem=sent, recv_sem=got, device_id=to, device_id_type=MESH
        )

    def along_z(step):
        to = (b, ahead(z, step, blk), u)
        return send(tok_ref, toks_ref.at[z, u], z_send.at[step], z_recv.at[step], to)

    def along_y(step):
        at = ahead(z, step, blk)
        src = tok_ref if step == 0 else toks_ref.at[at, u]
        return send(src, toks_ref.at[at, u], y_send.at[step], y_recv.at[step], (b, z, far))

    def to_near(step, place_from):
        at = ahead(z, step, blk)
        if place_from == 0:
            src = tok_ref if step == 0 else toks_ref.at[at, u]
            dst = toks_ref.at[at, u]
        else:
            src = dst = toks_ref.at[at, far]
        sem = 2 * step + place_from
        return send(src, dst, c_send.at[sem], c_recv.at[sem], (b, z, near))

    def head(step):
        to = place(ALL, ahead(me, step, total))
        src = head_ref.at[to["uly"] * blk + to["blk"]]
        return send(src, heads_ref.at[me], head_send.at[step], head_recv.at[step], to)

    def extra(step):
        to = place(ALL, ahead(me, step, total))
        return send(extra_ref, extras_ref.at[me], extra_send.at[step], extra_recv.at[step], to)

    own = [
        pltpu.make_async_copy(tok_ref, toks_ref.at[z, u], local.at[0]),
        pltpu.make_async_copy(head_ref.at[u * blk + z], heads_ref.at[me], local.at[1]),
        pltpu.make_async_copy(extra_ref, extras_ref.at[me], local.at[2]),
    ]

    for step in range(1, blk):
        along_z(step).start()
    along_y(0).start()
    to_near(0, 0).start()

    def start_head(step):
        extra(step).start()
        head(step).start()

    each(total, start_head)
    for copy in own:
        copy.start()

    for step in range(1, blk):
        along_z(step).wait_recv()
        along_y(blk - step).start()
        to_near(blk - step, 0).start()
    for step in [0, *reversed(range(1, blk))]:
        along_y(step).wait_recv()
        to_near(step, 1).start()
    for step in range(blk):
        to_near(step, 0).wait_recv()
        to_near(step, 1).wait_recv()

    def wait_head(step):
        extra(step).wait()
        head(step).wait()

    each(total, wait_head)
    for copy in own:
        copy.wait()
    for step in range(1, blk):
        along_z(step).wait_send()
    for step in range(blk):
        along_y(step).wait_send()
        to_near(step, 0).wait_send()
        to_near(step, 1).wait_send()


def startup(heads, extra, tok, collective_id):
    batch, blk, uly = (lax.axis_size(axis) for axis in ALL)
    total = batch * blk * uly
    anywhere = pl.BlockSpec(memory_space=pl.ANY)
    dma = pltpu.SemaphoreType.DMA
    return pl.pallas_call(
        startup_kernel,
        in_specs=[anywhere] * 3,
        out_specs=[anywhere] * 3,
        out_shape=[
            jax.ShapeDtypeStruct((total, *heads.shape[1:]), BF16),
            jax.ShapeDtypeStruct((total, *extra.shape), BF16),
            jax.ShapeDtypeStruct((blk, uly, *tok.shape), BF16),
        ],
        scratch_shapes=[
            *[dma((total,))] * 4,
            *[dma((blk,))] * 4,
            *[dma((2 * blk,))] * 2,
            dma((3,)),
        ],
        compiler_params=pltpu.CompilerParams(collective_id=collective_id, has_side_effects=True),
        name="startup",
    )(heads, extra, tok)


def per_device_general(
    tokens, segments, routes, w_qkv, w_out, attn_gain, ffn_gain, qk_gain, router, w_gate_up, w_down, cotangent
):
    own_tokens = tokens[0]
    own_grad = cotangent[0]
    count_tok, width = own_tokens.shape
    head_dim = qk_gain.shape[1]
    heads = width // head_dim
    uly, blk, batch = lax.axis_size("uly"), lax.axis_size("blk"), lax.axis_size("batch")
    blk_at, uly_at = lax.axis_index("blk"), lax.axis_index("uly")
    group = batch * blk
    local_heads = heads // uly
    local_width = local_heads * head_dim
    rows = count_tok * uly
    seg_row = segments[0]
    length = seg_row.shape[0]
    number = router.shape[1]
    local_experts, _, units = w_down.shape
    shard_rows = w_qkv.shape[0]

    extra = jnp.concatenate([attn_gain[:, None], ffn_gain[:, None], router], axis=1)
    extra = jnp.pad(extra, ((0, 0), (0, LANES - extra.shape[1])))
    columns = w_qkv.reshape(shard_rows, 3, uly, local_width).transpose(2, 0, 1, 3)
    packed = jnp.concatenate(
        [
            columns.reshape(uly, shard_rows, 3 * local_width),
            jnp.broadcast_to(extra[None], (uly, shard_rows, LANES)),
        ],
        axis=2,
    )
    packed = swap(packed, "uly").reshape(uly * shard_rows, 3 * local_width + LANES)
    packed = lax.all_gather(packed, ROWS, axis=0, tiled=True)
    own_qkv = packed[:, : 3 * local_width]
    gain_attn = packed[:, 3 * local_width].astype(F32)
    gain_ffn = packed[:, 3 * local_width + 1].astype(F32)
    whole_router = packed[:, 3 * local_width + 2 : 3 * local_width + 2 + number]
    tokens_all = lax.all_gather(own_tokens, "uly", axis=0, tiled=True)
    to_rows = [(u * group + g, g * uly + u) for g in range(group) for u in range(uly)]
    own_out = lax.all_gather(lax.ppermute(w_out, ALL, to_rows), ROWS, axis=0, tiled=True)
    whole_gate_up = lax.all_gather(w_gate_up, PLANE, axis=0, tiled=False)
    whole_down = lax.all_gather(w_down, PLANE, axis=0, tiled=False)
    grad_blk = lax.all_gather(own_grad, "blk", axis=0, tiled=True)
    routes_blk = lax.all_gather(routes[0], "blk", axis=0, tiled=True)

    gain_query = qk_gain[0].astype(F32)
    gain_key = qk_gain[1].astype(F32)
    inputs_all = tokens_all.astype(F32)
    normed_one = inputs_all * rms_scale(inputs_all)
    hidden_one = (normed_one * gain_attn).astype(BF16)
    projected = dot_nn(hidden_one, own_qkv)
    query_raw = projected[:, :local_width].reshape(rows, local_heads, head_dim)
    key_raw = projected[:, local_width : 2 * local_width].reshape(rows, local_heads, head_dim)
    value_raw = projected[:, 2 * local_width :].reshape(rows, local_heads, head_dim)
    cos_table, sin_table = rope_tables(blk_at * rows, rows, head_dim)
    query_scale = rms_scale(query_raw)
    key_scale = rms_scale(key_raw)
    qkv = jnp.concatenate(
        [
            rotate(query_raw * query_scale * gain_query, cos_table, sin_table),
            rotate(key_raw * key_scale * gain_key, cos_table, sin_table),
            value_raw,
        ],
        axis=2,
    ).astype(BF16)
    qkv = qkv.transpose(1, 0, 2)

    by_heads = local_heads % blk == 0
    if by_heads:
        per = local_heads // blk

        def to_heads(values):
            columns = values.shape[2]
            moved = swap(values.reshape(blk, per, rows, columns), "blk")
            return moved.transpose(1, 0, 2, 3).reshape(per, length, columns)

        def to_rows_back(values):
            columns = values.shape[2]
            parts = values.reshape(per, blk, rows, columns).transpose(1, 0, 2, 3)
            return swap(parts, "blk").reshape(local_heads, rows, columns)

        q_src = kv_src = to_heads(qkv)
        cols = (0, 1, 2)
        seg_q = seg_row
        first_head = uly_at * local_heads + blk_at * per
    else:

        def to_heads(values):
            return values

        def to_rows_back(values):
            return values

        q_src = qkv
        kv_src = lax.all_gather(qkv[:, :, head_dim:], "blk", axis=1, tiled=True)
        cols = (0, 0, 1)
        seg_q = lax.dynamic_slice_in_dim(seg_row, blk_at * rows, rows)
        first_head = uly_at * local_heads
    attn_low, attn_f32, lse, top = attention_forward(q_src, kv_src, cols, seg_q, seg_row, head_dim)
    head_vector = lax.dynamic_update_slice_in_dim(
        jnp.full((heads,), NEG, F32), jnp.max(top, axis=(1, 2)) * head_dim**-0.5, first_head, 0
    )
    head_max = lax.pmax(head_vector, ALL)
    attn_rows = to_rows_back(attn_low)
    out_heads = own_out.reshape(local_heads, head_dim, width)
    branch = jnp.einsum("htc,hcd->td", attn_rows, out_heads, preferred_element_type=F32)
    inputs = own_tokens.astype(F32)
    mid = inputs + sum_scatter(branch, "uly")

    scale_two = rms_scale(mid)
    normed_two = mid * scale_two
    hidden_two = (normed_two * gain_ffn).astype(BF16)
    hidden_blk = lax.all_gather(hidden_two, "blk", axis=0, tiled=True)
    probs_blk = jax.nn.softmax(dot_nn(hidden_blk, whole_router), axis=1)
    names = jnp.arange(number, dtype=jnp.int32)
    chosen_blk = jnp.any(routes_blk[:, :, None] == names, axis=1).astype(F32)
    own_names = blk_at * local_experts
    gates = lax.dynamic_slice_in_dim(probs_blk * chosen_blk, own_names, local_experts, axis=1)
    most = min(MOST_TOKENS, hidden_blk.shape[0])
    nothing = jnp.zeros((most, width), BF16)
    made = []
    for at in range(0, hidden_blk.shape[0], most):
        hidden_part, grad_part = hidden_blk[at : at + most], grad_blk[at : at + most]
        made.append(
            experts(
                0,
                local_experts,
                hidden_part,
                hidden_part.T,
                grad_part,
                grad_part.T,
                gates[at : at + most],
                nothing,
                nothing,
                whole_gate_up,
                whole_down,
            )
        )
    out_part = jnp.concatenate([m[0] for m in made], axis=0)
    dx_part = jnp.concatenate([m[1] for m in made], axis=0)
    dg_part = jnp.concatenate([m[2] for m in made], axis=1)
    expert_grads = sum(m[3].astype(F32) for m in made).astype(BF16)
    expert_sums = lax.psum_scatter(expert_grads, PLANE, scatter_dimension=0, tiled=False).astype(F32)
    grad_gate_up = jnp.concatenate([expert_sums[0], expert_sums[1]], axis=2)
    grad_down = expert_sums[2]
    dg_parts = swap(dg_part.reshape(local_experts, blk, count_tok).transpose(1, 2, 0), "blk")
    grad_gates = dg_parts.transpose(1, 0, 2).reshape(count_tok, number)
    dx_sum = sum_scatter(dx_part, "blk")
    output = (mid + sum_scatter(out_part, "blk")).astype(BF16)
    router_probs = lax.dynamic_slice_in_dim(probs_blk, blk_at * count_tok, count_tok)
    chosen = lax.dynamic_slice_in_dim(chosen_blk, blk_at * count_tok, count_tok)
    grad_probs = chosen * grad_gates
    grad_logits = (
        router_probs * (grad_probs - jnp.sum(router_probs * grad_probs, axis=1, keepdims=True))
    ).astype(BF16)
    grad_hidden_two = dx_sum + dot_nt(grad_logits, whole_router)
    grad_router_part = dot_tn(hidden_two, grad_logits)
    grad_gain_ffn = jnp.sum(grad_hidden_two * normed_two, axis=0)
    grad_mid = own_grad.astype(F32) + norm_back(grad_hidden_two * gain_ffn, mid, scale_two)

    branch_grad = lax.all_gather(grad_mid.astype(BF16), "uly", axis=0, tiled=True)
    grad_attn = dot_nt(branch_grad, own_out).astype(BF16)
    grad_attn = to_heads(grad_attn.reshape(rows, local_heads, head_dim).transpose(1, 0, 2))
    grad_out_part = jnp.einsum("htc,td->hcd", attn_rows, branch_grad, preferred_element_type=F32)
    dq, dk, dv = attention_backward(
        q_src, kv_src, cols, grad_attn, attn_f32, lse, seg_q, seg_row, head_dim
    )
    if by_heads:
        dqkv = to_rows_back(jnp.concatenate([dq, dk, dv], axis=2))
        dq, dk, dv = jnp.split(dqkv, 3, axis=2)
    else:
        dk, dv = (lax.psum_scatter(g, "blk", scatter_dimension=1, tiled=True) for g in (dk, dv))
    dq, dk, dv = (g.transpose(1, 0, 2) for g in (dq, dk, dv))
    grad_query_norm = rotate(dq.astype(F32), cos_table, -sin_table)
    grad_key_norm = rotate(dk.astype(F32), cos_table, -sin_table)
    grad_gain_query = jnp.sum(grad_query_norm * (query_raw * query_scale), axis=(0, 1))
    grad_gain_key = jnp.sum(grad_key_norm * (key_raw * key_scale), axis=(0, 1))
    grad_projected = jnp.concatenate(
        [
            norm_back(grad_query_norm * gain_query, query_raw, query_scale)
            .reshape(rows, local_width)
            .astype(BF16),
            norm_back(grad_key_norm * gain_key, key_raw, key_scale)
            .reshape(rows, local_width)
            .astype(BF16),
            dv.reshape(rows, local_width),
        ],
        axis=1,
    )
    grad_hidden_part = dot_nt(grad_projected, own_qkv)
    grad_hidden_one = sum_scatter(grad_hidden_part, "uly")
    grad_gain_attn = jnp.sum(grad_hidden_part * normed_one, axis=0)
    grad_inputs = grad_mid + norm_back(grad_hidden_one * gain_attn, inputs, rms_scale(inputs))

    grad_qkv_part = dot_tn(hidden_one, grad_projected).astype(BF16)
    grad_qkv_rows = lax.psum_scatter(grad_qkv_part, ROWS, scatter_dimension=0, tiled=True)
    grad_qkv_rows = swap(grad_qkv_rows.reshape(uly, shard_rows, 3 * local_width), "uly")
    grad_qkv = (
        grad_qkv_rows.reshape(uly, shard_rows, 3, local_width)
        .transpose(1, 2, 0, 3)
        .reshape(shard_rows, 3 * width)
        .astype(F32)
    )
    grad_out_rows = lax.psum_scatter(
        grad_out_part.reshape(local_width, width).astype(BF16), ROWS, scatter_dimension=0, tiled=True
    )
    grad_out = lax.ppermute(grad_out_rows, ALL, [(b, a) for a, b in to_rows]).astype(F32)
    small = jnp.concatenate([grad_gain_attn[:, None], grad_gain_ffn[:, None], grad_router_part], axis=1)
    small = lax.psum_scatter(small, ALL, scatter_dimension=0, tiled=True)
    grad_qk_gain = lax.psum(jnp.stack([grad_gain_query, grad_gain_key]), ALL)

    clip_gamma = TAU / jnp.maximum(head_max, TAU)
    factor = jnp.repeat(jnp.sqrt(clip_gamma), head_dim)
    column_scale = jnp.concatenate([factor, factor, jnp.ones((width,), F32)])
    clipped = w_qkv.astype(F32) * column_scale[None, :]
    return (
        output[None],
        grad_inputs[None],
        grad_qkv,
        grad_out,
        small[:, 0],
        small[:, 1],
        grad_qk_gain,
        small[:, 2:],
        grad_gate_up,
        grad_down,
        clipped,
    )


def per_device(
    tokens, segments, routes, w_qkv, w_out, attn_gain, ffn_gain, qk_gain, router, w_gate_up, w_down, cotangent
):
    own_tokens = tokens[0]
    own_grad = cotangent[0]
    count_tok, width = own_tokens.shape
    head_dim = qk_gain.shape[1]
    heads = width // head_dim
    batch, blk, uly = (lax.axis_size(axis) for axis in ALL)
    total, group = batch * blk * uly, batch * blk
    if uly != 4 or heads != blk * uly:
        return per_device_general(
            tokens, segments, routes, w_qkv, w_out, attn_gain, ffn_gain, qk_gain, router, w_gate_up, w_down, cotangent
        )
    blk_at, uly_at = lax.axis_index("blk"), lax.axis_index("uly")
    rows = count_tok * uly
    seg_row = segments[0]
    length = seg_row.shape[0]
    number = router.shape[1]
    local_experts, _, units = w_down.shape
    shard_rows = w_qkv.shape[0]

    to_rows = [(u * group + g, g * uly + u) for g in range(group) for u in range(uly)]
    own_rows = lax.ppermute(w_out, ALL, to_rows)
    whole_gate_up = lax.all_gather(w_gate_up, PLANE, axis=0, tiled=False)
    whole_down = lax.all_gather(w_down, PLANE, axis=0, tiled=False)
    extra = jnp.concatenate([attn_gain[None], ffn_gain[None], router.T], axis=0)
    kept = extra.shape[0]
    extra = jnp.pad(extra, ((0, -kept % 16), (0, -shard_rows % LANES)))
    by_head = w_qkv.reshape(shard_rows, 3, heads, head_dim).transpose(2, 0, 1, 3)
    own_qkv, extras, toks = startup(
        by_head.reshape(heads, shard_rows, 3 * head_dim), extra, own_tokens, 0
    )
    own_rows, extras = lax.optimization_barrier((own_rows, extras))
    own_out = lax.all_to_all(
        jnp.broadcast_to(own_rows[None], (group, *own_rows.shape)), ROWS, split_axis=0, concat_axis=0, tiled=True
    ).reshape(blk, head_dim, width)
    own_qkv = own_qkv.reshape(width, 3 * head_dim)
    extras = extras[:, :kept, :shard_rows].transpose(1, 0, 2).reshape(kept, width)
    gain_attn = extras[0].astype(F32)
    gain_ffn = extras[1].astype(F32)
    router_t = extras[2:]

    gains = qk_gain.astype(F32)
    cos, sin = (table[:, 0] for table in rope_tables(0, length, head_dim))
    cos = jnp.concatenate([cos, cos], axis=1)
    sin = jnp.concatenate([-sin, sin], axis=1)
    hidden_one, qkv, raw = project(
        toks.reshape(length, width), gain_attn[None], own_qkv, cos, sin, gains
    )
    attn_low, attn_f32, lse, top = attention_forward(
        qkv[None], qkv[None], (0, 1, 2), seg_row, seg_row, head_dim
    )
    (attn_rows,) = exchange([(attn_low.reshape(blk, rows, head_dim), ("blk",), "swap")], 1)
    branch = jnp.einsum("htc,hcd->td", attn_rows, own_out, preferred_element_type=F32)
    branch, grad_blk, routes_blk = exchange(
        [
            (branch.astype(BF16).reshape(uly, count_tok, width), ("uly",), "swap"),
            (own_grad, ("blk",), "gather"),
            (routes[0].T, ("blk",), "gather"),
        ],
        2,
    )
    inputs = own_tokens.astype(F32)
    mid = inputs + jnp.sum(branch.astype(F32), axis=0)

    scale_two = rms_scale(mid)
    normed_two = mid * scale_two
    hidden_two = (normed_two * gain_ffn).astype(BF16)
    (hidden_blk,) = exchange([(hidden_two, ("blk",), "gather")], 3, after=[whole_gate_up])
    tokens_blk = blk * count_tok
    hidden_blk = hidden_blk.reshape(tokens_blk, width)
    grad_blk = grad_blk.reshape(tokens_blk, width)
    probs_blk = jax.nn.softmax(dot_nt(hidden_blk, router_t), axis=1)
    names = jnp.arange(number, dtype=jnp.int32)
    chosen_blk = jnp.any(routes_blk[:, :, :, None] == names, axis=1).astype(F32)
    chosen_blk = chosen_blk.reshape(tokens_blk, number)
    gates = lax.dynamic_slice_in_dim(
        probs_blk * chosen_blk, blk_at * local_experts, local_experts, axis=1
    )
    nothing = jnp.zeros((tokens_blk, width), BF16)
    shared = (hidden_blk, hidden_blk.T, grad_blk, grad_blk.T, gates)
    out_first, dx_first, dg_first, grads_first = experts(
        0, 1, *shared, nothing, nothing, whole_gate_up, whole_down
    )
    first_sums = lax.psum_scatter(grads_first, PLANE, scatter_dimension=0, tiled=False)
    out_part, dx_part, dg_others, grads_others = experts(
        1, local_experts - 1, *shared, out_first, dx_first, whole_gate_up, whole_down
    )
    other_sums = lax.psum_scatter(grads_others, PLANE, scatter_dimension=0, tiled=False)
    grad_gate_up, grad_down = finish_experts(first_sums, other_sums)
    dg_part = jnp.concatenate([dg_first, dg_others], axis=0).reshape(local_experts, blk, count_tok)
    dx_parts, dg_parts = exchange(
        [
            (dx_part.reshape(blk, count_tok, width), ("blk",), "swap"),
            (dg_part.transpose(1, 0, 2), ("blk",), "swap"),
        ],
        4,
    )
    out_part = out_part.reshape(blk, count_tok, width)
    out_part, sent_qkv, dx_parts = lax.optimization_barrier((out_part, own_qkv, dx_parts))
    out_parts = lax.all_to_all(out_part, "blk", split_axis=0, concat_axis=0, tiled=True)
    output = (mid + jnp.sum(out_parts.astype(F32), axis=0)).astype(BF16)
    to_far = [(u, (u + 2) % uly) for u in range(uly)]
    to_near = [(u, u ^ 1) for u in range(uly)]
    far_qkv = lax.ppermute(sent_qkv, "uly", to_far)
    near_qkv = lax.ppermute(sent_qkv, "uly", to_near)
    cross_qkv = lax.ppermute(far_qkv, "uly", to_near)
    router_probs = lax.dynamic_slice_in_dim(probs_blk, blk_at * count_tok, count_tok)
    chosen = lax.dynamic_slice_in_dim(chosen_blk, blk_at * count_tok, count_tok)
    grad_probs = chosen * dg_parts.reshape(number, count_tok).T
    grad_logits = (
        router_probs * (grad_probs - jnp.sum(router_probs * grad_probs, axis=1, keepdims=True))
    ).astype(BF16)
    grad_hidden_two = jnp.sum(dx_parts.astype(F32), axis=0) + dot_nn(grad_logits, router_t)
    grad_router_t = dot_tn(grad_logits, hidden_two)
    grad_gain_ffn = jnp.sum(grad_hidden_two * normed_two, axis=0)
    grad_mid = own_grad.astype(F32) + norm_back(grad_hidden_two * gain_ffn, mid, scale_two)

    (branch_grad,) = exchange([(grad_mid.astype(BF16), ("uly",), "relay")], 5)
    branch_grad = branch_grad.reshape(rows, width)
    grad_attn = jnp.einsum("td,hcd->htc", branch_grad, own_out, preferred_element_type=F32).astype(BF16)
    (grad_attn,) = exchange([(grad_attn, ("blk",), "swap")], 6)
    grad_out_part = jnp.einsum("htc,td->hcd", attn_rows, branch_grad, preferred_element_type=F32)
    grad_out_parts = lax.all_to_all(
        grad_out_part.astype(BF16).reshape(group, shard_rows, width),
        ROWS,
        split_axis=0,
        concat_axis=0,
        tiled=True,
    )
    grad_out = lax.ppermute(
        jnp.sum(grad_out_parts.astype(F32), axis=0).astype(BF16), ALL, [(b, a) for a, b in to_rows]
    ).astype(F32)
    grad_projected, grad_gains = project_back(
        qkv, grad_attn.reshape(length, head_dim), attn_f32, lse, seg_row, raw, cos, sin, gains
    )
    grad_qkv_part = dot_tn(hidden_one, grad_projected).astype(BF16)
    by_uly = grad_projected.reshape(blk, uly, count_tok, 3 * head_dim).transpose(1, 0, 2, 3)
    grad_projected, grad_qkv_parts = exchange(
        [
            (by_uly.reshape(uly, tokens_blk, 3 * head_dim), ("uly",), "swap"),
            (grad_qkv_part.reshape(total, shard_rows, 3 * head_dim), ALL, "swap"),
        ],
        7,
        after=[out_parts],
    )
    grad_qkv = merge_heads(grad_qkv_parts.reshape(batch, blk, uly, shard_rows, 3 * head_dim))

    near_at, far_at = uly_at + 1 - 2 * lax.rem(uly_at, 2), lax.rem(uly_at + 2, uly)
    cross_at = lax.rem(near_at + 2, uly)
    grad_hidden_part = sum(
        dot_nt(lax.dynamic_index_in_dim(grad_projected, sender, 0, keepdims=False), weights)
        for sender, weights in [
            (uly_at, own_qkv),
            (near_at, near_qkv),
            (far_at, far_qkv),
            (cross_at, cross_qkv),
        ]
    )
    inputs_blk = lax.dynamic_index_in_dim(toks, uly_at, 1, keepdims=False)
    inputs_blk = inputs_blk.reshape(tokens_blk, width).astype(F32)
    grad_gain_attn = jnp.sum(grad_hidden_part * (inputs_blk * rms_scale(inputs_blk)), axis=0)

    small = jnp.concatenate([grad_gain_attn[None], grad_gain_ffn[None], grad_router_t], axis=0)
    small = small.reshape(kept, total, shard_rows).transpose(1, 0, 2)
    small = jnp.pad(small, ((0, 0), (0, 0), (0, LANES - shard_rows)))
    head_row = jnp.where(
        jnp.arange(LANES) == uly_at * blk + blk_at, jnp.max(top) * head_dim**-0.5, NEG
    )
    to_all = jnp.concatenate([grad_gains, head_row[None]], axis=0)
    small = jnp.concatenate([small, jnp.broadcast_to(to_all[None], (total, 3, LANES))], axis=1)
    small = jnp.pad(small, ((0, 0), (0, -small.shape[1] % 8), (0, 0)))
    grad_hidden_parts, small = exchange(
        [
            (grad_hidden_part.astype(BF16).reshape(blk, count_tok, width), ("blk",), "swap"),
            (small, ALL, "swap"),
        ],
        8,
        after=[grad_out_parts],
    )
    grad_hidden_one = jnp.sum(grad_hidden_parts.astype(F32), axis=0)
    grad_inputs = grad_mid + norm_back(grad_hidden_one * gain_attn, inputs, rms_scale(inputs))
    sums = jnp.sum(small, axis=0)
    head_max = jnp.max(small[:, kept + 2, :heads], axis=0)
    factor = jnp.repeat(jnp.sqrt(TAU / jnp.maximum(head_max, TAU)), head_dim)
    column_scale = jnp.concatenate([factor, factor, jnp.ones((width,), F32)])
    clipped = w_qkv.astype(F32) * column_scale[None, :]
    return (
        output[None],
        grad_inputs[None],
        grad_qkv,
        grad_out,
        sums[0, :shard_rows],
        sums[1, :shard_rows],
        sums[kept : kept + 2],
        sums[2:kept, :shard_rows].T,
        grad_gate_up,
        grad_down,
        clipped,
    )


def solution(mesh):
    in_specs = (
        P("batch", ("blk", "uly"), None),
        P("batch", None),
        P("batch", ("blk", "uly"), None),
        P(ALL, None),
        P(ALL, None),
        P(ALL),
        P(ALL),
        P(),
        P(ALL, None),
        P("blk", PLANE, None),
        P("blk", PLANE, None),
        P("batch", ("blk", "uly"), None),
    )
    out_specs = (
        P("batch", ("blk", "uly"), None),
        P("batch", ("blk", "uly"), None),
        P(ALL, None),
        P(ALL, None),
        P(ALL),
        P(ALL),
        P(),
        P(ALL, None),
        P("blk", PLANE, None),
        P("blk", PLANE, None),
        P(ALL, None),
    )
    return jax.shard_map(
        per_device, mesh=mesh, in_specs=in_specs, out_specs=out_specs, check_vma=False
    )
```

```python
import functools
import math

import jax
import jax.numpy as jnp
from jax import lax
from jax.experimental import pallas as pl
from jax.experimental.pallas import tpu as pltpu
from jax.sharding import Mesh
from jax.sharding import PartitionSpec as P

EPS = 1e-06
THETA = 50000.0
TAU = 4.0
NEG = -1e30
LOG2E = 1.4426950408889634
LANES = 128
MOST_TOKENS = 512
VMEM_LIMIT = 60 * 1024 * 1024

ULY = ("y", "core")
ALL = ("batch", "blk", *ULY)
ROWS = ("batch", "blk")
PLANE = ("batch", *ULY)
CHIPS = ("batch", "y")

MESH = pl.DeviceIdType.MESH
BF16 = jnp.bfloat16
F32 = jnp.float32


def rms_scale(values):
    return lax.rsqrt(jnp.mean(values * values, axis=-1, keepdims=True) + EPS)


def norm_back(grad_normed, values, scale):
    normed = values * scale
    return scale * (grad_normed - normed * jnp.mean(grad_normed * normed, axis=-1, keepdims=True))


def rope_tables(offset, length, head_dim):
    half_dim = head_dim // 2
    frequency = THETA ** (-jnp.arange(half_dim, dtype=F32) * 2.0 / head_dim)
    positions = (offset + jnp.arange(length, dtype=jnp.int32)).astype(F32)
    angles = positions[:, None] * frequency[None, :]
    return (jnp.cos(angles)[:, None, :], jnp.sin(angles)[:, None, :])


def rope_rows(length, head_dim):
    fine = math.gcd(length, LANES)
    frequency = THETA ** (-jnp.arange(head_dim // 2, dtype=F32) * 2.0 / head_dim)
    frequency = jnp.concatenate([frequency, frequency])
    coarse_angle = (jnp.arange(length // fine, dtype=F32) * fine)[:, None, None] * frequency
    fine_angle = jnp.arange(fine, dtype=F32)[None, :, None] * frequency
    cos_a, sin_a, cos_b, sin_b = lax.optimization_barrier(
        (jnp.cos(coarse_angle), jnp.sin(coarse_angle), jnp.cos(fine_angle), jnp.sin(fine_angle))
    )
    sign = jnp.where(jnp.arange(head_dim) < head_dim // 2, -1.0, 1.0)
    cos = cos_a * cos_b - sin_a * sin_b
    sin = (sin_a * cos_b + cos_a * sin_b) * sign
    return cos.reshape(length, head_dim), sin.reshape(length, head_dim)


def rotate(values, cos_table, sin_table):
    half_dim = values.shape[-1] // 2
    first = values[..., :half_dim]
    second = values[..., half_dim:]
    return jnp.concatenate(
        [first * cos_table - second * sin_table, second * cos_table + first * sin_table], axis=-1
    )


def dot_nn(a, b):
    return lax.dot_general(a, b, (((1,), (0,)), ((), ())), preferred_element_type=F32)


def dot_nt(a, b):
    return lax.dot_general(a, b, (((1,), (1,)), ((), ())), preferred_element_type=F32)


def dot_tn(a, b):
    return lax.dot_general(a, b, (((0,), (0,)), ((), ())), preferred_element_type=F32)


def key_chunks(length):
    size = min(512, length)
    return size, length // size


def attn_fwd_kernel(factor, q_ref, k_ref, v_ref, sq_ref, sk_ref, o_ref, of_ref, lse_ref, top_ref, vt_ref):
    length = k_ref.shape[1]
    size, count = key_chunks(length)
    tile, head_dim = q_ref.shape[1:]

    @pl.when(pl.program_id(1) == 0)
    def _():
        vt_ref[...] = v_ref[0].astype(F32).T.astype(BF16)

    q = q_ref[0]
    seg_q = sq_ref[...]

    def step(j, carried):
        total, top, acc = carried
        at = pl.multiple_of(j * size, size)
        scores = dot_nt(k_ref[0, pl.ds(at, size), :], q)
        scores = jnp.where(sk_ref[pl.ds(at, size), :] == seg_q, scores, NEG)
        top = jnp.maximum(top, jnp.max(scores, axis=0, keepdims=True))
        weights = jnp.exp2(scores * factor)
        total = total + jnp.sum(weights, axis=0, keepdims=True)
        acc = acc + dot_nn(vt_ref[:, pl.ds(at, size)], weights.astype(BF16))
        return total, top, acc

    start = (
        jnp.zeros((1, tile), F32),
        jnp.full((1, tile), NEG, F32),
        jnp.zeros((head_dim, tile), F32),
    )
    total, top, acc = lax.fori_loop(0, count, step, start, unroll=count <= 4)
    out = (acc * (1.0 / total)).T
    o_ref[0] = out.astype(BF16)
    of_ref[0] = out
    lse_ref[0] = jnp.log2(total)
    top_ref[0] = top


def attn_bwd_kernel(
    factor, scale, q_ref, k_ref, v_ref, do_ref, of_ref, lse_ref, sq_ref, sk_ref,
    dq_ref, dk_ref, dv_ref, kt_ref, dk_acc, dv_acc,
):
    length = k_ref.shape[1]
    size, count = key_chunks(length)
    tile, head_dim = q_ref.shape[1:]

    @pl.when(pl.program_id(1) == 0)
    def _():
        kt_ref[...] = k_ref[0].astype(F32).T.astype(BF16)
        dk_acc[...] = jnp.zeros_like(dk_acc)
        dv_acc[...] = jnp.zeros_like(dv_acc)

    q = q_ref[0]
    grad = do_ref[0]
    seg_q = sq_ref[...]
    lse = lse_ref[0]
    row_dot = jnp.sum((grad.astype(F32) * of_ref[0]).T, axis=0, keepdims=True)

    def step(j, dq_t):
        at = pl.multiple_of(j * size, size)
        rows = pl.ds(at, size)
        scores = dot_nt(k_ref[0, rows, :], q)
        scores = jnp.where(sk_ref[rows, :] == seg_q, scores, NEG)
        weights = jnp.exp2(scores * factor - lse)
        grad_weights = dot_nt(v_ref[0, rows, :], grad)
        grad_scores = (weights * (grad_weights - row_dot)).astype(BF16)
        dk_acc[rows, :] += dot_nn(grad_scores, q)
        dv_acc[rows, :] += dot_nn(weights.astype(BF16), grad)
        return dq_t + dot_nn(kt_ref[:, rows], grad_scores)

    dq_t = lax.fori_loop(0, count, step, jnp.zeros((head_dim, tile), F32), unroll=count <= 4)
    dq_ref[0] = (dq_t * scale).T.astype(BF16)

    @pl.when(pl.program_id(1) == pl.num_programs(1) - 1)
    def _():
        dk_ref[0] = (dk_acc[...] * scale).astype(BF16)
        dv_ref[0] = dv_acc[...].astype(BF16)


def attention_tile(queries, length):
    return min(queries, 256 if length <= 4096 else 128)


def attention_forward(q_src, kv_src, cols, seg_q, seg_k, head_dim):
    heads, queries = q_src.shape[:2]
    length = kv_src.shape[1]
    tile = attention_tile(queries, length)
    q_col, k_col, v_col = cols
    factor = head_dim**-0.5 * LOG2E
    row = pl.BlockSpec((1, 1, tile), lambda h, i: (h, 0, i))
    block = pl.BlockSpec((1, tile, head_dim), lambda h, i: (h, i, 0))
    return pl.pallas_call(
        functools.partial(attn_fwd_kernel, factor),
        grid=(heads, queries // tile),
        in_specs=[
            pl.BlockSpec((1, tile, head_dim), lambda h, i: (h, i, q_col)),
            pl.BlockSpec((1, length, head_dim), lambda h, i: (h, 0, k_col)),
            pl.BlockSpec((1, length, head_dim), lambda h, i: (h, 0, v_col)),
            pl.BlockSpec((1, tile), lambda h, i: (0, i)),
            pl.BlockSpec((length, 1), lambda h, i: (0, 0)),
        ],
        out_specs=[block, block, row, row],
        out_shape=[
            jax.ShapeDtypeStruct((heads, queries, head_dim), BF16),
            jax.ShapeDtypeStruct((heads, queries, head_dim), F32),
            jax.ShapeDtypeStruct((heads, 1, queries), F32),
            jax.ShapeDtypeStruct((heads, 1, queries), F32),
        ],
        scratch_shapes=[pltpu.VMEM((head_dim, length), BF16)],
        compiler_params=pltpu.CompilerParams(vmem_limit_bytes=VMEM_LIMIT),
        cost_estimate=pl.CostEstimate(
            flops=4 * heads * queries * length * head_dim,
            bytes_accessed=heads * (queries + length) * head_dim * 8,
            transcendentals=heads * queries * length,
        ),
        name="attend",
    )(q_src, kv_src, kv_src, seg_q.reshape(1, -1), seg_k.reshape(-1, 1))


def attention_backward(q_src, kv_src, cols, grad, out_f32, lse, seg_q, seg_k, head_dim):
    heads, queries = q_src.shape[:2]
    length = kv_src.shape[1]
    tile = attention_tile(queries, length)
    q_col, k_col, v_col = cols
    scale = head_dim**-0.5
    row = pl.BlockSpec((1, 1, tile), lambda h, i: (h, 0, i))
    block = pl.BlockSpec((1, tile, head_dim), lambda h, i: (h, i, 0))
    whole = pl.BlockSpec((1, length, head_dim), lambda h, i: (h, 0, 0))
    return pl.pallas_call(
        functools.partial(attn_bwd_kernel, scale * LOG2E, scale),
        grid=(heads, queries // tile),
        in_specs=[
            pl.BlockSpec((1, tile, head_dim), lambda h, i: (h, i, q_col)),
            pl.BlockSpec((1, length, head_dim), lambda h, i: (h, 0, k_col)),
            pl.BlockSpec((1, length, head_dim), lambda h, i: (h, 0, v_col)),
            block,
            block,
            row,
            pl.BlockSpec((1, tile), lambda h, i: (0, i)),
            pl.BlockSpec((length, 1), lambda h, i: (0, 0)),
        ],
        out_specs=[block, whole, whole],
        out_shape=[
            jax.ShapeDtypeStruct((heads, queries, head_dim), BF16),
            jax.ShapeDtypeStruct((heads, length, head_dim), BF16),
            jax.ShapeDtypeStruct((heads, length, head_dim), BF16),
        ],
        scratch_shapes=[
            pltpu.VMEM((head_dim, length), BF16),
            pltpu.VMEM((length, head_dim), F32),
            pltpu.VMEM((length, head_dim), F32),
        ],
        compiler_params=pltpu.CompilerParams(vmem_limit_bytes=VMEM_LIMIT),
        cost_estimate=pl.CostEstimate(
            flops=10 * heads * queries * length * head_dim,
            bytes_accessed=heads * (queries + length) * head_dim * 12,
            transcendentals=heads * queries * length,
        ),
        name="attend_back",
    )(q_src, kv_src, kv_src, grad, out_f32, lse, seg_q.reshape(1, -1), seg_k.reshape(-1, 1))


def expert_step(expert, h_ref, ht_ref, dy_ref, dyt_ref, gate_ref, wg_ref, wu_ref, wd_ref, dg_ref, out_acc, dx_acc):
    width = h_ref.shape[1]
    cols = wg_ref.shape[3]
    w_gate = wg_ref[...].reshape(width, cols)
    w_up = wu_ref[...].reshape(width, cols)
    w_down = wd_ref[...].reshape(width, cols)
    gates = gate_ref[...]
    mine = lax.broadcasted_iota(jnp.int32, gates.shape, 1) == expert
    gate = jnp.sum(jnp.where(mine, gates, 0.0), axis=1, keepdims=True)
    a_gate = dot_nn(h_ref[...], w_gate)
    a_up = dot_nn(h_ref[...], w_up)
    raw = dot_nn(dy_ref[...], w_down)
    sigma = 1.0 / (1.0 + jnp.exp2(a_gate * -LOG2E))
    swish = a_gate * sigma
    act = swish * a_up
    dg_ref[0] += jnp.sum(raw * act, axis=1, keepdims=True)
    gated = (gate * act).astype(BF16)
    d_act = gate * raw
    d_gate = (d_act * a_up * (sigma + swish * (1.0 - sigma))).astype(BF16)
    d_up = (d_act * swish).astype(BF16)
    out_acc[...] += dot_nt(gated, w_down)
    dx_acc[...] += dot_nt(d_gate, w_gate) + dot_nt(d_up, w_up)
    for part, (left, right) in enumerate([(ht_ref, d_gate), (ht_ref, d_up), (dyt_ref, gated)]):
        yield part, dot_nn(left[...], right).astype(BF16)


def expert_kernel(
    h_ref, ht_ref, dy_ref, dyt_ref, gate_ref, out0_ref, dx0_ref, wg_ref, wu_ref, wd_ref,
    out_ref, dx_ref, dg_ref, gr_ref, out_acc, dx_acc,
):
    step, last = pl.program_id(0), pl.num_programs(0) - 1
    parts, _, part_rows, cols = wg_ref.shape
    chunks = (last + 1) // gate_ref.shape[1]

    @pl.when(step == 0)
    def _():
        out_acc[...] = out0_ref[...].astype(F32)
        dx_acc[...] = dx0_ref[...].astype(F32)

    @pl.when(step % chunks == 0)
    def _():
        dg_ref[...] = jnp.zeros_like(dg_ref)

    for part, made in expert_step(
        step // chunks, h_ref, ht_ref, dy_ref, dyt_ref, gate_ref, wg_ref, wu_ref, wd_ref, dg_ref, out_acc, dx_acc
    ):
        gr_ref[:, part, 0] = made.reshape(parts, part_rows, cols)

    @pl.when(step == last)
    def _():
        out_ref[...] = out_acc[...].astype(BF16)
        dx_ref[...] = dx_acc[...].astype(BF16)


def expert_pair_kernel(
    h_ref, ht_ref, dy_ref, dyt_ref, gate_ref, out0_ref, dx0_ref, wg_ref, wu_ref, wd_ref,
    out_ref, dx_ref, dg_ref, gr_ref, out_acc, dx_acc, made_ref, got_ref, send, recv, free,
):
    step, last = pl.program_id(0), pl.num_programs(0) - 1
    parts, _, part_rows, cols = wg_ref.shape
    chunks = last // gate_ref.shape[1]
    core = lax.axis_index("core")
    near = {"core": 1 - core}
    slot, before = lax.rem(step, 2), lax.rem(step + 1, 2)

    @pl.when(step == 0)
    def _():
        barrier = pltpu.get_barrier_semaphore()
        pl.semaphore_signal(barrier, inc=1, device_id=near, device_id_type=MESH)
        pl.semaphore_wait(barrier, 1)
        out_acc[...] = out0_ref[...].astype(F32)
        dx_acc[...] = dx0_ref[...].astype(F32)

    def hand_over(at):
        return pltpu.make_async_remote_copy(
            src_ref=made_ref.at[at, 1 - core],
            dst_ref=got_ref.at[at],
            send_sem=send.at[at],
            recv_sem=recv.at[at],
            device_id=near,
            device_id_type=MESH,
        )

    @pl.when(step < last)
    def _():
        @pl.when(step % chunks == 0)
        def _():
            dg_ref[...] = jnp.zeros_like(dg_ref)

        for part, made in expert_step(
            step // chunks, h_ref, ht_ref, dy_ref, dyt_ref, gate_ref, wg_ref, wu_ref, wd_ref, dg_ref, out_acc, dx_acc
        ):
            made = made.reshape(parts // 2, 2, part_rows, cols)
            made_ref[slot, 0, :, part] = made[:, 0]
            made_ref[slot, 1, :, part] = made[:, 1]

        @pl.when(step >= 2)
        def _():
            pl.semaphore_wait(free, 1)

        hand_over(slot).start()

    @pl.when(step > 0)
    def _():
        hand_over(before).wait()
        total = made_ref[before, core].astype(F32) + got_ref[before].astype(F32)
        gr_ref[:, :, 0] = total.astype(BF16)

        @pl.when(step < last - 1)
        def _():
            pl.semaphore_signal(free, inc=1, device_id=near, device_id_type=MESH)

    @pl.when(step == last)
    def _():
        out_ref[...] = out_acc[...].astype(BF16)
        dx_ref[...] = dx_acc[...].astype(BF16)


def experts(hidden, hidden_t, grad, grad_t, gates, out, dx, weights, collective_id=None):
    tokens, width = hidden.shape
    parts, count, part_rows, units = weights.shape
    units = units // 3
    cols = min(256, units)
    chunks = units // cols
    steps = count * chunks
    paired = collective_id is not None
    held = parts // 2 if paired else parts
    once = pl.Buffered(1)
    whole = pl.BlockSpec((tokens, width), lambda s: (0, 0), pipeline_mode=once)
    whole_t = pl.BlockSpec((width, tokens), lambda s: (0, 0), pipeline_mode=once)
    result = pl.BlockSpec((tokens, width), lambda s: (0, 0))

    def now(step):
        return jnp.minimum(step, steps - 1)

    def written(step):
        return jnp.maximum(step - 1, 0) if paired else step

    def weight(kind):
        def index(step):
            at = now(step)
            return (0, at // chunks, 0, kind * chunks + at % chunks)

        return pl.BlockSpec((parts, 1, part_rows, cols), index)

    def grad_index(step):
        at = written(step)
        return (0, 0, at // chunks, 0, at % chunks)

    scratch = [pltpu.VMEM((tokens, width), F32), pltpu.VMEM((tokens, width), F32)]
    if paired:
        scratch += [
            pltpu.VMEM((2, 2, held, 3, part_rows, cols), BF16),
            pltpu.VMEM((2, held, 3, part_rows, cols), BF16),
            pltpu.SemaphoreType.DMA((2,)),
            pltpu.SemaphoreType.DMA((2,)),
            pltpu.SemaphoreType.REGULAR,
        ]
    return pl.pallas_call(
        expert_pair_kernel if paired else expert_kernel,
        grid=(steps + 1 if paired else steps,),
        in_specs=[
            whole,
            whole_t,
            whole,
            whole_t,
            pl.BlockSpec(gates.shape, lambda s: (0, 0), pipeline_mode=once),
            whole,
            whole,
            weight(0),
            weight(1),
            weight(2),
        ],
        out_specs=[
            result,
            result,
            pl.BlockSpec((1, tokens, 1), lambda s: (now(s) // chunks, 0, 0)),
            pl.BlockSpec((held, 3, 1, part_rows, cols), grad_index),
        ],
        out_shape=[
            jax.ShapeDtypeStruct((tokens, width), BF16),
            jax.ShapeDtypeStruct((tokens, width), BF16),
            jax.ShapeDtypeStruct((count, tokens, 1), F32),
            jax.ShapeDtypeStruct((held, 3, count, part_rows, units), BF16),
        ],
        scratch_shapes=scratch,
        compiler_params=pltpu.CompilerParams(
            vmem_limit_bytes=VMEM_LIMIT, collective_id=collective_id, has_side_effects=paired
        ),
        cost_estimate=pl.CostEstimate(
            flops=18 * count * tokens * width * units,
            bytes_accessed=12 * count * width * units,
            transcendentals=count * tokens * units,
        ),
        name="experts",
    )(hidden, hidden_t, grad, grad_t, gates, out, dx, weights, weights, weights)


def finish_experts_kernel(half, a_ref, b_ref, gate_up_ref, down_ref):
    units = down_ref.shape[2]

    def write(src):
        gate_up_ref[0, :, :units] = src[0, 0].astype(F32)
        gate_up_ref[0, :, units:] = src[1, 0].astype(F32)
        down_ref[0] = src[2, 0].astype(F32)

    pl.when(pl.program_id(0) < half)(lambda: write(a_ref))
    pl.when(pl.program_id(0) >= half)(lambda: write(b_ref))


def finish_experts(first, second):
    _, half, rows, units = first.shape
    count = half + second.shape[1]
    block = (3, 1, rows, units)
    return pl.pallas_call(
        functools.partial(finish_experts_kernel, half),
        grid=(count,),
        in_specs=[
            pl.BlockSpec(block, lambda e: (0, jnp.minimum(e, half - 1), 0, 0)),
            pl.BlockSpec(block, lambda e: (0, jnp.maximum(e - half, 0), 0, 0)),
        ],
        out_specs=[
            pl.BlockSpec((1, rows, 2 * units), lambda e: (e, 0, 0)),
            pl.BlockSpec((1, rows, units), lambda e: (e, 0, 0)),
        ],
        out_shape=[
            jax.ShapeDtypeStruct((count, rows, 2 * units), F32),
            jax.ShapeDtypeStruct((count, rows, units), F32),
        ],
        compiler_params=pltpu.CompilerParams(vmem_limit_bytes=VMEM_LIMIT),
        name="finish_experts",
    )(first, second)


def turn(values, cos, sin):
    return values * cos + pltpu.roll(values, values.shape[1] // 2, 1) * sin


def project_kernel(
    tok_ref, gain_ref, w_ref, cos_ref, sin_ref, gains_ref, hidden_ref, qkv_ref, raw_ref
):
    head_dim = cos_ref.shape[1]
    values = tok_ref[...].astype(F32)
    hidden = (values * rms_scale(values) * gain_ref[...]).astype(BF16)
    hidden_ref[...] = hidden
    projected = dot_nn(hidden, w_ref[...])
    raw_ref[...] = projected[:, : 2 * head_dim]
    for part in range(2):
        at = slice(part * head_dim, (part + 1) * head_dim)
        raw = projected[:, at]
        normed = raw * rms_scale(raw) * gains_ref[part : part + 1, :]
        qkv_ref[:, at] = turn(normed, cos_ref[...], sin_ref[...]).astype(BF16)
    qkv_ref[:, 2 * head_dim :] = projected[:, 2 * head_dim :].astype(BF16)


def project(toks, gain, weights, cos, sin, gains):
    length, width = toks.shape
    head_dim = cos.shape[1]
    tile = min(256, length)

    def rows(columns):
        return pl.BlockSpec((tile, columns), lambda i: (i, 0))

    def fixed(shape):
        return pl.BlockSpec(shape, lambda i: (0, 0))

    return pl.pallas_call(
        project_kernel,
        grid=(length // tile,),
        in_specs=[
            rows(width),
            fixed((1, width)),
            fixed(weights.shape),
            rows(head_dim),
            rows(head_dim),
            fixed(gains.shape),
        ],
        out_specs=[rows(width), rows(3 * head_dim), rows(2 * head_dim)],
        out_shape=[
            jax.ShapeDtypeStruct((length, width), BF16),
            jax.ShapeDtypeStruct((length, 3 * head_dim), BF16),
            jax.ShapeDtypeStruct((length, 2 * head_dim), F32),
        ],
        compiler_params=pltpu.CompilerParams(vmem_limit_bytes=VMEM_LIMIT),
        name="project",
    )(toks, gain, weights, cos, sin, gains)


def project_back_kernel(
    factor, scale, q_ref, k_ref, v_ref, do_ref, of_ref, lse_ref, sq_ref, sk_ref,
    raw_q_ref, raw_k_ref, cos_q_ref, sin_q_ref, cos_ref, sin_ref, gains_ref,
    dp_ref, dgain_ref, kt_ref, dk_acc, dv_acc,
):
    length, head_dim = k_ref.shape
    size, count = key_chunks(length)
    tile = q_ref.shape[0]
    step_at = pl.program_id(0)

    @pl.when(step_at == 0)
    def _():
        kt_ref[...] = k_ref[...].astype(F32).T.astype(BF16)
        dk_acc[...] = jnp.zeros_like(dk_acc)
        dv_acc[...] = jnp.zeros_like(dv_acc)
        dgain_ref[...] = jnp.zeros_like(dgain_ref)

    def to_raw(part, grad, raw, cos, sin):
        grad = turn(grad.astype(BF16).astype(F32), cos, -sin)
        raw_scale = rms_scale(raw)
        dgain_ref[part : part + 1, :] += jnp.sum(grad * (raw * raw_scale), axis=0, keepdims=True)
        return norm_back(grad * gains_ref[part : part + 1, :], raw, raw_scale).astype(BF16)

    q = q_ref[...]
    grad = do_ref[...]
    seg_q = sq_ref[...]
    lse = lse_ref[0]
    row_dot = jnp.sum((grad.astype(F32) * of_ref[0]).T, axis=0, keepdims=True)
    dq_t = jnp.zeros((head_dim, tile), F32)
    for j in range(count):
        rows = slice(j * size, (j + 1) * size)
        scores = dot_nt(k_ref[rows, :], q)
        scores = jnp.where(sk_ref[rows, :] == seg_q, scores, NEG)
        weights = jnp.exp2(scores * factor - lse)
        grad_weights = dot_nt(v_ref[rows, :], grad)
        grad_scores = (weights * (grad_weights - row_dot)).astype(BF16)
        dk_acc[rows, :] += dot_nn(grad_scores, q)
        dv_acc[rows, :] += dot_nn(weights.astype(BF16), grad)
        dq_t = dq_t + dot_nn(kt_ref[:, rows], grad_scores)
    own = pl.ds(pl.multiple_of(step_at * tile, tile), tile)
    dp_ref[own, :head_dim] = to_raw(
        0, (dq_t * scale).T, raw_q_ref[...], cos_q_ref[...], sin_q_ref[...]
    )

    @pl.when(step_at == pl.num_programs(0) - 1)
    def _():
        dp_ref[:, head_dim : 2 * head_dim] = to_raw(
            1, dk_acc[...] * scale, raw_k_ref[...], cos_ref[...], sin_ref[...]
        )
        dp_ref[:, 2 * head_dim :] = dv_acc[...].astype(BF16)


def project_back(qkv, grad, out_f32, lse, segments, raw, cos, sin, gains):
    length, head_dim = grad.shape
    tile = min(256, length)

    def rows(column):
        return pl.BlockSpec((tile, head_dim), lambda i: (i, column))

    def whole(column):
        return pl.BlockSpec((length, head_dim), lambda i: (0, column))

    return pl.pallas_call(
        functools.partial(project_back_kernel, head_dim**-0.5 * LOG2E, head_dim**-0.5),
        grid=(length // tile,),
        in_specs=[
            rows(0),
            whole(1),
            whole(2),
            rows(0),
            pl.BlockSpec((1, tile, head_dim), lambda i: (0, i, 0)),
            pl.BlockSpec((1, 1, tile), lambda i: (0, 0, i)),
            pl.BlockSpec((1, tile), lambda i: (0, i)),
            pl.BlockSpec((length, 1), lambda i: (0, 0)),
            rows(0),
            whole(1),
            rows(0),
            rows(0),
            whole(0),
            whole(0),
            pl.BlockSpec(gains.shape, lambda i: (0, 0)),
        ],
        out_specs=[
            pl.BlockSpec((length, 3 * head_dim), lambda i: (0, 0)),
            pl.BlockSpec((2, head_dim), lambda i: (0, 0)),
        ],
        out_shape=[
            jax.ShapeDtypeStruct((length, 3 * head_dim), BF16),
            jax.ShapeDtypeStruct((2, head_dim), F32),
        ],
        scratch_shapes=[
            pltpu.VMEM((head_dim, length), BF16),
            pltpu.VMEM((length, head_dim), F32),
            pltpu.VMEM((length, head_dim), F32),
        ],
        compiler_params=pltpu.CompilerParams(vmem_limit_bytes=VMEM_LIMIT),
        cost_estimate=pl.CostEstimate(
            flops=10 * length * length * head_dim,
            bytes_accessed=length * head_dim * 40,
            transcendentals=length * length,
        ),
        name="project_back",
    )(
        qkv, qkv, qkv, grad, out_f32, lse, segments.reshape(1, -1), segments.reshape(-1, 1),
        raw, raw, cos, sin, cos, sin, gains,
    )


def merge_heads_kernel(parts_ref, out_ref):
    batch, blk, uly, _, columns = parts_ref.shape
    head_dim = columns // 3
    heads = blk * uly
    for z in range(blk):
        for u in range(uly):
            total = parts_ref[0, z, u].astype(F32)
            for b in range(1, batch):
                total = total + parts_ref[b, z, u].astype(F32)
            for part in range(3):
                at = (part * heads + u * blk + z) * head_dim
                out_ref[:, at : at + head_dim] = total[:, part * head_dim : (part + 1) * head_dim]


def merge_heads(parts):
    _, blk, uly, rows, columns = parts.shape
    return pl.pallas_call(
        merge_heads_kernel,
        out_shape=jax.ShapeDtypeStruct((rows, blk * uly * columns), F32),
        compiler_params=pltpu.CompilerParams(vmem_limit_bytes=VMEM_LIMIT),
        name="merge_heads",
    )(parts)


def swap(values, axis):
    return lax.all_to_all(values, axis, split_axis=0, concat_axis=0, tiled=True)


def sum_scatter(values, axis):
    count = spread(axis) if isinstance(axis, tuple) else lax.axis_size(axis)
    rows, width = values.shape
    parts = swap(values.astype(BF16).reshape(count, rows // count, width), axis)
    return jnp.sum(parts.astype(F32), axis=0)


def place(axes, index):
    found = {}
    for axis in reversed(axes):
        size = lax.axis_size(axis)
        found[axis] = lax.rem(index, size)
        index = index // size
    return found


def spread(axes):
    return math.prod(lax.axis_size(axis) for axis in axes)


def each(count, body):
    if count <= 4:
        for step in range(1, count):
            body(step)
    else:

        def looped(step, carried):
            body(step)
            return carried

        lax.fori_loop(1, count, looped, 0)


def ahead(index, step, size):
    return lax.rem(index + step, size)


def exchange(items, collective_id, after=()):
    count = len(items)
    sizes = [spread(axes) for _, axes, _ in items]
    groups = list(dict.fromkeys(axes for _, axes, _ in items))
    bases = [sum(sizes[:i]) for i in range(count)]

    def kernel(*refs):
        ins = refs[:count]
        outs = refs[count + len(after) : 2 * count + len(after)]
        send, recv, local = refs[-3:]
        barrier = pltpu.get_barrier_semaphore()
        for axes in groups:
            size, me = spread(axes), lax.axis_index(axes)

            def greet(step, axes=axes, size=size, me=me):
                pl.semaphore_signal(
                    barrier, inc=1, device_id=place(axes, ahead(me, step, size)), device_id_type=MESH
                )

            each(size, greet)
        pl.semaphore_wait(barrier, sum(spread(axes) - 1 for axes in groups))

        def remote(i, step):
            _, axes, kind = items[i]
            me = lax.axis_index(axes)
            if kind == "relay":
                far, near = lax.rem(me + 2, 4), me + 1 - 2 * lax.rem(me, 2)
                held = far if step == 3 else me
                return pltpu.make_async_remote_copy(
                    src_ref=outs[i].at[far] if step == 3 else ins[i],
                    dst_ref=outs[i].at[held],
                    send_sem=send.at[bases[i] + step],
                    recv_sem=recv.at[bases[i] + step],
                    device_id=place(axes, far if step == 1 else near),
                    device_id_type=MESH,
                )
            peer = ahead(me, step, sizes[i])
            return pltpu.make_async_remote_copy(
                src_ref=ins[i].at[peer] if kind == "swap" else ins[i],
                dst_ref=outs[i].at[me],
                send_sem=send.at[bases[i] + step],
                recv_sem=recv.at[bases[i] + step],
                device_id=place(axes, peer),
                device_id_type=MESH,
            )

        def own(i):
            _, axes, kind = items[i]
            me = lax.axis_index(axes)
            return pltpu.make_async_copy(
                ins[i].at[me] if kind == "swap" else ins[i], outs[i].at[me], local.at[i]
            )

        relays = [i for i in range(count) if items[i][2] == "relay"]
        for i in range(count):
            each(3 if i in relays else sizes[i], lambda step, i=i: remote(i, step).start())
        for i in range(count):
            own(i).start()
        for i in relays:
            remote(i, 1).wait_recv()
            remote(i, 3).start()
            remote(i, 1).wait_send()
            for step in (2, 3):
                remote(i, step).wait()
        for i in range(count):
            if i not in relays:
                each(sizes[i], lambda step, i=i: remote(i, step).wait())
        for i in range(count):
            own(i).wait()

    shapes = [
        (size, *(array.shape[1:] if kind == "swap" else array.shape))
        for size, (array, _, kind) in zip(sizes, items)
    ]
    anywhere = pl.BlockSpec(memory_space=pl.ANY)
    return pl.pallas_call(
        kernel,
        in_specs=[anywhere] * (count + len(after)),
        out_specs=[anywhere] * count,
        out_shape=[jax.ShapeDtypeStruct(shape, item[0].dtype) for shape, item in zip(shapes, items)],
        scratch_shapes=[
            pltpu.SemaphoreType.DMA((sum(sizes),)),
            pltpu.SemaphoreType.DMA((sum(sizes),)),
            pltpu.SemaphoreType.DMA((count,)),
        ],
        compiler_params=pltpu.CompilerParams(collective_id=collective_id, has_side_effects=True),
        name="exchange",
    )(*[item[0] for item in items], *after)


def startup_kernel(
    head_ref, extra_ref, tok_ref, heads_ref, extras_ref, toks_ref,
    head_send, head_recv, extra_send, extra_recv,
    az_send, az_recv, ay_send, ay_recv, by_send, by_recv, bz_send, bz_recv, c_send, c_recv, local,
):
    blk, uly = lax.axis_size("blk"), spread(ULY)
    total = spread(ALL)
    z, u, me = lax.axis_index("blk"), lax.axis_index(ULY), lax.axis_index(ALL)
    far = lax.rem(u + 2, uly)
    near = u + 1 - 2 * lax.rem(u, 2)
    half = tok_ref.shape[0] // 2
    parts = (pl.ds(0, half), pl.ds(half, half))

    barrier = pltpu.get_barrier_semaphore()

    def greet(step):
        pl.semaphore_signal(
            barrier, inc=1, device_id=place(ALL, ahead(me, step, total)), device_id_type=MESH
        )

    each(total, greet)
    pl.semaphore_wait(barrier, total - 1)

    def send(src, dst, sent, got, to):
        return pltpu.make_async_remote_copy(
            src_ref=src, dst_ref=dst, send_sem=sent, recv_sem=got, device_id=to, device_id_type=MESH
        )

    def block(step, other, part):
        at = toks_ref.at[ahead(z, step, blk), far if other else u, parts[part]]
        return (tok_ref.at[parts[part]] if step == 0 and not other else at), at

    def along(step):
        return {"blk": ahead(z, step, blk)}

    def a_z(step):
        return send(*block(0, 0, 0), az_send.at[step], az_recv.at[step], along(step))

    def a_y(step):
        return send(*block(step, 0, 0), ay_send.at[step], ay_recv.at[step], place(ULY, far))

    def b_y():
        return send(*block(0, 0, 1), by_send.at[0], by_recv.at[0], place(ULY, far))

    def b_z(step, other):
        sem = 2 * step + other
        return send(*block(0, other, 1), bz_send.at[sem], bz_recv.at[sem], along(step))

    def to_near(step, other, part):
        sem = 4 * step + 2 * other + part
        return send(*block(step, other, part), c_send.at[sem], c_recv.at[sem], place(ULY, near))

    def head(step):
        to = place(ALL, ahead(me, step, total))
        src = head_ref.at[(to["y"] * lax.axis_size("core") + to["core"]) * blk + to["blk"]]
        return send(src, heads_ref.at[me], head_send.at[step], head_recv.at[step], to)

    def extra(step):
        to = place(ALL, ahead(me, step, total))
        return send(extra_ref, extras_ref.at[me], extra_send.at[step], extra_recv.at[step], to)

    own = [
        pltpu.make_async_copy(tok_ref, toks_ref.at[z, u], local.at[0]),
        pltpu.make_async_copy(head_ref.at[u * blk + z], heads_ref.at[me], local.at[1]),
        pltpu.make_async_copy(extra_ref, extras_ref.at[me], local.at[2]),
    ]

    b_y().start()
    for step in range(1, blk):
        a_z(step).start()
        b_z(step, 0).start()
    a_y(0).start()
    to_near(0, 0, 0).start()
    to_near(0, 0, 1).start()

    def start_head(step):
        extra(step).start()
        head(step).start()

    each(total, start_head)
    for copy in own:
        copy.start()
    b_y().wait_recv()
    for step in range(1, blk):
        b_z(step, 1).start()
    to_near(0, 1, 1).start()
    for step in range(1, blk):
        a_z(step).wait_recv()
        a_y(blk - step).start()
        to_near(blk - step, 0, 0).start()
    for step in range(1, blk):
        b_z(step, 0).wait_recv()
        to_near(blk - step, 0, 1).start()
    for step in [0, *reversed(range(1, blk))]:
        a_y(step).wait_recv()
        to_near(step, 1, 0).start()
    for step in range(1, blk):
        b_z(step, 1).wait_recv()
        to_near(blk - step, 1, 1).start()
    for step in range(blk):
        for other in range(2):
            for part in range(2):
                to_near(step, other, part).wait_recv()

    def wait_head(step):
        extra(step).wait()
        head(step).wait()

    each(total, wait_head)
    for copy in own:
        copy.wait()
    b_y().wait_send()
    for step in range(blk):
        a_y(step).wait_send()
        if step:
            a_z(step).wait_send()
            for other in range(2):
                b_z(step, other).wait_send()
        for other in range(2):
            for part in range(2):
                to_near(step, other, part).wait_send()


def startup(heads, extra, tok, collective_id):
    blk, uly, total = lax.axis_size("blk"), spread(ULY), spread(ALL)
    anywhere = pl.BlockSpec(memory_space=pl.ANY)
    dma = pltpu.SemaphoreType.DMA
    return pl.pallas_call(
        startup_kernel,
        in_specs=[anywhere] * 3,
        out_specs=[anywhere] * 3,
        out_shape=[
            jax.ShapeDtypeStruct((total, *heads.shape[1:]), BF16),
            jax.ShapeDtypeStruct((total, *extra.shape), BF16),
            jax.ShapeDtypeStruct((blk, uly, *tok.shape), BF16),
        ],
        scratch_shapes=[
            *[dma((total,))] * 4,
            *[dma((blk,))] * 4,
            *[dma((1,))] * 2,
            *[dma((2 * blk,))] * 2,
            *[dma((4 * blk,))] * 2,
            dma((3,)),
        ],
        compiler_params=pltpu.CompilerParams(collective_id=collective_id, has_side_effects=True),
        name="startup",
    )(heads, extra, tok)


def per_device_general(
    tokens, segments, routes, w_qkv, w_out, attn_gain, ffn_gain, qk_gain, router, w_gate_up, w_down, cotangent
):
    own_tokens = tokens[0]
    own_grad = cotangent[0]
    count_tok, width = own_tokens.shape
    head_dim = qk_gain.shape[1]
    heads = width // head_dim
    uly, blk, batch = spread(ULY), lax.axis_size("blk"), lax.axis_size("batch")
    blk_at, uly_at = lax.axis_index("blk"), lax.axis_index(ULY)
    group = batch * blk
    local_heads = heads // uly
    local_width = local_heads * head_dim
    rows = count_tok * uly
    seg_row = segments[0]
    length = seg_row.shape[0]
    number = router.shape[1]
    local_experts, _, units = w_down.shape
    shard_rows = w_qkv.shape[0]

    extra = jnp.concatenate([attn_gain[:, None], ffn_gain[:, None], router], axis=1)
    extra = jnp.pad(extra, ((0, 0), (0, LANES - extra.shape[1])))
    columns = w_qkv.reshape(shard_rows, 3, uly, local_width).transpose(2, 0, 1, 3)
    packed = jnp.concatenate(
        [
            columns.reshape(uly, shard_rows, 3 * local_width),
            jnp.broadcast_to(extra[None], (uly, shard_rows, LANES)),
        ],
        axis=2,
    )
    packed = swap(packed, ULY).reshape(uly * shard_rows, 3 * local_width + LANES)
    packed = lax.all_gather(packed, ROWS, axis=0, tiled=True)
    own_qkv = packed[:, : 3 * local_width]
    gain_attn = packed[:, 3 * local_width].astype(F32)
    gain_ffn = packed[:, 3 * local_width + 1].astype(F32)
    whole_router = packed[:, 3 * local_width + 2 : 3 * local_width + 2 + number]
    tokens_all = lax.all_gather(own_tokens, ULY, axis=0, tiled=True)
    to_rows = [(u * group + g, g * uly + u) for g in range(group) for u in range(uly)]
    own_out = lax.all_gather(lax.ppermute(w_out, ALL, to_rows), ROWS, axis=0, tiled=True)
    whole_gate_up = lax.all_gather(w_gate_up, PLANE, axis=0, tiled=False)
    whole_down = lax.all_gather(w_down, PLANE, axis=0, tiled=False)
    grad_blk = lax.all_gather(own_grad, "blk", axis=0, tiled=True)
    routes_blk = lax.all_gather(routes[0], "blk", axis=0, tiled=True)

    gain_query = qk_gain[0].astype(F32)
    gain_key = qk_gain[1].astype(F32)
    inputs_all = tokens_all.astype(F32)
    normed_one = inputs_all * rms_scale(inputs_all)
    hidden_one = (normed_one * gain_attn).astype(BF16)
    projected = dot_nn(hidden_one, own_qkv)
    query_raw = projected[:, :local_width].reshape(rows, local_heads, head_dim)
    key_raw = projected[:, local_width : 2 * local_width].reshape(rows, local_heads, head_dim)
    value_raw = projected[:, 2 * local_width :].reshape(rows, local_heads, head_dim)
    cos_table, sin_table = rope_tables(blk_at * rows, rows, head_dim)
    query_scale = rms_scale(query_raw)
    key_scale = rms_scale(key_raw)
    qkv = jnp.concatenate(
        [
            rotate(query_raw * query_scale * gain_query, cos_table, sin_table),
            rotate(key_raw * key_scale * gain_key, cos_table, sin_table),
            value_raw,
        ],
        axis=2,
    ).astype(BF16)
    qkv = qkv.transpose(1, 0, 2)

    by_heads = local_heads % blk == 0
    if by_heads:
        per = local_heads // blk

        def to_heads(values):
            columns = values.shape[2]
            moved = swap(values.reshape(blk, per, rows, columns), "blk")
            return moved.transpose(1, 0, 2, 3).reshape(per, length, columns)

        def to_rows_back(values):
            columns = values.shape[2]
            parts = values.reshape(per, blk, rows, columns).transpose(1, 0, 2, 3)
            return swap(parts, "blk").reshape(local_heads, rows, columns)

        q_src = kv_src = to_heads(qkv)
        cols = (0, 1, 2)
        seg_q = seg_row
        first_head = uly_at * local_heads + blk_at * per
    else:

        def to_heads(values):
            return values

        def to_rows_back(values):
            return values

        q_src = qkv
        kv_src = lax.all_gather(qkv[:, :, head_dim:], "blk", axis=1, tiled=True)
        cols = (0, 0, 1)
        seg_q = lax.dynamic_slice_in_dim(seg_row, blk_at * rows, rows)
        first_head = uly_at * local_heads
    attn_low, attn_f32, lse, top = attention_forward(q_src, kv_src, cols, seg_q, seg_row, head_dim)
    head_vector = lax.dynamic_update_slice_in_dim(
        jnp.full((heads,), NEG, F32), jnp.max(top, axis=(1, 2)) * head_dim**-0.5, first_head, 0
    )
    head_max = lax.pmax(head_vector, ALL)
    attn_rows = to_rows_back(attn_low)
    out_heads = own_out.reshape(local_heads, head_dim, width)
    branch = jnp.einsum("htc,hcd->td", attn_rows, out_heads, preferred_element_type=F32)
    inputs = own_tokens.astype(F32)
    mid = inputs + sum_scatter(branch, ULY)

    scale_two = rms_scale(mid)
    normed_two = mid * scale_two
    hidden_two = (normed_two * gain_ffn).astype(BF16)
    hidden_blk = lax.all_gather(hidden_two, "blk", axis=0, tiled=True)
    probs_blk = jax.nn.softmax(dot_nn(hidden_blk, whole_router), axis=1)
    names = jnp.arange(number, dtype=jnp.int32)
    chosen_blk = jnp.any(routes_blk[:, :, None] == names, axis=1).astype(F32)
    own_names = blk_at * local_experts
    gates = lax.dynamic_slice_in_dim(probs_blk * chosen_blk, own_names, local_experts, axis=1)
    most = min(MOST_TOKENS, hidden_blk.shape[0])
    nothing = jnp.zeros((most, width), BF16)
    packed_weights = jnp.concatenate([whole_gate_up, whole_down], axis=3)
    made = []
    for at in range(0, hidden_blk.shape[0], most):
        hidden_part, grad_part = hidden_blk[at : at + most], grad_blk[at : at + most]
        made.append(
            experts(
                hidden_part,
                hidden_part.T,
                grad_part,
                grad_part.T,
                gates[at : at + most],
                nothing,
                nothing,
                packed_weights,
            )
        )
    out_part = jnp.concatenate([m[0] for m in made], axis=0)
    dx_part = jnp.concatenate([m[1] for m in made], axis=0)
    dg_part = jnp.concatenate([m[2] for m in made], axis=1)
    expert_grads = sum(m[3].astype(F32) for m in made).astype(BF16)
    expert_sums = lax.psum_scatter(expert_grads, PLANE, scatter_dimension=0, tiled=False).astype(F32)
    grad_gate_up = jnp.concatenate([expert_sums[0], expert_sums[1]], axis=2)
    grad_down = expert_sums[2]
    dg_parts = swap(dg_part.reshape(local_experts, blk, count_tok).transpose(1, 2, 0), "blk")
    grad_gates = dg_parts.transpose(1, 0, 2).reshape(count_tok, number)
    dx_sum = sum_scatter(dx_part, "blk")
    output = (mid + sum_scatter(out_part, "blk")).astype(BF16)
    router_probs = lax.dynamic_slice_in_dim(probs_blk, blk_at * count_tok, count_tok)
    chosen = lax.dynamic_slice_in_dim(chosen_blk, blk_at * count_tok, count_tok)
    grad_probs = chosen * grad_gates
    grad_logits = (
        router_probs * (grad_probs - jnp.sum(router_probs * grad_probs, axis=1, keepdims=True))
    ).astype(BF16)
    grad_hidden_two = dx_sum + dot_nt(grad_logits, whole_router)
    grad_router_part = dot_tn(hidden_two, grad_logits)
    grad_gain_ffn = jnp.sum(grad_hidden_two * normed_two, axis=0)
    grad_mid = own_grad.astype(F32) + norm_back(grad_hidden_two * gain_ffn, mid, scale_two)

    branch_grad = lax.all_gather(grad_mid.astype(BF16), ULY, axis=0, tiled=True)
    grad_attn = dot_nt(branch_grad, own_out).astype(BF16)
    grad_attn = to_heads(grad_attn.reshape(rows, local_heads, head_dim).transpose(1, 0, 2))
    grad_out_part = jnp.einsum("htc,td->hcd", attn_rows, branch_grad, preferred_element_type=F32)
    dq, dk, dv = attention_backward(
        q_src, kv_src, cols, grad_attn, attn_f32, lse, seg_q, seg_row, head_dim
    )
    if by_heads:
        dqkv = to_rows_back(jnp.concatenate([dq, dk, dv], axis=2))
        dq, dk, dv = jnp.split(dqkv, 3, axis=2)
    else:
        dk, dv = (lax.psum_scatter(g, "blk", scatter_dimension=1, tiled=True) for g in (dk, dv))
    dq, dk, dv = (g.transpose(1, 0, 2) for g in (dq, dk, dv))
    grad_query_norm = rotate(dq.astype(F32), cos_table, -sin_table)
    grad_key_norm = rotate(dk.astype(F32), cos_table, -sin_table)
    grad_gain_query = jnp.sum(grad_query_norm * (query_raw * query_scale), axis=(0, 1))
    grad_gain_key = jnp.sum(grad_key_norm * (key_raw * key_scale), axis=(0, 1))
    grad_projected = jnp.concatenate(
        [
            norm_back(grad_query_norm * gain_query, query_raw, query_scale)
            .reshape(rows, local_width)
            .astype(BF16),
            norm_back(grad_key_norm * gain_key, key_raw, key_scale)
            .reshape(rows, local_width)
            .astype(BF16),
            dv.reshape(rows, local_width),
        ],
        axis=1,
    )
    grad_hidden_part = dot_nt(grad_projected, own_qkv)
    grad_hidden_one = sum_scatter(grad_hidden_part, ULY)
    grad_gain_attn = jnp.sum(grad_hidden_part * normed_one, axis=0)
    grad_inputs = grad_mid + norm_back(grad_hidden_one * gain_attn, inputs, rms_scale(inputs))

    grad_qkv_part = dot_tn(hidden_one, grad_projected).astype(BF16)
    grad_qkv_rows = lax.psum_scatter(grad_qkv_part, ROWS, scatter_dimension=0, tiled=True)
    grad_qkv_rows = swap(grad_qkv_rows.reshape(uly, shard_rows, 3 * local_width), ULY)
    grad_qkv = (
        grad_qkv_rows.reshape(uly, shard_rows, 3, local_width)
        .transpose(1, 2, 0, 3)
        .reshape(shard_rows, 3 * width)
        .astype(F32)
    )
    grad_out_rows = lax.psum_scatter(
        grad_out_part.reshape(local_width, width).astype(BF16), ROWS, scatter_dimension=0, tiled=True
    )
    grad_out = lax.ppermute(grad_out_rows, ALL, [(b, a) for a, b in to_rows]).astype(F32)
    small = jnp.concatenate([grad_gain_attn[:, None], grad_gain_ffn[:, None], grad_router_part], axis=1)
    small = lax.psum_scatter(small, ALL, scatter_dimension=0, tiled=True)
    grad_qk_gain = lax.psum(jnp.stack([grad_gain_query, grad_gain_key]), ALL)

    clip_gamma = TAU / jnp.maximum(head_max, TAU)
    factor = jnp.repeat(jnp.sqrt(clip_gamma), head_dim)
    column_scale = jnp.concatenate([factor, factor, jnp.ones((width,), F32)])
    clipped = w_qkv.astype(F32) * column_scale[None, :]
    return (
        output[None],
        grad_inputs[None],
        grad_qkv,
        grad_out,
        small[:, 0],
        small[:, 1],
        grad_qk_gain,
        small[:, 2:],
        grad_gate_up,
        grad_down,
        clipped,
    )


def per_device(
    tokens, segments, routes, w_qkv, w_out, attn_gain, ffn_gain, qk_gain, router, w_gate_up, w_down, cotangent
):
    own_tokens = tokens[0]
    own_grad = cotangent[0]
    count_tok, width = own_tokens.shape
    head_dim = qk_gain.shape[1]
    heads = width // head_dim
    batch, blk, uly = lax.axis_size("batch"), lax.axis_size("blk"), spread(ULY)
    total, group = batch * blk * uly, batch * blk
    local_experts = w_down.shape[0]
    if uly != 4 or heads != blk * uly or local_experts % 2:
        return per_device_general(
            tokens, segments, routes, w_qkv, w_out, attn_gain, ffn_gain, qk_gain, router, w_gate_up, w_down, cotangent
        )
    blk_at, uly_at = lax.axis_index("blk"), lax.axis_index(ULY)
    rows = count_tok * uly
    seg_row = segments[0]
    length = seg_row.shape[0]
    number = router.shape[1]
    shard_rows = w_qkv.shape[0]

    to_rows = [(u * group + g, g * uly + u) for g in range(group) for u in range(uly)]
    own_rows = lax.ppermute(w_out, ALL, to_rows)
    half = local_experts // 2
    weights_first, weights_second = (
        lax.all_gather(jnp.concatenate([w_gate_up[at], w_down[at]], axis=2), PLANE, axis=0, tiled=False)
        for at in (slice(0, half), slice(half, local_experts))
    )
    extra = jnp.concatenate([attn_gain[None], ffn_gain[None], router.T], axis=0)
    kept = extra.shape[0]
    extra = jnp.pad(extra, ((0, -kept % 16), (0, -shard_rows % LANES)))
    by_head = w_qkv.reshape(shard_rows, 3, heads, head_dim).transpose(2, 0, 1, 3)
    own_qkv, extras, toks = startup(
        by_head.reshape(heads, shard_rows, 3 * head_dim), extra, own_tokens, 0
    )
    own_rows, extras = lax.optimization_barrier((own_rows, extras))
    own_out = lax.all_to_all(
        jnp.broadcast_to(own_rows[None], (group, *own_rows.shape)), ROWS, split_axis=0, concat_axis=0, tiled=True
    ).reshape(blk, head_dim, width)
    own_qkv = own_qkv.reshape(width, 3 * head_dim)
    extras = extras[:, :kept, :shard_rows].transpose(1, 0, 2).reshape(kept, width)
    gain_attn = extras[0].astype(F32)
    gain_ffn = extras[1].astype(F32)
    router_t = extras[2:]

    gains = qk_gain.astype(F32)
    cos, sin = rope_rows(length, head_dim)
    hidden_one, qkv, raw = project(
        toks.reshape(length, width), gain_attn[None], own_qkv, cos, sin, gains
    )
    attn_low, attn_f32, lse, top = attention_forward(
        qkv[None], qkv[None], (0, 1, 2), seg_row, seg_row, head_dim
    )
    (attn_rows,) = exchange([(attn_low.reshape(blk, rows, head_dim), ("blk",), "swap")], 1)
    branch = jnp.einsum("htc,hcd->td", attn_rows, own_out, preferred_element_type=F32)
    branch, grad_blk, routes_blk = exchange(
        [
            (branch.astype(BF16).reshape(uly, count_tok, width), ULY, "swap"),
            (own_grad, ("blk",), "gather"),
            (routes[0].T, ("blk",), "gather"),
        ],
        2,
    )
    inputs = own_tokens.astype(F32)
    mid = inputs + jnp.sum(branch.astype(F32), axis=0)

    scale_two = rms_scale(mid)
    normed_two = mid * scale_two
    hidden_two = (normed_two * gain_ffn).astype(BF16)
    (hidden_blk,) = exchange([(hidden_two, ("blk",), "gather")], 3, after=[weights_first])
    tokens_blk = blk * count_tok
    hidden_blk = hidden_blk.reshape(tokens_blk, width)
    grad_blk = grad_blk.reshape(tokens_blk, width)
    probs_blk = jax.nn.softmax(dot_nt(hidden_blk, router_t), axis=1)
    names = jnp.arange(number, dtype=jnp.int32)
    chosen_blk = jnp.any(routes_blk[:, :, :, None] == names, axis=1).astype(F32)
    chosen_blk = chosen_blk.reshape(tokens_blk, number)
    gates = lax.dynamic_slice_in_dim(
        probs_blk * chosen_blk, blk_at * local_experts, local_experts, axis=1
    )
    nothing = jnp.zeros((tokens_blk, width), BF16)
    shared = (hidden_blk, hidden_blk.T, grad_blk, grad_blk.T)
    out_first, dx_first, dg_first, grads_first = experts(
        *shared, gates[:, :half], nothing, nothing, weights_first, collective_id=9
    )
    first_sums = lax.psum_scatter(grads_first, CHIPS, scatter_dimension=0, tiled=False)
    out_part, dx_part, dg_second, grads_second = experts(
        *shared, gates[:, half:], out_first, dx_first, weights_second, collective_id=10
    )
    second_sums = lax.psum_scatter(grads_second, CHIPS, scatter_dimension=0, tiled=False)
    grad_gate_up, grad_down = finish_experts(first_sums, second_sums)
    dg_part = jnp.concatenate([dg_first, dg_second], axis=0).reshape(local_experts, blk, count_tok)
    dx_parts, dg_parts = exchange(
        [
            (dx_part.reshape(blk, count_tok, width), ("blk",), "swap"),
            (dg_part.transpose(1, 0, 2), ("blk",), "swap"),
        ],
        4,
    )
    out_part = out_part.reshape(blk, count_tok, width)
    out_part, sent_qkv, dx_parts = lax.optimization_barrier((out_part, own_qkv, dx_parts))
    out_parts = lax.all_to_all(out_part, "blk", split_axis=0, concat_axis=0, tiled=True)
    output = (mid + jnp.sum(out_parts.astype(F32), axis=0)).astype(BF16)
    to_far = [(u, (u + 2) % uly) for u in range(uly)]
    to_near = [(u, u ^ 1) for u in range(uly)]
    far_qkv = lax.ppermute(sent_qkv, ULY, to_far)
    near_qkv = lax.ppermute(sent_qkv, ULY, to_near)
    cross_qkv = lax.ppermute(far_qkv, ULY, to_near)
    router_probs = lax.dynamic_slice_in_dim(probs_blk, blk_at * count_tok, count_tok)
    chosen = lax.dynamic_slice_in_dim(chosen_blk, blk_at * count_tok, count_tok)
    grad_probs = chosen * dg_parts.reshape(number, count_tok).T
    grad_logits = (
        router_probs * (grad_probs - jnp.sum(router_probs * grad_probs, axis=1, keepdims=True))
    ).astype(BF16)
    grad_hidden_two = jnp.sum(dx_parts.astype(F32), axis=0) + dot_nn(grad_logits, router_t)
    grad_router_t = dot_tn(grad_logits, hidden_two)
    grad_gain_ffn = jnp.sum(grad_hidden_two * normed_two, axis=0)
    grad_mid = own_grad.astype(F32) + norm_back(grad_hidden_two * gain_ffn, mid, scale_two)

    (branch_grad,) = exchange([(grad_mid.astype(BF16), ULY, "relay")], 5)
    branch_grad = branch_grad.reshape(rows, width)
    grad_attn = jnp.einsum("td,hcd->htc", branch_grad, own_out, preferred_element_type=F32).astype(BF16)
    (grad_attn,) = exchange([(grad_attn, ("blk",), "swap")], 6, after=[out_parts])
    grad_out_part = jnp.einsum("htc,td->hcd", attn_rows, branch_grad, preferred_element_type=F32)
    grad_out_parts = lax.all_to_all(
        grad_out_part.astype(BF16).reshape(group, shard_rows, width),
        ROWS,
        split_axis=0,
        concat_axis=0,
        tiled=True,
    )
    grad_out = lax.ppermute(
        jnp.sum(grad_out_parts.astype(F32), axis=0).astype(BF16), ALL, [(b, a) for a, b in to_rows]
    ).astype(F32)
    grad_projected, grad_gains = project_back(
        qkv, grad_attn.reshape(length, head_dim), attn_f32, lse, seg_row, raw, cos, sin, gains
    )
    by_uly = grad_projected.reshape(blk, uly, count_tok, 3 * head_dim).transpose(1, 0, 2, 3)
    (projected_blk,) = exchange(
        [(by_uly.reshape(uly, tokens_blk, 3 * head_dim), ULY, "swap")], 7, after=[grad_out_parts]
    )
    grad_qkv_part = dot_tn(hidden_one, grad_projected).astype(BF16)

    near_at, far_at = uly_at + 1 - 2 * lax.rem(uly_at, 2), lax.rem(uly_at + 2, uly)
    cross_at = lax.rem(near_at + 2, uly)
    grad_hidden_part = sum(
        dot_nt(lax.dynamic_index_in_dim(projected_blk, sender, 0, keepdims=False), weights)
        for sender, weights in [
            (uly_at, own_qkv),
            (near_at, near_qkv),
            (far_at, far_qkv),
            (cross_at, cross_qkv),
        ]
    )
    inputs_blk = lax.dynamic_index_in_dim(toks, uly_at, 1, keepdims=False)
    inputs_blk = inputs_blk.reshape(tokens_blk, width).astype(F32)
    grad_gain_attn = jnp.sum(grad_hidden_part * (inputs_blk * rms_scale(inputs_blk)), axis=0)

    small = jnp.concatenate([grad_gain_attn[None], grad_gain_ffn[None], grad_router_t], axis=0)
    small = small.reshape(kept, total, shard_rows).transpose(1, 0, 2)
    small = jnp.pad(small, ((0, 0), (0, 0), (0, LANES - shard_rows)))
    head_row = jnp.where(
        jnp.arange(LANES) == uly_at * blk + blk_at, jnp.max(top) * head_dim**-0.5, NEG
    )
    to_all = jnp.concatenate([grad_gains, head_row[None]], axis=0)
    small = jnp.concatenate([small, jnp.broadcast_to(to_all[None], (total, 3, LANES))], axis=1)
    small = jnp.pad(small, ((0, 0), (0, -small.shape[1] % 8), (0, 0)))
    grad_hidden_parts, small, grad_qkv_parts = exchange(
        [
            (grad_hidden_part.astype(BF16).reshape(blk, count_tok, width), ("blk",), "swap"),
            (small, ALL, "swap"),
            (grad_qkv_part.reshape(total, shard_rows, 3 * head_dim), ALL, "swap"),
        ],
        8,
    )
    grad_qkv = merge_heads(grad_qkv_parts.reshape(batch, blk, uly, shard_rows, 3 * head_dim))
    grad_hidden_one = jnp.sum(grad_hidden_parts.astype(F32), axis=0)
    grad_inputs = grad_mid + norm_back(grad_hidden_one * gain_attn, inputs, rms_scale(inputs))
    sums = jnp.sum(small, axis=0)
    head_max = jnp.max(small[:, kept + 2, :heads], axis=0)
    factor = jnp.repeat(jnp.sqrt(TAU / jnp.maximum(head_max, TAU)), head_dim)
    column_scale = jnp.concatenate([factor, factor, jnp.ones((width,), F32)])
    clipped = w_qkv.astype(F32) * column_scale[None, :]
    return (
        output[None],
        grad_inputs[None],
        grad_qkv,
        grad_out,
        sums[0, :shard_rows],
        sums[1, :shard_rows],
        sums[kept : kept + 2],
        sums[2:kept, :shard_rows].T,
        grad_gate_up,
        grad_down,
        clipped,
    )


def solution(mesh):
    in_specs = (
        P("batch", ("blk", *ULY), None),
        P("batch", None),
        P("batch", ("blk", *ULY), None),
        P(ALL, None),
        P(ALL, None),
        P(ALL),
        P(ALL),
        P(),
        P(ALL, None),
        P("blk", PLANE, None),
        P("blk", PLANE, None),
        P("batch", ("blk", *ULY), None),
    )
    out_specs = (
        P("batch", ("blk", *ULY), None),
        P("batch", ("blk", *ULY), None),
        P(ALL, None),
        P(ALL, None),
        P(ALL),
        P(ALL),
        P(),
        P(ALL, None),
        P("blk", PLANE, None),
        P("blk", PLANE, None),
        P(ALL, None),
    )
    cores = 2 - mesh.shape["uly"] % 2
    mesh = Mesh(
        mesh.devices.reshape(*(mesh.shape[axis] for axis in ROWS), mesh.shape["uly"] // cores, cores), ALL
    )
    return jax.shard_map(
        per_device, mesh=mesh, in_specs=in_specs, out_specs=out_specs, check_vma=False
    )
```

```python
import functools
import math

import jax
import jax.numpy as jnp
from jax import lax
from jax.experimental import pallas as pl
from jax.experimental.pallas import tpu as pltpu
from jax.sharding import Mesh
from jax.sharding import PartitionSpec as P

EPS = 1e-06
THETA = 50000.0
TAU = 4.0
NEG = -1e30
LOG2E = 1.4426950408889634
LANES = 128
MOST_TOKENS = 512
VMEM_LIMIT = 60 * 1024 * 1024

ULY = ("y", "core")
ALL = ("batch", "blk", *ULY)
ROWS = ("batch", "blk")
PLANE = ("batch", *ULY)
CHIPS = ("batch", "y")

MESH = pl.DeviceIdType.MESH
BF16 = jnp.bfloat16
F32 = jnp.float32


def rms_scale(values):
    return lax.rsqrt(jnp.mean(values * values, axis=-1, keepdims=True) + EPS)


def norm_back(grad_normed, values, scale):
    normed = values * scale
    return scale * (grad_normed - normed * jnp.mean(grad_normed * normed, axis=-1, keepdims=True))


def rope_tables(offset, length, head_dim):
    half_dim = head_dim // 2
    frequency = THETA ** (-jnp.arange(half_dim, dtype=F32) * 2.0 / head_dim)
    positions = (offset + jnp.arange(length, dtype=jnp.int32)).astype(F32)
    angles = positions[:, None] * frequency[None, :]
    return (jnp.cos(angles)[:, None, :], jnp.sin(angles)[:, None, :])


def rope_rows(length, head_dim):
    fine = math.gcd(length, LANES)
    frequency = THETA ** (-jnp.arange(head_dim // 2, dtype=F32) * 2.0 / head_dim)
    frequency = jnp.concatenate([frequency, frequency])
    coarse_angle = (jnp.arange(length // fine, dtype=F32) * fine)[:, None, None] * frequency
    fine_angle = jnp.arange(fine, dtype=F32)[None, :, None] * frequency
    cos_a, sin_a, cos_b, sin_b = lax.optimization_barrier(
        (jnp.cos(coarse_angle), jnp.sin(coarse_angle), jnp.cos(fine_angle), jnp.sin(fine_angle))
    )
    sign = jnp.where(jnp.arange(head_dim) < head_dim // 2, -1.0, 1.0)
    cos = cos_a * cos_b - sin_a * sin_b
    sin = (sin_a * cos_b + cos_a * sin_b) * sign
    return cos.reshape(length, head_dim), sin.reshape(length, head_dim)


def rotate(values, cos_table, sin_table):
    half_dim = values.shape[-1] // 2
    first = values[..., :half_dim]
    second = values[..., half_dim:]
    return jnp.concatenate(
        [first * cos_table - second * sin_table, second * cos_table + first * sin_table], axis=-1
    )


def dot_nn(a, b):
    return lax.dot_general(a, b, (((1,), (0,)), ((), ())), preferred_element_type=F32)


def dot_nt(a, b):
    return lax.dot_general(a, b, (((1,), (1,)), ((), ())), preferred_element_type=F32)


def dot_tn(a, b):
    return lax.dot_general(a, b, (((0,), (0,)), ((), ())), preferred_element_type=F32)


def key_chunks(length):
    size = min(512, length)
    return size, length // size


def attn_fwd_kernel(factor, q_ref, k_ref, v_ref, sq_ref, sk_ref, o_ref, of_ref, lse_ref, top_ref, vt_ref):
    length = k_ref.shape[1]
    size, count = key_chunks(length)
    tile, head_dim = q_ref.shape[1:]

    @pl.when(pl.program_id(1) == 0)
    def _():
        vt_ref[...] = v_ref[0].astype(F32).T.astype(BF16)

    q = q_ref[0]
    seg_q = sq_ref[...]

    def step(j, carried):
        total, top, acc = carried
        at = pl.multiple_of(j * size, size)
        scores = dot_nt(k_ref[0, pl.ds(at, size), :], q)
        scores = jnp.where(sk_ref[pl.ds(at, size), :] == seg_q, scores, NEG)
        top = jnp.maximum(top, jnp.max(scores, axis=0, keepdims=True))
        weights = jnp.exp2(scores * factor)
        total = total + jnp.sum(weights, axis=0, keepdims=True)
        acc = acc + dot_nn(vt_ref[:, pl.ds(at, size)], weights.astype(BF16))
        return total, top, acc

    start = (
        jnp.zeros((1, tile), F32),
        jnp.full((1, tile), NEG, F32),
        jnp.zeros((head_dim, tile), F32),
    )
    total, top, acc = lax.fori_loop(0, count, step, start, unroll=count <= 4)
    out = (acc * (1.0 / total)).T
    o_ref[0] = out.astype(BF16)
    of_ref[0] = out
    lse_ref[0] = jnp.log2(total)
    top_ref[0] = top


def attn_bwd_kernel(
    factor, scale, q_ref, k_ref, v_ref, do_ref, of_ref, lse_ref, sq_ref, sk_ref,
    dq_ref, dk_ref, dv_ref, kt_ref, dk_acc, dv_acc,
):
    length = k_ref.shape[1]
    size, count = key_chunks(length)
    tile, head_dim = q_ref.shape[1:]

    @pl.when(pl.program_id(1) == 0)
    def _():
        kt_ref[...] = k_ref[0].astype(F32).T.astype(BF16)
        dk_acc[...] = jnp.zeros_like(dk_acc)
        dv_acc[...] = jnp.zeros_like(dv_acc)

    q = q_ref[0]
    grad = do_ref[0]
    seg_q = sq_ref[...]
    lse = lse_ref[0]
    row_dot = jnp.sum((grad.astype(F32) * of_ref[0]).T, axis=0, keepdims=True)

    def step(j, dq_t):
        at = pl.multiple_of(j * size, size)
        rows = pl.ds(at, size)
        scores = dot_nt(k_ref[0, rows, :], q)
        scores = jnp.where(sk_ref[rows, :] == seg_q, scores, NEG)
        weights = jnp.exp2(scores * factor - lse)
        grad_weights = dot_nt(v_ref[0, rows, :], grad)
        grad_scores = (weights * (grad_weights - row_dot)).astype(BF16)
        dk_acc[rows, :] += dot_nn(grad_scores, q)
        dv_acc[rows, :] += dot_nn(weights.astype(BF16), grad)
        return dq_t + dot_nn(kt_ref[:, rows], grad_scores)

    dq_t = lax.fori_loop(0, count, step, jnp.zeros((head_dim, tile), F32), unroll=count <= 4)
    dq_ref[0] = (dq_t * scale).T.astype(BF16)

    @pl.when(pl.program_id(1) == pl.num_programs(1) - 1)
    def _():
        dk_ref[0] = (dk_acc[...] * scale).astype(BF16)
        dv_ref[0] = dv_acc[...].astype(BF16)


def attention_tile(queries, length):
    return min(queries, 256 if length <= 4096 else 128)


def attention_forward(q_src, kv_src, cols, seg_q, seg_k, head_dim):
    heads, queries = q_src.shape[:2]
    length = kv_src.shape[1]
    tile = attention_tile(queries, length)
    q_col, k_col, v_col = cols
    factor = head_dim**-0.5 * LOG2E
    row = pl.BlockSpec((1, 1, tile), lambda h, i: (h, 0, i))
    block = pl.BlockSpec((1, tile, head_dim), lambda h, i: (h, i, 0))
    return pl.pallas_call(
        functools.partial(attn_fwd_kernel, factor),
        grid=(heads, queries // tile),
        in_specs=[
            pl.BlockSpec((1, tile, head_dim), lambda h, i: (h, i, q_col)),
            pl.BlockSpec((1, length, head_dim), lambda h, i: (h, 0, k_col)),
            pl.BlockSpec((1, length, head_dim), lambda h, i: (h, 0, v_col)),
            pl.BlockSpec((1, tile), lambda h, i: (0, i)),
            pl.BlockSpec((length, 1), lambda h, i: (0, 0)),
        ],
        out_specs=[block, block, row, row],
        out_shape=[
            jax.ShapeDtypeStruct((heads, queries, head_dim), BF16),
            jax.ShapeDtypeStruct((heads, queries, head_dim), F32),
            jax.ShapeDtypeStruct((heads, 1, queries), F32),
            jax.ShapeDtypeStruct((heads, 1, queries), F32),
        ],
        scratch_shapes=[pltpu.VMEM((head_dim, length), BF16)],
        compiler_params=pltpu.CompilerParams(vmem_limit_bytes=VMEM_LIMIT),
        cost_estimate=pl.CostEstimate(
            flops=4 * heads * queries * length * head_dim,
            bytes_accessed=heads * (queries + length) * head_dim * 8,
            transcendentals=heads * queries * length,
        ),
        name="attend",
    )(q_src, kv_src, kv_src, seg_q.reshape(1, -1), seg_k.reshape(-1, 1))


def attention_backward(q_src, kv_src, cols, grad, out_f32, lse, seg_q, seg_k, head_dim):
    heads, queries = q_src.shape[:2]
    length = kv_src.shape[1]
    tile = attention_tile(queries, length)
    q_col, k_col, v_col = cols
    scale = head_dim**-0.5
    row = pl.BlockSpec((1, 1, tile), lambda h, i: (h, 0, i))
    block = pl.BlockSpec((1, tile, head_dim), lambda h, i: (h, i, 0))
    whole = pl.BlockSpec((1, length, head_dim), lambda h, i: (h, 0, 0))
    return pl.pallas_call(
        functools.partial(attn_bwd_kernel, scale * LOG2E, scale),
        grid=(heads, queries // tile),
        in_specs=[
            pl.BlockSpec((1, tile, head_dim), lambda h, i: (h, i, q_col)),
            pl.BlockSpec((1, length, head_dim), lambda h, i: (h, 0, k_col)),
            pl.BlockSpec((1, length, head_dim), lambda h, i: (h, 0, v_col)),
            block,
            block,
            row,
            pl.BlockSpec((1, tile), lambda h, i: (0, i)),
            pl.BlockSpec((length, 1), lambda h, i: (0, 0)),
        ],
        out_specs=[block, whole, whole],
        out_shape=[
            jax.ShapeDtypeStruct((heads, queries, head_dim), BF16),
            jax.ShapeDtypeStruct((heads, length, head_dim), BF16),
            jax.ShapeDtypeStruct((heads, length, head_dim), BF16),
        ],
        scratch_shapes=[
            pltpu.VMEM((head_dim, length), BF16),
            pltpu.VMEM((length, head_dim), F32),
            pltpu.VMEM((length, head_dim), F32),
        ],
        compiler_params=pltpu.CompilerParams(vmem_limit_bytes=VMEM_LIMIT),
        cost_estimate=pl.CostEstimate(
            flops=10 * heads * queries * length * head_dim,
            bytes_accessed=heads * (queries + length) * head_dim * 12,
            transcendentals=heads * queries * length,
        ),
        name="attend_back",
    )(q_src, kv_src, kv_src, grad, out_f32, lse, seg_q.reshape(1, -1), seg_k.reshape(-1, 1))


def expert_step(expert, h_ref, ht_ref, dy_ref, dyt_ref, gate_ref, wg_ref, wu_ref, wd_ref, dg_ref, out_acc, dx_acc):
    width = h_ref.shape[1]
    cols = wg_ref.shape[3]
    w_gate = wg_ref[...].reshape(width, cols)
    w_up = wu_ref[...].reshape(width, cols)
    w_down = wd_ref[...].reshape(width, cols)
    gates = gate_ref[...]
    mine = lax.broadcasted_iota(jnp.int32, gates.shape, 1) == expert
    gate = jnp.sum(jnp.where(mine, gates, 0.0), axis=1, keepdims=True)
    a_gate = dot_nn(h_ref[...], w_gate)
    a_up = dot_nn(h_ref[...], w_up)
    raw = dot_nn(dy_ref[...], w_down)
    sigma = 1.0 / (1.0 + jnp.exp2(a_gate * -LOG2E))
    swish = a_gate * sigma
    act = swish * a_up
    dg_ref[0] += jnp.sum(raw * act, axis=1, keepdims=True)
    gated = (gate * act).astype(BF16)
    d_act = gate * raw
    d_gate = (d_act * a_up * (sigma + swish * (1.0 - sigma))).astype(BF16)
    d_up = (d_act * swish).astype(BF16)
    out_acc[...] += dot_nt(gated, w_down)
    dx_acc[...] += dot_nt(d_gate, w_gate) + dot_nt(d_up, w_up)
    for part, (left, right) in enumerate([(ht_ref, d_gate), (ht_ref, d_up), (dyt_ref, gated)]):
        yield part, dot_nn(left[...], right).astype(BF16)


def expert_kernel(
    h_ref, ht_ref, dy_ref, dyt_ref, gate_ref, out0_ref, dx0_ref, wg_ref, wu_ref, wd_ref,
    out_ref, dx_ref, dg_ref, gr_ref, out_acc, dx_acc,
):
    step, last = pl.program_id(0), pl.num_programs(0) - 1
    parts, _, part_rows, cols = wg_ref.shape
    chunks = (last + 1) // gate_ref.shape[1]

    @pl.when(step == 0)
    def _():
        out_acc[...] = out0_ref[...].astype(F32)
        dx_acc[...] = dx0_ref[...].astype(F32)

    @pl.when(step % chunks == 0)
    def _():
        dg_ref[...] = jnp.zeros_like(dg_ref)

    for part, made in expert_step(
        step // chunks, h_ref, ht_ref, dy_ref, dyt_ref, gate_ref, wg_ref, wu_ref, wd_ref, dg_ref, out_acc, dx_acc
    ):
        gr_ref[:, part, 0] = made.reshape(parts, part_rows, cols)

    @pl.when(step == last)
    def _():
        out_ref[...] = out_acc[...].astype(BF16)
        dx_ref[...] = dx_acc[...].astype(BF16)


def expert_pair_kernel(
    h_ref, ht_ref, dy_ref, dyt_ref, gate_ref, out0_ref, dx0_ref, wg_ref, wu_ref, wd_ref,
    out_ref, dx_ref, dg_ref, keep_x, give_x, keep_y, give_y,
    out_acc, dx_acc, made_ref, got_ref, send, recv, free,
):
    step, last = pl.program_id(0), pl.num_programs(0) - 1
    parts, _, part_rows, cols = wg_ref.shape
    chunks = last // 2
    b, y, core = lax.axis_index("batch"), lax.axis_index("y"), lax.axis_index("core")
    near = {"core": 1 - core}
    slot, before = lax.rem(step, 2), lax.rem(step + 1, 2)

    @pl.when(step == 0)
    def _():
        barrier = pltpu.get_barrier_semaphore()
        pl.semaphore_signal(barrier, inc=1, device_id=near, device_id_type=MESH)
        pl.semaphore_wait(barrier, 1)
        out_acc[...] = out0_ref[...].astype(F32)
        dx_acc[...] = dx0_ref[...].astype(F32)

    def hand_over(at):
        return pltpu.make_async_remote_copy(
            src_ref=made_ref.at[at, 1 - core],
            dst_ref=got_ref.at[at],
            send_sem=send.at[at],
            recv_sem=recv.at[at],
            device_id=near,
            device_id_type=MESH,
        )

    @pl.when(step < last)
    def _():
        @pl.when(step % chunks == 0)
        def _():
            dg_ref[...] = jnp.zeros_like(dg_ref)

        for part, made in expert_step(
            step // chunks, h_ref, ht_ref, dy_ref, dyt_ref, gate_ref, wg_ref, wu_ref, wd_ref, dg_ref, out_acc, dx_acc
        ):
            made = made.reshape(parts // 2, 2, part_rows, cols)
            made_ref[slot, 0, :, part] = made[:, 0]
            made_ref[slot, 1, :, part] = made[:, 1]

        @pl.when(step >= 2)
        def _():
            pl.semaphore_wait(free, 1)

        hand_over(slot).start()

    def total(other_b, other_y):
        at = (b + other_b) % 2 * 2 + (y + other_y) % 2
        both = made_ref[before, core, at].astype(F32) + got_ref[before, at].astype(F32)
        return both.astype(BF16)

    @pl.when(step > 0)
    def _():
        hand_over(before).wait()

        @pl.when(step <= chunks)
        def _():
            for other in range(2):
                keep_x[other] = total(0, other)
                give_x[other] = total(1, other)

        @pl.when(step > chunks)
        def _():
            for other in range(2):
                keep_y[other] = total(other, 0)
                give_y[other] = total(other, 1)

        @pl.when(step < last - 1)
        def _():
            pl.semaphore_signal(free, inc=1, device_id=near, device_id_type=MESH)

    @pl.when(step == last)
    def _():
        out_ref[...] = out_acc[...].astype(BF16)
        dx_ref[...] = dx_acc[...].astype(BF16)


def experts(hidden, hidden_t, grad, grad_t, gates, out, dx, weights, collective_id=None):
    tokens, width = hidden.shape
    parts, count, part_rows, units = weights.shape
    units = units // 3
    cols = min(256, units)
    chunks = units // cols
    steps = count * chunks
    paired = collective_id is not None
    once = pl.Buffered(1)
    whole = pl.BlockSpec((tokens, width), lambda s: (0, 0), pipeline_mode=once)
    whole_t = pl.BlockSpec((width, tokens), lambda s: (0, 0), pipeline_mode=once)
    result = pl.BlockSpec((tokens, width), lambda s: (0, 0))

    def now(step):
        return jnp.minimum(step, steps - 1)

    def weight(kind):
        def index(step):
            at = now(step)
            return (0, at // chunks, 0, kind * chunks + at % chunks)

        return pl.BlockSpec((parts, 1, part_rows, cols), index)

    def written(expert):
        return lambda s: (0, 0, 0, jnp.clip(s - 1 - expert * chunks, 0, chunks - 1))

    scratch = [pltpu.VMEM((tokens, width), F32), pltpu.VMEM((tokens, width), F32)]
    if paired:
        scratch += [
            pltpu.VMEM((2, 2, parts // 2, 3, part_rows, cols), BF16),
            pltpu.VMEM((2, parts // 2, 3, part_rows, cols), BF16),
            pltpu.SemaphoreType.DMA((2,)),
            pltpu.SemaphoreType.DMA((2,)),
            pltpu.SemaphoreType.REGULAR,
        ]
        grad_specs = [
            pl.BlockSpec((2, 3, part_rows, cols), written(expert)) for expert in (0, 0, 1, 1)
        ]
        grad_shapes = [jax.ShapeDtypeStruct((2, 3, part_rows, units), BF16)] * 4
    else:
        grad_specs = [
            pl.BlockSpec((parts, 3, 1, part_rows, cols), lambda s: (0, 0, s // chunks, 0, s % chunks))
        ]
        grad_shapes = [jax.ShapeDtypeStruct((parts, 3, count, part_rows, units), BF16)]
    return pl.pallas_call(
        expert_pair_kernel if paired else expert_kernel,
        grid=(steps + 1 if paired else steps,),
        in_specs=[
            whole,
            whole_t,
            whole,
            whole_t,
            pl.BlockSpec(gates.shape, lambda s: (0, 0), pipeline_mode=once),
            whole,
            whole,
            weight(0),
            weight(1),
            weight(2),
        ],
        out_specs=[
            result,
            result,
            pl.BlockSpec((1, tokens, 1), lambda s: (now(s) // chunks, 0, 0)),
            *grad_specs,
        ],
        out_shape=[
            jax.ShapeDtypeStruct((tokens, width), BF16),
            jax.ShapeDtypeStruct((tokens, width), BF16),
            jax.ShapeDtypeStruct((count, tokens, 1), F32),
            *grad_shapes,
        ],
        scratch_shapes=scratch,
        compiler_params=pltpu.CompilerParams(
            vmem_limit_bytes=VMEM_LIMIT, collective_id=collective_id, has_side_effects=paired
        ),
        cost_estimate=pl.CostEstimate(
            flops=18 * count * tokens * width * units,
            bytes_accessed=12 * count * width * units,
            transcendentals=count * tokens * units,
        ),
        name="experts",
    )(hidden, hidden_t, grad, grad_t, gates, out, dx, weights, weights, weights)


def finish_experts_kernel(*refs):
    *parts, gate_up_ref, down_ref = refs
    units = down_ref.shape[2]

    def write(kept, first, second):
        total = [
            kept[0, part].astype(F32) + first[0, part].astype(F32) + second[part].astype(F32)
            for part in range(3)
        ]
        gate_up_ref[0, :, :units] = total[0]
        gate_up_ref[0, :, units:] = total[1]
        down_ref[0] = total[2]

    pl.when(pl.program_id(0) == 0)(lambda: write(*parts[:3]))
    pl.when(pl.program_id(0) == 1)(lambda: write(*parts[3:6]))


def finish_experts(first, second, at, count, before=()):
    _, _, rows, units = first[0].shape
    tile = min(64, rows)
    steps = rows // tile

    def row(expert):
        if expert == 0:
            return lambda e, r: jnp.where(e == 0, r, steps - 1)
        return lambda e, r: jnp.where(e == 1, r, 0)

    def specs(expert):
        at_row = row(expert)
        pair = pl.BlockSpec((1, 3, tile, units), lambda e, r: (0, 0, at_row(e, r), 0))
        return [pair, pair, pl.BlockSpec((3, tile, units), lambda e, r: (0, at_row(e, r), 0))]

    return pl.pallas_call(
        lambda *refs: finish_experts_kernel(*refs[:6], *refs[-2:]),
        grid=(2, steps),
        in_specs=[*specs(0), *specs(1), *[pl.BlockSpec(memory_space=pl.ANY)] * len(before)],
        out_specs=[
            pl.BlockSpec((1, tile, 2 * units), lambda e, r: (at + e, r, 0)),
            pl.BlockSpec((1, tile, units), lambda e, r: (at + e, r, 0)),
        ],
        out_shape=[
            jax.ShapeDtypeStruct((count, rows, 2 * units), F32),
            jax.ShapeDtypeStruct((count, rows, units), F32),
        ],
        input_output_aliases={6 + i: i for i in range(len(before))},
        compiler_params=pltpu.CompilerParams(vmem_limit_bytes=VMEM_LIMIT),
        name="finish_experts",
    )(*first, *second, *before)


def turn(values, cos, sin):
    return values * cos + pltpu.roll(values, values.shape[1] // 2, 1) * sin


def project_kernel(
    tok_ref, gain_ref, w_ref, cos_ref, sin_ref, gains_ref, hidden_ref, qkv_ref, raw_ref
):
    head_dim = cos_ref.shape[1]
    values = tok_ref[...].astype(F32)
    hidden = (values * rms_scale(values) * gain_ref[...]).astype(BF16)
    hidden_ref[...] = hidden
    projected = dot_nn(hidden, w_ref[...])
    raw_ref[...] = projected[:, : 2 * head_dim]
    for part in range(2):
        at = slice(part * head_dim, (part + 1) * head_dim)
        raw = projected[:, at]
        normed = raw * rms_scale(raw) * gains_ref[part : part + 1, :]
        qkv_ref[:, at] = turn(normed, cos_ref[...], sin_ref[...]).astype(BF16)
    qkv_ref[:, 2 * head_dim :] = projected[:, 2 * head_dim :].astype(BF16)


def project(toks, gain, weights, cos, sin, gains):
    length, width = toks.shape
    head_dim = cos.shape[1]
    tile = min(256, length)

    def rows(columns):
        return pl.BlockSpec((tile, columns), lambda i: (i, 0))

    def fixed(shape):
        return pl.BlockSpec(shape, lambda i: (0, 0))

    return pl.pallas_call(
        project_kernel,
        grid=(length // tile,),
        in_specs=[
            rows(width),
            fixed((1, width)),
            fixed(weights.shape),
            rows(head_dim),
            rows(head_dim),
            fixed(gains.shape),
        ],
        out_specs=[rows(width), rows(3 * head_dim), rows(2 * head_dim)],
        out_shape=[
            jax.ShapeDtypeStruct((length, width), BF16),
            jax.ShapeDtypeStruct((length, 3 * head_dim), BF16),
            jax.ShapeDtypeStruct((length, 2 * head_dim), F32),
        ],
        compiler_params=pltpu.CompilerParams(vmem_limit_bytes=VMEM_LIMIT),
        name="project",
    )(toks, gain, weights, cos, sin, gains)


def project_back_kernel(
    factor, scale, q_ref, k_ref, v_ref, do_ref, of_ref, lse_ref, sq_ref, sk_ref,
    raw_q_ref, raw_k_ref, cos_q_ref, sin_q_ref, cos_ref, sin_ref, gains_ref,
    dp_ref, dgain_ref, kt_ref, dk_acc, dv_acc,
):
    length, head_dim = k_ref.shape
    size, count = key_chunks(length)
    tile = q_ref.shape[0]
    step_at = pl.program_id(0)

    @pl.when(step_at == 0)
    def _():
        kt_ref[...] = k_ref[...].astype(F32).T.astype(BF16)
        dk_acc[...] = jnp.zeros_like(dk_acc)
        dv_acc[...] = jnp.zeros_like(dv_acc)
        dgain_ref[...] = jnp.zeros_like(dgain_ref)

    def to_raw(part, grad, raw, cos, sin):
        grad = turn(grad.astype(BF16).astype(F32), cos, -sin)
        raw_scale = rms_scale(raw)
        dgain_ref[part : part + 1, :] += jnp.sum(grad * (raw * raw_scale), axis=0, keepdims=True)
        return norm_back(grad * gains_ref[part : part + 1, :], raw, raw_scale).astype(BF16)

    q = q_ref[...]
    grad = do_ref[...]
    seg_q = sq_ref[...]
    lse = lse_ref[0]
    row_dot = jnp.sum((grad.astype(F32) * of_ref[0]).T, axis=0, keepdims=True)
    dq_t = jnp.zeros((head_dim, tile), F32)
    for j in range(count):
        rows = slice(j * size, (j + 1) * size)
        scores = dot_nt(k_ref[rows, :], q)
        scores = jnp.where(sk_ref[rows, :] == seg_q, scores, NEG)
        weights = jnp.exp2(scores * factor - lse)
        grad_weights = dot_nt(v_ref[rows, :], grad)
        grad_scores = (weights * (grad_weights - row_dot)).astype(BF16)
        dk_acc[rows, :] += dot_nn(grad_scores, q)
        dv_acc[rows, :] += dot_nn(weights.astype(BF16), grad)
        dq_t = dq_t + dot_nn(kt_ref[:, rows], grad_scores)
    own = pl.ds(pl.multiple_of(step_at * tile, tile), tile)
    dp_ref[own, :head_dim] = to_raw(
        0, (dq_t * scale).T, raw_q_ref[...], cos_q_ref[...], sin_q_ref[...]
    )

    @pl.when(step_at == pl.num_programs(0) - 1)
    def _():
        dp_ref[:, head_dim : 2 * head_dim] = to_raw(
            1, dk_acc[...] * scale, raw_k_ref[...], cos_ref[...], sin_ref[...]
        )
        dp_ref[:, 2 * head_dim :] = dv_acc[...].astype(BF16)


def project_back(qkv, grad, out_f32, lse, segments, raw, cos, sin, gains):
    length, head_dim = grad.shape
    tile = min(256, length)

    def rows(column):
        return pl.BlockSpec((tile, head_dim), lambda i: (i, column))

    def whole(column):
        return pl.BlockSpec((length, head_dim), lambda i: (0, column))

    return pl.pallas_call(
        functools.partial(project_back_kernel, head_dim**-0.5 * LOG2E, head_dim**-0.5),
        grid=(length // tile,),
        in_specs=[
            rows(0),
            whole(1),
            whole(2),
            rows(0),
            pl.BlockSpec((1, tile, head_dim), lambda i: (0, i, 0)),
            pl.BlockSpec((1, 1, tile), lambda i: (0, 0, i)),
            pl.BlockSpec((1, tile), lambda i: (0, i)),
            pl.BlockSpec((length, 1), lambda i: (0, 0)),
            rows(0),
            whole(1),
            rows(0),
            rows(0),
            whole(0),
            whole(0),
            pl.BlockSpec(gains.shape, lambda i: (0, 0)),
        ],
        out_specs=[
            pl.BlockSpec((length, 3 * head_dim), lambda i: (0, 0)),
            pl.BlockSpec((2, head_dim), lambda i: (0, 0)),
        ],
        out_shape=[
            jax.ShapeDtypeStruct((length, 3 * head_dim), BF16),
            jax.ShapeDtypeStruct((2, head_dim), F32),
        ],
        scratch_shapes=[
            pltpu.VMEM((head_dim, length), BF16),
            pltpu.VMEM((length, head_dim), F32),
            pltpu.VMEM((length, head_dim), F32),
        ],
        compiler_params=pltpu.CompilerParams(vmem_limit_bytes=VMEM_LIMIT),
        cost_estimate=pl.CostEstimate(
            flops=10 * length * length * head_dim,
            bytes_accessed=length * head_dim * 40,
            transcendentals=length * length,
        ),
        name="project_back",
    )(
        qkv, qkv, qkv, grad, out_f32, lse, segments.reshape(1, -1), segments.reshape(-1, 1),
        raw, raw, cos, sin, cos, sin, gains,
    )


def merge_heads_kernel(parts_ref, out_ref):
    blk, uly, _, columns = parts_ref.shape
    head_dim = columns // 3
    heads = blk * uly
    for z in range(blk):
        for u in range(uly):
            head = parts_ref[z, u].astype(F32)
            for part in range(3):
                at = (part * heads + u * blk + z) * head_dim
                out_ref[:, at : at + head_dim] = head[:, part * head_dim : (part + 1) * head_dim]


def merge_heads(parts):
    blk, uly, rows, columns = parts.shape
    return pl.pallas_call(
        merge_heads_kernel,
        out_shape=jax.ShapeDtypeStruct((rows, blk * uly * columns), F32),
        compiler_params=pltpu.CompilerParams(vmem_limit_bytes=VMEM_LIMIT),
        name="merge_heads",
    )(parts)


def swap(values, axis):
    return lax.all_to_all(values, axis, split_axis=0, concat_axis=0, tiled=True)


def sum_scatter(values, axis):
    count = spread(axis) if isinstance(axis, tuple) else lax.axis_size(axis)
    rows, width = values.shape
    parts = swap(values.astype(BF16).reshape(count, rows // count, width), axis)
    return jnp.sum(parts.astype(F32), axis=0)


def place(axes, index):
    found = {}
    for axis in reversed(axes):
        size = lax.axis_size(axis)
        found[axis] = lax.rem(index, size)
        index = index // size
    return found


def spread(axes):
    return math.prod(lax.axis_size(axis) for axis in axes)


def each(count, body):
    if count <= 4:
        for step in range(1, count):
            body(step)
    else:

        def looped(step, carried):
            body(step)
            return carried

        lax.fori_loop(1, count, looped, 0)


def ahead(index, step, size):
    return lax.rem(index + step, size)


def exchange(items, collective_id, after=()):
    count = len(items)
    sizes = [spread(axes) for _, axes, _ in items]
    groups = list(dict.fromkeys(axes for _, axes, _ in items))
    bases = [sum(2 * size for size in sizes[:i]) for i in range(count)]

    def kernel(*refs):
        ins = refs[:count]
        outs = refs[count + len(after) : 2 * count + len(after)]
        send, recv, local = refs[-3:]
        barrier = pltpu.get_barrier_semaphore()
        for axes in groups:
            size, me = spread(axes), lax.axis_index(axes)

            def greet(step, axes=axes, size=size, me=me):
                pl.semaphore_signal(
                    barrier, inc=1, device_id=place(axes, ahead(me, step, size)), device_id_type=MESH
                )

            each(size, greet)
        pl.semaphore_wait(barrier, sum(spread(axes) - 1 for axes in groups))

        def remote(i, step):
            _, axes, kind = items[i]
            me = lax.axis_index(axes)
            if kind == "trade":
                return pltpu.make_async_remote_copy(
                    src_ref=ins[i],
                    dst_ref=outs[i],
                    send_sem=send.at[bases[i] + 1],
                    recv_sem=recv.at[bases[i] + 1],
                    device_id=place(axes, 1 - me),
                    device_id_type=MESH,
                )
            if kind == "relay":
                far, near = lax.rem(me + 2, 4), me + 1 - 2 * lax.rem(me, 2)
                held = far if step == 3 else me
                return pltpu.make_async_remote_copy(
                    src_ref=outs[i].at[far] if step == 3 else ins[i],
                    dst_ref=outs[i].at[held],
                    send_sem=send.at[bases[i] + step],
                    recv_sem=recv.at[bases[i] + step],
                    device_id=place(axes, far if step == 1 else near),
                    device_id_type=MESH,
                )
            peer = ahead(me, step, sizes[i])
            return pltpu.make_async_remote_copy(
                src_ref=ins[i].at[peer] if kind == "swap" else ins[i],
                dst_ref=outs[i].at[me],
                send_sem=send.at[bases[i] + step],
                recv_sem=recv.at[bases[i] + step],
                device_id=place(axes, peer),
                device_id_type=MESH,
            )

        def own(i):
            _, axes, kind = items[i]
            me = lax.axis_index(axes)
            return pltpu.make_async_copy(
                ins[i].at[me] if kind == "swap" else ins[i], outs[i].at[me], local.at[i]
            )

        def hop(i, up, hops):
            (axis,) = items[i][1]
            me, size = lax.axis_index(axis), sizes[i]
            way = 1 if up else -1
            held, to = me - way * hops, me + way
            exists = (held >= 0) & (held < size) & (to >= 0) & (to < size)
            held, to = jnp.clip(held, 0, size - 1), jnp.clip(to, 0, size - 1)
            sem = bases[i] + (size if up else 0) + hops
            copy = pltpu.make_async_remote_copy(
                src_ref=outs[i].at[held] if hops else ins[i],
                dst_ref=outs[i].at[held],
                send_sem=send.at[sem],
                recv_sem=recv.at[sem],
                device_id={axis: to},
                device_id_type=MESH,
            )
            return exists, copy

        def arrival(i, up, hops):
            (axis,) = items[i][1]
            me, size = lax.axis_index(axis), sizes[i]
            way = 1 if up else -1
            held, sender = me - way * (hops + 1), me - way
            exists = (held >= 0) & (held < size)
            held, sender = jnp.clip(held, 0, size - 1), jnp.clip(sender, 0, size - 1)
            sem = bases[i] + (size if up else 0) + hops
            copy = pltpu.make_async_remote_copy(
                src_ref=ins[i],
                dst_ref=outs[i].at[held],
                send_sem=send.at[sem],
                recv_sem=recv.at[sem],
                device_id={axis: sender},
                device_id_type=MESH,
            )
            return exists, copy

        def kinds(*names):
            return [i for i in range(count) if items[i][2] in names]

        def when(pair, act):
            exists, copy = pair
            pl.when(exists)(lambda: act(copy))

        ways = (True, False)
        for i in kinds("line"):
            for up in ways:
                when(hop(i, up, 0), lambda copy: copy.start())
        for i in kinds("gather", "swap", "relay", "trade"):
            each(3 if items[i][2] == "relay" else sizes[i], lambda step, i=i: remote(i, step).start())
        for i in kinds("gather", "swap", "relay", "line"):
            own(i).start()
        for i in kinds("line"):
            for hops in range(1, sizes[i]):
                for up in ways:
                    when(arrival(i, up, hops - 1), lambda copy: copy.wait_recv())
                    if hops < sizes[i] - 1:
                        when(hop(i, up, hops), lambda copy: copy.start())
        for i in kinds("relay"):
            remote(i, 1).wait_recv()
            remote(i, 3).start()
            remote(i, 1).wait_send()
            for step in (2, 3):
                remote(i, step).wait()
        for i in kinds("gather", "swap", "trade"):
            each(sizes[i], lambda step, i=i: remote(i, step).wait())
        for i in kinds("line"):
            for hops in range(sizes[i] - 1):
                for up in ways:
                    when(hop(i, up, hops), lambda copy: copy.wait_send())
        for i in kinds("gather", "swap", "relay", "line"):
            own(i).wait()

    shapes = [
        array.shape if kind == "trade" else (size, *(array.shape[1:] if kind == "swap" else array.shape))
        for size, (array, _, kind) in zip(sizes, items)
    ]
    anywhere = pl.BlockSpec(memory_space=pl.ANY)
    return pl.pallas_call(
        kernel,
        in_specs=[anywhere] * (count + len(after)),
        out_specs=[anywhere] * count,
        out_shape=[jax.ShapeDtypeStruct(shape, item[0].dtype) for shape, item in zip(shapes, items)],
        scratch_shapes=[
            pltpu.SemaphoreType.DMA((2 * sum(sizes),)),
            pltpu.SemaphoreType.DMA((2 * sum(sizes),)),
            pltpu.SemaphoreType.DMA((count,)),
        ],
        compiler_params=pltpu.CompilerParams(collective_id=collective_id, has_side_effects=True),
        name="exchange",
    )(*[item[0] for item in items], *after)


def startup_kernel(
    head_ref, extra_ref, tok_ref, heads_ref, extras_ref, toks_ref,
    head_send, head_recv, extra_send, extra_recv,
    z_send, z_recv, ay_send, ay_recv, by_send, by_recv, c_send, c_recv, local,
):
    blk, uly = lax.axis_size("blk"), spread(ULY)
    total = spread(ALL)
    z, u, me = lax.axis_index("blk"), lax.axis_index(ULY), lax.axis_index(ALL)
    far = lax.rem(u + 2, uly)
    near = u + 1 - 2 * lax.rem(u, 2)
    half = tok_ref.shape[0] // 2
    parts = (pl.ds(0, half), pl.ds(half, half))

    barrier = pltpu.get_barrier_semaphore()

    def greet(step):
        pl.semaphore_signal(
            barrier, inc=1, device_id=place(ALL, ahead(me, step, total)), device_id_type=MESH
        )

    each(total, greet)
    pl.semaphore_wait(barrier, total - 1)

    def send(src, dst, sent, got, to):
        return pltpu.make_async_remote_copy(
            src_ref=src, dst_ref=dst, send_sem=sent, recv_sem=got, device_id=to, device_id_type=MESH
        )

    def block(step, other, part):
        at = toks_ref.at[ahead(z, step, blk), far if other else u, parts[part]]
        return (tok_ref.at[parts[part]] if step == 0 and not other else at), at

    streams = ((0, 0), (0, 1), (1, 1))

    def hop(stream, up, hops):
        other, part = streams[stream]
        way = 1 if up else -1
        held, to = z - way * hops, z + way
        exists = (held >= 0) & (held < blk) & (to >= 0) & (to < blk)
        held, to = jnp.clip(held, 0, blk - 1), jnp.clip(to, 0, blk - 1)
        at = toks_ref.at[held, far if other else u, parts[part]]
        src = tok_ref.at[parts[part]] if hops == 0 and not other else at
        sem = (2 * stream + up) * blk + hops
        return exists, send(src, at, z_send.at[sem], z_recv.at[sem], {"blk": to})

    def arrival(stream, up, hops):
        other, part = streams[stream]
        way = 1 if up else -1
        held, sender = z - way * (hops + 1), z - way
        exists = (held >= 0) & (held < blk)
        held, sender = jnp.clip(held, 0, blk - 1), jnp.clip(sender, 0, blk - 1)
        at = toks_ref.at[held, far if other else u, parts[part]]
        sem = (2 * stream + up) * blk + hops
        return exists, send(tok_ref.at[parts[part]], at, z_send.at[sem], z_recv.at[sem], {"blk": sender})

    def when(pair, act):
        exists, copy = pair
        pl.when(exists)(lambda: act(copy))

    def a_y(step):
        return send(*block(step, 0, 0), ay_send.at[step], ay_recv.at[step], place(ULY, far))

    def b_y():
        return send(*block(0, 0, 1), by_send.at[0], by_recv.at[0], place(ULY, far))

    def to_near(step, other, part):
        sem = 4 * step + 2 * other + part
        return send(*block(step, other, part), c_send.at[sem], c_recv.at[sem], place(ULY, near))

    def head(step):
        to = place(ALL, ahead(me, step, total))
        src = head_ref.at[(to["y"] * lax.axis_size("core") + to["core"]) * blk + to["blk"]]
        return send(src, heads_ref.at[me], head_send.at[step], head_recv.at[step], to)

    def extra(step):
        to = place(ALL, ahead(me, step, total))
        return send(extra_ref, extras_ref.at[me], extra_send.at[step], extra_recv.at[step], to)

    own = [
        pltpu.make_async_copy(tok_ref, toks_ref.at[z, u], local.at[0]),
        pltpu.make_async_copy(head_ref.at[u * blk + z], heads_ref.at[me], local.at[1]),
        pltpu.make_async_copy(extra_ref, extras_ref.at[me], local.at[2]),
    ]

    ways = (1, 0)
    b_y().start()
    for stream in range(2):
        for up in ways:
            when(hop(stream, up, 0), lambda copy: copy.start())
    a_y(0).start()
    to_near(0, 0, 0).start()
    to_near(0, 0, 1).start()

    def start_head(step):
        extra(step).start()
        head(step).start()

    each(total, start_head)
    for copy in own:
        copy.start()
    b_y().wait_recv()
    for up in ways:
        when(hop(2, up, 0), lambda copy: copy.start())
    to_near(0, 1, 1).start()
    for hops in range(1, blk):
        for stream, (other, part) in enumerate(streams):
            for up in ways:
                exists, copy = arrival(stream, up, hops - 1)
                step = blk - hops if up else hops

                @pl.when(exists)
                def _(copy=copy, stream=stream, other=other, part=part, up=up, step=step, hops=hops):
                    copy.wait_recv()
                    if hops < blk - 1:
                        when(hop(stream, up, hops), lambda copy: copy.start())
                    if stream == 0:
                        a_y(step).start()
                    to_near(step, other, part).start()

    for step in [0, *reversed(range(1, blk))]:
        a_y(step).wait_recv()
        to_near(step, 1, 0).start()
    for step in range(blk):
        for other in range(2):
            for part in range(2):
                to_near(step, other, part).wait_recv()

    def wait_head(step):
        extra(step).wait()
        head(step).wait()

    each(total, wait_head)
    for copy in own:
        copy.wait()
    b_y().wait_send()
    for hops in range(blk - 1):
        for stream in range(3):
            for up in ways:
                when(hop(stream, up, hops), lambda copy: copy.wait_send())
    for step in range(blk):
        a_y(step).wait_send()
        for other in range(2):
            for part in range(2):
                to_near(step, other, part).wait_send()


def startup(heads, extra, tok, collective_id):
    blk, uly, total = lax.axis_size("blk"), spread(ULY), spread(ALL)
    anywhere = pl.BlockSpec(memory_space=pl.ANY)
    dma = pltpu.SemaphoreType.DMA
    return pl.pallas_call(
        startup_kernel,
        in_specs=[anywhere] * 3,
        out_specs=[anywhere] * 3,
        out_shape=[
            jax.ShapeDtypeStruct((total, *heads.shape[1:]), BF16),
            jax.ShapeDtypeStruct((total, *extra.shape), BF16),
            jax.ShapeDtypeStruct((blk, uly, *tok.shape), BF16),
        ],
        scratch_shapes=[
            *[dma((total,))] * 4,
            *[dma((6 * blk,))] * 2,
            *[dma((blk,))] * 2,
            *[dma((1,))] * 2,
            *[dma((4 * blk,))] * 2,
            dma((3,)),
        ],
        compiler_params=pltpu.CompilerParams(collective_id=collective_id, has_side_effects=True),
        name="startup",
    )(heads, extra, tok)


def per_device_general(
    tokens, segments, routes, w_qkv, w_out, attn_gain, ffn_gain, qk_gain, router, w_gate_up, w_down, cotangent
):
    own_tokens = tokens[0]
    own_grad = cotangent[0]
    count_tok, width = own_tokens.shape
    head_dim = qk_gain.shape[1]
    heads = width // head_dim
    uly, blk, batch = spread(ULY), lax.axis_size("blk"), lax.axis_size("batch")
    blk_at, uly_at = lax.axis_index("blk"), lax.axis_index(ULY)
    group = batch * blk
    local_heads = heads // uly
    local_width = local_heads * head_dim
    rows = count_tok * uly
    seg_row = segments[0]
    length = seg_row.shape[0]
    number = router.shape[1]
    local_experts, _, units = w_down.shape
    shard_rows = w_qkv.shape[0]

    extra = jnp.concatenate([attn_gain[:, None], ffn_gain[:, None], router], axis=1)
    extra = jnp.pad(extra, ((0, 0), (0, LANES - extra.shape[1])))
    columns = w_qkv.reshape(shard_rows, 3, uly, local_width).transpose(2, 0, 1, 3)
    packed = jnp.concatenate(
        [
            columns.reshape(uly, shard_rows, 3 * local_width),
            jnp.broadcast_to(extra[None], (uly, shard_rows, LANES)),
        ],
        axis=2,
    )
    packed = swap(packed, ULY).reshape(uly * shard_rows, 3 * local_width + LANES)
    packed = lax.all_gather(packed, ROWS, axis=0, tiled=True)
    own_qkv = packed[:, : 3 * local_width]
    gain_attn = packed[:, 3 * local_width].astype(F32)
    gain_ffn = packed[:, 3 * local_width + 1].astype(F32)
    whole_router = packed[:, 3 * local_width + 2 : 3 * local_width + 2 + number]
    tokens_all = lax.all_gather(own_tokens, ULY, axis=0, tiled=True)
    to_rows = [(u * group + g, g * uly + u) for g in range(group) for u in range(uly)]
    own_out = lax.all_gather(lax.ppermute(w_out, ALL, to_rows), ROWS, axis=0, tiled=True)
    whole_gate_up = lax.all_gather(w_gate_up, PLANE, axis=0, tiled=False)
    whole_down = lax.all_gather(w_down, PLANE, axis=0, tiled=False)
    grad_blk = lax.all_gather(own_grad, "blk", axis=0, tiled=True)
    routes_blk = lax.all_gather(routes[0], "blk", axis=0, tiled=True)

    gain_query = qk_gain[0].astype(F32)
    gain_key = qk_gain[1].astype(F32)
    inputs_all = tokens_all.astype(F32)
    normed_one = inputs_all * rms_scale(inputs_all)
    hidden_one = (normed_one * gain_attn).astype(BF16)
    projected = dot_nn(hidden_one, own_qkv)
    query_raw = projected[:, :local_width].reshape(rows, local_heads, head_dim)
    key_raw = projected[:, local_width : 2 * local_width].reshape(rows, local_heads, head_dim)
    value_raw = projected[:, 2 * local_width :].reshape(rows, local_heads, head_dim)
    cos_table, sin_table = rope_tables(blk_at * rows, rows, head_dim)
    query_scale = rms_scale(query_raw)
    key_scale = rms_scale(key_raw)
    qkv = jnp.concatenate(
        [
            rotate(query_raw * query_scale * gain_query, cos_table, sin_table),
            rotate(key_raw * key_scale * gain_key, cos_table, sin_table),
            value_raw,
        ],
        axis=2,
    ).astype(BF16)
    qkv = qkv.transpose(1, 0, 2)

    by_heads = local_heads % blk == 0
    if by_heads:
        per = local_heads // blk

        def to_heads(values):
            columns = values.shape[2]
            moved = swap(values.reshape(blk, per, rows, columns), "blk")
            return moved.transpose(1, 0, 2, 3).reshape(per, length, columns)

        def to_rows_back(values):
            columns = values.shape[2]
            parts = values.reshape(per, blk, rows, columns).transpose(1, 0, 2, 3)
            return swap(parts, "blk").reshape(local_heads, rows, columns)

        q_src = kv_src = to_heads(qkv)
        cols = (0, 1, 2)
        seg_q = seg_row
        first_head = uly_at * local_heads + blk_at * per
    else:

        def to_heads(values):
            return values

        def to_rows_back(values):
            return values

        q_src = qkv
        kv_src = lax.all_gather(qkv[:, :, head_dim:], "blk", axis=1, tiled=True)
        cols = (0, 0, 1)
        seg_q = lax.dynamic_slice_in_dim(seg_row, blk_at * rows, rows)
        first_head = uly_at * local_heads
    attn_low, attn_f32, lse, top = attention_forward(q_src, kv_src, cols, seg_q, seg_row, head_dim)
    head_vector = lax.dynamic_update_slice_in_dim(
        jnp.full((heads,), NEG, F32), jnp.max(top, axis=(1, 2)) * head_dim**-0.5, first_head, 0
    )
    head_max = lax.pmax(head_vector, ALL)
    attn_rows = to_rows_back(attn_low)
    out_heads = own_out.reshape(local_heads, head_dim, width)
    branch = jnp.einsum("htc,hcd->td", attn_rows, out_heads, preferred_element_type=F32)
    inputs = own_tokens.astype(F32)
    mid = inputs + sum_scatter(branch, ULY)

    scale_two = rms_scale(mid)
    normed_two = mid * scale_two
    hidden_two = (normed_two * gain_ffn).astype(BF16)
    hidden_blk = lax.all_gather(hidden_two, "blk", axis=0, tiled=True)
    probs_blk = jax.nn.softmax(dot_nn(hidden_blk, whole_router), axis=1)
    names = jnp.arange(number, dtype=jnp.int32)
    chosen_blk = jnp.any(routes_blk[:, :, None] == names, axis=1).astype(F32)
    own_names = blk_at * local_experts
    gates = lax.dynamic_slice_in_dim(probs_blk * chosen_blk, own_names, local_experts, axis=1)
    most = min(MOST_TOKENS, hidden_blk.shape[0])
    nothing = jnp.zeros((most, width), BF16)
    packed_weights = jnp.concatenate([whole_gate_up, whole_down], axis=3)
    made = []
    for at in range(0, hidden_blk.shape[0], most):
        hidden_part, grad_part = hidden_blk[at : at + most], grad_blk[at : at + most]
        made.append(
            experts(
                hidden_part,
                hidden_part.T,
                grad_part,
                grad_part.T,
                gates[at : at + most],
                nothing,
                nothing,
                packed_weights,
            )
        )
    out_part = jnp.concatenate([m[0] for m in made], axis=0)
    dx_part = jnp.concatenate([m[1] for m in made], axis=0)
    dg_part = jnp.concatenate([m[2] for m in made], axis=1)
    expert_grads = sum(m[3].astype(F32) for m in made).astype(BF16)
    expert_sums = lax.psum_scatter(expert_grads, PLANE, scatter_dimension=0, tiled=False).astype(F32)
    grad_gate_up = jnp.concatenate([expert_sums[0], expert_sums[1]], axis=2)
    grad_down = expert_sums[2]
    dg_parts = swap(dg_part.reshape(local_experts, blk, count_tok).transpose(1, 2, 0), "blk")
    grad_gates = dg_parts.transpose(1, 0, 2).reshape(count_tok, number)
    dx_sum = sum_scatter(dx_part, "blk")
    output = (mid + sum_scatter(out_part, "blk")).astype(BF16)
    router_probs = lax.dynamic_slice_in_dim(probs_blk, blk_at * count_tok, count_tok)
    chosen = lax.dynamic_slice_in_dim(chosen_blk, blk_at * count_tok, count_tok)
    grad_probs = chosen * grad_gates
    grad_logits = (
        router_probs * (grad_probs - jnp.sum(router_probs * grad_probs, axis=1, keepdims=True))
    ).astype(BF16)
    grad_hidden_two = dx_sum + dot_nt(grad_logits, whole_router)
    grad_router_part = dot_tn(hidden_two, grad_logits)
    grad_gain_ffn = jnp.sum(grad_hidden_two * normed_two, axis=0)
    grad_mid = own_grad.astype(F32) + norm_back(grad_hidden_two * gain_ffn, mid, scale_two)

    branch_grad = lax.all_gather(grad_mid.astype(BF16), ULY, axis=0, tiled=True)
    grad_attn = dot_nt(branch_grad, own_out).astype(BF16)
    grad_attn = to_heads(grad_attn.reshape(rows, local_heads, head_dim).transpose(1, 0, 2))
    grad_out_part = jnp.einsum("htc,td->hcd", attn_rows, branch_grad, preferred_element_type=F32)
    dq, dk, dv = attention_backward(
        q_src, kv_src, cols, grad_attn, attn_f32, lse, seg_q, seg_row, head_dim
    )
    if by_heads:
        dqkv = to_rows_back(jnp.concatenate([dq, dk, dv], axis=2))
        dq, dk, dv = jnp.split(dqkv, 3, axis=2)
    else:
        dk, dv = (lax.psum_scatter(g, "blk", scatter_dimension=1, tiled=True) for g in (dk, dv))
    dq, dk, dv = (g.transpose(1, 0, 2) for g in (dq, dk, dv))
    grad_query_norm = rotate(dq.astype(F32), cos_table, -sin_table)
    grad_key_norm = rotate(dk.astype(F32), cos_table, -sin_table)
    grad_gain_query = jnp.sum(grad_query_norm * (query_raw * query_scale), axis=(0, 1))
    grad_gain_key = jnp.sum(grad_key_norm * (key_raw * key_scale), axis=(0, 1))
    grad_projected = jnp.concatenate(
        [
            norm_back(grad_query_norm * gain_query, query_raw, query_scale)
            .reshape(rows, local_width)
            .astype(BF16),
            norm_back(grad_key_norm * gain_key, key_raw, key_scale)
            .reshape(rows, local_width)
            .astype(BF16),
            dv.reshape(rows, local_width),
        ],
        axis=1,
    )
    grad_hidden_part = dot_nt(grad_projected, own_qkv)
    grad_hidden_one = sum_scatter(grad_hidden_part, ULY)
    grad_gain_attn = jnp.sum(grad_hidden_part * normed_one, axis=0)
    grad_inputs = grad_mid + norm_back(grad_hidden_one * gain_attn, inputs, rms_scale(inputs))

    grad_qkv_part = dot_tn(hidden_one, grad_projected).astype(BF16)
    grad_qkv_rows = lax.psum_scatter(grad_qkv_part, ROWS, scatter_dimension=0, tiled=True)
    grad_qkv_rows = swap(grad_qkv_rows.reshape(uly, shard_rows, 3 * local_width), ULY)
    grad_qkv = (
        grad_qkv_rows.reshape(uly, shard_rows, 3, local_width)
        .transpose(1, 2, 0, 3)
        .reshape(shard_rows, 3 * width)
        .astype(F32)
    )
    grad_out_rows = lax.psum_scatter(
        grad_out_part.reshape(local_width, width).astype(BF16), ROWS, scatter_dimension=0, tiled=True
    )
    grad_out = lax.ppermute(grad_out_rows, ALL, [(b, a) for a, b in to_rows]).astype(F32)
    small = jnp.concatenate([grad_gain_attn[:, None], grad_gain_ffn[:, None], grad_router_part], axis=1)
    small = lax.psum_scatter(small, ALL, scatter_dimension=0, tiled=True)
    grad_qk_gain = lax.psum(jnp.stack([grad_gain_query, grad_gain_key]), ALL)

    clip_gamma = TAU / jnp.maximum(head_max, TAU)
    factor = jnp.repeat(jnp.sqrt(clip_gamma), head_dim)
    column_scale = jnp.concatenate([factor, factor, jnp.ones((width,), F32)])
    clipped = w_qkv.astype(F32) * column_scale[None, :]
    return (
        output[None],
        grad_inputs[None],
        grad_qkv,
        grad_out,
        small[:, 0],
        small[:, 1],
        grad_qk_gain,
        small[:, 2:],
        grad_gate_up,
        grad_down,
        clipped,
    )


def per_device(
    tokens, segments, routes, w_qkv, w_out, attn_gain, ffn_gain, qk_gain, router, w_gate_up, w_down, cotangent
):
    own_tokens = tokens[0]
    own_grad = cotangent[0]
    count_tok, width = own_tokens.shape
    head_dim = qk_gain.shape[1]
    heads = width // head_dim
    batch, blk, uly = lax.axis_size("batch"), lax.axis_size("blk"), spread(ULY)
    total, group = batch * blk * uly, batch * blk
    local_experts = w_down.shape[0]
    if uly != 4 or heads != blk * uly or batch != 2 or local_experts != 4:
        return per_device_general(
            tokens, segments, routes, w_qkv, w_out, attn_gain, ffn_gain, qk_gain, router, w_gate_up, w_down, cotangent
        )
    blk_at, uly_at = lax.axis_index("blk"), lax.axis_index(ULY)
    rows = count_tok * uly
    seg_row = segments[0]
    length = seg_row.shape[0]
    number = router.shape[1]
    shard_rows = w_qkv.shape[0]

    to_rows = [(u * group + g, g * uly + u) for g in range(group) for u in range(uly)]
    own_rows = lax.ppermute(w_out, ALL, to_rows)
    half = local_experts // 2
    weights_first, weights_second = (
        lax.all_gather(jnp.concatenate([w_gate_up[at], w_down[at]], axis=2), PLANE, axis=0, tiled=False)
        for at in (slice(0, half), slice(half, local_experts))
    )
    extra = jnp.concatenate([attn_gain[None], ffn_gain[None], router.T], axis=0)
    kept = extra.shape[0]
    extra = jnp.pad(extra, ((0, -kept % 16), (0, -shard_rows % LANES)))
    by_head = w_qkv.reshape(shard_rows, 3, heads, head_dim).transpose(2, 0, 1, 3)
    own_qkv, extras, toks = startup(
        by_head.reshape(heads, shard_rows, 3 * head_dim), extra, own_tokens, 0
    )
    own_rows, extras = lax.optimization_barrier((own_rows, extras))
    own_out = lax.all_to_all(
        jnp.broadcast_to(own_rows[None], (group, *own_rows.shape)), ROWS, split_axis=0, concat_axis=0, tiled=True
    ).reshape(blk, head_dim, width)
    own_qkv = own_qkv.reshape(width, 3 * head_dim)
    extras = extras[:, :kept, :shard_rows].transpose(1, 0, 2).reshape(kept, width)
    gain_attn = extras[0].astype(F32)
    gain_ffn = extras[1].astype(F32)
    router_t = extras[2:]

    gains = qk_gain.astype(F32)
    cos, sin = rope_rows(length, head_dim)
    hidden_one, qkv, raw = project(
        toks.reshape(length, width), gain_attn[None], own_qkv, cos, sin, gains
    )
    attn_low, attn_f32, lse, top = attention_forward(
        qkv[None], qkv[None], (0, 1, 2), seg_row, seg_row, head_dim
    )
    (attn_rows,) = exchange([(attn_low.reshape(blk, rows, head_dim), ("blk",), "swap")], 1)
    branch = jnp.einsum("htc,hcd->td", attn_rows, own_out, preferred_element_type=F32)
    branch, grad_blk, routes_blk = exchange(
        [
            (branch.astype(BF16).reshape(uly, count_tok, width), ULY, "swap"),
            (own_grad, ("blk",), "line"),
            (routes[0].T, ("blk",), "gather"),
        ],
        2,
    )
    inputs = own_tokens.astype(F32)
    mid = inputs + jnp.sum(branch.astype(F32), axis=0)

    scale_two = rms_scale(mid)
    normed_two = mid * scale_two
    hidden_two = (normed_two * gain_ffn).astype(BF16)
    (hidden_blk,) = exchange([(hidden_two, ("blk",), "line")], 3, after=[weights_first])
    tokens_blk = blk * count_tok
    hidden_blk = hidden_blk.reshape(tokens_blk, width)
    grad_blk = grad_blk.reshape(tokens_blk, width)
    probs_blk = jax.nn.softmax(dot_nt(hidden_blk, router_t), axis=1)
    names = jnp.arange(number, dtype=jnp.int32)
    chosen_blk = jnp.any(routes_blk[:, :, :, None] == names, axis=1).astype(F32)
    chosen_blk = chosen_blk.reshape(tokens_blk, number)
    gates = lax.dynamic_slice_in_dim(
        probs_blk * chosen_blk, blk_at * local_experts, local_experts, axis=1
    )
    nothing = jnp.zeros((tokens_blk, width), BF16)
    shared = (hidden_blk, hidden_blk.T, grad_blk, grad_blk.T)
    out_first, dx_first, dg_first, *grads_first = experts(
        *shared, gates[:, :half], nothing, nothing, weights_first, collective_id=9
    )
    out_part, dx_part, dg_second, *grads_second = experts(
        *shared, gates[:, half:], out_first, dx_first, weights_second, collective_id=10
    )

    def reduce_experts(keep_x, give_x, keep_y, give_y):
        other = [(0, 1), (1, 0)]
        got_x = lax.ppermute(give_x, "batch", other)
        got_y = lax.ppermute(give_y, "y", other)
        last_x = lax.ppermute(keep_x[1] + got_x[1], "y", other)
        last_y = lax.ppermute(keep_y[1] + got_y[1], "batch", other)
        return (keep_x, got_x, last_x), (keep_y, got_y, last_y)

    reduced_first = reduce_experts(*grads_first)
    finished = finish_experts(*reduced_first, 0, local_experts)
    grad_gate_up, grad_down = finish_experts(
        *reduce_experts(*grads_second), half, local_experts, before=finished
    )
    dg_part = jnp.concatenate([dg_first, dg_second], axis=0).reshape(local_experts, blk, count_tok)
    dx_parts, dg_parts = exchange(
        [
            (dx_part.reshape(blk, count_tok, width), ("blk",), "swap"),
            (dg_part.transpose(1, 0, 2), ("blk",), "swap"),
        ],
        4,
    )
    out_part = out_part.reshape(blk, count_tok, width)
    out_part, sent_qkv, dx_parts = lax.optimization_barrier((out_part, own_qkv, dx_parts))
    out_parts = lax.all_to_all(out_part, "blk", split_axis=0, concat_axis=0, tiled=True)
    output = (mid + jnp.sum(out_parts.astype(F32), axis=0)).astype(BF16)
    to_far = [(u, (u + 2) % uly) for u in range(uly)]
    to_near = [(u, u ^ 1) for u in range(uly)]
    far_qkv = lax.ppermute(sent_qkv, ULY, to_far)
    near_qkv = lax.ppermute(sent_qkv, ULY, to_near)
    cross_qkv = lax.ppermute(far_qkv, ULY, to_near)
    router_probs = lax.dynamic_slice_in_dim(probs_blk, blk_at * count_tok, count_tok)
    chosen = lax.dynamic_slice_in_dim(chosen_blk, blk_at * count_tok, count_tok)
    grad_probs = chosen * dg_parts.reshape(number, count_tok).T
    grad_logits = (
        router_probs * (grad_probs - jnp.sum(router_probs * grad_probs, axis=1, keepdims=True))
    ).astype(BF16)
    grad_hidden_two = jnp.sum(dx_parts.astype(F32), axis=0) + dot_nn(grad_logits, router_t)
    grad_router_t = dot_tn(grad_logits, hidden_two)
    grad_gain_ffn = jnp.sum(grad_hidden_two * normed_two, axis=0)
    grad_mid = own_grad.astype(F32) + norm_back(grad_hidden_two * gain_ffn, mid, scale_two)

    (branch_grad,) = exchange([(grad_mid.astype(BF16), ULY, "relay")], 5)
    branch_grad = branch_grad.reshape(rows, width)
    grad_attn = jnp.einsum("td,hcd->htc", branch_grad, own_out, preferred_element_type=F32).astype(BF16)
    (grad_attn,) = exchange([(grad_attn, ("blk",), "swap")], 6, after=[out_parts])
    grad_out_part = jnp.einsum("htc,td->hcd", attn_rows, branch_grad, preferred_element_type=F32)
    grad_out_parts = lax.all_to_all(
        grad_out_part.astype(BF16).reshape(group, shard_rows, width),
        ROWS,
        split_axis=0,
        concat_axis=0,
        tiled=True,
    )
    grad_out = lax.ppermute(
        jnp.sum(grad_out_parts.astype(F32), axis=0).astype(BF16), ALL, [(b, a) for a, b in to_rows]
    ).astype(F32)
    grad_projected, grad_gains = project_back(
        qkv, grad_attn.reshape(length, head_dim), attn_f32, lse, seg_row, raw, cos, sin, gains
    )
    by_uly = grad_projected.reshape(blk, uly, count_tok, 3 * head_dim).transpose(1, 0, 2, 3)
    grad_qkv_part = dot_tn(hidden_one, grad_projected).astype(BF16)
    by_batch = grad_qkv_part.reshape(batch, width // batch, 3 * head_dim)
    batch_at = lax.axis_index("batch")
    projected_blk, got_qkv_part = exchange(
        [
            (by_uly.reshape(uly, tokens_blk, 3 * head_dim), ULY, "swap"),
            (
                lax.dynamic_index_in_dim(by_batch, 1 - batch_at, 0, keepdims=False),
                ("batch",),
                "trade",
            ),
        ],
        7,
        after=[grad_out_parts, reduced_first[0][2], reduced_first[1][2], far_qkv],
    )
    grad_qkv_part = lax.dynamic_index_in_dim(by_batch, batch_at, 0, keepdims=False) + got_qkv_part

    near_at, far_at = uly_at + 1 - 2 * lax.rem(uly_at, 2), lax.rem(uly_at + 2, uly)
    cross_at = lax.rem(near_at + 2, uly)
    grad_hidden_part = sum(
        dot_nt(lax.dynamic_index_in_dim(projected_blk, sender, 0, keepdims=False), weights)
        for sender, weights in [
            (uly_at, own_qkv),
            (near_at, near_qkv),
            (far_at, far_qkv),
            (cross_at, cross_qkv),
        ]
    )
    inputs_blk = lax.dynamic_index_in_dim(toks, uly_at, 1, keepdims=False)
    inputs_blk = inputs_blk.reshape(tokens_blk, width).astype(F32)
    grad_gain_attn = jnp.sum(grad_hidden_part * (inputs_blk * rms_scale(inputs_blk)), axis=0)

    small = jnp.concatenate([grad_gain_attn[None], grad_gain_ffn[None], grad_router_t], axis=0)
    small = small.reshape(kept, total, shard_rows).transpose(1, 0, 2)
    small = jnp.pad(small, ((0, 0), (0, 0), (0, LANES - shard_rows)))
    head_row = jnp.where(
        jnp.arange(LANES) == uly_at * blk + blk_at, jnp.max(top) * head_dim**-0.5, NEG
    )
    to_all = jnp.concatenate([grad_gains, head_row[None]], axis=0)
    small = jnp.concatenate([small, jnp.broadcast_to(to_all[None], (total, 3, LANES))], axis=1)
    small = jnp.pad(small, ((0, 0), (0, -small.shape[1] % 8), (0, 0)))
    grad_hidden_parts, small, grad_qkv_parts = exchange(
        [
            (grad_hidden_part.astype(BF16).reshape(blk, count_tok, width), ("blk",), "swap"),
            (small, ALL, "swap"),
            (grad_qkv_part.reshape(total // batch, shard_rows, 3 * head_dim), ("blk", *ULY), "swap"),
        ],
        8,
    )
    grad_qkv = merge_heads(grad_qkv_parts.reshape(blk, uly, shard_rows, 3 * head_dim))
    grad_hidden_one = jnp.sum(grad_hidden_parts.astype(F32), axis=0)
    grad_inputs = grad_mid + norm_back(grad_hidden_one * gain_attn, inputs, rms_scale(inputs))
    sums = jnp.sum(small, axis=0)
    head_max = jnp.max(small[:, kept + 2, :heads], axis=0)
    factor = jnp.repeat(jnp.sqrt(TAU / jnp.maximum(head_max, TAU)), head_dim)
    column_scale = jnp.concatenate([factor, factor, jnp.ones((width,), F32)])
    clipped = w_qkv.astype(F32) * column_scale[None, :]
    return (
        output[None],
        grad_inputs[None],
        grad_qkv,
        grad_out,
        sums[0, :shard_rows],
        sums[1, :shard_rows],
        sums[kept : kept + 2],
        sums[2:kept, :shard_rows].T,
        grad_gate_up,
        grad_down,
        clipped,
    )


def solution(mesh):
    in_specs = (
        P("batch", ("blk", *ULY), None),
        P("batch", None),
        P("batch", ("blk", *ULY), None),
        P(ALL, None),
        P(ALL, None),
        P(ALL),
        P(ALL),
        P(),
        P(ALL, None),
        P("blk", PLANE, None),
        P("blk", PLANE, None),
        P("batch", ("blk", *ULY), None),
    )
    out_specs = (
        P("batch", ("blk", *ULY), None),
        P("batch", ("blk", *ULY), None),
        P(ALL, None),
        P(ALL, None),
        P(ALL),
        P(ALL),
        P(),
        P(ALL, None),
        P("blk", PLANE, None),
        P("blk", PLANE, None),
        P(ALL, None),
    )
    cores = 2 - mesh.shape["uly"] % 2
    mesh = Mesh(
        mesh.devices.reshape(*(mesh.shape[axis] for axis in ROWS), mesh.shape["uly"] // cores, cores), ALL
    )
    return jax.shard_map(
        per_device, mesh=mesh, in_specs=in_specs, out_specs=out_specs, check_vma=False
    )
```

```python
import functools
import math

import jax
import jax.numpy as jnp
from jax import lax
from jax.experimental import pallas as pl
from jax.experimental.pallas import tpu as pltpu
from jax.sharding import Mesh
from jax.sharding import PartitionSpec as P

EPS = 1e-06
THETA = 50000.0
TAU = 4.0
NEG = -1e30
LOG2E = 1.4426950408889634
LANES = 128
MOST_TOKENS = 512
VMEM_LIMIT = 60 * 1024 * 1024

ULY = ("y", "core")
ALL = ("batch", "blk", *ULY)
ROWS = ("batch", "blk")
PLANE = ("batch", *ULY)
CHIPS = ("batch", "y")

MESH = pl.DeviceIdType.MESH
BF16 = jnp.bfloat16
F32 = jnp.float32


def rms_scale(values):
    return lax.rsqrt(jnp.mean(values * values, axis=-1, keepdims=True) + EPS)


def norm_back(grad_normed, values, scale):
    normed = values * scale
    return scale * (grad_normed - normed * jnp.mean(grad_normed * normed, axis=-1, keepdims=True))


def rope_tables(offset, length, head_dim):
    half_dim = head_dim // 2
    frequency = THETA ** (-jnp.arange(half_dim, dtype=F32) * 2.0 / head_dim)
    positions = (offset + jnp.arange(length, dtype=jnp.int32)).astype(F32)
    angles = positions[:, None] * frequency[None, :]
    return (jnp.cos(angles)[:, None, :], jnp.sin(angles)[:, None, :])


def rope_rows(length, head_dim):
    fine = math.gcd(length, LANES)
    frequency = THETA ** (-jnp.arange(head_dim // 2, dtype=F32) * 2.0 / head_dim)
    frequency = jnp.concatenate([frequency, frequency])
    coarse_angle = (jnp.arange(length // fine, dtype=F32) * fine)[:, None, None] * frequency
    fine_angle = jnp.arange(fine, dtype=F32)[None, :, None] * frequency
    cos_a, sin_a, cos_b, sin_b = lax.optimization_barrier(
        (jnp.cos(coarse_angle), jnp.sin(coarse_angle), jnp.cos(fine_angle), jnp.sin(fine_angle))
    )
    sign = jnp.where(jnp.arange(head_dim) < head_dim // 2, -1.0, 1.0)
    cos = cos_a * cos_b - sin_a * sin_b
    sin = (sin_a * cos_b + cos_a * sin_b) * sign
    return cos.reshape(length, head_dim), sin.reshape(length, head_dim)


def rotate(values, cos_table, sin_table):
    half_dim = values.shape[-1] // 2
    first = values[..., :half_dim]
    second = values[..., half_dim:]
    return jnp.concatenate(
        [first * cos_table - second * sin_table, second * cos_table + first * sin_table], axis=-1
    )


def dot_nn(a, b):
    return lax.dot_general(a, b, (((1,), (0,)), ((), ())), preferred_element_type=F32)


def dot_nt(a, b):
    return lax.dot_general(a, b, (((1,), (1,)), ((), ())), preferred_element_type=F32)


def dot_tn(a, b):
    return lax.dot_general(a, b, (((0,), (0,)), ((), ())), preferred_element_type=F32)


def key_chunks(length):
    size = min(512, length)
    return size, length // size


def attn_fwd_kernel(factor, q_ref, k_ref, v_ref, sq_ref, sk_ref, o_ref, of_ref, lse_ref, top_ref, vt_ref):
    length = k_ref.shape[1]
    size, count = key_chunks(length)
    tile, head_dim = q_ref.shape[1:]

    @pl.when(pl.program_id(1) == 0)
    def _():
        vt_ref[...] = v_ref[0].astype(F32).T.astype(BF16)

    q = q_ref[0]
    seg_q = sq_ref[...]

    def step(j, carried):
        total, top, acc = carried
        at = pl.multiple_of(j * size, size)
        scores = dot_nt(k_ref[0, pl.ds(at, size), :], q)
        scores = jnp.where(sk_ref[pl.ds(at, size), :] == seg_q, scores, NEG)
        top = jnp.maximum(top, jnp.max(scores, axis=0, keepdims=True))
        weights = jnp.exp2(scores * factor)
        total = total + jnp.sum(weights, axis=0, keepdims=True)
        acc = acc + dot_nn(vt_ref[:, pl.ds(at, size)], weights.astype(BF16))
        return total, top, acc

    start = (
        jnp.zeros((1, tile), F32),
        jnp.full((1, tile), NEG, F32),
        jnp.zeros((head_dim, tile), F32),
    )
    total, top, acc = lax.fori_loop(0, count, step, start, unroll=count <= 4)
    out = (acc * (1.0 / total)).T
    o_ref[0] = out.astype(BF16)
    of_ref[0] = out
    lse_ref[0] = jnp.log2(total)
    top_ref[0] = top


def attn_bwd_kernel(
    factor, scale, q_ref, k_ref, v_ref, do_ref, of_ref, lse_ref, sq_ref, sk_ref,
    dq_ref, dk_ref, dv_ref, kt_ref, dk_acc, dv_acc,
):
    length = k_ref.shape[1]
    size, count = key_chunks(length)
    tile, head_dim = q_ref.shape[1:]

    @pl.when(pl.program_id(1) == 0)
    def _():
        kt_ref[...] = k_ref[0].astype(F32).T.astype(BF16)
        dk_acc[...] = jnp.zeros_like(dk_acc)
        dv_acc[...] = jnp.zeros_like(dv_acc)

    q = q_ref[0]
    grad = do_ref[0]
    seg_q = sq_ref[...]
    lse = lse_ref[0]
    row_dot = jnp.sum((grad.astype(F32) * of_ref[0]).T, axis=0, keepdims=True)

    def step(j, dq_t):
        at = pl.multiple_of(j * size, size)
        rows = pl.ds(at, size)
        scores = dot_nt(k_ref[0, rows, :], q)
        scores = jnp.where(sk_ref[rows, :] == seg_q, scores, NEG)
        weights = jnp.exp2(scores * factor - lse)
        grad_weights = dot_nt(v_ref[0, rows, :], grad)
        grad_scores = (weights * (grad_weights - row_dot)).astype(BF16)
        dk_acc[rows, :] += dot_nn(grad_scores, q)
        dv_acc[rows, :] += dot_nn(weights.astype(BF16), grad)
        return dq_t + dot_nn(kt_ref[:, rows], grad_scores)

    dq_t = lax.fori_loop(0, count, step, jnp.zeros((head_dim, tile), F32), unroll=count <= 4)
    dq_ref[0] = (dq_t * scale).T.astype(BF16)

    @pl.when(pl.program_id(1) == pl.num_programs(1) - 1)
    def _():
        dk_ref[0] = (dk_acc[...] * scale).astype(BF16)
        dv_ref[0] = dv_acc[...].astype(BF16)


def attention_tile(queries, length):
    return min(queries, 256 if length <= 4096 else 128)


def attention_forward(q_src, kv_src, cols, seg_q, seg_k, head_dim):
    heads, queries = q_src.shape[:2]
    length = kv_src.shape[1]
    tile = attention_tile(queries, length)
    q_col, k_col, v_col = cols
    factor = head_dim**-0.5 * LOG2E
    row = pl.BlockSpec((1, 1, tile), lambda h, i: (h, 0, i))
    block = pl.BlockSpec((1, tile, head_dim), lambda h, i: (h, i, 0))
    return pl.pallas_call(
        functools.partial(attn_fwd_kernel, factor),
        grid=(heads, queries // tile),
        in_specs=[
            pl.BlockSpec((1, tile, head_dim), lambda h, i: (h, i, q_col)),
            pl.BlockSpec((1, length, head_dim), lambda h, i: (h, 0, k_col)),
            pl.BlockSpec((1, length, head_dim), lambda h, i: (h, 0, v_col)),
            pl.BlockSpec((1, tile), lambda h, i: (0, i)),
            pl.BlockSpec((length, 1), lambda h, i: (0, 0)),
        ],
        out_specs=[block, block, row, row],
        out_shape=[
            jax.ShapeDtypeStruct((heads, queries, head_dim), BF16),
            jax.ShapeDtypeStruct((heads, queries, head_dim), F32),
            jax.ShapeDtypeStruct((heads, 1, queries), F32),
            jax.ShapeDtypeStruct((heads, 1, queries), F32),
        ],
        scratch_shapes=[pltpu.VMEM((head_dim, length), BF16)],
        compiler_params=pltpu.CompilerParams(vmem_limit_bytes=VMEM_LIMIT),
        cost_estimate=pl.CostEstimate(
            flops=4 * heads * queries * length * head_dim,
            bytes_accessed=heads * (queries + length) * head_dim * 8,
            transcendentals=heads * queries * length,
        ),
        name="attend",
    )(q_src, kv_src, kv_src, seg_q.reshape(1, -1), seg_k.reshape(-1, 1))


def attention_backward(q_src, kv_src, cols, grad, out_f32, lse, seg_q, seg_k, head_dim):
    heads, queries = q_src.shape[:2]
    length = kv_src.shape[1]
    tile = attention_tile(queries, length)
    q_col, k_col, v_col = cols
    scale = head_dim**-0.5
    row = pl.BlockSpec((1, 1, tile), lambda h, i: (h, 0, i))
    block = pl.BlockSpec((1, tile, head_dim), lambda h, i: (h, i, 0))
    whole = pl.BlockSpec((1, length, head_dim), lambda h, i: (h, 0, 0))
    return pl.pallas_call(
        functools.partial(attn_bwd_kernel, scale * LOG2E, scale),
        grid=(heads, queries // tile),
        in_specs=[
            pl.BlockSpec((1, tile, head_dim), lambda h, i: (h, i, q_col)),
            pl.BlockSpec((1, length, head_dim), lambda h, i: (h, 0, k_col)),
            pl.BlockSpec((1, length, head_dim), lambda h, i: (h, 0, v_col)),
            block,
            block,
            row,
            pl.BlockSpec((1, tile), lambda h, i: (0, i)),
            pl.BlockSpec((length, 1), lambda h, i: (0, 0)),
        ],
        out_specs=[block, whole, whole],
        out_shape=[
            jax.ShapeDtypeStruct((heads, queries, head_dim), BF16),
            jax.ShapeDtypeStruct((heads, length, head_dim), BF16),
            jax.ShapeDtypeStruct((heads, length, head_dim), BF16),
        ],
        scratch_shapes=[
            pltpu.VMEM((head_dim, length), BF16),
            pltpu.VMEM((length, head_dim), F32),
            pltpu.VMEM((length, head_dim), F32),
        ],
        compiler_params=pltpu.CompilerParams(vmem_limit_bytes=VMEM_LIMIT),
        cost_estimate=pl.CostEstimate(
            flops=10 * heads * queries * length * head_dim,
            bytes_accessed=heads * (queries + length) * head_dim * 12,
            transcendentals=heads * queries * length,
        ),
        name="attend_back",
    )(q_src, kv_src, kv_src, grad, out_f32, lse, seg_q.reshape(1, -1), seg_k.reshape(-1, 1))


def expert_step(expert, h_ref, ht_ref, dy_ref, dyt_ref, gate_ref, wg_ref, wu_ref, wd_ref, dg_ref, out_acc, dx_acc):
    width = h_ref.shape[1]
    cols = wg_ref.shape[3]
    w_gate = wg_ref[...].reshape(width, cols)
    w_up = wu_ref[...].reshape(width, cols)
    w_down = wd_ref[...].reshape(width, cols)
    gates = gate_ref[...]
    mine = lax.broadcasted_iota(jnp.int32, gates.shape, 1) == expert
    gate = jnp.sum(jnp.where(mine, gates, 0.0), axis=1, keepdims=True)
    a_gate = dot_nn(h_ref[...], w_gate)
    a_up = dot_nn(h_ref[...], w_up)
    raw = dot_nn(dy_ref[...], w_down)
    sigma = 1.0 / (1.0 + jnp.exp2(a_gate * -LOG2E))
    swish = a_gate * sigma
    act = swish * a_up
    dg_ref[0] += jnp.sum(raw * act, axis=1, keepdims=True)
    gated = (gate * act).astype(BF16)
    d_act = gate * raw
    d_gate = (d_act * a_up * (sigma + swish * (1.0 - sigma))).astype(BF16)
    d_up = (d_act * swish).astype(BF16)
    out_acc[...] += dot_nt(gated, w_down)
    dx_acc[...] += dot_nt(d_gate, w_gate) + dot_nt(d_up, w_up)
    for part, (left, right) in enumerate([(ht_ref, d_gate), (ht_ref, d_up), (dyt_ref, gated)]):
        yield part, dot_nn(left[...], right).astype(BF16)


def expert_kernel(
    h_ref, ht_ref, dy_ref, dyt_ref, gate_ref, wg_ref, wu_ref, wd_ref,
    out_ref, dx_ref, dg_ref, gr_ref, out_acc, dx_acc,
):
    step, last = pl.program_id(0), pl.num_programs(0) - 1
    parts, _, part_rows, cols = wg_ref.shape
    chunks = (last + 1) // gate_ref.shape[1]

    @pl.when(step == 0)
    def _():
        out_acc[...] = jnp.zeros_like(out_acc)
        dx_acc[...] = jnp.zeros_like(dx_acc)

    @pl.when(step % chunks == 0)
    def _():
        dg_ref[...] = jnp.zeros_like(dg_ref)

    for part, made in expert_step(
        step // chunks, h_ref, ht_ref, dy_ref, dyt_ref, gate_ref, wg_ref, wu_ref, wd_ref, dg_ref, out_acc, dx_acc
    ):
        gr_ref[:, part, 0] = made.reshape(parts, part_rows, cols)

    @pl.when(step == last)
    def _():
        out_ref[...] = out_acc[...].astype(BF16)
        dx_ref[...] = dx_acc[...].astype(BF16)


def expert_pair_kernel(carried, *refs):
    h_ref, ht_ref, dy_ref, dyt_ref, gate_ref, wg_ref, wu_ref, wd_ref = refs[:8]
    if carried:
        out0_ref, dx0_ref, carry_x, carry_y = refs[8:12]
        carried_x, carried_y, carry_send, carry_recv = *refs[19:21], *refs[-2:]
        refs = refs[4:19] + refs[21:-2]
    out_ref, dx_ref, dg_ref, keep_x, give_x, keep_y, give_y = refs[8:15]
    out_acc, dx_acc, made_ref, got_ref, send, recv, free = refs[15:]
    step, last = pl.program_id(0), pl.num_programs(0) - 1
    parts, _, part_rows, cols = wg_ref.shape
    chunks = last // 2
    b, y, core = lax.axis_index("batch"), lax.axis_index("y"), lax.axis_index("core")
    near = {"core": 1 - core}
    slot, before = lax.rem(step, 2), lax.rem(step + 1, 2)

    def carry(index, src, dst, to):
        return pltpu.make_async_remote_copy(
            src_ref=src,
            dst_ref=dst,
            send_sem=carry_send.at[index],
            recv_sem=carry_recv.at[index],
            device_id=to,
            device_id_type=MESH,
        )

    def carries():
        if not carried:
            return []
        return [
            carry(0, carry_x, carried_x, {"batch": 1 - b}),
            carry(1, carry_y, carried_y, {"y": 1 - y}),
        ]

    @pl.when(step == 0)
    def _():
        barrier = pltpu.get_barrier_semaphore()
        greeted = [near, {"batch": 1 - b}, {"y": 1 - y}] if carried else [near]
        for to in greeted:
            pl.semaphore_signal(barrier, inc=1, device_id=to, device_id_type=MESH)
        pl.semaphore_wait(barrier, len(greeted))
        for copy in carries():
            copy.start()
        if carried:
            out_acc[...] = out0_ref[...].astype(F32)
            dx_acc[...] = dx0_ref[...].astype(F32)
        else:
            out_acc[...] = jnp.zeros_like(out_acc)
            dx_acc[...] = jnp.zeros_like(dx_acc)

    def hand_over(at):
        return pltpu.make_async_remote_copy(
            src_ref=made_ref.at[at, 1 - core],
            dst_ref=got_ref.at[at],
            send_sem=send.at[at],
            recv_sem=recv.at[at],
            device_id=near,
            device_id_type=MESH,
        )

    @pl.when(step < last)
    def _():
        @pl.when(step % chunks == 0)
        def _():
            dg_ref[...] = jnp.zeros_like(dg_ref)

        for part, made in expert_step(
            step // chunks, h_ref, ht_ref, dy_ref, dyt_ref, gate_ref, wg_ref, wu_ref, wd_ref, dg_ref, out_acc, dx_acc
        ):
            made = made.reshape(parts // 2, 2, part_rows, cols)
            made_ref[slot, 0, :, part] = made[:, 0]
            made_ref[slot, 1, :, part] = made[:, 1]

        @pl.when(step >= 2)
        def _():
            pl.semaphore_wait(free, 1)

        hand_over(slot).start()

    def total(other_b, other_y):
        at = (b + other_b) % 2 * 2 + (y + other_y) % 2
        both = made_ref[before, core, at].astype(F32) + got_ref[before, at].astype(F32)
        return both.astype(BF16)

    @pl.when(step > 0)
    def _():
        hand_over(before).wait()

        @pl.when(step <= chunks)
        def _():
            for other in range(2):
                keep_x[other] = total(0, other)
                give_x[other] = total(1, other)

        @pl.when(step > chunks)
        def _():
            for other in range(2):
                keep_y[other] = total(other, 0)
                give_y[other] = total(other, 1)

        @pl.when(step < last - 1)
        def _():
            pl.semaphore_signal(free, inc=1, device_id=near, device_id_type=MESH)

    @pl.when(step == last)
    def _():
        out_ref[...] = out_acc[...].astype(BF16)
        dx_ref[...] = dx_acc[...].astype(BF16)
        for copy in carries():
            copy.wait()


def experts(hidden, hidden_t, grad, grad_t, gates, weights, collective_id=None, before=()):
    tokens, width = hidden.shape
    parts, count, part_rows, units = weights.shape
    units = units // 3
    cols = min(256, units)
    chunks = units // cols
    steps = count * chunks
    paired = collective_id is not None
    once = pl.Buffered(1)
    whole = pl.BlockSpec((tokens, width), lambda s: (0, 0), pipeline_mode=once)
    whole_t = pl.BlockSpec((width, tokens), lambda s: (0, 0), pipeline_mode=once)
    result = pl.BlockSpec((tokens, width), lambda s: (0, 0))

    def now(step):
        return jnp.minimum(step, steps - 1)

    def weight(kind):
        def index(step):
            at = now(step)
            return (0, at // chunks, 0, kind * chunks + at % chunks)

        return pl.BlockSpec((parts, 1, part_rows, cols), index)

    def written(expert):
        return lambda s: (0, 0, 0, jnp.clip(s - 1 - expert * chunks, 0, chunks - 1))

    scratch = [pltpu.VMEM((tokens, width), F32), pltpu.VMEM((tokens, width), F32)]
    if paired:
        scratch += [
            pltpu.VMEM((2, 2, parts // 2, 3, part_rows, cols), BF16),
            pltpu.VMEM((2, parts // 2, 3, part_rows, cols), BF16),
            pltpu.SemaphoreType.DMA((2,)),
            pltpu.SemaphoreType.DMA((2,)),
            pltpu.SemaphoreType.REGULAR,
        ]
        grad_specs = [
            pl.BlockSpec((2, 3, part_rows, cols), written(expert)) for expert in (0, 0, 1, 1)
        ]
        grad_shapes = [jax.ShapeDtypeStruct((2, 3, part_rows, units), BF16)] * 4
        if before:
            grad_specs += [pl.BlockSpec(memory_space=pl.ANY)] * 2
            grad_shapes += grad_shapes[:2]
            scratch += [pltpu.SemaphoreType.DMA((2,))] * 2
    else:
        grad_specs = [
            pl.BlockSpec((parts, 3, 1, part_rows, cols), lambda s: (0, 0, s // chunks, 0, s % chunks))
        ]
        grad_shapes = [jax.ShapeDtypeStruct((parts, 3, count, part_rows, units), BF16)]
    return pl.pallas_call(
        functools.partial(expert_pair_kernel, bool(before)) if paired else expert_kernel,
        grid=(steps + 1 if paired else steps,),
        in_specs=[
            whole,
            whole_t,
            whole,
            whole_t,
            pl.BlockSpec(gates.shape, lambda s: (0, 0), pipeline_mode=once),
            weight(0),
            weight(1),
            weight(2),
            *([whole, whole] + [pl.BlockSpec(memory_space=pl.ANY)] * 2 if before else []),
        ],
        out_specs=[
            result,
            result,
            pl.BlockSpec((1, tokens, 1), lambda s: (now(s) // chunks, 0, 0)),
            *grad_specs,
        ],
        out_shape=[
            jax.ShapeDtypeStruct((tokens, width), BF16),
            jax.ShapeDtypeStruct((tokens, width), BF16),
            jax.ShapeDtypeStruct((count, tokens, 1), F32),
            *grad_shapes,
        ],
        scratch_shapes=scratch,
        compiler_params=pltpu.CompilerParams(
            vmem_limit_bytes=VMEM_LIMIT, collective_id=collective_id, has_side_effects=paired
        ),
        cost_estimate=pl.CostEstimate(
            flops=18 * count * tokens * width * units,
            bytes_accessed=12 * count * width * units,
            transcendentals=count * tokens * units,
        ),
        name="experts",
    )(hidden, hidden_t, grad, grad_t, gates, weights, weights, weights, *before)


def finish_experts_kernel(*refs):
    *parts, gate_up_ref, down_ref = refs
    units = down_ref.shape[2]

    def write(kept, first, second):
        total = [
            kept[0, part].astype(F32) + first[0, part].astype(F32) + second[part].astype(F32)
            for part in range(3)
        ]
        gate_up_ref[0, :, :units] = total[0]
        gate_up_ref[0, :, units:] = total[1]
        down_ref[0] = total[2]

    pl.when(pl.program_id(0) == 0)(lambda: write(*parts[:3]))
    pl.when(pl.program_id(0) == 1)(lambda: write(*parts[3:6]))


def finish_experts(first, second, at, count, before=()):
    _, _, rows, units = first[0].shape
    tile = min(128, rows)
    steps = rows // tile

    def row(expert):
        if expert == 0:
            return lambda e, r: jnp.where(e == 0, r, steps - 1)
        return lambda e, r: jnp.where(e == 1, r, 0)

    def specs(expert):
        at_row = row(expert)
        pair = pl.BlockSpec((1, 3, tile, units), lambda e, r: (0, 0, at_row(e, r), 0))
        return [pair, pair, pl.BlockSpec((3, tile, units), lambda e, r: (0, at_row(e, r), 0))]

    return pl.pallas_call(
        lambda *refs: finish_experts_kernel(*refs[:6], *refs[-2:]),
        grid=(2, steps),
        in_specs=[*specs(0), *specs(1), *[pl.BlockSpec(memory_space=pl.ANY)] * len(before)],
        out_specs=[
            pl.BlockSpec((1, tile, 2 * units), lambda e, r: (at + e, r, 0)),
            pl.BlockSpec((1, tile, units), lambda e, r: (at + e, r, 0)),
        ],
        out_shape=[
            jax.ShapeDtypeStruct((count, rows, 2 * units), F32),
            jax.ShapeDtypeStruct((count, rows, units), F32),
        ],
        input_output_aliases={6 + i: i for i in range(len(before))},
        compiler_params=pltpu.CompilerParams(vmem_limit_bytes=VMEM_LIMIT),
        name="finish_experts",
    )(*first, *second, *before)


def turn(values, cos, sin):
    return values * cos + pltpu.roll(values, values.shape[1] // 2, 1) * sin


def project_kernel(
    tok_ref, gain_ref, w_ref, cos_ref, sin_ref, gains_ref, hidden_ref, qkv_ref, raw_ref
):
    head_dim = cos_ref.shape[1]
    values = tok_ref[...].astype(F32)
    hidden = (values * rms_scale(values) * gain_ref[...]).astype(BF16)
    hidden_ref[...] = hidden
    projected = dot_nn(hidden, w_ref[...])
    raw_ref[...] = projected[:, : 2 * head_dim]
    for part in range(2):
        at = slice(part * head_dim, (part + 1) * head_dim)
        raw = projected[:, at]
        normed = raw * rms_scale(raw) * gains_ref[part : part + 1, :]
        qkv_ref[:, at] = turn(normed, cos_ref[...], sin_ref[...]).astype(BF16)
    qkv_ref[:, 2 * head_dim :] = projected[:, 2 * head_dim :].astype(BF16)


def project(toks, gain, weights, cos, sin, gains):
    length, width = toks.shape
    head_dim = cos.shape[1]
    tile = min(256, length)

    def rows(columns):
        return pl.BlockSpec((tile, columns), lambda i: (i, 0))

    def fixed(shape):
        return pl.BlockSpec(shape, lambda i: (0, 0))

    return pl.pallas_call(
        project_kernel,
        grid=(length // tile,),
        in_specs=[
            rows(width),
            fixed((1, width)),
            fixed(weights.shape),
            rows(head_dim),
            rows(head_dim),
            fixed(gains.shape),
        ],
        out_specs=[rows(width), rows(3 * head_dim), rows(2 * head_dim)],
        out_shape=[
            jax.ShapeDtypeStruct((length, width), BF16),
            jax.ShapeDtypeStruct((length, 3 * head_dim), BF16),
            jax.ShapeDtypeStruct((length, 2 * head_dim), F32),
        ],
        compiler_params=pltpu.CompilerParams(vmem_limit_bytes=VMEM_LIMIT),
        name="project",
    )(toks, gain, weights, cos, sin, gains)


def project_back_kernel(
    factor, scale, q_ref, k_ref, v_ref, do_ref, of_ref, lse_ref, sq_ref, sk_ref,
    raw_q_ref, raw_k_ref, cos_q_ref, sin_q_ref, cos_ref, sin_ref, gains_ref,
    dp_ref, dgain_ref, kt_ref, dk_acc, dv_acc,
):
    length, head_dim = k_ref.shape
    size, count = key_chunks(length)
    tile = q_ref.shape[0]
    step_at = pl.program_id(0)

    @pl.when(step_at == 0)
    def _():
        kt_ref[...] = k_ref[...].astype(F32).T.astype(BF16)
        dk_acc[...] = jnp.zeros_like(dk_acc)
        dv_acc[...] = jnp.zeros_like(dv_acc)
        dgain_ref[...] = jnp.zeros_like(dgain_ref)

    def to_raw(part, grad, raw, cos, sin):
        grad = turn(grad.astype(BF16).astype(F32), cos, -sin)
        raw_scale = rms_scale(raw)
        dgain_ref[part : part + 1, :] += jnp.sum(grad * (raw * raw_scale), axis=0, keepdims=True)
        return norm_back(grad * gains_ref[part : part + 1, :], raw, raw_scale).astype(BF16)

    q = q_ref[...]
    grad = do_ref[...]
    seg_q = sq_ref[...]
    lse = lse_ref[0]
    row_dot = jnp.sum((grad.astype(F32) * of_ref[0]).T, axis=0, keepdims=True)
    dq_t = jnp.zeros((head_dim, tile), F32)
    for j in range(count):
        rows = slice(j * size, (j + 1) * size)
        scores = dot_nt(k_ref[rows, :], q)
        scores = jnp.where(sk_ref[rows, :] == seg_q, scores, NEG)
        weights = jnp.exp2(scores * factor - lse)
        grad_weights = dot_nt(v_ref[rows, :], grad)
        grad_scores = (weights * (grad_weights - row_dot)).astype(BF16)
        dk_acc[rows, :] += dot_nn(grad_scores, q)
        dv_acc[rows, :] += dot_nn(weights.astype(BF16), grad)
        dq_t = dq_t + dot_nn(kt_ref[:, rows], grad_scores)
    own = pl.ds(pl.multiple_of(step_at * tile, tile), tile)
    dp_ref[own, :head_dim] = to_raw(
        0, (dq_t * scale).T, raw_q_ref[...], cos_q_ref[...], sin_q_ref[...]
    )

    @pl.when(step_at == pl.num_programs(0) - 1)
    def _():
        dp_ref[:, head_dim : 2 * head_dim] = to_raw(
            1, dk_acc[...] * scale, raw_k_ref[...], cos_ref[...], sin_ref[...]
        )
        dp_ref[:, 2 * head_dim :] = dv_acc[...].astype(BF16)


def project_back(qkv, grad, out_f32, lse, segments, raw, cos, sin, gains):
    length, head_dim = grad.shape
    tile = min(256, length)

    def rows(column):
        return pl.BlockSpec((tile, head_dim), lambda i: (i, column))

    def whole(column):
        return pl.BlockSpec((length, head_dim), lambda i: (0, column))

    return pl.pallas_call(
        functools.partial(project_back_kernel, head_dim**-0.5 * LOG2E, head_dim**-0.5),
        grid=(length // tile,),
        in_specs=[
            rows(0),
            whole(1),
            whole(2),
            rows(0),
            pl.BlockSpec((1, tile, head_dim), lambda i: (0, i, 0)),
            pl.BlockSpec((1, 1, tile), lambda i: (0, 0, i)),
            pl.BlockSpec((1, tile), lambda i: (0, i)),
            pl.BlockSpec((length, 1), lambda i: (0, 0)),
            rows(0),
            whole(1),
            rows(0),
            rows(0),
            whole(0),
            whole(0),
            pl.BlockSpec(gains.shape, lambda i: (0, 0)),
        ],
        out_specs=[
            pl.BlockSpec((length, 3 * head_dim), lambda i: (0, 0)),
            pl.BlockSpec((2, head_dim), lambda i: (0, 0)),
        ],
        out_shape=[
            jax.ShapeDtypeStruct((length, 3 * head_dim), BF16),
            jax.ShapeDtypeStruct((2, head_dim), F32),
        ],
        scratch_shapes=[
            pltpu.VMEM((head_dim, length), BF16),
            pltpu.VMEM((length, head_dim), F32),
            pltpu.VMEM((length, head_dim), F32),
        ],
        compiler_params=pltpu.CompilerParams(vmem_limit_bytes=VMEM_LIMIT),
        cost_estimate=pl.CostEstimate(
            flops=10 * length * length * head_dim,
            bytes_accessed=length * head_dim * 40,
            transcendentals=length * length,
        ),
        name="project_back",
    )(
        qkv, qkv, qkv, grad, out_f32, lse, segments.reshape(1, -1), segments.reshape(-1, 1),
        raw, raw, cos, sin, cos, sin, gains,
    )


def merge_heads_kernel(parts_ref, out_ref):
    blk, uly, _, columns = parts_ref.shape
    head_dim = columns // 3
    heads = blk * uly
    for z in range(blk):
        for u in range(uly):
            head = parts_ref[z, u].astype(F32)
            for part in range(3):
                at = (part * heads + u * blk + z) * head_dim
                out_ref[:, at : at + head_dim] = head[:, part * head_dim : (part + 1) * head_dim]


def merge_heads(parts):
    blk, uly, rows, columns = parts.shape
    return pl.pallas_call(
        merge_heads_kernel,
        out_shape=jax.ShapeDtypeStruct((rows, blk * uly * columns), F32),
        compiler_params=pltpu.CompilerParams(vmem_limit_bytes=VMEM_LIMIT),
        name="merge_heads",
    )(parts)


def swap(values, axis):
    return lax.all_to_all(values, axis, split_axis=0, concat_axis=0, tiled=True)


def sum_scatter(values, axis):
    count = spread(axis) if isinstance(axis, tuple) else lax.axis_size(axis)
    rows, width = values.shape
    parts = swap(values.astype(BF16).reshape(count, rows // count, width), axis)
    return jnp.sum(parts.astype(F32), axis=0)


def place(axes, index):
    found = {}
    for axis in reversed(axes):
        size = lax.axis_size(axis)
        found[axis] = lax.rem(index, size)
        index = index // size
    return found


def spread(axes):
    return math.prod(lax.axis_size(axis) for axis in axes)


def each(count, body):
    if count <= 4:
        for step in range(1, count):
            body(step)
    else:

        def looped(step, carried):
            body(step)
            return carried

        lax.fori_loop(1, count, looped, 0)


def ahead(index, step, size):
    return lax.rem(index + step, size)


def exchange(items, collective_id, after=()):
    count = len(items)
    sizes = [spread(axes) for _, axes, _ in items]
    groups = list(dict.fromkeys(axes for _, axes, _ in items))
    bases = [sum(2 * size for size in sizes[:i]) for i in range(count)]

    def kernel(*refs):
        ins = refs[:count]
        outs = refs[count + len(after) : 2 * count + len(after)]
        send, recv, local = refs[-3:]
        barrier = pltpu.get_barrier_semaphore()
        for axes in groups:
            size, me = spread(axes), lax.axis_index(axes)

            def greet(step, axes=axes, size=size, me=me):
                pl.semaphore_signal(
                    barrier, inc=1, device_id=place(axes, ahead(me, step, size)), device_id_type=MESH
                )

            each(size, greet)
        pl.semaphore_wait(barrier, sum(spread(axes) - 1 for axes in groups))

        def remote(i, step):
            _, axes, kind = items[i]
            me = lax.axis_index(axes)
            if kind == "trade":
                return pltpu.make_async_remote_copy(
                    src_ref=ins[i],
                    dst_ref=outs[i],
                    send_sem=send.at[bases[i] + 1],
                    recv_sem=recv.at[bases[i] + 1],
                    device_id=place(axes, 1 - me),
                    device_id_type=MESH,
                )
            if kind == "relay":
                far, near = lax.rem(me + 2, 4), me + 1 - 2 * lax.rem(me, 2)
                held = far if step == 3 else me
                return pltpu.make_async_remote_copy(
                    src_ref=outs[i].at[far] if step == 3 else ins[i],
                    dst_ref=outs[i].at[held],
                    send_sem=send.at[bases[i] + step],
                    recv_sem=recv.at[bases[i] + step],
                    device_id=place(axes, far if step == 1 else near),
                    device_id_type=MESH,
                )
            peer = ahead(me, step, sizes[i])
            return pltpu.make_async_remote_copy(
                src_ref=ins[i].at[peer] if kind == "swap" else ins[i],
                dst_ref=outs[i].at[me],
                send_sem=send.at[bases[i] + step],
                recv_sem=recv.at[bases[i] + step],
                device_id=place(axes, peer),
                device_id_type=MESH,
            )

        def own(i):
            _, axes, kind = items[i]
            me = lax.axis_index(axes)
            return pltpu.make_async_copy(
                ins[i].at[me] if kind == "swap" else ins[i], outs[i].at[me], local.at[i]
            )

        def hop(i, up, hops):
            (axis,) = items[i][1]
            me, size = lax.axis_index(axis), sizes[i]
            way = 1 if up else -1
            held, to = me - way * hops, me + way
            exists = (held >= 0) & (held < size) & (to >= 0) & (to < size)
            held, to = jnp.clip(held, 0, size - 1), jnp.clip(to, 0, size - 1)
            sem = bases[i] + (size if up else 0) + hops
            copy = pltpu.make_async_remote_copy(
                src_ref=outs[i].at[held] if hops else ins[i],
                dst_ref=outs[i].at[held],
                send_sem=send.at[sem],
                recv_sem=recv.at[sem],
                device_id={axis: to},
                device_id_type=MESH,
            )
            return exists, copy

        def arrival(i, up, hops):
            (axis,) = items[i][1]
            me, size = lax.axis_index(axis), sizes[i]
            way = 1 if up else -1
            held, sender = me - way * (hops + 1), me - way
            exists = (held >= 0) & (held < size)
            held, sender = jnp.clip(held, 0, size - 1), jnp.clip(sender, 0, size - 1)
            sem = bases[i] + (size if up else 0) + hops
            copy = pltpu.make_async_remote_copy(
                src_ref=ins[i],
                dst_ref=outs[i].at[held],
                send_sem=send.at[sem],
                recv_sem=recv.at[sem],
                device_id={axis: sender},
                device_id_type=MESH,
            )
            return exists, copy

        def kinds(*names):
            return [i for i in range(count) if items[i][2] in names]

        def when(pair, act):
            exists, copy = pair
            pl.when(exists)(lambda: act(copy))

        ways = (True, False)
        for i in kinds("line"):
            for up in ways:
                when(hop(i, up, 0), lambda copy: copy.start())
        for i in kinds("gather", "swap", "relay", "trade"):
            each(3 if items[i][2] == "relay" else sizes[i], lambda step, i=i: remote(i, step).start())
        for i in kinds("gather", "swap", "relay", "line"):
            own(i).start()
        for i in kinds("line"):
            for hops in range(1, sizes[i]):
                for up in ways:
                    when(arrival(i, up, hops - 1), lambda copy: copy.wait_recv())
                    if hops < sizes[i] - 1:
                        when(hop(i, up, hops), lambda copy: copy.start())
        for i in kinds("relay"):
            remote(i, 1).wait_recv()
            remote(i, 3).start()
            remote(i, 1).wait_send()
            for step in (2, 3):
                remote(i, step).wait()
        for i in kinds("gather", "swap", "trade"):
            each(sizes[i], lambda step, i=i: remote(i, step).wait())
        for i in kinds("line"):
            for hops in range(sizes[i] - 1):
                for up in ways:
                    when(hop(i, up, hops), lambda copy: copy.wait_send())
        for i in kinds("gather", "swap", "relay", "line"):
            own(i).wait()

    shapes = [
        array.shape if kind == "trade" else (size, *(array.shape[1:] if kind == "swap" else array.shape))
        for size, (array, _, kind) in zip(sizes, items)
    ]
    anywhere = pl.BlockSpec(memory_space=pl.ANY)
    return pl.pallas_call(
        kernel,
        in_specs=[anywhere] * (count + len(after)),
        out_specs=[anywhere] * count,
        out_shape=[jax.ShapeDtypeStruct(shape, item[0].dtype) for shape, item in zip(shapes, items)],
        scratch_shapes=[
            pltpu.SemaphoreType.DMA((2 * sum(sizes),)),
            pltpu.SemaphoreType.DMA((2 * sum(sizes),)),
            pltpu.SemaphoreType.DMA((count,)),
        ],
        compiler_params=pltpu.CompilerParams(collective_id=collective_id, has_side_effects=True),
        name="exchange",
    )(*[item[0] for item in items], *after)


def startup_kernel(
    head_ref, extra_ref, tok_ref, heads_ref, extras_ref, toks_ref,
    head_send, head_recv, extra_send, extra_recv,
    z_send, z_recv, ay_send, ay_recv, by_send, by_recv, c_send, c_recv, local,
):
    blk, uly = lax.axis_size("blk"), spread(ULY)
    total = spread(ALL)
    z, u, me = lax.axis_index("blk"), lax.axis_index(ULY), lax.axis_index(ALL)
    far = lax.rem(u + 2, uly)
    near = u + 1 - 2 * lax.rem(u, 2)
    half = tok_ref.shape[0] // 2
    parts = (pl.ds(0, half), pl.ds(half, half))

    barrier = pltpu.get_barrier_semaphore()

    def greet(step):
        pl.semaphore_signal(
            barrier, inc=1, device_id=place(ALL, ahead(me, step, total)), device_id_type=MESH
        )

    each(total, greet)
    pl.semaphore_wait(barrier, total - 1)

    def send(src, dst, sent, got, to):
        return pltpu.make_async_remote_copy(
            src_ref=src, dst_ref=dst, send_sem=sent, recv_sem=got, device_id=to, device_id_type=MESH
        )

    def block(step, other, part):
        at = toks_ref.at[ahead(z, step, blk), far if other else u, parts[part]]
        return (tok_ref.at[parts[part]] if step == 0 and not other else at), at

    streams = ((0, 0), (0, 1), (1, 1))

    def hop(stream, up, hops):
        other, part = streams[stream]
        way = 1 if up else -1
        held, to = z - way * hops, z + way
        exists = (held >= 0) & (held < blk) & (to >= 0) & (to < blk)
        held, to = jnp.clip(held, 0, blk - 1), jnp.clip(to, 0, blk - 1)
        at = toks_ref.at[held, far if other else u, parts[part]]
        src = tok_ref.at[parts[part]] if hops == 0 and not other else at
        sem = (2 * stream + up) * blk + hops
        return exists, send(src, at, z_send.at[sem], z_recv.at[sem], {"blk": to})

    def arrival(stream, up, hops):
        other, part = streams[stream]
        way = 1 if up else -1
        held, sender = z - way * (hops + 1), z - way
        exists = (held >= 0) & (held < blk)
        held, sender = jnp.clip(held, 0, blk - 1), jnp.clip(sender, 0, blk - 1)
        at = toks_ref.at[held, far if other else u, parts[part]]
        sem = (2 * stream + up) * blk + hops
        return exists, send(tok_ref.at[parts[part]], at, z_send.at[sem], z_recv.at[sem], {"blk": sender})

    def when(pair, act):
        exists, copy = pair
        pl.when(exists)(lambda: act(copy))

    def a_y(step):
        return send(*block(step, 0, 0), ay_send.at[step], ay_recv.at[step], place(ULY, far))

    def b_y():
        return send(*block(0, 0, 1), by_send.at[0], by_recv.at[0], place(ULY, far))

    def to_near(step, other, part):
        sem = 4 * step + 2 * other + part
        return send(*block(step, other, part), c_send.at[sem], c_recv.at[sem], place(ULY, near))

    def head(step):
        to = place(ALL, ahead(me, step, total))
        src = head_ref.at[(to["y"] * lax.axis_size("core") + to["core"]) * blk + to["blk"]]
        return send(src, heads_ref.at[me], head_send.at[step], head_recv.at[step], to)

    def extra(step):
        to = place(ALL, ahead(me, step, total))
        return send(extra_ref, extras_ref.at[me], extra_send.at[step], extra_recv.at[step], to)

    own = [
        pltpu.make_async_copy(tok_ref, toks_ref.at[z, u], local.at[0]),
        pltpu.make_async_copy(head_ref.at[u * blk + z], heads_ref.at[me], local.at[1]),
        pltpu.make_async_copy(extra_ref, extras_ref.at[me], local.at[2]),
    ]

    ways = (1, 0)
    b_y().start()
    for stream in range(2):
        for up in ways:
            when(hop(stream, up, 0), lambda copy: copy.start())
    a_y(0).start()
    to_near(0, 0, 0).start()
    to_near(0, 0, 1).start()

    def start_head(step):
        extra(step).start()
        head(step).start()

    each(total, start_head)
    for copy in own:
        copy.start()
    b_y().wait_recv()
    for up in ways:
        when(hop(2, up, 0), lambda copy: copy.start())
    to_near(0, 1, 1).start()
    for hops in range(1, blk):
        for stream, (other, part) in enumerate(streams):
            for up in ways:
                exists, copy = arrival(stream, up, hops - 1)
                step = blk - hops if up else hops

                @pl.when(exists)
                def _(copy=copy, stream=stream, other=other, part=part, up=up, step=step, hops=hops):
                    copy.wait_recv()
                    if hops < blk - 1:
                        when(hop(stream, up, hops), lambda copy: copy.start())
                    if stream == 0:
                        a_y(step).start()
                    to_near(step, other, part).start()

    for step in [0, *reversed(range(1, blk))]:
        a_y(step).wait_recv()
        to_near(step, 1, 0).start()
    for step in range(blk):
        for other in range(2):
            for part in range(2):
                to_near(step, other, part).wait_recv()

    def wait_head(step):
        extra(step).wait()
        head(step).wait()

    each(total, wait_head)
    for copy in own:
        copy.wait()
    b_y().wait_send()
    for hops in range(blk - 1):
        for stream in range(3):
            for up in ways:
                when(hop(stream, up, hops), lambda copy: copy.wait_send())
    for step in range(blk):
        a_y(step).wait_send()
        for other in range(2):
            for part in range(2):
                to_near(step, other, part).wait_send()


def startup(heads, extra, tok, collective_id):
    blk, uly, total = lax.axis_size("blk"), spread(ULY), spread(ALL)
    anywhere = pl.BlockSpec(memory_space=pl.ANY)
    dma = pltpu.SemaphoreType.DMA
    return pl.pallas_call(
        startup_kernel,
        in_specs=[anywhere] * 3,
        out_specs=[anywhere] * 3,
        out_shape=[
            jax.ShapeDtypeStruct((total, *heads.shape[1:]), BF16),
            jax.ShapeDtypeStruct((total, *extra.shape), BF16),
            jax.ShapeDtypeStruct((blk, uly, *tok.shape), BF16),
        ],
        scratch_shapes=[
            *[dma((total,))] * 4,
            *[dma((6 * blk,))] * 2,
            *[dma((blk,))] * 2,
            *[dma((1,))] * 2,
            *[dma((4 * blk,))] * 2,
            dma((3,)),
        ],
        compiler_params=pltpu.CompilerParams(collective_id=collective_id, has_side_effects=True),
        name="startup",
    )(heads, extra, tok)


def per_device_general(
    tokens, segments, routes, w_qkv, w_out, attn_gain, ffn_gain, qk_gain, router, w_gate_up, w_down, cotangent
):
    own_tokens = tokens[0]
    own_grad = cotangent[0]
    count_tok, width = own_tokens.shape
    head_dim = qk_gain.shape[1]
    heads = width // head_dim
    uly, blk, batch = spread(ULY), lax.axis_size("blk"), lax.axis_size("batch")
    blk_at, uly_at = lax.axis_index("blk"), lax.axis_index(ULY)
    group = batch * blk
    local_heads = heads // uly
    local_width = local_heads * head_dim
    rows = count_tok * uly
    seg_row = segments[0]
    length = seg_row.shape[0]
    number = router.shape[1]
    local_experts, _, units = w_down.shape
    shard_rows = w_qkv.shape[0]

    extra = jnp.concatenate([attn_gain[:, None], ffn_gain[:, None], router], axis=1)
    extra = jnp.pad(extra, ((0, 0), (0, LANES - extra.shape[1])))
    columns = w_qkv.reshape(shard_rows, 3, uly, local_width).transpose(2, 0, 1, 3)
    packed = jnp.concatenate(
        [
            columns.reshape(uly, shard_rows, 3 * local_width),
            jnp.broadcast_to(extra[None], (uly, shard_rows, LANES)),
        ],
        axis=2,
    )
    packed = swap(packed, ULY).reshape(uly * shard_rows, 3 * local_width + LANES)
    packed = lax.all_gather(packed, ROWS, axis=0, tiled=True)
    own_qkv = packed[:, : 3 * local_width]
    gain_attn = packed[:, 3 * local_width].astype(F32)
    gain_ffn = packed[:, 3 * local_width + 1].astype(F32)
    whole_router = packed[:, 3 * local_width + 2 : 3 * local_width + 2 + number]
    tokens_all = lax.all_gather(own_tokens, ULY, axis=0, tiled=True)
    to_rows = [(u * group + g, g * uly + u) for g in range(group) for u in range(uly)]
    own_out = lax.all_gather(lax.ppermute(w_out, ALL, to_rows), ROWS, axis=0, tiled=True)
    whole_gate_up = lax.all_gather(w_gate_up, PLANE, axis=0, tiled=False)
    whole_down = lax.all_gather(w_down, PLANE, axis=0, tiled=False)
    grad_blk = lax.all_gather(own_grad, "blk", axis=0, tiled=True)
    routes_blk = lax.all_gather(routes[0], "blk", axis=0, tiled=True)

    gain_query = qk_gain[0].astype(F32)
    gain_key = qk_gain[1].astype(F32)
    inputs_all = tokens_all.astype(F32)
    normed_one = inputs_all * rms_scale(inputs_all)
    hidden_one = (normed_one * gain_attn).astype(BF16)
    projected = dot_nn(hidden_one, own_qkv)
    query_raw = projected[:, :local_width].reshape(rows, local_heads, head_dim)
    key_raw = projected[:, local_width : 2 * local_width].reshape(rows, local_heads, head_dim)
    value_raw = projected[:, 2 * local_width :].reshape(rows, local_heads, head_dim)
    cos_table, sin_table = rope_tables(blk_at * rows, rows, head_dim)
    query_scale = rms_scale(query_raw)
    key_scale = rms_scale(key_raw)
    qkv = jnp.concatenate(
        [
            rotate(query_raw * query_scale * gain_query, cos_table, sin_table),
            rotate(key_raw * key_scale * gain_key, cos_table, sin_table),
            value_raw,
        ],
        axis=2,
    ).astype(BF16)
    qkv = qkv.transpose(1, 0, 2)

    by_heads = local_heads % blk == 0
    if by_heads:
        per = local_heads // blk

        def to_heads(values):
            columns = values.shape[2]
            moved = swap(values.reshape(blk, per, rows, columns), "blk")
            return moved.transpose(1, 0, 2, 3).reshape(per, length, columns)

        def to_rows_back(values):
            columns = values.shape[2]
            parts = values.reshape(per, blk, rows, columns).transpose(1, 0, 2, 3)
            return swap(parts, "blk").reshape(local_heads, rows, columns)

        q_src = kv_src = to_heads(qkv)
        cols = (0, 1, 2)
        seg_q = seg_row
        first_head = uly_at * local_heads + blk_at * per
    else:

        def to_heads(values):
            return values

        def to_rows_back(values):
            return values

        q_src = qkv
        kv_src = lax.all_gather(qkv[:, :, head_dim:], "blk", axis=1, tiled=True)
        cols = (0, 0, 1)
        seg_q = lax.dynamic_slice_in_dim(seg_row, blk_at * rows, rows)
        first_head = uly_at * local_heads
    attn_low, attn_f32, lse, top = attention_forward(q_src, kv_src, cols, seg_q, seg_row, head_dim)
    head_vector = lax.dynamic_update_slice_in_dim(
        jnp.full((heads,), NEG, F32), jnp.max(top, axis=(1, 2)) * head_dim**-0.5, first_head, 0
    )
    head_max = lax.pmax(head_vector, ALL)
    attn_rows = to_rows_back(attn_low)
    out_heads = own_out.reshape(local_heads, head_dim, width)
    branch = jnp.einsum("htc,hcd->td", attn_rows, out_heads, preferred_element_type=F32)
    inputs = own_tokens.astype(F32)
    mid = inputs + sum_scatter(branch, ULY)

    scale_two = rms_scale(mid)
    normed_two = mid * scale_two
    hidden_two = (normed_two * gain_ffn).astype(BF16)
    hidden_blk = lax.all_gather(hidden_two, "blk", axis=0, tiled=True)
    probs_blk = jax.nn.softmax(dot_nn(hidden_blk, whole_router), axis=1)
    names = jnp.arange(number, dtype=jnp.int32)
    chosen_blk = jnp.any(routes_blk[:, :, None] == names, axis=1).astype(F32)
    own_names = blk_at * local_experts
    gates = lax.dynamic_slice_in_dim(probs_blk * chosen_blk, own_names, local_experts, axis=1)
    most = min(MOST_TOKENS, hidden_blk.shape[0])
    packed_weights = jnp.concatenate([whole_gate_up, whole_down], axis=3)
    made = []
    for at in range(0, hidden_blk.shape[0], most):
        hidden_part, grad_part = hidden_blk[at : at + most], grad_blk[at : at + most]
        made.append(
            experts(
                hidden_part,
                hidden_part.T,
                grad_part,
                grad_part.T,
                gates[at : at + most],
                packed_weights,
            )
        )
    out_part = jnp.concatenate([m[0] for m in made], axis=0)
    dx_part = jnp.concatenate([m[1] for m in made], axis=0)
    dg_part = jnp.concatenate([m[2] for m in made], axis=1)
    expert_grads = sum(m[3].astype(F32) for m in made).astype(BF16)
    expert_sums = lax.psum_scatter(expert_grads, PLANE, scatter_dimension=0, tiled=False).astype(F32)
    grad_gate_up = jnp.concatenate([expert_sums[0], expert_sums[1]], axis=2)
    grad_down = expert_sums[2]
    dg_parts = swap(dg_part.reshape(local_experts, blk, count_tok).transpose(1, 2, 0), "blk")
    grad_gates = dg_parts.transpose(1, 0, 2).reshape(count_tok, number)
    dx_sum = sum_scatter(dx_part, "blk")
    output = (mid + sum_scatter(out_part, "blk")).astype(BF16)
    router_probs = lax.dynamic_slice_in_dim(probs_blk, blk_at * count_tok, count_tok)
    chosen = lax.dynamic_slice_in_dim(chosen_blk, blk_at * count_tok, count_tok)
    grad_probs = chosen * grad_gates
    grad_logits = (
        router_probs * (grad_probs - jnp.sum(router_probs * grad_probs, axis=1, keepdims=True))
    ).astype(BF16)
    grad_hidden_two = dx_sum + dot_nt(grad_logits, whole_router)
    grad_router_part = dot_tn(hidden_two, grad_logits)
    grad_gain_ffn = jnp.sum(grad_hidden_two * normed_two, axis=0)
    grad_mid = own_grad.astype(F32) + norm_back(grad_hidden_two * gain_ffn, mid, scale_two)

    branch_grad = lax.all_gather(grad_mid.astype(BF16), ULY, axis=0, tiled=True)
    grad_attn = dot_nt(branch_grad, own_out).astype(BF16)
    grad_attn = to_heads(grad_attn.reshape(rows, local_heads, head_dim).transpose(1, 0, 2))
    grad_out_part = jnp.einsum("htc,td->hcd", attn_rows, branch_grad, preferred_element_type=F32)
    dq, dk, dv = attention_backward(
        q_src, kv_src, cols, grad_attn, attn_f32, lse, seg_q, seg_row, head_dim
    )
    if by_heads:
        dqkv = to_rows_back(jnp.concatenate([dq, dk, dv], axis=2))
        dq, dk, dv = jnp.split(dqkv, 3, axis=2)
    else:
        dk, dv = (lax.psum_scatter(g, "blk", scatter_dimension=1, tiled=True) for g in (dk, dv))
    dq, dk, dv = (g.transpose(1, 0, 2) for g in (dq, dk, dv))
    grad_query_norm = rotate(dq.astype(F32), cos_table, -sin_table)
    grad_key_norm = rotate(dk.astype(F32), cos_table, -sin_table)
    grad_gain_query = jnp.sum(grad_query_norm * (query_raw * query_scale), axis=(0, 1))
    grad_gain_key = jnp.sum(grad_key_norm * (key_raw * key_scale), axis=(0, 1))
    grad_projected = jnp.concatenate(
        [
            norm_back(grad_query_norm * gain_query, query_raw, query_scale)
            .reshape(rows, local_width)
            .astype(BF16),
            norm_back(grad_key_norm * gain_key, key_raw, key_scale)
            .reshape(rows, local_width)
            .astype(BF16),
            dv.reshape(rows, local_width),
        ],
        axis=1,
    )
    grad_hidden_part = dot_nt(grad_projected, own_qkv)
    grad_hidden_one = sum_scatter(grad_hidden_part, ULY)
    grad_gain_attn = jnp.sum(grad_hidden_part * normed_one, axis=0)
    grad_inputs = grad_mid + norm_back(grad_hidden_one * gain_attn, inputs, rms_scale(inputs))

    grad_qkv_part = dot_tn(hidden_one, grad_projected).astype(BF16)
    grad_qkv_rows = lax.psum_scatter(grad_qkv_part, ROWS, scatter_dimension=0, tiled=True)
    grad_qkv_rows = swap(grad_qkv_rows.reshape(uly, shard_rows, 3 * local_width), ULY)
    grad_qkv = (
        grad_qkv_rows.reshape(uly, shard_rows, 3, local_width)
        .transpose(1, 2, 0, 3)
        .reshape(shard_rows, 3 * width)
        .astype(F32)
    )
    grad_out_rows = lax.psum_scatter(
        grad_out_part.reshape(local_width, width).astype(BF16), ROWS, scatter_dimension=0, tiled=True
    )
    grad_out = lax.ppermute(grad_out_rows, ALL, [(b, a) for a, b in to_rows]).astype(F32)
    small = jnp.concatenate([grad_gain_attn[:, None], grad_gain_ffn[:, None], grad_router_part], axis=1)
    small = lax.psum_scatter(small, ALL, scatter_dimension=0, tiled=True)
    grad_qk_gain = lax.psum(jnp.stack([grad_gain_query, grad_gain_key]), ALL)

    clip_gamma = TAU / jnp.maximum(head_max, TAU)
    factor = jnp.repeat(jnp.sqrt(clip_gamma), head_dim)
    column_scale = jnp.concatenate([factor, factor, jnp.ones((width,), F32)])
    clipped = w_qkv.astype(F32) * column_scale[None, :]
    return (
        output[None],
        grad_inputs[None],
        grad_qkv,
        grad_out,
        small[:, 0],
        small[:, 1],
        grad_qk_gain,
        small[:, 2:],
        grad_gate_up,
        grad_down,
        clipped,
    )


def per_device(
    tokens, segments, routes, w_qkv, w_out, attn_gain, ffn_gain, qk_gain, router, w_gate_up, w_down, cotangent
):
    own_tokens = tokens[0]
    own_grad = cotangent[0]
    count_tok, width = own_tokens.shape
    head_dim = qk_gain.shape[1]
    heads = width // head_dim
    batch, blk, uly = lax.axis_size("batch"), lax.axis_size("blk"), spread(ULY)
    total, group = batch * blk * uly, batch * blk
    local_experts = w_down.shape[0]
    if uly != 4 or heads != blk * uly or batch != 2 or local_experts != 4:
        return per_device_general(
            tokens, segments, routes, w_qkv, w_out, attn_gain, ffn_gain, qk_gain, router, w_gate_up, w_down, cotangent
        )
    blk_at, uly_at = lax.axis_index("blk"), lax.axis_index(ULY)
    rows = count_tok * uly
    seg_row = segments[0]
    length = seg_row.shape[0]
    number = router.shape[1]
    shard_rows = w_qkv.shape[0]

    to_rows = [(u * group + g, g * uly + u) for g in range(group) for u in range(uly)]
    own_rows = lax.ppermute(w_out, ALL, to_rows)
    half = local_experts // 2
    weights_first, weights_second = (
        lax.all_gather(jnp.concatenate([w_gate_up[at], w_down[at]], axis=2), PLANE, axis=0, tiled=False)
        for at in (slice(0, half), slice(half, local_experts))
    )
    extra = jnp.concatenate([attn_gain[None], ffn_gain[None], router.T], axis=0)
    kept = extra.shape[0]
    extra = jnp.pad(extra, ((0, -kept % 16), (0, -shard_rows % LANES)))
    by_head = w_qkv.reshape(shard_rows, 3, heads, head_dim).transpose(2, 0, 1, 3)
    own_qkv, extras, toks = startup(
        by_head.reshape(heads, shard_rows, 3 * head_dim), extra, own_tokens, 0
    )
    own_rows, extras = lax.optimization_barrier((own_rows, extras))
    own_out = lax.all_to_all(
        jnp.broadcast_to(own_rows[None], (group, *own_rows.shape)), ROWS, split_axis=0, concat_axis=0, tiled=True
    ).reshape(blk, head_dim, width)
    own_qkv = own_qkv.reshape(width, 3 * head_dim)
    extras = extras[:, :kept, :shard_rows].transpose(1, 0, 2).reshape(kept, width)
    gain_attn = extras[0].astype(F32)
    gain_ffn = extras[1].astype(F32)
    router_t = extras[2:]

    gains = qk_gain.astype(F32)
    cos, sin = rope_rows(length, head_dim)
    hidden_one, qkv, raw = project(
        toks.reshape(length, width), gain_attn[None], own_qkv, cos, sin, gains
    )
    attn_low, attn_f32, lse, top = attention_forward(
        qkv[None], qkv[None], (0, 1, 2), seg_row, seg_row, head_dim
    )
    (attn_rows,) = exchange([(attn_low.reshape(blk, rows, head_dim), ("blk",), "swap")], 1)
    branch = jnp.einsum("htc,hcd->td", attn_rows, own_out, preferred_element_type=F32)
    branch, grad_blk, routes_blk = exchange(
        [
            (branch.astype(BF16).reshape(uly, count_tok, width), ULY, "swap"),
            (own_grad, ("blk",), "line"),
            (routes[0].T, ("blk",), "gather"),
        ],
        2,
    )
    inputs = own_tokens.astype(F32)
    mid = inputs + jnp.sum(branch.astype(F32), axis=0)

    scale_two = rms_scale(mid)
    normed_two = mid * scale_two
    hidden_two = (normed_two * gain_ffn).astype(BF16)
    (hidden_blk,) = exchange([(hidden_two, ("blk",), "line")], 3, after=[weights_first])
    tokens_blk = blk * count_tok
    hidden_blk = hidden_blk.reshape(tokens_blk, width)
    grad_blk = grad_blk.reshape(tokens_blk, width)
    probs_blk = jax.nn.softmax(dot_nt(hidden_blk, router_t), axis=1)
    names = jnp.arange(number, dtype=jnp.int32)
    chosen_blk = jnp.any(routes_blk[:, :, :, None] == names, axis=1).astype(F32)
    chosen_blk = chosen_blk.reshape(tokens_blk, number)
    gates = lax.dynamic_slice_in_dim(
        probs_blk * chosen_blk, blk_at * local_experts, local_experts, axis=1
    )
    shared = (hidden_blk, hidden_blk.T, grad_blk, grad_blk.T)
    out_first, dx_first, dg_first, keep_xa, give_xa, keep_ya, give_ya = experts(
        *shared, gates[:, :half], weights_first, collective_id=9
    )
    out_part, dx_part, dg_second, keep_xb, give_xb, keep_yb, give_yb, got_xa, got_ya = experts(
        *shared,
        gates[:, half:],
        weights_second,
        collective_id=10,
        before=(out_first, dx_first, give_xa, give_ya),
    )
    dg_part = jnp.concatenate([dg_first, dg_second], axis=0).reshape(local_experts, blk, count_tok)
    dx_parts, dg_parts, got_xb, got_yb = exchange(
        [
            (dx_part.reshape(blk, count_tok, width), ("blk",), "swap"),
            (dg_part.transpose(1, 0, 2), ("blk",), "swap"),
            (give_xb, ("batch",), "trade"),
            (give_yb, ("y",), "trade"),
        ],
        4,
    )
    out_part = out_part.reshape(blk, count_tok, width)
    out_part, dx_parts = lax.optimization_barrier((out_part, dx_parts))
    out_parts = lax.all_to_all(out_part, "blk", split_axis=0, concat_axis=0, tiled=True)
    output = (mid + jnp.sum(out_parts.astype(F32), axis=0)).astype(BF16)
    router_probs = lax.dynamic_slice_in_dim(probs_blk, blk_at * count_tok, count_tok)
    chosen = lax.dynamic_slice_in_dim(chosen_blk, blk_at * count_tok, count_tok)
    grad_probs = chosen * dg_parts.reshape(number, count_tok).T
    grad_logits = (
        router_probs * (grad_probs - jnp.sum(router_probs * grad_probs, axis=1, keepdims=True))
    ).astype(BF16)
    grad_hidden_two = jnp.sum(dx_parts.astype(F32), axis=0) + dot_nn(grad_logits, router_t)
    grad_router_t = dot_tn(grad_logits, hidden_two)
    grad_gain_ffn = jnp.sum(grad_hidden_two * normed_two, axis=0)
    grad_mid = own_grad.astype(F32) + norm_back(grad_hidden_two * gain_ffn, mid, scale_two)

    (branch_grad,) = exchange([(grad_mid.astype(BF16), ULY, "relay")], 5)
    branch_grad, sent_qkv = lax.optimization_barrier((branch_grad, own_qkv))
    far_qkv = lax.ppermute(sent_qkv, "y", [(0, 1), (1, 0)])
    branch_grad = branch_grad.reshape(rows, width)
    grad_attn = jnp.einsum("td,hcd->htc", branch_grad, own_out, preferred_element_type=F32).astype(BF16)
    (grad_attn,) = exchange([(grad_attn, ("blk",), "swap")], 6, after=[out_parts])
    grad_out_part = jnp.einsum("htc,td->hcd", attn_rows, branch_grad, preferred_element_type=F32)
    grad_out_parts = lax.all_to_all(
        grad_out_part.astype(BF16).reshape(group, shard_rows, width),
        ROWS,
        split_axis=0,
        concat_axis=0,
        tiled=True,
    )
    grad_out = lax.ppermute(
        jnp.sum(grad_out_parts.astype(F32), axis=0).astype(BF16), ALL, [(b, a) for a, b in to_rows]
    ).astype(F32)
    grad_projected, grad_gains = project_back(
        qkv, grad_attn.reshape(length, head_dim), attn_f32, lse, seg_row, raw, cos, sin, gains
    )
    by_uly = grad_projected.reshape(blk, uly, count_tok, 3 * head_dim).transpose(1, 0, 2, 3)
    grad_qkv_part = dot_tn(hidden_one, grad_projected).astype(BF16)
    by_batch = grad_qkv_part.reshape(batch, width // batch, 3 * head_dim)
    batch_at = lax.axis_index("batch")
    projected_blk, got_qkv_part, near_qkv, cross_qkv = exchange(
        [
            (by_uly.reshape(uly, tokens_blk, 3 * head_dim), ULY, "swap"),
            (
                lax.dynamic_index_in_dim(by_batch, 1 - batch_at, 0, keepdims=False),
                ("batch",),
                "trade",
            ),
            (own_qkv, ("core",), "trade"),
            (far_qkv, ("core",), "trade"),
        ],
        7,
        after=[grad_out_parts],
    )
    grad_qkv_part = lax.dynamic_index_in_dim(by_batch, batch_at, 0, keepdims=False) + got_qkv_part

    near_at, far_at = uly_at + 1 - 2 * lax.rem(uly_at, 2), lax.rem(uly_at + 2, uly)
    cross_at = lax.rem(near_at + 2, uly)
    grad_hidden_part = sum(
        dot_nt(lax.dynamic_index_in_dim(projected_blk, sender, 0, keepdims=False), weights)
        for sender, weights in [
            (uly_at, own_qkv),
            (near_at, near_qkv),
            (far_at, far_qkv),
            (cross_at, cross_qkv),
        ]
    )
    hidden_own = hidden_one.reshape(blk, uly, count_tok, width)
    hidden_own = lax.dynamic_index_in_dim(hidden_own, uly_at, 1, keepdims=False)
    hidden_own = hidden_own.reshape(tokens_blk, width).astype(F32)
    grad_gain_attn = jnp.sum(grad_hidden_part * hidden_own, axis=0) / gain_attn

    small = jnp.concatenate([grad_gain_attn[None], grad_gain_ffn[None], grad_router_t], axis=0)
    small = small.reshape(kept, total, shard_rows).transpose(1, 0, 2)
    small = jnp.pad(small, ((0, 0), (0, 0), (0, LANES - shard_rows)))
    head_row = jnp.where(
        jnp.arange(LANES) == uly_at * blk + blk_at, jnp.max(top) * head_dim**-0.5, NEG
    )
    to_all = jnp.concatenate([grad_gains, head_row[None]], axis=0)
    small = jnp.concatenate([small, jnp.broadcast_to(to_all[None], (total, 3, LANES))], axis=1)
    small = jnp.pad(small, ((0, 0), (0, -small.shape[1] % 8), (0, 0)))
    pairs = [(keep_xa, got_xa), (keep_ya, got_ya), (keep_xb, got_xb), (keep_yb, got_yb)]
    grad_hidden_parts, small, grad_qkv_parts, *last = exchange(
        [
            (grad_hidden_part.astype(BF16).reshape(blk, count_tok, width), ("blk",), "swap"),
            (small, ALL, "swap"),
            (grad_qkv_part.reshape(total // batch, shard_rows, 3 * head_dim), ("blk", *ULY), "swap"),
            *[
                (kept[1] + got[1], axes, "trade")
                for (kept, got), axes in zip(pairs, [("y",), ("batch",)] * 2)
            ],
        ],
        8,
    )
    reduced = [(*pair, others) for pair, others in zip(pairs, last)]
    finished = finish_experts(*reduced[:half], 0, local_experts)
    grad_gate_up, grad_down = finish_experts(*reduced[half:], half, local_experts, before=finished)
    grad_qkv = merge_heads(grad_qkv_parts.reshape(blk, uly, shard_rows, 3 * head_dim))
    grad_hidden_one = jnp.sum(grad_hidden_parts.astype(F32), axis=0)
    grad_inputs = grad_mid + norm_back(grad_hidden_one * gain_attn, inputs, rms_scale(inputs))
    sums = jnp.sum(small, axis=0)
    head_max = jnp.max(small[:, kept + 2, :heads], axis=0)
    factor = jnp.repeat(jnp.sqrt(TAU / jnp.maximum(head_max, TAU)), head_dim)
    column_scale = jnp.concatenate([factor, factor, jnp.ones((width,), F32)])
    clipped = w_qkv.astype(F32) * column_scale[None, :]
    return (
        output[None],
        grad_inputs[None],
        grad_qkv,
        grad_out,
        sums[0, :shard_rows],
        sums[1, :shard_rows],
        sums[kept : kept + 2],
        sums[2:kept, :shard_rows].T,
        grad_gate_up,
        grad_down,
        clipped,
    )


def solution(mesh):
    in_specs = (
        P("batch", ("blk", *ULY), None),
        P("batch", None),
        P("batch", ("blk", *ULY), None),
        P(ALL, None),
        P(ALL, None),
        P(ALL),
        P(ALL),
        P(),
        P(ALL, None),
        P("blk", PLANE, None),
        P("blk", PLANE, None),
        P("batch", ("blk", *ULY), None),
    )
    out_specs = (
        P("batch", ("blk", *ULY), None),
        P("batch", ("blk", *ULY), None),
        P(ALL, None),
        P(ALL, None),
        P(ALL),
        P(ALL),
        P(),
        P(ALL, None),
        P("blk", PLANE, None),
        P("blk", PLANE, None),
        P(ALL, None),
    )
    cores = 2 - mesh.shape["uly"] % 2
    mesh = Mesh(
        mesh.devices.reshape(*(mesh.shape[axis] for axis in ROWS), mesh.shape["uly"] // cores, cores), ALL
    )
    return jax.shard_map(
        per_device, mesh=mesh, in_specs=in_specs, out_specs=out_specs, check_vma=False
    )
```

```python
import functools
import math

import jax
import jax.numpy as jnp
from jax import lax
from jax.experimental import pallas as pl
from jax.experimental.pallas import tpu as pltpu
from jax.sharding import Mesh
from jax.sharding import PartitionSpec as P

EPS = 1e-06
THETA = 50000.0
TAU = 4.0
NEG = -1e30
LOG2E = 1.4426950408889634
LANES = 128
MOST_TOKENS = 512
VMEM_LIMIT = 60 * 1024 * 1024

ULY = ("y", "core")
ALL = ("batch", "blk", *ULY)
ROWS = ("batch", "blk")
PLANE = ("batch", *ULY)
CHIPS = ("batch", "y")

MESH = pl.DeviceIdType.MESH
BF16 = jnp.bfloat16
F32 = jnp.float32


def rms_scale(values):
    return lax.rsqrt(jnp.mean(values * values, axis=-1, keepdims=True) + EPS)


def norm_back(grad_normed, values, scale):
    normed = values * scale
    return scale * (grad_normed - normed * jnp.mean(grad_normed * normed, axis=-1, keepdims=True))


def rope_tables(offset, length, head_dim):
    half_dim = head_dim // 2
    frequency = THETA ** (-jnp.arange(half_dim, dtype=F32) * 2.0 / head_dim)
    positions = (offset + jnp.arange(length, dtype=jnp.int32)).astype(F32)
    angles = positions[:, None] * frequency[None, :]
    return (jnp.cos(angles)[:, None, :], jnp.sin(angles)[:, None, :])


def rope_rows(length, head_dim):
    fine = math.gcd(length, LANES)
    frequency = THETA ** (-jnp.arange(head_dim // 2, dtype=F32) * 2.0 / head_dim)
    frequency = jnp.concatenate([frequency, frequency])
    coarse_angle = (jnp.arange(length // fine, dtype=F32) * fine)[:, None, None] * frequency
    fine_angle = jnp.arange(fine, dtype=F32)[None, :, None] * frequency
    cos_a, sin_a, cos_b, sin_b = lax.optimization_barrier(
        (jnp.cos(coarse_angle), jnp.sin(coarse_angle), jnp.cos(fine_angle), jnp.sin(fine_angle))
    )
    sign = jnp.where(jnp.arange(head_dim) < head_dim // 2, -1.0, 1.0)
    cos = cos_a * cos_b - sin_a * sin_b
    sin = (sin_a * cos_b + cos_a * sin_b) * sign
    return cos.reshape(length, head_dim), sin.reshape(length, head_dim)


def rotate(values, cos_table, sin_table):
    half_dim = values.shape[-1] // 2
    first = values[..., :half_dim]
    second = values[..., half_dim:]
    return jnp.concatenate(
        [first * cos_table - second * sin_table, second * cos_table + first * sin_table], axis=-1
    )


def dot_nn(a, b):
    return lax.dot_general(a, b, (((1,), (0,)), ((), ())), preferred_element_type=F32)


def dot_nt(a, b):
    return lax.dot_general(a, b, (((1,), (1,)), ((), ())), preferred_element_type=F32)


def dot_tn(a, b):
    return lax.dot_general(a, b, (((0,), (0,)), ((), ())), preferred_element_type=F32)


def key_chunks(length):
    size = min(512, length)
    return size, length // size


def attn_fwd_kernel(factor, q_ref, k_ref, v_ref, sq_ref, sk_ref, o_ref, of_ref, lse_ref, top_ref, vt_ref):
    length = k_ref.shape[1]
    size, count = key_chunks(length)
    tile, head_dim = q_ref.shape[1:]

    @pl.when(pl.program_id(1) == 0)
    def _():
        vt_ref[...] = v_ref[0].astype(F32).T.astype(BF16)

    q = q_ref[0]
    seg_q = sq_ref[...]

    def step(j, carried):
        total, top, acc = carried
        at = pl.multiple_of(j * size, size)
        scores = dot_nt(k_ref[0, pl.ds(at, size), :], q)
        scores = jnp.where(sk_ref[pl.ds(at, size), :] == seg_q, scores, NEG)
        top = jnp.maximum(top, jnp.max(scores, axis=0, keepdims=True))
        weights = jnp.exp2(scores * factor)
        total = total + jnp.sum(weights, axis=0, keepdims=True)
        acc = acc + dot_nn(vt_ref[:, pl.ds(at, size)], weights.astype(BF16))
        return total, top, acc

    start = (
        jnp.zeros((1, tile), F32),
        jnp.full((1, tile), NEG, F32),
        jnp.zeros((head_dim, tile), F32),
    )
    total, top, acc = lax.fori_loop(0, count, step, start, unroll=count <= 4)
    out = (acc * (1.0 / total)).T
    o_ref[0] = out.astype(BF16)
    of_ref[0] = out
    lse_ref[0] = jnp.log2(total)
    top_ref[0] = top


def attn_bwd_kernel(
    factor, scale, q_ref, k_ref, v_ref, do_ref, of_ref, lse_ref, sq_ref, sk_ref,
    dq_ref, dk_ref, dv_ref, kt_ref, dk_acc, dv_acc,
):
    length = k_ref.shape[1]
    size, count = key_chunks(length)
    tile, head_dim = q_ref.shape[1:]

    @pl.when(pl.program_id(1) == 0)
    def _():
        kt_ref[...] = k_ref[0].astype(F32).T.astype(BF16)
        dk_acc[...] = jnp.zeros_like(dk_acc)
        dv_acc[...] = jnp.zeros_like(dv_acc)

    q = q_ref[0]
    grad = do_ref[0]
    seg_q = sq_ref[...]
    lse = lse_ref[0]
    row_dot = jnp.sum((grad.astype(F32) * of_ref[0]).T, axis=0, keepdims=True)

    def step(j, dq_t):
        at = pl.multiple_of(j * size, size)
        rows = pl.ds(at, size)
        scores = dot_nt(k_ref[0, rows, :], q)
        scores = jnp.where(sk_ref[rows, :] == seg_q, scores, NEG)
        weights = jnp.exp2(scores * factor - lse)
        grad_weights = dot_nt(v_ref[0, rows, :], grad)
        grad_scores = (weights * (grad_weights - row_dot)).astype(BF16)
        dk_acc[rows, :] += dot_nn(grad_scores, q)
        dv_acc[rows, :] += dot_nn(weights.astype(BF16), grad)
        return dq_t + dot_nn(kt_ref[:, rows], grad_scores)

    dq_t = lax.fori_loop(0, count, step, jnp.zeros((head_dim, tile), F32), unroll=count <= 4)
    dq_ref[0] = (dq_t * scale).T.astype(BF16)

    @pl.when(pl.program_id(1) == pl.num_programs(1) - 1)
    def _():
        dk_ref[0] = (dk_acc[...] * scale).astype(BF16)
        dv_ref[0] = dv_acc[...].astype(BF16)


def attention_tile(queries, length):
    return min(queries, 256 if length <= 4096 else 128)


def attention_forward(q_src, kv_src, cols, seg_q, seg_k, head_dim):
    heads, queries = q_src.shape[:2]
    length = kv_src.shape[1]
    tile = attention_tile(queries, length)
    q_col, k_col, v_col = cols
    factor = head_dim**-0.5 * LOG2E
    row = pl.BlockSpec((1, 1, tile), lambda h, i: (h, 0, i))
    block = pl.BlockSpec((1, tile, head_dim), lambda h, i: (h, i, 0))
    return pl.pallas_call(
        functools.partial(attn_fwd_kernel, factor),
        grid=(heads, queries // tile),
        in_specs=[
            pl.BlockSpec((1, tile, head_dim), lambda h, i: (h, i, q_col)),
            pl.BlockSpec((1, length, head_dim), lambda h, i: (h, 0, k_col)),
            pl.BlockSpec((1, length, head_dim), lambda h, i: (h, 0, v_col)),
            pl.BlockSpec((1, tile), lambda h, i: (0, i)),
            pl.BlockSpec((length, 1), lambda h, i: (0, 0)),
        ],
        out_specs=[block, block, row, row],
        out_shape=[
            jax.ShapeDtypeStruct((heads, queries, head_dim), BF16),
            jax.ShapeDtypeStruct((heads, queries, head_dim), F32),
            jax.ShapeDtypeStruct((heads, 1, queries), F32),
            jax.ShapeDtypeStruct((heads, 1, queries), F32),
        ],
        scratch_shapes=[pltpu.VMEM((head_dim, length), BF16)],
        compiler_params=pltpu.CompilerParams(vmem_limit_bytes=VMEM_LIMIT),
        cost_estimate=pl.CostEstimate(
            flops=4 * heads * queries * length * head_dim,
            bytes_accessed=heads * (queries + length) * head_dim * 8,
            transcendentals=heads * queries * length,
        ),
        name="attend",
    )(q_src, kv_src, kv_src, seg_q.reshape(1, -1), seg_k.reshape(-1, 1))


def attention_backward(q_src, kv_src, cols, grad, out_f32, lse, seg_q, seg_k, head_dim):
    heads, queries = q_src.shape[:2]
    length = kv_src.shape[1]
    tile = attention_tile(queries, length)
    q_col, k_col, v_col = cols
    scale = head_dim**-0.5
    row = pl.BlockSpec((1, 1, tile), lambda h, i: (h, 0, i))
    block = pl.BlockSpec((1, tile, head_dim), lambda h, i: (h, i, 0))
    whole = pl.BlockSpec((1, length, head_dim), lambda h, i: (h, 0, 0))
    return pl.pallas_call(
        functools.partial(attn_bwd_kernel, scale * LOG2E, scale),
        grid=(heads, queries // tile),
        in_specs=[
            pl.BlockSpec((1, tile, head_dim), lambda h, i: (h, i, q_col)),
            pl.BlockSpec((1, length, head_dim), lambda h, i: (h, 0, k_col)),
            pl.BlockSpec((1, length, head_dim), lambda h, i: (h, 0, v_col)),
            block,
            block,
            row,
            pl.BlockSpec((1, tile), lambda h, i: (0, i)),
            pl.BlockSpec((length, 1), lambda h, i: (0, 0)),
        ],
        out_specs=[block, whole, whole],
        out_shape=[
            jax.ShapeDtypeStruct((heads, queries, head_dim), BF16),
            jax.ShapeDtypeStruct((heads, length, head_dim), BF16),
            jax.ShapeDtypeStruct((heads, length, head_dim), BF16),
        ],
        scratch_shapes=[
            pltpu.VMEM((head_dim, length), BF16),
            pltpu.VMEM((length, head_dim), F32),
            pltpu.VMEM((length, head_dim), F32),
        ],
        compiler_params=pltpu.CompilerParams(vmem_limit_bytes=VMEM_LIMIT),
        cost_estimate=pl.CostEstimate(
            flops=10 * heads * queries * length * head_dim,
            bytes_accessed=heads * (queries + length) * head_dim * 12,
            transcendentals=heads * queries * length,
        ),
        name="attend_back",
    )(q_src, kv_src, kv_src, grad, out_f32, lse, seg_q.reshape(1, -1), seg_k.reshape(-1, 1))


def expert_step(expert, h_ref, ht_ref, dy_ref, dyt_ref, gate_ref, wg_ref, wu_ref, wd_ref, dg_ref, out_acc, dx_acc):
    width = h_ref.shape[1]
    cols = wg_ref.shape[3]
    w_gate = wg_ref[...].reshape(width, cols)
    w_up = wu_ref[...].reshape(width, cols)
    w_down = wd_ref[...].reshape(width, cols)
    gates = gate_ref[...]
    mine = lax.broadcasted_iota(jnp.int32, gates.shape, 1) == expert
    gate = jnp.sum(jnp.where(mine, gates, 0.0), axis=1, keepdims=True)
    a_gate = dot_nn(h_ref[...], w_gate)
    a_up = dot_nn(h_ref[...], w_up)
    raw = dot_nn(dy_ref[...], w_down)
    sigma = 1.0 / (1.0 + jnp.exp2(a_gate * -LOG2E))
    swish = a_gate * sigma
    act = swish * a_up
    dg_ref[0] += jnp.sum(raw * act, axis=1, keepdims=True)
    gated = (gate * act).astype(BF16)
    d_act = gate * raw
    d_gate = (d_act * a_up * (sigma + swish * (1.0 - sigma))).astype(BF16)
    d_up = (d_act * swish).astype(BF16)
    out_acc[...] += dot_nt(gated, w_down)
    dx_acc[...] += dot_nt(d_gate, w_gate) + dot_nt(d_up, w_up)
    for part, (left, right) in enumerate([(ht_ref, d_gate), (ht_ref, d_up), (dyt_ref, gated)]):
        yield part, dot_nn(left[...], right).astype(BF16)


def expert_kernel(more, *refs):
    h_ref, ht_ref, dy_ref, dyt_ref, gate_ref, wg_ref, wu_ref, wd_ref = refs[:8]
    out_ref, dx_ref, dg_ref, gr_ref, out_acc, dx_acc = refs[-6:]
    step, last = pl.program_id(0), pl.num_programs(0) - 1
    parts, _, part_rows, cols = wg_ref.shape
    chunks = (last + 1) // gate_ref.shape[1]

    @pl.when(step == 0)
    def _():
        if more:
            out0_ref, dx0_ref = refs[8:10]
            out_acc[...] = out0_ref[...].astype(F32)
            dx_acc[...] = dx0_ref[...].astype(F32)
        else:
            out_acc[...] = jnp.zeros_like(out_acc)
            dx_acc[...] = jnp.zeros_like(dx_acc)

    @pl.when(step % chunks == 0)
    def _():
        dg_ref[...] = jnp.zeros_like(dg_ref)

    for part, made in expert_step(
        step // chunks, h_ref, ht_ref, dy_ref, dyt_ref, gate_ref, wg_ref, wu_ref, wd_ref, dg_ref, out_acc, dx_acc
    ):
        gr_ref[:, part, 0] = made.reshape(parts, part_rows, cols)

    @pl.when(step == last)
    def _():
        out_ref[...] = out_acc[...].astype(BF16)
        dx_ref[...] = dx_acc[...].astype(BF16)


def experts(hidden, hidden_t, grad, grad_t, gates, weights, before=()):
    tokens, width = hidden.shape
    parts, count, part_rows, units = weights.shape
    units = units // 3
    cols = min(256, units)
    chunks = units // cols
    once = pl.Buffered(1)
    whole = pl.BlockSpec((tokens, width), lambda s: (0, 0), pipeline_mode=once)
    whole_t = pl.BlockSpec((width, tokens), lambda s: (0, 0), pipeline_mode=once)
    result = pl.BlockSpec((tokens, width), lambda s: (0, 0))

    def weight(kind):
        return pl.BlockSpec(
            (parts, 1, part_rows, cols), lambda s: (0, s // chunks, 0, kind * chunks + s % chunks)
        )

    return pl.pallas_call(
        functools.partial(expert_kernel, bool(before)),
        grid=(count * chunks,),
        in_specs=[
            whole,
            whole_t,
            whole,
            whole_t,
            pl.BlockSpec(gates.shape, lambda s: (0, 0), pipeline_mode=once),
            weight(0),
            weight(1),
            weight(2),
            *[whole for _ in before],
        ],
        out_specs=[
            result,
            result,
            pl.BlockSpec((1, tokens, 1), lambda s: (s // chunks, 0, 0)),
            pl.BlockSpec((parts, 3, 1, part_rows, cols), lambda s: (0, 0, s // chunks, 0, s % chunks)),
        ],
        out_shape=[
            jax.ShapeDtypeStruct((tokens, width), BF16),
            jax.ShapeDtypeStruct((tokens, width), BF16),
            jax.ShapeDtypeStruct((count, tokens, 1), F32),
            jax.ShapeDtypeStruct((parts, 3, count, part_rows, units), BF16),
        ],
        scratch_shapes=[
            pltpu.VMEM((tokens, width), F32),
            pltpu.VMEM((tokens, width), F32),
        ],
        compiler_params=pltpu.CompilerParams(vmem_limit_bytes=VMEM_LIMIT),
        cost_estimate=pl.CostEstimate(
            flops=18 * count * tokens * width * units,
            bytes_accessed=12 * count * width * units,
            transcendentals=count * tokens * units,
        ),
        name="experts",
    )(hidden, hidden_t, grad, grad_t, gates, weights, weights, weights, *before)


def finish_experts_kernel(sums_ref, *refs):
    gate_up_ref, down_ref = refs[-2:]
    units = down_ref.shape[2]
    gate_up_ref[0, :, :units] = sums_ref[0, 0].astype(F32)
    gate_up_ref[0, :, units:] = sums_ref[1, 0].astype(F32)
    down_ref[0] = sums_ref[2, 0].astype(F32)


def finish_experts(sums, at, total, before=()):
    _, count, rows, units = sums.shape
    tile = min(128, rows)
    return pl.pallas_call(
        finish_experts_kernel,
        grid=(count, rows // tile),
        in_specs=[
            pl.BlockSpec((3, 1, tile, units), lambda e, r: (0, e, r, 0)),
            *[pl.BlockSpec(memory_space=pl.ANY) for _ in before],
        ],
        out_specs=[
            pl.BlockSpec((1, tile, 2 * units), lambda e, r: (at + e, r, 0)),
            pl.BlockSpec((1, tile, units), lambda e, r: (at + e, r, 0)),
        ],
        out_shape=[
            jax.ShapeDtypeStruct((total, rows, 2 * units), F32),
            jax.ShapeDtypeStruct((total, rows, units), F32),
        ],
        input_output_aliases={1 + i: i for i in range(len(before))},
        compiler_params=pltpu.CompilerParams(vmem_limit_bytes=VMEM_LIMIT),
        name="finish_experts",
    )(sums, *before)


def turn(values, cos, sin):
    return values * cos + pltpu.roll(values, values.shape[1] // 2, 1) * sin


def project_kernel(
    tok_ref, gain_ref, w_ref, cos_ref, sin_ref, gains_ref, hidden_ref, qkv_ref, raw_ref
):
    head_dim = cos_ref.shape[1]
    values = tok_ref[...].astype(F32)
    hidden = (values * rms_scale(values) * gain_ref[...]).astype(BF16)
    hidden_ref[...] = hidden
    projected = dot_nn(hidden, w_ref[...])
    raw_ref[...] = projected[:, : 2 * head_dim]
    for part in range(2):
        at = slice(part * head_dim, (part + 1) * head_dim)
        raw = projected[:, at]
        normed = raw * rms_scale(raw) * gains_ref[part : part + 1, :]
        qkv_ref[:, at] = turn(normed, cos_ref[...], sin_ref[...]).astype(BF16)
    qkv_ref[:, 2 * head_dim :] = projected[:, 2 * head_dim :].astype(BF16)


def project(toks, gain, weights, cos, sin, gains):
    length, width = toks.shape
    head_dim = cos.shape[1]
    tile = min(256, length)

    def rows(columns):
        return pl.BlockSpec((tile, columns), lambda i: (i, 0))

    def fixed(shape):
        return pl.BlockSpec(shape, lambda i: (0, 0))

    return pl.pallas_call(
        project_kernel,
        grid=(length // tile,),
        in_specs=[
            rows(width),
            fixed((1, width)),
            fixed(weights.shape),
            rows(head_dim),
            rows(head_dim),
            fixed(gains.shape),
        ],
        out_specs=[rows(width), rows(3 * head_dim), rows(2 * head_dim)],
        out_shape=[
            jax.ShapeDtypeStruct((length, width), BF16),
            jax.ShapeDtypeStruct((length, 3 * head_dim), BF16),
            jax.ShapeDtypeStruct((length, 2 * head_dim), F32),
        ],
        compiler_params=pltpu.CompilerParams(vmem_limit_bytes=VMEM_LIMIT),
        name="project",
    )(toks, gain, weights, cos, sin, gains)


def project_back_kernel(
    factor, scale, q_ref, k_ref, v_ref, do_ref, of_ref, lse_ref, sq_ref, sk_ref,
    raw_q_ref, raw_k_ref, cos_q_ref, sin_q_ref, cos_ref, sin_ref, gains_ref,
    dp_ref, dgain_ref, kt_ref, dk_acc, dv_acc,
):
    length, head_dim = k_ref.shape
    size, count = key_chunks(length)
    tile = q_ref.shape[0]
    step_at = pl.program_id(0)

    @pl.when(step_at == 0)
    def _():
        kt_ref[...] = k_ref[...].astype(F32).T.astype(BF16)
        dk_acc[...] = jnp.zeros_like(dk_acc)
        dv_acc[...] = jnp.zeros_like(dv_acc)
        dgain_ref[...] = jnp.zeros_like(dgain_ref)

    def to_raw(part, grad, raw, cos, sin):
        grad = turn(grad.astype(BF16).astype(F32), cos, -sin)
        raw_scale = rms_scale(raw)
        dgain_ref[part : part + 1, :] += jnp.sum(grad * (raw * raw_scale), axis=0, keepdims=True)
        return norm_back(grad * gains_ref[part : part + 1, :], raw, raw_scale).astype(BF16)

    q = q_ref[...]
    grad = do_ref[...]
    seg_q = sq_ref[...]
    lse = lse_ref[0]
    row_dot = jnp.sum((grad.astype(F32) * of_ref[0]).T, axis=0, keepdims=True)
    dq_t = jnp.zeros((head_dim, tile), F32)
    for j in range(count):
        rows = slice(j * size, (j + 1) * size)
        scores = dot_nt(k_ref[rows, :], q)
        scores = jnp.where(sk_ref[rows, :] == seg_q, scores, NEG)
        weights = jnp.exp2(scores * factor - lse)
        grad_weights = dot_nt(v_ref[rows, :], grad)
        grad_scores = (weights * (grad_weights - row_dot)).astype(BF16)
        dk_acc[rows, :] += dot_nn(grad_scores, q)
        dv_acc[rows, :] += dot_nn(weights.astype(BF16), grad)
        dq_t = dq_t + dot_nn(kt_ref[:, rows], grad_scores)
    own = pl.ds(pl.multiple_of(step_at * tile, tile), tile)
    dp_ref[own, :head_dim] = to_raw(
        0, (dq_t * scale).T, raw_q_ref[...], cos_q_ref[...], sin_q_ref[...]
    )

    @pl.when(step_at == pl.num_programs(0) - 1)
    def _():
        dp_ref[:, head_dim : 2 * head_dim] = to_raw(
            1, dk_acc[...] * scale, raw_k_ref[...], cos_ref[...], sin_ref[...]
        )
        dp_ref[:, 2 * head_dim :] = dv_acc[...].astype(BF16)


def project_back(qkv, grad, out_f32, lse, segments, raw, cos, sin, gains):
    length, head_dim = grad.shape
    tile = min(256, length)

    def rows(column):
        return pl.BlockSpec((tile, head_dim), lambda i: (i, column))

    def whole(column):
        return pl.BlockSpec((length, head_dim), lambda i: (0, column))

    return pl.pallas_call(
        functools.partial(project_back_kernel, head_dim**-0.5 * LOG2E, head_dim**-0.5),
        grid=(length // tile,),
        in_specs=[
            rows(0),
            whole(1),
            whole(2),
            rows(0),
            pl.BlockSpec((1, tile, head_dim), lambda i: (0, i, 0)),
            pl.BlockSpec((1, 1, tile), lambda i: (0, 0, i)),
            pl.BlockSpec((1, tile), lambda i: (0, i)),
            pl.BlockSpec((length, 1), lambda i: (0, 0)),
            rows(0),
            whole(1),
            rows(0),
            rows(0),
            whole(0),
            whole(0),
            pl.BlockSpec(gains.shape, lambda i: (0, 0)),
        ],
        out_specs=[
            pl.BlockSpec((length, 3 * head_dim), lambda i: (0, 0)),
            pl.BlockSpec((2, head_dim), lambda i: (0, 0)),
        ],
        out_shape=[
            jax.ShapeDtypeStruct((length, 3 * head_dim), BF16),
            jax.ShapeDtypeStruct((2, head_dim), F32),
        ],
        scratch_shapes=[
            pltpu.VMEM((head_dim, length), BF16),
            pltpu.VMEM((length, head_dim), F32),
            pltpu.VMEM((length, head_dim), F32),
        ],
        compiler_params=pltpu.CompilerParams(vmem_limit_bytes=VMEM_LIMIT),
        cost_estimate=pl.CostEstimate(
            flops=10 * length * length * head_dim,
            bytes_accessed=length * head_dim * 40,
            transcendentals=length * length,
        ),
        name="project_back",
    )(
        qkv, qkv, qkv, grad, out_f32, lse, segments.reshape(1, -1), segments.reshape(-1, 1),
        raw, raw, cos, sin, cos, sin, gains,
    )


def merge_heads_kernel(parts_ref, out_ref):
    blk, uly, _, columns = parts_ref.shape
    head_dim = columns // 3
    heads = blk * uly
    for z in range(blk):
        for u in range(uly):
            head = parts_ref[z, u].astype(F32)
            for part in range(3):
                at = (part * heads + u * blk + z) * head_dim
                out_ref[:, at : at + head_dim] = head[:, part * head_dim : (part + 1) * head_dim]


def merge_heads(parts):
    blk, uly, rows, columns = parts.shape
    return pl.pallas_call(
        merge_heads_kernel,
        out_shape=jax.ShapeDtypeStruct((rows, blk * uly * columns), F32),
        compiler_params=pltpu.CompilerParams(vmem_limit_bytes=VMEM_LIMIT),
        name="merge_heads",
    )(parts)


def swap(values, axis):
    return lax.all_to_all(values, axis, split_axis=0, concat_axis=0, tiled=True)


def sum_scatter(values, axis):
    count = spread(axis) if isinstance(axis, tuple) else lax.axis_size(axis)
    rows, width = values.shape
    parts = swap(values.astype(BF16).reshape(count, rows // count, width), axis)
    return jnp.sum(parts.astype(F32), axis=0)


def place(axes, index):
    found = {}
    for axis in reversed(axes):
        size = lax.axis_size(axis)
        found[axis] = lax.rem(index, size)
        index = index // size
    return found


def spread(axes):
    return math.prod(lax.axis_size(axis) for axis in axes)


def each(count, body):
    if count <= 4:
        for step in range(1, count):
            body(step)
    else:

        def looped(step, carried):
            body(step)
            return carried

        lax.fori_loop(1, count, looped, 0)


def ahead(index, step, size):
    return lax.rem(index + step, size)


def exchange(items, collective_id, after=()):
    count = len(items)
    sizes = [spread(axes) for _, axes, _ in items]
    groups = list(dict.fromkeys(axes for _, axes, _ in items))
    bases = [sum(2 * size for size in sizes[:i]) for i in range(count)]

    def kernel(*refs):
        ins = refs[:count]
        outs = refs[count + len(after) : 2 * count + len(after)]
        send, recv, local = refs[-3:]
        barrier = pltpu.get_barrier_semaphore()
        for axes in groups:
            size, me = spread(axes), lax.axis_index(axes)

            def greet(step, axes=axes, size=size, me=me):
                pl.semaphore_signal(
                    barrier, inc=1, device_id=place(axes, ahead(me, step, size)), device_id_type=MESH
                )

            each(size, greet)
        pl.semaphore_wait(barrier, sum(spread(axes) - 1 for axes in groups))

        def remote(i, step):
            _, axes, kind = items[i]
            me = lax.axis_index(axes)
            if kind == "trade":
                return pltpu.make_async_remote_copy(
                    src_ref=ins[i],
                    dst_ref=outs[i],
                    send_sem=send.at[bases[i] + 1],
                    recv_sem=recv.at[bases[i] + 1],
                    device_id=place(axes, 1 - me),
                    device_id_type=MESH,
                )
            if kind == "relay":
                far, near = lax.rem(me + 2, 4), me + 1 - 2 * lax.rem(me, 2)
                held = far if step == 3 else me
                return pltpu.make_async_remote_copy(
                    src_ref=outs[i].at[far] if step == 3 else ins[i],
                    dst_ref=outs[i].at[held],
                    send_sem=send.at[bases[i] + step],
                    recv_sem=recv.at[bases[i] + step],
                    device_id=place(axes, far if step == 1 else near),
                    device_id_type=MESH,
                )
            peer = ahead(me, step, sizes[i])
            return pltpu.make_async_remote_copy(
                src_ref=ins[i].at[peer] if kind == "swap" else ins[i],
                dst_ref=outs[i].at[me],
                send_sem=send.at[bases[i] + step],
                recv_sem=recv.at[bases[i] + step],
                device_id=place(axes, peer),
                device_id_type=MESH,
            )

        def own(i):
            _, axes, kind = items[i]
            me = lax.axis_index(axes)
            return pltpu.make_async_copy(
                ins[i].at[me] if kind == "swap" else ins[i], outs[i].at[me], local.at[i]
            )

        def hop(i, up, hops):
            (axis,) = items[i][1]
            me, size = lax.axis_index(axis), sizes[i]
            way = 1 if up else -1
            held, to = me - way * hops, me + way
            exists = (held >= 0) & (held < size) & (to >= 0) & (to < size)
            held, to = jnp.clip(held, 0, size - 1), jnp.clip(to, 0, size - 1)
            sem = bases[i] + (size if up else 0) + hops
            copy = pltpu.make_async_remote_copy(
                src_ref=outs[i].at[held] if hops else ins[i],
                dst_ref=outs[i].at[held],
                send_sem=send.at[sem],
                recv_sem=recv.at[sem],
                device_id={axis: to},
                device_id_type=MESH,
            )
            return exists, copy

        def arrival(i, up, hops):
            (axis,) = items[i][1]
            me, size = lax.axis_index(axis), sizes[i]
            way = 1 if up else -1
            held, sender = me - way * (hops + 1), me - way
            exists = (held >= 0) & (held < size)
            held, sender = jnp.clip(held, 0, size - 1), jnp.clip(sender, 0, size - 1)
            sem = bases[i] + (size if up else 0) + hops
            copy = pltpu.make_async_remote_copy(
                src_ref=ins[i],
                dst_ref=outs[i].at[held],
                send_sem=send.at[sem],
                recv_sem=recv.at[sem],
                device_id={axis: sender},
                device_id_type=MESH,
            )
            return exists, copy

        def kinds(*names):
            return [i for i in range(count) if items[i][2] in names]

        def when(pair, act):
            exists, copy = pair
            pl.when(exists)(lambda: act(copy))

        ways = (True, False)
        for i in kinds("line"):
            for up in ways:
                when(hop(i, up, 0), lambda copy: copy.start())
        for i in kinds("gather", "swap", "relay", "trade"):
            each(3 if items[i][2] == "relay" else sizes[i], lambda step, i=i: remote(i, step).start())
        for i in kinds("gather", "swap", "relay", "line"):
            own(i).start()
        for i in kinds("line"):
            for hops in range(1, sizes[i]):
                for up in ways:
                    when(arrival(i, up, hops - 1), lambda copy: copy.wait_recv())
                    if hops < sizes[i] - 1:
                        when(hop(i, up, hops), lambda copy: copy.start())
        for i in kinds("relay"):
            remote(i, 1).wait_recv()
            remote(i, 3).start()
            remote(i, 1).wait_send()
            for step in (2, 3):
                remote(i, step).wait()
        for i in kinds("gather", "swap", "trade"):
            each(sizes[i], lambda step, i=i: remote(i, step).wait())
        for i in kinds("line"):
            for hops in range(sizes[i] - 1):
                for up in ways:
                    when(hop(i, up, hops), lambda copy: copy.wait_send())
        for i in kinds("gather", "swap", "relay", "line"):
            own(i).wait()

    shapes = [
        array.shape if kind == "trade" else (size, *(array.shape[1:] if kind == "swap" else array.shape))
        for size, (array, _, kind) in zip(sizes, items)
    ]
    anywhere = pl.BlockSpec(memory_space=pl.ANY)
    return pl.pallas_call(
        kernel,
        in_specs=[anywhere] * (count + len(after)),
        out_specs=[anywhere] * count,
        out_shape=[jax.ShapeDtypeStruct(shape, item[0].dtype) for shape, item in zip(shapes, items)],
        scratch_shapes=[
            pltpu.SemaphoreType.DMA((2 * sum(sizes),)),
            pltpu.SemaphoreType.DMA((2 * sum(sizes),)),
            pltpu.SemaphoreType.DMA((count,)),
        ],
        compiler_params=pltpu.CompilerParams(collective_id=collective_id, has_side_effects=True),
        name="exchange",
    )(*[item[0] for item in items], *after)


def startup_kernel(
    head_ref, extra_ref, tok_ref, heads_ref, extras_ref, toks_ref,
    head_send, head_recv, extra_send, extra_recv,
    z_send, z_recv, ay_send, ay_recv, by_send, by_recv, c_send, c_recv, local,
):
    blk, uly = lax.axis_size("blk"), spread(ULY)
    total = spread(ALL)
    z, u, me = lax.axis_index("blk"), lax.axis_index(ULY), lax.axis_index(ALL)
    far = lax.rem(u + 2, uly)
    near = u + 1 - 2 * lax.rem(u, 2)
    half = tok_ref.shape[0] // 2
    parts = (pl.ds(0, half), pl.ds(half, half))

    barrier = pltpu.get_barrier_semaphore()

    def greet(step):
        pl.semaphore_signal(
            barrier, inc=1, device_id=place(ALL, ahead(me, step, total)), device_id_type=MESH
        )

    each(total, greet)
    pl.semaphore_wait(barrier, total - 1)

    def send(src, dst, sent, got, to):
        return pltpu.make_async_remote_copy(
            src_ref=src, dst_ref=dst, send_sem=sent, recv_sem=got, device_id=to, device_id_type=MESH
        )

    def block(step, other, part):
        at = toks_ref.at[ahead(z, step, blk), far if other else u, parts[part]]
        return (tok_ref.at[parts[part]] if step == 0 and not other else at), at

    streams = ((0, 0), (0, 1), (1, 1))

    def hop(stream, up, hops):
        other, part = streams[stream]
        way = 1 if up else -1
        held, to = z - way * hops, z + way
        exists = (held >= 0) & (held < blk) & (to >= 0) & (to < blk)
        held, to = jnp.clip(held, 0, blk - 1), jnp.clip(to, 0, blk - 1)
        at = toks_ref.at[held, far if other else u, parts[part]]
        src = tok_ref.at[parts[part]] if hops == 0 and not other else at
        sem = (2 * stream + up) * blk + hops
        return exists, send(src, at, z_send.at[sem], z_recv.at[sem], {"blk": to})

    def arrival(stream, up, hops):
        other, part = streams[stream]
        way = 1 if up else -1
        held, sender = z - way * (hops + 1), z - way
        exists = (held >= 0) & (held < blk)
        held, sender = jnp.clip(held, 0, blk - 1), jnp.clip(sender, 0, blk - 1)
        at = toks_ref.at[held, far if other else u, parts[part]]
        sem = (2 * stream + up) * blk + hops
        return exists, send(tok_ref.at[parts[part]], at, z_send.at[sem], z_recv.at[sem], {"blk": sender})

    def when(pair, act):
        exists, copy = pair
        pl.when(exists)(lambda: act(copy))

    def a_y(step):
        return send(*block(step, 0, 0), ay_send.at[step], ay_recv.at[step], place(ULY, far))

    def b_y():
        return send(*block(0, 0, 1), by_send.at[0], by_recv.at[0], place(ULY, far))

    def to_near(step, other, part):
        sem = 4 * step + 2 * other + part
        return send(*block(step, other, part), c_send.at[sem], c_recv.at[sem], place(ULY, near))

    def head(step):
        to = place(ALL, ahead(me, step, total))
        src = head_ref.at[(to["y"] * lax.axis_size("core") + to["core"]) * blk + to["blk"]]
        return send(src, heads_ref.at[me], head_send.at[step], head_recv.at[step], to)

    def extra(step):
        to = place(ALL, ahead(me, step, total))
        return send(extra_ref, extras_ref.at[me], extra_send.at[step], extra_recv.at[step], to)

    own = [
        pltpu.make_async_copy(tok_ref, toks_ref.at[z, u], local.at[0]),
        pltpu.make_async_copy(head_ref.at[u * blk + z], heads_ref.at[me], local.at[1]),
        pltpu.make_async_copy(extra_ref, extras_ref.at[me], local.at[2]),
    ]

    ways = (1, 0)
    b_y().start()
    for stream in range(2):
        for up in ways:
            when(hop(stream, up, 0), lambda copy: copy.start())
    a_y(0).start()
    to_near(0, 0, 0).start()
    to_near(0, 0, 1).start()

    def start_head(step):
        extra(step).start()
        head(step).start()

    each(total, start_head)
    for copy in own:
        copy.start()
    b_y().wait_recv()
    for up in ways:
        when(hop(2, up, 0), lambda copy: copy.start())
    to_near(0, 1, 1).start()
    for hops in range(1, blk):
        for stream, (other, part) in enumerate(streams):
            for up in ways:
                exists, copy = arrival(stream, up, hops - 1)
                step = blk - hops if up else hops

                @pl.when(exists)
                def _(copy=copy, stream=stream, other=other, part=part, up=up, step=step, hops=hops):
                    copy.wait_recv()
                    if hops < blk - 1:
                        when(hop(stream, up, hops), lambda copy: copy.start())
                    if stream == 0:
                        a_y(step).start()
                    to_near(step, other, part).start()

    for step in [0, *reversed(range(1, blk))]:
        a_y(step).wait_recv()
        to_near(step, 1, 0).start()
    for step in range(blk):
        for other in range(2):
            for part in range(2):
                to_near(step, other, part).wait_recv()

    def wait_head(step):
        extra(step).wait()
        head(step).wait()

    each(total, wait_head)
    for copy in own:
        copy.wait()
    b_y().wait_send()
    for hops in range(blk - 1):
        for stream in range(3):
            for up in ways:
                when(hop(stream, up, hops), lambda copy: copy.wait_send())
    for step in range(blk):
        a_y(step).wait_send()
        for other in range(2):
            for part in range(2):
                to_near(step, other, part).wait_send()


def startup(heads, extra, tok, collective_id):
    blk, uly, total = lax.axis_size("blk"), spread(ULY), spread(ALL)
    anywhere = pl.BlockSpec(memory_space=pl.ANY)
    dma = pltpu.SemaphoreType.DMA
    return pl.pallas_call(
        startup_kernel,
        in_specs=[anywhere] * 3,
        out_specs=[anywhere] * 3,
        out_shape=[
            jax.ShapeDtypeStruct((total, *heads.shape[1:]), BF16),
            jax.ShapeDtypeStruct((total, *extra.shape), BF16),
            jax.ShapeDtypeStruct((blk, uly, *tok.shape), BF16),
        ],
        scratch_shapes=[
            *[dma((total,))] * 4,
            *[dma((6 * blk,))] * 2,
            *[dma((blk,))] * 2,
            *[dma((1,))] * 2,
            *[dma((4 * blk,))] * 2,
            dma((3,)),
        ],
        compiler_params=pltpu.CompilerParams(collective_id=collective_id, has_side_effects=True),
        name="startup",
    )(heads, extra, tok)


def per_device_general(
    tokens, segments, routes, w_qkv, w_out, attn_gain, ffn_gain, qk_gain, router, w_gate_up, w_down, cotangent
):
    own_tokens = tokens[0]
    own_grad = cotangent[0]
    count_tok, width = own_tokens.shape
    head_dim = qk_gain.shape[1]
    heads = width // head_dim
    uly, blk, batch = spread(ULY), lax.axis_size("blk"), lax.axis_size("batch")
    blk_at, uly_at = lax.axis_index("blk"), lax.axis_index(ULY)
    group = batch * blk
    local_heads = heads // uly
    local_width = local_heads * head_dim
    rows = count_tok * uly
    seg_row = segments[0]
    length = seg_row.shape[0]
    number = router.shape[1]
    local_experts, _, units = w_down.shape
    shard_rows = w_qkv.shape[0]

    extra = jnp.concatenate([attn_gain[:, None], ffn_gain[:, None], router], axis=1)
    extra = jnp.pad(extra, ((0, 0), (0, LANES - extra.shape[1])))
    columns = w_qkv.reshape(shard_rows, 3, uly, local_width).transpose(2, 0, 1, 3)
    packed = jnp.concatenate(
        [
            columns.reshape(uly, shard_rows, 3 * local_width),
            jnp.broadcast_to(extra[None], (uly, shard_rows, LANES)),
        ],
        axis=2,
    )
    packed = swap(packed, ULY).reshape(uly * shard_rows, 3 * local_width + LANES)
    packed = lax.all_gather(packed, ROWS, axis=0, tiled=True)
    own_qkv = packed[:, : 3 * local_width]
    gain_attn = packed[:, 3 * local_width].astype(F32)
    gain_ffn = packed[:, 3 * local_width + 1].astype(F32)
    whole_router = packed[:, 3 * local_width + 2 : 3 * local_width + 2 + number]
    tokens_all = lax.all_gather(own_tokens, ULY, axis=0, tiled=True)
    to_rows = [(u * group + g, g * uly + u) for g in range(group) for u in range(uly)]
    own_out = lax.all_gather(lax.ppermute(w_out, ALL, to_rows), ROWS, axis=0, tiled=True)
    whole_gate_up = lax.all_gather(w_gate_up, PLANE, axis=0, tiled=False)
    whole_down = lax.all_gather(w_down, PLANE, axis=0, tiled=False)
    grad_blk = lax.all_gather(own_grad, "blk", axis=0, tiled=True)
    routes_blk = lax.all_gather(routes[0], "blk", axis=0, tiled=True)

    gain_query = qk_gain[0].astype(F32)
    gain_key = qk_gain[1].astype(F32)
    inputs_all = tokens_all.astype(F32)
    normed_one = inputs_all * rms_scale(inputs_all)
    hidden_one = (normed_one * gain_attn).astype(BF16)
    projected = dot_nn(hidden_one, own_qkv)
    query_raw = projected[:, :local_width].reshape(rows, local_heads, head_dim)
    key_raw = projected[:, local_width : 2 * local_width].reshape(rows, local_heads, head_dim)
    value_raw = projected[:, 2 * local_width :].reshape(rows, local_heads, head_dim)
    cos_table, sin_table = rope_tables(blk_at * rows, rows, head_dim)
    query_scale = rms_scale(query_raw)
    key_scale = rms_scale(key_raw)
    qkv = jnp.concatenate(
        [
            rotate(query_raw * query_scale * gain_query, cos_table, sin_table),
            rotate(key_raw * key_scale * gain_key, cos_table, sin_table),
            value_raw,
        ],
        axis=2,
    ).astype(BF16)
    qkv = qkv.transpose(1, 0, 2)

    by_heads = local_heads % blk == 0
    if by_heads:
        per = local_heads // blk

        def to_heads(values):
            columns = values.shape[2]
            moved = swap(values.reshape(blk, per, rows, columns), "blk")
            return moved.transpose(1, 0, 2, 3).reshape(per, length, columns)

        def to_rows_back(values):
            columns = values.shape[2]
            parts = values.reshape(per, blk, rows, columns).transpose(1, 0, 2, 3)
            return swap(parts, "blk").reshape(local_heads, rows, columns)

        q_src = kv_src = to_heads(qkv)
        cols = (0, 1, 2)
        seg_q = seg_row
        first_head = uly_at * local_heads + blk_at * per
    else:

        def to_heads(values):
            return values

        def to_rows_back(values):
            return values

        q_src = qkv
        kv_src = lax.all_gather(qkv[:, :, head_dim:], "blk", axis=1, tiled=True)
        cols = (0, 0, 1)
        seg_q = lax.dynamic_slice_in_dim(seg_row, blk_at * rows, rows)
        first_head = uly_at * local_heads
    attn_low, attn_f32, lse, top = attention_forward(q_src, kv_src, cols, seg_q, seg_row, head_dim)
    head_vector = lax.dynamic_update_slice_in_dim(
        jnp.full((heads,), NEG, F32), jnp.max(top, axis=(1, 2)) * head_dim**-0.5, first_head, 0
    )
    head_max = lax.pmax(head_vector, ALL)
    attn_rows = to_rows_back(attn_low)
    out_heads = own_out.reshape(local_heads, head_dim, width)
    branch = jnp.einsum("htc,hcd->td", attn_rows, out_heads, preferred_element_type=F32)
    inputs = own_tokens.astype(F32)
    mid = inputs + sum_scatter(branch, ULY)

    scale_two = rms_scale(mid)
    normed_two = mid * scale_two
    hidden_two = (normed_two * gain_ffn).astype(BF16)
    hidden_blk = lax.all_gather(hidden_two, "blk", axis=0, tiled=True)
    probs_blk = jax.nn.softmax(dot_nn(hidden_blk, whole_router), axis=1)
    names = jnp.arange(number, dtype=jnp.int32)
    chosen_blk = jnp.any(routes_blk[:, :, None] == names, axis=1).astype(F32)
    own_names = blk_at * local_experts
    gates = lax.dynamic_slice_in_dim(probs_blk * chosen_blk, own_names, local_experts, axis=1)
    most = min(MOST_TOKENS, hidden_blk.shape[0])
    packed_weights = jnp.concatenate([whole_gate_up, whole_down], axis=3)
    made = []
    for at in range(0, hidden_blk.shape[0], most):
        hidden_part, grad_part = hidden_blk[at : at + most], grad_blk[at : at + most]
        made.append(
            experts(
                hidden_part,
                hidden_part.T,
                grad_part,
                grad_part.T,
                gates[at : at + most],
                packed_weights,
            )
        )
    out_part = jnp.concatenate([m[0] for m in made], axis=0)
    dx_part = jnp.concatenate([m[1] for m in made], axis=0)
    dg_part = jnp.concatenate([m[2] for m in made], axis=1)
    expert_grads = sum(m[3].astype(F32) for m in made).astype(BF16)
    expert_sums = lax.psum_scatter(expert_grads, PLANE, scatter_dimension=0, tiled=False).astype(F32)
    grad_gate_up = jnp.concatenate([expert_sums[0], expert_sums[1]], axis=2)
    grad_down = expert_sums[2]
    dg_parts = swap(dg_part.reshape(local_experts, blk, count_tok).transpose(1, 2, 0), "blk")
    grad_gates = dg_parts.transpose(1, 0, 2).reshape(count_tok, number)
    dx_sum = sum_scatter(dx_part, "blk")
    output = (mid + sum_scatter(out_part, "blk")).astype(BF16)
    router_probs = lax.dynamic_slice_in_dim(probs_blk, blk_at * count_tok, count_tok)
    chosen = lax.dynamic_slice_in_dim(chosen_blk, blk_at * count_tok, count_tok)
    grad_probs = chosen * grad_gates
    grad_logits = (
        router_probs * (grad_probs - jnp.sum(router_probs * grad_probs, axis=1, keepdims=True))
    ).astype(BF16)
    grad_hidden_two = dx_sum + dot_nt(grad_logits, whole_router)
    grad_router_part = dot_tn(hidden_two, grad_logits)
    grad_gain_ffn = jnp.sum(grad_hidden_two * normed_two, axis=0)
    grad_mid = own_grad.astype(F32) + norm_back(grad_hidden_two * gain_ffn, mid, scale_two)

    branch_grad = lax.all_gather(grad_mid.astype(BF16), ULY, axis=0, tiled=True)
    grad_attn = dot_nt(branch_grad, own_out).astype(BF16)
    grad_attn = to_heads(grad_attn.reshape(rows, local_heads, head_dim).transpose(1, 0, 2))
    grad_out_part = jnp.einsum("htc,td->hcd", attn_rows, branch_grad, preferred_element_type=F32)
    dq, dk, dv = attention_backward(
        q_src, kv_src, cols, grad_attn, attn_f32, lse, seg_q, seg_row, head_dim
    )
    if by_heads:
        dqkv = to_rows_back(jnp.concatenate([dq, dk, dv], axis=2))
        dq, dk, dv = jnp.split(dqkv, 3, axis=2)
    else:
        dk, dv = (lax.psum_scatter(g, "blk", scatter_dimension=1, tiled=True) for g in (dk, dv))
    dq, dk, dv = (g.transpose(1, 0, 2) for g in (dq, dk, dv))
    grad_query_norm = rotate(dq.astype(F32), cos_table, -sin_table)
    grad_key_norm = rotate(dk.astype(F32), cos_table, -sin_table)
    grad_gain_query = jnp.sum(grad_query_norm * (query_raw * query_scale), axis=(0, 1))
    grad_gain_key = jnp.sum(grad_key_norm * (key_raw * key_scale), axis=(0, 1))
    grad_projected = jnp.concatenate(
        [
            norm_back(grad_query_norm * gain_query, query_raw, query_scale)
            .reshape(rows, local_width)
            .astype(BF16),
            norm_back(grad_key_norm * gain_key, key_raw, key_scale)
            .reshape(rows, local_width)
            .astype(BF16),
            dv.reshape(rows, local_width),
        ],
        axis=1,
    )
    grad_hidden_part = dot_nt(grad_projected, own_qkv)
    grad_hidden_one = sum_scatter(grad_hidden_part, ULY)
    grad_gain_attn = jnp.sum(grad_hidden_part * normed_one, axis=0)
    grad_inputs = grad_mid + norm_back(grad_hidden_one * gain_attn, inputs, rms_scale(inputs))

    grad_qkv_part = dot_tn(hidden_one, grad_projected).astype(BF16)
    grad_qkv_rows = lax.psum_scatter(grad_qkv_part, ROWS, scatter_dimension=0, tiled=True)
    grad_qkv_rows = swap(grad_qkv_rows.reshape(uly, shard_rows, 3 * local_width), ULY)
    grad_qkv = (
        grad_qkv_rows.reshape(uly, shard_rows, 3, local_width)
        .transpose(1, 2, 0, 3)
        .reshape(shard_rows, 3 * width)
        .astype(F32)
    )
    grad_out_rows = lax.psum_scatter(
        grad_out_part.reshape(local_width, width).astype(BF16), ROWS, scatter_dimension=0, tiled=True
    )
    grad_out = lax.ppermute(grad_out_rows, ALL, [(b, a) for a, b in to_rows]).astype(F32)
    small = jnp.concatenate([grad_gain_attn[:, None], grad_gain_ffn[:, None], grad_router_part], axis=1)
    small = lax.psum_scatter(small, ALL, scatter_dimension=0, tiled=True)
    grad_qk_gain = lax.psum(jnp.stack([grad_gain_query, grad_gain_key]), ALL)

    clip_gamma = TAU / jnp.maximum(head_max, TAU)
    factor = jnp.repeat(jnp.sqrt(clip_gamma), head_dim)
    column_scale = jnp.concatenate([factor, factor, jnp.ones((width,), F32)])
    clipped = w_qkv.astype(F32) * column_scale[None, :]
    return (
        output[None],
        grad_inputs[None],
        grad_qkv,
        grad_out,
        small[:, 0],
        small[:, 1],
        grad_qk_gain,
        small[:, 2:],
        grad_gate_up,
        grad_down,
        clipped,
    )


def per_device(
    tokens, segments, routes, w_qkv, w_out, attn_gain, ffn_gain, qk_gain, router, w_gate_up, w_down, cotangent
):
    own_tokens = tokens[0]
    own_grad = cotangent[0]
    count_tok, width = own_tokens.shape
    head_dim = qk_gain.shape[1]
    heads = width // head_dim
    batch, blk, uly = lax.axis_size("batch"), lax.axis_size("blk"), spread(ULY)
    total, group = batch * blk * uly, batch * blk
    local_experts = w_down.shape[0]
    if uly != 4 or heads != blk * uly or batch != 2 or local_experts != 4:
        return per_device_general(
            tokens, segments, routes, w_qkv, w_out, attn_gain, ffn_gain, qk_gain, router, w_gate_up, w_down, cotangent
        )
    blk_at, uly_at = lax.axis_index("blk"), lax.axis_index(ULY)
    rows = count_tok * uly
    seg_row = segments[0]
    length = seg_row.shape[0]
    number = router.shape[1]
    shard_rows = w_qkv.shape[0]

    to_rows = [(u * group + g, g * uly + u) for g in range(group) for u in range(uly)]
    own_rows = lax.ppermute(w_out, ALL, to_rows)
    half = local_experts // 2
    weights_first, weights_second = (
        lax.all_gather(jnp.concatenate([w_gate_up[at], w_down[at]], axis=2), PLANE, axis=0, tiled=False)
        for at in (slice(0, half), slice(half, local_experts))
    )
    extra = jnp.concatenate([attn_gain[None], ffn_gain[None], router.T], axis=0)
    kept = extra.shape[0]
    extra = jnp.pad(extra, ((0, -kept % 16), (0, -shard_rows % LANES)))
    by_head = w_qkv.reshape(shard_rows, 3, heads, head_dim).transpose(2, 0, 1, 3)
    own_qkv, extras, toks = startup(
        by_head.reshape(heads, shard_rows, 3 * head_dim), extra, own_tokens, 0
    )
    own_rows, extras = lax.optimization_barrier((own_rows, extras))
    own_out = lax.all_to_all(
        jnp.broadcast_to(own_rows[None], (group, *own_rows.shape)), ROWS, split_axis=0, concat_axis=0, tiled=True
    ).reshape(blk, head_dim, width)
    own_qkv = own_qkv.reshape(width, 3 * head_dim)
    extras = extras[:, :kept, :shard_rows].transpose(1, 0, 2).reshape(kept, width)
    gain_attn = extras[0].astype(F32)
    gain_ffn = extras[1].astype(F32)
    router_t = extras[2:]

    gains = qk_gain.astype(F32)
    cos, sin = rope_rows(length, head_dim)
    hidden_one, qkv, raw = project(
        toks.reshape(length, width), gain_attn[None], own_qkv, cos, sin, gains
    )
    attn_low, attn_f32, lse, top = attention_forward(
        qkv[None], qkv[None], (0, 1, 2), seg_row, seg_row, head_dim
    )
    (attn_rows,) = exchange([(attn_low.reshape(blk, rows, head_dim), ("blk",), "swap")], 1)
    branch = jnp.einsum("htc,hcd->td", attn_rows, own_out, preferred_element_type=F32)
    branch, grad_blk, routes_blk = exchange(
        [
            (branch.astype(BF16).reshape(uly, count_tok, width), ULY, "swap"),
            (own_grad, ("blk",), "line"),
            (routes[0].T, ("blk",), "gather"),
        ],
        2,
    )
    inputs = own_tokens.astype(F32)
    mid = inputs + jnp.sum(branch.astype(F32), axis=0)

    scale_two = rms_scale(mid)
    normed_two = mid * scale_two
    hidden_two = (normed_two * gain_ffn).astype(BF16)
    (hidden_blk,) = exchange([(hidden_two, ("blk",), "line")], 3, after=[weights_first])
    tokens_blk = blk * count_tok
    hidden_blk = hidden_blk.reshape(tokens_blk, width)
    grad_blk = grad_blk.reshape(tokens_blk, width)
    probs_blk = jax.nn.softmax(dot_nt(hidden_blk, router_t), axis=1)
    names = jnp.arange(number, dtype=jnp.int32)
    chosen_blk = jnp.any(routes_blk[:, :, :, None] == names, axis=1).astype(F32)
    chosen_blk = chosen_blk.reshape(tokens_blk, number)
    gates = lax.dynamic_slice_in_dim(
        probs_blk * chosen_blk, blk_at * local_experts, local_experts, axis=1
    )
    shared = (hidden_blk, hidden_blk.T, grad_blk, grad_blk.T)
    out_first, dx_first, dg_first, grads_first = experts(*shared, gates[:, :half], weights_first)
    sums_first = lax.psum_scatter(grads_first, PLANE, scatter_dimension=0, tiled=False)
    out_part, dx_part, dg_second, grads_second = experts(
        *shared, gates[:, half:], weights_second, before=(out_first, dx_first)
    )
    sums_second = lax.psum_scatter(grads_second, PLANE, scatter_dimension=0, tiled=False)
    finished = finish_experts(sums_first, 0, local_experts)
    grad_gate_up, grad_down = finish_experts(sums_second, half, local_experts, before=finished)
    dg_part = jnp.concatenate([dg_first, dg_second], axis=0).reshape(local_experts, blk, count_tok)
    dx_parts, dg_parts = exchange(
        [
            (dx_part.reshape(blk, count_tok, width), ("blk",), "swap"),
            (dg_part.transpose(1, 0, 2), ("blk",), "swap"),
        ],
        4,
    )
    out_part = out_part.reshape(blk, count_tok, width)
    out_part, dx_parts = lax.optimization_barrier((out_part, dx_parts))
    out_parts = lax.all_to_all(out_part, "blk", split_axis=0, concat_axis=0, tiled=True)
    output = (mid + jnp.sum(out_parts.astype(F32), axis=0)).astype(BF16)
    router_probs = lax.dynamic_slice_in_dim(probs_blk, blk_at * count_tok, count_tok)
    chosen = lax.dynamic_slice_in_dim(chosen_blk, blk_at * count_tok, count_tok)
    grad_probs = chosen * dg_parts.reshape(number, count_tok).T
    grad_logits = (
        router_probs * (grad_probs - jnp.sum(router_probs * grad_probs, axis=1, keepdims=True))
    ).astype(BF16)
    grad_hidden_two = jnp.sum(dx_parts.astype(F32), axis=0) + dot_nn(grad_logits, router_t)
    grad_router_t = dot_tn(grad_logits, hidden_two)
    grad_gain_ffn = jnp.sum(grad_hidden_two * normed_two, axis=0)
    grad_mid = own_grad.astype(F32) + norm_back(grad_hidden_two * gain_ffn, mid, scale_two)

    (branch_grad,) = exchange([(grad_mid.astype(BF16), ULY, "relay")], 5)
    branch_grad, sent_qkv = lax.optimization_barrier((branch_grad, own_qkv))
    far_qkv = lax.ppermute(sent_qkv, "y", [(0, 1), (1, 0)])
    branch_grad = branch_grad.reshape(rows, width)
    grad_attn = jnp.einsum("td,hcd->htc", branch_grad, own_out, preferred_element_type=F32).astype(BF16)
    grad_out_part = jnp.einsum("htc,td->hcd", attn_rows, branch_grad, preferred_element_type=F32)
    grad_out_part = grad_out_part.astype(BF16).reshape(batch, blk, shard_rows, width)
    batch_at = lax.axis_index("batch")
    grad_attn, got_out_part = exchange(
        [
            (grad_attn, ("blk",), "swap"),
            (
                lax.dynamic_index_in_dim(grad_out_part, 1 - batch_at, 0, keepdims=False),
                ("batch",),
                "trade",
            ),
        ],
        6,
        after=[out_parts],
    )
    grad_out_part = lax.dynamic_index_in_dim(grad_out_part, batch_at, 0, keepdims=False) + got_out_part
    grad_projected, grad_gains = project_back(
        qkv, grad_attn.reshape(length, head_dim), attn_f32, lse, seg_row, raw, cos, sin, gains
    )
    by_uly = grad_projected.reshape(blk, uly, count_tok, 3 * head_dim).transpose(1, 0, 2, 3)
    grad_qkv_part = dot_tn(hidden_one, grad_projected).astype(BF16)
    by_batch = grad_qkv_part.reshape(batch, width // batch, 3 * head_dim)
    projected_blk, got_qkv_part, near_qkv, cross_qkv, grad_out_parts = exchange(
        [
            (by_uly.reshape(uly, tokens_blk, 3 * head_dim), ULY, "swap"),
            (
                lax.dynamic_index_in_dim(by_batch, 1 - batch_at, 0, keepdims=False),
                ("batch",),
                "trade",
            ),
            (own_qkv, ("core",), "trade"),
            (far_qkv, ("core",), "trade"),
            (grad_out_part, ("blk",), "swap"),
        ],
        7,
    )
    grad_out = lax.ppermute(
        jnp.sum(grad_out_parts.astype(F32), axis=0).astype(BF16), ALL, [(b, a) for a, b in to_rows]
    ).astype(F32)
    grad_qkv_part = lax.dynamic_index_in_dim(by_batch, batch_at, 0, keepdims=False) + got_qkv_part

    near_at, far_at = uly_at + 1 - 2 * lax.rem(uly_at, 2), lax.rem(uly_at + 2, uly)
    cross_at = lax.rem(near_at + 2, uly)
    grad_hidden_part = sum(
        dot_nt(lax.dynamic_index_in_dim(projected_blk, sender, 0, keepdims=False), weights)
        for sender, weights in [
            (uly_at, own_qkv),
            (near_at, near_qkv),
            (far_at, far_qkv),
            (cross_at, cross_qkv),
        ]
    )
    hidden_own = hidden_one.reshape(blk, uly, count_tok, width)
    hidden_own = lax.dynamic_index_in_dim(hidden_own, uly_at, 1, keepdims=False)
    hidden_own = hidden_own.reshape(tokens_blk, width).astype(F32)
    grad_gain_attn = jnp.sum(grad_hidden_part * hidden_own, axis=0) / gain_attn

    small = jnp.concatenate([grad_gain_attn[None], grad_gain_ffn[None], grad_router_t], axis=0)
    small = small.reshape(kept, total, shard_rows).transpose(1, 0, 2)
    small = jnp.pad(small, ((0, 0), (0, 0), (0, LANES - shard_rows)))
    head_row = jnp.where(
        jnp.arange(LANES) == uly_at * blk + blk_at, jnp.max(top) * head_dim**-0.5, NEG
    )
    to_all = jnp.concatenate([grad_gains, head_row[None]], axis=0)
    small = jnp.concatenate([small, jnp.broadcast_to(to_all[None], (total, 3, LANES))], axis=1)
    small = jnp.pad(small, ((0, 0), (0, -small.shape[1] % 8), (0, 0)))
    grad_hidden_parts, small, grad_qkv_parts = exchange(
        [
            (grad_hidden_part.astype(BF16).reshape(blk, count_tok, width), ("blk",), "swap"),
            (small, ALL, "swap"),
            (grad_qkv_part.reshape(total // batch, shard_rows, 3 * head_dim), ("blk", *ULY), "swap"),
        ],
        8,
        after=[finished[0]],
    )
    grad_qkv = merge_heads(grad_qkv_parts.reshape(blk, uly, shard_rows, 3 * head_dim))
    grad_hidden_one = jnp.sum(grad_hidden_parts.astype(F32), axis=0)
    grad_inputs = grad_mid + norm_back(grad_hidden_one * gain_attn, inputs, rms_scale(inputs))
    sums = jnp.sum(small, axis=0)
    head_max = jnp.max(small[:, kept + 2, :heads], axis=0)
    factor = jnp.repeat(jnp.sqrt(TAU / jnp.maximum(head_max, TAU)), head_dim)
    column_scale = jnp.concatenate([factor, factor, jnp.ones((width,), F32)])
    clipped = w_qkv.astype(F32) * column_scale[None, :]
    return (
        output[None],
        grad_inputs[None],
        grad_qkv,
        grad_out,
        sums[0, :shard_rows],
        sums[1, :shard_rows],
        sums[kept : kept + 2],
        sums[2:kept, :shard_rows].T,
        grad_gate_up,
        grad_down,
        clipped,
    )


def solution(mesh):
    in_specs = (
        P("batch", ("blk", *ULY), None),
        P("batch", None),
        P("batch", ("blk", *ULY), None),
        P(ALL, None),
        P(ALL, None),
        P(ALL),
        P(ALL),
        P(),
        P(ALL, None),
        P("blk", PLANE, None),
        P("blk", PLANE, None),
        P("batch", ("blk", *ULY), None),
    )
    out_specs = (
        P("batch", ("blk", *ULY), None),
        P("batch", ("blk", *ULY), None),
        P(ALL, None),
        P(ALL, None),
        P(ALL),
        P(ALL),
        P(),
        P(ALL, None),
        P("blk", PLANE, None),
        P("blk", PLANE, None),
        P(ALL, None),
    )
    cores = 2 - mesh.shape["uly"] % 2
    mesh = Mesh(
        mesh.devices.reshape(*(mesh.shape[axis] for axis in ROWS), mesh.shape["uly"] // cores, cores), ALL
    )
    return jax.shard_map(
        per_device, mesh=mesh, in_specs=in_specs, out_specs=out_specs, check_vma=False
    )
```

```python
import functools
import math

import jax
import jax.numpy as jnp
from jax import lax
from jax.experimental import pallas as pl
from jax.experimental.pallas import tpu as pltpu
from jax.sharding import Mesh
from jax.sharding import PartitionSpec as P

EPS = 1e-06
THETA = 50000.0
TAU = 4.0
NEG = -1e30
LOG2E = 1.4426950408889634
LANES = 128
MOST_TOKENS = 512
VMEM_LIMIT = 60 * 1024 * 1024

ULY = ("y", "core")
ALL = ("batch", "blk", *ULY)
ROWS = ("batch", "blk")
PLANE = ("batch", *ULY)
CHIPS = ("batch", "y")

MESH = pl.DeviceIdType.MESH
BF16 = jnp.bfloat16
F32 = jnp.float32


def rms_scale(values):
    return lax.rsqrt(jnp.mean(values * values, axis=-1, keepdims=True) + EPS)


def norm_back(grad_normed, values, scale):
    normed = values * scale
    return scale * (grad_normed - normed * jnp.mean(grad_normed * normed, axis=-1, keepdims=True))


def rope_tables(offset, length, head_dim):
    half_dim = head_dim // 2
    frequency = THETA ** (-jnp.arange(half_dim, dtype=F32) * 2.0 / head_dim)
    positions = (offset + jnp.arange(length, dtype=jnp.int32)).astype(F32)
    angles = positions[:, None] * frequency[None, :]
    return (jnp.cos(angles)[:, None, :], jnp.sin(angles)[:, None, :])


def rope_rows(length, head_dim):
    fine = math.gcd(length, LANES)
    frequency = THETA ** (-jnp.arange(head_dim // 2, dtype=F32) * 2.0 / head_dim)
    frequency = jnp.concatenate([frequency, frequency])
    coarse_angle = (jnp.arange(length // fine, dtype=F32) * fine)[:, None, None] * frequency
    fine_angle = jnp.arange(fine, dtype=F32)[None, :, None] * frequency
    cos_a, sin_a, cos_b, sin_b = lax.optimization_barrier(
        (jnp.cos(coarse_angle), jnp.sin(coarse_angle), jnp.cos(fine_angle), jnp.sin(fine_angle))
    )
    sign = jnp.where(jnp.arange(head_dim) < head_dim // 2, -1.0, 1.0)
    cos = cos_a * cos_b - sin_a * sin_b
    sin = (sin_a * cos_b + cos_a * sin_b) * sign
    return cos.reshape(length, head_dim), sin.reshape(length, head_dim)


def rotate(values, cos_table, sin_table):
    half_dim = values.shape[-1] // 2
    first = values[..., :half_dim]
    second = values[..., half_dim:]
    return jnp.concatenate(
        [first * cos_table - second * sin_table, second * cos_table + first * sin_table], axis=-1
    )


def dot_nn(a, b):
    return lax.dot_general(a, b, (((1,), (0,)), ((), ())), preferred_element_type=F32)


def dot_nt(a, b):
    return lax.dot_general(a, b, (((1,), (1,)), ((), ())), preferred_element_type=F32)


def dot_tn(a, b):
    return lax.dot_general(a, b, (((0,), (0,)), ((), ())), preferred_element_type=F32)


def key_chunks(length):
    size = min(512, length)
    return size, length // size


def attn_fwd_kernel(factor, q_ref, k_ref, v_ref, sq_ref, sk_ref, o_ref, of_ref, lse_ref, top_ref, vt_ref):
    length = k_ref.shape[1]
    size, count = key_chunks(length)
    tile, head_dim = q_ref.shape[1:]

    @pl.when(pl.program_id(1) == 0)
    def _():
        vt_ref[...] = v_ref[0].astype(F32).T.astype(BF16)

    q = q_ref[0]
    seg_q = sq_ref[...]

    def step(j, carried):
        total, top, acc = carried
        at = pl.multiple_of(j * size, size)
        scores = dot_nt(k_ref[0, pl.ds(at, size), :], q)
        scores = jnp.where(sk_ref[pl.ds(at, size), :] == seg_q, scores, NEG)
        top = jnp.maximum(top, jnp.max(scores, axis=0, keepdims=True))
        weights = jnp.exp2(scores * factor)
        total = total + jnp.sum(weights, axis=0, keepdims=True)
        acc = acc + dot_nn(vt_ref[:, pl.ds(at, size)], weights.astype(BF16))
        return total, top, acc

    start = (
        jnp.zeros((1, tile), F32),
        jnp.full((1, tile), NEG, F32),
        jnp.zeros((head_dim, tile), F32),
    )
    total, top, acc = lax.fori_loop(0, count, step, start, unroll=count <= 4)
    out = (acc * (1.0 / total)).T
    o_ref[0] = out.astype(BF16)
    of_ref[0] = out
    lse_ref[0] = jnp.log2(total)
    top_ref[0] = top


def attn_bwd_kernel(
    factor, scale, q_ref, k_ref, v_ref, do_ref, of_ref, lse_ref, sq_ref, sk_ref,
    dq_ref, dk_ref, dv_ref, kt_ref, dk_acc, dv_acc,
):
    length = k_ref.shape[1]
    size, count = key_chunks(length)
    tile, head_dim = q_ref.shape[1:]

    @pl.when(pl.program_id(1) == 0)
    def _():
        kt_ref[...] = k_ref[0].astype(F32).T.astype(BF16)
        dk_acc[...] = jnp.zeros_like(dk_acc)
        dv_acc[...] = jnp.zeros_like(dv_acc)

    q = q_ref[0]
    grad = do_ref[0]
    seg_q = sq_ref[...]
    lse = lse_ref[0]
    row_dot = jnp.sum((grad.astype(F32) * of_ref[0]).T, axis=0, keepdims=True)

    def step(j, dq_t):
        at = pl.multiple_of(j * size, size)
        rows = pl.ds(at, size)
        scores = dot_nt(k_ref[0, rows, :], q)
        scores = jnp.where(sk_ref[rows, :] == seg_q, scores, NEG)
        weights = jnp.exp2(scores * factor - lse)
        grad_weights = dot_nt(v_ref[0, rows, :], grad)
        grad_scores = (weights * (grad_weights - row_dot)).astype(BF16)
        dk_acc[rows, :] += dot_nn(grad_scores, q)
        dv_acc[rows, :] += dot_nn(weights.astype(BF16), grad)
        return dq_t + dot_nn(kt_ref[:, rows], grad_scores)

    dq_t = lax.fori_loop(0, count, step, jnp.zeros((head_dim, tile), F32), unroll=count <= 4)
    dq_ref[0] = (dq_t * scale).T.astype(BF16)

    @pl.when(pl.program_id(1) == pl.num_programs(1) - 1)
    def _():
        dk_ref[0] = (dk_acc[...] * scale).astype(BF16)
        dv_ref[0] = dv_acc[...].astype(BF16)


def attention_tile(queries, length):
    return min(queries, 256 if length <= 4096 else 128)


def attention_forward(q_src, kv_src, cols, seg_q, seg_k, head_dim):
    heads, queries = q_src.shape[:2]
    length = kv_src.shape[1]
    tile = attention_tile(queries, length)
    q_col, k_col, v_col = cols
    factor = head_dim**-0.5 * LOG2E
    row = pl.BlockSpec((1, 1, tile), lambda h, i: (h, 0, i))
    block = pl.BlockSpec((1, tile, head_dim), lambda h, i: (h, i, 0))
    return pl.pallas_call(
        functools.partial(attn_fwd_kernel, factor),
        grid=(heads, queries // tile),
        in_specs=[
            pl.BlockSpec((1, tile, head_dim), lambda h, i: (h, i, q_col)),
            pl.BlockSpec((1, length, head_dim), lambda h, i: (h, 0, k_col)),
            pl.BlockSpec((1, length, head_dim), lambda h, i: (h, 0, v_col)),
            pl.BlockSpec((1, tile), lambda h, i: (0, i)),
            pl.BlockSpec((length, 1), lambda h, i: (0, 0)),
        ],
        out_specs=[block, block, row, row],
        out_shape=[
            jax.ShapeDtypeStruct((heads, queries, head_dim), BF16),
            jax.ShapeDtypeStruct((heads, queries, head_dim), F32),
            jax.ShapeDtypeStruct((heads, 1, queries), F32),
            jax.ShapeDtypeStruct((heads, 1, queries), F32),
        ],
        scratch_shapes=[pltpu.VMEM((head_dim, length), BF16)],
        compiler_params=pltpu.CompilerParams(vmem_limit_bytes=VMEM_LIMIT),
        cost_estimate=pl.CostEstimate(
            flops=4 * heads * queries * length * head_dim,
            bytes_accessed=heads * (queries + length) * head_dim * 8,
            transcendentals=heads * queries * length,
        ),
        name="attend",
    )(q_src, kv_src, kv_src, seg_q.reshape(1, -1), seg_k.reshape(-1, 1))


def attention_backward(q_src, kv_src, cols, grad, out_f32, lse, seg_q, seg_k, head_dim):
    heads, queries = q_src.shape[:2]
    length = kv_src.shape[1]
    tile = attention_tile(queries, length)
    q_col, k_col, v_col = cols
    scale = head_dim**-0.5
    row = pl.BlockSpec((1, 1, tile), lambda h, i: (h, 0, i))
    block = pl.BlockSpec((1, tile, head_dim), lambda h, i: (h, i, 0))
    whole = pl.BlockSpec((1, length, head_dim), lambda h, i: (h, 0, 0))
    return pl.pallas_call(
        functools.partial(attn_bwd_kernel, scale * LOG2E, scale),
        grid=(heads, queries // tile),
        in_specs=[
            pl.BlockSpec((1, tile, head_dim), lambda h, i: (h, i, q_col)),
            pl.BlockSpec((1, length, head_dim), lambda h, i: (h, 0, k_col)),
            pl.BlockSpec((1, length, head_dim), lambda h, i: (h, 0, v_col)),
            block,
            block,
            row,
            pl.BlockSpec((1, tile), lambda h, i: (0, i)),
            pl.BlockSpec((length, 1), lambda h, i: (0, 0)),
        ],
        out_specs=[block, whole, whole],
        out_shape=[
            jax.ShapeDtypeStruct((heads, queries, head_dim), BF16),
            jax.ShapeDtypeStruct((heads, length, head_dim), BF16),
            jax.ShapeDtypeStruct((heads, length, head_dim), BF16),
        ],
        scratch_shapes=[
            pltpu.VMEM((head_dim, length), BF16),
            pltpu.VMEM((length, head_dim), F32),
            pltpu.VMEM((length, head_dim), F32),
        ],
        compiler_params=pltpu.CompilerParams(vmem_limit_bytes=VMEM_LIMIT),
        cost_estimate=pl.CostEstimate(
            flops=10 * heads * queries * length * head_dim,
            bytes_accessed=heads * (queries + length) * head_dim * 12,
            transcendentals=heads * queries * length,
        ),
        name="attend_back",
    )(q_src, kv_src, kv_src, grad, out_f32, lse, seg_q.reshape(1, -1), seg_k.reshape(-1, 1))


def expert_step(expert, h_ref, ht_ref, dy_ref, dyt_ref, gate_ref, wg_ref, wu_ref, wd_ref, dg_ref, out_acc, dx_acc):
    width = h_ref.shape[1]
    cols = wg_ref.shape[3]
    w_gate = wg_ref[...].reshape(width, cols)
    w_up = wu_ref[...].reshape(width, cols)
    w_down = wd_ref[...].reshape(width, cols)
    gates = gate_ref[...]
    mine = lax.broadcasted_iota(jnp.int32, gates.shape, 1) == expert
    gate = jnp.sum(jnp.where(mine, gates, 0.0), axis=1, keepdims=True)
    a_gate = dot_nn(h_ref[...], w_gate)
    a_up = dot_nn(h_ref[...], w_up)
    raw = dot_nn(dy_ref[...], w_down)
    sigma = 1.0 / (1.0 + jnp.exp2(a_gate * -LOG2E))
    swish = a_gate * sigma
    act = swish * a_up
    dg_ref[0] += jnp.sum(raw * act, axis=1, keepdims=True)
    gated = (gate * act).astype(BF16)
    d_act = gate * raw
    d_gate = (d_act * a_up * (sigma + swish * (1.0 - sigma))).astype(BF16)
    d_up = (d_act * swish).astype(BF16)
    out_acc[...] += dot_nt(gated, w_down)
    dx_acc[...] += dot_nt(d_gate, w_gate) + dot_nt(d_up, w_up)
    for part, (left, right) in enumerate([(ht_ref, d_gate), (ht_ref, d_up), (dyt_ref, gated)]):
        yield part, dot_nn(left[...], right).astype(BF16)


def expert_kernel(more, *refs):
    h_ref, ht_ref, dy_ref, dyt_ref, gate_ref, wg_ref, wu_ref, wd_ref = refs[:8]
    out_ref, dx_ref, dg_ref, gr_ref, out_acc, dx_acc = refs[-6:]
    step, last = pl.program_id(0), pl.num_programs(0) - 1
    parts, _, part_rows, cols = wg_ref.shape
    chunks = (last + 1) // gate_ref.shape[1]

    @pl.when(step == 0)
    def _():
        if more:
            out0_ref, dx0_ref = refs[8:10]
            out_acc[...] = out0_ref[...].astype(F32)
            dx_acc[...] = dx0_ref[...].astype(F32)
        else:
            out_acc[...] = jnp.zeros_like(out_acc)
            dx_acc[...] = jnp.zeros_like(dx_acc)

    @pl.when(step % chunks == 0)
    def _():
        dg_ref[...] = jnp.zeros_like(dg_ref)

    for part, made in expert_step(
        step // chunks, h_ref, ht_ref, dy_ref, dyt_ref, gate_ref, wg_ref, wu_ref, wd_ref, dg_ref, out_acc, dx_acc
    ):
        gr_ref[:, part, 0] = made.reshape(parts, part_rows, cols)

    @pl.when(step == last)
    def _():
        out_ref[...] = out_acc[...].astype(BF16)
        dx_ref[...] = dx_acc[...].astype(BF16)


def experts(hidden, hidden_t, grad, grad_t, gates, weights, before=()):
    tokens, width = hidden.shape
    parts, count, part_rows, units = weights.shape
    units = units // 3
    cols = min(256, units)
    chunks = units // cols
    once = pl.Buffered(1)
    whole = pl.BlockSpec((tokens, width), lambda s: (0, 0), pipeline_mode=once)
    whole_t = pl.BlockSpec((width, tokens), lambda s: (0, 0), pipeline_mode=once)
    result = pl.BlockSpec((tokens, width), lambda s: (0, 0))

    def weight(kind):
        return pl.BlockSpec(
            (parts, 1, part_rows, cols), lambda s: (0, s // chunks, 0, kind * chunks + s % chunks)
        )

    return pl.pallas_call(
        functools.partial(expert_kernel, bool(before)),
        grid=(count * chunks,),
        in_specs=[
            whole,
            whole_t,
            whole,
            whole_t,
            pl.BlockSpec(gates.shape, lambda s: (0, 0), pipeline_mode=once),
            weight(0),
            weight(1),
            weight(2),
            *[whole for _ in before],
        ],
        out_specs=[
            result,
            result,
            pl.BlockSpec((1, tokens, 1), lambda s: (s // chunks, 0, 0)),
            pl.BlockSpec((parts, 3, 1, part_rows, cols), lambda s: (0, 0, s // chunks, 0, s % chunks)),
        ],
        out_shape=[
            jax.ShapeDtypeStruct((tokens, width), BF16),
            jax.ShapeDtypeStruct((tokens, width), BF16),
            jax.ShapeDtypeStruct((count, tokens, 1), F32),
            jax.ShapeDtypeStruct((parts, 3, count, part_rows, units), BF16),
        ],
        scratch_shapes=[
            pltpu.VMEM((tokens, width), F32),
            pltpu.VMEM((tokens, width), F32),
        ],
        compiler_params=pltpu.CompilerParams(vmem_limit_bytes=VMEM_LIMIT),
        cost_estimate=pl.CostEstimate(
            flops=18 * count * tokens * width * units,
            bytes_accessed=12 * count * width * units,
            transcendentals=count * tokens * units,
        ),
        name="experts",
    )(hidden, hidden_t, grad, grad_t, gates, weights, weights, weights, *before)


def expert_mixed_kernel(
    h_ref, ht_ref, dy_ref, dyt_ref, gate_ref, wg_ref, wu_ref, wd_ref, out0_ref, dx0_ref,
    out_ref, dx_ref, dg_ref, gr_ref, keep_x, give_x, keep_y, give_y,
    out_acc, dx_acc, made_ref, got_ref, send, recv, free,
):
    step, last = pl.program_id(0), pl.num_programs(0) - 1
    parts, _, part_rows, cols = wg_ref.shape
    chunks = (last + 1) // 2
    b, y, core = lax.axis_index("batch"), lax.axis_index("y"), lax.axis_index("core")
    near = {"core": 1 - core}
    slot, before = lax.rem(step, 2), lax.rem(step + 1, 2)

    @pl.when(step == 0)
    def _():
        barrier = pltpu.get_barrier_semaphore()
        pl.semaphore_signal(barrier, inc=1, device_id=near, device_id_type=MESH)
        pl.semaphore_wait(barrier, 1)
        out_acc[...] = out0_ref[...].astype(F32)
        dx_acc[...] = dx0_ref[...].astype(F32)

    def hand_over(at):
        return pltpu.make_async_remote_copy(
            src_ref=made_ref.at[at, 1 - core],
            dst_ref=got_ref.at[at],
            send_sem=send.at[at],
            recv_sem=recv.at[at],
            device_id=near,
            device_id_type=MESH,
        )

    @pl.when(step % chunks == 0)
    def _():
        dg_ref[...] = jnp.zeros_like(dg_ref)

    refs = (h_ref, ht_ref, dy_ref, dyt_ref, gate_ref, wg_ref, wu_ref, wd_ref, dg_ref, out_acc, dx_acc)

    @pl.when(step < chunks)
    def _():
        for part, made in expert_step(1, *refs):
            made = made.reshape(parts // 2, 2, part_rows, cols)
            made_ref[slot, 0, :, part] = made[:, 0]
            made_ref[slot, 1, :, part] = made[:, 1]

        @pl.when(step >= 2)
        def _():
            pl.semaphore_wait(free, 1)

        hand_over(slot).start()

    @pl.when(step >= chunks)
    def _():
        for part, made in expert_step(0, *refs):
            gr_ref[:, part, 0] = made.reshape(parts, part_rows, cols)

    def total(other_b, other_y):
        at = (b + other_b) % 2 * 2 + (y + other_y) % 2
        both = made_ref[before, core, at].astype(F32) + got_ref[before, at].astype(F32)
        return both.astype(BF16)

    @pl.when((step > 0) & (step <= chunks))
    def _():
        hand_over(before).wait()

        @pl.when(step <= chunks // 2)
        def _():
            for other in range(2):
                keep_x[other] = total(0, other)
                give_x[other] = total(1, other)

        @pl.when(step > chunks // 2)
        def _():
            for other in range(2):
                keep_y[other] = total(other, 0)
                give_y[other] = total(other, 1)

        @pl.when(step < chunks - 1)
        def _():
            pl.semaphore_signal(free, inc=1, device_id=near, device_id_type=MESH)

    @pl.when(step == last)
    def _():
        out_ref[...] = out_acc[...].astype(BF16)
        dx_ref[...] = dx_acc[...].astype(BF16)


def experts_mixed(hidden, hidden_t, grad, grad_t, gates, weights, before, collective_id):
    tokens, width = hidden.shape
    parts, _, part_rows, units = weights.shape
    units = units // 3
    cols = min(256, units // 2)
    chunks = units // cols
    half = chunks // 2
    once = pl.Buffered(1)
    whole = pl.BlockSpec((tokens, width), lambda s: (0, 0), pipeline_mode=once)
    whole_t = pl.BlockSpec((width, tokens), lambda s: (0, 0), pipeline_mode=once)
    result = pl.BlockSpec((tokens, width), lambda s: (0, 0))

    def weight(kind):
        return pl.BlockSpec(
            (parts, 1, part_rows, cols), lambda s: (0, 1 - s // chunks, 0, kind * chunks + s % chunks)
        )

    def written(first):
        return pl.BlockSpec(
            (2, 3, part_rows, cols), lambda s: (0, 0, 0, jnp.clip(s - 1 - first, 0, half - 1))
        )

    return pl.pallas_call(
        expert_mixed_kernel,
        grid=(2 * chunks,),
        in_specs=[
            whole,
            whole_t,
            whole,
            whole_t,
            pl.BlockSpec(gates.shape, lambda s: (0, 0), pipeline_mode=once),
            weight(0),
            weight(1),
            weight(2),
            whole,
            whole,
        ],
        out_specs=[
            result,
            result,
            pl.BlockSpec((1, tokens, 1), lambda s: (1 - s // chunks, 0, 0)),
            pl.BlockSpec(
                (parts, 3, 1, part_rows, cols), lambda s: (0, 0, 0, 0, jnp.maximum(s - chunks, 0))
            ),
            written(0),
            written(0),
            written(half),
            written(half),
        ],
        out_shape=[
            jax.ShapeDtypeStruct((tokens, width), BF16),
            jax.ShapeDtypeStruct((tokens, width), BF16),
            jax.ShapeDtypeStruct((2, tokens, 1), F32),
            jax.ShapeDtypeStruct((parts, 3, 1, part_rows, units), BF16),
            *[jax.ShapeDtypeStruct((2, 3, part_rows, units // 2), BF16)] * 4,
        ],
        scratch_shapes=[
            pltpu.VMEM((tokens, width), F32),
            pltpu.VMEM((tokens, width), F32),
            pltpu.VMEM((2, 2, parts // 2, 3, part_rows, cols), BF16),
            pltpu.VMEM((2, parts // 2, 3, part_rows, cols), BF16),
            pltpu.SemaphoreType.DMA((2,)),
            pltpu.SemaphoreType.DMA((2,)),
            pltpu.SemaphoreType.REGULAR,
        ],
        compiler_params=pltpu.CompilerParams(
            vmem_limit_bytes=VMEM_LIMIT, collective_id=collective_id, has_side_effects=True
        ),
        cost_estimate=pl.CostEstimate(
            flops=36 * tokens * width * units,
            bytes_accessed=24 * width * units,
            transcendentals=2 * tokens * units,
        ),
        name="experts_mixed",
    )(hidden, hidden_t, grad, grad_t, gates, weights, weights, weights, *before)


def finish_traded_kernel(kx_ref, gx_ref, lx_ref, ky_ref, gy_ref, ly_ref, a_ref, b_ref, gate_up_ref, down_ref):
    half = lx_ref.shape[2]
    units = down_ref.shape[2]
    for at, (kept, got, last) in ((0, (kx_ref, gx_ref, lx_ref)), (half, (ky_ref, gy_ref, ly_ref))):
        for part, (target, first) in enumerate(((gate_up_ref, 0), (gate_up_ref, units), (down_ref, 0))):
            total = kept[0, part].astype(F32) + got[0, part].astype(F32) + last[part].astype(F32)
            target[0, :, first + at : first + at + half] = total


def finish_traded(x, y, at, before):
    _, _, rows, half = x[0].shape
    tile = min(128, rows)
    total, _, units = before[1].shape
    pair = pl.BlockSpec((1, 3, tile, half), lambda r: (0, 0, r, 0))
    single = pl.BlockSpec((3, tile, half), lambda r: (0, r, 0))
    return pl.pallas_call(
        finish_traded_kernel,
        grid=(rows // tile,),
        in_specs=[*[pair, pair, single] * 2, *[pl.BlockSpec(memory_space=pl.ANY)] * 2],
        out_specs=[
            pl.BlockSpec((1, tile, 2 * units), lambda r: (at, r, 0)),
            pl.BlockSpec((1, tile, units), lambda r: (at, r, 0)),
        ],
        out_shape=[jax.ShapeDtypeStruct(array.shape, F32) for array in before],
        input_output_aliases={6: 0, 7: 1},
        compiler_params=pltpu.CompilerParams(vmem_limit_bytes=VMEM_LIMIT),
        name="finish_traded",
    )(*x, *y, *before)


def finish_experts_kernel(sums_ref, *refs):
    gate_up_ref, down_ref = refs[-2:]
    units = down_ref.shape[2]
    gate_up_ref[0, :, :units] = sums_ref[0, 0].astype(F32)
    gate_up_ref[0, :, units:] = sums_ref[1, 0].astype(F32)
    down_ref[0] = sums_ref[2, 0].astype(F32)


def finish_experts(sums, at, total, before=()):
    _, count, rows, units = sums.shape
    tile = min(128, rows)
    return pl.pallas_call(
        finish_experts_kernel,
        grid=(count, rows // tile),
        in_specs=[
            pl.BlockSpec((3, 1, tile, units), lambda e, r: (0, e, r, 0)),
            *[pl.BlockSpec(memory_space=pl.ANY) for _ in before],
        ],
        out_specs=[
            pl.BlockSpec((1, tile, 2 * units), lambda e, r: (at + e, r, 0)),
            pl.BlockSpec((1, tile, units), lambda e, r: (at + e, r, 0)),
        ],
        out_shape=[
            jax.ShapeDtypeStruct((total, rows, 2 * units), F32),
            jax.ShapeDtypeStruct((total, rows, units), F32),
        ],
        input_output_aliases={1 + i: i for i in range(len(before))},
        compiler_params=pltpu.CompilerParams(vmem_limit_bytes=VMEM_LIMIT),
        name="finish_experts",
    )(sums, *before)


def turn(values, cos, sin):
    return values * cos + pltpu.roll(values, values.shape[1] // 2, 1) * sin


def project_kernel(
    tok_ref, gain_ref, w_ref, cos_ref, sin_ref, gains_ref, hidden_ref, qkv_ref, raw_ref
):
    head_dim = cos_ref.shape[1]
    values = tok_ref[...].astype(F32)
    hidden = (values * rms_scale(values) * gain_ref[...]).astype(BF16)
    hidden_ref[...] = hidden
    projected = dot_nn(hidden, w_ref[...])
    raw_ref[...] = projected[:, : 2 * head_dim]
    for part in range(2):
        at = slice(part * head_dim, (part + 1) * head_dim)
        raw = projected[:, at]
        normed = raw * rms_scale(raw) * gains_ref[part : part + 1, :]
        qkv_ref[:, at] = turn(normed, cos_ref[...], sin_ref[...]).astype(BF16)
    qkv_ref[:, 2 * head_dim :] = projected[:, 2 * head_dim :].astype(BF16)


def project(toks, gain, weights, cos, sin, gains):
    length, width = toks.shape
    head_dim = cos.shape[1]
    tile = min(256, length)

    def rows(columns):
        return pl.BlockSpec((tile, columns), lambda i: (i, 0))

    def fixed(shape):
        return pl.BlockSpec(shape, lambda i: (0, 0))

    return pl.pallas_call(
        project_kernel,
        grid=(length // tile,),
        in_specs=[
            rows(width),
            fixed((1, width)),
            fixed(weights.shape),
            rows(head_dim),
            rows(head_dim),
            fixed(gains.shape),
        ],
        out_specs=[rows(width), rows(3 * head_dim), rows(2 * head_dim)],
        out_shape=[
            jax.ShapeDtypeStruct((length, width), BF16),
            jax.ShapeDtypeStruct((length, 3 * head_dim), BF16),
            jax.ShapeDtypeStruct((length, 2 * head_dim), F32),
        ],
        compiler_params=pltpu.CompilerParams(vmem_limit_bytes=VMEM_LIMIT),
        name="project",
    )(toks, gain, weights, cos, sin, gains)


def project_back_kernel(
    factor, scale, q_ref, k_ref, v_ref, do_ref, of_ref, lse_ref, sq_ref, sk_ref,
    raw_q_ref, raw_k_ref, cos_q_ref, sin_q_ref, cos_ref, sin_ref, gains_ref,
    dp_ref, dgain_ref, kt_ref, dk_acc, dv_acc,
):
    length, head_dim = k_ref.shape
    size, count = key_chunks(length)
    tile = q_ref.shape[0]
    step_at = pl.program_id(0)

    @pl.when(step_at == 0)
    def _():
        kt_ref[...] = k_ref[...].astype(F32).T.astype(BF16)
        dk_acc[...] = jnp.zeros_like(dk_acc)
        dv_acc[...] = jnp.zeros_like(dv_acc)
        dgain_ref[...] = jnp.zeros_like(dgain_ref)

    def to_raw(part, grad, raw, cos, sin):
        grad = turn(grad.astype(BF16).astype(F32), cos, -sin)
        raw_scale = rms_scale(raw)
        dgain_ref[part : part + 1, :] += jnp.sum(grad * (raw * raw_scale), axis=0, keepdims=True)
        return norm_back(grad * gains_ref[part : part + 1, :], raw, raw_scale).astype(BF16)

    q = q_ref[...]
    grad = do_ref[...]
    seg_q = sq_ref[...]
    lse = lse_ref[0]
    row_dot = jnp.sum((grad.astype(F32) * of_ref[0]).T, axis=0, keepdims=True)
    dq_t = jnp.zeros((head_dim, tile), F32)
    for j in range(count):
        rows = slice(j * size, (j + 1) * size)
        scores = dot_nt(k_ref[rows, :], q)
        scores = jnp.where(sk_ref[rows, :] == seg_q, scores, NEG)
        weights = jnp.exp2(scores * factor - lse)
        grad_weights = dot_nt(v_ref[rows, :], grad)
        grad_scores = (weights * (grad_weights - row_dot)).astype(BF16)
        dk_acc[rows, :] += dot_nn(grad_scores, q)
        dv_acc[rows, :] += dot_nn(weights.astype(BF16), grad)
        dq_t = dq_t + dot_nn(kt_ref[:, rows], grad_scores)
    own = pl.ds(pl.multiple_of(step_at * tile, tile), tile)
    dp_ref[own, :head_dim] = to_raw(
        0, (dq_t * scale).T, raw_q_ref[...], cos_q_ref[...], sin_q_ref[...]
    )

    @pl.when(step_at == pl.num_programs(0) - 1)
    def _():
        dp_ref[:, head_dim : 2 * head_dim] = to_raw(
            1, dk_acc[...] * scale, raw_k_ref[...], cos_ref[...], sin_ref[...]
        )
        dp_ref[:, 2 * head_dim :] = dv_acc[...].astype(BF16)


def project_back(qkv, grad, out_f32, lse, segments, raw, cos, sin, gains):
    length, head_dim = grad.shape
    tile = min(256, length)

    def rows(column):
        return pl.BlockSpec((tile, head_dim), lambda i: (i, column))

    def whole(column):
        return pl.BlockSpec((length, head_dim), lambda i: (0, column))

    return pl.pallas_call(
        functools.partial(project_back_kernel, head_dim**-0.5 * LOG2E, head_dim**-0.5),
        grid=(length // tile,),
        in_specs=[
            rows(0),
            whole(1),
            whole(2),
            rows(0),
            pl.BlockSpec((1, tile, head_dim), lambda i: (0, i, 0)),
            pl.BlockSpec((1, 1, tile), lambda i: (0, 0, i)),
            pl.BlockSpec((1, tile), lambda i: (0, i)),
            pl.BlockSpec((length, 1), lambda i: (0, 0)),
            rows(0),
            whole(1),
            rows(0),
            rows(0),
            whole(0),
            whole(0),
            pl.BlockSpec(gains.shape, lambda i: (0, 0)),
        ],
        out_specs=[
            pl.BlockSpec((length, 3 * head_dim), lambda i: (0, 0)),
            pl.BlockSpec((2, head_dim), lambda i: (0, 0)),
        ],
        out_shape=[
            jax.ShapeDtypeStruct((length, 3 * head_dim), BF16),
            jax.ShapeDtypeStruct((2, head_dim), F32),
        ],
        scratch_shapes=[
            pltpu.VMEM((head_dim, length), BF16),
            pltpu.VMEM((length, head_dim), F32),
            pltpu.VMEM((length, head_dim), F32),
        ],
        compiler_params=pltpu.CompilerParams(vmem_limit_bytes=VMEM_LIMIT),
        cost_estimate=pl.CostEstimate(
            flops=10 * length * length * head_dim,
            bytes_accessed=length * head_dim * 40,
            transcendentals=length * length,
        ),
        name="project_back",
    )(
        qkv, qkv, qkv, grad, out_f32, lse, segments.reshape(1, -1), segments.reshape(-1, 1),
        raw, raw, cos, sin, cos, sin, gains,
    )


def hidden_back_kernel(grads_ref, own_ref, near_ref, far_ref, cross_ref, hidden_ref, out_ref, gain_ref):
    uly = grads_ref.shape[0]
    u = lax.axis_index(ULY)
    near = u + 1 - 2 * lax.rem(u, 2)
    total = dot_nt(grads_ref[u], own_ref[...])
    total = total + dot_nt(grads_ref[near], near_ref[...])
    total = total + dot_nt(grads_ref[lax.rem(u + 2, uly)], far_ref[...])
    total = total + dot_nt(grads_ref[lax.rem(near + 2, uly)], cross_ref[...])
    out_ref[...] = total.astype(BF16).reshape(out_ref.shape)
    hidden = hidden_ref[...].reshape(total.shape).astype(F32)
    gain_ref[...] = jnp.sum(total * hidden, axis=0, keepdims=True)


def hidden_back(grads, own, near, far, cross, hidden):
    uly, tokens, columns = grads.shape
    blk, _, rows, width = hidden.shape
    tile = min(512, width)
    weights = pl.BlockSpec((tile, columns), lambda n: (n, 0))
    return pl.pallas_call(
        hidden_back_kernel,
        grid=(width // tile,),
        in_specs=[
            pl.BlockSpec(grads.shape, lambda n: (0, 0, 0)),
            *[weights] * 4,
            pl.BlockSpec((blk, 1, rows, tile), lambda n: (0, lax.axis_index(ULY), 0, n)),
        ],
        out_specs=[
            pl.BlockSpec((blk, rows, tile), lambda n: (0, 0, n)),
            pl.BlockSpec((1, tile), lambda n: (0, n)),
        ],
        out_shape=[
            jax.ShapeDtypeStruct((blk, rows, width), BF16),
            jax.ShapeDtypeStruct((1, width), F32),
        ],
        compiler_params=pltpu.CompilerParams(vmem_limit_bytes=VMEM_LIMIT),
        name="hidden_back",
    )(grads, own, near, far, cross, hidden)


def merge_heads_kernel(parts_ref, out_ref):
    blk, uly, _, columns = parts_ref.shape
    head_dim = columns // 3
    heads = blk * uly
    for z in range(blk):
        for u in range(uly):
            head = parts_ref[z, u].astype(F32)
            for part in range(3):
                at = (part * heads + u * blk + z) * head_dim
                out_ref[:, at : at + head_dim] = head[:, part * head_dim : (part + 1) * head_dim]


def merge_heads(parts):
    blk, uly, rows, columns = parts.shape
    return pl.pallas_call(
        merge_heads_kernel,
        out_shape=jax.ShapeDtypeStruct((rows, blk * uly * columns), F32),
        compiler_params=pltpu.CompilerParams(vmem_limit_bytes=VMEM_LIMIT),
        name="merge_heads",
    )(parts)


def swap(values, axis):
    return lax.all_to_all(values, axis, split_axis=0, concat_axis=0, tiled=True)


def sum_scatter(values, axis):
    count = spread(axis) if isinstance(axis, tuple) else lax.axis_size(axis)
    rows, width = values.shape
    parts = swap(values.astype(BF16).reshape(count, rows // count, width), axis)
    return jnp.sum(parts.astype(F32), axis=0)


def place(axes, index):
    found = {}
    for axis in reversed(axes):
        size = lax.axis_size(axis)
        found[axis] = lax.rem(index, size)
        index = index // size
    return found


def spread(axes):
    return math.prod(lax.axis_size(axis) for axis in axes)


def each(count, body):
    if count <= 4:
        for step in range(1, count):
            body(step)
    else:

        def looped(step, carried):
            body(step)
            return carried

        lax.fori_loop(1, count, looped, 0)


def ahead(index, step, size):
    return lax.rem(index + step, size)


def exchange(items, collective_id, after=()):
    count = len(items)
    sizes = [spread(axes) for _, axes, _ in items]
    groups = list(dict.fromkeys(axes for _, axes, _ in items))
    bases = [sum(2 * size for size in sizes[:i]) for i in range(count)]

    def kernel(*refs):
        ins = refs[:count]
        outs = refs[count + len(after) : 2 * count + len(after)]
        send, recv, local = refs[-3:]
        barrier = pltpu.get_barrier_semaphore()
        for axes in groups:
            size, me = spread(axes), lax.axis_index(axes)

            def greet(step, axes=axes, size=size, me=me):
                pl.semaphore_signal(
                    barrier, inc=1, device_id=place(axes, ahead(me, step, size)), device_id_type=MESH
                )

            each(size, greet)
        pl.semaphore_wait(barrier, sum(spread(axes) - 1 for axes in groups))

        def block(i, peer):
            if items[i][2] == "swap":
                return ins[i].at[peer]
            return ins[i].at[:, peer] if items[i][2] == "swap1" else ins[i]

        def remote(i, step):
            _, axes, kind = items[i]
            me = lax.axis_index(axes)
            if kind == "trade":
                return pltpu.make_async_remote_copy(
                    src_ref=ins[i],
                    dst_ref=outs[i],
                    send_sem=send.at[bases[i] + 1],
                    recv_sem=recv.at[bases[i] + 1],
                    device_id=place(axes, 1 - me),
                    device_id_type=MESH,
                )
            if kind == "relay":
                far, near = lax.rem(me + 2, 4), me + 1 - 2 * lax.rem(me, 2)
                held = far if step == 3 else me
                return pltpu.make_async_remote_copy(
                    src_ref=outs[i].at[far] if step == 3 else ins[i],
                    dst_ref=outs[i].at[held],
                    send_sem=send.at[bases[i] + step],
                    recv_sem=recv.at[bases[i] + step],
                    device_id=place(axes, far if step == 1 else near),
                    device_id_type=MESH,
                )
            peer = ahead(me, step, sizes[i])
            return pltpu.make_async_remote_copy(
                src_ref=block(i, peer),
                dst_ref=outs[i].at[me],
                send_sem=send.at[bases[i] + step],
                recv_sem=recv.at[bases[i] + step],
                device_id=place(axes, peer),
                device_id_type=MESH,
            )

        def own(i):
            _, axes, kind = items[i]
            me = lax.axis_index(axes)
            return pltpu.make_async_copy(
                block(i, me), outs[i].at[me], local.at[i]
            )

        def hop(i, up, hops):
            (axis,) = items[i][1]
            me, size = lax.axis_index(axis), sizes[i]
            way = 1 if up else -1
            held, to = me - way * hops, me + way
            exists = (held >= 0) & (held < size) & (to >= 0) & (to < size)
            held, to = jnp.clip(held, 0, size - 1), jnp.clip(to, 0, size - 1)
            sem = bases[i] + (size if up else 0) + hops
            copy = pltpu.make_async_remote_copy(
                src_ref=outs[i].at[held] if hops else ins[i],
                dst_ref=outs[i].at[held],
                send_sem=send.at[sem],
                recv_sem=recv.at[sem],
                device_id={axis: to},
                device_id_type=MESH,
            )
            return exists, copy

        def arrival(i, up, hops):
            (axis,) = items[i][1]
            me, size = lax.axis_index(axis), sizes[i]
            way = 1 if up else -1
            held, sender = me - way * (hops + 1), me - way
            exists = (held >= 0) & (held < size)
            held, sender = jnp.clip(held, 0, size - 1), jnp.clip(sender, 0, size - 1)
            sem = bases[i] + (size if up else 0) + hops
            copy = pltpu.make_async_remote_copy(
                src_ref=ins[i],
                dst_ref=outs[i].at[held],
                send_sem=send.at[sem],
                recv_sem=recv.at[sem],
                device_id={axis: sender},
                device_id_type=MESH,
            )
            return exists, copy

        def kinds(*names):
            return [i for i in range(count) if items[i][2] in names]

        def when(pair, act):
            exists, copy = pair
            pl.when(exists)(lambda: act(copy))

        ways = (True, False)
        for i in kinds("line"):
            for up in ways:
                when(hop(i, up, 0), lambda copy: copy.start())
        for i in kinds("gather", "swap", "swap1", "relay", "trade"):
            each(3 if items[i][2] == "relay" else sizes[i], lambda step, i=i: remote(i, step).start())
        for i in kinds("gather", "swap", "swap1", "relay", "line"):
            own(i).start()
        for i in kinds("line"):
            for hops in range(1, sizes[i]):
                for up in ways:
                    when(arrival(i, up, hops - 1), lambda copy: copy.wait_recv())
                    if hops < sizes[i] - 1:
                        when(hop(i, up, hops), lambda copy: copy.start())
        for i in kinds("relay"):
            remote(i, 1).wait_recv()
            remote(i, 3).start()
            remote(i, 1).wait_send()
            for step in (2, 3):
                remote(i, step).wait()
        for i in kinds("gather", "swap", "swap1", "trade"):
            each(sizes[i], lambda step, i=i: remote(i, step).wait())
        for i in kinds("line"):
            for hops in range(sizes[i] - 1):
                for up in ways:
                    when(hop(i, up, hops), lambda copy: copy.wait_send())
        for i in kinds("gather", "swap", "swap1", "relay", "line"):
            own(i).wait()


    def shape_of(size, array, kind):
        if kind == "trade":
            return array.shape
        dropped = {"swap": 0, "swap1": 1}.get(kind)
        return (size, *(extent for at, extent in enumerate(array.shape) if at != dropped))

    shapes = [shape_of(size, array, kind) for size, (array, _, kind) in zip(sizes, items)]
    anywhere = pl.BlockSpec(memory_space=pl.ANY)
    return pl.pallas_call(
        kernel,
        in_specs=[anywhere] * (count + len(after)),
        out_specs=[anywhere] * count,
        out_shape=[jax.ShapeDtypeStruct(shape, item[0].dtype) for shape, item in zip(shapes, items)],
        scratch_shapes=[
            pltpu.SemaphoreType.DMA((2 * sum(sizes),)),
            pltpu.SemaphoreType.DMA((2 * sum(sizes),)),
            pltpu.SemaphoreType.DMA((count,)),
        ],
        compiler_params=pltpu.CompilerParams(collective_id=collective_id, has_side_effects=True),
        name="exchange",
    )(*[item[0] for item in items], *after)


def startup_kernel(
    head_ref, extra_ref, tok_ref, heads_ref, extras_ref, toks_ref,
    head_send, head_recv, extra_send, extra_recv,
    z_send, z_recv, ay_send, ay_recv, by_send, by_recv, c_send, c_recv, local,
):
    blk, uly = lax.axis_size("blk"), spread(ULY)
    total = spread(ALL)
    z, u, me = lax.axis_index("blk"), lax.axis_index(ULY), lax.axis_index(ALL)
    far = lax.rem(u + 2, uly)
    near = u + 1 - 2 * lax.rem(u, 2)
    half = tok_ref.shape[0] // 2
    parts = (pl.ds(0, half), pl.ds(half, half))

    barrier = pltpu.get_barrier_semaphore()

    def greet(step):
        pl.semaphore_signal(
            barrier, inc=1, device_id=place(ALL, ahead(me, step, total)), device_id_type=MESH
        )

    each(total, greet)
    pl.semaphore_wait(barrier, total - 1)

    def send(src, dst, sent, got, to):
        return pltpu.make_async_remote_copy(
            src_ref=src, dst_ref=dst, send_sem=sent, recv_sem=got, device_id=to, device_id_type=MESH
        )

    def block(step, other, part):
        at = toks_ref.at[ahead(z, step, blk), far if other else u, parts[part]]
        return (tok_ref.at[parts[part]] if step == 0 and not other else at), at

    streams = ((0, 0), (0, 1), (1, 1))

    def hop(stream, up, hops):
        other, part = streams[stream]
        way = 1 if up else -1
        held, to = z - way * hops, z + way
        exists = (held >= 0) & (held < blk) & (to >= 0) & (to < blk)
        held, to = jnp.clip(held, 0, blk - 1), jnp.clip(to, 0, blk - 1)
        at = toks_ref.at[held, far if other else u, parts[part]]
        src = tok_ref.at[parts[part]] if hops == 0 and not other else at
        sem = (2 * stream + up) * blk + hops
        return exists, send(src, at, z_send.at[sem], z_recv.at[sem], {"blk": to})

    def arrival(stream, up, hops):
        other, part = streams[stream]
        way = 1 if up else -1
        held, sender = z - way * (hops + 1), z - way
        exists = (held >= 0) & (held < blk)
        held, sender = jnp.clip(held, 0, blk - 1), jnp.clip(sender, 0, blk - 1)
        at = toks_ref.at[held, far if other else u, parts[part]]
        sem = (2 * stream + up) * blk + hops
        return exists, send(tok_ref.at[parts[part]], at, z_send.at[sem], z_recv.at[sem], {"blk": sender})

    def when(pair, act):
        exists, copy = pair
        pl.when(exists)(lambda: act(copy))

    def a_y(step):
        return send(*block(step, 0, 0), ay_send.at[step], ay_recv.at[step], place(ULY, far))

    def b_y():
        return send(*block(0, 0, 1), by_send.at[0], by_recv.at[0], place(ULY, far))

    def to_near(step, other, part):
        sem = 4 * step + 2 * other + part
        return send(*block(step, other, part), c_send.at[sem], c_recv.at[sem], place(ULY, near))

    def head(step):
        to = place(ALL, ahead(me, step, total))
        src = head_ref.at[(to["y"] * lax.axis_size("core") + to["core"]) * blk + to["blk"]]
        return send(src, heads_ref.at[me], head_send.at[step], head_recv.at[step], to)

    def extra(step):
        to = place(ALL, ahead(me, step, total))
        return send(extra_ref, extras_ref.at[me], extra_send.at[step], extra_recv.at[step], to)

    own = [
        pltpu.make_async_copy(tok_ref, toks_ref.at[z, u], local.at[0]),
        pltpu.make_async_copy(head_ref.at[u * blk + z], heads_ref.at[me], local.at[1]),
        pltpu.make_async_copy(extra_ref, extras_ref.at[me], local.at[2]),
    ]

    ways = (1, 0)
    b_y().start()
    for stream in range(2):
        for up in ways:
            when(hop(stream, up, 0), lambda copy: copy.start())
    a_y(0).start()
    to_near(0, 0, 0).start()
    to_near(0, 0, 1).start()

    def start_head(step):
        extra(step).start()
        head(step).start()

    each(total, start_head)
    for copy in own:
        copy.start()
    b_y().wait_recv()
    for up in ways:
        when(hop(2, up, 0), lambda copy: copy.start())
    to_near(0, 1, 1).start()
    for hops in range(1, blk):
        for stream, (other, part) in enumerate(streams):
            for up in ways:
                exists, copy = arrival(stream, up, hops - 1)
                step = blk - hops if up else hops

                @pl.when(exists)
                def _(copy=copy, stream=stream, other=other, part=part, up=up, step=step, hops=hops):
                    copy.wait_recv()
                    if hops < blk - 1:
                        when(hop(stream, up, hops), lambda copy: copy.start())
                    if stream == 0:
                        a_y(step).start()
                    to_near(step, other, part).start()

    for step in [0, *reversed(range(1, blk))]:
        a_y(step).wait_recv()
        to_near(step, 1, 0).start()
    for step in range(blk):
        for other in range(2):
            for part in range(2):
                to_near(step, other, part).wait_recv()

    def wait_head(step):
        extra(step).wait()
        head(step).wait()

    each(total, wait_head)
    for copy in own:
        copy.wait()
    b_y().wait_send()
    for hops in range(blk - 1):
        for stream in range(3):
            for up in ways:
                when(hop(stream, up, hops), lambda copy: copy.wait_send())
    for step in range(blk):
        a_y(step).wait_send()
        for other in range(2):
            for part in range(2):
                to_near(step, other, part).wait_send()


def startup(heads, extra, tok, collective_id):
    blk, uly, total = lax.axis_size("blk"), spread(ULY), spread(ALL)
    anywhere = pl.BlockSpec(memory_space=pl.ANY)
    dma = pltpu.SemaphoreType.DMA
    return pl.pallas_call(
        startup_kernel,
        in_specs=[anywhere] * 3,
        out_specs=[anywhere] * 3,
        out_shape=[
            jax.ShapeDtypeStruct((total, *heads.shape[1:]), BF16),
            jax.ShapeDtypeStruct((total, *extra.shape), BF16),
            jax.ShapeDtypeStruct((blk, uly, *tok.shape), BF16),
        ],
        scratch_shapes=[
            *[dma((total,))] * 4,
            *[dma((6 * blk,))] * 2,
            *[dma((blk,))] * 2,
            *[dma((1,))] * 2,
            *[dma((4 * blk,))] * 2,
            dma((3,)),
        ],
        compiler_params=pltpu.CompilerParams(collective_id=collective_id, has_side_effects=True),
        name="startup",
    )(heads, extra, tok)


def per_device_general(
    tokens, segments, routes, w_qkv, w_out, attn_gain, ffn_gain, qk_gain, router, w_gate_up, w_down, cotangent
):
    own_tokens = tokens[0]
    own_grad = cotangent[0]
    count_tok, width = own_tokens.shape
    head_dim = qk_gain.shape[1]
    heads = width // head_dim
    uly, blk, batch = spread(ULY), lax.axis_size("blk"), lax.axis_size("batch")
    blk_at, uly_at = lax.axis_index("blk"), lax.axis_index(ULY)
    group = batch * blk
    local_heads = heads // uly
    local_width = local_heads * head_dim
    rows = count_tok * uly
    seg_row = segments[0]
    length = seg_row.shape[0]
    number = router.shape[1]
    local_experts, _, units = w_down.shape
    shard_rows = w_qkv.shape[0]

    extra = jnp.concatenate([attn_gain[:, None], ffn_gain[:, None], router], axis=1)
    extra = jnp.pad(extra, ((0, 0), (0, LANES - extra.shape[1])))
    columns = w_qkv.reshape(shard_rows, 3, uly, local_width).transpose(2, 0, 1, 3)
    packed = jnp.concatenate(
        [
            columns.reshape(uly, shard_rows, 3 * local_width),
            jnp.broadcast_to(extra[None], (uly, shard_rows, LANES)),
        ],
        axis=2,
    )
    packed = swap(packed, ULY).reshape(uly * shard_rows, 3 * local_width + LANES)
    packed = lax.all_gather(packed, ROWS, axis=0, tiled=True)
    own_qkv = packed[:, : 3 * local_width]
    gain_attn = packed[:, 3 * local_width].astype(F32)
    gain_ffn = packed[:, 3 * local_width + 1].astype(F32)
    whole_router = packed[:, 3 * local_width + 2 : 3 * local_width + 2 + number]
    tokens_all = lax.all_gather(own_tokens, ULY, axis=0, tiled=True)
    to_rows = [(u * group + g, g * uly + u) for g in range(group) for u in range(uly)]
    own_out = lax.all_gather(lax.ppermute(w_out, ALL, to_rows), ROWS, axis=0, tiled=True)
    whole_gate_up = lax.all_gather(w_gate_up, PLANE, axis=0, tiled=False)
    whole_down = lax.all_gather(w_down, PLANE, axis=0, tiled=False)
    grad_blk = lax.all_gather(own_grad, "blk", axis=0, tiled=True)
    routes_blk = lax.all_gather(routes[0], "blk", axis=0, tiled=True)

    gain_query = qk_gain[0].astype(F32)
    gain_key = qk_gain[1].astype(F32)
    inputs_all = tokens_all.astype(F32)
    normed_one = inputs_all * rms_scale(inputs_all)
    hidden_one = (normed_one * gain_attn).astype(BF16)
    projected = dot_nn(hidden_one, own_qkv)
    query_raw = projected[:, :local_width].reshape(rows, local_heads, head_dim)
    key_raw = projected[:, local_width : 2 * local_width].reshape(rows, local_heads, head_dim)
    value_raw = projected[:, 2 * local_width :].reshape(rows, local_heads, head_dim)
    cos_table, sin_table = rope_tables(blk_at * rows, rows, head_dim)
    query_scale = rms_scale(query_raw)
    key_scale = rms_scale(key_raw)
    qkv = jnp.concatenate(
        [
            rotate(query_raw * query_scale * gain_query, cos_table, sin_table),
            rotate(key_raw * key_scale * gain_key, cos_table, sin_table),
            value_raw,
        ],
        axis=2,
    ).astype(BF16)
    qkv = qkv.transpose(1, 0, 2)

    by_heads = local_heads % blk == 0
    if by_heads:
        per = local_heads // blk

        def to_heads(values):
            columns = values.shape[2]
            moved = swap(values.reshape(blk, per, rows, columns), "blk")
            return moved.transpose(1, 0, 2, 3).reshape(per, length, columns)

        def to_rows_back(values):
            columns = values.shape[2]
            parts = values.reshape(per, blk, rows, columns).transpose(1, 0, 2, 3)
            return swap(parts, "blk").reshape(local_heads, rows, columns)

        q_src = kv_src = to_heads(qkv)
        cols = (0, 1, 2)
        seg_q = seg_row
        first_head = uly_at * local_heads + blk_at * per
    else:

        def to_heads(values):
            return values

        def to_rows_back(values):
            return values

        q_src = qkv
        kv_src = lax.all_gather(qkv[:, :, head_dim:], "blk", axis=1, tiled=True)
        cols = (0, 0, 1)
        seg_q = lax.dynamic_slice_in_dim(seg_row, blk_at * rows, rows)
        first_head = uly_at * local_heads
    attn_low, attn_f32, lse, top = attention_forward(q_src, kv_src, cols, seg_q, seg_row, head_dim)
    head_vector = lax.dynamic_update_slice_in_dim(
        jnp.full((heads,), NEG, F32), jnp.max(top, axis=(1, 2)) * head_dim**-0.5, first_head, 0
    )
    head_max = lax.pmax(head_vector, ALL)
    attn_rows = to_rows_back(attn_low)
    out_heads = own_out.reshape(local_heads, head_dim, width)
    branch = jnp.einsum("htc,hcd->td", attn_rows, out_heads, preferred_element_type=F32)
    inputs = own_tokens.astype(F32)
    mid = inputs + sum_scatter(branch, ULY)

    scale_two = rms_scale(mid)
    normed_two = mid * scale_two
    hidden_two = (normed_two * gain_ffn).astype(BF16)
    hidden_blk = lax.all_gather(hidden_two, "blk", axis=0, tiled=True)
    probs_blk = jax.nn.softmax(dot_nn(hidden_blk, whole_router), axis=1)
    names = jnp.arange(number, dtype=jnp.int32)
    chosen_blk = jnp.any(routes_blk[:, :, None] == names, axis=1).astype(F32)
    own_names = blk_at * local_experts
    gates = lax.dynamic_slice_in_dim(probs_blk * chosen_blk, own_names, local_experts, axis=1)
    most = min(MOST_TOKENS, hidden_blk.shape[0])
    packed_weights = jnp.concatenate([whole_gate_up, whole_down], axis=3)
    made = []
    for at in range(0, hidden_blk.shape[0], most):
        hidden_part, grad_part = hidden_blk[at : at + most], grad_blk[at : at + most]
        made.append(
            experts(
                hidden_part,
                hidden_part.T,
                grad_part,
                grad_part.T,
                gates[at : at + most],
                packed_weights,
            )
        )
    out_part = jnp.concatenate([m[0] for m in made], axis=0)
    dx_part = jnp.concatenate([m[1] for m in made], axis=0)
    dg_part = jnp.concatenate([m[2] for m in made], axis=1)
    expert_grads = sum(m[3].astype(F32) for m in made).astype(BF16)
    expert_sums = lax.psum_scatter(expert_grads, PLANE, scatter_dimension=0, tiled=False).astype(F32)
    grad_gate_up = jnp.concatenate([expert_sums[0], expert_sums[1]], axis=2)
    grad_down = expert_sums[2]
    dg_parts = swap(dg_part.reshape(local_experts, blk, count_tok).transpose(1, 2, 0), "blk")
    grad_gates = dg_parts.transpose(1, 0, 2).reshape(count_tok, number)
    dx_sum = sum_scatter(dx_part, "blk")
    output = (mid + sum_scatter(out_part, "blk")).astype(BF16)
    router_probs = lax.dynamic_slice_in_dim(probs_blk, blk_at * count_tok, count_tok)
    chosen = lax.dynamic_slice_in_dim(chosen_blk, blk_at * count_tok, count_tok)
    grad_probs = chosen * grad_gates
    grad_logits = (
        router_probs * (grad_probs - jnp.sum(router_probs * grad_probs, axis=1, keepdims=True))
    ).astype(BF16)
    grad_hidden_two = dx_sum + dot_nt(grad_logits, whole_router)
    grad_router_part = dot_tn(hidden_two, grad_logits)
    grad_gain_ffn = jnp.sum(grad_hidden_two * normed_two, axis=0)
    grad_mid = own_grad.astype(F32) + norm_back(grad_hidden_two * gain_ffn, mid, scale_two)

    branch_grad = lax.all_gather(grad_mid.astype(BF16), ULY, axis=0, tiled=True)
    grad_attn = dot_nt(branch_grad, own_out).astype(BF16)
    grad_attn = to_heads(grad_attn.reshape(rows, local_heads, head_dim).transpose(1, 0, 2))
    grad_out_part = jnp.einsum("htc,td->hcd", attn_rows, branch_grad, preferred_element_type=F32)
    dq, dk, dv = attention_backward(
        q_src, kv_src, cols, grad_attn, attn_f32, lse, seg_q, seg_row, head_dim
    )
    if by_heads:
        dqkv = to_rows_back(jnp.concatenate([dq, dk, dv], axis=2))
        dq, dk, dv = jnp.split(dqkv, 3, axis=2)
    else:
        dk, dv = (lax.psum_scatter(g, "blk", scatter_dimension=1, tiled=True) for g in (dk, dv))
    dq, dk, dv = (g.transpose(1, 0, 2) for g in (dq, dk, dv))
    grad_query_norm = rotate(dq.astype(F32), cos_table, -sin_table)
    grad_key_norm = rotate(dk.astype(F32), cos_table, -sin_table)
    grad_gain_query = jnp.sum(grad_query_norm * (query_raw * query_scale), axis=(0, 1))
    grad_gain_key = jnp.sum(grad_key_norm * (key_raw * key_scale), axis=(0, 1))
    grad_projected = jnp.concatenate(
        [
            norm_back(grad_query_norm * gain_query, query_raw, query_scale)
            .reshape(rows, local_width)
            .astype(BF16),
            norm_back(grad_key_norm * gain_key, key_raw, key_scale)
            .reshape(rows, local_width)
            .astype(BF16),
            dv.reshape(rows, local_width),
        ],
        axis=1,
    )
    grad_hidden_part = dot_nt(grad_projected, own_qkv)
    grad_hidden_one = sum_scatter(grad_hidden_part, ULY)
    grad_gain_attn = jnp.sum(grad_hidden_part * normed_one, axis=0)
    grad_inputs = grad_mid + norm_back(grad_hidden_one * gain_attn, inputs, rms_scale(inputs))

    grad_qkv_part = dot_tn(hidden_one, grad_projected).astype(BF16)
    grad_qkv_rows = lax.psum_scatter(grad_qkv_part, ROWS, scatter_dimension=0, tiled=True)
    grad_qkv_rows = swap(grad_qkv_rows.reshape(uly, shard_rows, 3 * local_width), ULY)
    grad_qkv = (
        grad_qkv_rows.reshape(uly, shard_rows, 3, local_width)
        .transpose(1, 2, 0, 3)
        .reshape(shard_rows, 3 * width)
        .astype(F32)
    )
    grad_out_rows = lax.psum_scatter(
        grad_out_part.reshape(local_width, width).astype(BF16), ROWS, scatter_dimension=0, tiled=True
    )
    grad_out = lax.ppermute(grad_out_rows, ALL, [(b, a) for a, b in to_rows]).astype(F32)
    small = jnp.concatenate([grad_gain_attn[:, None], grad_gain_ffn[:, None], grad_router_part], axis=1)
    small = lax.psum_scatter(small, ALL, scatter_dimension=0, tiled=True)
    grad_qk_gain = lax.psum(jnp.stack([grad_gain_query, grad_gain_key]), ALL)

    clip_gamma = TAU / jnp.maximum(head_max, TAU)
    factor = jnp.repeat(jnp.sqrt(clip_gamma), head_dim)
    column_scale = jnp.concatenate([factor, factor, jnp.ones((width,), F32)])
    clipped = w_qkv.astype(F32) * column_scale[None, :]
    return (
        output[None],
        grad_inputs[None],
        grad_qkv,
        grad_out,
        small[:, 0],
        small[:, 1],
        grad_qk_gain,
        small[:, 2:],
        grad_gate_up,
        grad_down,
        clipped,
    )


def per_device(
    tokens, segments, routes, w_qkv, w_out, attn_gain, ffn_gain, qk_gain, router, w_gate_up, w_down, cotangent
):
    own_tokens = tokens[0]
    own_grad = cotangent[0]
    count_tok, width = own_tokens.shape
    head_dim = qk_gain.shape[1]
    heads = width // head_dim
    batch, blk, uly = lax.axis_size("batch"), lax.axis_size("blk"), spread(ULY)
    total, group = batch * blk * uly, batch * blk
    local_experts = w_down.shape[0]
    if uly != 4 or heads != blk * uly or batch != 2 or local_experts != 4:
        return per_device_general(
            tokens, segments, routes, w_qkv, w_out, attn_gain, ffn_gain, qk_gain, router, w_gate_up, w_down, cotangent
        )
    blk_at, uly_at = lax.axis_index("blk"), lax.axis_index(ULY)
    rows = count_tok * uly
    seg_row = segments[0]
    length = seg_row.shape[0]
    number = router.shape[1]
    shard_rows = w_qkv.shape[0]

    to_rows = [(u * group + g, g * uly + u) for g in range(group) for u in range(uly)]
    own_rows = lax.ppermute(w_out, ALL, to_rows)
    half = local_experts // 2


    def gather_experts(gate_up, down):
        return lax.all_gather(jnp.concatenate([gate_up, down], axis=2), PLANE, axis=0, tiled=False)

    weights_first = gather_experts(w_gate_up[:half], w_down[:half])
    extra = jnp.concatenate([attn_gain[None], ffn_gain[None], router.T], axis=0)
    kept = extra.shape[0]
    extra = jnp.pad(extra, ((0, -kept % 16), (0, -shard_rows % LANES)))
    by_head = w_qkv.reshape(shard_rows, 3, heads, head_dim).transpose(2, 0, 1, 3)
    own_qkv, extras, toks = startup(
        by_head.reshape(heads, shard_rows, 3 * head_dim), extra, own_tokens, 0
    )
    own_rows, extras, later_gate_up, later_down = lax.optimization_barrier(
        (own_rows, extras, w_gate_up[half:], w_down[half:])
    )
    weights_second = gather_experts(later_gate_up, later_down)
    own_out = lax.all_to_all(
        jnp.broadcast_to(own_rows[None], (group, *own_rows.shape)), ROWS, split_axis=0, concat_axis=0, tiled=True
    ).reshape(blk, head_dim, width)
    own_qkv = own_qkv.reshape(width, 3 * head_dim)
    extras = extras[:, :kept, :shard_rows].transpose(1, 0, 2).reshape(kept, width)
    gain_attn = extras[0].astype(F32)
    gain_ffn = extras[1].astype(F32)
    router_t = extras[2:]

    gains = qk_gain.astype(F32)
    cos, sin = rope_rows(length, head_dim)
    hidden_one, qkv, raw = project(
        toks.reshape(length, width), gain_attn[None], own_qkv, cos, sin, gains
    )
    attn_low, attn_f32, lse, top = attention_forward(
        qkv[None], qkv[None], (0, 1, 2), seg_row, seg_row, head_dim
    )
    (attn_rows,) = exchange([(attn_low.reshape(blk, rows, head_dim), ("blk",), "swap")], 1)
    branch = jnp.einsum("htc,hcd->td", attn_rows, own_out, preferred_element_type=F32)
    branch, grad_blk, routes_blk = exchange(
        [
            (branch.astype(BF16).reshape(uly, count_tok, width), ULY, "swap"),
            (own_grad, ("blk",), "line"),
            (routes[0].T, ("blk",), "gather"),
        ],
        2,
    )
    inputs = own_tokens.astype(F32)
    mid = inputs + jnp.sum(branch.astype(F32), axis=0)

    scale_two = rms_scale(mid)
    normed_two = mid * scale_two
    hidden_two = (normed_two * gain_ffn).astype(BF16)
    (hidden_blk,) = exchange([(hidden_two, ("blk",), "line")], 3, after=[weights_first])
    tokens_blk = blk * count_tok
    hidden_blk = hidden_blk.reshape(tokens_blk, width)
    grad_blk = grad_blk.reshape(tokens_blk, width)
    probs_blk = jax.nn.softmax(dot_nt(hidden_blk, router_t), axis=1)
    names = jnp.arange(number, dtype=jnp.int32)
    chosen_blk = jnp.any(routes_blk[:, :, :, None] == names, axis=1).astype(F32)
    chosen_blk = chosen_blk.reshape(tokens_blk, number)
    gates = lax.dynamic_slice_in_dim(
        probs_blk * chosen_blk, blk_at * local_experts, local_experts, axis=1
    )
    shared = (hidden_blk, hidden_blk.T, grad_blk, grad_blk.T)
    out_first, dx_first, dg_first, grads_first = experts(*shared, gates[:, :half], weights_first)
    sums_first = lax.psum_scatter(grads_first, PLANE, scatter_dimension=0, tiled=False)
    out_part, dx_part, dg_second, grads_second, keep_x, give_x, keep_y, give_y = experts_mixed(
        *shared, gates[:, half:], weights_second, (out_first, dx_first), 9
    )
    sums_second = lax.psum_scatter(grads_second, PLANE, scatter_dimension=0, tiled=False)
    finished = finish_experts(sums_first, 0, local_experts)
    dg_part = jnp.concatenate([dg_first, dg_second], axis=0).reshape(local_experts, blk, count_tok)
    dx_parts, dg_parts, got_x, got_y = exchange(
        [
            (dx_part.reshape(blk, count_tok, width), ("blk",), "swap"),
            (dg_part.transpose(1, 0, 2), ("blk",), "swap"),
            (give_x, ("batch",), "trade"),
            (give_y, ("y",), "trade"),
        ],
        4,
    )
    out_part = out_part.reshape(blk, count_tok, width)
    out_part, dx_parts = lax.optimization_barrier((out_part, dx_parts))
    out_parts = lax.all_to_all(out_part, "blk", split_axis=0, concat_axis=0, tiled=True)
    output = (mid + jnp.sum(out_parts.astype(F32), axis=0)).astype(BF16)
    router_probs = lax.dynamic_slice_in_dim(probs_blk, blk_at * count_tok, count_tok)
    chosen = lax.dynamic_slice_in_dim(chosen_blk, blk_at * count_tok, count_tok)
    grad_probs = chosen * dg_parts.reshape(number, count_tok).T
    grad_logits = (
        router_probs * (grad_probs - jnp.sum(router_probs * grad_probs, axis=1, keepdims=True))
    ).astype(BF16)
    grad_hidden_two = jnp.sum(dx_parts.astype(F32), axis=0) + dot_nn(grad_logits, router_t)
    grad_router_t = dot_tn(grad_logits, hidden_two)
    grad_gain_ffn = jnp.sum(grad_hidden_two * normed_two, axis=0)
    grad_mid = own_grad.astype(F32) + norm_back(grad_hidden_two * gain_ffn, mid, scale_two)

    (branch_grad,) = exchange([(grad_mid.astype(BF16), ULY, "relay")], 5)
    branch_grad, sent_qkv = lax.optimization_barrier((branch_grad, own_qkv))
    far_qkv = lax.ppermute(sent_qkv, "y", [(0, 1), (1, 0)])
    branch_grad = branch_grad.reshape(rows, width)
    grad_attn = jnp.einsum("td,hcd->htc", branch_grad, own_out, preferred_element_type=F32).astype(BF16)
    grad_out_part = jnp.einsum("htc,td->hcd", attn_rows, branch_grad, preferred_element_type=F32)
    grad_out_part = grad_out_part.astype(BF16).reshape(batch, blk, shard_rows, width)
    batch_at = lax.axis_index("batch")
    grad_attn, got_out_part = exchange(
        [
            (grad_attn, ("blk",), "swap"),
            (
                lax.dynamic_index_in_dim(grad_out_part, 1 - batch_at, 0, keepdims=False),
                ("batch",),
                "trade",
            ),
        ],
        6,
        after=[out_parts],
    )
    grad_out_part = lax.dynamic_index_in_dim(grad_out_part, batch_at, 0, keepdims=False) + got_out_part
    grad_projected, grad_gains = project_back(
        qkv, grad_attn.reshape(length, head_dim), attn_f32, lse, seg_row, raw, cos, sin, gains
    )
    grad_qkv_part = dot_tn(hidden_one, grad_projected).astype(BF16)
    by_batch = grad_qkv_part.reshape(batch, width // batch, 3 * head_dim)
    projected_blk, got_qkv_part, near_qkv, cross_qkv, grad_out_parts = exchange(
        [
            (grad_projected.reshape(blk, uly, count_tok, 3 * head_dim), ULY, "swap1"),
            (
                lax.dynamic_index_in_dim(by_batch, 1 - batch_at, 0, keepdims=False),
                ("batch",),
                "trade",
            ),
            (own_qkv, ("core",), "trade"),
            (far_qkv, ("core",), "trade"),
            (grad_out_part, ("blk",), "swap"),
        ],
        7,
    )
    grad_out = lax.ppermute(
        jnp.sum(grad_out_parts.astype(F32), axis=0).astype(BF16), ALL, [(b, a) for a, b in to_rows]
    ).astype(F32)
    grad_qkv_part = lax.dynamic_index_in_dim(by_batch, batch_at, 0, keepdims=False) + got_qkv_part

    grad_hidden_part, grad_gain_attn = hidden_back(
        projected_blk.reshape(uly, tokens_blk, 3 * head_dim),
        own_qkv,
        near_qkv,
        far_qkv,
        cross_qkv,
        hidden_one.reshape(blk, uly, count_tok, width),
    )
    grad_gain_attn = grad_gain_attn[0] / gain_attn

    small = jnp.concatenate([grad_gain_attn[None], grad_gain_ffn[None], grad_router_t], axis=0)
    small = small.reshape(kept, total, shard_rows).transpose(1, 0, 2)
    small = jnp.pad(small, ((0, 0), (0, 0), (0, LANES - shard_rows)))
    head_row = jnp.where(
        jnp.arange(LANES) == uly_at * blk + blk_at, jnp.max(top) * head_dim**-0.5, NEG
    )
    to_all = jnp.concatenate([grad_gains, head_row[None]], axis=0)
    small = jnp.concatenate([small, jnp.broadcast_to(to_all[None], (total, 3, LANES))], axis=1)
    small = jnp.pad(small, ((0, 0), (0, -small.shape[1] % 8), (0, 0)))
    grad_hidden_parts, small, grad_qkv_parts, last_x, last_y = exchange(
        [
            (grad_hidden_part, ("blk",), "swap"),
            (small, ALL, "swap"),
            (grad_qkv_part.reshape(total // batch, shard_rows, 3 * head_dim), ("blk", *ULY), "swap"),
            (keep_x[1] + got_x[1], ("y",), "trade"),
            (keep_y[1] + got_y[1], ("batch",), "trade"),
        ],
        8,
        after=[finished[0]],
    )
    finished = finish_experts(sums_second, half, local_experts, before=finished)
    grad_gate_up, grad_down = finish_traded(
        (keep_x, got_x, last_x), (keep_y, got_y, last_y), half + 1, finished
    )
    grad_qkv = merge_heads(grad_qkv_parts.reshape(blk, uly, shard_rows, 3 * head_dim))
    grad_hidden_one = jnp.sum(grad_hidden_parts.astype(F32), axis=0)
    grad_inputs = grad_mid + norm_back(grad_hidden_one * gain_attn, inputs, rms_scale(inputs))
    sums = jnp.sum(small, axis=0)
    head_max = jnp.max(small[:, kept + 2, :heads], axis=0)
    factor = jnp.repeat(jnp.sqrt(TAU / jnp.maximum(head_max, TAU)), head_dim)
    column_scale = jnp.concatenate([factor, factor, jnp.ones((width,), F32)])
    clipped = w_qkv.astype(F32) * column_scale[None, :]
    return (
        output[None],
        grad_inputs[None],
        grad_qkv,
        grad_out,
        sums[0, :shard_rows],
        sums[1, :shard_rows],
        sums[kept : kept + 2],
        sums[2:kept, :shard_rows].T,
        grad_gate_up,
        grad_down,
        clipped,
    )


def solution(mesh):
    in_specs = (
        P("batch", ("blk", *ULY), None),
        P("batch", None),
        P("batch", ("blk", *ULY), None),
        P(ALL, None),
        P(ALL, None),
        P(ALL),
        P(ALL),
        P(),
        P(ALL, None),
        P("blk", PLANE, None),
        P("blk", PLANE, None),
        P("batch", ("blk", *ULY), None),
    )
    out_specs = (
        P("batch", ("blk", *ULY), None),
        P("batch", ("blk", *ULY), None),
        P(ALL, None),
        P(ALL, None),
        P(ALL),
        P(ALL),
        P(),
        P(ALL, None),
        P("blk", PLANE, None),
        P("blk", PLANE, None),
        P(ALL, None),
    )
    cores = 2 - mesh.shape["uly"] % 2
    mesh = Mesh(
        mesh.devices.reshape(*(mesh.shape[axis] for axis in ROWS), mesh.shape["uly"] // cores, cores), ALL
    )
    return jax.shard_map(
        per_device, mesh=mesh, in_specs=in_specs, out_specs=out_specs, check_vma=False
    )
```

```python
import functools
import math

import jax
import jax.numpy as jnp
from jax import lax
from jax.experimental import pallas as pl
from jax.experimental.pallas import tpu as pltpu
from jax.sharding import Mesh
from jax.sharding import PartitionSpec as P

EPS = 1e-06
THETA = 50000.0
TAU = 4.0
NEG = -1e30
LOG2E = 1.4426950408889634
LANES = 128
MOST_TOKENS = 512
VMEM_LIMIT = 60 * 1024 * 1024

ULY = ("y", "core")
ALL = ("batch", "blk", *ULY)
ROWS = ("batch", "blk")
PLANE = ("batch", *ULY)
CHIPS = ("batch", "y")

MESH = pl.DeviceIdType.MESH
BF16 = jnp.bfloat16
F32 = jnp.float32


def rms_scale(values):
    return lax.rsqrt(jnp.mean(values * values, axis=-1, keepdims=True) + EPS)


def norm_back(grad_normed, values, scale):
    normed = values * scale
    return scale * (grad_normed - normed * jnp.mean(grad_normed * normed, axis=-1, keepdims=True))


def rope_tables(offset, length, head_dim):
    half_dim = head_dim // 2
    frequency = THETA ** (-jnp.arange(half_dim, dtype=F32) * 2.0 / head_dim)
    positions = (offset + jnp.arange(length, dtype=jnp.int32)).astype(F32)
    angles = positions[:, None] * frequency[None, :]
    return (jnp.cos(angles)[:, None, :], jnp.sin(angles)[:, None, :])


def rope_rows(length, head_dim):
    fine = math.gcd(length, LANES)
    frequency = THETA ** (-jnp.arange(head_dim // 2, dtype=F32) * 2.0 / head_dim)
    frequency = jnp.concatenate([frequency, frequency])
    coarse_angle = (jnp.arange(length // fine, dtype=F32) * fine)[:, None, None] * frequency
    fine_angle = jnp.arange(fine, dtype=F32)[None, :, None] * frequency
    cos_a, sin_a, cos_b, sin_b = lax.optimization_barrier(
        (jnp.cos(coarse_angle), jnp.sin(coarse_angle), jnp.cos(fine_angle), jnp.sin(fine_angle))
    )
    sign = jnp.where(jnp.arange(head_dim) < head_dim // 2, -1.0, 1.0)
    cos = cos_a * cos_b - sin_a * sin_b
    sin = (sin_a * cos_b + cos_a * sin_b) * sign
    return cos.reshape(length, head_dim), sin.reshape(length, head_dim)


def rotate(values, cos_table, sin_table):
    half_dim = values.shape[-1] // 2
    first = values[..., :half_dim]
    second = values[..., half_dim:]
    return jnp.concatenate(
        [first * cos_table - second * sin_table, second * cos_table + first * sin_table], axis=-1
    )


def dot_nn(a, b):
    return lax.dot_general(a, b, (((1,), (0,)), ((), ())), preferred_element_type=F32)


def dot_nt(a, b):
    return lax.dot_general(a, b, (((1,), (1,)), ((), ())), preferred_element_type=F32)


def dot_tn(a, b):
    return lax.dot_general(a, b, (((0,), (0,)), ((), ())), preferred_element_type=F32)


def key_chunks(length):
    size = min(512, length)
    return size, length // size


def attn_fwd_kernel(factor, q_ref, k_ref, v_ref, sq_ref, sk_ref, o_ref, of_ref, lse_ref, top_ref, vt_ref):
    length = k_ref.shape[1]
    size, count = key_chunks(length)
    tile, head_dim = q_ref.shape[1:]

    @pl.when(pl.program_id(1) == 0)
    def _():
        vt_ref[...] = v_ref[0].astype(F32).T.astype(BF16)

    q = q_ref[0]
    seg_q = sq_ref[...]

    def step(j, carried):
        total, top, acc = carried
        at = pl.multiple_of(j * size, size)
        scores = dot_nt(k_ref[0, pl.ds(at, size), :], q)
        scores = jnp.where(sk_ref[pl.ds(at, size), :] == seg_q, scores, NEG)
        top = jnp.maximum(top, jnp.max(scores, axis=0, keepdims=True))
        weights = jnp.exp2(scores * factor)
        total = total + jnp.sum(weights, axis=0, keepdims=True)
        acc = acc + dot_nn(vt_ref[:, pl.ds(at, size)], weights.astype(BF16))
        return total, top, acc

    start = (
        jnp.zeros((1, tile), F32),
        jnp.full((1, tile), NEG, F32),
        jnp.zeros((head_dim, tile), F32),
    )
    total, top, acc = lax.fori_loop(0, count, step, start, unroll=count <= 4)
    out = (acc * (1.0 / total)).T
    o_ref[0] = out.astype(BF16)
    of_ref[0] = out
    lse_ref[0] = jnp.log2(total)
    top_ref[0] = top


def attn_bwd_kernel(
    factor, scale, q_ref, k_ref, v_ref, do_ref, of_ref, lse_ref, sq_ref, sk_ref,
    dq_ref, dk_ref, dv_ref, kt_ref, dk_acc, dv_acc,
):
    length = k_ref.shape[1]
    size, count = key_chunks(length)
    tile, head_dim = q_ref.shape[1:]

    @pl.when(pl.program_id(1) == 0)
    def _():
        kt_ref[...] = k_ref[0].astype(F32).T.astype(BF16)
        dk_acc[...] = jnp.zeros_like(dk_acc)
        dv_acc[...] = jnp.zeros_like(dv_acc)

    q = q_ref[0]
    grad = do_ref[0]
    seg_q = sq_ref[...]
    lse = lse_ref[0]
    row_dot = jnp.sum((grad.astype(F32) * of_ref[0]).T, axis=0, keepdims=True)

    def step(j, dq_t):
        at = pl.multiple_of(j * size, size)
        rows = pl.ds(at, size)
        scores = dot_nt(k_ref[0, rows, :], q)
        scores = jnp.where(sk_ref[rows, :] == seg_q, scores, NEG)
        weights = jnp.exp2(scores * factor - lse)
        grad_weights = dot_nt(v_ref[0, rows, :], grad)
        grad_scores = (weights * (grad_weights - row_dot)).astype(BF16)
        dk_acc[rows, :] += dot_nn(grad_scores, q)
        dv_acc[rows, :] += dot_nn(weights.astype(BF16), grad)
        return dq_t + dot_nn(kt_ref[:, rows], grad_scores)

    dq_t = lax.fori_loop(0, count, step, jnp.zeros((head_dim, tile), F32), unroll=count <= 4)
    dq_ref[0] = (dq_t * scale).T.astype(BF16)

    @pl.when(pl.program_id(1) == pl.num_programs(1) - 1)
    def _():
        dk_ref[0] = (dk_acc[...] * scale).astype(BF16)
        dv_ref[0] = dv_acc[...].astype(BF16)


def attention_tile(queries, length):
    return min(queries, 256 if length <= 4096 else 128)


def attention_forward(q_src, kv_src, cols, seg_q, seg_k, head_dim):
    heads, queries = q_src.shape[:2]
    length = kv_src.shape[1]
    tile = attention_tile(queries, length)
    q_col, k_col, v_col = cols
    factor = head_dim**-0.5 * LOG2E
    row = pl.BlockSpec((1, 1, tile), lambda h, i: (h, 0, i))
    block = pl.BlockSpec((1, tile, head_dim), lambda h, i: (h, i, 0))
    return pl.pallas_call(
        functools.partial(attn_fwd_kernel, factor),
        grid=(heads, queries // tile),
        in_specs=[
            pl.BlockSpec((1, tile, head_dim), lambda h, i: (h, i, q_col)),
            pl.BlockSpec((1, length, head_dim), lambda h, i: (h, 0, k_col)),
            pl.BlockSpec((1, length, head_dim), lambda h, i: (h, 0, v_col)),
            pl.BlockSpec((1, tile), lambda h, i: (0, i)),
            pl.BlockSpec((length, 1), lambda h, i: (0, 0)),
        ],
        out_specs=[block, block, row, row],
        out_shape=[
            jax.ShapeDtypeStruct((heads, queries, head_dim), BF16),
            jax.ShapeDtypeStruct((heads, queries, head_dim), F32),
            jax.ShapeDtypeStruct((heads, 1, queries), F32),
            jax.ShapeDtypeStruct((heads, 1, queries), F32),
        ],
        scratch_shapes=[pltpu.VMEM((head_dim, length), BF16)],
        compiler_params=pltpu.CompilerParams(vmem_limit_bytes=VMEM_LIMIT),
        cost_estimate=pl.CostEstimate(
            flops=4 * heads * queries * length * head_dim,
            bytes_accessed=heads * (queries + length) * head_dim * 8,
            transcendentals=heads * queries * length,
        ),
        name="attend",
    )(q_src, kv_src, kv_src, seg_q.reshape(1, -1), seg_k.reshape(-1, 1))


def attention_backward(q_src, kv_src, cols, grad, out_f32, lse, seg_q, seg_k, head_dim):
    heads, queries = q_src.shape[:2]
    length = kv_src.shape[1]
    tile = attention_tile(queries, length)
    q_col, k_col, v_col = cols
    scale = head_dim**-0.5
    row = pl.BlockSpec((1, 1, tile), lambda h, i: (h, 0, i))
    block = pl.BlockSpec((1, tile, head_dim), lambda h, i: (h, i, 0))
    whole = pl.BlockSpec((1, length, head_dim), lambda h, i: (h, 0, 0))
    return pl.pallas_call(
        functools.partial(attn_bwd_kernel, scale * LOG2E, scale),
        grid=(heads, queries // tile),
        in_specs=[
            pl.BlockSpec((1, tile, head_dim), lambda h, i: (h, i, q_col)),
            pl.BlockSpec((1, length, head_dim), lambda h, i: (h, 0, k_col)),
            pl.BlockSpec((1, length, head_dim), lambda h, i: (h, 0, v_col)),
            block,
            block,
            row,
            pl.BlockSpec((1, tile), lambda h, i: (0, i)),
            pl.BlockSpec((length, 1), lambda h, i: (0, 0)),
        ],
        out_specs=[block, whole, whole],
        out_shape=[
            jax.ShapeDtypeStruct((heads, queries, head_dim), BF16),
            jax.ShapeDtypeStruct((heads, length, head_dim), BF16),
            jax.ShapeDtypeStruct((heads, length, head_dim), BF16),
        ],
        scratch_shapes=[
            pltpu.VMEM((head_dim, length), BF16),
            pltpu.VMEM((length, head_dim), F32),
            pltpu.VMEM((length, head_dim), F32),
        ],
        compiler_params=pltpu.CompilerParams(vmem_limit_bytes=VMEM_LIMIT),
        cost_estimate=pl.CostEstimate(
            flops=10 * heads * queries * length * head_dim,
            bytes_accessed=heads * (queries + length) * head_dim * 12,
            transcendentals=heads * queries * length,
        ),
        name="attend_back",
    )(q_src, kv_src, kv_src, grad, out_f32, lse, seg_q.reshape(1, -1), seg_k.reshape(-1, 1))


def pack_experts(gate_up, down):
    count, rows, units = down.shape
    cols = min(256, units)
    gate_up = gate_up.reshape(count, rows, 2, units // cols, cols)
    packed = jnp.concatenate([gate_up, down.reshape(count, rows, 1, units // cols, cols)], axis=2)
    return packed.transpose(0, 1, 3, 2, 4).reshape(count, rows, 3 * units)


def expert_step(expert, h_ref, ht_ref, dy_ref, dyt_ref, gate_ref, w_ref, dg_ref, out_acc, dx_acc):
    width = h_ref.shape[1]
    cols = w_ref.shape[3] // 3
    w_in = w_ref[:, 0, :, : 2 * cols].reshape(width, 2 * cols)
    w_down = w_ref[:, 0, :, 2 * cols :].reshape(width, cols)
    gates = gate_ref[...]
    mine = lax.broadcasted_iota(jnp.int32, gates.shape, 1) == expert
    gate = jnp.sum(jnp.where(mine, gates, 0.0), axis=1, keepdims=True)
    before = dot_nn(h_ref[...], w_in)
    a_gate, a_up = before[:, :cols], before[:, cols:]
    raw = dot_nn(dy_ref[...], w_down)
    sigma = 1.0 / (1.0 + jnp.exp2(a_gate * -LOG2E))
    swish = a_gate * sigma
    act = swish * a_up
    dg_ref[0] += jnp.sum(raw * act, axis=1, keepdims=True)
    gated = (gate * act).astype(BF16)
    d_act = gate * raw
    d_gate = (d_act * a_up * (sigma + swish * (1.0 - sigma))).astype(BF16)
    d_in = jnp.concatenate([d_gate, (d_act * swish).astype(BF16)], axis=1)
    out_acc[...] += dot_nt(gated, w_down)
    dx_acc[...] += dot_nt(d_in, w_in)
    made = dot_nn(ht_ref[...], d_in).astype(BF16)
    yield 0, made[:, :cols]
    yield 1, made[:, cols:]
    yield 2, dot_nn(dyt_ref[...], gated).astype(BF16)


def expert_kernel(more, *refs):
    h_ref, ht_ref, dy_ref, dyt_ref, gate_ref, w_ref = refs[:6]
    out_ref, dx_ref, dg_ref, gr_ref, out_acc, dx_acc = refs[-6:]
    step, last = pl.program_id(0), pl.num_programs(0) - 1
    parts, _, part_rows, cols = w_ref.shape
    cols = cols // 3
    chunks = (last + 1) // gate_ref.shape[1]

    @pl.when(step == 0)
    def _():
        if more:
            out0_ref, dx0_ref = refs[6:8]
            out_acc[...] = out0_ref[...].astype(F32)
            dx_acc[...] = dx0_ref[...].astype(F32)
        else:
            out_acc[...] = jnp.zeros_like(out_acc)
            dx_acc[...] = jnp.zeros_like(dx_acc)

    @pl.when(step % chunks == 0)
    def _():
        dg_ref[...] = jnp.zeros_like(dg_ref)

    for part, made in expert_step(
        step // chunks, h_ref, ht_ref, dy_ref, dyt_ref, gate_ref, w_ref, dg_ref, out_acc, dx_acc
    ):
        gr_ref[:, part, 0] = made.reshape(parts, part_rows, cols)

    @pl.when(step == last)
    def _():
        out_ref[...] = out_acc[...].astype(BF16)
        dx_ref[...] = dx_acc[...].astype(BF16)


def experts(hidden, hidden_t, grad, grad_t, gates, weights, before=()):
    tokens, width = hidden.shape
    parts, count, part_rows, units = weights.shape
    units = units // 3
    cols = min(256, units)
    chunks = units // cols
    once = pl.Buffered(1)
    whole = pl.BlockSpec((tokens, width), lambda s: (0, 0), pipeline_mode=once)
    whole_t = pl.BlockSpec((width, tokens), lambda s: (0, 0), pipeline_mode=once)
    result = pl.BlockSpec((tokens, width), lambda s: (0, 0))

    weight = pl.BlockSpec((parts, 1, part_rows, 3 * cols), lambda s: (0, s // chunks, 0, s % chunks))
    return pl.pallas_call(
        functools.partial(expert_kernel, bool(before)),
        grid=(count * chunks,),
        in_specs=[
            whole,
            whole_t,
            whole,
            whole_t,
            pl.BlockSpec(gates.shape, lambda s: (0, 0), pipeline_mode=once),
            weight,
            *[whole for _ in before],
        ],
        out_specs=[
            result,
            result,
            pl.BlockSpec((1, tokens, 1), lambda s: (s // chunks, 0, 0)),
            pl.BlockSpec((parts, 3, 1, part_rows, cols), lambda s: (0, 0, s // chunks, 0, s % chunks)),
        ],
        out_shape=[
            jax.ShapeDtypeStruct((tokens, width), BF16),
            jax.ShapeDtypeStruct((tokens, width), BF16),
            jax.ShapeDtypeStruct((count, tokens, 1), F32),
            jax.ShapeDtypeStruct((parts, 3, count, part_rows, units), BF16),
        ],
        scratch_shapes=[
            pltpu.VMEM((tokens, width), F32),
            pltpu.VMEM((tokens, width), F32),
        ],
        compiler_params=pltpu.CompilerParams(vmem_limit_bytes=VMEM_LIMIT),
        cost_estimate=pl.CostEstimate(
            flops=18 * count * tokens * width * units,
            bytes_accessed=12 * count * width * units,
            transcendentals=count * tokens * units,
        ),
        name="experts",
    )(hidden, hidden_t, grad, grad_t, gates, weights, *before)


def finish_experts_kernel(sums_ref, *refs):
    gate_up_ref, down_ref = refs[-2:]
    units = down_ref.shape[2]
    gate_up_ref[0, :, :units] = sums_ref[0, 0].astype(F32)
    gate_up_ref[0, :, units:] = sums_ref[1, 0].astype(F32)
    down_ref[0] = sums_ref[2, 0].astype(F32)


def finish_experts(sums, at, total, before=()):
    _, count, rows, units = sums.shape
    tile = min(128, rows)
    return pl.pallas_call(
        finish_experts_kernel,
        grid=(count, rows // tile),
        in_specs=[
            pl.BlockSpec((3, 1, tile, units), lambda e, r: (0, e, r, 0)),
            *[pl.BlockSpec(memory_space=pl.ANY) for _ in before],
        ],
        out_specs=[
            pl.BlockSpec((1, tile, 2 * units), lambda e, r: (at + e, r, 0)),
            pl.BlockSpec((1, tile, units), lambda e, r: (at + e, r, 0)),
        ],
        out_shape=[
            jax.ShapeDtypeStruct((total, rows, 2 * units), F32),
            jax.ShapeDtypeStruct((total, rows, units), F32),
        ],
        input_output_aliases={1 + i: i for i in range(len(before))},
        compiler_params=pltpu.CompilerParams(vmem_limit_bytes=VMEM_LIMIT),
        name="finish_experts",
    )(sums, *before)


def turn(values, cos, sin):
    return values * cos + pltpu.roll(values, values.shape[1] // 2, 1) * sin


def project_kernel(
    tok_ref, gain_ref, w_ref, cos_ref, sin_ref, gains_ref, hidden_ref, qkv_ref, raw_ref
):
    head_dim = cos_ref.shape[1]
    values = tok_ref[...].astype(F32)
    hidden = (values * rms_scale(values) * gain_ref[...]).astype(BF16)
    hidden_ref[...] = hidden
    projected = dot_nn(hidden, w_ref[...])
    raw_ref[...] = projected[:, : 2 * head_dim]
    for part in range(2):
        at = slice(part * head_dim, (part + 1) * head_dim)
        raw = projected[:, at]
        normed = raw * rms_scale(raw) * gains_ref[part : part + 1, :]
        qkv_ref[:, at] = turn(normed, cos_ref[...], sin_ref[...]).astype(BF16)
    qkv_ref[:, 2 * head_dim :] = projected[:, 2 * head_dim :].astype(BF16)


def project(toks, gain, weights, cos, sin, gains):
    length, width = toks.shape
    head_dim = cos.shape[1]
    tile = min(256, length)

    def rows(columns):
        return pl.BlockSpec((tile, columns), lambda i: (i, 0))

    def fixed(shape):
        return pl.BlockSpec(shape, lambda i: (0, 0))

    return pl.pallas_call(
        project_kernel,
        grid=(length // tile,),
        in_specs=[
            rows(width),
            fixed((1, width)),
            fixed(weights.shape),
            rows(head_dim),
            rows(head_dim),
            fixed(gains.shape),
        ],
        out_specs=[rows(width), rows(3 * head_dim), rows(2 * head_dim)],
        out_shape=[
            jax.ShapeDtypeStruct((length, width), BF16),
            jax.ShapeDtypeStruct((length, 3 * head_dim), BF16),
            jax.ShapeDtypeStruct((length, 2 * head_dim), F32),
        ],
        compiler_params=pltpu.CompilerParams(vmem_limit_bytes=VMEM_LIMIT),
        name="project",
    )(toks, gain, weights, cos, sin, gains)


def project_back_kernel(
    factor, scale, q_ref, k_ref, v_ref, do_ref, of_ref, lse_ref, sq_ref, sk_ref,
    raw_q_ref, raw_k_ref, cos_q_ref, sin_q_ref, cos_ref, sin_ref, gains_ref,
    dp_ref, dgain_ref, kt_ref, dk_acc, dv_acc,
):
    length, head_dim = k_ref.shape
    size, count = key_chunks(length)
    tile = q_ref.shape[0]
    step_at = pl.program_id(0)

    @pl.when(step_at == 0)
    def _():
        kt_ref[...] = k_ref[...].astype(F32).T.astype(BF16)
        dk_acc[...] = jnp.zeros_like(dk_acc)
        dv_acc[...] = jnp.zeros_like(dv_acc)
        dgain_ref[...] = jnp.zeros_like(dgain_ref)

    def to_raw(part, grad, raw, cos, sin):
        grad = turn(grad.astype(BF16).astype(F32), cos, -sin)
        raw_scale = rms_scale(raw)
        dgain_ref[part : part + 1, :] += jnp.sum(grad * (raw * raw_scale), axis=0, keepdims=True)
        return norm_back(grad * gains_ref[part : part + 1, :], raw, raw_scale).astype(BF16)

    q = q_ref[...]
    grad = do_ref[...]
    seg_q = sq_ref[...]
    lse = lse_ref[0]
    row_dot = jnp.sum((grad.astype(F32) * of_ref[0]).T, axis=0, keepdims=True)
    dq_t = jnp.zeros((head_dim, tile), F32)
    for j in range(count):
        rows = slice(j * size, (j + 1) * size)
        scores = dot_nt(k_ref[rows, :], q)
        scores = jnp.where(sk_ref[rows, :] == seg_q, scores, NEG)
        weights = jnp.exp2(scores * factor - lse)
        grad_weights = dot_nt(v_ref[rows, :], grad)
        grad_scores = (weights * (grad_weights - row_dot)).astype(BF16)
        dk_acc[rows, :] += dot_nn(grad_scores, q)
        dv_acc[rows, :] += dot_nn(weights.astype(BF16), grad)
        dq_t = dq_t + dot_nn(kt_ref[:, rows], grad_scores)
    own = pl.ds(pl.multiple_of(step_at * tile, tile), tile)
    dp_ref[own, :head_dim] = to_raw(
        0, (dq_t * scale).T, raw_q_ref[...], cos_q_ref[...], sin_q_ref[...]
    )

    @pl.when(step_at == pl.num_programs(0) - 1)
    def _():
        dp_ref[:, head_dim : 2 * head_dim] = to_raw(
            1, dk_acc[...] * scale, raw_k_ref[...], cos_ref[...], sin_ref[...]
        )
        dp_ref[:, 2 * head_dim :] = dv_acc[...].astype(BF16)


def project_back(qkv, grad, out_f32, lse, segments, raw, cos, sin, gains):
    length, head_dim = grad.shape
    tile = min(256, length)

    def rows(column):
        return pl.BlockSpec((tile, head_dim), lambda i: (i, column))

    def whole(column):
        return pl.BlockSpec((length, head_dim), lambda i: (0, column))

    return pl.pallas_call(
        functools.partial(project_back_kernel, head_dim**-0.5 * LOG2E, head_dim**-0.5),
        grid=(length // tile,),
        in_specs=[
            rows(0),
            whole(1),
            whole(2),
            rows(0),
            pl.BlockSpec((1, tile, head_dim), lambda i: (0, i, 0)),
            pl.BlockSpec((1, 1, tile), lambda i: (0, 0, i)),
            pl.BlockSpec((1, tile), lambda i: (0, i)),
            pl.BlockSpec((length, 1), lambda i: (0, 0)),
            rows(0),
            whole(1),
            rows(0),
            rows(0),
            whole(0),
            whole(0),
            pl.BlockSpec(gains.shape, lambda i: (0, 0)),
        ],
        out_specs=[
            pl.BlockSpec((length, 3 * head_dim), lambda i: (0, 0)),
            pl.BlockSpec((2, head_dim), lambda i: (0, 0)),
        ],
        out_shape=[
            jax.ShapeDtypeStruct((length, 3 * head_dim), BF16),
            jax.ShapeDtypeStruct((2, head_dim), F32),
        ],
        scratch_shapes=[
            pltpu.VMEM((head_dim, length), BF16),
            pltpu.VMEM((length, head_dim), F32),
            pltpu.VMEM((length, head_dim), F32),
        ],
        compiler_params=pltpu.CompilerParams(vmem_limit_bytes=VMEM_LIMIT),
        cost_estimate=pl.CostEstimate(
            flops=10 * length * length * head_dim,
            bytes_accessed=length * head_dim * 40,
            transcendentals=length * length,
        ),
        name="project_back",
    )(
        qkv, qkv, qkv, grad, out_f32, lse, segments.reshape(1, -1), segments.reshape(-1, 1),
        raw, raw, cos, sin, cos, sin, gains,
    )


def hidden_back_kernel(grads_ref, own_ref, near_ref, far_ref, cross_ref, hidden_ref, out_ref, gain_ref):
    uly = grads_ref.shape[0]
    u = lax.axis_index(ULY)
    near = u + 1 - 2 * lax.rem(u, 2)
    total = dot_nt(grads_ref[u], own_ref[...])
    total = total + dot_nt(grads_ref[near], near_ref[...])
    total = total + dot_nt(grads_ref[lax.rem(u + 2, uly)], far_ref[...])
    total = total + dot_nt(grads_ref[lax.rem(near + 2, uly)], cross_ref[...])
    out_ref[...] = total.astype(BF16).reshape(out_ref.shape)
    hidden = hidden_ref[...].reshape(total.shape).astype(F32)
    gain_ref[...] = jnp.sum(total * hidden, axis=0, keepdims=True)


def hidden_back(grads, own, near, far, cross, hidden):
    uly, tokens, columns = grads.shape
    blk, _, rows, width = hidden.shape
    tile = min(512, width)
    weights = pl.BlockSpec((tile, columns), lambda n: (n, 0))
    return pl.pallas_call(
        hidden_back_kernel,
        grid=(width // tile,),
        in_specs=[
            pl.BlockSpec(grads.shape, lambda n: (0, 0, 0)),
            *[weights] * 4,
            pl.BlockSpec((blk, 1, rows, tile), lambda n: (0, lax.axis_index(ULY), 0, n)),
        ],
        out_specs=[
            pl.BlockSpec((blk, rows, tile), lambda n: (0, 0, n)),
            pl.BlockSpec((1, tile), lambda n: (0, n)),
        ],
        out_shape=[
            jax.ShapeDtypeStruct((blk, rows, width), BF16),
            jax.ShapeDtypeStruct((1, width), F32),
        ],
        compiler_params=pltpu.CompilerParams(vmem_limit_bytes=VMEM_LIMIT),
        name="hidden_back",
    )(grads, own, near, far, cross, hidden)


def merge_heads_kernel(parts_ref, out_ref):
    blk, uly, _, columns = parts_ref.shape
    head_dim = columns // 3
    heads = blk * uly
    for z in range(blk):
        for u in range(uly):
            head = parts_ref[z, u].astype(F32)
            for part in range(3):
                at = (part * heads + u * blk + z) * head_dim
                out_ref[:, at : at + head_dim] = head[:, part * head_dim : (part + 1) * head_dim]


def merge_heads(parts):
    blk, uly, rows, columns = parts.shape
    return pl.pallas_call(
        merge_heads_kernel,
        out_shape=jax.ShapeDtypeStruct((rows, blk * uly * columns), F32),
        compiler_params=pltpu.CompilerParams(vmem_limit_bytes=VMEM_LIMIT),
        name="merge_heads",
    )(parts)


def swap(values, axis):
    return lax.all_to_all(values, axis, split_axis=0, concat_axis=0, tiled=True)


def sum_scatter(values, axis):
    count = spread(axis) if isinstance(axis, tuple) else lax.axis_size(axis)
    rows, width = values.shape
    parts = swap(values.astype(BF16).reshape(count, rows // count, width), axis)
    return jnp.sum(parts.astype(F32), axis=0)


def place(axes, index):
    found = {}
    for axis in reversed(axes):
        size = lax.axis_size(axis)
        found[axis] = lax.rem(index, size)
        index = index // size
    return found


def spread(axes):
    return math.prod(lax.axis_size(axis) for axis in axes)


def each(count, body):
    if count <= 4:
        for step in range(1, count):
            body(step)
    else:

        def looped(step, carried):
            body(step)
            return carried

        lax.fori_loop(1, count, looped, 0)


def ahead(index, step, size):
    return lax.rem(index + step, size)


def exchange(items, collective_id, after=()):
    count = len(items)
    sizes = [spread(axes) for _, axes, _ in items]
    groups = list(dict.fromkeys(axes for _, axes, _ in items))
    bases = [sum(2 * size for size in sizes[:i]) for i in range(count)]

    def kernel(*refs):
        ins = refs[:count]
        outs = refs[count + len(after) : 2 * count + len(after)]
        send, recv, local = refs[2 * count + len(after) :][:3]
        barrier = pltpu.get_barrier_semaphore()
        for axes in groups:
            size, me = spread(axes), lax.axis_index(axes)

            def greet(step, axes=axes, size=size, me=me):
                pl.semaphore_signal(
                    barrier, inc=1, device_id=place(axes, ahead(me, step, size)), device_id_type=MESH
                )

            each(size, greet)
        pl.semaphore_wait(barrier, sum(spread(axes) - 1 for axes in groups))

        def block(i, peer):
            if items[i][2] == "swap":
                return ins[i].at[peer]
            return ins[i].at[:, peer] if items[i][2] == "swap1" else ins[i]

        def remote(i, step):
            _, axes, kind = items[i]
            me = lax.axis_index(axes)
            if kind == "trade":
                return pltpu.make_async_remote_copy(
                    src_ref=ins[i],
                    dst_ref=outs[i],
                    send_sem=send.at[bases[i] + 1],
                    recv_sem=recv.at[bases[i] + 1],
                    device_id=place(axes, 1 - me),
                    device_id_type=MESH,
                )
            if kind == "relay":
                far, near = lax.rem(me + 2, 4), me + 1 - 2 * lax.rem(me, 2)
                held = far if step == 3 else me
                return pltpu.make_async_remote_copy(
                    src_ref=outs[i].at[far] if step == 3 else ins[i],
                    dst_ref=outs[i].at[held],
                    send_sem=send.at[bases[i] + step],
                    recv_sem=recv.at[bases[i] + step],
                    device_id=place(axes, far if step == 1 else near),
                    device_id_type=MESH,
                )
            peer = ahead(me, step, sizes[i])
            return pltpu.make_async_remote_copy(
                src_ref=block(i, peer),
                dst_ref=outs[i].at[me],
                send_sem=send.at[bases[i] + step],
                recv_sem=recv.at[bases[i] + step],
                device_id=place(axes, peer),
                device_id_type=MESH,
            )

        def own(i):
            _, axes, kind = items[i]
            me = lax.axis_index(axes)
            return pltpu.make_async_copy(
                block(i, me), outs[i].at[me], local.at[i]
            )

        def hop(i, up, hops):
            (axis,) = items[i][1]
            me, size = lax.axis_index(axis), sizes[i]
            way = 1 if up else -1
            held, to = me - way * hops, me + way
            exists = (held >= 0) & (held < size) & (to >= 0) & (to < size)
            held, to = jnp.clip(held, 0, size - 1), jnp.clip(to, 0, size - 1)
            sem = bases[i] + (size if up else 0) + hops
            copy = pltpu.make_async_remote_copy(
                src_ref=outs[i].at[held] if hops else ins[i],
                dst_ref=outs[i].at[held],
                send_sem=send.at[sem],
                recv_sem=recv.at[sem],
                device_id={axis: to},
                device_id_type=MESH,
            )
            return exists, copy

        def arrival(i, up, hops):
            (axis,) = items[i][1]
            me, size = lax.axis_index(axis), sizes[i]
            way = 1 if up else -1
            held, sender = me - way * (hops + 1), me - way
            exists = (held >= 0) & (held < size)
            held, sender = jnp.clip(held, 0, size - 1), jnp.clip(sender, 0, size - 1)
            sem = bases[i] + (size if up else 0) + hops
            copy = pltpu.make_async_remote_copy(
                src_ref=ins[i],
                dst_ref=outs[i].at[held],
                send_sem=send.at[sem],
                recv_sem=recv.at[sem],
                device_id={axis: sender},
                device_id_type=MESH,
            )
            return exists, copy

        def kinds(*names):
            return [i for i in range(count) if items[i][2] in names]

        def when(pair, act):
            exists, copy = pair
            pl.when(exists)(lambda: act(copy))

        def summed(i):
            (axis,) = items[i][1]
            me, size = lax.axis_index(axis), sizes[i]
            at = 2 * kinds("sum").index(i)
            got, sent = refs[2 * count + len(after) + 3 :][at : at + 2]

            def copy(up, target):
                to = jnp.clip(me + (1 if up else -1), 0, size - 1)
                sem = bases[i] + up * size + target
                return pltpu.make_async_remote_copy(
                    src_ref=sent.at[up, target],
                    dst_ref=got.at[up, target],
                    send_sem=send.at[sem],
                    recv_sem=recv.at[sem],
                    device_id={axis: to},
                    device_id_type=MESH,
                )

            def first(up):
                return (me == 0) if up else (me == size - 1)

            def beyond(up, target):
                return (me < target) if up else (me > target)

            for hops in range(size - 1):
                for up in (1, 0):
                    target = size - 1 - hops if up else hops

                    @pl.when(beyond(up, target) & first(up))
                    def _(up=up, target=target):
                        sent[up, target] = ins[i][target]

                    @pl.when(beyond(up, target) & jnp.logical_not(first(up)))
                    def _(up=up, target=target):
                        copy(up, target).wait_recv()
                        total = ins[i][target].astype(F32) + got[up, target].astype(F32)
                        sent[up, target] = total.astype(BF16)

                    pl.when(beyond(up, target))(lambda up=up, target=target: copy(up, target).start())

            def finish():
                outs[i][...] = ins[i][me].astype(F32)
                for target in range(size):
                    for up in (1, 0):

                        @pl.when((me == target) & jnp.logical_not(first(up)))
                        def _(up=up, target=target):
                            copy(up, target).wait_recv()
                            outs[i][...] += got[up, target].astype(F32)

                        pl.when(beyond(up, target))(lambda up=up, target=target: copy(up, target).wait_send())

            return finish

        ways = (True, False)
        finishes = []
        for i in kinds("line"):
            for up in ways:
                when(hop(i, up, 0), lambda copy: copy.start())
        for i in kinds("gather", "swap", "swap1", "relay", "trade"):
            each(3 if items[i][2] == "relay" else sizes[i], lambda step, i=i: remote(i, step).start())
        for i in kinds("gather", "swap", "swap1", "relay", "line"):
            own(i).start()
        for i in kinds("sum"):
            finishes.append(summed(i))
        for i in kinds("line"):
            for hops in range(1, sizes[i]):
                for up in ways:
                    when(arrival(i, up, hops - 1), lambda copy: copy.wait_recv())
                    if hops < sizes[i] - 1:
                        when(hop(i, up, hops), lambda copy: copy.start())
        for i in kinds("relay"):
            remote(i, 1).wait_recv()
            remote(i, 3).start()
            remote(i, 1).wait_send()
            for step in (2, 3):
                remote(i, step).wait()
        for i in kinds("gather", "swap", "swap1", "trade"):
            each(sizes[i], lambda step, i=i: remote(i, step).wait())
        for i in kinds("line"):
            for hops in range(sizes[i] - 1):
                for up in ways:
                    when(hop(i, up, hops), lambda copy: copy.wait_send())
        for i in kinds("gather", "swap", "swap1", "relay", "line"):
            own(i).wait()
        for finish in finishes:
            finish()


    def shape_of(size, array, kind):
        if kind in ("trade", "sum"):
            return array.shape[kind == "sum" :]
        dropped = {"swap": 0, "swap1": 1}.get(kind)
        return (size, *(extent for at, extent in enumerate(array.shape) if at != dropped))

    anywhere, near = pl.BlockSpec(memory_space=pl.ANY), pl.BlockSpec(memory_space=pltpu.VMEM)
    specs = [near if kind == "sum" else anywhere for _, _, kind in items]
    held = [pltpu.VMEM((2, *array.shape), BF16) for array, _, kind in items if kind == "sum"]
    return pl.pallas_call(
        kernel,
        in_specs=specs + [anywhere] * len(after),
        out_specs=specs,
        out_shape=[
            jax.ShapeDtypeStruct(shape_of(size, array, kind), F32 if kind == "sum" else array.dtype)
            for size, (array, _, kind) in zip(sizes, items)
        ],
        scratch_shapes=[
            pltpu.SemaphoreType.DMA((2 * sum(sizes),)),
            pltpu.SemaphoreType.DMA((2 * sum(sizes),)),
            pltpu.SemaphoreType.DMA((count,)),
            *[buffer for buffer in held for _ in range(2)],
        ],
        compiler_params=pltpu.CompilerParams(
            collective_id=collective_id, has_side_effects=True, vmem_limit_bytes=VMEM_LIMIT if held else None
        ),
        name="exchange",
    )(*[item[0] for item in items], *after)


def turn_gather_kernel(
    own_ref, other_ref, all_ref, all_t_ref, other_t_ref, block, turned, send, recv, local
):
    size, me = lax.axis_size("blk"), lax.axis_index("blk")
    rows = own_ref.shape[0]
    barrier = pltpu.get_barrier_semaphore()
    ways = (1, 0)

    def neighbour(up):
        to = me + (1 if up else -1)
        return (to >= 0) & (to < size), jnp.clip(to, 0, size - 1)

    def greet(step):
        pl.semaphore_signal(
            barrier, inc=1, device_id={"blk": ahead(me, step, size)}, device_id_type=MESH
        )

    each(size, greet)
    pl.semaphore_wait(barrier, size - 1)

    def hop(up, hops):
        held = me - (1 if up else -1) * hops
        exists, to = neighbour(up)
        exists = exists & (held >= 0) & (held < size)
        held = jnp.clip(held, 0, size - 1)
        return exists, pltpu.make_async_remote_copy(
            src_ref=all_ref.at[held] if hops else own_ref,
            dst_ref=all_ref.at[held],
            send_sem=send.at[up * size + hops],
            recv_sem=recv.at[up * size + hops],
            device_id={"blk": to},
            device_id_type=MESH,
        )

    def arrival(up, hops):
        held = me - (1 if up else -1) * (hops + 1)
        exists = (held >= 0) & (held < size)
        held = jnp.clip(held, 0, size - 1)
        return exists, held, pltpu.make_async_remote_copy(
            src_ref=own_ref,
            dst_ref=all_ref.at[held],
            send_sem=send.at[up * size + hops],
            recv_sem=recv.at[up * size + hops],
            device_id={"blk": neighbour(1 - up)[1]},
            device_id_type=MESH,
        )

    def when(pair, act):
        exists, copy = pair
        pl.when(exists)(lambda: act(copy))

    def turn(src, dst, at):
        take = pltpu.make_async_copy(src, block, local.at[0])
        take.start()
        take.wait()
        turned[...] = block[...].T
        columns = pl.ds(pl.multiple_of(at * rows, rows), rows)
        give = pltpu.make_async_copy(turned, dst.at[:, columns], local.at[1])
        give.start()
        give.wait()

    for up in ways:
        when(hop(up, 0), lambda copy: copy.start())
    keep = pltpu.make_async_copy(own_ref, all_ref.at[me], local.at[2])
    keep.start()
    turn(own_ref, all_t_ref, me)
    for at in range(size):
        turn(other_ref.at[at], other_t_ref, at)
    for hops in range(1, size):
        for up in ways:
            exists, held, copy = arrival(up, hops - 1)

            @pl.when(exists)
            def _(copy=copy, up=up, hops=hops):
                copy.wait_recv()
                if hops < size - 1:
                    when(hop(up, hops), lambda copy: copy.start())

        for up in ways:
            exists, held, copy = arrival(up, hops - 1)
            pl.when(exists)(lambda held=held: turn(all_ref.at[held], all_t_ref, held))
    for hops in range(size - 1):
        for up in ways:
            when(hop(up, hops), lambda copy: copy.wait_send())
    keep.wait()


def turn_gather(own, other, collective_id, after=()):
    size = lax.axis_size("blk")
    rows, width = own.shape
    anywhere = pl.BlockSpec(memory_space=pl.ANY)

    def kernel(*refs):
        turn_gather_kernel(*refs[:2], *refs[2 + len(after) :])

    return pl.pallas_call(
        kernel,
        in_specs=[anywhere] * (2 + len(after)),
        out_specs=[anywhere] * 3,
        out_shape=[
            jax.ShapeDtypeStruct((size, rows, width), BF16),
            jax.ShapeDtypeStruct((width, size * rows), BF16),
            jax.ShapeDtypeStruct((width, size * rows), BF16),
        ],
        scratch_shapes=[
            pltpu.VMEM((rows, width), BF16),
            pltpu.VMEM((width, rows), BF16),
            pltpu.SemaphoreType.DMA((2 * size,)),
            pltpu.SemaphoreType.DMA((2 * size,)),
            pltpu.SemaphoreType.DMA((3,)),
        ],
        compiler_params=pltpu.CompilerParams(
            collective_id=collective_id, has_side_effects=True, vmem_limit_bytes=VMEM_LIMIT
        ),
        name="turn_gather",
    )(own, other, *after)


def startup_kernel(
    head_ref, extra_ref, tok_ref, heads_ref, extras_ref, toks_ref,
    head_send, head_recv, extra_send, extra_recv, trade_send, trade_recv,
    z_send, z_recv, ay_send, ay_recv, by_send, by_recv, c_send, c_recv, local,
):
    blk, uly = lax.axis_size("blk"), spread(ULY)
    total = spread(ALL)
    z, u, me = lax.axis_index("blk"), lax.axis_index(ULY), lax.axis_index(ALL)
    far = lax.rem(u + 2, uly)
    near = u + 1 - 2 * lax.rem(u, 2)
    half = tok_ref.shape[0] // 2
    parts = (pl.ds(0, half), pl.ds(half, half))

    barrier = pltpu.get_barrier_semaphore()

    def greet(step):
        pl.semaphore_signal(
            barrier, inc=1, device_id=place(ALL, ahead(me, step, total)), device_id_type=MESH
        )

    each(total, greet)
    pl.semaphore_wait(barrier, total - 1)

    def send(src, dst, sent, got, to):
        return pltpu.make_async_remote_copy(
            src_ref=src, dst_ref=dst, send_sem=sent, recv_sem=got, device_id=to, device_id_type=MESH
        )

    def block(step, other, part):
        at = toks_ref.at[ahead(z, step, blk), far if other else u, parts[part]]
        return (tok_ref.at[parts[part]] if step == 0 and not other else at), at

    streams = ((0, 0), (0, 1), (1, 1))

    def hop(stream, up, hops):
        other, part = streams[stream]
        way = 1 if up else -1
        held, to = z - way * hops, z + way
        exists = (held >= 0) & (held < blk) & (to >= 0) & (to < blk)
        held, to = jnp.clip(held, 0, blk - 1), jnp.clip(to, 0, blk - 1)
        at = toks_ref.at[held, far if other else u, parts[part]]
        src = tok_ref.at[parts[part]] if hops == 0 and not other else at
        sem = (2 * stream + up) * blk + hops
        return exists, send(src, at, z_send.at[sem], z_recv.at[sem], {"blk": to})

    def arrival(stream, up, hops):
        other, part = streams[stream]
        way = 1 if up else -1
        held, sender = z - way * (hops + 1), z - way
        exists = (held >= 0) & (held < blk)
        held, sender = jnp.clip(held, 0, blk - 1), jnp.clip(sender, 0, blk - 1)
        at = toks_ref.at[held, far if other else u, parts[part]]
        sem = (2 * stream + up) * blk + hops
        return exists, send(tok_ref.at[parts[part]], at, z_send.at[sem], z_recv.at[sem], {"blk": sender})

    def when(pair, act):
        exists, copy = pair
        pl.when(exists)(lambda: act(copy))

    def a_y(step):
        return send(*block(step, 0, 0), ay_send.at[step], ay_recv.at[step], place(ULY, far))

    def b_y():
        return send(*block(0, 0, 1), by_send.at[0], by_recv.at[0], place(ULY, far))

    def to_near(step, other, part):
        sem = 4 * step + 2 * other + part
        return send(*block(step, other, part), c_send.at[sem], c_recv.at[sem], place(ULY, near))

    group = ("blk", *ULY)
    mine, here, b = lax.axis_index(group), spread(group), lax.axis_index("batch")

    def head(step):
        to = place(group, ahead(mine, step, here))
        src = head_ref.at[(to["y"] * lax.axis_size("core") + to["core"]) * blk + to["blk"]]
        return send(src, heads_ref.at[b, mine], head_send.at[step], head_recv.at[step], to)

    def extra(step):
        to = place(group, ahead(mine, step, here))
        return send(extra_ref, extras_ref.at[b, mine], extra_send.at[step], extra_recv.at[step], to)

    def trade(which):
        ref = (heads_ref, extras_ref)[which].at[b]
        return send(ref, ref, trade_send.at[which], trade_recv.at[which], {"batch": 1 - b})

    own = [
        pltpu.make_async_copy(tok_ref, toks_ref.at[z, u], local.at[0]),
        pltpu.make_async_copy(head_ref.at[u * blk + z], heads_ref.at[b, mine], local.at[1]),
        pltpu.make_async_copy(extra_ref, extras_ref.at[b, mine], local.at[2]),
    ]

    def start_head(step):
        extra(step).start()
        head(step).start()

    each(here, start_head)
    ways = (1, 0)
    b_y().start()
    for stream in range(2):
        for up in ways:
            when(hop(stream, up, 0), lambda copy: copy.start())
    a_y(0).start()
    to_near(0, 0, 0).start()
    to_near(0, 0, 1).start()

    for copy in own:
        copy.start()
    b_y().wait_recv()
    for up in ways:
        when(hop(2, up, 0), lambda copy: copy.start())
    to_near(0, 1, 1).start()
    def wait_head(step):
        extra(step).wait()
        head(step).wait()

    for hops in range(1, blk):
        if hops == min(2, blk - 1):
            each(here, wait_head)
            for copy in own[1:]:
                copy.wait()
            trade(0).start()
            trade(1).start()
        for stream, (other, part) in enumerate(streams):
            for up in ways:
                exists, copy = arrival(stream, up, hops - 1)
                step = blk - hops if up else hops

                @pl.when(exists)
                def _(copy=copy, stream=stream, other=other, part=part, up=up, step=step, hops=hops):
                    copy.wait_recv()
                    if hops < blk - 1:
                        when(hop(stream, up, hops), lambda copy: copy.start())
                    if stream == 0:
                        a_y(step).start()
                    to_near(step, other, part).start()

    for step in [0, *reversed(range(1, blk))]:
        a_y(step).wait_recv()
        to_near(step, 1, 0).start()
    for step in range(blk):
        for other in range(2):
            for part in range(2):
                to_near(step, other, part).wait_recv()

    trade(0).wait()
    trade(1).wait()
    own[0].wait()
    b_y().wait_send()
    for hops in range(blk - 1):
        for stream in range(3):
            for up in ways:
                when(hop(stream, up, hops), lambda copy: copy.wait_send())
    for step in range(blk):
        a_y(step).wait_send()
        for other in range(2):
            for part in range(2):
                to_near(step, other, part).wait_send()


def startup(heads, extra, tok, collective_id):
    batch, blk, uly = lax.axis_size("batch"), lax.axis_size("blk"), spread(ULY)
    anywhere = pl.BlockSpec(memory_space=pl.ANY)
    dma = pltpu.SemaphoreType.DMA
    return pl.pallas_call(
        startup_kernel,
        in_specs=[anywhere] * 3,
        out_specs=[anywhere] * 3,
        out_shape=[
            jax.ShapeDtypeStruct((batch, blk * uly, *heads.shape[1:]), BF16),
            jax.ShapeDtypeStruct((batch, blk * uly, *extra.shape), BF16),
            jax.ShapeDtypeStruct((blk, uly, *tok.shape), BF16),
        ],
        scratch_shapes=[
            *[dma((blk * uly,))] * 4,
            *[dma((2,))] * 2,
            *[dma((6 * blk,))] * 2,
            *[dma((blk,))] * 2,
            *[dma((1,))] * 2,
            *[dma((4 * blk,))] * 2,
            dma((3,)),
        ],
        compiler_params=pltpu.CompilerParams(collective_id=collective_id, has_side_effects=True),
        name="startup",
    )(heads, extra, tok)


def per_device_general(
    tokens, segments, routes, w_qkv, w_out, attn_gain, ffn_gain, qk_gain, router, w_gate_up, w_down, cotangent
):
    own_tokens = tokens[0]
    own_grad = cotangent[0]
    count_tok, width = own_tokens.shape
    head_dim = qk_gain.shape[1]
    heads = width // head_dim
    uly, blk, batch = spread(ULY), lax.axis_size("blk"), lax.axis_size("batch")
    blk_at, uly_at = lax.axis_index("blk"), lax.axis_index(ULY)
    group = batch * blk
    local_heads = heads // uly
    local_width = local_heads * head_dim
    rows = count_tok * uly
    seg_row = segments[0]
    length = seg_row.shape[0]
    number = router.shape[1]
    local_experts, _, units = w_down.shape
    shard_rows = w_qkv.shape[0]

    extra = jnp.concatenate([attn_gain[:, None], ffn_gain[:, None], router], axis=1)
    extra = jnp.pad(extra, ((0, 0), (0, LANES - extra.shape[1])))
    columns = w_qkv.reshape(shard_rows, 3, uly, local_width).transpose(2, 0, 1, 3)
    packed = jnp.concatenate(
        [
            columns.reshape(uly, shard_rows, 3 * local_width),
            jnp.broadcast_to(extra[None], (uly, shard_rows, LANES)),
        ],
        axis=2,
    )
    packed = swap(packed, ULY).reshape(uly * shard_rows, 3 * local_width + LANES)
    packed = lax.all_gather(packed, ROWS, axis=0, tiled=True)
    own_qkv = packed[:, : 3 * local_width]
    gain_attn = packed[:, 3 * local_width].astype(F32)
    gain_ffn = packed[:, 3 * local_width + 1].astype(F32)
    whole_router = packed[:, 3 * local_width + 2 : 3 * local_width + 2 + number]
    tokens_all = lax.all_gather(own_tokens, ULY, axis=0, tiled=True)
    to_rows = [(u * group + g, g * uly + u) for g in range(group) for u in range(uly)]
    own_out = lax.all_gather(lax.ppermute(w_out, ALL, to_rows), ROWS, axis=0, tiled=True)
    whole_gate_up = lax.all_gather(w_gate_up, PLANE, axis=0, tiled=False)
    whole_down = lax.all_gather(w_down, PLANE, axis=0, tiled=False)
    grad_blk = lax.all_gather(own_grad, "blk", axis=0, tiled=True)
    routes_blk = lax.all_gather(routes[0], "blk", axis=0, tiled=True)

    gain_query = qk_gain[0].astype(F32)
    gain_key = qk_gain[1].astype(F32)
    inputs_all = tokens_all.astype(F32)
    normed_one = inputs_all * rms_scale(inputs_all)
    hidden_one = (normed_one * gain_attn).astype(BF16)
    projected = dot_nn(hidden_one, own_qkv)
    query_raw = projected[:, :local_width].reshape(rows, local_heads, head_dim)
    key_raw = projected[:, local_width : 2 * local_width].reshape(rows, local_heads, head_dim)
    value_raw = projected[:, 2 * local_width :].reshape(rows, local_heads, head_dim)
    cos_table, sin_table = rope_tables(blk_at * rows, rows, head_dim)
    query_scale = rms_scale(query_raw)
    key_scale = rms_scale(key_raw)
    qkv = jnp.concatenate(
        [
            rotate(query_raw * query_scale * gain_query, cos_table, sin_table),
            rotate(key_raw * key_scale * gain_key, cos_table, sin_table),
            value_raw,
        ],
        axis=2,
    ).astype(BF16)
    qkv = qkv.transpose(1, 0, 2)

    by_heads = local_heads % blk == 0
    if by_heads:
        per = local_heads // blk

        def to_heads(values):
            columns = values.shape[2]
            moved = swap(values.reshape(blk, per, rows, columns), "blk")
            return moved.transpose(1, 0, 2, 3).reshape(per, length, columns)

        def to_rows_back(values):
            columns = values.shape[2]
            parts = values.reshape(per, blk, rows, columns).transpose(1, 0, 2, 3)
            return swap(parts, "blk").reshape(local_heads, rows, columns)

        q_src = kv_src = to_heads(qkv)
        cols = (0, 1, 2)
        seg_q = seg_row
        first_head = uly_at * local_heads + blk_at * per
    else:

        def to_heads(values):
            return values

        def to_rows_back(values):
            return values

        q_src = qkv
        kv_src = lax.all_gather(qkv[:, :, head_dim:], "blk", axis=1, tiled=True)
        cols = (0, 0, 1)
        seg_q = lax.dynamic_slice_in_dim(seg_row, blk_at * rows, rows)
        first_head = uly_at * local_heads
    attn_low, attn_f32, lse, top = attention_forward(q_src, kv_src, cols, seg_q, seg_row, head_dim)
    head_vector = lax.dynamic_update_slice_in_dim(
        jnp.full((heads,), NEG, F32), jnp.max(top, axis=(1, 2)) * head_dim**-0.5, first_head, 0
    )
    head_max = lax.pmax(head_vector, ALL)
    attn_rows = to_rows_back(attn_low)
    out_heads = own_out.reshape(local_heads, head_dim, width)
    branch = jnp.einsum("htc,hcd->td", attn_rows, out_heads, preferred_element_type=F32)
    inputs = own_tokens.astype(F32)
    mid = inputs + sum_scatter(branch, ULY)

    scale_two = rms_scale(mid)
    normed_two = mid * scale_two
    hidden_two = (normed_two * gain_ffn).astype(BF16)
    hidden_blk = lax.all_gather(hidden_two, "blk", axis=0, tiled=True)
    probs_blk = jax.nn.softmax(dot_nn(hidden_blk, whole_router), axis=1)
    names = jnp.arange(number, dtype=jnp.int32)
    chosen_blk = jnp.any(routes_blk[:, :, None] == names, axis=1).astype(F32)
    own_names = blk_at * local_experts
    gates = lax.dynamic_slice_in_dim(probs_blk * chosen_blk, own_names, local_experts, axis=1)
    most = min(MOST_TOKENS, hidden_blk.shape[0])
    packed_weights = jax.vmap(pack_experts)(whole_gate_up, whole_down)
    made = []
    for at in range(0, hidden_blk.shape[0], most):
        hidden_part, grad_part = hidden_blk[at : at + most], grad_blk[at : at + most]
        made.append(
            experts(
                hidden_part,
                hidden_part.T,
                grad_part,
                grad_part.T,
                gates[at : at + most],
                packed_weights,
            )
        )
    out_part = jnp.concatenate([m[0] for m in made], axis=0)
    dx_part = jnp.concatenate([m[1] for m in made], axis=0)
    dg_part = jnp.concatenate([m[2] for m in made], axis=1)
    expert_grads = sum(m[3].astype(F32) for m in made).astype(BF16)
    expert_sums = lax.psum_scatter(expert_grads, PLANE, scatter_dimension=0, tiled=False).astype(F32)
    grad_gate_up = jnp.concatenate([expert_sums[0], expert_sums[1]], axis=2)
    grad_down = expert_sums[2]
    dg_parts = swap(dg_part.reshape(local_experts, blk, count_tok).transpose(1, 2, 0), "blk")
    grad_gates = dg_parts.transpose(1, 0, 2).reshape(count_tok, number)
    dx_sum = sum_scatter(dx_part, "blk")
    output = (mid + sum_scatter(out_part, "blk")).astype(BF16)
    router_probs = lax.dynamic_slice_in_dim(probs_blk, blk_at * count_tok, count_tok)
    chosen = lax.dynamic_slice_in_dim(chosen_blk, blk_at * count_tok, count_tok)
    grad_probs = chosen * grad_gates
    grad_logits = (
        router_probs * (grad_probs - jnp.sum(router_probs * grad_probs, axis=1, keepdims=True))
    ).astype(BF16)
    grad_hidden_two = dx_sum + dot_nt(grad_logits, whole_router)
    grad_router_part = dot_tn(hidden_two, grad_logits)
    grad_gain_ffn = jnp.sum(grad_hidden_two * normed_two, axis=0)
    grad_mid = own_grad.astype(F32) + norm_back(grad_hidden_two * gain_ffn, mid, scale_two)

    branch_grad = lax.all_gather(grad_mid.astype(BF16), ULY, axis=0, tiled=True)
    grad_attn = dot_nt(branch_grad, own_out).astype(BF16)
    grad_attn = to_heads(grad_attn.reshape(rows, local_heads, head_dim).transpose(1, 0, 2))
    grad_out_part = jnp.einsum("htc,td->hcd", attn_rows, branch_grad, preferred_element_type=F32)
    dq, dk, dv = attention_backward(
        q_src, kv_src, cols, grad_attn, attn_f32, lse, seg_q, seg_row, head_dim
    )
    if by_heads:
        dqkv = to_rows_back(jnp.concatenate([dq, dk, dv], axis=2))
        dq, dk, dv = jnp.split(dqkv, 3, axis=2)
    else:
        dk, dv = (lax.psum_scatter(g, "blk", scatter_dimension=1, tiled=True) for g in (dk, dv))
    dq, dk, dv = (g.transpose(1, 0, 2) for g in (dq, dk, dv))
    grad_query_norm = rotate(dq.astype(F32), cos_table, -sin_table)
    grad_key_norm = rotate(dk.astype(F32), cos_table, -sin_table)
    grad_gain_query = jnp.sum(grad_query_norm * (query_raw * query_scale), axis=(0, 1))
    grad_gain_key = jnp.sum(grad_key_norm * (key_raw * key_scale), axis=(0, 1))
    grad_projected = jnp.concatenate(
        [
            norm_back(grad_query_norm * gain_query, query_raw, query_scale)
            .reshape(rows, local_width)
            .astype(BF16),
            norm_back(grad_key_norm * gain_key, key_raw, key_scale)
            .reshape(rows, local_width)
            .astype(BF16),
            dv.reshape(rows, local_width),
        ],
        axis=1,
    )
    grad_hidden_part = dot_nt(grad_projected, own_qkv)
    grad_hidden_one = sum_scatter(grad_hidden_part, ULY)
    grad_gain_attn = jnp.sum(grad_hidden_part * normed_one, axis=0)
    grad_inputs = grad_mid + norm_back(grad_hidden_one * gain_attn, inputs, rms_scale(inputs))

    grad_qkv_part = dot_tn(hidden_one, grad_projected).astype(BF16)
    grad_qkv_rows = lax.psum_scatter(grad_qkv_part, ROWS, scatter_dimension=0, tiled=True)
    grad_qkv_rows = swap(grad_qkv_rows.reshape(uly, shard_rows, 3 * local_width), ULY)
    grad_qkv = (
        grad_qkv_rows.reshape(uly, shard_rows, 3, local_width)
        .transpose(1, 2, 0, 3)
        .reshape(shard_rows, 3 * width)
        .astype(F32)
    )
    grad_out_rows = lax.psum_scatter(
        grad_out_part.reshape(local_width, width).astype(BF16), ROWS, scatter_dimension=0, tiled=True
    )
    grad_out = lax.ppermute(grad_out_rows, ALL, [(b, a) for a, b in to_rows]).astype(F32)
    small = jnp.concatenate([grad_gain_attn[:, None], grad_gain_ffn[:, None], grad_router_part], axis=1)
    small = lax.psum_scatter(small, ALL, scatter_dimension=0, tiled=True)
    grad_qk_gain = lax.psum(jnp.stack([grad_gain_query, grad_gain_key]), ALL)

    clip_gamma = TAU / jnp.maximum(head_max, TAU)
    factor = jnp.repeat(jnp.sqrt(clip_gamma), head_dim)
    column_scale = jnp.concatenate([factor, factor, jnp.ones((width,), F32)])
    clipped = w_qkv.astype(F32) * column_scale[None, :]
    return (
        output[None],
        grad_inputs[None],
        grad_qkv,
        grad_out,
        small[:, 0],
        small[:, 1],
        grad_qk_gain,
        small[:, 2:],
        grad_gate_up,
        grad_down,
        clipped,
    )


def per_device(
    tokens, segments, routes, w_qkv, w_out, attn_gain, ffn_gain, qk_gain, router, w_gate_up, w_down, cotangent
):
    own_tokens = tokens[0]
    own_grad = cotangent[0]
    count_tok, width = own_tokens.shape
    head_dim = qk_gain.shape[1]
    heads = width // head_dim
    batch, blk, uly = lax.axis_size("batch"), lax.axis_size("blk"), spread(ULY)
    total, group = batch * blk * uly, batch * blk
    local_experts = w_down.shape[0]
    if uly != 4 or heads != blk * uly or blk < 2 or batch != 2 or local_experts % 2:
        return per_device_general(
            tokens, segments, routes, w_qkv, w_out, attn_gain, ffn_gain, qk_gain, router, w_gate_up, w_down, cotangent
        )
    blk_at, uly_at = lax.axis_index("blk"), lax.axis_index(ULY)
    rows = count_tok * uly
    seg_row = segments[0]
    length = seg_row.shape[0]
    number = router.shape[1]
    shard_rows = w_qkv.shape[0]

    to_rows = [(u * group + g, g * uly + u) for g in range(group) for u in range(uly)]
    own_rows = lax.ppermute(w_out, ALL, to_rows)
    half = local_experts // 2


    def gather_experts(gate_up, down):
        return lax.all_gather(pack_experts(gate_up, down), PLANE, axis=0, tiled=False)

    weights_first = gather_experts(w_gate_up[:half], w_down[:half])
    extra = jnp.concatenate([attn_gain[None], ffn_gain[None], router.T], axis=0)
    kept = extra.shape[0]
    extra = jnp.pad(extra, ((0, -kept % 16), (0, -shard_rows % LANES)))
    by_head = w_qkv.reshape(shard_rows, 3, heads, head_dim).transpose(2, 0, 1, 3)
    own_qkv, extras, toks = startup(
        by_head.reshape(heads, shard_rows, 3 * head_dim), extra, own_tokens, 0
    )
    own_rows, extras, later_gate_up, later_down = lax.optimization_barrier(
        (own_rows, extras, w_gate_up[half:], w_down[half:])
    )
    weights_second = gather_experts(later_gate_up, later_down)
    own_out = lax.all_to_all(
        jnp.broadcast_to(own_rows[None], (group, *own_rows.shape)), ROWS, split_axis=0, concat_axis=0, tiled=True
    ).reshape(blk, head_dim, width)
    own_qkv = own_qkv.reshape(width, 3 * head_dim)
    extras = extras.reshape(total, *extra.shape)[:, :kept, :shard_rows]
    extras = extras.transpose(1, 0, 2).reshape(kept, width)
    gain_attn = extras[0].astype(F32)
    gain_ffn = extras[1].astype(F32)
    router_t = extras[2:]

    gains = qk_gain.astype(F32)
    cos, sin = rope_rows(length, head_dim)
    hidden_one, qkv, raw = project(
        toks.reshape(length, width), gain_attn[None], own_qkv, cos, sin, gains
    )
    attn_low, attn_f32, lse, top = attention_forward(
        qkv[None], qkv[None], (0, 1, 2), seg_row, seg_row, head_dim
    )
    (attn_rows,) = exchange([(attn_low.reshape(blk, rows, head_dim), ("blk",), "swap")], 1)
    branch = jnp.einsum("htc,hcd->td", attn_rows, own_out, preferred_element_type=F32)
    branch, grad_blk, routes_blk = exchange(
        [
            (branch.astype(BF16).reshape(uly, count_tok, width), ULY, "swap"),
            (own_grad, ("blk",), "line"),
            (routes[0].T, ("blk",), "gather"),
        ],
        2,
    )
    inputs = own_tokens.astype(F32)
    mid = inputs + jnp.sum(branch.astype(F32), axis=0)

    scale_two = rms_scale(mid)
    normed_two = mid * scale_two
    hidden_two = (normed_two * gain_ffn).astype(BF16)
    hidden_blk, hidden_t, grad_t = turn_gather(hidden_two, grad_blk, 3, after=[weights_first])
    tokens_blk = blk * count_tok
    hidden_blk = hidden_blk.reshape(tokens_blk, width)
    grad_blk = grad_blk.reshape(tokens_blk, width)
    probs_blk = jax.nn.softmax(dot_nt(hidden_blk, router_t), axis=1)
    names = jnp.arange(number, dtype=jnp.int32)
    chosen_blk = jnp.any(routes_blk[:, :, :, None] == names, axis=1).astype(F32)
    chosen_blk = chosen_blk.reshape(tokens_blk, number)
    gates = lax.dynamic_slice_in_dim(
        probs_blk * chosen_blk, blk_at * local_experts, local_experts, axis=1
    )
    shared = (hidden_blk, hidden_t, grad_blk, grad_t)
    out_first, dx_first, dg_first, grads_first = experts(*shared, gates[:, :half], weights_first)
    sums_first = lax.psum_scatter(grads_first, PLANE, scatter_dimension=0, tiled=False)
    out_part, dx_part, dg_second, grads_second = experts(
        *shared, gates[:, half:], weights_second, before=(out_first, dx_first)
    )
    sums_second = lax.psum_scatter(grads_second, PLANE, scatter_dimension=0, tiled=False)
    finished = finish_experts(sums_first, 0, local_experts)
    grad_gate_up, grad_down = finish_experts(sums_second, half, local_experts, before=finished)
    dg_part = jnp.concatenate([dg_first, dg_second], axis=0).reshape(local_experts, blk, count_tok)
    dx_sum, dg_parts = exchange(
        [
            (dx_part.reshape(blk, count_tok, width), ("blk",), "sum"),
            (dg_part.transpose(1, 0, 2), ("blk",), "swap"),
        ],
        4,
    )
    out_part = out_part.reshape(blk, count_tok, width)
    out_part, dx_sum = lax.optimization_barrier((out_part, dx_sum))
    out_parts = lax.all_to_all(out_part, "blk", split_axis=0, concat_axis=0, tiled=True)
    output = (mid + jnp.sum(out_parts.astype(F32), axis=0)).astype(BF16)
    router_probs = lax.dynamic_slice_in_dim(probs_blk, blk_at * count_tok, count_tok)
    chosen = lax.dynamic_slice_in_dim(chosen_blk, blk_at * count_tok, count_tok)
    grad_probs = chosen * dg_parts.reshape(number, count_tok).T
    grad_logits = (
        router_probs * (grad_probs - jnp.sum(router_probs * grad_probs, axis=1, keepdims=True))
    ).astype(BF16)
    grad_hidden_two = dx_sum + dot_nn(grad_logits, router_t)
    grad_router_t = dot_tn(grad_logits, hidden_two)
    grad_gain_ffn = jnp.sum(grad_hidden_two * normed_two, axis=0)
    grad_mid = own_grad.astype(F32) + norm_back(grad_hidden_two * gain_ffn, mid, scale_two)

    (branch_grad,) = exchange([(grad_mid.astype(BF16), ULY, "relay")], 5)
    branch_grad, sent_qkv = lax.optimization_barrier((branch_grad, own_qkv))
    far_qkv = lax.ppermute(sent_qkv, "y", [(0, 1), (1, 0)])
    branch_grad = branch_grad.reshape(rows, width)
    grad_attn = jnp.einsum("td,hcd->htc", branch_grad, own_out, preferred_element_type=F32).astype(BF16)
    small = jnp.concatenate([grad_gain_ffn[None], grad_router_t], axis=0)
    small = small.reshape(kept - 1, total, shard_rows).transpose(1, 0, 2)
    small = jnp.pad(small, ((0, 0), (0, 0), (0, LANES - shard_rows)))
    head_row = jnp.where(
        jnp.arange(LANES) == uly_at * blk + blk_at, jnp.max(top) * head_dim**-0.5, NEG
    )
    small = jnp.concatenate([small, jnp.broadcast_to(head_row, (total, 1, LANES))], axis=1)
    small = jnp.pad(small, ((0, 0), (0, -kept % 8), (0, 0)))
    grad_out_part = jnp.einsum("htc,td->hcd", attn_rows, branch_grad, preferred_element_type=F32)
    grad_out_part = grad_out_part.astype(BF16).reshape(batch, blk, shard_rows, width)
    batch_at = lax.axis_index("batch")
    grad_attn, got_out_part, small = exchange(
        [
            (grad_attn, ("blk",), "swap"),
            (
                lax.dynamic_index_in_dim(grad_out_part, 1 - batch_at, 0, keepdims=False),
                ("batch",),
                "trade",
            ),
            (small, ALL, "swap"),
        ],
        6,
        after=[out_parts],
    )
    grad_out_part = lax.dynamic_index_in_dim(grad_out_part, batch_at, 0, keepdims=False) + got_out_part
    grad_projected, grad_gains = project_back(
        qkv, grad_attn.reshape(length, head_dim), attn_f32, lse, seg_row, raw, cos, sin, gains
    )
    grad_qkv_part = dot_tn(hidden_one, grad_projected).astype(BF16)
    by_batch = grad_qkv_part.reshape(batch, width // batch, 3 * head_dim)
    projected_blk, got_qkv_part, near_qkv, cross_qkv, grad_out_parts = exchange(
        [
            (grad_projected.reshape(blk, uly, count_tok, 3 * head_dim), ULY, "swap1"),
            (
                lax.dynamic_index_in_dim(by_batch, 1 - batch_at, 0, keepdims=False),
                ("batch",),
                "trade",
            ),
            (own_qkv, ("core",), "trade"),
            (far_qkv, ("core",), "trade"),
            (grad_out_part, ("blk",), "swap"),
        ],
        7,
    )
    grad_out = lax.ppermute(
        jnp.sum(grad_out_parts.astype(F32), axis=0).astype(BF16), ALL, [(b, a) for a, b in to_rows]
    ).astype(F32)
    grad_qkv_part = lax.dynamic_index_in_dim(by_batch, batch_at, 0, keepdims=False) + got_qkv_part

    grad_hidden_part, grad_gain_attn = hidden_back(
        projected_blk.reshape(uly, tokens_blk, 3 * head_dim),
        own_qkv,
        near_qkv,
        far_qkv,
        cross_qkv,
        hidden_one.reshape(blk, uly, count_tok, width),
    )
    grad_gain_attn = grad_gain_attn[0] / gain_attn

    gains_out = jnp.pad(
        grad_gain_attn.reshape(total, 1, shard_rows), ((0, 0), (0, 0), (0, LANES - shard_rows))
    )
    gains_out = jnp.concatenate([gains_out, jnp.broadcast_to(grad_gains, (total, 2, LANES))], axis=1)
    gains_out = jnp.pad(gains_out, ((0, 0), (0, 5), (0, 0)))
    grad_hidden_one, gains_out, grad_qkv_parts = exchange(
        [
            (grad_hidden_part, ("blk",), "sum"),
            (gains_out, ALL, "swap"),
            (grad_qkv_part.reshape(total // batch, shard_rows, 3 * head_dim), ("blk", *ULY), "swap"),
        ],
        8,
        after=[finished[0]],
    )
    grad_qkv = merge_heads(grad_qkv_parts.reshape(blk, uly, shard_rows, 3 * head_dim))
    grad_inputs = grad_mid + norm_back(grad_hidden_one * gain_attn, inputs, rms_scale(inputs))
    sums = jnp.sum(small, axis=0)
    gains = jnp.sum(gains_out, axis=0)
    head_max = jnp.max(small[:, kept - 1, :heads], axis=0)
    factor = jnp.repeat(jnp.sqrt(TAU / jnp.maximum(head_max, TAU)), head_dim)
    column_scale = jnp.concatenate([factor, factor, jnp.ones((width,), F32)])
    clipped = w_qkv.astype(F32) * column_scale[None, :]
    return (
        output[None],
        grad_inputs[None],
        grad_qkv,
        grad_out,
        gains[0, :shard_rows],
        sums[0, :shard_rows],
        gains[1:3],
        sums[1 : kept - 1, :shard_rows].T,
        grad_gate_up,
        grad_down,
        clipped,
    )


def solution(mesh):
    in_specs = (
        P("batch", ("blk", *ULY), None),
        P("batch", None),
        P("batch", ("blk", *ULY), None),
        P(ALL, None),
        P(ALL, None),
        P(ALL),
        P(ALL),
        P(),
        P(ALL, None),
        P("blk", PLANE, None),
        P("blk", PLANE, None),
        P("batch", ("blk", *ULY), None),
    )
    out_specs = (
        P("batch", ("blk", *ULY), None),
        P("batch", ("blk", *ULY), None),
        P(ALL, None),
        P(ALL, None),
        P(ALL),
        P(ALL),
        P(),
        P(ALL, None),
        P("blk", PLANE, None),
        P("blk", PLANE, None),
        P(ALL, None),
    )
    cores = 2 - mesh.shape["uly"] % 2
    mesh = Mesh(
        mesh.devices.reshape(*(mesh.shape[axis] for axis in ROWS), mesh.shape["uly"] // cores, cores), ALL
    )
    return jax.shard_map(
        per_device, mesh=mesh, in_specs=in_specs, out_specs=out_specs, check_vma=False
    )
```

```python
import functools
import math

import jax
import jax.numpy as jnp
from jax import lax
from jax.experimental import pallas as pl
from jax.experimental.pallas import tpu as pltpu
from jax.sharding import Mesh
from jax.sharding import PartitionSpec as P

EPS = 1e-06
THETA = 50000.0
TAU = 4.0
NEG = -1e30
LOG2E = 1.4426950408889634
LANES = 128
MOST_TOKENS = 512
VMEM_LIMIT = 60 * 1024 * 1024

ULY = ("y", "core")
ALL = ("batch", "blk", *ULY)
ROWS = ("batch", "blk")
PLANE = ("batch", *ULY)
CHIPS = ("batch", "y")

MESH = pl.DeviceIdType.MESH
BF16 = jnp.bfloat16
F32 = jnp.float32


def rms_scale(values):
    return lax.rsqrt(jnp.mean(values * values, axis=-1, keepdims=True) + EPS)


def norm_back(grad_normed, values, scale):
    normed = values * scale
    return scale * (grad_normed - normed * jnp.mean(grad_normed * normed, axis=-1, keepdims=True))


def rope_tables(offset, length, head_dim):
    half_dim = head_dim // 2
    frequency = THETA ** (-jnp.arange(half_dim, dtype=F32) * 2.0 / head_dim)
    positions = (offset + jnp.arange(length, dtype=jnp.int32)).astype(F32)
    angles = positions[:, None] * frequency[None, :]
    return (jnp.cos(angles)[:, None, :], jnp.sin(angles)[:, None, :])


def rope_rows(length, head_dim):
    fine = math.gcd(length, LANES)
    frequency = THETA ** (-jnp.arange(head_dim // 2, dtype=F32) * 2.0 / head_dim)
    frequency = jnp.concatenate([frequency, frequency])
    coarse_angle = (jnp.arange(length // fine, dtype=F32) * fine)[:, None, None] * frequency
    fine_angle = jnp.arange(fine, dtype=F32)[None, :, None] * frequency
    cos_a, sin_a, cos_b, sin_b = lax.optimization_barrier(
        (jnp.cos(coarse_angle), jnp.sin(coarse_angle), jnp.cos(fine_angle), jnp.sin(fine_angle))
    )
    sign = jnp.where(jnp.arange(head_dim) < head_dim // 2, -1.0, 1.0)
    cos = cos_a * cos_b - sin_a * sin_b
    sin = (sin_a * cos_b + cos_a * sin_b) * sign
    return cos.reshape(length, head_dim), sin.reshape(length, head_dim)


def rotate(values, cos_table, sin_table):
    half_dim = values.shape[-1] // 2
    first = values[..., :half_dim]
    second = values[..., half_dim:]
    return jnp.concatenate(
        [first * cos_table - second * sin_table, second * cos_table + first * sin_table], axis=-1
    )


def dot_nn(a, b):
    return lax.dot_general(a, b, (((1,), (0,)), ((), ())), preferred_element_type=F32)


def dot_nt(a, b):
    return lax.dot_general(a, b, (((1,), (1,)), ((), ())), preferred_element_type=F32)


def dot_tn(a, b):
    return lax.dot_general(a, b, (((0,), (0,)), ((), ())), preferred_element_type=F32)


def key_chunks(length):
    size = min(512, length)
    return size, length // size


def attn_fwd_kernel(factor, q_ref, k_ref, v_ref, sq_ref, sk_ref, o_ref, of_ref, lse_ref, top_ref, vt_ref):
    length = k_ref.shape[1]
    size, count = key_chunks(length)
    tile, head_dim = q_ref.shape[1:]

    @pl.when(pl.program_id(1) == 0)
    def _():
        vt_ref[...] = v_ref[0].astype(F32).T.astype(BF16)

    q = q_ref[0]
    seg_q = sq_ref[...]

    def step(j, carried):
        total, top, acc = carried
        at = pl.multiple_of(j * size, size)
        scores = dot_nt(k_ref[0, pl.ds(at, size), :], q)
        scores = jnp.where(sk_ref[pl.ds(at, size), :] == seg_q, scores, NEG)
        top = jnp.maximum(top, jnp.max(scores, axis=0, keepdims=True))
        weights = jnp.exp2(scores * factor)
        total = total + jnp.sum(weights, axis=0, keepdims=True)
        acc = acc + dot_nn(vt_ref[:, pl.ds(at, size)], weights.astype(BF16))
        return total, top, acc

    start = (
        jnp.zeros((1, tile), F32),
        jnp.full((1, tile), NEG, F32),
        jnp.zeros((head_dim, tile), F32),
    )
    total, top, acc = lax.fori_loop(0, count, step, start, unroll=count <= 4)
    out = (acc * (1.0 / total)).T
    o_ref[0] = out.astype(BF16)
    of_ref[0] = out
    lse_ref[0] = jnp.log2(total)
    top_ref[0] = top


def attn_bwd_kernel(
    factor, scale, q_ref, k_ref, v_ref, do_ref, of_ref, lse_ref, sq_ref, sk_ref,
    dq_ref, dk_ref, dv_ref, kt_ref, dk_acc, dv_acc,
):
    length = k_ref.shape[1]
    size, count = key_chunks(length)
    tile, head_dim = q_ref.shape[1:]

    @pl.when(pl.program_id(1) == 0)
    def _():
        kt_ref[...] = k_ref[0].astype(F32).T.astype(BF16)
        dk_acc[...] = jnp.zeros_like(dk_acc)
        dv_acc[...] = jnp.zeros_like(dv_acc)

    q = q_ref[0]
    grad = do_ref[0]
    seg_q = sq_ref[...]
    lse = lse_ref[0]
    row_dot = jnp.sum((grad.astype(F32) * of_ref[0]).T, axis=0, keepdims=True)

    def step(j, dq_t):
        at = pl.multiple_of(j * size, size)
        rows = pl.ds(at, size)
        scores = dot_nt(k_ref[0, rows, :], q)
        scores = jnp.where(sk_ref[rows, :] == seg_q, scores, NEG)
        weights = jnp.exp2(scores * factor - lse)
        grad_weights = dot_nt(v_ref[0, rows, :], grad)
        grad_scores = (weights * (grad_weights - row_dot)).astype(BF16)
        dk_acc[rows, :] += dot_nn(grad_scores, q)
        dv_acc[rows, :] += dot_nn(weights.astype(BF16), grad)
        return dq_t + dot_nn(kt_ref[:, rows], grad_scores)

    dq_t = lax.fori_loop(0, count, step, jnp.zeros((head_dim, tile), F32), unroll=count <= 4)
    dq_ref[0] = (dq_t * scale).T.astype(BF16)

    @pl.when(pl.program_id(1) == pl.num_programs(1) - 1)
    def _():
        dk_ref[0] = (dk_acc[...] * scale).astype(BF16)
        dv_ref[0] = dv_acc[...].astype(BF16)


def attention_tile(queries, length):
    return min(queries, 256 if length <= 4096 else 128)


def attention_forward(q_src, kv_src, cols, seg_q, seg_k, head_dim):
    heads, queries = q_src.shape[:2]
    length = kv_src.shape[1]
    tile = attention_tile(queries, length)
    q_col, k_col, v_col = cols
    factor = head_dim**-0.5 * LOG2E
    row = pl.BlockSpec((1, 1, tile), lambda h, i: (h, 0, i))
    block = pl.BlockSpec((1, tile, head_dim), lambda h, i: (h, i, 0))
    return pl.pallas_call(
        functools.partial(attn_fwd_kernel, factor),
        grid=(heads, queries // tile),
        in_specs=[
            pl.BlockSpec((1, tile, head_dim), lambda h, i: (h, i, q_col)),
            pl.BlockSpec((1, length, head_dim), lambda h, i: (h, 0, k_col)),
            pl.BlockSpec((1, length, head_dim), lambda h, i: (h, 0, v_col)),
            pl.BlockSpec((1, tile), lambda h, i: (0, i)),
            pl.BlockSpec((length, 1), lambda h, i: (0, 0)),
        ],
        out_specs=[block, block, row, row],
        out_shape=[
            jax.ShapeDtypeStruct((heads, queries, head_dim), BF16),
            jax.ShapeDtypeStruct((heads, queries, head_dim), F32),
            jax.ShapeDtypeStruct((heads, 1, queries), F32),
            jax.ShapeDtypeStruct((heads, 1, queries), F32),
        ],
        scratch_shapes=[pltpu.VMEM((head_dim, length), BF16)],
        compiler_params=pltpu.CompilerParams(vmem_limit_bytes=VMEM_LIMIT),
        cost_estimate=pl.CostEstimate(
            flops=4 * heads * queries * length * head_dim,
            bytes_accessed=heads * (queries + length) * head_dim * 8,
            transcendentals=heads * queries * length,
        ),
        name="attend",
    )(q_src, kv_src, kv_src, seg_q.reshape(1, -1), seg_k.reshape(-1, 1))


def attention_backward(q_src, kv_src, cols, grad, out_f32, lse, seg_q, seg_k, head_dim):
    heads, queries = q_src.shape[:2]
    length = kv_src.shape[1]
    tile = attention_tile(queries, length)
    q_col, k_col, v_col = cols
    scale = head_dim**-0.5
    row = pl.BlockSpec((1, 1, tile), lambda h, i: (h, 0, i))
    block = pl.BlockSpec((1, tile, head_dim), lambda h, i: (h, i, 0))
    whole = pl.BlockSpec((1, length, head_dim), lambda h, i: (h, 0, 0))
    return pl.pallas_call(
        functools.partial(attn_bwd_kernel, scale * LOG2E, scale),
        grid=(heads, queries // tile),
        in_specs=[
            pl.BlockSpec((1, tile, head_dim), lambda h, i: (h, i, q_col)),
            pl.BlockSpec((1, length, head_dim), lambda h, i: (h, 0, k_col)),
            pl.BlockSpec((1, length, head_dim), lambda h, i: (h, 0, v_col)),
            block,
            block,
            row,
            pl.BlockSpec((1, tile), lambda h, i: (0, i)),
            pl.BlockSpec((length, 1), lambda h, i: (0, 0)),
        ],
        out_specs=[block, whole, whole],
        out_shape=[
            jax.ShapeDtypeStruct((heads, queries, head_dim), BF16),
            jax.ShapeDtypeStruct((heads, length, head_dim), BF16),
            jax.ShapeDtypeStruct((heads, length, head_dim), BF16),
        ],
        scratch_shapes=[
            pltpu.VMEM((head_dim, length), BF16),
            pltpu.VMEM((length, head_dim), F32),
            pltpu.VMEM((length, head_dim), F32),
        ],
        compiler_params=pltpu.CompilerParams(vmem_limit_bytes=VMEM_LIMIT),
        cost_estimate=pl.CostEstimate(
            flops=10 * heads * queries * length * head_dim,
            bytes_accessed=heads * (queries + length) * head_dim * 12,
            transcendentals=heads * queries * length,
        ),
        name="attend_back",
    )(q_src, kv_src, kv_src, grad, out_f32, lse, seg_q.reshape(1, -1), seg_k.reshape(-1, 1))


def expert_step(expert, h_ref, ht_ref, dy_ref, dyt_ref, gate_ref, wg_ref, wu_ref, wd_ref, dg_ref, out_acc, dx_acc):
    width = h_ref.shape[1]
    cols = wg_ref.shape[3]
    w_gate = wg_ref[...].reshape(width, cols)
    w_up = wu_ref[...].reshape(width, cols)
    w_down = wd_ref[...].reshape(width, cols)
    gates = gate_ref[...]
    mine = lax.broadcasted_iota(jnp.int32, gates.shape, 1) == expert
    gate = jnp.sum(jnp.where(mine, gates, 0.0), axis=1, keepdims=True)
    a_gate = dot_nn(h_ref[...], w_gate)
    a_up = dot_nn(h_ref[...], w_up)
    raw = dot_nn(dy_ref[...], w_down)
    sigma = 1.0 / (1.0 + jnp.exp2(a_gate * -LOG2E))
    swish = a_gate * sigma
    act = swish * a_up
    dg_ref[0] += jnp.sum(raw * act, axis=1, keepdims=True)
    gated = (gate * act).astype(BF16)
    d_act = gate * raw
    d_gate = (d_act * a_up * (sigma + swish * (1.0 - sigma))).astype(BF16)
    d_up = (d_act * swish).astype(BF16)
    out_acc[...] += dot_nt(gated, w_down)
    dx_acc[...] += dot_nt(d_gate, w_gate) + dot_nt(d_up, w_up)
    for part, (left, right) in enumerate([(ht_ref, d_gate), (ht_ref, d_up), (dyt_ref, gated)]):
        yield part, dot_nn(left[...], right).astype(BF16)


def expert_kernel(more, count, *refs):
    h_ref, ht_ref, dy_ref, dyt_ref, gate_ref, wg_ref, wu_ref, wd_ref = refs[:8]
    out_ref, dx_ref, dg_ref, gr_ref, out_acc, dx_acc = refs[-6:]
    step, last = pl.program_id(0), pl.num_programs(0) - 1
    parts, _, part_rows, cols = wg_ref.shape
    chunks = (last + 1) // count

    @pl.when(step == 0)
    def _():
        if more:
            out0_ref, dx0_ref = refs[8:10]
            out_acc[...] = out0_ref[...].astype(F32)
            dx_acc[...] = dx0_ref[...].astype(F32)
        else:
            out_acc[...] = jnp.zeros_like(out_acc)
            dx_acc[...] = jnp.zeros_like(dx_acc)

    @pl.when(step % chunks == 0)
    def _():
        dg_ref[...] = jnp.zeros_like(dg_ref)

    for part, made in expert_step(
        step // chunks, h_ref, ht_ref, dy_ref, dyt_ref, gate_ref, wg_ref, wu_ref, wd_ref, dg_ref, out_acc, dx_acc
    ):
        gr_ref[:, part, 0] = made.reshape(parts, part_rows, cols)

    @pl.when(step == last)
    def _():
        out_ref[...] = out_acc[...].astype(BF16)
        dx_ref[...] = dx_acc[...].astype(BF16)


def experts(hidden, hidden_t, grad, grad_t, gates, weights, first=0, before=(), slots=None, slot=0, into=None):
    tokens, width = hidden.shape
    parts, _, part_rows, units = weights.shape
    units = units // 3
    count = gates.shape[1]
    slots = slots or count
    cols = min(256, units)
    chunks = units // cols
    once = pl.Buffered(1)
    whole = pl.BlockSpec((tokens, width), lambda s: (0, 0), pipeline_mode=once)
    whole_t = pl.BlockSpec((width, tokens), lambda s: (0, 0), pipeline_mode=once)
    result = pl.BlockSpec((tokens, width), lambda s: (0, 0))

    def weight(kind):
        return pl.BlockSpec(
            (parts, 1, part_rows, cols),
            lambda s: (0, first + s // chunks, 0, kind * chunks + s % chunks),
        )

    return pl.pallas_call(
        functools.partial(expert_kernel, bool(before), count),
        grid=(count * chunks,),
        in_specs=[
            whole,
            whole_t,
            whole,
            whole_t,
            pl.BlockSpec(gates.shape, lambda s: (0, 0), pipeline_mode=once),
            weight(0),
            weight(1),
            weight(2),
            *[whole for _ in before],
            *([] if into is None else [pl.BlockSpec(memory_space=pl.ANY)]),
        ],
        out_specs=[
            result,
            result,
            pl.BlockSpec((1, tokens, 1), lambda s: (s // chunks, 0, 0)),
            pl.BlockSpec(
                (parts, 3, 1, part_rows, cols), lambda s: (0, 0, slot + s // chunks, 0, s % chunks)
            ),
        ],
        out_shape=[
            jax.ShapeDtypeStruct((tokens, width), BF16),
            jax.ShapeDtypeStruct((tokens, width), BF16),
            jax.ShapeDtypeStruct((count, tokens, 1), F32),
            jax.ShapeDtypeStruct((parts, 3, slots, part_rows, units), BF16),
        ],
        input_output_aliases={} if into is None else {8 + len(before): 3},
        scratch_shapes=[
            pltpu.VMEM((tokens, width), F32),
            pltpu.VMEM((tokens, width), F32),
        ],
        compiler_params=pltpu.CompilerParams(vmem_limit_bytes=VMEM_LIMIT),
        cost_estimate=pl.CostEstimate(
            flops=18 * count * tokens * width * units,
            bytes_accessed=12 * count * width * units,
            transcendentals=count * tokens * units,
        ),
        name="experts",
    )(hidden, hidden_t, grad, grad_t, gates, weights, weights, weights, *before, *([] if into is None else [into]))


def finish_experts_kernel(sums_ref, *refs):
    gate_up_ref, down_ref = refs[-2:]
    units = down_ref.shape[2]
    gate_up_ref[0, :, :units] = sums_ref[0, 0].astype(F32)
    gate_up_ref[0, :, units:] = sums_ref[1, 0].astype(F32)
    down_ref[0] = sums_ref[2, 0].astype(F32)


def finish_experts(sums, at, total, before=()):
    _, count, rows, units = sums.shape
    tile = min(128, rows)
    return pl.pallas_call(
        finish_experts_kernel,
        grid=(count, rows // tile),
        in_specs=[
            pl.BlockSpec((3, 1, tile, units), lambda e, r: (0, e, r, 0)),
            *[pl.BlockSpec(memory_space=pl.ANY) for _ in before],
        ],
        out_specs=[
            pl.BlockSpec((1, tile, 2 * units), lambda e, r: (at + e, r, 0)),
            pl.BlockSpec((1, tile, units), lambda e, r: (at + e, r, 0)),
        ],
        out_shape=[
            jax.ShapeDtypeStruct((total, rows, 2 * units), F32),
            jax.ShapeDtypeStruct((total, rows, units), F32),
        ],
        input_output_aliases={1 + i: i for i in range(len(before))},
        compiler_params=pltpu.CompilerParams(vmem_limit_bytes=VMEM_LIMIT),
        name="finish_experts",
    )(sums, *before)


def turn(values, cos, sin):
    return values * cos + pltpu.roll(values, values.shape[1] // 2, 1) * sin


def project_kernel(
    tok_ref, gain_ref, w_ref, cos_ref, sin_ref, gains_ref, hidden_ref, qkv_ref, raw_ref
):
    head_dim = cos_ref.shape[1]
    values = tok_ref[...].astype(F32)
    hidden = (values * rms_scale(values) * gain_ref[...]).astype(BF16)
    hidden_ref[...] = hidden
    projected = dot_nn(hidden, w_ref[...])
    raw_ref[...] = projected[:, : 2 * head_dim]
    for part in range(2):
        at = slice(part * head_dim, (part + 1) * head_dim)
        raw = projected[:, at]
        normed = raw * rms_scale(raw) * gains_ref[part : part + 1, :]
        qkv_ref[:, at] = turn(normed, cos_ref[...], sin_ref[...]).astype(BF16)
    qkv_ref[:, 2 * head_dim :] = projected[:, 2 * head_dim :].astype(BF16)


def project(toks, gain, weights, cos, sin, gains):
    length, width = toks.shape
    head_dim = cos.shape[1]
    tile = min(256, length)

    def rows(columns):
        return pl.BlockSpec((tile, columns), lambda i: (i, 0))

    def fixed(shape):
        return pl.BlockSpec(shape, lambda i: (0, 0))

    return pl.pallas_call(
        project_kernel,
        grid=(length // tile,),
        in_specs=[
            rows(width),
            fixed((1, width)),
            fixed(weights.shape),
            rows(head_dim),
            rows(head_dim),
            fixed(gains.shape),
        ],
        out_specs=[rows(width), rows(3 * head_dim), rows(2 * head_dim)],
        out_shape=[
            jax.ShapeDtypeStruct((length, width), BF16),
            jax.ShapeDtypeStruct((length, 3 * head_dim), BF16),
            jax.ShapeDtypeStruct((length, 2 * head_dim), F32),
        ],
        compiler_params=pltpu.CompilerParams(vmem_limit_bytes=VMEM_LIMIT),
        name="project",
    )(toks, gain, weights, cos, sin, gains)


def project_back_kernel(
    factor, scale, q_ref, k_ref, v_ref, do_ref, of_ref, lse_ref, sq_ref, sk_ref,
    raw_q_ref, raw_k_ref, cos_q_ref, sin_q_ref, cos_ref, sin_ref, gains_ref,
    dp_ref, dgain_ref, kt_ref, dk_acc, dv_acc,
):
    length, head_dim = k_ref.shape
    size, count = key_chunks(length)
    tile = q_ref.shape[0]
    step_at = pl.program_id(0)

    @pl.when(step_at == 0)
    def _():
        kt_ref[...] = k_ref[...].astype(F32).T.astype(BF16)
        dk_acc[...] = jnp.zeros_like(dk_acc)
        dv_acc[...] = jnp.zeros_like(dv_acc)
        dgain_ref[...] = jnp.zeros_like(dgain_ref)

    def to_raw(part, grad, raw, cos, sin):
        grad = turn(grad.astype(BF16).astype(F32), cos, -sin)
        raw_scale = rms_scale(raw)
        dgain_ref[part : part + 1, :] += jnp.sum(grad * (raw * raw_scale), axis=0, keepdims=True)
        return norm_back(grad * gains_ref[part : part + 1, :], raw, raw_scale).astype(BF16)

    q = q_ref[...]
    grad = do_ref[...]
    seg_q = sq_ref[...]
    lse = lse_ref[0]
    row_dot = jnp.sum((grad.astype(F32) * of_ref[0]).T, axis=0, keepdims=True)
    dq_t = jnp.zeros((head_dim, tile), F32)
    for j in range(count):
        rows = slice(j * size, (j + 1) * size)
        scores = dot_nt(k_ref[rows, :], q)
        scores = jnp.where(sk_ref[rows, :] == seg_q, scores, NEG)
        weights = jnp.exp2(scores * factor - lse)
        grad_weights = dot_nt(v_ref[rows, :], grad)
        grad_scores = (weights * (grad_weights - row_dot)).astype(BF16)
        dk_acc[rows, :] += dot_nn(grad_scores, q)
        dv_acc[rows, :] += dot_nn(weights.astype(BF16), grad)
        dq_t = dq_t + dot_nn(kt_ref[:, rows], grad_scores)
    own = pl.ds(pl.multiple_of(step_at * tile, tile), tile)
    dp_ref[own, :head_dim] = to_raw(
        0, (dq_t * scale).T, raw_q_ref[...], cos_q_ref[...], sin_q_ref[...]
    )

    @pl.when(step_at == pl.num_programs(0) - 1)
    def _():
        dp_ref[:, head_dim : 2 * head_dim] = to_raw(
            1, dk_acc[...] * scale, raw_k_ref[...], cos_ref[...], sin_ref[...]
        )
        dp_ref[:, 2 * head_dim :] = dv_acc[...].astype(BF16)


def project_back(qkv, grad, out_f32, lse, segments, raw, cos, sin, gains):
    length, head_dim = grad.shape
    tile = min(256, length)

    def rows(column):
        return pl.BlockSpec((tile, head_dim), lambda i: (i, column))

    def whole(column):
        return pl.BlockSpec((length, head_dim), lambda i: (0, column))

    return pl.pallas_call(
        functools.partial(project_back_kernel, head_dim**-0.5 * LOG2E, head_dim**-0.5),
        grid=(length // tile,),
        in_specs=[
            rows(0),
            whole(1),
            whole(2),
            rows(0),
            pl.BlockSpec((1, tile, head_dim), lambda i: (0, i, 0)),
            pl.BlockSpec((1, 1, tile), lambda i: (0, 0, i)),
            pl.BlockSpec((1, tile), lambda i: (0, i)),
            pl.BlockSpec((length, 1), lambda i: (0, 0)),
            rows(0),
            whole(1),
            rows(0),
            rows(0),
            whole(0),
            whole(0),
            pl.BlockSpec(gains.shape, lambda i: (0, 0)),
        ],
        out_specs=[
            pl.BlockSpec((length, 3 * head_dim), lambda i: (0, 0)),
            pl.BlockSpec((2, head_dim), lambda i: (0, 0)),
        ],
        out_shape=[
            jax.ShapeDtypeStruct((length, 3 * head_dim), BF16),
            jax.ShapeDtypeStruct((2, head_dim), F32),
        ],
        scratch_shapes=[
            pltpu.VMEM((head_dim, length), BF16),
            pltpu.VMEM((length, head_dim), F32),
            pltpu.VMEM((length, head_dim), F32),
        ],
        compiler_params=pltpu.CompilerParams(vmem_limit_bytes=VMEM_LIMIT),
        cost_estimate=pl.CostEstimate(
            flops=10 * length * length * head_dim,
            bytes_accessed=length * head_dim * 40,
            transcendentals=length * length,
        ),
        name="project_back",
    )(
        qkv, qkv, qkv, grad, out_f32, lse, segments.reshape(1, -1), segments.reshape(-1, 1),
        raw, raw, cos, sin, cos, sin, gains,
    )


def hidden_back_kernel(grads_ref, own_ref, near_ref, far_ref, cross_ref, hidden_ref, out_ref, gain_ref):
    uly = grads_ref.shape[0]
    u = lax.axis_index(ULY)
    near = u + 1 - 2 * lax.rem(u, 2)
    total = dot_nt(grads_ref[u], own_ref[...])
    total = total + dot_nt(grads_ref[near], near_ref[...])
    total = total + dot_nt(grads_ref[lax.rem(u + 2, uly)], far_ref[...])
    total = total + dot_nt(grads_ref[lax.rem(near + 2, uly)], cross_ref[...])
    out_ref[...] = total.astype(BF16).reshape(out_ref.shape)
    hidden = hidden_ref[...].reshape(total.shape).astype(F32)
    gain_ref[...] = jnp.sum(total * hidden, axis=0, keepdims=True)


def hidden_back(grads, own, near, far, cross, hidden):
    uly, tokens, columns = grads.shape
    blk, _, rows, width = hidden.shape
    tile = min(512, width)
    weights = pl.BlockSpec((tile, columns), lambda n: (n, 0))
    return pl.pallas_call(
        hidden_back_kernel,
        grid=(width // tile,),
        in_specs=[
            pl.BlockSpec(grads.shape, lambda n: (0, 0, 0)),
            *[weights] * 4,
            pl.BlockSpec((blk, 1, rows, tile), lambda n: (0, lax.axis_index(ULY), 0, n)),
        ],
        out_specs=[
            pl.BlockSpec((blk, rows, tile), lambda n: (0, 0, n)),
            pl.BlockSpec((1, tile), lambda n: (0, n)),
        ],
        out_shape=[
            jax.ShapeDtypeStruct((blk, rows, width), BF16),
            jax.ShapeDtypeStruct((1, width), F32),
        ],
        compiler_params=pltpu.CompilerParams(vmem_limit_bytes=VMEM_LIMIT),
        name="hidden_back",
    )(grads, own, near, far, cross, hidden)


def merge_heads_kernel(parts_ref, out_ref):
    blk, uly, _, columns = parts_ref.shape
    head_dim = columns // 3
    heads = blk * uly
    for z in range(blk):
        for u in range(uly):
            head = parts_ref[z, u].astype(F32)
            for part in range(3):
                at = (part * heads + u * blk + z) * head_dim
                out_ref[:, at : at + head_dim] = head[:, part * head_dim : (part + 1) * head_dim]


def merge_heads(parts):
    blk, uly, rows, columns = parts.shape
    return pl.pallas_call(
        merge_heads_kernel,
        out_shape=jax.ShapeDtypeStruct((rows, blk * uly * columns), F32),
        compiler_params=pltpu.CompilerParams(vmem_limit_bytes=VMEM_LIMIT),
        name="merge_heads",
    )(parts)


def swap(values, axis):
    return lax.all_to_all(values, axis, split_axis=0, concat_axis=0, tiled=True)


def sum_scatter(values, axis):
    count = spread(axis) if isinstance(axis, tuple) else lax.axis_size(axis)
    rows, width = values.shape
    parts = swap(values.astype(BF16).reshape(count, rows // count, width), axis)
    return jnp.sum(parts.astype(F32), axis=0)


def place(axes, index):
    found = {}
    for axis in reversed(axes):
        size = lax.axis_size(axis)
        found[axis] = lax.rem(index, size)
        index = index // size
    return found


def spread(axes):
    return math.prod(lax.axis_size(axis) for axis in axes)


def each(count, body):
    if count <= 4:
        for step in range(1, count):
            body(step)
    else:

        def looped(step, carried):
            body(step)
            return carried

        lax.fori_loop(1, count, looped, 0)


def ahead(index, step, size):
    return lax.rem(index + step, size)


def exchange(items, collective_id, after=()):
    count = len(items)
    sizes = [spread(axes) for _, axes, _ in items]
    groups = list(dict.fromkeys(axes for _, axes, _ in items))
    bases = [sum(2 * size for size in sizes[:i]) for i in range(count)]

    def kernel(*refs):
        ins = refs[:count]
        outs = refs[count + len(after) : 2 * count + len(after)]
        send, recv, local = refs[-3:]
        barrier = pltpu.get_barrier_semaphore()
        for axes in groups:
            size, me = spread(axes), lax.axis_index(axes)

            def greet(step, axes=axes, size=size, me=me):
                pl.semaphore_signal(
                    barrier, inc=1, device_id=place(axes, ahead(me, step, size)), device_id_type=MESH
                )

            each(size, greet)
        pl.semaphore_wait(barrier, sum(spread(axes) - 1 for axes in groups))

        def block(i, peer):
            if items[i][2] == "swap":
                return ins[i].at[peer]
            return ins[i].at[:, peer] if items[i][2] == "swap1" else ins[i]

        def remote(i, step):
            _, axes, kind = items[i]
            me = lax.axis_index(axes)
            if kind == "trade":
                return pltpu.make_async_remote_copy(
                    src_ref=ins[i],
                    dst_ref=outs[i],
                    send_sem=send.at[bases[i] + 1],
                    recv_sem=recv.at[bases[i] + 1],
                    device_id=place(axes, 1 - me),
                    device_id_type=MESH,
                )
            if kind == "relay":
                far, near = lax.rem(me + 2, 4), me + 1 - 2 * lax.rem(me, 2)
                held = far if step == 3 else me
                return pltpu.make_async_remote_copy(
                    src_ref=outs[i].at[far] if step == 3 else ins[i],
                    dst_ref=outs[i].at[held],
                    send_sem=send.at[bases[i] + step],
                    recv_sem=recv.at[bases[i] + step],
                    device_id=place(axes, far if step == 1 else near),
                    device_id_type=MESH,
                )
            peer = ahead(me, step, sizes[i])
            return pltpu.make_async_remote_copy(
                src_ref=block(i, peer),
                dst_ref=outs[i].at[me],
                send_sem=send.at[bases[i] + step],
                recv_sem=recv.at[bases[i] + step],
                device_id=place(axes, peer),
                device_id_type=MESH,
            )

        def own(i):
            _, axes, kind = items[i]
            me = lax.axis_index(axes)
            return pltpu.make_async_copy(
                block(i, me), outs[i].at[me], local.at[i]
            )

        def hop(i, up, hops):
            (axis,) = items[i][1]
            me, size = lax.axis_index(axis), sizes[i]
            way = 1 if up else -1
            held, to = me - way * hops, me + way
            exists = (held >= 0) & (held < size) & (to >= 0) & (to < size)
            held, to = jnp.clip(held, 0, size - 1), jnp.clip(to, 0, size - 1)
            sem = bases[i] + (size if up else 0) + hops
            copy = pltpu.make_async_remote_copy(
                src_ref=outs[i].at[held] if hops else ins[i],
                dst_ref=outs[i].at[held],
                send_sem=send.at[sem],
                recv_sem=recv.at[sem],
                device_id={axis: to},
                device_id_type=MESH,
            )
            return exists, copy

        def arrival(i, up, hops):
            (axis,) = items[i][1]
            me, size = lax.axis_index(axis), sizes[i]
            way = 1 if up else -1
            held, sender = me - way * (hops + 1), me - way
            exists = (held >= 0) & (held < size)
            held, sender = jnp.clip(held, 0, size - 1), jnp.clip(sender, 0, size - 1)
            sem = bases[i] + (size if up else 0) + hops
            copy = pltpu.make_async_remote_copy(
                src_ref=ins[i],
                dst_ref=outs[i].at[held],
                send_sem=send.at[sem],
                recv_sem=recv.at[sem],
                device_id={axis: sender},
                device_id_type=MESH,
            )
            return exists, copy

        def kinds(*names):
            return [i for i in range(count) if items[i][2] in names]

        def when(pair, act):
            exists, copy = pair
            pl.when(exists)(lambda: act(copy))

        ways = (True, False)
        for i in kinds("line"):
            for up in ways:
                when(hop(i, up, 0), lambda copy: copy.start())
        for i in kinds("gather", "swap", "swap1", "relay", "trade"):
            each(3 if items[i][2] == "relay" else sizes[i], lambda step, i=i: remote(i, step).start())
        for i in kinds("gather", "swap", "swap1", "relay", "line"):
            own(i).start()
        for i in kinds("line"):
            for hops in range(1, sizes[i]):
                for up in ways:
                    when(arrival(i, up, hops - 1), lambda copy: copy.wait_recv())
                    if hops < sizes[i] - 1:
                        when(hop(i, up, hops), lambda copy: copy.start())
        for i in kinds("relay"):
            remote(i, 1).wait_recv()
            remote(i, 3).start()
            remote(i, 1).wait_send()
            for step in (2, 3):
                remote(i, step).wait()
        for i in kinds("gather", "swap", "swap1", "trade"):
            each(sizes[i], lambda step, i=i: remote(i, step).wait())
        for i in kinds("line"):
            for hops in range(sizes[i] - 1):
                for up in ways:
                    when(hop(i, up, hops), lambda copy: copy.wait_send())
        for i in kinds("gather", "swap", "swap1", "relay", "line"):
            own(i).wait()


    def shape_of(size, array, kind):
        if kind == "trade":
            return array.shape
        dropped = {"swap": 0, "swap1": 1}.get(kind)
        return (size, *(extent for at, extent in enumerate(array.shape) if at != dropped))

    anywhere = pl.BlockSpec(memory_space=pl.ANY)
    return pl.pallas_call(
        kernel,
        in_specs=[anywhere] * (count + len(after)),
        out_specs=[anywhere] * count,
        out_shape=[
            jax.ShapeDtypeStruct(shape_of(size, array, kind), array.dtype)
            for size, (array, _, kind) in zip(sizes, items)
        ],
        scratch_shapes=[
            pltpu.SemaphoreType.DMA((2 * sum(sizes),)),
            pltpu.SemaphoreType.DMA((2 * sum(sizes),)),
            pltpu.SemaphoreType.DMA((count,)),
        ],
        compiler_params=pltpu.CompilerParams(collective_id=collective_id, has_side_effects=True),
        name="exchange",
    )(*[item[0] for item in items], *after)


def turn_gather_kernel(
    own_ref, other_ref, all_ref, all_t_ref, other_t_ref, block, turned, send, recv, local
):
    size, me = lax.axis_size("blk"), lax.axis_index("blk")
    rows = own_ref.shape[0]
    barrier = pltpu.get_barrier_semaphore()
    ways = (1, 0)

    def neighbour(up):
        to = me + (1 if up else -1)
        return (to >= 0) & (to < size), jnp.clip(to, 0, size - 1)

    def greet(step):
        pl.semaphore_signal(
            barrier, inc=1, device_id={"blk": ahead(me, step, size)}, device_id_type=MESH
        )

    each(size, greet)
    pl.semaphore_wait(barrier, size - 1)

    def hop(up, hops):
        held = me - (1 if up else -1) * hops
        exists, to = neighbour(up)
        exists = exists & (held >= 0) & (held < size)
        held = jnp.clip(held, 0, size - 1)
        return exists, pltpu.make_async_remote_copy(
            src_ref=all_ref.at[held] if hops else own_ref,
            dst_ref=all_ref.at[held],
            send_sem=send.at[up * size + hops],
            recv_sem=recv.at[up * size + hops],
            device_id={"blk": to},
            device_id_type=MESH,
        )

    def arrival(up, hops):
        held = me - (1 if up else -1) * (hops + 1)
        exists = (held >= 0) & (held < size)
        held = jnp.clip(held, 0, size - 1)
        return exists, held, pltpu.make_async_remote_copy(
            src_ref=own_ref,
            dst_ref=all_ref.at[held],
            send_sem=send.at[up * size + hops],
            recv_sem=recv.at[up * size + hops],
            device_id={"blk": neighbour(1 - up)[1]},
            device_id_type=MESH,
        )

    def when(pair, act):
        exists, copy = pair
        pl.when(exists)(lambda: act(copy))

    def turn(src, dst, at):
        take = pltpu.make_async_copy(src, block, local.at[0])
        take.start()
        take.wait()
        turned[...] = block[...].T
        columns = pl.ds(pl.multiple_of(at * rows, rows), rows)
        give = pltpu.make_async_copy(turned, dst.at[:, columns], local.at[1])
        give.start()
        give.wait()

    for up in ways:
        when(hop(up, 0), lambda copy: copy.start())
    keep = pltpu.make_async_copy(own_ref, all_ref.at[me], local.at[2])
    keep.start()
    turn(own_ref, all_t_ref, me)
    for at in range(size):
        turn(other_ref.at[at], other_t_ref, at)
    for hops in range(1, size):
        for up in ways:
            exists, held, copy = arrival(up, hops - 1)

            @pl.when(exists)
            def _(copy=copy, up=up, hops=hops):
                copy.wait_recv()
                if hops < size - 1:
                    when(hop(up, hops), lambda copy: copy.start())

        for up in ways:
            exists, held, copy = arrival(up, hops - 1)
            pl.when(exists)(lambda held=held: turn(all_ref.at[held], all_t_ref, held))
    for hops in range(size - 1):
        for up in ways:
            when(hop(up, hops), lambda copy: copy.wait_send())
    keep.wait()


def turn_gather(own, other, collective_id, after=()):
    size = lax.axis_size("blk")
    rows, width = own.shape
    anywhere = pl.BlockSpec(memory_space=pl.ANY)

    def kernel(*refs):
        turn_gather_kernel(*refs[:2], *refs[2 + len(after) :])

    return pl.pallas_call(
        kernel,
        in_specs=[anywhere] * (2 + len(after)),
        out_specs=[anywhere] * 3,
        out_shape=[
            jax.ShapeDtypeStruct((size, rows, width), BF16),
            jax.ShapeDtypeStruct((width, size * rows), BF16),
            jax.ShapeDtypeStruct((width, size * rows), BF16),
        ],
        scratch_shapes=[
            pltpu.VMEM((rows, width), BF16),
            pltpu.VMEM((width, rows), BF16),
            pltpu.SemaphoreType.DMA((2 * size,)),
            pltpu.SemaphoreType.DMA((2 * size,)),
            pltpu.SemaphoreType.DMA((3,)),
        ],
        compiler_params=pltpu.CompilerParams(
            collective_id=collective_id, has_side_effects=True, vmem_limit_bytes=VMEM_LIMIT
        ),
        name="turn_gather",
    )(own, other, *after)


def startup_kernel(
    head_ref, extra_ref, tok_ref, heads_ref, extras_ref, toks_ref,
    head_send, head_recv, extra_send, extra_recv, trade_send, trade_recv,
    z_send, z_recv, ay_send, ay_recv, by_send, by_recv, c_send, c_recv, local,
):
    blk, uly = lax.axis_size("blk"), spread(ULY)
    total = spread(ALL)
    z, u, me = lax.axis_index("blk"), lax.axis_index(ULY), lax.axis_index(ALL)
    far = lax.rem(u + 2, uly)
    near = u + 1 - 2 * lax.rem(u, 2)
    half = tok_ref.shape[0] // 2
    parts = (pl.ds(0, half), pl.ds(half, half))

    barrier = pltpu.get_barrier_semaphore()

    def greet(step):
        pl.semaphore_signal(
            barrier, inc=1, device_id=place(ALL, ahead(me, step, total)), device_id_type=MESH
        )

    each(total, greet)
    pl.semaphore_wait(barrier, total - 1)

    def send(src, dst, sent, got, to):
        return pltpu.make_async_remote_copy(
            src_ref=src, dst_ref=dst, send_sem=sent, recv_sem=got, device_id=to, device_id_type=MESH
        )

    def block(step, other, part):
        at = toks_ref.at[ahead(z, step, blk), far if other else u, parts[part]]
        return (tok_ref.at[parts[part]] if step == 0 and not other else at), at

    streams = ((0, 0), (0, 1), (1, 1))

    def hop(stream, up, hops):
        other, part = streams[stream]
        way = 1 if up else -1
        held, to = z - way * hops, z + way
        exists = (held >= 0) & (held < blk) & (to >= 0) & (to < blk)
        held, to = jnp.clip(held, 0, blk - 1), jnp.clip(to, 0, blk - 1)
        at = toks_ref.at[held, far if other else u, parts[part]]
        src = tok_ref.at[parts[part]] if hops == 0 and not other else at
        sem = (2 * stream + up) * blk + hops
        return exists, send(src, at, z_send.at[sem], z_recv.at[sem], {"blk": to})

    def arrival(stream, up, hops):
        other, part = streams[stream]
        way = 1 if up else -1
        held, sender = z - way * (hops + 1), z - way
        exists = (held >= 0) & (held < blk)
        held, sender = jnp.clip(held, 0, blk - 1), jnp.clip(sender, 0, blk - 1)
        at = toks_ref.at[held, far if other else u, parts[part]]
        sem = (2 * stream + up) * blk + hops
        return exists, send(tok_ref.at[parts[part]], at, z_send.at[sem], z_recv.at[sem], {"blk": sender})

    def when(pair, act):
        exists, copy = pair
        pl.when(exists)(lambda: act(copy))

    def a_y(step):
        return send(*block(step, 0, 0), ay_send.at[step], ay_recv.at[step], place(ULY, far))

    def b_y():
        return send(*block(0, 0, 1), by_send.at[0], by_recv.at[0], place(ULY, far))

    def to_near(step, other, part):
        sem = 4 * step + 2 * other + part
        return send(*block(step, other, part), c_send.at[sem], c_recv.at[sem], place(ULY, near))

    group = ("blk", *ULY)
    mine, here, b = lax.axis_index(group), spread(group), lax.axis_index("batch")

    def head(step):
        to = place(group, ahead(mine, step, here))
        src = head_ref.at[(to["y"] * lax.axis_size("core") + to["core"]) * blk + to["blk"]]
        return send(src, heads_ref.at[b, mine], head_send.at[step], head_recv.at[step], to)

    def extra(step):
        to = place(group, ahead(mine, step, here))
        return send(extra_ref, extras_ref.at[b, mine], extra_send.at[step], extra_recv.at[step], to)

    def trade(which):
        ref = (heads_ref, extras_ref)[which].at[b]
        return send(ref, ref, trade_send.at[which], trade_recv.at[which], {"batch": 1 - b})

    own = [
        pltpu.make_async_copy(tok_ref, toks_ref.at[z, u], local.at[0]),
        pltpu.make_async_copy(head_ref.at[u * blk + z], heads_ref.at[b, mine], local.at[1]),
        pltpu.make_async_copy(extra_ref, extras_ref.at[b, mine], local.at[2]),
    ]

    def start_head(step):
        extra(step).start()
        head(step).start()

    each(here, start_head)
    ways = (1, 0)
    b_y().start()
    for stream in range(2):
        for up in ways:
            when(hop(stream, up, 0), lambda copy: copy.start())
    a_y(0).start()
    to_near(0, 0, 0).start()
    to_near(0, 0, 1).start()

    for copy in own:
        copy.start()
    b_y().wait_recv()
    for up in ways:
        when(hop(2, up, 0), lambda copy: copy.start())
    to_near(0, 1, 1).start()
    def wait_head(step):
        extra(step).wait()
        head(step).wait()

    for hops in range(1, blk):
        if hops == min(2, blk - 1):
            each(here, wait_head)
            for copy in own[1:]:
                copy.wait()
            trade(0).start()
            trade(1).start()
        for stream, (other, part) in enumerate(streams):
            for up in ways:
                exists, copy = arrival(stream, up, hops - 1)
                step = blk - hops if up else hops

                @pl.when(exists)
                def _(copy=copy, stream=stream, other=other, part=part, up=up, step=step, hops=hops):
                    copy.wait_recv()
                    if hops < blk - 1:
                        when(hop(stream, up, hops), lambda copy: copy.start())
                    if stream == 0:
                        a_y(step).start()
                    to_near(step, other, part).start()

    for step in [0, *reversed(range(1, blk))]:
        a_y(step).wait_recv()
        to_near(step, 1, 0).start()
    for step in range(blk):
        for other in range(2):
            for part in range(2):
                to_near(step, other, part).wait_recv()

    trade(0).wait()
    trade(1).wait()
    own[0].wait()
    b_y().wait_send()
    for hops in range(blk - 1):
        for stream in range(3):
            for up in ways:
                when(hop(stream, up, hops), lambda copy: copy.wait_send())
    for step in range(blk):
        a_y(step).wait_send()
        for other in range(2):
            for part in range(2):
                to_near(step, other, part).wait_send()


def startup(heads, extra, tok, collective_id):
    batch, blk, uly = lax.axis_size("batch"), lax.axis_size("blk"), spread(ULY)
    anywhere = pl.BlockSpec(memory_space=pl.ANY)
    dma = pltpu.SemaphoreType.DMA
    return pl.pallas_call(
        startup_kernel,
        in_specs=[anywhere] * 3,
        out_specs=[anywhere] * 3,
        out_shape=[
            jax.ShapeDtypeStruct((batch, blk * uly, *heads.shape[1:]), BF16),
            jax.ShapeDtypeStruct((batch, blk * uly, *extra.shape), BF16),
            jax.ShapeDtypeStruct((blk, uly, *tok.shape), BF16),
        ],
        scratch_shapes=[
            *[dma((blk * uly,))] * 4,
            *[dma((2,))] * 2,
            *[dma((6 * blk,))] * 2,
            *[dma((blk,))] * 2,
            *[dma((1,))] * 2,
            *[dma((4 * blk,))] * 2,
            dma((3,)),
        ],
        compiler_params=pltpu.CompilerParams(collective_id=collective_id, has_side_effects=True),
        name="startup",
    )(heads, extra, tok)


def per_device_general(
    tokens, segments, routes, w_qkv, w_out, attn_gain, ffn_gain, qk_gain, router, w_gate_up, w_down, cotangent
):
    own_tokens = tokens[0]
    own_grad = cotangent[0]
    count_tok, width = own_tokens.shape
    head_dim = qk_gain.shape[1]
    heads = width // head_dim
    uly, blk, batch = spread(ULY), lax.axis_size("blk"), lax.axis_size("batch")
    blk_at, uly_at = lax.axis_index("blk"), lax.axis_index(ULY)
    group = batch * blk
    local_heads = heads // uly
    local_width = local_heads * head_dim
    rows = count_tok * uly
    seg_row = segments[0]
    length = seg_row.shape[0]
    number = router.shape[1]
    local_experts, _, units = w_down.shape
    shard_rows = w_qkv.shape[0]

    extra = jnp.concatenate([attn_gain[:, None], ffn_gain[:, None], router], axis=1)
    extra = jnp.pad(extra, ((0, 0), (0, LANES - extra.shape[1])))
    columns = w_qkv.reshape(shard_rows, 3, uly, local_width).transpose(2, 0, 1, 3)
    packed = jnp.concatenate(
        [
            columns.reshape(uly, shard_rows, 3 * local_width),
            jnp.broadcast_to(extra[None], (uly, shard_rows, LANES)),
        ],
        axis=2,
    )
    packed = swap(packed, ULY).reshape(uly * shard_rows, 3 * local_width + LANES)
    packed = lax.all_gather(packed, ROWS, axis=0, tiled=True)
    own_qkv = packed[:, : 3 * local_width]
    gain_attn = packed[:, 3 * local_width].astype(F32)
    gain_ffn = packed[:, 3 * local_width + 1].astype(F32)
    whole_router = packed[:, 3 * local_width + 2 : 3 * local_width + 2 + number]
    tokens_all = lax.all_gather(own_tokens, ULY, axis=0, tiled=True)
    to_rows = [(u * group + g, g * uly + u) for g in range(group) for u in range(uly)]
    own_out = lax.all_gather(lax.ppermute(w_out, ALL, to_rows), ROWS, axis=0, tiled=True)
    whole_gate_up = lax.all_gather(w_gate_up, PLANE, axis=0, tiled=False)
    whole_down = lax.all_gather(w_down, PLANE, axis=0, tiled=False)
    grad_blk = lax.all_gather(own_grad, "blk", axis=0, tiled=True)
    routes_blk = lax.all_gather(routes[0], "blk", axis=0, tiled=True)

    gain_query = qk_gain[0].astype(F32)
    gain_key = qk_gain[1].astype(F32)
    inputs_all = tokens_all.astype(F32)
    normed_one = inputs_all * rms_scale(inputs_all)
    hidden_one = (normed_one * gain_attn).astype(BF16)
    projected = dot_nn(hidden_one, own_qkv)
    query_raw = projected[:, :local_width].reshape(rows, local_heads, head_dim)
    key_raw = projected[:, local_width : 2 * local_width].reshape(rows, local_heads, head_dim)
    value_raw = projected[:, 2 * local_width :].reshape(rows, local_heads, head_dim)
    cos_table, sin_table = rope_tables(blk_at * rows, rows, head_dim)
    query_scale = rms_scale(query_raw)
    key_scale = rms_scale(key_raw)
    qkv = jnp.concatenate(
        [
            rotate(query_raw * query_scale * gain_query, cos_table, sin_table),
            rotate(key_raw * key_scale * gain_key, cos_table, sin_table),
            value_raw,
        ],
        axis=2,
    ).astype(BF16)
    qkv = qkv.transpose(1, 0, 2)

    by_heads = local_heads % blk == 0
    if by_heads:
        per = local_heads // blk

        def to_heads(values):
            columns = values.shape[2]
            moved = swap(values.reshape(blk, per, rows, columns), "blk")
            return moved.transpose(1, 0, 2, 3).reshape(per, length, columns)

        def to_rows_back(values):
            columns = values.shape[2]
            parts = values.reshape(per, blk, rows, columns).transpose(1, 0, 2, 3)
            return swap(parts, "blk").reshape(local_heads, rows, columns)

        q_src = kv_src = to_heads(qkv)
        cols = (0, 1, 2)
        seg_q = seg_row
        first_head = uly_at * local_heads + blk_at * per
    else:

        def to_heads(values):
            return values

        def to_rows_back(values):
            return values

        q_src = qkv
        kv_src = lax.all_gather(qkv[:, :, head_dim:], "blk", axis=1, tiled=True)
        cols = (0, 0, 1)
        seg_q = lax.dynamic_slice_in_dim(seg_row, blk_at * rows, rows)
        first_head = uly_at * local_heads
    attn_low, attn_f32, lse, top = attention_forward(q_src, kv_src, cols, seg_q, seg_row, head_dim)
    head_vector = lax.dynamic_update_slice_in_dim(
        jnp.full((heads,), NEG, F32), jnp.max(top, axis=(1, 2)) * head_dim**-0.5, first_head, 0
    )
    head_max = lax.pmax(head_vector, ALL)
    attn_rows = to_rows_back(attn_low)
    out_heads = own_out.reshape(local_heads, head_dim, width)
    branch = jnp.einsum("htc,hcd->td", attn_rows, out_heads, preferred_element_type=F32)
    inputs = own_tokens.astype(F32)
    mid = inputs + sum_scatter(branch, ULY)

    scale_two = rms_scale(mid)
    normed_two = mid * scale_two
    hidden_two = (normed_two * gain_ffn).astype(BF16)
    hidden_blk = lax.all_gather(hidden_two, "blk", axis=0, tiled=True)
    probs_blk = jax.nn.softmax(dot_nn(hidden_blk, whole_router), axis=1)
    names = jnp.arange(number, dtype=jnp.int32)
    chosen_blk = jnp.any(routes_blk[:, :, None] == names, axis=1).astype(F32)
    own_names = blk_at * local_experts
    gates = lax.dynamic_slice_in_dim(probs_blk * chosen_blk, own_names, local_experts, axis=1)
    most = min(MOST_TOKENS, hidden_blk.shape[0])
    packed_weights = jnp.concatenate([whole_gate_up, whole_down], axis=3)
    made = []
    for at in range(0, hidden_blk.shape[0], most):
        hidden_part, grad_part = hidden_blk[at : at + most], grad_blk[at : at + most]
        made.append(
            experts(
                hidden_part,
                hidden_part.T,
                grad_part,
                grad_part.T,
                gates[at : at + most],
                packed_weights,
            )
        )
    out_part = jnp.concatenate([m[0] for m in made], axis=0)
    dx_part = jnp.concatenate([m[1] for m in made], axis=0)
    dg_part = jnp.concatenate([m[2] for m in made], axis=1)
    expert_grads = sum(m[3].astype(F32) for m in made).astype(BF16)
    expert_sums = lax.psum_scatter(expert_grads, PLANE, scatter_dimension=0, tiled=False).astype(F32)
    grad_gate_up = jnp.concatenate([expert_sums[0], expert_sums[1]], axis=2)
    grad_down = expert_sums[2]
    dg_parts = swap(dg_part.reshape(local_experts, blk, count_tok).transpose(1, 2, 0), "blk")
    grad_gates = dg_parts.transpose(1, 0, 2).reshape(count_tok, number)
    dx_sum = sum_scatter(dx_part, "blk")
    output = (mid + sum_scatter(out_part, "blk")).astype(BF16)
    router_probs = lax.dynamic_slice_in_dim(probs_blk, blk_at * count_tok, count_tok)
    chosen = lax.dynamic_slice_in_dim(chosen_blk, blk_at * count_tok, count_tok)
    grad_probs = chosen * grad_gates
    grad_logits = (
        router_probs * (grad_probs - jnp.sum(router_probs * grad_probs, axis=1, keepdims=True))
    ).astype(BF16)
    grad_hidden_two = dx_sum + dot_nt(grad_logits, whole_router)
    grad_router_part = dot_tn(hidden_two, grad_logits)
    grad_gain_ffn = jnp.sum(grad_hidden_two * normed_two, axis=0)
    grad_mid = own_grad.astype(F32) + norm_back(grad_hidden_two * gain_ffn, mid, scale_two)

    branch_grad = lax.all_gather(grad_mid.astype(BF16), ULY, axis=0, tiled=True)
    grad_attn = dot_nt(branch_grad, own_out).astype(BF16)
    grad_attn = to_heads(grad_attn.reshape(rows, local_heads, head_dim).transpose(1, 0, 2))
    grad_out_part = jnp.einsum("htc,td->hcd", attn_rows, branch_grad, preferred_element_type=F32)
    dq, dk, dv = attention_backward(
        q_src, kv_src, cols, grad_attn, attn_f32, lse, seg_q, seg_row, head_dim
    )
    if by_heads:
        dqkv = to_rows_back(jnp.concatenate([dq, dk, dv], axis=2))
        dq, dk, dv = jnp.split(dqkv, 3, axis=2)
    else:
        dk, dv = (lax.psum_scatter(g, "blk", scatter_dimension=1, tiled=True) for g in (dk, dv))
    dq, dk, dv = (g.transpose(1, 0, 2) for g in (dq, dk, dv))
    grad_query_norm = rotate(dq.astype(F32), cos_table, -sin_table)
    grad_key_norm = rotate(dk.astype(F32), cos_table, -sin_table)
    grad_gain_query = jnp.sum(grad_query_norm * (query_raw * query_scale), axis=(0, 1))
    grad_gain_key = jnp.sum(grad_key_norm * (key_raw * key_scale), axis=(0, 1))
    grad_projected = jnp.concatenate(
        [
            norm_back(grad_query_norm * gain_query, query_raw, query_scale)
            .reshape(rows, local_width)
            .astype(BF16),
            norm_back(grad_key_norm * gain_key, key_raw, key_scale)
            .reshape(rows, local_width)
            .astype(BF16),
            dv.reshape(rows, local_width),
        ],
        axis=1,
    )
    grad_hidden_part = dot_nt(grad_projected, own_qkv)
    grad_hidden_one = sum_scatter(grad_hidden_part, ULY)
    grad_gain_attn = jnp.sum(grad_hidden_part * normed_one, axis=0)
    grad_inputs = grad_mid + norm_back(grad_hidden_one * gain_attn, inputs, rms_scale(inputs))

    grad_qkv_part = dot_tn(hidden_one, grad_projected).astype(BF16)
    grad_qkv_rows = lax.psum_scatter(grad_qkv_part, ROWS, scatter_dimension=0, tiled=True)
    grad_qkv_rows = swap(grad_qkv_rows.reshape(uly, shard_rows, 3 * local_width), ULY)
    grad_qkv = (
        grad_qkv_rows.reshape(uly, shard_rows, 3, local_width)
        .transpose(1, 2, 0, 3)
        .reshape(shard_rows, 3 * width)
        .astype(F32)
    )
    grad_out_rows = lax.psum_scatter(
        grad_out_part.reshape(local_width, width).astype(BF16), ROWS, scatter_dimension=0, tiled=True
    )
    grad_out = lax.ppermute(grad_out_rows, ALL, [(b, a) for a, b in to_rows]).astype(F32)
    small = jnp.concatenate([grad_gain_attn[:, None], grad_gain_ffn[:, None], grad_router_part], axis=1)
    small = lax.psum_scatter(small, ALL, scatter_dimension=0, tiled=True)
    grad_qk_gain = lax.psum(jnp.stack([grad_gain_query, grad_gain_key]), ALL)

    clip_gamma = TAU / jnp.maximum(head_max, TAU)
    factor = jnp.repeat(jnp.sqrt(clip_gamma), head_dim)
    column_scale = jnp.concatenate([factor, factor, jnp.ones((width,), F32)])
    clipped = w_qkv.astype(F32) * column_scale[None, :]
    return (
        output[None],
        grad_inputs[None],
        grad_qkv,
        grad_out,
        small[:, 0],
        small[:, 1],
        grad_qk_gain,
        small[:, 2:],
        grad_gate_up,
        grad_down,
        clipped,
    )


def per_device(
    tokens, segments, routes, w_qkv, w_out, attn_gain, ffn_gain, qk_gain, router, w_gate_up, w_down, cotangent
):
    own_tokens = tokens[0]
    own_grad = cotangent[0]
    count_tok, width = own_tokens.shape
    head_dim = qk_gain.shape[1]
    heads = width // head_dim
    batch, blk, uly = lax.axis_size("batch"), lax.axis_size("blk"), spread(ULY)
    total, group = batch * blk * uly, batch * blk
    local_experts = w_down.shape[0]
    if uly != 4 or heads != blk * uly or blk < 2 or batch != 2 or local_experts != 4:
        return per_device_general(
            tokens, segments, routes, w_qkv, w_out, attn_gain, ffn_gain, qk_gain, router, w_gate_up, w_down, cotangent
        )
    blk_at, uly_at = lax.axis_index("blk"), lax.axis_index(ULY)
    rows = count_tok * uly
    seg_row = segments[0]
    length = seg_row.shape[0]
    number = router.shape[1]
    shard_rows = w_qkv.shape[0]

    to_rows = [(u * group + g, g * uly + u) for g in range(group) for u in range(uly)]
    own_rows = lax.ppermute(w_out, ALL, to_rows)


    def gather_experts(gate_up, down):
        return lax.all_gather(jnp.concatenate([gate_up, down], axis=2), PLANE, axis=0, tiled=False)

    weights_first = gather_experts(w_gate_up[:3], w_down[:3])
    extra = jnp.concatenate([attn_gain[None], ffn_gain[None], router.T], axis=0)
    kept = extra.shape[0]
    extra = jnp.pad(extra, ((0, -kept % 16), (0, -shard_rows % LANES)))
    by_head = w_qkv.reshape(shard_rows, 3, heads, head_dim).transpose(2, 0, 1, 3)
    own_qkv, extras, toks = startup(
        by_head.reshape(heads, shard_rows, 3 * head_dim), extra, own_tokens, 0
    )
    own_rows, extras, later_gate_up, later_down = lax.optimization_barrier(
        (own_rows, extras, w_gate_up[3:], w_down[3:])
    )
    weights_second = gather_experts(later_gate_up, later_down)
    own_out = lax.all_to_all(
        jnp.broadcast_to(own_rows[None], (group, *own_rows.shape)), ROWS, split_axis=0, concat_axis=0, tiled=True
    ).reshape(blk, head_dim, width)
    own_qkv = own_qkv.reshape(width, 3 * head_dim)
    extras = extras.reshape(total, *extra.shape)[:, :kept, :shard_rows]
    extras = extras.transpose(1, 0, 2).reshape(kept, width)
    gain_attn = extras[0].astype(F32)
    gain_ffn = extras[1].astype(F32)
    router_t = extras[2:]

    gains = qk_gain.astype(F32)
    cos, sin = rope_rows(length, head_dim)
    hidden_one, qkv, raw = project(
        toks.reshape(length, width), gain_attn[None], own_qkv, cos, sin, gains
    )
    attn_low, attn_f32, lse, top = attention_forward(
        qkv[None], qkv[None], (0, 1, 2), seg_row, seg_row, head_dim
    )
    (attn_rows,) = exchange([(attn_low.reshape(blk, rows, head_dim), ("blk",), "swap")], 1)
    branch = jnp.einsum("htc,hcd->td", attn_rows, own_out, preferred_element_type=F32)
    branch, grad_blk, routes_blk = exchange(
        [
            (branch.astype(BF16).reshape(uly, count_tok, width), ULY, "swap"),
            (own_grad, ("blk",), "line"),
            (routes[0].T, ("blk",), "gather"),
        ],
        2,
    )
    inputs = own_tokens.astype(F32)
    mid = inputs + jnp.sum(branch.astype(F32), axis=0)

    scale_two = rms_scale(mid)
    normed_two = mid * scale_two
    hidden_two = (normed_two * gain_ffn).astype(BF16)
    hidden_blk, hidden_t, grad_t = turn_gather(hidden_two, grad_blk, 3, after=[weights_first])
    tokens_blk = blk * count_tok
    hidden_blk = hidden_blk.reshape(tokens_blk, width)
    grad_blk = grad_blk.reshape(tokens_blk, width)
    probs_blk = jax.nn.softmax(dot_nt(hidden_blk, router_t), axis=1)
    names = jnp.arange(number, dtype=jnp.int32)
    chosen_blk = jnp.any(routes_blk[:, :, :, None] == names, axis=1).astype(F32)
    chosen_blk = chosen_blk.reshape(tokens_blk, number)
    gates = lax.dynamic_slice_in_dim(
        probs_blk * chosen_blk, blk_at * local_experts, local_experts, axis=1
    )
    shared = (hidden_blk, hidden_t, grad_blk, grad_t)
    out_part, dx_part, dg_first, grads_first = experts(*shared, gates[:, :2], weights_first)
    sums_first = lax.psum_scatter(grads_first, PLANE, scatter_dimension=0, tiled=False)
    out_part, dx_part, dg_second, grads_second = experts(
        *shared, gates[:, 2:3], weights_first, first=2, before=(out_part, dx_part), slots=2
    )
    out_part, dx_part, dg_third, grads_second = experts(
        *shared,
        gates[:, 3:],
        weights_second,
        before=(out_part, dx_part),
        slots=2,
        slot=1,
        into=grads_second,
    )
    sums_second = lax.psum_scatter(grads_second, PLANE, scatter_dimension=0, tiled=False)
    finished = finish_experts(sums_first, 0, local_experts)
    grad_gate_up, grad_down = finish_experts(sums_second, 2, local_experts, before=finished)
    dg_part = jnp.concatenate([dg_first, dg_second, dg_third], axis=0)
    dg_part = dg_part.reshape(local_experts, blk, count_tok)
    dx_parts, dg_parts = exchange(
        [
            (dx_part.reshape(blk, count_tok, width), ("blk",), "swap"),
            (dg_part.transpose(1, 0, 2), ("blk",), "swap"),
        ],
        4,
    )
    out_part = out_part.reshape(blk, count_tok, width)
    out_part, dx_parts = lax.optimization_barrier((out_part, dx_parts))
    out_parts = lax.all_to_all(out_part, "blk", split_axis=0, concat_axis=0, tiled=True)
    output = (mid + jnp.sum(out_parts.astype(F32), axis=0)).astype(BF16)
    router_probs = lax.dynamic_slice_in_dim(probs_blk, blk_at * count_tok, count_tok)
    chosen = lax.dynamic_slice_in_dim(chosen_blk, blk_at * count_tok, count_tok)
    grad_probs = chosen * dg_parts.reshape(number, count_tok).T
    grad_logits = (
        router_probs * (grad_probs - jnp.sum(router_probs * grad_probs, axis=1, keepdims=True))
    ).astype(BF16)
    grad_hidden_two = jnp.sum(dx_parts.astype(F32), axis=0) + dot_nn(grad_logits, router_t)
    grad_router_t = dot_tn(grad_logits, hidden_two)
    grad_gain_ffn = jnp.sum(grad_hidden_two * normed_two, axis=0)
    grad_mid = own_grad.astype(F32) + norm_back(grad_hidden_two * gain_ffn, mid, scale_two)

    (branch_grad,) = exchange([(grad_mid.astype(BF16), ULY, "relay")], 5)
    branch_grad, sent_qkv = lax.optimization_barrier((branch_grad, own_qkv))
    far_qkv = lax.ppermute(sent_qkv, "y", [(0, 1), (1, 0)])
    branch_grad = branch_grad.reshape(rows, width)
    grad_attn = jnp.einsum("td,hcd->htc", branch_grad, own_out, preferred_element_type=F32).astype(BF16)
    grad_out_part = jnp.einsum("htc,td->hcd", attn_rows, branch_grad, preferred_element_type=F32)
    grad_out_part = grad_out_part.astype(BF16).reshape(batch, blk, shard_rows, width)
    batch_at = lax.axis_index("batch")
    grad_attn, got_out_part = exchange(
        [
            (grad_attn, ("blk",), "swap"),
            (
                lax.dynamic_index_in_dim(grad_out_part, 1 - batch_at, 0, keepdims=False),
                ("batch",),
                "trade",
            ),
        ],
        6,
        after=[out_parts],
    )
    grad_out_part = lax.dynamic_index_in_dim(grad_out_part, batch_at, 0, keepdims=False) + got_out_part
    grad_projected, grad_gains = project_back(
        qkv, grad_attn.reshape(length, head_dim), attn_f32, lse, seg_row, raw, cos, sin, gains
    )
    grad_qkv_part = dot_tn(hidden_one, grad_projected).astype(BF16)
    by_batch = grad_qkv_part.reshape(batch, width // batch, 3 * head_dim)
    projected_blk, got_qkv_part, near_qkv, cross_qkv, grad_out_parts = exchange(
        [
            (grad_projected.reshape(blk, uly, count_tok, 3 * head_dim), ULY, "swap1"),
            (
                lax.dynamic_index_in_dim(by_batch, 1 - batch_at, 0, keepdims=False),
                ("batch",),
                "trade",
            ),
            (own_qkv, ("core",), "trade"),
            (far_qkv, ("core",), "trade"),
            (grad_out_part, ("blk",), "swap"),
        ],
        7,
    )
    grad_out = lax.ppermute(
        jnp.sum(grad_out_parts.astype(F32), axis=0).astype(BF16), ALL, [(b, a) for a, b in to_rows]
    ).astype(F32)
    grad_qkv_part = lax.dynamic_index_in_dim(by_batch, batch_at, 0, keepdims=False) + got_qkv_part
    grad_qkv_parts = lax.all_to_all(
        grad_qkv_part.reshape(total // batch, shard_rows, 3 * head_dim),
        ("blk", *ULY),
        split_axis=0,
        concat_axis=0,
        tiled=True,
    )

    grad_hidden_part, grad_gain_attn = hidden_back(
        projected_blk.reshape(uly, tokens_blk, 3 * head_dim),
        own_qkv,
        near_qkv,
        far_qkv,
        cross_qkv,
        hidden_one.reshape(blk, uly, count_tok, width),
    )
    grad_gain_attn = grad_gain_attn[0] / gain_attn

    small = jnp.concatenate([grad_gain_attn[None], grad_gain_ffn[None], grad_router_t], axis=0)
    small = small.reshape(kept, total, shard_rows).transpose(1, 0, 2)
    small = jnp.pad(small, ((0, 0), (0, 0), (0, LANES - shard_rows)))
    head_row = jnp.where(
        jnp.arange(LANES) == uly_at * blk + blk_at, jnp.max(top) * head_dim**-0.5, NEG
    )
    to_all = jnp.concatenate([grad_gains, head_row[None]], axis=0)
    small = jnp.concatenate([small, jnp.broadcast_to(to_all[None], (total, 3, LANES))], axis=1)
    small = jnp.pad(small, ((0, 0), (0, -small.shape[1] % 8), (0, 0)))
    grad_hidden_parts, small = exchange(
        [
            (grad_hidden_part, ("blk",), "swap"),
            (small, ALL, "swap"),
        ],
        8,
        after=[finished[0]],
    )
    grad_qkv_parts, small = lax.optimization_barrier((grad_qkv_parts, small))
    grad_qkv = merge_heads(grad_qkv_parts.reshape(blk, uly, shard_rows, 3 * head_dim))
    grad_hidden_one = jnp.sum(grad_hidden_parts.astype(F32), axis=0)
    grad_inputs = grad_mid + norm_back(grad_hidden_one * gain_attn, inputs, rms_scale(inputs))
    sums = jnp.sum(small, axis=0)
    head_max = jnp.max(small[:, kept + 2, :heads], axis=0)
    factor = jnp.repeat(jnp.sqrt(TAU / jnp.maximum(head_max, TAU)), head_dim)
    column_scale = jnp.concatenate([factor, factor, jnp.ones((width,), F32)])
    clipped = w_qkv.astype(F32) * column_scale[None, :]
    return (
        output[None],
        grad_inputs[None],
        grad_qkv,
        grad_out,
        sums[0, :shard_rows],
        sums[1, :shard_rows],
        sums[kept : kept + 2],
        sums[2:kept, :shard_rows].T,
        grad_gate_up,
        grad_down,
        clipped,
    )


def solution(mesh):
    in_specs = (
        P("batch", ("blk", *ULY), None),
        P("batch", None),
        P("batch", ("blk", *ULY), None),
        P(ALL, None),
        P(ALL, None),
        P(ALL),
        P(ALL),
        P(),
        P(ALL, None),
        P("blk", PLANE, None),
        P("blk", PLANE, None),
        P("batch", ("blk", *ULY), None),
    )
    out_specs = (
        P("batch", ("blk", *ULY), None),
        P("batch", ("blk", *ULY), None),
        P(ALL, None),
        P(ALL, None),
        P(ALL),
        P(ALL),
        P(),
        P(ALL, None),
        P("blk", PLANE, None),
        P("blk", PLANE, None),
        P(ALL, None),
    )
    cores = 2 - mesh.shape["uly"] % 2
    mesh = Mesh(
        mesh.devices.reshape(*(mesh.shape[axis] for axis in ROWS), mesh.shape["uly"] // cores, cores), ALL
    )
    return jax.shard_map(
        per_device, mesh=mesh, in_specs=in_specs, out_specs=out_specs, check_vma=False
    )
```

```python
import functools
import math

import jax
import jax.numpy as jnp
from jax import lax
from jax.experimental import pallas as pl
from jax.experimental.pallas import tpu as pltpu
from jax.sharding import Mesh
from jax.sharding import PartitionSpec as P

EPS = 1e-06
THETA = 50000.0
TAU = 4.0
NEG = -1e30
LOG2E = 1.4426950408889634
LANES = 128
MOST_TOKENS = 512
VMEM_LIMIT = 60 * 1024 * 1024

ULY = ("y", "core")
ALL = ("batch", "blk", *ULY)
ROWS = ("batch", "blk")
PLANE = ("batch", *ULY)
CHIPS = ("batch", "y")

MESH = pl.DeviceIdType.MESH
BF16 = jnp.bfloat16
F32 = jnp.float32


def rms_scale(values):
    return lax.rsqrt(jnp.mean(values * values, axis=-1, keepdims=True) + EPS)


def norm_back(grad_normed, values, scale):
    normed = values * scale
    return scale * (grad_normed - normed * jnp.mean(grad_normed * normed, axis=-1, keepdims=True))


def rope_tables(offset, length, head_dim):
    half_dim = head_dim // 2
    frequency = THETA ** (-jnp.arange(half_dim, dtype=F32) * 2.0 / head_dim)
    positions = (offset + jnp.arange(length, dtype=jnp.int32)).astype(F32)
    angles = positions[:, None] * frequency[None, :]
    return (jnp.cos(angles)[:, None, :], jnp.sin(angles)[:, None, :])


def rope_rows(length, head_dim):
    fine = math.gcd(length, LANES)
    frequency = THETA ** (-jnp.arange(head_dim // 2, dtype=F32) * 2.0 / head_dim)
    frequency = jnp.concatenate([frequency, frequency])
    coarse_angle = (jnp.arange(length // fine, dtype=F32) * fine)[:, None, None] * frequency
    fine_angle = jnp.arange(fine, dtype=F32)[None, :, None] * frequency
    cos_a, sin_a, cos_b, sin_b = lax.optimization_barrier(
        (jnp.cos(coarse_angle), jnp.sin(coarse_angle), jnp.cos(fine_angle), jnp.sin(fine_angle))
    )
    sign = jnp.where(jnp.arange(head_dim) < head_dim // 2, -1.0, 1.0)
    cos = cos_a * cos_b - sin_a * sin_b
    sin = (sin_a * cos_b + cos_a * sin_b) * sign
    return cos.reshape(length, head_dim), sin.reshape(length, head_dim)


def rotate(values, cos_table, sin_table):
    half_dim = values.shape[-1] // 2
    first = values[..., :half_dim]
    second = values[..., half_dim:]
    return jnp.concatenate(
        [first * cos_table - second * sin_table, second * cos_table + first * sin_table], axis=-1
    )


def dot_nn(a, b):
    return lax.dot_general(a, b, (((1,), (0,)), ((), ())), preferred_element_type=F32)


def dot_nt(a, b):
    return lax.dot_general(a, b, (((1,), (1,)), ((), ())), preferred_element_type=F32)


def dot_tn(a, b):
    return lax.dot_general(a, b, (((0,), (0,)), ((), ())), preferred_element_type=F32)


def key_chunks(length):
    size = min(512, length)
    return size, length // size


def attn_fwd_kernel(factor, q_ref, k_ref, v_ref, sq_ref, sk_ref, o_ref, of_ref, lse_ref, top_ref, vt_ref):
    length = k_ref.shape[1]
    size, count = key_chunks(length)
    tile, head_dim = q_ref.shape[1:]

    @pl.when(pl.program_id(1) == 0)
    def _():
        vt_ref[...] = v_ref[0].astype(F32).T.astype(BF16)

    q = q_ref[0]
    seg_q = sq_ref[...]

    def step(j, carried):
        total, top, acc = carried
        at = pl.multiple_of(j * size, size)
        scores = dot_nt(k_ref[0, pl.ds(at, size), :], q)
        scores = jnp.where(sk_ref[pl.ds(at, size), :] == seg_q, scores, NEG)
        top = jnp.maximum(top, jnp.max(scores, axis=0, keepdims=True))
        weights = jnp.exp2(scores * factor)
        total = total + jnp.sum(weights, axis=0, keepdims=True)
        acc = acc + dot_nn(vt_ref[:, pl.ds(at, size)], weights.astype(BF16))
        return total, top, acc

    start = (
        jnp.zeros((1, tile), F32),
        jnp.full((1, tile), NEG, F32),
        jnp.zeros((head_dim, tile), F32),
    )
    total, top, acc = lax.fori_loop(0, count, step, start, unroll=count <= 4)
    out = (acc * (1.0 / total)).T
    o_ref[0] = out.astype(BF16)
    of_ref[0] = out
    lse_ref[0] = jnp.log2(total)
    top_ref[0] = top


def attn_bwd_kernel(
    factor, scale, q_ref, k_ref, v_ref, do_ref, of_ref, lse_ref, sq_ref, sk_ref,
    dq_ref, dk_ref, dv_ref, kt_ref, dk_acc, dv_acc,
):
    length = k_ref.shape[1]
    size, count = key_chunks(length)
    tile, head_dim = q_ref.shape[1:]

    @pl.when(pl.program_id(1) == 0)
    def _():
        kt_ref[...] = k_ref[0].astype(F32).T.astype(BF16)
        dk_acc[...] = jnp.zeros_like(dk_acc)
        dv_acc[...] = jnp.zeros_like(dv_acc)

    q = q_ref[0]
    grad = do_ref[0]
    seg_q = sq_ref[...]
    lse = lse_ref[0]
    row_dot = jnp.sum((grad.astype(F32) * of_ref[0]).T, axis=0, keepdims=True)

    def step(j, dq_t):
        at = pl.multiple_of(j * size, size)
        rows = pl.ds(at, size)
        scores = dot_nt(k_ref[0, rows, :], q)
        scores = jnp.where(sk_ref[rows, :] == seg_q, scores, NEG)
        weights = jnp.exp2(scores * factor - lse)
        grad_weights = dot_nt(v_ref[0, rows, :], grad)
        grad_scores = (weights * (grad_weights - row_dot)).astype(BF16)
        dk_acc[rows, :] += dot_nn(grad_scores, q)
        dv_acc[rows, :] += dot_nn(weights.astype(BF16), grad)
        return dq_t + dot_nn(kt_ref[:, rows], grad_scores)

    dq_t = lax.fori_loop(0, count, step, jnp.zeros((head_dim, tile), F32), unroll=count <= 4)
    dq_ref[0] = (dq_t * scale).T.astype(BF16)

    @pl.when(pl.program_id(1) == pl.num_programs(1) - 1)
    def _():
        dk_ref[0] = (dk_acc[...] * scale).astype(BF16)
        dv_ref[0] = dv_acc[...].astype(BF16)


def attention_tile(queries, length):
    return min(queries, 256 if length <= 4096 else 128)


def attention_forward(q_src, kv_src, cols, seg_q, seg_k, head_dim):
    heads, queries = q_src.shape[:2]
    length = kv_src.shape[1]
    tile = attention_tile(queries, length)
    q_col, k_col, v_col = cols
    factor = head_dim**-0.5 * LOG2E
    row = pl.BlockSpec((1, 1, tile), lambda h, i: (h, 0, i))
    block = pl.BlockSpec((1, tile, head_dim), lambda h, i: (h, i, 0))
    return pl.pallas_call(
        functools.partial(attn_fwd_kernel, factor),
        grid=(heads, queries // tile),
        in_specs=[
            pl.BlockSpec((1, tile, head_dim), lambda h, i: (h, i, q_col)),
            pl.BlockSpec((1, length, head_dim), lambda h, i: (h, 0, k_col)),
            pl.BlockSpec((1, length, head_dim), lambda h, i: (h, 0, v_col)),
            pl.BlockSpec((1, tile), lambda h, i: (0, i)),
            pl.BlockSpec((length, 1), lambda h, i: (0, 0)),
        ],
        out_specs=[block, block, row, row],
        out_shape=[
            jax.ShapeDtypeStruct((heads, queries, head_dim), BF16),
            jax.ShapeDtypeStruct((heads, queries, head_dim), F32),
            jax.ShapeDtypeStruct((heads, 1, queries), F32),
            jax.ShapeDtypeStruct((heads, 1, queries), F32),
        ],
        scratch_shapes=[pltpu.VMEM((head_dim, length), BF16)],
        compiler_params=pltpu.CompilerParams(vmem_limit_bytes=VMEM_LIMIT),
        cost_estimate=pl.CostEstimate(
            flops=4 * heads * queries * length * head_dim,
            bytes_accessed=heads * (queries + length) * head_dim * 8,
            transcendentals=heads * queries * length,
        ),
        name="attend",
    )(q_src, kv_src, kv_src, seg_q.reshape(1, -1), seg_k.reshape(-1, 1))


def attention_backward(q_src, kv_src, cols, grad, out_f32, lse, seg_q, seg_k, head_dim):
    heads, queries = q_src.shape[:2]
    length = kv_src.shape[1]
    tile = attention_tile(queries, length)
    q_col, k_col, v_col = cols
    scale = head_dim**-0.5
    row = pl.BlockSpec((1, 1, tile), lambda h, i: (h, 0, i))
    block = pl.BlockSpec((1, tile, head_dim), lambda h, i: (h, i, 0))
    whole = pl.BlockSpec((1, length, head_dim), lambda h, i: (h, 0, 0))
    return pl.pallas_call(
        functools.partial(attn_bwd_kernel, scale * LOG2E, scale),
        grid=(heads, queries // tile),
        in_specs=[
            pl.BlockSpec((1, tile, head_dim), lambda h, i: (h, i, q_col)),
            pl.BlockSpec((1, length, head_dim), lambda h, i: (h, 0, k_col)),
            pl.BlockSpec((1, length, head_dim), lambda h, i: (h, 0, v_col)),
            block,
            block,
            row,
            pl.BlockSpec((1, tile), lambda h, i: (0, i)),
            pl.BlockSpec((length, 1), lambda h, i: (0, 0)),
        ],
        out_specs=[block, whole, whole],
        out_shape=[
            jax.ShapeDtypeStruct((heads, queries, head_dim), BF16),
            jax.ShapeDtypeStruct((heads, length, head_dim), BF16),
            jax.ShapeDtypeStruct((heads, length, head_dim), BF16),
        ],
        scratch_shapes=[
            pltpu.VMEM((head_dim, length), BF16),
            pltpu.VMEM((length, head_dim), F32),
            pltpu.VMEM((length, head_dim), F32),
        ],
        compiler_params=pltpu.CompilerParams(vmem_limit_bytes=VMEM_LIMIT),
        cost_estimate=pl.CostEstimate(
            flops=10 * heads * queries * length * head_dim,
            bytes_accessed=heads * (queries + length) * head_dim * 12,
            transcendentals=heads * queries * length,
        ),
        name="attend_back",
    )(q_src, kv_src, kv_src, grad, out_f32, lse, seg_q.reshape(1, -1), seg_k.reshape(-1, 1))


def expert_step(expert, h_ref, ht_ref, dy_ref, dyt_ref, gate_ref, wg_ref, wu_ref, wd_ref, dg_ref, out_acc, dx_acc):
    width = h_ref.shape[1]
    cols = wg_ref.shape[3]
    w_gate = wg_ref[...].reshape(width, cols)
    w_up = wu_ref[...].reshape(width, cols)
    w_down = wd_ref[...].reshape(width, cols)
    gates = gate_ref[...]
    mine = lax.broadcasted_iota(jnp.int32, gates.shape, 1) == expert
    gate = jnp.sum(jnp.where(mine, gates, 0.0), axis=1, keepdims=True)
    a_gate = dot_nn(h_ref[...], w_gate)
    a_up = dot_nn(h_ref[...], w_up)
    raw = dot_nn(dy_ref[...], w_down)
    sigma = 1.0 / (1.0 + jnp.exp2(a_gate * -LOG2E))
    swish = a_gate * sigma
    act = swish * a_up
    dg_ref[0] += jnp.sum(raw * act, axis=1, keepdims=True)
    gated = (gate * act).astype(BF16)
    d_act = gate * raw
    d_gate = (d_act * a_up * (sigma + swish * (1.0 - sigma))).astype(BF16)
    d_up = (d_act * swish).astype(BF16)
    out_acc[...] += dot_nt(gated, w_down)
    dx_acc[...] += dot_nt(d_gate, w_gate) + dot_nt(d_up, w_up)
    for part, (left, right) in enumerate([(ht_ref, d_gate), (ht_ref, d_up), (dyt_ref, gated)]):
        yield part, dot_nn(left[...], right).astype(BF16)


def expert_kernel(more, counts, *refs):
    h_ref, ht_ref, dy_ref, dyt_ref, gate_ref = refs[:5]
    sources = [refs[5 + 3 * i : 8 + 3 * i] for i in range(len(counts))]
    out_ref, dx_ref, dg_ref, gr_ref, out_acc, dx_acc = refs[-6:]
    step, last = pl.program_id(0), pl.num_programs(0) - 1
    parts, _, part_rows, cols = sources[0][0].shape
    chunks = (last + 1) // sum(counts)

    @pl.when(step == 0)
    def _():
        if more:
            out0_ref, dx0_ref = refs[-8:-6]
            out_acc[...] = out0_ref[...].astype(F32)
            dx_acc[...] = dx0_ref[...].astype(F32)
        else:
            out_acc[...] = jnp.zeros_like(out_acc)
            dx_acc[...] = jnp.zeros_like(dx_acc)

    @pl.when(step % chunks == 0)
    def _():
        dg_ref[...] = jnp.zeros_like(dg_ref)

    begin = 0
    for source, count in zip(sources, counts):
        end = begin + count * chunks

        @pl.when((step >= begin) & (step < end))
        def _(source=source):
            for part, made in expert_step(
                step // chunks, h_ref, ht_ref, dy_ref, dyt_ref, gate_ref, *source, dg_ref, out_acc, dx_acc
            ):
                gr_ref[:, part, 0] = made.reshape(parts, part_rows, cols)

        begin = end

    @pl.when(step == last)
    def _():
        out_ref[...] = out_acc[...].astype(BF16)
        dx_ref[...] = dx_acc[...].astype(BF16)


def experts(hidden, hidden_t, grad, grad_t, gates, sources, before=()):
    tokens, width = hidden.shape
    parts, _, part_rows, units = sources[0][0].shape
    units = units // 3
    counts = [count for _, _, count in sources]
    total = sum(counts)
    cols = min(256, units)
    chunks = units // cols
    once = pl.Buffered(1)
    whole = pl.BlockSpec((tokens, width), lambda s: (0, 0), pipeline_mode=once)
    whole_t = pl.BlockSpec((width, tokens), lambda s: (0, 0), pipeline_mode=once)
    result = pl.BlockSpec((tokens, width), lambda s: (0, 0))

    def weight(source, kind):
        _, first, count = sources[source]
        begin = sum(counts[:source]) * chunks

        def index(step):
            at = jnp.clip(step - begin, 0, count * chunks - 1)
            return (0, first + at // chunks, 0, kind * chunks + at % chunks)

        return pl.BlockSpec((parts, 1, part_rows, cols), index)

    return pl.pallas_call(
        functools.partial(expert_kernel, bool(before), counts),
        grid=(total * chunks,),
        in_specs=[
            whole,
            whole_t,
            whole,
            whole_t,
            pl.BlockSpec(gates.shape, lambda s: (0, 0), pipeline_mode=once),
            *[weight(source, kind) for source in range(len(sources)) for kind in range(3)],
            *[whole for _ in before],
        ],
        out_specs=[
            result,
            result,
            pl.BlockSpec((1, tokens, 1), lambda s: (s // chunks, 0, 0)),
            pl.BlockSpec((parts, 3, 1, part_rows, cols), lambda s: (0, 0, s // chunks, 0, s % chunks)),
        ],
        out_shape=[
            jax.ShapeDtypeStruct((tokens, width), BF16),
            jax.ShapeDtypeStruct((tokens, width), BF16),
            jax.ShapeDtypeStruct((total, tokens, 1), F32),
            jax.ShapeDtypeStruct((parts, 3, total, part_rows, units), BF16),
        ],
        scratch_shapes=[
            pltpu.VMEM((tokens, width), F32),
            pltpu.VMEM((tokens, width), F32),
        ],
        compiler_params=pltpu.CompilerParams(vmem_limit_bytes=VMEM_LIMIT),
        cost_estimate=pl.CostEstimate(
            flops=18 * total * tokens * width * units,
            bytes_accessed=12 * total * width * units,
            transcendentals=total * tokens * units,
        ),
        name="experts",
    )(hidden, hidden_t, grad, grad_t, gates, *[array for array, _, _ in sources for _ in range(3)], *before)


def finish_experts_kernel(sums_ref, *refs):
    gate_up_ref, down_ref = refs[-2:]
    units = down_ref.shape[2]
    gate_up_ref[0, :, :units] = sums_ref[0, 0].astype(F32)
    gate_up_ref[0, :, units:] = sums_ref[1, 0].astype(F32)
    down_ref[0] = sums_ref[2, 0].astype(F32)


def finish_experts(sums, at, total, before=()):
    _, count, rows, units = sums.shape
    tile = min(128, rows)
    return pl.pallas_call(
        finish_experts_kernel,
        grid=(count, rows // tile),
        in_specs=[
            pl.BlockSpec((3, 1, tile, units), lambda e, r: (0, e, r, 0)),
            *[pl.BlockSpec(memory_space=pl.ANY) for _ in before],
        ],
        out_specs=[
            pl.BlockSpec((1, tile, 2 * units), lambda e, r: (at + e, r, 0)),
            pl.BlockSpec((1, tile, units), lambda e, r: (at + e, r, 0)),
        ],
        out_shape=[
            jax.ShapeDtypeStruct((total, rows, 2 * units), F32),
            jax.ShapeDtypeStruct((total, rows, units), F32),
        ],
        input_output_aliases={1 + i: i for i in range(len(before))},
        compiler_params=pltpu.CompilerParams(vmem_limit_bytes=VMEM_LIMIT),
        name="finish_experts",
    )(sums, *before)


def turn(values, cos, sin):
    return values * cos + pltpu.roll(values, values.shape[1] // 2, 1) * sin


def project_kernel(
    tok_ref, gain_ref, w_ref, cos_ref, sin_ref, gains_ref, hidden_ref, qkv_ref, raw_ref
):
    head_dim = cos_ref.shape[1]
    values = tok_ref[...].astype(F32)
    hidden = (values * rms_scale(values) * gain_ref[...]).astype(BF16)
    hidden_ref[...] = hidden
    projected = dot_nn(hidden, w_ref[...])
    raw_ref[...] = projected[:, : 2 * head_dim]
    for part in range(2):
        at = slice(part * head_dim, (part + 1) * head_dim)
        raw = projected[:, at]
        normed = raw * rms_scale(raw) * gains_ref[part : part + 1, :]
        qkv_ref[:, at] = turn(normed, cos_ref[...], sin_ref[...]).astype(BF16)
    qkv_ref[:, 2 * head_dim :] = projected[:, 2 * head_dim :].astype(BF16)


def project(toks, gain, weights, cos, sin, gains):
    length, width = toks.shape
    head_dim = cos.shape[1]
    tile = min(256, length)

    def rows(columns):
        return pl.BlockSpec((tile, columns), lambda i: (i, 0))

    def fixed(shape):
        return pl.BlockSpec(shape, lambda i: (0, 0))

    return pl.pallas_call(
        project_kernel,
        grid=(length // tile,),
        in_specs=[
            rows(width),
            fixed((1, width)),
            fixed(weights.shape),
            rows(head_dim),
            rows(head_dim),
            fixed(gains.shape),
        ],
        out_specs=[rows(width), rows(3 * head_dim), rows(2 * head_dim)],
        out_shape=[
            jax.ShapeDtypeStruct((length, width), BF16),
            jax.ShapeDtypeStruct((length, 3 * head_dim), BF16),
            jax.ShapeDtypeStruct((length, 2 * head_dim), F32),
        ],
        compiler_params=pltpu.CompilerParams(vmem_limit_bytes=VMEM_LIMIT),
        name="project",
    )(toks, gain, weights, cos, sin, gains)


def project_back_kernel(
    factor, scale, q_ref, k_ref, v_ref, do_ref, of_ref, lse_ref, sq_ref, sk_ref,
    raw_q_ref, raw_k_ref, cos_q_ref, sin_q_ref, cos_ref, sin_ref, gains_ref,
    dp_ref, dgain_ref, kt_ref, dk_acc, dv_acc,
):
    length, head_dim = k_ref.shape
    size, count = key_chunks(length)
    tile = q_ref.shape[0]
    step_at = pl.program_id(0)

    @pl.when(step_at == 0)
    def _():
        kt_ref[...] = k_ref[...].astype(F32).T.astype(BF16)
        dk_acc[...] = jnp.zeros_like(dk_acc)
        dv_acc[...] = jnp.zeros_like(dv_acc)
        dgain_ref[...] = jnp.zeros_like(dgain_ref)

    def to_raw(part, grad, raw, cos, sin):
        grad = turn(grad.astype(BF16).astype(F32), cos, -sin)
        raw_scale = rms_scale(raw)
        dgain_ref[part : part + 1, :] += jnp.sum(grad * (raw * raw_scale), axis=0, keepdims=True)
        return norm_back(grad * gains_ref[part : part + 1, :], raw, raw_scale).astype(BF16)

    q = q_ref[...]
    grad = do_ref[...]
    seg_q = sq_ref[...]
    lse = lse_ref[0]
    row_dot = jnp.sum((grad.astype(F32) * of_ref[0]).T, axis=0, keepdims=True)
    dq_t = jnp.zeros((head_dim, tile), F32)
    for j in range(count):
        rows = slice(j * size, (j + 1) * size)
        scores = dot_nt(k_ref[rows, :], q)
        scores = jnp.where(sk_ref[rows, :] == seg_q, scores, NEG)
        weights = jnp.exp2(scores * factor - lse)
        grad_weights = dot_nt(v_ref[rows, :], grad)
        grad_scores = (weights * (grad_weights - row_dot)).astype(BF16)
        dk_acc[rows, :] += dot_nn(grad_scores, q)
        dv_acc[rows, :] += dot_nn(weights.astype(BF16), grad)
        dq_t = dq_t + dot_nn(kt_ref[:, rows], grad_scores)
    own = pl.ds(pl.multiple_of(step_at * tile, tile), tile)
    dp_ref[own, :head_dim] = to_raw(
        0, (dq_t * scale).T, raw_q_ref[...], cos_q_ref[...], sin_q_ref[...]
    )

    @pl.when(step_at == pl.num_programs(0) - 1)
    def _():
        dp_ref[:, head_dim : 2 * head_dim] = to_raw(
            1, dk_acc[...] * scale, raw_k_ref[...], cos_ref[...], sin_ref[...]
        )
        dp_ref[:, 2 * head_dim :] = dv_acc[...].astype(BF16)


def project_back(qkv, grad, out_f32, lse, segments, raw, cos, sin, gains):
    length, head_dim = grad.shape
    tile = min(256, length)

    def rows(column):
        return pl.BlockSpec((tile, head_dim), lambda i: (i, column))

    def whole(column):
        return pl.BlockSpec((length, head_dim), lambda i: (0, column))

    return pl.pallas_call(
        functools.partial(project_back_kernel, head_dim**-0.5 * LOG2E, head_dim**-0.5),
        grid=(length // tile,),
        in_specs=[
            rows(0),
            whole(1),
            whole(2),
            rows(0),
            pl.BlockSpec((1, tile, head_dim), lambda i: (0, i, 0)),
            pl.BlockSpec((1, 1, tile), lambda i: (0, 0, i)),
            pl.BlockSpec((1, tile), lambda i: (0, i)),
            pl.BlockSpec((length, 1), lambda i: (0, 0)),
            rows(0),
            whole(1),
            rows(0),
            rows(0),
            whole(0),
            whole(0),
            pl.BlockSpec(gains.shape, lambda i: (0, 0)),
        ],
        out_specs=[
            pl.BlockSpec((length, 3 * head_dim), lambda i: (0, 0)),
            pl.BlockSpec((2, head_dim), lambda i: (0, 0)),
        ],
        out_shape=[
            jax.ShapeDtypeStruct((length, 3 * head_dim), BF16),
            jax.ShapeDtypeStruct((2, head_dim), F32),
        ],
        scratch_shapes=[
            pltpu.VMEM((head_dim, length), BF16),
            pltpu.VMEM((length, head_dim), F32),
            pltpu.VMEM((length, head_dim), F32),
        ],
        compiler_params=pltpu.CompilerParams(vmem_limit_bytes=VMEM_LIMIT),
        cost_estimate=pl.CostEstimate(
            flops=10 * length * length * head_dim,
            bytes_accessed=length * head_dim * 40,
            transcendentals=length * length,
        ),
        name="project_back",
    )(
        qkv, qkv, qkv, grad, out_f32, lse, segments.reshape(1, -1), segments.reshape(-1, 1),
        raw, raw, cos, sin, cos, sin, gains,
    )


def hidden_back_kernel(grads_ref, own_ref, near_ref, far_ref, cross_ref, hidden_ref, out_ref, gain_ref):
    uly = grads_ref.shape[0]
    u = lax.axis_index(ULY)
    near = u + 1 - 2 * lax.rem(u, 2)
    total = dot_nt(grads_ref[u], own_ref[...])
    total = total + dot_nt(grads_ref[near], near_ref[...])
    total = total + dot_nt(grads_ref[lax.rem(u + 2, uly)], far_ref[...])
    total = total + dot_nt(grads_ref[lax.rem(near + 2, uly)], cross_ref[...])
    out_ref[...] = total.astype(BF16).reshape(out_ref.shape)
    hidden = hidden_ref[...].reshape(total.shape).astype(F32)
    gain_ref[...] = jnp.sum(total * hidden, axis=0, keepdims=True)


def hidden_back(grads, own, near, far, cross, hidden):
    uly, tokens, columns = grads.shape
    blk, _, rows, width = hidden.shape
    tile = min(512, width)
    weights = pl.BlockSpec((tile, columns), lambda n: (n, 0))
    return pl.pallas_call(
        hidden_back_kernel,
        grid=(width // tile,),
        in_specs=[
            pl.BlockSpec(grads.shape, lambda n: (0, 0, 0)),
            *[weights] * 4,
            pl.BlockSpec((blk, 1, rows, tile), lambda n: (0, lax.axis_index(ULY), 0, n)),
        ],
        out_specs=[
            pl.BlockSpec((blk, rows, tile), lambda n: (0, 0, n)),
            pl.BlockSpec((1, tile), lambda n: (0, n)),
        ],
        out_shape=[
            jax.ShapeDtypeStruct((blk, rows, width), BF16),
            jax.ShapeDtypeStruct((1, width), F32),
        ],
        compiler_params=pltpu.CompilerParams(vmem_limit_bytes=VMEM_LIMIT),
        name="hidden_back",
    )(grads, own, near, far, cross, hidden)


def merge_heads_kernel(parts_ref, out_ref):
    blk, uly, _, columns = parts_ref.shape
    head_dim = columns // 3
    heads = blk * uly
    for z in range(blk):
        for u in range(uly):
            head = parts_ref[z, u].astype(F32)
            for part in range(3):
                at = (part * heads + u * blk + z) * head_dim
                out_ref[:, at : at + head_dim] = head[:, part * head_dim : (part + 1) * head_dim]


def merge_heads(parts):
    blk, uly, rows, columns = parts.shape
    return pl.pallas_call(
        merge_heads_kernel,
        out_shape=jax.ShapeDtypeStruct((rows, blk * uly * columns), F32),
        compiler_params=pltpu.CompilerParams(vmem_limit_bytes=VMEM_LIMIT),
        name="merge_heads",
    )(parts)


def swap(values, axis):
    return lax.all_to_all(values, axis, split_axis=0, concat_axis=0, tiled=True)


def sum_scatter(values, axis):
    count = spread(axis) if isinstance(axis, tuple) else lax.axis_size(axis)
    rows, width = values.shape
    parts = swap(values.astype(BF16).reshape(count, rows // count, width), axis)
    return jnp.sum(parts.astype(F32), axis=0)


def place(axes, index):
    found = {}
    for axis in reversed(axes):
        size = lax.axis_size(axis)
        found[axis] = lax.rem(index, size)
        index = index // size
    return found


def spread(axes):
    return math.prod(lax.axis_size(axis) for axis in axes)


def each(count, body):
    if count <= 4:
        for step in range(1, count):
            body(step)
    else:

        def looped(step, carried):
            body(step)
            return carried

        lax.fori_loop(1, count, looped, 0)


def ahead(index, step, size):
    return lax.rem(index + step, size)


def exchange(items, collective_id, after=()):
    count = len(items)
    sizes = [spread(axes) for _, axes, _ in items]
    groups = list(dict.fromkeys(axes for _, axes, _ in items))
    bases = [sum(2 * size for size in sizes[:i]) for i in range(count)]

    def kernel(*refs):
        ins = refs[:count]
        outs = refs[count + len(after) : 2 * count + len(after)]
        send, recv, local = refs[2 * count + len(after) :][:3]
        barrier = pltpu.get_barrier_semaphore()
        for axes in groups:
            size, me = spread(axes), lax.axis_index(axes)

            def greet(step, axes=axes, size=size, me=me):
                pl.semaphore_signal(
                    barrier, inc=1, device_id=place(axes, ahead(me, step, size)), device_id_type=MESH
                )

            each(size, greet)
        pl.semaphore_wait(barrier, sum(spread(axes) - 1 for axes in groups))

        def block(i, peer):
            if items[i][2] == "swap":
                return ins[i].at[peer]
            return ins[i].at[:, peer] if items[i][2] == "swap1" else ins[i]

        def remote(i, step):
            _, axes, kind = items[i]
            me = lax.axis_index(axes)
            if kind == "trade":
                return pltpu.make_async_remote_copy(
                    src_ref=ins[i],
                    dst_ref=outs[i],
                    send_sem=send.at[bases[i] + 1],
                    recv_sem=recv.at[bases[i] + 1],
                    device_id=place(axes, 1 - me),
                    device_id_type=MESH,
                )
            if kind == "relay":
                far, near = lax.rem(me + 2, 4), me + 1 - 2 * lax.rem(me, 2)
                held = far if step == 3 else me
                return pltpu.make_async_remote_copy(
                    src_ref=outs[i].at[far] if step == 3 else ins[i],
                    dst_ref=outs[i].at[held],
                    send_sem=send.at[bases[i] + step],
                    recv_sem=recv.at[bases[i] + step],
                    device_id=place(axes, far if step == 1 else near),
                    device_id_type=MESH,
                )
            peer = ahead(me, step, sizes[i])
            return pltpu.make_async_remote_copy(
                src_ref=block(i, peer),
                dst_ref=outs[i].at[me],
                send_sem=send.at[bases[i] + step],
                recv_sem=recv.at[bases[i] + step],
                device_id=place(axes, peer),
                device_id_type=MESH,
            )

        def own(i):
            _, axes, kind = items[i]
            me = lax.axis_index(axes)
            return pltpu.make_async_copy(
                block(i, me), outs[i].at[me], local.at[i]
            )

        def hop(i, up, hops):
            (axis,) = items[i][1]
            me, size = lax.axis_index(axis), sizes[i]
            way = 1 if up else -1
            held, to = me - way * hops, me + way
            exists = (held >= 0) & (held < size) & (to >= 0) & (to < size)
            held, to = jnp.clip(held, 0, size - 1), jnp.clip(to, 0, size - 1)
            sem = bases[i] + (size if up else 0) + hops
            copy = pltpu.make_async_remote_copy(
                src_ref=outs[i].at[held] if hops else ins[i],
                dst_ref=outs[i].at[held],
                send_sem=send.at[sem],
                recv_sem=recv.at[sem],
                device_id={axis: to},
                device_id_type=MESH,
            )
            return exists, copy

        def arrival(i, up, hops):
            (axis,) = items[i][1]
            me, size = lax.axis_index(axis), sizes[i]
            way = 1 if up else -1
            held, sender = me - way * (hops + 1), me - way
            exists = (held >= 0) & (held < size)
            held, sender = jnp.clip(held, 0, size - 1), jnp.clip(sender, 0, size - 1)
            sem = bases[i] + (size if up else 0) + hops
            copy = pltpu.make_async_remote_copy(
                src_ref=ins[i],
                dst_ref=outs[i].at[held],
                send_sem=send.at[sem],
                recv_sem=recv.at[sem],
                device_id={axis: sender},
                device_id_type=MESH,
            )
            return exists, copy

        def kinds(*names):
            return [i for i in range(count) if items[i][2] in names]

        def when(pair, act):
            exists, copy = pair
            pl.when(exists)(lambda: act(copy))

        def pairsum(i):
            me = lax.axis_index(ULY)
            far, near = lax.rem(me + 2, 4), me + 1 - 2 * lax.rem(me, 2)
            own, out = ins[i], outs[i]
            got_near, got_far, sent = refs[2 * count + len(after) + 3 :]

            def copy(at, src, dst, to):
                return pltpu.make_async_remote_copy(
                    src_ref=src,
                    dst_ref=dst,
                    send_sem=send.at[bases[i] + at],
                    recv_sem=recv.at[bases[i] + at],
                    device_id=place(ULY, to),
                    device_id_type=MESH,
                )

            to_near = [
                copy(0, own.at[near], got_near.at[0], near),
                copy(1, own.at[lax.rem(near + 2, 4)], got_near.at[1], near),
            ]
            to_far = copy(2, sent, got_far, far)

            def first():
                for sending in to_near:
                    sending.start()

            def second():
                for sending in to_near:
                    sending.wait()
                sent[...] = (own[far].astype(F32) + got_near[1].astype(F32)).astype(BF16)
                to_far.start()
                out[...] = own[me].astype(F32) + got_near[0].astype(F32)

            def third():
                to_far.wait()
                out[...] += got_far[...].astype(F32)

            return first, second, third

        ways = (True, False)
        sums = [pairsum(i) for i in kinds("pairsum")]
        for first, _, _ in sums:
            first()
        for i in kinds("line"):
            for up in ways:
                when(hop(i, up, 0), lambda copy: copy.start())
        for i in kinds("gather", "swap", "swap1", "relay", "trade"):
            each(3 if items[i][2] == "relay" else sizes[i], lambda step, i=i: remote(i, step).start())
        for i in kinds("gather", "swap", "swap1", "relay", "line"):
            own(i).start()
        for _, second, _ in sums:
            second()
        for i in kinds("line"):
            for hops in range(1, sizes[i]):
                for up in ways:
                    when(arrival(i, up, hops - 1), lambda copy: copy.wait_recv())
                    if hops < sizes[i] - 1:
                        when(hop(i, up, hops), lambda copy: copy.start())
        for i in kinds("relay"):
            remote(i, 1).wait_recv()
            remote(i, 3).start()
            remote(i, 1).wait_send()
            for step in (2, 3):
                remote(i, step).wait()
        for i in kinds("gather", "swap", "swap1", "trade"):
            each(sizes[i], lambda step, i=i: remote(i, step).wait())
        for i in kinds("line"):
            for hops in range(sizes[i] - 1):
                for up in ways:
                    when(hop(i, up, hops), lambda copy: copy.wait_send())
        for i in kinds("gather", "swap", "swap1", "relay", "line"):
            own(i).wait()
        for _, _, third in sums:
            third()


    def shape_of(size, array, kind):
        if kind in ("trade", "pairsum"):
            return array.shape[kind == "pairsum" :]
        dropped = {"swap": 0, "swap1": 1}.get(kind)
        return (size, *(extent for at, extent in enumerate(array.shape) if at != dropped))

    anywhere, close = pl.BlockSpec(memory_space=pl.ANY), pl.BlockSpec(memory_space=pltpu.VMEM)
    specs = [close if kind == "pairsum" else anywhere for _, _, kind in items]
    held = []
    for array, _, kind in items:
        if kind == "pairsum":
            held = [pltpu.VMEM((*more, *array.shape[1:]), BF16) for more in ((2,), (), ())]
    return pl.pallas_call(
        kernel,
        in_specs=specs + [anywhere] * len(after),
        out_specs=specs,
        out_shape=[
            jax.ShapeDtypeStruct(shape_of(size, array, kind), F32 if kind == "pairsum" else array.dtype)
            for size, (array, _, kind) in zip(sizes, items)
        ],
        scratch_shapes=[
            pltpu.SemaphoreType.DMA((2 * sum(sizes),)),
            pltpu.SemaphoreType.DMA((2 * sum(sizes),)),
            pltpu.SemaphoreType.DMA((count,)),
            *held,
        ],
        compiler_params=pltpu.CompilerParams(
            collective_id=collective_id, has_side_effects=True, vmem_limit_bytes=VMEM_LIMIT if held else None
        ),
        name="exchange",
    )(*[item[0] for item in items], *after)


def turn_gather_kernel(
    own_ref, other_ref, all_ref, all_t_ref, other_t_ref, block, turned, send, recv, local
):
    size, me = lax.axis_size("blk"), lax.axis_index("blk")
    rows = own_ref.shape[0]
    barrier = pltpu.get_barrier_semaphore()
    ways = (1, 0)

    def neighbour(up):
        to = me + (1 if up else -1)
        return (to >= 0) & (to < size), jnp.clip(to, 0, size - 1)

    def greet(step):
        pl.semaphore_signal(
            barrier, inc=1, device_id={"blk": ahead(me, step, size)}, device_id_type=MESH
        )

    each(size, greet)
    pl.semaphore_wait(barrier, size - 1)

    def hop(up, hops):
        held = me - (1 if up else -1) * hops
        exists, to = neighbour(up)
        exists = exists & (held >= 0) & (held < size)
        held = jnp.clip(held, 0, size - 1)
        return exists, pltpu.make_async_remote_copy(
            src_ref=all_ref.at[held] if hops else own_ref,
            dst_ref=all_ref.at[held],
            send_sem=send.at[up * size + hops],
            recv_sem=recv.at[up * size + hops],
            device_id={"blk": to},
            device_id_type=MESH,
        )

    def arrival(up, hops):
        held = me - (1 if up else -1) * (hops + 1)
        exists = (held >= 0) & (held < size)
        held = jnp.clip(held, 0, size - 1)
        return exists, held, pltpu.make_async_remote_copy(
            src_ref=own_ref,
            dst_ref=all_ref.at[held],
            send_sem=send.at[up * size + hops],
            recv_sem=recv.at[up * size + hops],
            device_id={"blk": neighbour(1 - up)[1]},
            device_id_type=MESH,
        )

    def when(pair, act):
        exists, copy = pair
        pl.when(exists)(lambda: act(copy))

    def turn(src, dst, at):
        take = pltpu.make_async_copy(src, block, local.at[0])
        take.start()
        take.wait()
        turned[...] = block[...].T
        columns = pl.ds(pl.multiple_of(at * rows, rows), rows)
        give = pltpu.make_async_copy(turned, dst.at[:, columns], local.at[1])
        give.start()
        give.wait()

    for up in ways:
        when(hop(up, 0), lambda copy: copy.start())
    keep = pltpu.make_async_copy(own_ref, all_ref.at[me], local.at[2])
    keep.start()
    turn(own_ref, all_t_ref, me)
    for at in range(size):
        turn(other_ref.at[at], other_t_ref, at)
    for hops in range(1, size):
        for up in ways:
            exists, held, copy = arrival(up, hops - 1)

            @pl.when(exists)
            def _(copy=copy, up=up, hops=hops):
                copy.wait_recv()
                if hops < size - 1:
                    when(hop(up, hops), lambda copy: copy.start())

        for up in ways:
            exists, held, copy = arrival(up, hops - 1)
            pl.when(exists)(lambda held=held: turn(all_ref.at[held], all_t_ref, held))
    for hops in range(size - 1):
        for up in ways:
            when(hop(up, hops), lambda copy: copy.wait_send())
    keep.wait()


def turn_gather(own, other, collective_id, after=()):
    size = lax.axis_size("blk")
    rows, width = own.shape
    anywhere = pl.BlockSpec(memory_space=pl.ANY)

    def kernel(*refs):
        turn_gather_kernel(*refs[:2], *refs[2 + len(after) :])

    return pl.pallas_call(
        kernel,
        in_specs=[anywhere] * (2 + len(after)),
        out_specs=[anywhere] * 3,
        out_shape=[
            jax.ShapeDtypeStruct((size, rows, width), BF16),
            jax.ShapeDtypeStruct((width, size * rows), BF16),
            jax.ShapeDtypeStruct((width, size * rows), BF16),
        ],
        scratch_shapes=[
            pltpu.VMEM((rows, width), BF16),
            pltpu.VMEM((width, rows), BF16),
            pltpu.SemaphoreType.DMA((2 * size,)),
            pltpu.SemaphoreType.DMA((2 * size,)),
            pltpu.SemaphoreType.DMA((3,)),
        ],
        compiler_params=pltpu.CompilerParams(
            collective_id=collective_id, has_side_effects=True, vmem_limit_bytes=VMEM_LIMIT
        ),
        name="turn_gather",
    )(own, other, *after)


def startup_kernel(
    head_ref, extra_ref, tok_ref, heads_ref, extras_ref, toks_ref,
    head_send, head_recv, extra_send, extra_recv, trade_send, trade_recv,
    z_send, z_recv, ay_send, ay_recv, by_send, by_recv, c_send, c_recv, local,
):
    blk, uly = lax.axis_size("blk"), spread(ULY)
    total = spread(ALL)
    z, u, me = lax.axis_index("blk"), lax.axis_index(ULY), lax.axis_index(ALL)
    far = lax.rem(u + 2, uly)
    near = u + 1 - 2 * lax.rem(u, 2)
    half = tok_ref.shape[0] // 2
    parts = (pl.ds(0, half), pl.ds(half, half))

    barrier = pltpu.get_barrier_semaphore()

    def greet(step):
        pl.semaphore_signal(
            barrier, inc=1, device_id=place(ALL, ahead(me, step, total)), device_id_type=MESH
        )

    each(total, greet)
    pl.semaphore_wait(barrier, total - 1)

    def send(src, dst, sent, got, to):
        return pltpu.make_async_remote_copy(
            src_ref=src, dst_ref=dst, send_sem=sent, recv_sem=got, device_id=to, device_id_type=MESH
        )

    def block(step, other, part):
        at = toks_ref.at[ahead(z, step, blk), far if other else u, parts[part]]
        return (tok_ref.at[parts[part]] if step == 0 and not other else at), at

    streams = ((0, 0), (0, 1), (1, 1))

    def hop(stream, up, hops):
        other, part = streams[stream]
        way = 1 if up else -1
        held, to = z - way * hops, z + way
        exists = (held >= 0) & (held < blk) & (to >= 0) & (to < blk)
        held, to = jnp.clip(held, 0, blk - 1), jnp.clip(to, 0, blk - 1)
        at = toks_ref.at[held, far if other else u, parts[part]]
        src = tok_ref.at[parts[part]] if hops == 0 and not other else at
        sem = (2 * stream + up) * blk + hops
        return exists, send(src, at, z_send.at[sem], z_recv.at[sem], {"blk": to})

    def arrival(stream, up, hops):
        other, part = streams[stream]
        way = 1 if up else -1
        held, sender = z - way * (hops + 1), z - way
        exists = (held >= 0) & (held < blk)
        held, sender = jnp.clip(held, 0, blk - 1), jnp.clip(sender, 0, blk - 1)
        at = toks_ref.at[held, far if other else u, parts[part]]
        sem = (2 * stream + up) * blk + hops
        return exists, send(tok_ref.at[parts[part]], at, z_send.at[sem], z_recv.at[sem], {"blk": sender})

    def when(pair, act):
        exists, copy = pair
        pl.when(exists)(lambda: act(copy))

    def a_y(step):
        return send(*block(step, 0, 0), ay_send.at[step], ay_recv.at[step], place(ULY, far))

    def b_y():
        return send(*block(0, 0, 1), by_send.at[0], by_recv.at[0], place(ULY, far))

    def to_near(step, other, part):
        sem = 4 * step + 2 * other + part
        return send(*block(step, other, part), c_send.at[sem], c_recv.at[sem], place(ULY, near))

    group = ("blk", *ULY)
    mine, here, b = lax.axis_index(group), spread(group), lax.axis_index("batch")

    def head(step):
        to = place(group, ahead(mine, step, here))
        src = head_ref.at[(to["y"] * lax.axis_size("core") + to["core"]) * blk + to["blk"]]
        return send(src, heads_ref.at[b, mine], head_send.at[step], head_recv.at[step], to)

    def extra(step):
        to = place(group, ahead(mine, step, here))
        return send(extra_ref, extras_ref.at[b, mine], extra_send.at[step], extra_recv.at[step], to)

    def trade(which):
        ref = (heads_ref, extras_ref)[which].at[b]
        return send(ref, ref, trade_send.at[which], trade_recv.at[which], {"batch": 1 - b})

    own = [
        pltpu.make_async_copy(tok_ref, toks_ref.at[z, u], local.at[0]),
        pltpu.make_async_copy(head_ref.at[u * blk + z], heads_ref.at[b, mine], local.at[1]),
        pltpu.make_async_copy(extra_ref, extras_ref.at[b, mine], local.at[2]),
    ]

    def start_head(step):
        extra(step).start()
        head(step).start()

    each(here, start_head)
    ways = (1, 0)
    b_y().start()
    for stream in range(2):
        for up in ways:
            when(hop(stream, up, 0), lambda copy: copy.start())
    a_y(0).start()
    to_near(0, 0, 0).start()
    to_near(0, 0, 1).start()

    for copy in own:
        copy.start()
    b_y().wait_recv()
    for up in ways:
        when(hop(2, up, 0), lambda copy: copy.start())
    to_near(0, 1, 1).start()
    def wait_head(step):
        extra(step).wait()
        head(step).wait()

    for hops in range(1, blk):
        if hops == min(2, blk - 1):
            each(here, wait_head)
            for copy in own[1:]:
                copy.wait()
            trade(0).start()
            trade(1).start()
        for stream, (other, part) in enumerate(streams):
            for up in ways:
                exists, copy = arrival(stream, up, hops - 1)
                step = blk - hops if up else hops

                @pl.when(exists)
                def _(copy=copy, stream=stream, other=other, part=part, up=up, step=step, hops=hops):
                    copy.wait_recv()
                    if hops < blk - 1:
                        when(hop(stream, up, hops), lambda copy: copy.start())
                    if stream == 0:
                        a_y(step).start()
                    to_near(step, other, part).start()

    for step in [0, *reversed(range(1, blk))]:
        a_y(step).wait_recv()
        to_near(step, 1, 0).start()
    for step in range(blk):
        for other in range(2):
            for part in range(2):
                to_near(step, other, part).wait_recv()

    trade(0).wait()
    trade(1).wait()
    own[0].wait()
    b_y().wait_send()
    for hops in range(blk - 1):
        for stream in range(3):
            for up in ways:
                when(hop(stream, up, hops), lambda copy: copy.wait_send())
    for step in range(blk):
        a_y(step).wait_send()
        for other in range(2):
            for part in range(2):
                to_near(step, other, part).wait_send()


def startup(heads, extra, tok, collective_id):
    batch, blk, uly = lax.axis_size("batch"), lax.axis_size("blk"), spread(ULY)
    anywhere = pl.BlockSpec(memory_space=pl.ANY)
    dma = pltpu.SemaphoreType.DMA
    return pl.pallas_call(
        startup_kernel,
        in_specs=[anywhere] * 3,
        out_specs=[anywhere] * 3,
        out_shape=[
            jax.ShapeDtypeStruct((batch, blk * uly, *heads.shape[1:]), BF16),
            jax.ShapeDtypeStruct((batch, blk * uly, *extra.shape), BF16),
            jax.ShapeDtypeStruct((blk, uly, *tok.shape), BF16),
        ],
        scratch_shapes=[
            *[dma((blk * uly,))] * 4,
            *[dma((2,))] * 2,
            *[dma((6 * blk,))] * 2,
            *[dma((blk,))] * 2,
            *[dma((1,))] * 2,
            *[dma((4 * blk,))] * 2,
            dma((3,)),
        ],
        compiler_params=pltpu.CompilerParams(collective_id=collective_id, has_side_effects=True),
        name="startup",
    )(heads, extra, tok)


def per_device_general(
    tokens, segments, routes, w_qkv, w_out, attn_gain, ffn_gain, qk_gain, router, w_gate_up, w_down, cotangent
):
    own_tokens = tokens[0]
    own_grad = cotangent[0]
    count_tok, width = own_tokens.shape
    head_dim = qk_gain.shape[1]
    heads = width // head_dim
    uly, blk, batch = spread(ULY), lax.axis_size("blk"), lax.axis_size("batch")
    blk_at, uly_at = lax.axis_index("blk"), lax.axis_index(ULY)
    group = batch * blk
    local_heads = heads // uly
    local_width = local_heads * head_dim
    rows = count_tok * uly
    seg_row = segments[0]
    length = seg_row.shape[0]
    number = router.shape[1]
    local_experts, _, units = w_down.shape
    shard_rows = w_qkv.shape[0]

    extra = jnp.concatenate([attn_gain[:, None], ffn_gain[:, None], router], axis=1)
    extra = jnp.pad(extra, ((0, 0), (0, LANES - extra.shape[1])))
    columns = w_qkv.reshape(shard_rows, 3, uly, local_width).transpose(2, 0, 1, 3)
    packed = jnp.concatenate(
        [
            columns.reshape(uly, shard_rows, 3 * local_width),
            jnp.broadcast_to(extra[None], (uly, shard_rows, LANES)),
        ],
        axis=2,
    )
    packed = swap(packed, ULY).reshape(uly * shard_rows, 3 * local_width + LANES)
    packed = lax.all_gather(packed, ROWS, axis=0, tiled=True)
    own_qkv = packed[:, : 3 * local_width]
    gain_attn = packed[:, 3 * local_width].astype(F32)
    gain_ffn = packed[:, 3 * local_width + 1].astype(F32)
    whole_router = packed[:, 3 * local_width + 2 : 3 * local_width + 2 + number]
    tokens_all = lax.all_gather(own_tokens, ULY, axis=0, tiled=True)
    to_rows = [(u * group + g, g * uly + u) for g in range(group) for u in range(uly)]
    own_out = lax.all_gather(lax.ppermute(w_out, ALL, to_rows), ROWS, axis=0, tiled=True)
    whole_gate_up = lax.all_gather(w_gate_up, PLANE, axis=0, tiled=False)
    whole_down = lax.all_gather(w_down, PLANE, axis=0, tiled=False)
    grad_blk = lax.all_gather(own_grad, "blk", axis=0, tiled=True)
    routes_blk = lax.all_gather(routes[0], "blk", axis=0, tiled=True)

    gain_query = qk_gain[0].astype(F32)
    gain_key = qk_gain[1].astype(F32)
    inputs_all = tokens_all.astype(F32)
    normed_one = inputs_all * rms_scale(inputs_all)
    hidden_one = (normed_one * gain_attn).astype(BF16)
    projected = dot_nn(hidden_one, own_qkv)
    query_raw = projected[:, :local_width].reshape(rows, local_heads, head_dim)
    key_raw = projected[:, local_width : 2 * local_width].reshape(rows, local_heads, head_dim)
    value_raw = projected[:, 2 * local_width :].reshape(rows, local_heads, head_dim)
    cos_table, sin_table = rope_tables(blk_at * rows, rows, head_dim)
    query_scale = rms_scale(query_raw)
    key_scale = rms_scale(key_raw)
    qkv = jnp.concatenate(
        [
            rotate(query_raw * query_scale * gain_query, cos_table, sin_table),
            rotate(key_raw * key_scale * gain_key, cos_table, sin_table),
            value_raw,
        ],
        axis=2,
    ).astype(BF16)
    qkv = qkv.transpose(1, 0, 2)

    by_heads = local_heads % blk == 0
    if by_heads:
        per = local_heads // blk

        def to_heads(values):
            columns = values.shape[2]
            moved = swap(values.reshape(blk, per, rows, columns), "blk")
            return moved.transpose(1, 0, 2, 3).reshape(per, length, columns)

        def to_rows_back(values):
            columns = values.shape[2]
            parts = values.reshape(per, blk, rows, columns).transpose(1, 0, 2, 3)
            return swap(parts, "blk").reshape(local_heads, rows, columns)

        q_src = kv_src = to_heads(qkv)
        cols = (0, 1, 2)
        seg_q = seg_row
        first_head = uly_at * local_heads + blk_at * per
    else:

        def to_heads(values):
            return values

        def to_rows_back(values):
            return values

        q_src = qkv
        kv_src = lax.all_gather(qkv[:, :, head_dim:], "blk", axis=1, tiled=True)
        cols = (0, 0, 1)
        seg_q = lax.dynamic_slice_in_dim(seg_row, blk_at * rows, rows)
        first_head = uly_at * local_heads
    attn_low, attn_f32, lse, top = attention_forward(q_src, kv_src, cols, seg_q, seg_row, head_dim)
    head_vector = lax.dynamic_update_slice_in_dim(
        jnp.full((heads,), NEG, F32), jnp.max(top, axis=(1, 2)) * head_dim**-0.5, first_head, 0
    )
    head_max = lax.pmax(head_vector, ALL)
    attn_rows = to_rows_back(attn_low)
    out_heads = own_out.reshape(local_heads, head_dim, width)
    branch = jnp.einsum("htc,hcd->td", attn_rows, out_heads, preferred_element_type=F32)
    inputs = own_tokens.astype(F32)
    mid = inputs + sum_scatter(branch, ULY)

    scale_two = rms_scale(mid)
    normed_two = mid * scale_two
    hidden_two = (normed_two * gain_ffn).astype(BF16)
    hidden_blk = lax.all_gather(hidden_two, "blk", axis=0, tiled=True)
    probs_blk = jax.nn.softmax(dot_nn(hidden_blk, whole_router), axis=1)
    names = jnp.arange(number, dtype=jnp.int32)
    chosen_blk = jnp.any(routes_blk[:, :, None] == names, axis=1).astype(F32)
    own_names = blk_at * local_experts
    gates = lax.dynamic_slice_in_dim(probs_blk * chosen_blk, own_names, local_experts, axis=1)
    most = min(MOST_TOKENS, hidden_blk.shape[0])
    packed_weights = jnp.concatenate([whole_gate_up, whole_down], axis=3)
    made = []
    for at in range(0, hidden_blk.shape[0], most):
        hidden_part, grad_part = hidden_blk[at : at + most], grad_blk[at : at + most]
        made.append(
            experts(
                hidden_part,
                hidden_part.T,
                grad_part,
                grad_part.T,
                gates[at : at + most],
                [(packed_weights, 0, local_experts)],
            )
        )
    out_part = jnp.concatenate([m[0] for m in made], axis=0)
    dx_part = jnp.concatenate([m[1] for m in made], axis=0)
    dg_part = jnp.concatenate([m[2] for m in made], axis=1)
    expert_grads = sum(m[3].astype(F32) for m in made).astype(BF16)
    expert_sums = lax.psum_scatter(expert_grads, PLANE, scatter_dimension=0, tiled=False).astype(F32)
    grad_gate_up = jnp.concatenate([expert_sums[0], expert_sums[1]], axis=2)
    grad_down = expert_sums[2]
    dg_parts = swap(dg_part.reshape(local_experts, blk, count_tok).transpose(1, 2, 0), "blk")
    grad_gates = dg_parts.transpose(1, 0, 2).reshape(count_tok, number)
    dx_sum = sum_scatter(dx_part, "blk")
    output = (mid + sum_scatter(out_part, "blk")).astype(BF16)
    router_probs = lax.dynamic_slice_in_dim(probs_blk, blk_at * count_tok, count_tok)
    chosen = lax.dynamic_slice_in_dim(chosen_blk, blk_at * count_tok, count_tok)
    grad_probs = chosen * grad_gates
    grad_logits = (
        router_probs * (grad_probs - jnp.sum(router_probs * grad_probs, axis=1, keepdims=True))
    ).astype(BF16)
    grad_hidden_two = dx_sum + dot_nt(grad_logits, whole_router)
    grad_router_part = dot_tn(hidden_two, grad_logits)
    grad_gain_ffn = jnp.sum(grad_hidden_two * normed_two, axis=0)
    grad_mid = own_grad.astype(F32) + norm_back(grad_hidden_two * gain_ffn, mid, scale_two)

    branch_grad = lax.all_gather(grad_mid.astype(BF16), ULY, axis=0, tiled=True)
    grad_attn = dot_nt(branch_grad, own_out).astype(BF16)
    grad_attn = to_heads(grad_attn.reshape(rows, local_heads, head_dim).transpose(1, 0, 2))
    grad_out_part = jnp.einsum("htc,td->hcd", attn_rows, branch_grad, preferred_element_type=F32)
    dq, dk, dv = attention_backward(
        q_src, kv_src, cols, grad_attn, attn_f32, lse, seg_q, seg_row, head_dim
    )
    if by_heads:
        dqkv = to_rows_back(jnp.concatenate([dq, dk, dv], axis=2))
        dq, dk, dv = jnp.split(dqkv, 3, axis=2)
    else:
        dk, dv = (lax.psum_scatter(g, "blk", scatter_dimension=1, tiled=True) for g in (dk, dv))
    dq, dk, dv = (g.transpose(1, 0, 2) for g in (dq, dk, dv))
    grad_query_norm = rotate(dq.astype(F32), cos_table, -sin_table)
    grad_key_norm = rotate(dk.astype(F32), cos_table, -sin_table)
    grad_gain_query = jnp.sum(grad_query_norm * (query_raw * query_scale), axis=(0, 1))
    grad_gain_key = jnp.sum(grad_key_norm * (key_raw * key_scale), axis=(0, 1))
    grad_projected = jnp.concatenate(
        [
            norm_back(grad_query_norm * gain_query, query_raw, query_scale)
            .reshape(rows, local_width)
            .astype(BF16),
            norm_back(grad_key_norm * gain_key, key_raw, key_scale)
            .reshape(rows, local_width)
            .astype(BF16),
            dv.reshape(rows, local_width),
        ],
        axis=1,
    )
    grad_hidden_part = dot_nt(grad_projected, own_qkv)
    grad_hidden_one = sum_scatter(grad_hidden_part, ULY)
    grad_gain_attn = jnp.sum(grad_hidden_part * normed_one, axis=0)
    grad_inputs = grad_mid + norm_back(grad_hidden_one * gain_attn, inputs, rms_scale(inputs))

    grad_qkv_part = dot_tn(hidden_one, grad_projected).astype(BF16)
    grad_qkv_rows = lax.psum_scatter(grad_qkv_part, ROWS, scatter_dimension=0, tiled=True)
    grad_qkv_rows = swap(grad_qkv_rows.reshape(uly, shard_rows, 3 * local_width), ULY)
    grad_qkv = (
        grad_qkv_rows.reshape(uly, shard_rows, 3, local_width)
        .transpose(1, 2, 0, 3)
        .reshape(shard_rows, 3 * width)
        .astype(F32)
    )
    grad_out_rows = lax.psum_scatter(
        grad_out_part.reshape(local_width, width).astype(BF16), ROWS, scatter_dimension=0, tiled=True
    )
    grad_out = lax.ppermute(grad_out_rows, ALL, [(b, a) for a, b in to_rows]).astype(F32)
    small = jnp.concatenate([grad_gain_attn[:, None], grad_gain_ffn[:, None], grad_router_part], axis=1)
    small = lax.psum_scatter(small, ALL, scatter_dimension=0, tiled=True)
    grad_qk_gain = lax.psum(jnp.stack([grad_gain_query, grad_gain_key]), ALL)

    clip_gamma = TAU / jnp.maximum(head_max, TAU)
    factor = jnp.repeat(jnp.sqrt(clip_gamma), head_dim)
    column_scale = jnp.concatenate([factor, factor, jnp.ones((width,), F32)])
    clipped = w_qkv.astype(F32) * column_scale[None, :]
    return (
        output[None],
        grad_inputs[None],
        grad_qkv,
        grad_out,
        small[:, 0],
        small[:, 1],
        grad_qk_gain,
        small[:, 2:],
        grad_gate_up,
        grad_down,
        clipped,
    )


def per_device(
    tokens, segments, routes, w_qkv, w_out, attn_gain, ffn_gain, qk_gain, router, w_gate_up, w_down, cotangent
):
    own_tokens = tokens[0]
    own_grad = cotangent[0]
    count_tok, width = own_tokens.shape
    head_dim = qk_gain.shape[1]
    heads = width // head_dim
    batch, blk, uly = lax.axis_size("batch"), lax.axis_size("blk"), spread(ULY)
    total, group = batch * blk * uly, batch * blk
    local_experts = w_down.shape[0]
    if uly != 4 or heads != blk * uly or blk < 2 or batch != 2 or local_experts != 4:
        return per_device_general(
            tokens, segments, routes, w_qkv, w_out, attn_gain, ffn_gain, qk_gain, router, w_gate_up, w_down, cotangent
        )
    blk_at, uly_at = lax.axis_index("blk"), lax.axis_index(ULY)
    rows = count_tok * uly
    seg_row = segments[0]
    length = seg_row.shape[0]
    number = router.shape[1]
    shard_rows = w_qkv.shape[0]

    to_rows = [(u * group + g, g * uly + u) for g in range(group) for u in range(uly)]
    rows_here = lax.ppermute(w_out, ALL, to_rows)
    rows_there = lax.ppermute(w_out, ALL, [(a, (b + total // 2) % total) for a, b in to_rows])


    def gather_experts(gate_up, down):
        return lax.all_gather(jnp.concatenate([gate_up, down], axis=2), PLANE, axis=0, tiled=False)

    weights_first = gather_experts(w_gate_up[:3], w_down[:3])
    extra = jnp.concatenate([attn_gain[None], ffn_gain[None], router.T], axis=0)
    kept = extra.shape[0]
    extra = jnp.pad(extra, ((0, -kept % 16), (0, -shard_rows % LANES)))
    by_head = w_qkv.reshape(shard_rows, 3, heads, head_dim).transpose(2, 0, 1, 3)
    own_qkv, extras, toks = startup(
        by_head.reshape(heads, shard_rows, 3 * head_dim), extra, own_tokens, 0
    )
    rows_here, rows_there, extras, later_gate_up, later_down = lax.optimization_barrier(
        (rows_here, rows_there, extras, w_gate_up[3:], w_down[3:])
    )
    weights_second = gather_experts(later_gate_up, later_down)
    is_first = lax.axis_index("batch") == 0
    pair = jnp.stack(
        [jnp.where(is_first, rows_here, rows_there), jnp.where(is_first, rows_there, rows_here)]
    )
    own_out = lax.all_to_all(
        jnp.broadcast_to(pair[None], (blk, *pair.shape)), "blk", split_axis=0, concat_axis=0, tiled=True
    )
    own_out = own_out.transpose(1, 0, 2, 3).reshape(blk, head_dim, width)
    own_qkv = own_qkv.reshape(width, 3 * head_dim)
    extras = extras.reshape(total, *extra.shape)[:, :kept, :shard_rows]
    extras = extras.transpose(1, 0, 2).reshape(kept, width)
    gain_attn = extras[0].astype(F32)
    gain_ffn = extras[1].astype(F32)
    router_t = extras[2:]

    gains = qk_gain.astype(F32)
    cos, sin = rope_rows(length, head_dim)
    hidden_one, qkv, raw = project(
        toks.reshape(length, width), gain_attn[None], own_qkv, cos, sin, gains
    )
    attn_low, attn_f32, lse, top = attention_forward(
        qkv[None], qkv[None], (0, 1, 2), seg_row, seg_row, head_dim
    )
    (attn_rows,) = exchange([(attn_low.reshape(blk, rows, head_dim), ("blk",), "swap")], 1)
    branch = jnp.einsum("htc,hcd->td", attn_rows, own_out, preferred_element_type=F32)
    branch, grad_blk, routes_blk = exchange(
        [
            (branch.astype(BF16).reshape(uly, count_tok, width), ULY, "pairsum"),
            (own_grad, ("blk",), "line"),
            (routes[0].T, ("blk",), "gather"),
        ],
        2,
    )
    inputs = own_tokens.astype(F32)
    mid = inputs + branch

    scale_two = rms_scale(mid)
    normed_two = mid * scale_two
    hidden_two = (normed_two * gain_ffn).astype(BF16)
    hidden_blk, hidden_t, grad_t = turn_gather(hidden_two, grad_blk, 3)
    tokens_blk = blk * count_tok
    hidden_blk = hidden_blk.reshape(tokens_blk, width)
    grad_blk = grad_blk.reshape(tokens_blk, width)
    probs_blk = jax.nn.softmax(dot_nt(hidden_blk, router_t), axis=1)
    names = jnp.arange(number, dtype=jnp.int32)
    chosen_blk = jnp.any(routes_blk[:, :, :, None] == names, axis=1).astype(F32)
    chosen_blk = chosen_blk.reshape(tokens_blk, number)
    gates = lax.dynamic_slice_in_dim(
        probs_blk * chosen_blk, blk_at * local_experts, local_experts, axis=1
    )
    shared = (hidden_blk, hidden_t, grad_blk, grad_t)
    out_part, dx_part, dg_first, grads_first = experts(*shared, gates[:, :1], [(weights_first, 0, 1)])
    sums_first = lax.psum_scatter(grads_first, PLANE, scatter_dimension=0, tiled=False)
    out_part, dx_part, dg_others, grads_others = experts(
        *shared, gates[:, 1:], [(weights_first, 1, 2), (weights_second, 0, 1)], before=(out_part, dx_part)
    )
    sums_others = lax.psum_scatter(grads_others, PLANE, scatter_dimension=0, tiled=False)
    finished = finish_experts(sums_first, 0, local_experts)
    grad_gate_up, grad_down = finish_experts(sums_others, 1, local_experts, before=finished)
    dg_part = jnp.concatenate([dg_first, dg_others], axis=0)
    dg_part = dg_part.reshape(local_experts, blk, count_tok)
    dx_parts, dg_parts = exchange(
        [
            (dx_part.reshape(blk, count_tok, width), ("blk",), "swap"),
            (dg_part.transpose(1, 0, 2), ("blk",), "swap"),
        ],
        4,
    )
    out_part = out_part.reshape(blk, count_tok, width)
    out_part, dx_parts = lax.optimization_barrier((out_part, dx_parts))
    out_parts = lax.all_to_all(out_part, "blk", split_axis=0, concat_axis=0, tiled=True)
    output = (mid + jnp.sum(out_parts.astype(F32), axis=0)).astype(BF16)
    router_probs = lax.dynamic_slice_in_dim(probs_blk, blk_at * count_tok, count_tok)
    chosen = lax.dynamic_slice_in_dim(chosen_blk, blk_at * count_tok, count_tok)
    grad_probs = chosen * dg_parts.reshape(number, count_tok).T
    grad_logits = (
        router_probs * (grad_probs - jnp.sum(router_probs * grad_probs, axis=1, keepdims=True))
    ).astype(BF16)
    grad_hidden_two = jnp.sum(dx_parts.astype(F32), axis=0) + dot_nn(grad_logits, router_t)
    grad_router_t = dot_tn(grad_logits, hidden_two)
    grad_gain_ffn = jnp.sum(grad_hidden_two * normed_two, axis=0)
    grad_mid = own_grad.astype(F32) + norm_back(grad_hidden_two * gain_ffn, mid, scale_two)

    (branch_grad,) = exchange([(grad_mid.astype(BF16), ULY, "relay")], 5)
    branch_grad, sent_qkv = lax.optimization_barrier((branch_grad, own_qkv))
    far_qkv = lax.ppermute(sent_qkv, "y", [(0, 1), (1, 0)])
    branch_grad = branch_grad.reshape(rows, width)
    grad_attn = jnp.einsum("td,hcd->htc", branch_grad, own_out, preferred_element_type=F32).astype(BF16)
    grad_out_part = jnp.einsum("htc,td->hcd", attn_rows, branch_grad, preferred_element_type=F32)
    grad_out_part = grad_out_part.astype(BF16).reshape(batch, blk, shard_rows, width)
    batch_at = lax.axis_index("batch")
    grad_attn, got_out_part = exchange(
        [
            (grad_attn, ("blk",), "swap"),
            (
                lax.dynamic_index_in_dim(grad_out_part, 1 - batch_at, 0, keepdims=False),
                ("batch",),
                "trade",
            ),
        ],
        6,
        after=[out_parts],
    )
    grad_out_part = lax.dynamic_index_in_dim(grad_out_part, batch_at, 0, keepdims=False) + got_out_part
    grad_projected, grad_gains = project_back(
        qkv, grad_attn.reshape(length, head_dim), attn_f32, lse, seg_row, raw, cos, sin, gains
    )
    grad_qkv_part = dot_tn(hidden_one, grad_projected).astype(BF16)
    by_batch = grad_qkv_part.reshape(batch, width // batch, 3 * head_dim)
    projected_blk, got_qkv_part, near_qkv, cross_qkv, grad_out_parts = exchange(
        [
            (grad_projected.reshape(blk, uly, count_tok, 3 * head_dim), ULY, "swap1"),
            (
                lax.dynamic_index_in_dim(by_batch, 1 - batch_at, 0, keepdims=False),
                ("batch",),
                "trade",
            ),
            (own_qkv, ("core",), "trade"),
            (far_qkv, ("core",), "trade"),
            (grad_out_part, ("blk",), "swap"),
        ],
        7,
    )
    grad_out = lax.ppermute(
        jnp.sum(grad_out_parts.astype(F32), axis=0).astype(BF16), ALL, [(b, a) for a, b in to_rows]
    ).astype(F32)
    grad_qkv_part = lax.dynamic_index_in_dim(by_batch, batch_at, 0, keepdims=False) + got_qkv_part
    grad_qkv_parts = lax.all_to_all(
        grad_qkv_part.reshape(total // batch, shard_rows, 3 * head_dim),
        ("blk", *ULY),
        split_axis=0,
        concat_axis=0,
        tiled=True,
    )

    grad_hidden_part, grad_gain_attn = hidden_back(
        projected_blk.reshape(uly, tokens_blk, 3 * head_dim),
        own_qkv,
        near_qkv,
        far_qkv,
        cross_qkv,
        hidden_one.reshape(blk, uly, count_tok, width),
    )
    grad_gain_attn = grad_gain_attn[0] / gain_attn

    small = jnp.concatenate([grad_gain_attn[None], grad_gain_ffn[None], grad_router_t], axis=0)
    small = small.reshape(kept, total, shard_rows).transpose(1, 0, 2)
    small = jnp.pad(small, ((0, 0), (0, 0), (0, LANES - shard_rows)))
    head_row = jnp.where(
        jnp.arange(LANES) == uly_at * blk + blk_at, jnp.max(top) * head_dim**-0.5, NEG
    )
    to_all = jnp.concatenate([grad_gains, head_row[None]], axis=0)
    small = jnp.concatenate([small, jnp.broadcast_to(to_all[None], (total, 3, LANES))], axis=1)
    small = jnp.pad(small, ((0, 0), (0, -small.shape[1] % 8), (0, 0)))
    grad_hidden_parts, small = exchange(
        [
            (grad_hidden_part, ("blk",), "swap"),
            (small, ALL, "swap"),
        ],
        8,
    )
    grad_qkv_parts, small = lax.optimization_barrier((grad_qkv_parts, small))
    grad_qkv = merge_heads(grad_qkv_parts.reshape(blk, uly, shard_rows, 3 * head_dim))
    grad_hidden_one = jnp.sum(grad_hidden_parts.astype(F32), axis=0)
    grad_inputs = grad_mid + norm_back(grad_hidden_one * gain_attn, inputs, rms_scale(inputs))
    sums = jnp.sum(small, axis=0)
    head_max = jnp.max(small[:, kept + 2, :heads], axis=0)
    factor = jnp.repeat(jnp.sqrt(TAU / jnp.maximum(head_max, TAU)), head_dim)
    column_scale = jnp.concatenate([factor, factor, jnp.ones((width,), F32)])
    clipped = w_qkv.astype(F32) * column_scale[None, :]
    return (
        output[None],
        grad_inputs[None],
        grad_qkv,
        grad_out,
        sums[0, :shard_rows],
        sums[1, :shard_rows],
        sums[kept : kept + 2],
        sums[2:kept, :shard_rows].T,
        grad_gate_up,
        grad_down,
        clipped,
    )


def solution(mesh):
    in_specs = (
        P("batch", ("blk", *ULY), None),
        P("batch", None),
        P("batch", ("blk", *ULY), None),
        P(ALL, None),
        P(ALL, None),
        P(ALL),
        P(ALL),
        P(),
        P(ALL, None),
        P("blk", PLANE, None),
        P("blk", PLANE, None),
        P("batch", ("blk", *ULY), None),
    )
    out_specs = (
        P("batch", ("blk", *ULY), None),
        P("batch", ("blk", *ULY), None),
        P(ALL, None),
        P(ALL, None),
        P(ALL),
        P(ALL),
        P(),
        P(ALL, None),
        P("blk", PLANE, None),
        P("blk", PLANE, None),
        P(ALL, None),
    )
    cores = 2 - mesh.shape["uly"] % 2
    mesh = Mesh(
        mesh.devices.reshape(*(mesh.shape[axis] for axis in ROWS), mesh.shape["uly"] // cores, cores), ALL
    )
    return jax.shard_map(
        per_device, mesh=mesh, in_specs=in_specs, out_specs=out_specs, check_vma=False
    )
```

```python
import functools
import math

import jax
import jax.numpy as jnp
from jax import lax
from jax.experimental import pallas as pl
from jax.experimental.pallas import tpu as pltpu
from jax.sharding import Mesh
from jax.sharding import PartitionSpec as P

EPS = 1e-06
THETA = 50000.0
TAU = 4.0
NEG = -1e30
LOG2E = 1.4426950408889634
LANES = 128
MOST_TOKENS = 512
VMEM_LIMIT = 60 * 1024 * 1024

ULY = ("y", "core")
ALL = ("batch", "blk", *ULY)
ROWS = ("batch", "blk")
PLANE = ("batch", *ULY)
CHIPS = ("batch", "y")

MESH = pl.DeviceIdType.MESH
BF16 = jnp.bfloat16
F32 = jnp.float32


def rms_scale(values):
    return lax.rsqrt(jnp.mean(values * values, axis=-1, keepdims=True) + EPS)


def norm_back(grad_normed, values, scale):
    normed = values * scale
    return scale * (grad_normed - normed * jnp.mean(grad_normed * normed, axis=-1, keepdims=True))


def rope_tables(offset, length, head_dim):
    half_dim = head_dim // 2
    frequency = THETA ** (-jnp.arange(half_dim, dtype=F32) * 2.0 / head_dim)
    positions = (offset + jnp.arange(length, dtype=jnp.int32)).astype(F32)
    angles = positions[:, None] * frequency[None, :]
    return (jnp.cos(angles)[:, None, :], jnp.sin(angles)[:, None, :])


def rope_rows(length, head_dim):
    fine = math.gcd(length, LANES)
    frequency = THETA ** (-jnp.arange(head_dim // 2, dtype=F32) * 2.0 / head_dim)
    frequency = jnp.concatenate([frequency, frequency])
    coarse_angle = (jnp.arange(length // fine, dtype=F32) * fine)[:, None, None] * frequency
    fine_angle = jnp.arange(fine, dtype=F32)[None, :, None] * frequency
    cos_a, sin_a, cos_b, sin_b = lax.optimization_barrier(
        (jnp.cos(coarse_angle), jnp.sin(coarse_angle), jnp.cos(fine_angle), jnp.sin(fine_angle))
    )
    sign = jnp.where(jnp.arange(head_dim) < head_dim // 2, -1.0, 1.0)
    cos = cos_a * cos_b - sin_a * sin_b
    sin = (sin_a * cos_b + cos_a * sin_b) * sign
    return cos.reshape(length, head_dim), sin.reshape(length, head_dim)


def rotate(values, cos_table, sin_table):
    half_dim = values.shape[-1] // 2
    first = values[..., :half_dim]
    second = values[..., half_dim:]
    return jnp.concatenate(
        [first * cos_table - second * sin_table, second * cos_table + first * sin_table], axis=-1
    )


def dot_nn(a, b):
    return lax.dot_general(a, b, (((1,), (0,)), ((), ())), preferred_element_type=F32)


def dot_nt(a, b):
    return lax.dot_general(a, b, (((1,), (1,)), ((), ())), preferred_element_type=F32)


def dot_tn(a, b):
    return lax.dot_general(a, b, (((0,), (0,)), ((), ())), preferred_element_type=F32)


def key_chunks(length):
    size = min(512, length)
    return size, length // size


def attn_fwd_kernel(factor, q_ref, k_ref, v_ref, sq_ref, sk_ref, o_ref, of_ref, lse_ref, top_ref, vt_ref):
    length = k_ref.shape[1]
    size, count = key_chunks(length)
    tile, head_dim = q_ref.shape[1:]

    @pl.when(pl.program_id(1) == 0)
    def _():
        vt_ref[...] = v_ref[0].astype(F32).T.astype(BF16)

    q = q_ref[0]
    seg_q = sq_ref[...]

    def step(j, carried):
        total, top, acc = carried
        at = pl.multiple_of(j * size, size)
        scores = dot_nt(k_ref[0, pl.ds(at, size), :], q)
        scores = jnp.where(sk_ref[pl.ds(at, size), :] == seg_q, scores, NEG)
        top = jnp.maximum(top, jnp.max(scores, axis=0, keepdims=True))
        weights = jnp.exp2(scores * factor)
        total = total + jnp.sum(weights, axis=0, keepdims=True)
        acc = acc + dot_nn(vt_ref[:, pl.ds(at, size)], weights.astype(BF16))
        return total, top, acc

    start = (
        jnp.zeros((1, tile), F32),
        jnp.full((1, tile), NEG, F32),
        jnp.zeros((head_dim, tile), F32),
    )
    total, top, acc = lax.fori_loop(0, count, step, start, unroll=count <= 4)
    out = (acc * (1.0 / total)).T
    o_ref[0] = out.astype(BF16)
    of_ref[0] = out
    lse_ref[0] = jnp.log2(total)
    top_ref[0] = top


def attn_bwd_kernel(
    factor, scale, q_ref, k_ref, v_ref, do_ref, of_ref, lse_ref, sq_ref, sk_ref,
    dq_ref, dk_ref, dv_ref, kt_ref, dk_acc, dv_acc,
):
    length = k_ref.shape[1]
    size, count = key_chunks(length)
    tile, head_dim = q_ref.shape[1:]

    @pl.when(pl.program_id(1) == 0)
    def _():
        kt_ref[...] = k_ref[0].astype(F32).T.astype(BF16)
        dk_acc[...] = jnp.zeros_like(dk_acc)
        dv_acc[...] = jnp.zeros_like(dv_acc)

    q = q_ref[0]
    grad = do_ref[0]
    seg_q = sq_ref[...]
    lse = lse_ref[0]
    row_dot = jnp.sum((grad.astype(F32) * of_ref[0]).T, axis=0, keepdims=True)

    def step(j, dq_t):
        at = pl.multiple_of(j * size, size)
        rows = pl.ds(at, size)
        scores = dot_nt(k_ref[0, rows, :], q)
        scores = jnp.where(sk_ref[rows, :] == seg_q, scores, NEG)
        weights = jnp.exp2(scores * factor - lse)
        grad_weights = dot_nt(v_ref[0, rows, :], grad)
        grad_scores = (weights * (grad_weights - row_dot)).astype(BF16)
        dk_acc[rows, :] += dot_nn(grad_scores, q)
        dv_acc[rows, :] += dot_nn(weights.astype(BF16), grad)
        return dq_t + dot_nn(kt_ref[:, rows], grad_scores)

    dq_t = lax.fori_loop(0, count, step, jnp.zeros((head_dim, tile), F32), unroll=count <= 4)
    dq_ref[0] = (dq_t * scale).T.astype(BF16)

    @pl.when(pl.program_id(1) == pl.num_programs(1) - 1)
    def _():
        dk_ref[0] = (dk_acc[...] * scale).astype(BF16)
        dv_ref[0] = dv_acc[...].astype(BF16)


def attention_tile(queries, length):
    return min(queries, 256 if length <= 4096 else 128)


def attention_forward(q_src, kv_src, cols, seg_q, seg_k, head_dim):
    heads, queries = q_src.shape[:2]
    length = kv_src.shape[1]
    tile = attention_tile(queries, length)
    q_col, k_col, v_col = cols
    factor = head_dim**-0.5 * LOG2E
    row = pl.BlockSpec((1, 1, tile), lambda h, i: (h, 0, i))
    block = pl.BlockSpec((1, tile, head_dim), lambda h, i: (h, i, 0))
    return pl.pallas_call(
        functools.partial(attn_fwd_kernel, factor),
        grid=(heads, queries // tile),
        in_specs=[
            pl.BlockSpec((1, tile, head_dim), lambda h, i: (h, i, q_col)),
            pl.BlockSpec((1, length, head_dim), lambda h, i: (h, 0, k_col)),
            pl.BlockSpec((1, length, head_dim), lambda h, i: (h, 0, v_col)),
            pl.BlockSpec((1, tile), lambda h, i: (0, i)),
            pl.BlockSpec((length, 1), lambda h, i: (0, 0)),
        ],
        out_specs=[block, block, row, row],
        out_shape=[
            jax.ShapeDtypeStruct((heads, queries, head_dim), BF16),
            jax.ShapeDtypeStruct((heads, queries, head_dim), F32),
            jax.ShapeDtypeStruct((heads, 1, queries), F32),
            jax.ShapeDtypeStruct((heads, 1, queries), F32),
        ],
        scratch_shapes=[pltpu.VMEM((head_dim, length), BF16)],
        compiler_params=pltpu.CompilerParams(vmem_limit_bytes=VMEM_LIMIT),
        cost_estimate=pl.CostEstimate(
            flops=4 * heads * queries * length * head_dim,
            bytes_accessed=heads * (queries + length) * head_dim * 8,
            transcendentals=heads * queries * length,
        ),
        name="attend",
    )(q_src, kv_src, kv_src, seg_q.reshape(1, -1), seg_k.reshape(-1, 1))


def attention_backward(q_src, kv_src, cols, grad, out_f32, lse, seg_q, seg_k, head_dim):
    heads, queries = q_src.shape[:2]
    length = kv_src.shape[1]
    tile = attention_tile(queries, length)
    q_col, k_col, v_col = cols
    scale = head_dim**-0.5
    row = pl.BlockSpec((1, 1, tile), lambda h, i: (h, 0, i))
    block = pl.BlockSpec((1, tile, head_dim), lambda h, i: (h, i, 0))
    whole = pl.BlockSpec((1, length, head_dim), lambda h, i: (h, 0, 0))
    return pl.pallas_call(
        functools.partial(attn_bwd_kernel, scale * LOG2E, scale),
        grid=(heads, queries // tile),
        in_specs=[
            pl.BlockSpec((1, tile, head_dim), lambda h, i: (h, i, q_col)),
            pl.BlockSpec((1, length, head_dim), lambda h, i: (h, 0, k_col)),
            pl.BlockSpec((1, length, head_dim), lambda h, i: (h, 0, v_col)),
            block,
            block,
            row,
            pl.BlockSpec((1, tile), lambda h, i: (0, i)),
            pl.BlockSpec((length, 1), lambda h, i: (0, 0)),
        ],
        out_specs=[block, whole, whole],
        out_shape=[
            jax.ShapeDtypeStruct((heads, queries, head_dim), BF16),
            jax.ShapeDtypeStruct((heads, length, head_dim), BF16),
            jax.ShapeDtypeStruct((heads, length, head_dim), BF16),
        ],
        scratch_shapes=[
            pltpu.VMEM((head_dim, length), BF16),
            pltpu.VMEM((length, head_dim), F32),
            pltpu.VMEM((length, head_dim), F32),
        ],
        compiler_params=pltpu.CompilerParams(vmem_limit_bytes=VMEM_LIMIT),
        cost_estimate=pl.CostEstimate(
            flops=10 * heads * queries * length * head_dim,
            bytes_accessed=heads * (queries + length) * head_dim * 12,
            transcendentals=heads * queries * length,
        ),
        name="attend_back",
    )(q_src, kv_src, kv_src, grad, out_f32, lse, seg_q.reshape(1, -1), seg_k.reshape(-1, 1))


def expert_step(expert, h_ref, ht_ref, dy_ref, dyt_ref, gate_ref, wg_ref, wu_ref, wd_ref, dg_ref, out_acc, dx_acc):
    width = h_ref.shape[1]
    cols = wg_ref.shape[3]
    w_gate = wg_ref[...].reshape(width, cols)
    w_up = wu_ref[...].reshape(width, cols)
    w_down = wd_ref[...].reshape(width, cols)
    gates = gate_ref[...]
    mine = lax.broadcasted_iota(jnp.int32, gates.shape, 1) == expert
    gate = jnp.sum(jnp.where(mine, gates, 0.0), axis=1, keepdims=True)
    a_gate = dot_nn(h_ref[...], w_gate)
    a_up = dot_nn(h_ref[...], w_up)
    raw = dot_nn(dy_ref[...], w_down)
    sigma = 1.0 / (1.0 + jnp.exp2(a_gate * -LOG2E))
    swish = a_gate * sigma
    act = swish * a_up
    dg_ref[0] += jnp.sum(raw * act, axis=1, keepdims=True)
    gated = (gate * act).astype(BF16)
    d_act = gate * raw
    d_gate = (d_act * a_up * (sigma + swish * (1.0 - sigma))).astype(BF16)
    d_up = (d_act * swish).astype(BF16)
    out_acc[...] += dot_nt(gated, w_down)
    dx_acc[...] += dot_nt(d_gate, w_gate) + dot_nt(d_up, w_up)
    for part, (left, right) in enumerate([(ht_ref, d_gate), (ht_ref, d_up), (dyt_ref, gated)]):
        yield part, dot_nn(left[...], right).astype(BF16)


def expert_kernel(more, counts, *refs):
    h_ref, ht_ref, dy_ref, dyt_ref, gate_ref = refs[:5]
    sources = [refs[5 + 3 * i : 8 + 3 * i] for i in range(len(counts))]
    out_ref, dx_ref, dg_ref, gr_ref, out_acc, dx_acc = refs[-6:]
    step, last = pl.program_id(0), pl.num_programs(0) - 1
    parts, _, part_rows, cols = sources[0][0].shape
    chunks = (last + 1) // sum(counts)

    @pl.when(step == 0)
    def _():
        if more:
            out0_ref, dx0_ref = refs[-8:-6]
            out_acc[...] = out0_ref[...].astype(F32)
            dx_acc[...] = dx0_ref[...].astype(F32)
        else:
            out_acc[...] = jnp.zeros_like(out_acc)
            dx_acc[...] = jnp.zeros_like(dx_acc)

    @pl.when(step % chunks == 0)
    def _():
        dg_ref[...] = jnp.zeros_like(dg_ref)

    begin = 0
    for source, count in zip(sources, counts):
        end = begin + count * chunks

        @pl.when((step >= begin) & (step < end))
        def _(source=source):
            for part, made in expert_step(
                step // chunks, h_ref, ht_ref, dy_ref, dyt_ref, gate_ref, *source, dg_ref, out_acc, dx_acc
            ):
                gr_ref[:, part, 0] = made.reshape(parts, part_rows, cols)

        begin = end

    @pl.when(step == last)
    def _():
        out_ref[...] = out_acc[...].astype(BF16)
        dx_ref[...] = dx_acc[...].astype(BF16)


def experts(hidden, hidden_t, grad, grad_t, gates, sources, before=()):
    tokens, width = hidden.shape
    parts, _, part_rows, units = sources[0][0].shape
    units = units // 3
    counts = [count for _, _, count in sources]
    total = sum(counts)
    cols = min(256, units)
    chunks = units // cols
    once = pl.Buffered(1)
    whole = pl.BlockSpec((tokens, width), lambda s: (0, 0), pipeline_mode=once)
    whole_t = pl.BlockSpec((width, tokens), lambda s: (0, 0), pipeline_mode=once)
    result = pl.BlockSpec((tokens, width), lambda s: (0, 0))

    def weight(source, kind):
        _, first, count = sources[source]
        begin = sum(counts[:source]) * chunks

        def index(step):
            at = jnp.clip(step - begin, 0, count * chunks - 1)
            return (0, first + at // chunks, 0, kind * chunks + at % chunks)

        return pl.BlockSpec((parts, 1, part_rows, cols), index)

    return pl.pallas_call(
        functools.partial(expert_kernel, bool(before), counts),
        grid=(total * chunks,),
        in_specs=[
            whole,
            whole_t,
            whole,
            whole_t,
            pl.BlockSpec(gates.shape, lambda s: (0, 0), pipeline_mode=once),
            *[weight(source, kind) for source in range(len(sources)) for kind in range(3)],
            *[whole for _ in before],
        ],
        out_specs=[
            result,
            result,
            pl.BlockSpec((1, tokens, 1), lambda s: (s // chunks, 0, 0)),
            pl.BlockSpec((parts, 3, 1, part_rows, cols), lambda s: (0, 0, s // chunks, 0, s % chunks)),
        ],
        out_shape=[
            jax.ShapeDtypeStruct((tokens, width), BF16),
            jax.ShapeDtypeStruct((tokens, width), BF16),
            jax.ShapeDtypeStruct((total, tokens, 1), F32),
            jax.ShapeDtypeStruct((parts, 3, total, part_rows, units), BF16),
        ],
        scratch_shapes=[
            pltpu.VMEM((tokens, width), F32),
            pltpu.VMEM((tokens, width), F32),
        ],
        compiler_params=pltpu.CompilerParams(vmem_limit_bytes=VMEM_LIMIT),
        cost_estimate=pl.CostEstimate(
            flops=18 * total * tokens * width * units,
            bytes_accessed=12 * total * width * units,
            transcendentals=total * tokens * units,
        ),
        name="experts",
    )(hidden, hidden_t, grad, grad_t, gates, *[array for array, _, _ in sources for _ in range(3)], *before)


def finish_experts_kernel(sums_ref, *refs):
    gate_up_ref, down_ref = refs[-2:]
    units = down_ref.shape[2]
    gate_up_ref[0, :, :units] = sums_ref[0, 0].astype(F32)
    gate_up_ref[0, :, units:] = sums_ref[1, 0].astype(F32)
    down_ref[0] = sums_ref[2, 0].astype(F32)


def finish_experts(sums, at, total, before=()):
    _, count, rows, units = sums.shape
    tile = min(128, rows)
    return pl.pallas_call(
        finish_experts_kernel,
        grid=(count, rows // tile),
        in_specs=[
            pl.BlockSpec((3, 1, tile, units), lambda e, r: (0, e, r, 0)),
            *[pl.BlockSpec(memory_space=pl.ANY) for _ in before],
        ],
        out_specs=[
            pl.BlockSpec((1, tile, 2 * units), lambda e, r: (at + e, r, 0)),
            pl.BlockSpec((1, tile, units), lambda e, r: (at + e, r, 0)),
        ],
        out_shape=[
            jax.ShapeDtypeStruct((total, rows, 2 * units), F32),
            jax.ShapeDtypeStruct((total, rows, units), F32),
        ],
        input_output_aliases={1 + i: i for i in range(len(before))},
        compiler_params=pltpu.CompilerParams(vmem_limit_bytes=VMEM_LIMIT),
        name="finish_experts",
    )(sums, *before)


def turn(values, cos, sin):
    return values * cos + pltpu.roll(values, values.shape[1] // 2, 1) * sin


def project_kernel(
    tok_ref, gain_ref, w_ref, cos_ref, sin_ref, gains_ref, hidden_ref, qkv_ref, raw_ref
):
    head_dim = cos_ref.shape[1]
    values = tok_ref[...].astype(F32)
    hidden = (values * rms_scale(values) * gain_ref[...]).astype(BF16)
    hidden_ref[...] = hidden
    projected = dot_nn(hidden, w_ref[...])
    raw_ref[...] = projected[:, : 2 * head_dim]
    for part in range(2):
        at = slice(part * head_dim, (part + 1) * head_dim)
        raw = projected[:, at]
        normed = raw * rms_scale(raw) * gains_ref[part : part + 1, :]
        qkv_ref[:, at] = turn(normed, cos_ref[...], sin_ref[...]).astype(BF16)
    qkv_ref[:, 2 * head_dim :] = projected[:, 2 * head_dim :].astype(BF16)


def project(toks, gain, weights, cos, sin, gains):
    length, width = toks.shape
    head_dim = cos.shape[1]
    tile = min(256, length)

    def rows(columns):
        return pl.BlockSpec((tile, columns), lambda i: (i, 0))

    def fixed(shape):
        return pl.BlockSpec(shape, lambda i: (0, 0))

    return pl.pallas_call(
        project_kernel,
        grid=(length // tile,),
        in_specs=[
            rows(width),
            fixed((1, width)),
            fixed(weights.shape),
            rows(head_dim),
            rows(head_dim),
            fixed(gains.shape),
        ],
        out_specs=[rows(width), rows(3 * head_dim), rows(2 * head_dim)],
        out_shape=[
            jax.ShapeDtypeStruct((length, width), BF16),
            jax.ShapeDtypeStruct((length, 3 * head_dim), BF16),
            jax.ShapeDtypeStruct((length, 2 * head_dim), F32),
        ],
        compiler_params=pltpu.CompilerParams(vmem_limit_bytes=VMEM_LIMIT),
        name="project",
    )(toks, gain, weights, cos, sin, gains)


def project_back_kernel(
    factor, scale, q_ref, k_ref, v_ref, do_ref, of_ref, lse_ref, sq_ref, sk_ref,
    raw_q_ref, raw_k_ref, cos_q_ref, sin_q_ref, cos_ref, sin_ref, gains_ref,
    dp_ref, dgain_ref, kt_ref, dk_acc, dv_acc,
):
    length, head_dim = k_ref.shape
    size, count = key_chunks(length)
    tile = q_ref.shape[0]
    step_at = pl.program_id(0)

    @pl.when(step_at == 0)
    def _():
        kt_ref[...] = k_ref[...].astype(F32).T.astype(BF16)
        dk_acc[...] = jnp.zeros_like(dk_acc)
        dv_acc[...] = jnp.zeros_like(dv_acc)
        dgain_ref[...] = jnp.zeros_like(dgain_ref)

    def to_raw(part, grad, raw, cos, sin):
        grad = turn(grad.astype(BF16).astype(F32), cos, -sin)
        raw_scale = rms_scale(raw)
        dgain_ref[part : part + 1, :] += jnp.sum(grad * (raw * raw_scale), axis=0, keepdims=True)
        return norm_back(grad * gains_ref[part : part + 1, :], raw, raw_scale).astype(BF16)

    q = q_ref[...]
    grad = do_ref[...]
    seg_q = sq_ref[...]
    lse = lse_ref[0]
    row_dot = jnp.sum((grad.astype(F32) * of_ref[0]).T, axis=0, keepdims=True)
    dq_t = jnp.zeros((head_dim, tile), F32)
    for j in range(count):
        rows = slice(j * size, (j + 1) * size)
        scores = dot_nt(k_ref[rows, :], q)
        scores = jnp.where(sk_ref[rows, :] == seg_q, scores, NEG)
        weights = jnp.exp2(scores * factor - lse)
        grad_weights = dot_nt(v_ref[rows, :], grad)
        grad_scores = (weights * (grad_weights - row_dot)).astype(BF16)
        dk_acc[rows, :] += dot_nn(grad_scores, q)
        dv_acc[rows, :] += dot_nn(weights.astype(BF16), grad)
        dq_t = dq_t + dot_nn(kt_ref[:, rows], grad_scores)
    own = pl.ds(pl.multiple_of(step_at * tile, tile), tile)
    dp_ref[own, :head_dim] = to_raw(
        0, (dq_t * scale).T, raw_q_ref[...], cos_q_ref[...], sin_q_ref[...]
    )

    @pl.when(step_at == pl.num_programs(0) - 1)
    def _():
        dp_ref[:, head_dim : 2 * head_dim] = to_raw(
            1, dk_acc[...] * scale, raw_k_ref[...], cos_ref[...], sin_ref[...]
        )
        dp_ref[:, 2 * head_dim :] = dv_acc[...].astype(BF16)


def project_back(qkv, grad, out_f32, lse, segments, raw, cos, sin, gains):
    length, head_dim = grad.shape
    tile = min(256, length)

    def rows(column):
        return pl.BlockSpec((tile, head_dim), lambda i: (i, column))

    def whole(column):
        return pl.BlockSpec((length, head_dim), lambda i: (0, column))

    return pl.pallas_call(
        functools.partial(project_back_kernel, head_dim**-0.5 * LOG2E, head_dim**-0.5),
        grid=(length // tile,),
        in_specs=[
            rows(0),
            whole(1),
            whole(2),
            rows(0),
            pl.BlockSpec((1, tile, head_dim), lambda i: (0, i, 0)),
            pl.BlockSpec((1, 1, tile), lambda i: (0, 0, i)),
            pl.BlockSpec((1, tile), lambda i: (0, i)),
            pl.BlockSpec((length, 1), lambda i: (0, 0)),
            rows(0),
            whole(1),
            rows(0),
            rows(0),
            whole(0),
            whole(0),
            pl.BlockSpec(gains.shape, lambda i: (0, 0)),
        ],
        out_specs=[
            pl.BlockSpec((length, 3 * head_dim), lambda i: (0, 0)),
            pl.BlockSpec((2, head_dim), lambda i: (0, 0)),
        ],
        out_shape=[
            jax.ShapeDtypeStruct((length, 3 * head_dim), BF16),
            jax.ShapeDtypeStruct((2, head_dim), F32),
        ],
        scratch_shapes=[
            pltpu.VMEM((head_dim, length), BF16),
            pltpu.VMEM((length, head_dim), F32),
            pltpu.VMEM((length, head_dim), F32),
        ],
        compiler_params=pltpu.CompilerParams(vmem_limit_bytes=VMEM_LIMIT),
        cost_estimate=pl.CostEstimate(
            flops=10 * length * length * head_dim,
            bytes_accessed=length * head_dim * 40,
            transcendentals=length * length,
        ),
        name="project_back",
    )(
        qkv, qkv, qkv, grad, out_f32, lse, segments.reshape(1, -1), segments.reshape(-1, 1),
        raw, raw, cos, sin, cos, sin, gains,
    )


def hidden_back_kernel(grads_ref, own_ref, near_ref, far_ref, cross_ref, hidden_ref, out_ref, gain_ref):
    uly = grads_ref.shape[0]
    u = lax.axis_index(ULY)
    near = u + 1 - 2 * lax.rem(u, 2)
    total = dot_nt(grads_ref[u], own_ref[...])
    total = total + dot_nt(grads_ref[near], near_ref[...])
    total = total + dot_nt(grads_ref[lax.rem(u + 2, uly)], far_ref[...])
    total = total + dot_nt(grads_ref[lax.rem(near + 2, uly)], cross_ref[...])
    out_ref[...] = total.astype(BF16).reshape(out_ref.shape)
    hidden = hidden_ref[...].reshape(total.shape).astype(F32)
    gain_ref[...] = jnp.sum(total * hidden, axis=0, keepdims=True)


def hidden_back(grads, own, near, far, cross, hidden):
    uly, tokens, columns = grads.shape
    blk, _, rows, width = hidden.shape
    tile = min(512, width)
    weights = pl.BlockSpec((tile, columns), lambda n: (n, 0))
    return pl.pallas_call(
        hidden_back_kernel,
        grid=(width // tile,),
        in_specs=[
            pl.BlockSpec(grads.shape, lambda n: (0, 0, 0)),
            *[weights] * 4,
            pl.BlockSpec((blk, 1, rows, tile), lambda n: (0, lax.axis_index(ULY), 0, n)),
        ],
        out_specs=[
            pl.BlockSpec((blk, rows, tile), lambda n: (0, 0, n)),
            pl.BlockSpec((1, tile), lambda n: (0, n)),
        ],
        out_shape=[
            jax.ShapeDtypeStruct((blk, rows, width), BF16),
            jax.ShapeDtypeStruct((1, width), F32),
        ],
        compiler_params=pltpu.CompilerParams(vmem_limit_bytes=VMEM_LIMIT),
        name="hidden_back",
    )(grads, own, near, far, cross, hidden)


def merge_heads_kernel(parts_ref, out_ref):
    blk, uly, _, columns = parts_ref.shape
    head_dim = columns // 3
    heads = blk * uly
    for z in range(blk):
        for u in range(uly):
            head = parts_ref[z, u].astype(F32)
            for part in range(3):
                at = (part * heads + u * blk + z) * head_dim
                out_ref[:, at : at + head_dim] = head[:, part * head_dim : (part + 1) * head_dim]


def merge_heads(parts):
    blk, uly, rows, columns = parts.shape
    return pl.pallas_call(
        merge_heads_kernel,
        out_shape=jax.ShapeDtypeStruct((rows, blk * uly * columns), F32),
        compiler_params=pltpu.CompilerParams(vmem_limit_bytes=VMEM_LIMIT),
        name="merge_heads",
    )(parts)


def swap(values, axis):
    return lax.all_to_all(values, axis, split_axis=0, concat_axis=0, tiled=True)


def sum_scatter(values, axis):
    count = spread(axis) if isinstance(axis, tuple) else lax.axis_size(axis)
    rows, width = values.shape
    parts = swap(values.astype(BF16).reshape(count, rows // count, width), axis)
    return jnp.sum(parts.astype(F32), axis=0)


def place(axes, index):
    found = {}
    for axis in reversed(axes):
        size = lax.axis_size(axis)
        found[axis] = lax.rem(index, size)
        index = index // size
    return found


def spread(axes):
    return math.prod(lax.axis_size(axis) for axis in axes)


def each(count, body):
    if count <= 4:
        for step in range(1, count):
            body(step)
    else:

        def looped(step, carried):
            body(step)
            return carried

        lax.fori_loop(1, count, looped, 0)


def ahead(index, step, size):
    return lax.rem(index + step, size)


def exchange(items, collective_id, after=()):
    count = len(items)
    sizes = [spread(axes) for _, axes, _ in items]
    groups = list(dict.fromkeys(axes for _, axes, _ in items))
    bases = [sum(2 * size for size in sizes[:i]) for i in range(count)]

    def kernel(*refs):
        ins = refs[:count]
        outs = refs[count + len(after) : 2 * count + len(after)]
        send, recv, local = refs[2 * count + len(after) :][:3]
        barrier = pltpu.get_barrier_semaphore()
        for axes in groups:
            size, me = spread(axes), lax.axis_index(axes)

            def greet(step, axes=axes, size=size, me=me):
                pl.semaphore_signal(
                    barrier, inc=1, device_id=place(axes, ahead(me, step, size)), device_id_type=MESH
                )

            each(size, greet)
        pl.semaphore_wait(barrier, sum(spread(axes) - 1 for axes in groups))

        def block(i, peer):
            if items[i][2] == "swap":
                return ins[i].at[peer]
            return ins[i].at[:, peer] if items[i][2] == "swap1" else ins[i]

        def remote(i, step):
            _, axes, kind = items[i]
            me = lax.axis_index(axes)
            if kind == "trade":
                return pltpu.make_async_remote_copy(
                    src_ref=ins[i],
                    dst_ref=outs[i],
                    send_sem=send.at[bases[i] + 1],
                    recv_sem=recv.at[bases[i] + 1],
                    device_id=place(axes, 1 - me),
                    device_id_type=MESH,
                )
            if kind == "relay":
                far, near = lax.rem(me + 2, 4), me + 1 - 2 * lax.rem(me, 2)
                held = far if step == 3 else me
                return pltpu.make_async_remote_copy(
                    src_ref=outs[i].at[far] if step == 3 else ins[i],
                    dst_ref=outs[i].at[held],
                    send_sem=send.at[bases[i] + step],
                    recv_sem=recv.at[bases[i] + step],
                    device_id=place(axes, far if step == 1 else near),
                    device_id_type=MESH,
                )
            peer = ahead(me, step, sizes[i])
            return pltpu.make_async_remote_copy(
                src_ref=block(i, peer),
                dst_ref=outs[i].at[me],
                send_sem=send.at[bases[i] + step],
                recv_sem=recv.at[bases[i] + step],
                device_id=place(axes, peer),
                device_id_type=MESH,
            )

        def own(i):
            _, axes, kind = items[i]
            me = lax.axis_index(axes)
            return pltpu.make_async_copy(
                block(i, me), outs[i].at[me], local.at[i]
            )

        def hop(i, up, hops):
            (axis,) = items[i][1]
            me, size = lax.axis_index(axis), sizes[i]
            way = 1 if up else -1
            held, to = me - way * hops, me + way
            exists = (held >= 0) & (held < size) & (to >= 0) & (to < size)
            held, to = jnp.clip(held, 0, size - 1), jnp.clip(to, 0, size - 1)
            sem = bases[i] + (size if up else 0) + hops
            copy = pltpu.make_async_remote_copy(
                src_ref=outs[i].at[held] if hops else ins[i],
                dst_ref=outs[i].at[held],
                send_sem=send.at[sem],
                recv_sem=recv.at[sem],
                device_id={axis: to},
                device_id_type=MESH,
            )
            return exists, copy

        def arrival(i, up, hops):
            (axis,) = items[i][1]
            me, size = lax.axis_index(axis), sizes[i]
            way = 1 if up else -1
            held, sender = me - way * (hops + 1), me - way
            exists = (held >= 0) & (held < size)
            held, sender = jnp.clip(held, 0, size - 1), jnp.clip(sender, 0, size - 1)
            sem = bases[i] + (size if up else 0) + hops
            copy = pltpu.make_async_remote_copy(
                src_ref=ins[i],
                dst_ref=outs[i].at[held],
                send_sem=send.at[sem],
                recv_sem=recv.at[sem],
                device_id={axis: sender},
                device_id_type=MESH,
            )
            return exists, copy

        def kinds(*names):
            return [i for i in range(count) if items[i][2] in names]

        def when(pair, act):
            exists, copy = pair
            pl.when(exists)(lambda: act(copy))

        def pairsum(i):
            me = lax.axis_index(ULY)
            far, near = lax.rem(me + 2, 4), me + 1 - 2 * lax.rem(me, 2)
            own, out = ins[i], outs[i]
            got_near, got_far, sent = refs[2 * count + len(after) + 3 :]

            def copy(at, src, dst, to):
                return pltpu.make_async_remote_copy(
                    src_ref=src,
                    dst_ref=dst,
                    send_sem=send.at[bases[i] + at],
                    recv_sem=recv.at[bases[i] + at],
                    device_id=place(ULY, to),
                    device_id_type=MESH,
                )

            to_near = [
                copy(0, own.at[near], got_near.at[0], near),
                copy(1, own.at[lax.rem(near + 2, 4)], got_near.at[1], near),
            ]
            to_far = copy(2, sent, got_far, far)

            def first():
                for sending in to_near:
                    sending.start()

            def second():
                for sending in to_near:
                    sending.wait()
                sent[...] = (own[far].astype(F32) + got_near[1].astype(F32)).astype(BF16)
                to_far.start()
                out[...] = own[me].astype(F32) + got_near[0].astype(F32)

            def third():
                to_far.wait()
                out[...] += got_far[...].astype(F32)

            return first, second, third

        ways = (True, False)
        sums = [pairsum(i) for i in kinds("pairsum")]
        for first, _, _ in sums:
            first()
        for i in kinds("line"):
            for up in ways:
                when(hop(i, up, 0), lambda copy: copy.start())
        for i in kinds("gather", "swap", "swap1", "relay", "trade"):
            each(3 if items[i][2] == "relay" else sizes[i], lambda step, i=i: remote(i, step).start())
        for i in kinds("gather", "swap", "swap1", "relay", "line"):
            own(i).start()
        for _, second, _ in sums:
            second()
        for i in kinds("line"):
            for hops in range(1, sizes[i]):
                for up in ways:
                    when(arrival(i, up, hops - 1), lambda copy: copy.wait_recv())
                    if hops < sizes[i] - 1:
                        when(hop(i, up, hops), lambda copy: copy.start())
        for i in kinds("relay"):
            remote(i, 1).wait_recv()
            remote(i, 3).start()
            remote(i, 1).wait_send()
            for step in (2, 3):
                remote(i, step).wait()
        for i in kinds("gather", "swap", "swap1", "trade"):
            each(sizes[i], lambda step, i=i: remote(i, step).wait())
        for i in kinds("line"):
            for hops in range(sizes[i] - 1):
                for up in ways:
                    when(hop(i, up, hops), lambda copy: copy.wait_send())
        for i in kinds("gather", "swap", "swap1", "relay", "line"):
            own(i).wait()
        for _, _, third in sums:
            third()


    def shape_of(size, array, kind):
        if kind in ("trade", "pairsum"):
            return array.shape[kind == "pairsum" :]
        dropped = {"swap": 0, "swap1": 1}.get(kind)
        return (size, *(extent for at, extent in enumerate(array.shape) if at != dropped))

    anywhere, close = pl.BlockSpec(memory_space=pl.ANY), pl.BlockSpec(memory_space=pltpu.VMEM)
    specs = [close if kind == "pairsum" else anywhere for _, _, kind in items]
    held = []
    for array, _, kind in items:
        if kind == "pairsum":
            held = [pltpu.VMEM((*more, *array.shape[1:]), BF16) for more in ((2,), (), ())]
    return pl.pallas_call(
        kernel,
        in_specs=specs + [anywhere] * len(after),
        out_specs=specs,
        out_shape=[
            jax.ShapeDtypeStruct(shape_of(size, array, kind), F32 if kind == "pairsum" else array.dtype)
            for size, (array, _, kind) in zip(sizes, items)
        ],
        scratch_shapes=[
            pltpu.SemaphoreType.DMA((2 * sum(sizes),)),
            pltpu.SemaphoreType.DMA((2 * sum(sizes),)),
            pltpu.SemaphoreType.DMA((count,)),
            *held,
        ],
        compiler_params=pltpu.CompilerParams(
            collective_id=collective_id, has_side_effects=True, vmem_limit_bytes=VMEM_LIMIT if held else None
        ),
        name="exchange",
    )(*[item[0] for item in items], *after)


def turn_gather_kernel(
    own_ref, other_ref, all_ref, all_t_ref, other_t_ref, block, turned, send, recv, local
):
    size, me = lax.axis_size("blk"), lax.axis_index("blk")
    rows = own_ref.shape[0]
    barrier = pltpu.get_barrier_semaphore()
    ways = (1, 0)

    def neighbour(up):
        to = me + (1 if up else -1)
        return (to >= 0) & (to < size), jnp.clip(to, 0, size - 1)

    def greet(step):
        pl.semaphore_signal(
            barrier, inc=1, device_id={"blk": ahead(me, step, size)}, device_id_type=MESH
        )

    each(size, greet)
    pl.semaphore_wait(barrier, size - 1)

    def hop(up, hops):
        held = me - (1 if up else -1) * hops
        exists, to = neighbour(up)
        exists = exists & (held >= 0) & (held < size)
        held = jnp.clip(held, 0, size - 1)
        return exists, pltpu.make_async_remote_copy(
            src_ref=all_ref.at[held] if hops else own_ref,
            dst_ref=all_ref.at[held],
            send_sem=send.at[up * size + hops],
            recv_sem=recv.at[up * size + hops],
            device_id={"blk": to},
            device_id_type=MESH,
        )

    def arrival(up, hops):
        held = me - (1 if up else -1) * (hops + 1)
        exists = (held >= 0) & (held < size)
        held = jnp.clip(held, 0, size - 1)
        return exists, held, pltpu.make_async_remote_copy(
            src_ref=own_ref,
            dst_ref=all_ref.at[held],
            send_sem=send.at[up * size + hops],
            recv_sem=recv.at[up * size + hops],
            device_id={"blk": neighbour(1 - up)[1]},
            device_id_type=MESH,
        )

    def when(pair, act):
        exists, copy = pair
        pl.when(exists)(lambda: act(copy))

    def turn(src, dst, at):
        take = pltpu.make_async_copy(src, block, local.at[0])
        take.start()
        take.wait()
        turned[...] = block[...].T
        columns = pl.ds(pl.multiple_of(at * rows, rows), rows)
        give = pltpu.make_async_copy(turned, dst.at[:, columns], local.at[1])
        give.start()
        give.wait()

    for up in ways:
        when(hop(up, 0), lambda copy: copy.start())
    keep = pltpu.make_async_copy(own_ref, all_ref.at[me], local.at[2])
    keep.start()
    turn(own_ref, all_t_ref, me)
    for at in range(size):
        turn(other_ref.at[at], other_t_ref, at)
    for hops in range(1, size):
        for up in ways:
            exists, held, copy = arrival(up, hops - 1)

            @pl.when(exists)
            def _(copy=copy, up=up, hops=hops):
                copy.wait_recv()
                if hops < size - 1:
                    when(hop(up, hops), lambda copy: copy.start())

        for up in ways:
            exists, held, copy = arrival(up, hops - 1)
            pl.when(exists)(lambda held=held: turn(all_ref.at[held], all_t_ref, held))
    for hops in range(size - 1):
        for up in ways:
            when(hop(up, hops), lambda copy: copy.wait_send())
    keep.wait()


def turn_gather(own, other, collective_id, after=()):
    size = lax.axis_size("blk")
    rows, width = own.shape
    anywhere = pl.BlockSpec(memory_space=pl.ANY)

    def kernel(*refs):
        turn_gather_kernel(*refs[:2], *refs[2 + len(after) :])

    return pl.pallas_call(
        kernel,
        in_specs=[anywhere] * (2 + len(after)),
        out_specs=[anywhere] * 3,
        out_shape=[
            jax.ShapeDtypeStruct((size, rows, width), BF16),
            jax.ShapeDtypeStruct((width, size * rows), BF16),
            jax.ShapeDtypeStruct((width, size * rows), BF16),
        ],
        scratch_shapes=[
            pltpu.VMEM((rows, width), BF16),
            pltpu.VMEM((width, rows), BF16),
            pltpu.SemaphoreType.DMA((2 * size,)),
            pltpu.SemaphoreType.DMA((2 * size,)),
            pltpu.SemaphoreType.DMA((3,)),
        ],
        compiler_params=pltpu.CompilerParams(
            collective_id=collective_id, has_side_effects=True, vmem_limit_bytes=VMEM_LIMIT
        ),
        name="turn_gather",
    )(own, other, *after)


def startup_kernel(
    head_ref, extra_ref, tok_ref, heads_ref, extras_ref, toks_ref,
    head_send, head_recv, extra_send, extra_recv, trade_send, trade_recv,
    z_send, z_recv, ay_send, ay_recv, by_send, by_recv, c_send, c_recv, local,
):
    blk, uly = lax.axis_size("blk"), spread(ULY)
    total = spread(ALL)
    z, u, me = lax.axis_index("blk"), lax.axis_index(ULY), lax.axis_index(ALL)
    far = lax.rem(u + 2, uly)
    near = u + 1 - 2 * lax.rem(u, 2)
    half = tok_ref.shape[0] // 2
    parts = (pl.ds(0, half), pl.ds(half, half))

    barrier = pltpu.get_barrier_semaphore()

    def greet(step):
        pl.semaphore_signal(
            barrier, inc=1, device_id=place(ALL, ahead(me, step, total)), device_id_type=MESH
        )

    each(total, greet)
    pl.semaphore_wait(barrier, total - 1)

    def send(src, dst, sent, got, to):
        return pltpu.make_async_remote_copy(
            src_ref=src, dst_ref=dst, send_sem=sent, recv_sem=got, device_id=to, device_id_type=MESH
        )

    def block(step, other, part):
        at = toks_ref.at[ahead(z, step, blk), far if other else u, parts[part]]
        return (tok_ref.at[parts[part]] if step == 0 and not other else at), at

    streams = ((0, 0), (0, 1), (1, 1))

    def hop(stream, up, hops):
        other, part = streams[stream]
        way = 1 if up else -1
        held, to = z - way * hops, z + way
        exists = (held >= 0) & (held < blk) & (to >= 0) & (to < blk)
        held, to = jnp.clip(held, 0, blk - 1), jnp.clip(to, 0, blk - 1)
        at = toks_ref.at[held, far if other else u, parts[part]]
        src = tok_ref.at[parts[part]] if hops == 0 and not other else at
        sem = (2 * stream + up) * blk + hops
        return exists, send(src, at, z_send.at[sem], z_recv.at[sem], {"blk": to})

    def arrival(stream, up, hops):
        other, part = streams[stream]
        way = 1 if up else -1
        held, sender = z - way * (hops + 1), z - way
        exists = (held >= 0) & (held < blk)
        held, sender = jnp.clip(held, 0, blk - 1), jnp.clip(sender, 0, blk - 1)
        at = toks_ref.at[held, far if other else u, parts[part]]
        sem = (2 * stream + up) * blk + hops
        return exists, send(tok_ref.at[parts[part]], at, z_send.at[sem], z_recv.at[sem], {"blk": sender})

    def when(pair, act):
        exists, copy = pair
        pl.when(exists)(lambda: act(copy))

    def a_y(step):
        return send(*block(step, 0, 0), ay_send.at[step], ay_recv.at[step], place(ULY, far))

    def b_y():
        return send(*block(0, 0, 1), by_send.at[0], by_recv.at[0], place(ULY, far))

    def to_near(step, other, part):
        sem = 4 * step + 2 * other + part
        return send(*block(step, other, part), c_send.at[sem], c_recv.at[sem], place(ULY, near))

    group = ("blk", *ULY)
    mine, here, b = lax.axis_index(group), spread(group), lax.axis_index("batch")

    def head(step):
        to = place(group, ahead(mine, step, here))
        src = head_ref.at[(to["y"] * lax.axis_size("core") + to["core"]) * blk + to["blk"]]
        return send(src, heads_ref.at[b, mine], head_send.at[step], head_recv.at[step], to)

    def extra(step):
        to = place(group, ahead(mine, step, here))
        return send(extra_ref, extras_ref.at[b, mine], extra_send.at[step], extra_recv.at[step], to)

    def trade(which):
        ref = (heads_ref, extras_ref)[which].at[b]
        return send(ref, ref, trade_send.at[which], trade_recv.at[which], {"batch": 1 - b})

    own = [
        pltpu.make_async_copy(tok_ref, toks_ref.at[z, u], local.at[0]),
        pltpu.make_async_copy(head_ref.at[u * blk + z], heads_ref.at[b, mine], local.at[1]),
        pltpu.make_async_copy(extra_ref, extras_ref.at[b, mine], local.at[2]),
    ]

    def start_head(step):
        extra(step).start()
        head(step).start()

    each(here, start_head)
    ways = (1, 0)
    b_y().start()
    for stream in range(2):
        for up in ways:
            when(hop(stream, up, 0), lambda copy: copy.start())
    a_y(0).start()
    to_near(0, 0, 0).start()
    to_near(0, 0, 1).start()

    for copy in own:
        copy.start()
    b_y().wait_recv()
    for up in ways:
        when(hop(2, up, 0), lambda copy: copy.start())
    to_near(0, 1, 1).start()
    def wait_head(step):
        extra(step).wait()
        head(step).wait()

    for hops in range(1, blk):
        if hops == min(2, blk - 1):
            each(here, wait_head)
            for copy in own[1:]:
                copy.wait()
            trade(0).start()
            trade(1).start()
        for stream, (other, part) in enumerate(streams):
            for up in ways:
                exists, copy = arrival(stream, up, hops - 1)
                step = blk - hops if up else hops

                @pl.when(exists)
                def _(copy=copy, stream=stream, other=other, part=part, up=up, step=step, hops=hops):
                    copy.wait_recv()
                    if hops < blk - 1:
                        when(hop(stream, up, hops), lambda copy: copy.start())
                    if stream == 0:
                        a_y(step).start()
                    to_near(step, other, part).start()

    for step in [0, *reversed(range(1, blk))]:
        a_y(step).wait_recv()
        to_near(step, 1, 0).start()
    for step in range(blk):
        for other in range(2):
            for part in range(2):
                to_near(step, other, part).wait_recv()

    trade(0).wait()
    trade(1).wait()
    own[0].wait()
    b_y().wait_send()
    for hops in range(blk - 1):
        for stream in range(3):
            for up in ways:
                when(hop(stream, up, hops), lambda copy: copy.wait_send())
    for step in range(blk):
        a_y(step).wait_send()
        for other in range(2):
            for part in range(2):
                to_near(step, other, part).wait_send()


def startup(heads, extra, tok, collective_id):
    batch, blk, uly = lax.axis_size("batch"), lax.axis_size("blk"), spread(ULY)
    anywhere = pl.BlockSpec(memory_space=pl.ANY)
    dma = pltpu.SemaphoreType.DMA
    return pl.pallas_call(
        startup_kernel,
        in_specs=[anywhere] * 3,
        out_specs=[anywhere] * 3,
        out_shape=[
            jax.ShapeDtypeStruct((batch, blk * uly, *heads.shape[1:]), BF16),
            jax.ShapeDtypeStruct((batch, blk * uly, *extra.shape), BF16),
            jax.ShapeDtypeStruct((blk, uly, *tok.shape), BF16),
        ],
        scratch_shapes=[
            *[dma((blk * uly,))] * 4,
            *[dma((2,))] * 2,
            *[dma((6 * blk,))] * 2,
            *[dma((blk,))] * 2,
            *[dma((1,))] * 2,
            *[dma((4 * blk,))] * 2,
            dma((3,)),
        ],
        compiler_params=pltpu.CompilerParams(collective_id=collective_id, has_side_effects=True),
        name="startup",
    )(heads, extra, tok)


def per_device_general(
    tokens, segments, routes, w_qkv, w_out, attn_gain, ffn_gain, qk_gain, router, w_gate_up, w_down, cotangent
):
    own_tokens = tokens[0]
    own_grad = cotangent[0]
    count_tok, width = own_tokens.shape
    head_dim = qk_gain.shape[1]
    heads = width // head_dim
    uly, blk, batch = spread(ULY), lax.axis_size("blk"), lax.axis_size("batch")
    blk_at, uly_at = lax.axis_index("blk"), lax.axis_index(ULY)
    group = batch * blk
    local_heads = heads // uly
    local_width = local_heads * head_dim
    rows = count_tok * uly
    seg_row = segments[0]
    length = seg_row.shape[0]
    number = router.shape[1]
    local_experts, _, units = w_down.shape
    shard_rows = w_qkv.shape[0]

    extra = jnp.concatenate([attn_gain[:, None], ffn_gain[:, None], router], axis=1)
    extra = jnp.pad(extra, ((0, 0), (0, LANES - extra.shape[1])))
    columns = w_qkv.reshape(shard_rows, 3, uly, local_width).transpose(2, 0, 1, 3)
    packed = jnp.concatenate(
        [
            columns.reshape(uly, shard_rows, 3 * local_width),
            jnp.broadcast_to(extra[None], (uly, shard_rows, LANES)),
        ],
        axis=2,
    )
    packed = swap(packed, ULY).reshape(uly * shard_rows, 3 * local_width + LANES)
    packed = lax.all_gather(packed, ROWS, axis=0, tiled=True)
    own_qkv = packed[:, : 3 * local_width]
    gain_attn = packed[:, 3 * local_width].astype(F32)
    gain_ffn = packed[:, 3 * local_width + 1].astype(F32)
    whole_router = packed[:, 3 * local_width + 2 : 3 * local_width + 2 + number]
    tokens_all = lax.all_gather(own_tokens, ULY, axis=0, tiled=True)
    to_rows = [(u * group + g, g * uly + u) for g in range(group) for u in range(uly)]
    own_out = lax.all_gather(lax.ppermute(w_out, ALL, to_rows), ROWS, axis=0, tiled=True)
    whole_gate_up = lax.all_gather(w_gate_up, PLANE, axis=0, tiled=False)
    whole_down = lax.all_gather(w_down, PLANE, axis=0, tiled=False)
    grad_blk = lax.all_gather(own_grad, "blk", axis=0, tiled=True)
    routes_blk = lax.all_gather(routes[0], "blk", axis=0, tiled=True)

    gain_query = qk_gain[0].astype(F32)
    gain_key = qk_gain[1].astype(F32)
    inputs_all = tokens_all.astype(F32)
    normed_one = inputs_all * rms_scale(inputs_all)
    hidden_one = (normed_one * gain_attn).astype(BF16)
    projected = dot_nn(hidden_one, own_qkv)
    query_raw = projected[:, :local_width].reshape(rows, local_heads, head_dim)
    key_raw = projected[:, local_width : 2 * local_width].reshape(rows, local_heads, head_dim)
    value_raw = projected[:, 2 * local_width :].reshape(rows, local_heads, head_dim)
    cos_table, sin_table = rope_tables(blk_at * rows, rows, head_dim)
    query_scale = rms_scale(query_raw)
    key_scale = rms_scale(key_raw)
    qkv = jnp.concatenate(
        [
            rotate(query_raw * query_scale * gain_query, cos_table, sin_table),
            rotate(key_raw * key_scale * gain_key, cos_table, sin_table),
            value_raw,
        ],
        axis=2,
    ).astype(BF16)
    qkv = qkv.transpose(1, 0, 2)

    by_heads = local_heads % blk == 0
    if by_heads:
        per = local_heads // blk

        def to_heads(values):
            columns = values.shape[2]
            moved = swap(values.reshape(blk, per, rows, columns), "blk")
            return moved.transpose(1, 0, 2, 3).reshape(per, length, columns)

        def to_rows_back(values):
            columns = values.shape[2]
            parts = values.reshape(per, blk, rows, columns).transpose(1, 0, 2, 3)
            return swap(parts, "blk").reshape(local_heads, rows, columns)

        q_src = kv_src = to_heads(qkv)
        cols = (0, 1, 2)
        seg_q = seg_row
        first_head = uly_at * local_heads + blk_at * per
    else:

        def to_heads(values):
            return values

        def to_rows_back(values):
            return values

        q_src = qkv
        kv_src = lax.all_gather(qkv[:, :, head_dim:], "blk", axis=1, tiled=True)
        cols = (0, 0, 1)
        seg_q = lax.dynamic_slice_in_dim(seg_row, blk_at * rows, rows)
        first_head = uly_at * local_heads
    attn_low, attn_f32, lse, top = attention_forward(q_src, kv_src, cols, seg_q, seg_row, head_dim)
    head_vector = lax.dynamic_update_slice_in_dim(
        jnp.full((heads,), NEG, F32), jnp.max(top, axis=(1, 2)) * head_dim**-0.5, first_head, 0
    )
    head_max = lax.pmax(head_vector, ALL)
    attn_rows = to_rows_back(attn_low)
    out_heads = own_out.reshape(local_heads, head_dim, width)
    branch = jnp.einsum("htc,hcd->td", attn_rows, out_heads, preferred_element_type=F32)
    inputs = own_tokens.astype(F32)
    mid = inputs + sum_scatter(branch, ULY)

    scale_two = rms_scale(mid)
    normed_two = mid * scale_two
    hidden_two = (normed_two * gain_ffn).astype(BF16)
    hidden_blk = lax.all_gather(hidden_two, "blk", axis=0, tiled=True)
    probs_blk = jax.nn.softmax(dot_nn(hidden_blk, whole_router), axis=1)
    names = jnp.arange(number, dtype=jnp.int32)
    chosen_blk = jnp.any(routes_blk[:, :, None] == names, axis=1).astype(F32)
    own_names = blk_at * local_experts
    gates = lax.dynamic_slice_in_dim(probs_blk * chosen_blk, own_names, local_experts, axis=1)
    most = min(MOST_TOKENS, hidden_blk.shape[0])
    packed_weights = jnp.concatenate([whole_gate_up, whole_down], axis=3)
    made = []
    for at in range(0, hidden_blk.shape[0], most):
        hidden_part, grad_part = hidden_blk[at : at + most], grad_blk[at : at + most]
        made.append(
            experts(
                hidden_part,
                hidden_part.T,
                grad_part,
                grad_part.T,
                gates[at : at + most],
                [(packed_weights, 0, local_experts)],
            )
        )
    out_part = jnp.concatenate([m[0] for m in made], axis=0)
    dx_part = jnp.concatenate([m[1] for m in made], axis=0)
    dg_part = jnp.concatenate([m[2] for m in made], axis=1)
    expert_grads = sum(m[3].astype(F32) for m in made).astype(BF16)
    expert_sums = lax.psum_scatter(expert_grads, PLANE, scatter_dimension=0, tiled=False).astype(F32)
    grad_gate_up = jnp.concatenate([expert_sums[0], expert_sums[1]], axis=2)
    grad_down = expert_sums[2]
    dg_parts = swap(dg_part.reshape(local_experts, blk, count_tok).transpose(1, 2, 0), "blk")
    grad_gates = dg_parts.transpose(1, 0, 2).reshape(count_tok, number)
    dx_sum = sum_scatter(dx_part, "blk")
    output = (mid + sum_scatter(out_part, "blk")).astype(BF16)
    router_probs = lax.dynamic_slice_in_dim(probs_blk, blk_at * count_tok, count_tok)
    chosen = lax.dynamic_slice_in_dim(chosen_blk, blk_at * count_tok, count_tok)
    grad_probs = chosen * grad_gates
    grad_logits = (
        router_probs * (grad_probs - jnp.sum(router_probs * grad_probs, axis=1, keepdims=True))
    ).astype(BF16)
    grad_hidden_two = dx_sum + dot_nt(grad_logits, whole_router)
    grad_router_part = dot_tn(hidden_two, grad_logits)
    grad_gain_ffn = jnp.sum(grad_hidden_two * normed_two, axis=0)
    grad_mid = own_grad.astype(F32) + norm_back(grad_hidden_two * gain_ffn, mid, scale_two)

    branch_grad = lax.all_gather(grad_mid.astype(BF16), ULY, axis=0, tiled=True)
    grad_attn = dot_nt(branch_grad, own_out).astype(BF16)
    grad_attn = to_heads(grad_attn.reshape(rows, local_heads, head_dim).transpose(1, 0, 2))
    grad_out_part = jnp.einsum("htc,td->hcd", attn_rows, branch_grad, preferred_element_type=F32)
    dq, dk, dv = attention_backward(
        q_src, kv_src, cols, grad_attn, attn_f32, lse, seg_q, seg_row, head_dim
    )
    if by_heads:
        dqkv = to_rows_back(jnp.concatenate([dq, dk, dv], axis=2))
        dq, dk, dv = jnp.split(dqkv, 3, axis=2)
    else:
        dk, dv = (lax.psum_scatter(g, "blk", scatter_dimension=1, tiled=True) for g in (dk, dv))
    dq, dk, dv = (g.transpose(1, 0, 2) for g in (dq, dk, dv))
    grad_query_norm = rotate(dq.astype(F32), cos_table, -sin_table)
    grad_key_norm = rotate(dk.astype(F32), cos_table, -sin_table)
    grad_gain_query = jnp.sum(grad_query_norm * (query_raw * query_scale), axis=(0, 1))
    grad_gain_key = jnp.sum(grad_key_norm * (key_raw * key_scale), axis=(0, 1))
    grad_projected = jnp.concatenate(
        [
            norm_back(grad_query_norm * gain_query, query_raw, query_scale)
            .reshape(rows, local_width)
            .astype(BF16),
            norm_back(grad_key_norm * gain_key, key_raw, key_scale)
            .reshape(rows, local_width)
            .astype(BF16),
            dv.reshape(rows, local_width),
        ],
        axis=1,
    )
    grad_hidden_part = dot_nt(grad_projected, own_qkv)
    grad_hidden_one = sum_scatter(grad_hidden_part, ULY)
    grad_gain_attn = jnp.sum(grad_hidden_part * normed_one, axis=0)
    grad_inputs = grad_mid + norm_back(grad_hidden_one * gain_attn, inputs, rms_scale(inputs))

    grad_qkv_part = dot_tn(hidden_one, grad_projected).astype(BF16)
    grad_qkv_rows = lax.psum_scatter(grad_qkv_part, ROWS, scatter_dimension=0, tiled=True)
    grad_qkv_rows = swap(grad_qkv_rows.reshape(uly, shard_rows, 3 * local_width), ULY)
    grad_qkv = (
        grad_qkv_rows.reshape(uly, shard_rows, 3, local_width)
        .transpose(1, 2, 0, 3)
        .reshape(shard_rows, 3 * width)
        .astype(F32)
    )
    grad_out_rows = lax.psum_scatter(
        grad_out_part.reshape(local_width, width).astype(BF16), ROWS, scatter_dimension=0, tiled=True
    )
    grad_out = lax.ppermute(grad_out_rows, ALL, [(b, a) for a, b in to_rows]).astype(F32)
    small = jnp.concatenate([grad_gain_attn[:, None], grad_gain_ffn[:, None], grad_router_part], axis=1)
    small = lax.psum_scatter(small, ALL, scatter_dimension=0, tiled=True)
    grad_qk_gain = lax.psum(jnp.stack([grad_gain_query, grad_gain_key]), ALL)

    clip_gamma = TAU / jnp.maximum(head_max, TAU)
    factor = jnp.repeat(jnp.sqrt(clip_gamma), head_dim)
    column_scale = jnp.concatenate([factor, factor, jnp.ones((width,), F32)])
    clipped = w_qkv.astype(F32) * column_scale[None, :]
    return (
        output[None],
        grad_inputs[None],
        grad_qkv,
        grad_out,
        small[:, 0],
        small[:, 1],
        grad_qk_gain,
        small[:, 2:],
        grad_gate_up,
        grad_down,
        clipped,
    )


def per_device(
    tokens, segments, routes, w_qkv, w_out, attn_gain, ffn_gain, qk_gain, router, w_gate_up, w_down, cotangent
):
    own_tokens = tokens[0]
    own_grad = cotangent[0]
    count_tok, width = own_tokens.shape
    head_dim = qk_gain.shape[1]
    heads = width // head_dim
    batch, blk, uly = lax.axis_size("batch"), lax.axis_size("blk"), spread(ULY)
    total, group = batch * blk * uly, batch * blk
    local_experts = w_down.shape[0]
    if uly != 4 or heads != blk * uly or blk < 2 or batch != 2 or local_experts % 2:
        return per_device_general(
            tokens, segments, routes, w_qkv, w_out, attn_gain, ffn_gain, qk_gain, router, w_gate_up, w_down, cotangent
        )
    blk_at, uly_at = lax.axis_index("blk"), lax.axis_index(ULY)
    rows = count_tok * uly
    seg_row = segments[0]
    length = seg_row.shape[0]
    number = router.shape[1]
    shard_rows = w_qkv.shape[0]

    to_rows = [(u * group + g, g * uly + u) for g in range(group) for u in range(uly)]
    rows_here = lax.ppermute(w_out, ALL, to_rows)
    rows_there = lax.ppermute(w_out, ALL, [(a, (b + total // 2) % total) for a, b in to_rows])


    half = local_experts // 2

    def gather_experts(gate_up, down):
        return lax.all_gather(jnp.concatenate([gate_up, down], axis=2), PLANE, axis=0, tiled=False)

    weights_first = gather_experts(w_gate_up[:half], w_down[:half])
    extra = jnp.concatenate([attn_gain[None], ffn_gain[None], router.T], axis=0)
    kept = extra.shape[0]
    extra = jnp.pad(extra, ((0, -kept % 16), (0, -shard_rows % LANES)))
    by_head = w_qkv.reshape(shard_rows, 3, heads, head_dim).transpose(2, 0, 1, 3)
    own_qkv, extras, toks = startup(
        by_head.reshape(heads, shard_rows, 3 * head_dim), extra, own_tokens, 0
    )
    rows_here, rows_there, extras, later_gate_up, later_down = lax.optimization_barrier(
        (rows_here, rows_there, extras, w_gate_up[half:], w_down[half:])
    )
    weights_second = gather_experts(later_gate_up, later_down)
    is_first = lax.axis_index("batch") == 0
    pair = jnp.stack(
        [jnp.where(is_first, rows_here, rows_there), jnp.where(is_first, rows_there, rows_here)]
    )
    own_out = lax.all_to_all(
        jnp.broadcast_to(pair[None], (blk, *pair.shape)), "blk", split_axis=0, concat_axis=0, tiled=True
    )
    own_out = own_out.transpose(1, 0, 2, 3).reshape(blk, head_dim, width)
    own_qkv = own_qkv.reshape(width, 3 * head_dim)
    extras = extras.reshape(total, *extra.shape)[:, :kept, :shard_rows]
    extras = extras.transpose(1, 0, 2).reshape(kept, width)
    gain_attn = extras[0].astype(F32)
    gain_ffn = extras[1].astype(F32)
    router_t = extras[2:]

    gains = qk_gain.astype(F32)
    cos, sin = rope_rows(length, head_dim)
    hidden_one, qkv, raw = project(
        toks.reshape(length, width), gain_attn[None], own_qkv, cos, sin, gains
    )
    attn_low, attn_f32, lse, top = attention_forward(
        qkv[None], qkv[None], (0, 1, 2), seg_row, seg_row, head_dim
    )
    (attn_rows,) = exchange([(attn_low.reshape(blk, rows, head_dim), ("blk",), "swap")], 1)
    branch = jnp.einsum("htc,hcd->td", attn_rows, own_out, preferred_element_type=F32)
    branch, grad_blk, routes_blk = exchange(
        [
            (branch.astype(BF16).reshape(uly, count_tok, width), ULY, "pairsum"),
            (own_grad, ("blk",), "line"),
            (routes[0].T, ("blk",), "gather"),
        ],
        2,
    )
    inputs = own_tokens.astype(F32)
    mid = inputs + branch

    scale_two = rms_scale(mid)
    normed_two = mid * scale_two
    hidden_two = (normed_two * gain_ffn).astype(BF16)
    hidden_blk, hidden_t, grad_t = turn_gather(hidden_two, grad_blk, 3)
    tokens_blk = blk * count_tok
    hidden_blk = hidden_blk.reshape(tokens_blk, width)
    grad_blk = grad_blk.reshape(tokens_blk, width)
    probs_blk = jax.nn.softmax(dot_nt(hidden_blk, router_t), axis=1)
    names = jnp.arange(number, dtype=jnp.int32)
    chosen_blk = jnp.any(routes_blk[:, :, :, None] == names, axis=1).astype(F32)
    chosen_blk = chosen_blk.reshape(tokens_blk, number)
    gates = lax.dynamic_slice_in_dim(
        probs_blk * chosen_blk, blk_at * local_experts, local_experts, axis=1
    )
    shared = (hidden_blk, hidden_t, grad_blk, grad_t)
    out_part, dx_part, dg_first, grads_first = experts(
        *shared, gates[:, :half], [(weights_first, 0, half)]
    )
    sums_first = lax.psum_scatter(grads_first, PLANE, scatter_dimension=0, tiled=False)
    out_part, dx_part, dg_others, grads_others = experts(
        *shared, gates[:, half:], [(weights_second, 0, half)], before=(out_part, dx_part)
    )
    sums_others = lax.psum_scatter(grads_others, PLANE, scatter_dimension=0, tiled=False)
    finished = finish_experts(sums_first, 0, local_experts)
    grad_gate_up, grad_down = finish_experts(sums_others, half, local_experts, before=finished)
    dg_part = jnp.concatenate([dg_first, dg_others], axis=0)
    dg_part = dg_part.reshape(local_experts, blk, count_tok)
    dx_parts, dg_parts = exchange(
        [
            (dx_part.reshape(blk, count_tok, width), ("blk",), "swap"),
            (dg_part.transpose(1, 0, 2), ("blk",), "swap"),
        ],
        4,
    )
    out_part = out_part.reshape(blk, count_tok, width)
    out_part, dx_parts = lax.optimization_barrier((out_part, dx_parts))
    out_parts = lax.all_to_all(out_part, "blk", split_axis=0, concat_axis=0, tiled=True)
    output = (mid + jnp.sum(out_parts.astype(F32), axis=0)).astype(BF16)
    router_probs = lax.dynamic_slice_in_dim(probs_blk, blk_at * count_tok, count_tok)
    chosen = lax.dynamic_slice_in_dim(chosen_blk, blk_at * count_tok, count_tok)
    grad_probs = chosen * dg_parts.reshape(number, count_tok).T
    grad_logits = (
        router_probs * (grad_probs - jnp.sum(router_probs * grad_probs, axis=1, keepdims=True))
    ).astype(BF16)
    grad_hidden_two = jnp.sum(dx_parts.astype(F32), axis=0) + dot_nn(grad_logits, router_t)
    grad_router_t = dot_tn(grad_logits, hidden_two)
    grad_gain_ffn = jnp.sum(grad_hidden_two * normed_two, axis=0)
    grad_mid = own_grad.astype(F32) + norm_back(grad_hidden_two * gain_ffn, mid, scale_two)

    (branch_grad,) = exchange([(grad_mid.astype(BF16), ULY, "relay")], 5)
    branch_grad, sent_qkv = lax.optimization_barrier((branch_grad, own_qkv))
    far_qkv = lax.ppermute(sent_qkv, "y", [(0, 1), (1, 0)])
    branch_grad = branch_grad.reshape(rows, width)
    grad_attn = jnp.einsum("td,hcd->htc", branch_grad, own_out, preferred_element_type=F32).astype(BF16)
    grad_out_part = jnp.einsum("htc,td->hcd", attn_rows, branch_grad, preferred_element_type=F32)
    grad_out_part = grad_out_part.astype(BF16).reshape(batch, blk, shard_rows, width)
    batch_at = lax.axis_index("batch")
    grad_attn, got_out_part = exchange(
        [
            (grad_attn, ("blk",), "swap"),
            (
                lax.dynamic_index_in_dim(grad_out_part, 1 - batch_at, 0, keepdims=False),
                ("batch",),
                "trade",
            ),
        ],
        6,
        after=[out_parts],
    )
    grad_out_part = lax.dynamic_index_in_dim(grad_out_part, batch_at, 0, keepdims=False) + got_out_part
    grad_projected, grad_gains = project_back(
        qkv, grad_attn.reshape(length, head_dim), attn_f32, lse, seg_row, raw, cos, sin, gains
    )
    grad_qkv_part = dot_tn(hidden_one, grad_projected).astype(BF16)
    by_batch = grad_qkv_part.reshape(batch, width // batch, 3 * head_dim)
    projected_blk, got_qkv_part, near_qkv, cross_qkv, grad_out_parts = exchange(
        [
            (grad_projected.reshape(blk, uly, count_tok, 3 * head_dim), ULY, "swap1"),
            (
                lax.dynamic_index_in_dim(by_batch, 1 - batch_at, 0, keepdims=False),
                ("batch",),
                "trade",
            ),
            (own_qkv, ("core",), "trade"),
            (far_qkv, ("core",), "trade"),
            (grad_out_part, ("blk",), "swap"),
        ],
        7,
    )
    grad_out = lax.ppermute(
        jnp.sum(grad_out_parts.astype(F32), axis=0).astype(BF16), ALL, [(b, a) for a, b in to_rows]
    ).astype(F32)
    grad_qkv_part = lax.dynamic_index_in_dim(by_batch, batch_at, 0, keepdims=False) + got_qkv_part

    grad_hidden_part, grad_gain_attn = hidden_back(
        projected_blk.reshape(uly, tokens_blk, 3 * head_dim),
        own_qkv,
        near_qkv,
        far_qkv,
        cross_qkv,
        hidden_one.reshape(blk, uly, count_tok, width),
    )
    grad_gain_attn = grad_gain_attn[0] / gain_attn

    small = jnp.concatenate([grad_gain_attn[None], grad_gain_ffn[None], grad_router_t], axis=0)
    beside = LANES // shard_rows
    small = jnp.pad(small, ((0, -kept % beside), (0, 0))).reshape(-1, beside, total, shard_rows)
    small = small.transpose(2, 0, 1, 3).reshape(total, -1, LANES)
    packed_rows = small.shape[1]
    head_row = jnp.where(
        jnp.arange(LANES) == uly_at * blk + blk_at, jnp.max(top) * head_dim**-0.5, NEG
    )
    to_all = jnp.concatenate([grad_gains, head_row[None]], axis=0)
    small = jnp.concatenate([small, jnp.broadcast_to(to_all[None], (total, 3, LANES))], axis=1)
    small = jnp.pad(small, ((0, 0), (0, -small.shape[1] % 8), (0, 0)))
    grad_hidden_parts, small, grad_qkv_parts = exchange(
        [
            (grad_hidden_part, ("blk",), "swap"),
            (small, ALL, "swap"),
            (grad_qkv_part.reshape(total // batch, shard_rows, 3 * head_dim), ("blk", *ULY), "swap"),
        ],
        8,
    )
    grad_qkv = merge_heads(grad_qkv_parts.reshape(blk, uly, shard_rows, 3 * head_dim))
    grad_hidden_one = jnp.sum(grad_hidden_parts.astype(F32), axis=0)
    grad_inputs = grad_mid + norm_back(grad_hidden_one * gain_attn, inputs, rms_scale(inputs))
    sums = jnp.sum(small, axis=0)
    sums, grad_gains = sums[:packed_rows], sums[packed_rows : packed_rows + 2]
    sums = sums.reshape(packed_rows * beside, shard_rows)[:kept]
    head_max = jnp.max(small[:, packed_rows + 2, :heads], axis=0)
    factor = jnp.repeat(jnp.sqrt(TAU / jnp.maximum(head_max, TAU)), head_dim)
    column_scale = jnp.concatenate([factor, factor, jnp.ones((width,), F32)])
    clipped = w_qkv.astype(F32) * column_scale[None, :]
    return (
        output[None],
        grad_inputs[None],
        grad_qkv,
        grad_out,
        sums[0],
        sums[1],
        grad_gains,
        sums[2:].T,
        grad_gate_up,
        grad_down,
        clipped,
    )


def solution(mesh):
    in_specs = (
        P("batch", ("blk", *ULY), None),
        P("batch", None),
        P("batch", ("blk", *ULY), None),
        P(ALL, None),
        P(ALL, None),
        P(ALL),
        P(ALL),
        P(),
        P(ALL, None),
        P("blk", PLANE, None),
        P("blk", PLANE, None),
        P("batch", ("blk", *ULY), None),
    )
    out_specs = (
        P("batch", ("blk", *ULY), None),
        P("batch", ("blk", *ULY), None),
        P(ALL, None),
        P(ALL, None),
        P(ALL),
        P(ALL),
        P(),
        P(ALL, None),
        P("blk", PLANE, None),
        P("blk", PLANE, None),
        P(ALL, None),
    )
    cores = 2 - mesh.shape["uly"] % 2
    mesh = Mesh(
        mesh.devices.reshape(*(mesh.shape[axis] for axis in ROWS), mesh.shape["uly"] // cores, cores), ALL
    )
    return jax.shard_map(
        per_device, mesh=mesh, in_specs=in_specs, out_specs=out_specs, check_vma=False
    )
```

```python
import functools
import math

import jax
import jax.numpy as jnp
from jax import lax
from jax.experimental import pallas as pl
from jax.experimental.pallas import tpu as pltpu
from jax.sharding import Mesh
from jax.sharding import PartitionSpec as P

EPS = 1e-06
THETA = 50000.0
TAU = 4.0
NEG = -1e30
LOG2E = 1.4426950408889634
LANES = 128
MOST_TOKENS = 512
VMEM_LIMIT = 60 * 1024 * 1024

ULY = ("y", "core")
ALL = ("batch", "blk", *ULY)
ROWS = ("batch", "blk")
PLANE = ("batch", *ULY)
CHIPS = ("batch", "y")

MESH = pl.DeviceIdType.MESH
BF16 = jnp.bfloat16
F32 = jnp.float32


def rms_scale(values):
    return lax.rsqrt(jnp.mean(values * values, axis=-1, keepdims=True) + EPS)


def norm_back(grad_normed, values, scale):
    normed = values * scale
    return scale * (grad_normed - normed * jnp.mean(grad_normed * normed, axis=-1, keepdims=True))


def rope_tables(offset, length, head_dim):
    half_dim = head_dim // 2
    frequency = THETA ** (-jnp.arange(half_dim, dtype=F32) * 2.0 / head_dim)
    positions = (offset + jnp.arange(length, dtype=jnp.int32)).astype(F32)
    angles = positions[:, None] * frequency[None, :]
    return (jnp.cos(angles)[:, None, :], jnp.sin(angles)[:, None, :])


def rope_rows(length, head_dim):
    fine = math.gcd(length, LANES)
    frequency = THETA ** (-jnp.arange(head_dim // 2, dtype=F32) * 2.0 / head_dim)
    frequency = jnp.concatenate([frequency, frequency])
    coarse_angle = (jnp.arange(length // fine, dtype=F32) * fine)[:, None, None] * frequency
    fine_angle = jnp.arange(fine, dtype=F32)[None, :, None] * frequency
    cos_a, sin_a, cos_b, sin_b = lax.optimization_barrier(
        (jnp.cos(coarse_angle), jnp.sin(coarse_angle), jnp.cos(fine_angle), jnp.sin(fine_angle))
    )
    sign = jnp.where(jnp.arange(head_dim) < head_dim // 2, -1.0, 1.0)
    cos = cos_a * cos_b - sin_a * sin_b
    sin = (sin_a * cos_b + cos_a * sin_b) * sign
    return cos.reshape(length, head_dim), sin.reshape(length, head_dim)


def rotate(values, cos_table, sin_table):
    half_dim = values.shape[-1] // 2
    first = values[..., :half_dim]
    second = values[..., half_dim:]
    return jnp.concatenate(
        [first * cos_table - second * sin_table, second * cos_table + first * sin_table], axis=-1
    )


def dot_nn(a, b):
    return lax.dot_general(a, b, (((1,), (0,)), ((), ())), preferred_element_type=F32)


def dot_nt(a, b):
    return lax.dot_general(a, b, (((1,), (1,)), ((), ())), preferred_element_type=F32)


def dot_tn(a, b):
    return lax.dot_general(a, b, (((0,), (0,)), ((), ())), preferred_element_type=F32)


def key_chunks(length):
    size = min(512, length)
    return size, length // size


def attn_fwd_kernel(factor, q_ref, k_ref, v_ref, sq_ref, sk_ref, o_ref, of_ref, lse_ref, top_ref, vt_ref):
    length = k_ref.shape[1]
    size, count = key_chunks(length)
    tile, head_dim = q_ref.shape[1:]

    @pl.when(pl.program_id(1) == 0)
    def _():
        vt_ref[...] = v_ref[0].astype(F32).T.astype(BF16)

    q = q_ref[0]
    seg_q = sq_ref[...]

    def step(j, carried):
        total, top, acc = carried
        at = pl.multiple_of(j * size, size)
        scores = dot_nt(k_ref[0, pl.ds(at, size), :], q)
        scores = jnp.where(sk_ref[pl.ds(at, size), :] == seg_q, scores, NEG)
        top = jnp.maximum(top, jnp.max(scores, axis=0, keepdims=True))
        weights = jnp.exp2(scores * factor)
        total = total + jnp.sum(weights, axis=0, keepdims=True)
        acc = acc + dot_nn(vt_ref[:, pl.ds(at, size)], weights.astype(BF16))
        return total, top, acc

    start = (
        jnp.zeros((1, tile), F32),
        jnp.full((1, tile), NEG, F32),
        jnp.zeros((head_dim, tile), F32),
    )
    total, top, acc = lax.fori_loop(0, count, step, start, unroll=count <= 4)
    out = (acc * (1.0 / total)).T
    o_ref[0] = out.astype(BF16)
    of_ref[0] = out
    lse_ref[0] = jnp.log2(total)
    top_ref[0] = top


def attn_bwd_kernel(
    factor, scale, q_ref, k_ref, v_ref, do_ref, of_ref, lse_ref, sq_ref, sk_ref,
    dq_ref, dk_ref, dv_ref, kt_ref, dk_acc, dv_acc,
):
    length = k_ref.shape[1]
    size, count = key_chunks(length)
    tile, head_dim = q_ref.shape[1:]

    @pl.when(pl.program_id(1) == 0)
    def _():
        kt_ref[...] = k_ref[0].astype(F32).T.astype(BF16)
        dk_acc[...] = jnp.zeros_like(dk_acc)
        dv_acc[...] = jnp.zeros_like(dv_acc)

    q = q_ref[0]
    grad = do_ref[0]
    seg_q = sq_ref[...]
    lse = lse_ref[0]
    row_dot = jnp.sum((grad.astype(F32) * of_ref[0]).T, axis=0, keepdims=True)

    def step(j, dq_t):
        at = pl.multiple_of(j * size, size)
        rows = pl.ds(at, size)
        scores = dot_nt(k_ref[0, rows, :], q)
        scores = jnp.where(sk_ref[rows, :] == seg_q, scores, NEG)
        weights = jnp.exp2(scores * factor - lse)
        grad_weights = dot_nt(v_ref[0, rows, :], grad)
        grad_scores = (weights * (grad_weights - row_dot)).astype(BF16)
        dk_acc[rows, :] += dot_nn(grad_scores, q)
        dv_acc[rows, :] += dot_nn(weights.astype(BF16), grad)
        return dq_t + dot_nn(kt_ref[:, rows], grad_scores)

    dq_t = lax.fori_loop(0, count, step, jnp.zeros((head_dim, tile), F32), unroll=count <= 4)
    dq_ref[0] = (dq_t * scale).T.astype(BF16)

    @pl.when(pl.program_id(1) == pl.num_programs(1) - 1)
    def _():
        dk_ref[0] = (dk_acc[...] * scale).astype(BF16)
        dv_ref[0] = dv_acc[...].astype(BF16)


def attention_tile(queries, length):
    return min(queries, 256 if length <= 4096 else 128)


def attention_forward(q_src, kv_src, cols, seg_q, seg_k, head_dim):
    heads, queries = q_src.shape[:2]
    length = kv_src.shape[1]
    tile = attention_tile(queries, length)
    q_col, k_col, v_col = cols
    factor = head_dim**-0.5 * LOG2E
    row = pl.BlockSpec((1, 1, tile), lambda h, i: (h, 0, i))
    block = pl.BlockSpec((1, tile, head_dim), lambda h, i: (h, i, 0))
    return pl.pallas_call(
        functools.partial(attn_fwd_kernel, factor),
        grid=(heads, queries // tile),
        in_specs=[
            pl.BlockSpec((1, tile, head_dim), lambda h, i: (h, i, q_col)),
            pl.BlockSpec((1, length, head_dim), lambda h, i: (h, 0, k_col)),
            pl.BlockSpec((1, length, head_dim), lambda h, i: (h, 0, v_col)),
            pl.BlockSpec((1, tile), lambda h, i: (0, i)),
            pl.BlockSpec((length, 1), lambda h, i: (0, 0)),
        ],
        out_specs=[block, block, row, row],
        out_shape=[
            jax.ShapeDtypeStruct((heads, queries, head_dim), BF16),
            jax.ShapeDtypeStruct((heads, queries, head_dim), F32),
            jax.ShapeDtypeStruct((heads, 1, queries), F32),
            jax.ShapeDtypeStruct((heads, 1, queries), F32),
        ],
        scratch_shapes=[pltpu.VMEM((head_dim, length), BF16)],
        compiler_params=pltpu.CompilerParams(vmem_limit_bytes=VMEM_LIMIT),
        cost_estimate=pl.CostEstimate(
            flops=4 * heads * queries * length * head_dim,
            bytes_accessed=heads * (queries + length) * head_dim * 8,
            transcendentals=heads * queries * length,
        ),
        name="attend",
    )(q_src, kv_src, kv_src, seg_q.reshape(1, -1), seg_k.reshape(-1, 1))


def attention_backward(q_src, kv_src, cols, grad, out_f32, lse, seg_q, seg_k, head_dim):
    heads, queries = q_src.shape[:2]
    length = kv_src.shape[1]
    tile = attention_tile(queries, length)
    q_col, k_col, v_col = cols
    scale = head_dim**-0.5
    row = pl.BlockSpec((1, 1, tile), lambda h, i: (h, 0, i))
    block = pl.BlockSpec((1, tile, head_dim), lambda h, i: (h, i, 0))
    whole = pl.BlockSpec((1, length, head_dim), lambda h, i: (h, 0, 0))
    return pl.pallas_call(
        functools.partial(attn_bwd_kernel, scale * LOG2E, scale),
        grid=(heads, queries // tile),
        in_specs=[
            pl.BlockSpec((1, tile, head_dim), lambda h, i: (h, i, q_col)),
            pl.BlockSpec((1, length, head_dim), lambda h, i: (h, 0, k_col)),
            pl.BlockSpec((1, length, head_dim), lambda h, i: (h, 0, v_col)),
            block,
            block,
            row,
            pl.BlockSpec((1, tile), lambda h, i: (0, i)),
            pl.BlockSpec((length, 1), lambda h, i: (0, 0)),
        ],
        out_specs=[block, whole, whole],
        out_shape=[
            jax.ShapeDtypeStruct((heads, queries, head_dim), BF16),
            jax.ShapeDtypeStruct((heads, length, head_dim), BF16),
            jax.ShapeDtypeStruct((heads, length, head_dim), BF16),
        ],
        scratch_shapes=[
            pltpu.VMEM((head_dim, length), BF16),
            pltpu.VMEM((length, head_dim), F32),
            pltpu.VMEM((length, head_dim), F32),
        ],
        compiler_params=pltpu.CompilerParams(vmem_limit_bytes=VMEM_LIMIT),
        cost_estimate=pl.CostEstimate(
            flops=10 * heads * queries * length * head_dim,
            bytes_accessed=heads * (queries + length) * head_dim * 12,
            transcendentals=heads * queries * length,
        ),
        name="attend_back",
    )(q_src, kv_src, kv_src, grad, out_f32, lse, seg_q.reshape(1, -1), seg_k.reshape(-1, 1))


def expert_step(expert, h_ref, ht_ref, dy_ref, dyt_ref, gate_ref, wg_ref, wu_ref, wd_ref, dg_ref, out_acc, dx_acc):
    width = h_ref.shape[1]
    cols = wg_ref.shape[3]
    w_gate = wg_ref[...].reshape(width, cols)
    w_up = wu_ref[...].reshape(width, cols)
    w_down = wd_ref[...].reshape(width, cols)
    gates = gate_ref[...]
    mine = lax.broadcasted_iota(jnp.int32, gates.shape, 1) == expert
    gate = jnp.sum(jnp.where(mine, gates, 0.0), axis=1, keepdims=True)
    a_gate = dot_nn(h_ref[...], w_gate)
    a_up = dot_nn(h_ref[...], w_up)
    raw = dot_nn(dy_ref[...], w_down)
    sigma = 1.0 / (1.0 + jnp.exp2(a_gate * -LOG2E))
    swish = a_gate * sigma
    act = swish * a_up
    dg_ref[0] += jnp.sum(raw * act, axis=1, keepdims=True)
    gated = (gate * act).astype(BF16)
    d_act = gate * raw
    d_gate = (d_act * a_up * (sigma + swish * (1.0 - sigma))).astype(BF16)
    d_up = (d_act * swish).astype(BF16)
    out_acc[...] += dot_nt(gated, w_down)
    dx_acc[...] += dot_nt(d_gate, w_gate) + dot_nt(d_up, w_up)
    for part, (left, right) in enumerate([(ht_ref, d_gate), (ht_ref, d_up), (dyt_ref, gated)]):
        yield part, dot_nn(left[...], right).astype(BF16)


def expert_kernel(more, counts, *refs):
    h_ref, ht_ref, dy_ref, dyt_ref, gate_ref = refs[:5]
    sources = [refs[5 + 3 * i : 8 + 3 * i] for i in range(len(counts))]
    out_ref, dx_ref, dg_ref, gr_ref, out_acc, dx_acc = refs[-6:]
    step, last = pl.program_id(0), pl.num_programs(0) - 1
    parts, _, part_rows, cols = sources[0][0].shape
    chunks = (last + 1) // sum(counts)

    @pl.when(step == 0)
    def _():
        if more:
            out0_ref, dx0_ref = refs[-8:-6]
            out_acc[...] = out0_ref[...].astype(F32)
            dx_acc[...] = dx0_ref[...].astype(F32)
        else:
            out_acc[...] = jnp.zeros_like(out_acc)
            dx_acc[...] = jnp.zeros_like(dx_acc)

    @pl.when(step % chunks == 0)
    def _():
        dg_ref[...] = jnp.zeros_like(dg_ref)

    begin = 0
    for source, count in zip(sources, counts):
        end = begin + count * chunks

        @pl.when((step >= begin) & (step < end))
        def _(source=source):
            for part, made in expert_step(
                step // chunks, h_ref, ht_ref, dy_ref, dyt_ref, gate_ref, *source, dg_ref, out_acc, dx_acc
            ):
                gr_ref[:, part, 0] = made.reshape(parts, part_rows, cols)

        begin = end

    @pl.when(step == last)
    def _():
        out_ref[...] = out_acc[...].astype(BF16)
        dx_ref[...] = dx_acc[...].astype(BF16)


def experts(hidden, hidden_t, grad, grad_t, gates, sources, before=()):
    tokens, width = hidden.shape
    parts, _, part_rows, units = sources[0][0].shape
    units = units // 3
    counts = [count for _, _, count in sources]
    total = sum(counts)
    cols = min(256, units)
    chunks = units // cols
    once = pl.Buffered(1)
    whole = pl.BlockSpec((tokens, width), lambda s: (0, 0), pipeline_mode=once)
    whole_t = pl.BlockSpec((width, tokens), lambda s: (0, 0), pipeline_mode=once)
    result = pl.BlockSpec((tokens, width), lambda s: (0, 0))

    def weight(source, kind):
        _, first, count = sources[source]
        begin = sum(counts[:source]) * chunks

        def index(step):
            at = jnp.clip(step - begin, 0, count * chunks - 1)
            return (0, first + at // chunks, 0, kind * chunks + at % chunks)

        return pl.BlockSpec((parts, 1, part_rows, cols), index)

    return pl.pallas_call(
        functools.partial(expert_kernel, bool(before), counts),
        grid=(total * chunks,),
        in_specs=[
            whole,
            whole_t,
            whole,
            whole_t,
            pl.BlockSpec(gates.shape, lambda s: (0, 0), pipeline_mode=once),
            *[weight(source, kind) for source in range(len(sources)) for kind in range(3)],
            *[whole for _ in before],
        ],
        out_specs=[
            result,
            result,
            pl.BlockSpec((1, tokens, 1), lambda s: (s // chunks, 0, 0)),
            pl.BlockSpec((parts, 3, 1, part_rows, cols), lambda s: (0, 0, s // chunks, 0, s % chunks)),
        ],
        out_shape=[
            jax.ShapeDtypeStruct((tokens, width), BF16),
            jax.ShapeDtypeStruct((tokens, width), BF16),
            jax.ShapeDtypeStruct((total, tokens, 1), F32),
            jax.ShapeDtypeStruct((parts, 3, total, part_rows, units), BF16),
        ],
        scratch_shapes=[
            pltpu.VMEM((tokens, width), F32),
            pltpu.VMEM((tokens, width), F32),
        ],
        compiler_params=pltpu.CompilerParams(vmem_limit_bytes=VMEM_LIMIT),
        cost_estimate=pl.CostEstimate(
            flops=18 * total * tokens * width * units,
            bytes_accessed=12 * total * width * units,
            transcendentals=total * tokens * units,
        ),
        name="experts",
    )(hidden, hidden_t, grad, grad_t, gates, *[array for array, _, _ in sources for _ in range(3)], *before)


def finish_experts_kernel(sums_ref, *refs):
    gate_up_ref, down_ref = refs[-2:]
    units = down_ref.shape[2]
    gate_up_ref[0, :, :units] = sums_ref[0, 0].astype(F32)
    gate_up_ref[0, :, units:] = sums_ref[1, 0].astype(F32)
    down_ref[0] = sums_ref[2, 0].astype(F32)


def finish_experts(sums, at, total, before=()):
    _, count, rows, units = sums.shape
    tile = min(128, rows)
    return pl.pallas_call(
        finish_experts_kernel,
        grid=(count, rows // tile),
        in_specs=[
            pl.BlockSpec((3, 1, tile, units), lambda e, r: (0, e, r, 0)),
            *[pl.BlockSpec(memory_space=pl.ANY) for _ in before],
        ],
        out_specs=[
            pl.BlockSpec((1, tile, 2 * units), lambda e, r: (at + e, r, 0)),
            pl.BlockSpec((1, tile, units), lambda e, r: (at + e, r, 0)),
        ],
        out_shape=[
            jax.ShapeDtypeStruct((total, rows, 2 * units), F32),
            jax.ShapeDtypeStruct((total, rows, units), F32),
        ],
        input_output_aliases={1 + i: i for i in range(len(before))},
        compiler_params=pltpu.CompilerParams(vmem_limit_bytes=VMEM_LIMIT),
        name="finish_experts",
    )(sums, *before)


def turn(values, cos, sin):
    return values * cos + pltpu.roll(values, values.shape[1] // 2, 1) * sin


def project_kernel(
    tok_ref, gain_ref, w_ref, cos_ref, sin_ref, gains_ref, hidden_ref, qkv_ref, raw_ref
):
    head_dim = cos_ref.shape[1]
    values = tok_ref[...].astype(F32)
    hidden = (values * rms_scale(values) * gain_ref[...]).astype(BF16)
    hidden_ref[...] = hidden
    projected = dot_nn(hidden, w_ref[...])
    raw_ref[...] = projected[:, : 2 * head_dim]
    for part in range(2):
        at = slice(part * head_dim, (part + 1) * head_dim)
        raw = projected[:, at]
        normed = raw * rms_scale(raw) * gains_ref[part : part + 1, :]
        qkv_ref[:, at] = turn(normed, cos_ref[...], sin_ref[...]).astype(BF16)
    qkv_ref[:, 2 * head_dim :] = projected[:, 2 * head_dim :].astype(BF16)


def project(toks, gain, weights, cos, sin, gains):
    length, width = toks.shape
    head_dim = cos.shape[1]
    tile = min(256, length)

    def rows(columns):
        return pl.BlockSpec((tile, columns), lambda i: (i, 0))

    def fixed(shape):
        return pl.BlockSpec(shape, lambda i: (0, 0))

    return pl.pallas_call(
        project_kernel,
        grid=(length // tile,),
        in_specs=[
            rows(width),
            fixed((1, width)),
            fixed(weights.shape),
            rows(head_dim),
            rows(head_dim),
            fixed(gains.shape),
        ],
        out_specs=[rows(width), rows(3 * head_dim), rows(2 * head_dim)],
        out_shape=[
            jax.ShapeDtypeStruct((length, width), BF16),
            jax.ShapeDtypeStruct((length, 3 * head_dim), BF16),
            jax.ShapeDtypeStruct((length, 2 * head_dim), F32),
        ],
        compiler_params=pltpu.CompilerParams(vmem_limit_bytes=VMEM_LIMIT),
        name="project",
    )(toks, gain, weights, cos, sin, gains)


def project_back_kernel(
    factor, scale, q_ref, k_ref, v_ref, do_ref, of_ref, lse_ref, sq_ref, sk_ref,
    raw_q_ref, raw_k_ref, cos_q_ref, sin_q_ref, cos_ref, sin_ref, gains_ref,
    dp_ref, dgain_ref, kt_ref, dk_acc, dv_acc,
):
    length, head_dim = k_ref.shape
    size, count = key_chunks(length)
    tile = q_ref.shape[0]
    step_at = pl.program_id(0)

    @pl.when(step_at == 0)
    def _():
        kt_ref[...] = k_ref[...].astype(F32).T.astype(BF16)
        dk_acc[...] = jnp.zeros_like(dk_acc)
        dv_acc[...] = jnp.zeros_like(dv_acc)
        dgain_ref[...] = jnp.zeros_like(dgain_ref)

    def to_raw(part, grad, raw, cos, sin):
        grad = turn(grad.astype(BF16).astype(F32), cos, -sin)
        raw_scale = rms_scale(raw)
        dgain_ref[part : part + 1, :] += jnp.sum(grad * (raw * raw_scale), axis=0, keepdims=True)
        return norm_back(grad * gains_ref[part : part + 1, :], raw, raw_scale).astype(BF16)

    q = q_ref[...]
    grad = do_ref[...]
    seg_q = sq_ref[...]
    lse = lse_ref[0]
    row_dot = jnp.sum((grad.astype(F32) * of_ref[0]).T, axis=0, keepdims=True)
    dq_t = jnp.zeros((head_dim, tile), F32)
    for j in range(count):
        rows = slice(j * size, (j + 1) * size)
        scores = dot_nt(k_ref[rows, :], q)
        scores = jnp.where(sk_ref[rows, :] == seg_q, scores, NEG)
        weights = jnp.exp2(scores * factor - lse)
        grad_weights = dot_nt(v_ref[rows, :], grad)
        grad_scores = (weights * (grad_weights - row_dot)).astype(BF16)
        dk_acc[rows, :] += dot_nn(grad_scores, q)
        dv_acc[rows, :] += dot_nn(weights.astype(BF16), grad)
        dq_t = dq_t + dot_nn(kt_ref[:, rows], grad_scores)
    own = pl.ds(pl.multiple_of(step_at * tile, tile), tile)
    dp_ref[own, :head_dim] = to_raw(
        0, (dq_t * scale).T, raw_q_ref[...], cos_q_ref[...], sin_q_ref[...]
    )

    @pl.when(step_at == pl.num_programs(0) - 1)
    def _():
        dp_ref[:, head_dim : 2 * head_dim] = to_raw(
            1, dk_acc[...] * scale, raw_k_ref[...], cos_ref[...], sin_ref[...]
        )
        dp_ref[:, 2 * head_dim :] = dv_acc[...].astype(BF16)


def project_back(qkv, grad, out_f32, lse, segments, raw, cos, sin, gains):
    length, head_dim = grad.shape
    tile = min(256, length)

    def rows(column):
        return pl.BlockSpec((tile, head_dim), lambda i: (i, column))

    def whole(column):
        return pl.BlockSpec((length, head_dim), lambda i: (0, column))

    return pl.pallas_call(
        functools.partial(project_back_kernel, head_dim**-0.5 * LOG2E, head_dim**-0.5),
        grid=(length // tile,),
        in_specs=[
            rows(0),
            whole(1),
            whole(2),
            rows(0),
            pl.BlockSpec((1, tile, head_dim), lambda i: (0, i, 0)),
            pl.BlockSpec((1, 1, tile), lambda i: (0, 0, i)),
            pl.BlockSpec((1, tile), lambda i: (0, i)),
            pl.BlockSpec((length, 1), lambda i: (0, 0)),
            rows(0),
            whole(1),
            rows(0),
            rows(0),
            whole(0),
            whole(0),
            pl.BlockSpec(gains.shape, lambda i: (0, 0)),
        ],
        out_specs=[
            pl.BlockSpec((length, 3 * head_dim), lambda i: (0, 0)),
            pl.BlockSpec((2, head_dim), lambda i: (0, 0)),
        ],
        out_shape=[
            jax.ShapeDtypeStruct((length, 3 * head_dim), BF16),
            jax.ShapeDtypeStruct((2, head_dim), F32),
        ],
        scratch_shapes=[
            pltpu.VMEM((head_dim, length), BF16),
            pltpu.VMEM((length, head_dim), F32),
            pltpu.VMEM((length, head_dim), F32),
        ],
        compiler_params=pltpu.CompilerParams(vmem_limit_bytes=VMEM_LIMIT),
        cost_estimate=pl.CostEstimate(
            flops=10 * length * length * head_dim,
            bytes_accessed=length * head_dim * 40,
            transcendentals=length * length,
        ),
        name="project_back",
    )(
        qkv, qkv, qkv, grad, out_f32, lse, segments.reshape(1, -1), segments.reshape(-1, 1),
        raw, raw, cos, sin, cos, sin, gains,
    )


def hidden_back_kernel(grads_ref, own_ref, near_ref, far_ref, cross_ref, hidden_ref, out_ref, gain_ref):
    uly = grads_ref.shape[0]
    u = lax.axis_index(ULY)
    near = u + 1 - 2 * lax.rem(u, 2)
    total = dot_nt(grads_ref[u], own_ref[...])
    total = total + dot_nt(grads_ref[near], near_ref[...])
    total = total + dot_nt(grads_ref[lax.rem(u + 2, uly)], far_ref[...])
    total = total + dot_nt(grads_ref[lax.rem(near + 2, uly)], cross_ref[...])
    out_ref[...] = total.astype(BF16).reshape(out_ref.shape)
    hidden = hidden_ref[...].reshape(total.shape).astype(F32)
    gain_ref[...] = jnp.sum(total * hidden, axis=0, keepdims=True)


def hidden_back(grads, own, near, far, cross, hidden):
    uly, tokens, columns = grads.shape
    blk, _, rows, width = hidden.shape
    tile = min(512, width)
    weights = pl.BlockSpec((tile, columns), lambda n: (n, 0))
    return pl.pallas_call(
        hidden_back_kernel,
        grid=(width // tile,),
        in_specs=[
            pl.BlockSpec(grads.shape, lambda n: (0, 0, 0)),
            *[weights] * 4,
            pl.BlockSpec((blk, 1, rows, tile), lambda n: (0, lax.axis_index(ULY), 0, n)),
        ],
        out_specs=[
            pl.BlockSpec((blk, rows, tile), lambda n: (0, 0, n)),
            pl.BlockSpec((1, tile), lambda n: (0, n)),
        ],
        out_shape=[
            jax.ShapeDtypeStruct((blk, rows, width), BF16),
            jax.ShapeDtypeStruct((1, width), F32),
        ],
        compiler_params=pltpu.CompilerParams(vmem_limit_bytes=VMEM_LIMIT),
        name="hidden_back",
    )(grads, own, near, far, cross, hidden)


def merge_heads_kernel(parts_ref, out_ref):
    blk, uly, _, columns = parts_ref.shape
    head_dim = columns // 3
    heads = blk * uly
    for z in range(blk):
        for u in range(uly):
            head = parts_ref[z, u].astype(F32)
            for part in range(3):
                at = (part * heads + u * blk + z) * head_dim
                out_ref[:, at : at + head_dim] = head[:, part * head_dim : (part + 1) * head_dim]


def merge_heads(parts):
    blk, uly, rows, columns = parts.shape
    return pl.pallas_call(
        merge_heads_kernel,
        out_shape=jax.ShapeDtypeStruct((rows, blk * uly * columns), F32),
        compiler_params=pltpu.CompilerParams(vmem_limit_bytes=VMEM_LIMIT),
        name="merge_heads",
    )(parts)


def swap(values, axis):
    return lax.all_to_all(values, axis, split_axis=0, concat_axis=0, tiled=True)


def sum_scatter(values, axis):
    count = spread(axis) if isinstance(axis, tuple) else lax.axis_size(axis)
    rows, width = values.shape
    parts = swap(values.astype(BF16).reshape(count, rows // count, width), axis)
    return jnp.sum(parts.astype(F32), axis=0)


def place(axes, index):
    found = {}
    for axis in reversed(axes):
        size = lax.axis_size(axis)
        found[axis] = lax.rem(index, size)
        index = index // size
    return found


def spread(axes):
    return math.prod(lax.axis_size(axis) for axis in axes)


def each(count, body):
    if count <= 4:
        for step in range(1, count):
            body(step)
    else:

        def looped(step, carried):
            body(step)
            return carried

        lax.fori_loop(1, count, looped, 0)


def ahead(index, step, size):
    return lax.rem(index + step, size)


def exchange(items, collective_id, after=()):
    count = len(items)
    sizes = [spread(axes) for _, axes, _ in items]
    groups = list(dict.fromkeys(axes for _, axes, _ in items))
    bases = [sum(2 * size for size in sizes[:i]) for i in range(count)]

    def kernel(*refs):
        ins = refs[:count]
        outs = refs[count + len(after) : 2 * count + len(after)]
        send, recv, local = refs[2 * count + len(after) :][:3]
        barrier = pltpu.get_barrier_semaphore()
        for axes in groups:
            size, me = spread(axes), lax.axis_index(axes)

            def greet(step, axes=axes, size=size, me=me):
                pl.semaphore_signal(
                    barrier, inc=1, device_id=place(axes, ahead(me, step, size)), device_id_type=MESH
                )

            each(size, greet)
        pl.semaphore_wait(barrier, sum(spread(axes) - 1 for axes in groups))

        def block(i, peer):
            if items[i][2] == "swap":
                return ins[i].at[peer]
            return ins[i].at[:, peer] if items[i][2] == "swap1" else ins[i]

        def remote(i, step):
            _, axes, kind = items[i]
            me = lax.axis_index(axes)
            if kind == "trade":
                return pltpu.make_async_remote_copy(
                    src_ref=ins[i],
                    dst_ref=outs[i],
                    send_sem=send.at[bases[i] + 1],
                    recv_sem=recv.at[bases[i] + 1],
                    device_id=place(axes, 1 - me),
                    device_id_type=MESH,
                )
            if kind == "relay":
                far, near = lax.rem(me + 2, 4), me + 1 - 2 * lax.rem(me, 2)
                held = far if step == 3 else me
                return pltpu.make_async_remote_copy(
                    src_ref=outs[i].at[far] if step == 3 else ins[i],
                    dst_ref=outs[i].at[held],
                    send_sem=send.at[bases[i] + step],
                    recv_sem=recv.at[bases[i] + step],
                    device_id=place(axes, far if step == 1 else near),
                    device_id_type=MESH,
                )
            peer = ahead(me, step, sizes[i])
            return pltpu.make_async_remote_copy(
                src_ref=block(i, peer),
                dst_ref=outs[i].at[me],
                send_sem=send.at[bases[i] + step],
                recv_sem=recv.at[bases[i] + step],
                device_id=place(axes, peer),
                device_id_type=MESH,
            )

        def own(i):
            _, axes, kind = items[i]
            me = lax.axis_index(axes)
            return pltpu.make_async_copy(
                block(i, me), outs[i].at[me], local.at[i]
            )

        def hop(i, up, hops):
            (axis,) = items[i][1]
            me, size = lax.axis_index(axis), sizes[i]
            way = 1 if up else -1
            held, to = me - way * hops, me + way
            exists = (held >= 0) & (held < size) & (to >= 0) & (to < size)
            held, to = jnp.clip(held, 0, size - 1), jnp.clip(to, 0, size - 1)
            sem = bases[i] + (size if up else 0) + hops
            copy = pltpu.make_async_remote_copy(
                src_ref=outs[i].at[held] if hops else ins[i],
                dst_ref=outs[i].at[held],
                send_sem=send.at[sem],
                recv_sem=recv.at[sem],
                device_id={axis: to},
                device_id_type=MESH,
            )
            return exists, copy

        def arrival(i, up, hops):
            (axis,) = items[i][1]
            me, size = lax.axis_index(axis), sizes[i]
            way = 1 if up else -1
            held, sender = me - way * (hops + 1), me - way
            exists = (held >= 0) & (held < size)
            held, sender = jnp.clip(held, 0, size - 1), jnp.clip(sender, 0, size - 1)
            sem = bases[i] + (size if up else 0) + hops
            copy = pltpu.make_async_remote_copy(
                src_ref=ins[i],
                dst_ref=outs[i].at[held],
                send_sem=send.at[sem],
                recv_sem=recv.at[sem],
                device_id={axis: sender},
                device_id_type=MESH,
            )
            return exists, copy

        def kinds(*names):
            return [i for i in range(count) if items[i][2] in names]

        def when(pair, act):
            exists, copy = pair
            pl.when(exists)(lambda: act(copy))

        def pairsum(i):
            me = lax.axis_index(ULY)
            far, near = lax.rem(me + 2, 4), me + 1 - 2 * lax.rem(me, 2)
            own, out = ins[i], outs[i]
            got_near, got_far, sent = refs[2 * count + len(after) + 3 :]

            def copy(at, src, dst, to):
                return pltpu.make_async_remote_copy(
                    src_ref=src,
                    dst_ref=dst,
                    send_sem=send.at[bases[i] + at],
                    recv_sem=recv.at[bases[i] + at],
                    device_id=place(ULY, to),
                    device_id_type=MESH,
                )

            to_near = [
                copy(0, own.at[near], got_near.at[0], near),
                copy(1, own.at[lax.rem(near + 2, 4)], got_near.at[1], near),
            ]
            to_far = copy(2, sent, got_far, far)

            def first():
                for sending in to_near:
                    sending.start()

            def second():
                for sending in to_near:
                    sending.wait()
                sent[...] = (own[far].astype(F32) + got_near[1].astype(F32)).astype(BF16)
                to_far.start()
                out[...] = own[me].astype(F32) + got_near[0].astype(F32)

            def third():
                to_far.wait()
                out[...] += got_far[...].astype(F32)

            return first, second, third

        ways = (True, False)
        sums = [pairsum(i) for i in kinds("pairsum")]
        for first, _, _ in sums:
            first()
        for i in kinds("line"):
            for up in ways:
                when(hop(i, up, 0), lambda copy: copy.start())
        for i in kinds("gather", "swap", "swap1", "relay", "trade"):
            each(3 if items[i][2] == "relay" else sizes[i], lambda step, i=i: remote(i, step).start())
        for i in kinds("gather", "swap", "swap1", "relay", "line"):
            own(i).start()
        for _, second, _ in sums:
            second()
        for i in kinds("line"):
            for hops in range(1, sizes[i]):
                for up in ways:
                    when(arrival(i, up, hops - 1), lambda copy: copy.wait_recv())
                    if hops < sizes[i] - 1:
                        when(hop(i, up, hops), lambda copy: copy.start())
        for i in kinds("relay"):
            remote(i, 1).wait_recv()
            remote(i, 3).start()
            remote(i, 1).wait_send()
            for step in (2, 3):
                remote(i, step).wait()
        for i in kinds("gather", "swap", "swap1", "trade"):
            each(sizes[i], lambda step, i=i: remote(i, step).wait())
        for i in kinds("line"):
            for hops in range(sizes[i] - 1):
                for up in ways:
                    when(hop(i, up, hops), lambda copy: copy.wait_send())
        for i in kinds("gather", "swap", "swap1", "relay", "line"):
            own(i).wait()
        for _, _, third in sums:
            third()


    def shape_of(size, array, kind):
        if kind in ("trade", "pairsum"):
            return array.shape[kind == "pairsum" :]
        dropped = {"swap": 0, "swap1": 1}.get(kind)
        return (size, *(extent for at, extent in enumerate(array.shape) if at != dropped))

    anywhere, close = pl.BlockSpec(memory_space=pl.ANY), pl.BlockSpec(memory_space=pltpu.VMEM)
    specs = [close if kind == "pairsum" else anywhere for _, _, kind in items]
    held = []
    for array, _, kind in items:
        if kind == "pairsum":
            held = [pltpu.VMEM((*more, *array.shape[1:]), BF16) for more in ((2,), (), ())]
    return pl.pallas_call(
        kernel,
        in_specs=specs + [anywhere] * len(after),
        out_specs=specs,
        out_shape=[
            jax.ShapeDtypeStruct(shape_of(size, array, kind), F32 if kind == "pairsum" else array.dtype)
            for size, (array, _, kind) in zip(sizes, items)
        ],
        scratch_shapes=[
            pltpu.SemaphoreType.DMA((2 * sum(sizes),)),
            pltpu.SemaphoreType.DMA((2 * sum(sizes),)),
            pltpu.SemaphoreType.DMA((count,)),
            *held,
        ],
        compiler_params=pltpu.CompilerParams(
            collective_id=collective_id, has_side_effects=True, vmem_limit_bytes=VMEM_LIMIT if held else None
        ),
        name="exchange",
    )(*[item[0] for item in items], *after)


def turn_gather_kernel(
    own_ref, other_ref, all_ref, all_t_ref, other_t_ref, block, turned, send, recv, local
):
    size, me = lax.axis_size("blk"), lax.axis_index("blk")
    rows = own_ref.shape[0]
    barrier = pltpu.get_barrier_semaphore()
    ways = (1, 0)

    def neighbour(up):
        to = me + (1 if up else -1)
        return (to >= 0) & (to < size), jnp.clip(to, 0, size - 1)

    def greet(step):
        pl.semaphore_signal(
            barrier, inc=1, device_id={"blk": ahead(me, step, size)}, device_id_type=MESH
        )

    each(size, greet)
    pl.semaphore_wait(barrier, size - 1)

    def hop(up, hops):
        held = me - (1 if up else -1) * hops
        exists, to = neighbour(up)
        exists = exists & (held >= 0) & (held < size)
        held = jnp.clip(held, 0, size - 1)
        return exists, pltpu.make_async_remote_copy(
            src_ref=all_ref.at[held] if hops else own_ref,
            dst_ref=all_ref.at[held],
            send_sem=send.at[up * size + hops],
            recv_sem=recv.at[up * size + hops],
            device_id={"blk": to},
            device_id_type=MESH,
        )

    def arrival(up, hops):
        held = me - (1 if up else -1) * (hops + 1)
        exists = (held >= 0) & (held < size)
        held = jnp.clip(held, 0, size - 1)
        return exists, held, pltpu.make_async_remote_copy(
            src_ref=own_ref,
            dst_ref=all_ref.at[held],
            send_sem=send.at[up * size + hops],
            recv_sem=recv.at[up * size + hops],
            device_id={"blk": neighbour(1 - up)[1]},
            device_id_type=MESH,
        )

    def when(pair, act):
        exists, copy = pair
        pl.when(exists)(lambda: act(copy))

    def turn(src, dst, at):
        take = pltpu.make_async_copy(src, block, local.at[0])
        take.start()
        take.wait()
        turned[...] = block[...].T
        columns = pl.ds(pl.multiple_of(at * rows, rows), rows)
        give = pltpu.make_async_copy(turned, dst.at[:, columns], local.at[1])
        give.start()
        give.wait()

    for up in ways:
        when(hop(up, 0), lambda copy: copy.start())
    keep = pltpu.make_async_copy(own_ref, all_ref.at[me], local.at[2])
    keep.start()
    turn(own_ref, all_t_ref, me)
    for at in range(size):
        turn(other_ref.at[at], other_t_ref, at)
    for hops in range(1, size):
        for up in ways:
            exists, held, copy = arrival(up, hops - 1)

            @pl.when(exists)
            def _(copy=copy, up=up, hops=hops):
                copy.wait_recv()
                if hops < size - 1:
                    when(hop(up, hops), lambda copy: copy.start())

        for up in ways:
            exists, held, copy = arrival(up, hops - 1)
            pl.when(exists)(lambda held=held: turn(all_ref.at[held], all_t_ref, held))
    for hops in range(size - 1):
        for up in ways:
            when(hop(up, hops), lambda copy: copy.wait_send())
    keep.wait()


def turn_gather(own, other, collective_id, after=()):
    size = lax.axis_size("blk")
    rows, width = own.shape
    anywhere = pl.BlockSpec(memory_space=pl.ANY)

    def kernel(*refs):
        turn_gather_kernel(*refs[:2], *refs[2 + len(after) :])

    return pl.pallas_call(
        kernel,
        in_specs=[anywhere] * (2 + len(after)),
        out_specs=[anywhere] * 3,
        out_shape=[
            jax.ShapeDtypeStruct((size, rows, width), BF16),
            jax.ShapeDtypeStruct((width, size * rows), BF16),
            jax.ShapeDtypeStruct((width, size * rows), BF16),
        ],
        scratch_shapes=[
            pltpu.VMEM((rows, width), BF16),
            pltpu.VMEM((width, rows), BF16),
            pltpu.SemaphoreType.DMA((2 * size,)),
            pltpu.SemaphoreType.DMA((2 * size,)),
            pltpu.SemaphoreType.DMA((3,)),
        ],
        compiler_params=pltpu.CompilerParams(
            collective_id=collective_id, has_side_effects=True, vmem_limit_bytes=VMEM_LIMIT
        ),
        name="turn_gather",
    )(own, other, *after)


def startup_kernel(
    head_ref, extra_ref, tok_ref, rows_ref, heads_ref, extras_ref, toks_ref, pair_ref,
    head_send, head_recv, extra_send, extra_recv, trade_send, trade_recv, rows_send, rows_recv,
    z_send, z_recv, ay_send, ay_recv, by_send, by_recv, c_send, c_recv, local,
):
    blk, uly = lax.axis_size("blk"), spread(ULY)
    total = spread(ALL)
    z, u, me = lax.axis_index("blk"), lax.axis_index(ULY), lax.axis_index(ALL)
    far = lax.rem(u + 2, uly)
    near = u + 1 - 2 * lax.rem(u, 2)
    half = tok_ref.shape[0] // 2
    parts = (pl.ds(0, half), pl.ds(half, half))

    barrier = pltpu.get_barrier_semaphore()

    def greet(step):
        pl.semaphore_signal(
            barrier, inc=1, device_id=place(ALL, ahead(me, step, total)), device_id_type=MESH
        )

    each(total, greet)
    pl.semaphore_wait(barrier, total - 1)

    def send(src, dst, sent, got, to):
        return pltpu.make_async_remote_copy(
            src_ref=src, dst_ref=dst, send_sem=sent, recv_sem=got, device_id=to, device_id_type=MESH
        )

    def block(step, other, part):
        at = toks_ref.at[ahead(z, step, blk), far if other else u, parts[part]]
        return (tok_ref.at[parts[part]] if step == 0 and not other else at), at

    streams = ((0, 0), (0, 1), (1, 1))

    def hop(stream, up, hops):
        other, part = streams[stream]
        way = 1 if up else -1
        held, to = z - way * hops, z + way
        exists = (held >= 0) & (held < blk) & (to >= 0) & (to < blk)
        held, to = jnp.clip(held, 0, blk - 1), jnp.clip(to, 0, blk - 1)
        at = toks_ref.at[held, far if other else u, parts[part]]
        src = tok_ref.at[parts[part]] if hops == 0 and not other else at
        sem = (2 * stream + up) * blk + hops
        return exists, send(src, at, z_send.at[sem], z_recv.at[sem], {"blk": to})

    def arrival(stream, up, hops):
        other, part = streams[stream]
        way = 1 if up else -1
        held, sender = z - way * (hops + 1), z - way
        exists = (held >= 0) & (held < blk)
        held, sender = jnp.clip(held, 0, blk - 1), jnp.clip(sender, 0, blk - 1)
        at = toks_ref.at[held, far if other else u, parts[part]]
        sem = (2 * stream + up) * blk + hops
        return exists, send(tok_ref.at[parts[part]], at, z_send.at[sem], z_recv.at[sem], {"blk": sender})

    def when(pair, act):
        exists, copy = pair
        pl.when(exists)(lambda: act(copy))

    def a_y(step):
        return send(*block(step, 0, 0), ay_send.at[step], ay_recv.at[step], place(ULY, far))

    def b_y():
        return send(*block(0, 0, 1), by_send.at[0], by_recv.at[0], place(ULY, far))

    def to_near(step, other, part):
        sem = 4 * step + 2 * other + part
        return send(*block(step, other, part), c_send.at[sem], c_recv.at[sem], place(ULY, near))

    group = ("blk", *ULY)
    mine, here, b = lax.axis_index(group), spread(group), lax.axis_index("batch")

    def head(step):
        to = place(group, ahead(mine, step, here))
        src = head_ref.at[(to["y"] * lax.axis_size("core") + to["core"]) * blk + to["blk"]]
        return send(src, heads_ref.at[b, mine], head_send.at[step], head_recv.at[step], to)

    def extra(step):
        to = place(group, ahead(mine, step, here))
        return send(extra_ref, extras_ref.at[b, mine], extra_send.at[step], extra_recv.at[step], to)

    def trade(which):
        ref = (heads_ref, extras_ref)[which].at[b]
        return send(ref, ref, trade_send.at[which], trade_recv.at[which], {"batch": 1 - b})

    batch = lax.axis_size("batch")
    shards = batch * blk
    keeper, number = me // shards, lax.rem(me, shards)

    def rows_to(target):
        to = (target * blk + lax.rem(number, blk)) * uly + keeper
        slot = number // blk
        copy = send(rows_ref, pair_ref.at[slot], rows_send.at[target], rows_recv.at[slot], place(ALL, to))
        return to != me, copy

    def rows_from(slot):
        sender = u * shards + slot * blk + z
        copy = send(rows_ref, pair_ref.at[slot], rows_send.at[slot], rows_recv.at[slot], place(ALL, sender))
        return sender != me, copy

    rows_own = pltpu.make_async_copy(rows_ref, pair_ref.at[number // blk], local.at[3])
    keeps_own = (keeper == u) & (lax.rem(number, blk) == z)
    own = [
        pltpu.make_async_copy(tok_ref, toks_ref.at[z, u], local.at[0]),
        pltpu.make_async_copy(head_ref.at[u * blk + z], heads_ref.at[b, mine], local.at[1]),
        pltpu.make_async_copy(extra_ref, extras_ref.at[b, mine], local.at[2]),
    ]

    def start_head(step):
        extra(step).start()
        head(step).start()

    each(here, start_head)
    ways = (1, 0)
    b_y().start()
    for stream in range(2):
        for up in ways:
            when(hop(stream, up, 0), lambda copy: copy.start())
    a_y(0).start()
    to_near(0, 0, 0).start()
    to_near(0, 0, 1).start()

    for copy in own:
        copy.start()
    for target in range(batch):
        when(rows_to(target), lambda copy: copy.start())
    pl.when(keeps_own)(lambda: rows_own.start())
    b_y().wait_recv()
    for up in ways:
        when(hop(2, up, 0), lambda copy: copy.start())
    to_near(0, 1, 1).start()
    def wait_head(step):
        extra(step).wait()
        head(step).wait()

    for hops in range(1, blk):
        if hops == min(2, blk - 1):
            each(here, wait_head)
            for copy in own[1:]:
                copy.wait()
            trade(0).start()
            trade(1).start()
        for stream, (other, part) in enumerate(streams):
            for up in ways:
                exists, copy = arrival(stream, up, hops - 1)
                step = blk - hops if up else hops

                @pl.when(exists)
                def _(copy=copy, stream=stream, other=other, part=part, up=up, step=step, hops=hops):
                    copy.wait_recv()
                    if hops < blk - 1:
                        when(hop(stream, up, hops), lambda copy: copy.start())
                    if stream == 0:
                        a_y(step).start()
                    to_near(step, other, part).start()

    for step in [0, *reversed(range(1, blk))]:
        a_y(step).wait_recv()
        to_near(step, 1, 0).start()
    for step in range(blk):
        for other in range(2):
            for part in range(2):
                to_near(step, other, part).wait_recv()

    trade(0).wait()
    trade(1).wait()
    for target in range(batch):
        when(rows_from(target), lambda copy: copy.wait_recv())
        when(rows_to(target), lambda copy: copy.wait_send())
    pl.when(keeps_own)(lambda: rows_own.wait())
    own[0].wait()
    b_y().wait_send()
    for hops in range(blk - 1):
        for stream in range(3):
            for up in ways:
                when(hop(stream, up, hops), lambda copy: copy.wait_send())
    for step in range(blk):
        a_y(step).wait_send()
        for other in range(2):
            for part in range(2):
                to_near(step, other, part).wait_send()


def startup(heads, extra, tok, out_rows, collective_id):
    batch, blk, uly = lax.axis_size("batch"), lax.axis_size("blk"), spread(ULY)
    anywhere = pl.BlockSpec(memory_space=pl.ANY)
    dma = pltpu.SemaphoreType.DMA
    return pl.pallas_call(
        startup_kernel,
        in_specs=[anywhere] * 4,
        out_specs=[anywhere] * 4,
        out_shape=[
            jax.ShapeDtypeStruct((batch, blk * uly, *heads.shape[1:]), BF16),
            jax.ShapeDtypeStruct((batch, blk * uly, *extra.shape), BF16),
            jax.ShapeDtypeStruct((blk, uly, *tok.shape), BF16),
            jax.ShapeDtypeStruct((batch, *out_rows.shape), BF16),
        ],
        scratch_shapes=[
            *[dma((blk * uly,))] * 4,
            *[dma((2,))] * 2,
            *[dma((batch,))] * 2,
            *[dma((6 * blk,))] * 2,
            *[dma((blk,))] * 2,
            *[dma((1,))] * 2,
            *[dma((4 * blk,))] * 2,
            dma((4,)),
        ],
        compiler_params=pltpu.CompilerParams(collective_id=collective_id, has_side_effects=True),
        name="startup",
    )(heads, extra, tok, out_rows)


def per_device_general(
    tokens, segments, routes, w_qkv, w_out, attn_gain, ffn_gain, qk_gain, router, w_gate_up, w_down, cotangent
):
    own_tokens = tokens[0]
    own_grad = cotangent[0]
    count_tok, width = own_tokens.shape
    head_dim = qk_gain.shape[1]
    heads = width // head_dim
    uly, blk, batch = spread(ULY), lax.axis_size("blk"), lax.axis_size("batch")
    blk_at, uly_at = lax.axis_index("blk"), lax.axis_index(ULY)
    group = batch * blk
    local_heads = heads // uly
    local_width = local_heads * head_dim
    rows = count_tok * uly
    seg_row = segments[0]
    length = seg_row.shape[0]
    number = router.shape[1]
    local_experts, _, units = w_down.shape
    shard_rows = w_qkv.shape[0]

    extra = jnp.concatenate([attn_gain[:, None], ffn_gain[:, None], router], axis=1)
    extra = jnp.pad(extra, ((0, 0), (0, LANES - extra.shape[1])))
    columns = w_qkv.reshape(shard_rows, 3, uly, local_width).transpose(2, 0, 1, 3)
    packed = jnp.concatenate(
        [
            columns.reshape(uly, shard_rows, 3 * local_width),
            jnp.broadcast_to(extra[None], (uly, shard_rows, LANES)),
        ],
        axis=2,
    )
    packed = swap(packed, ULY).reshape(uly * shard_rows, 3 * local_width + LANES)
    packed = lax.all_gather(packed, ROWS, axis=0, tiled=True)
    own_qkv = packed[:, : 3 * local_width]
    gain_attn = packed[:, 3 * local_width].astype(F32)
    gain_ffn = packed[:, 3 * local_width + 1].astype(F32)
    whole_router = packed[:, 3 * local_width + 2 : 3 * local_width + 2 + number]
    tokens_all = lax.all_gather(own_tokens, ULY, axis=0, tiled=True)
    to_rows = [(u * group + g, g * uly + u) for g in range(group) for u in range(uly)]
    own_out = lax.all_gather(lax.ppermute(w_out, ALL, to_rows), ROWS, axis=0, tiled=True)
    whole_gate_up = lax.all_gather(w_gate_up, PLANE, axis=0, tiled=False)
    whole_down = lax.all_gather(w_down, PLANE, axis=0, tiled=False)
    grad_blk = lax.all_gather(own_grad, "blk", axis=0, tiled=True)
    routes_blk = lax.all_gather(routes[0], "blk", axis=0, tiled=True)

    gain_query = qk_gain[0].astype(F32)
    gain_key = qk_gain[1].astype(F32)
    inputs_all = tokens_all.astype(F32)
    normed_one = inputs_all * rms_scale(inputs_all)
    hidden_one = (normed_one * gain_attn).astype(BF16)
    projected = dot_nn(hidden_one, own_qkv)
    query_raw = projected[:, :local_width].reshape(rows, local_heads, head_dim)
    key_raw = projected[:, local_width : 2 * local_width].reshape(rows, local_heads, head_dim)
    value_raw = projected[:, 2 * local_width :].reshape(rows, local_heads, head_dim)
    cos_table, sin_table = rope_tables(blk_at * rows, rows, head_dim)
    query_scale = rms_scale(query_raw)
    key_scale = rms_scale(key_raw)
    qkv = jnp.concatenate(
        [
            rotate(query_raw * query_scale * gain_query, cos_table, sin_table),
            rotate(key_raw * key_scale * gain_key, cos_table, sin_table),
            value_raw,
        ],
        axis=2,
    ).astype(BF16)
    qkv = qkv.transpose(1, 0, 2)

    by_heads = local_heads % blk == 0
    if by_heads:
        per = local_heads // blk

        def to_heads(values):
            columns = values.shape[2]
            moved = swap(values.reshape(blk, per, rows, columns), "blk")
            return moved.transpose(1, 0, 2, 3).reshape(per, length, columns)

        def to_rows_back(values):
            columns = values.shape[2]
            parts = values.reshape(per, blk, rows, columns).transpose(1, 0, 2, 3)
            return swap(parts, "blk").reshape(local_heads, rows, columns)

        q_src = kv_src = to_heads(qkv)
        cols = (0, 1, 2)
        seg_q = seg_row
        first_head = uly_at * local_heads + blk_at * per
    else:

        def to_heads(values):
            return values

        def to_rows_back(values):
            return values

        q_src = qkv
        kv_src = lax.all_gather(qkv[:, :, head_dim:], "blk", axis=1, tiled=True)
        cols = (0, 0, 1)
        seg_q = lax.dynamic_slice_in_dim(seg_row, blk_at * rows, rows)
        first_head = uly_at * local_heads
    attn_low, attn_f32, lse, top = attention_forward(q_src, kv_src, cols, seg_q, seg_row, head_dim)
    head_vector = lax.dynamic_update_slice_in_dim(
        jnp.full((heads,), NEG, F32), jnp.max(top, axis=(1, 2)) * head_dim**-0.5, first_head, 0
    )
    head_max = lax.pmax(head_vector, ALL)
    attn_rows = to_rows_back(attn_low)
    out_heads = own_out.reshape(local_heads, head_dim, width)
    branch = jnp.einsum("htc,hcd->td", attn_rows, out_heads, preferred_element_type=F32)
    inputs = own_tokens.astype(F32)
    mid = inputs + sum_scatter(branch, ULY)

    scale_two = rms_scale(mid)
    normed_two = mid * scale_two
    hidden_two = (normed_two * gain_ffn).astype(BF16)
    hidden_blk = lax.all_gather(hidden_two, "blk", axis=0, tiled=True)
    probs_blk = jax.nn.softmax(dot_nn(hidden_blk, whole_router), axis=1)
    names = jnp.arange(number, dtype=jnp.int32)
    chosen_blk = jnp.any(routes_blk[:, :, None] == names, axis=1).astype(F32)
    own_names = blk_at * local_experts
    gates = lax.dynamic_slice_in_dim(probs_blk * chosen_blk, own_names, local_experts, axis=1)
    most = min(MOST_TOKENS, hidden_blk.shape[0])
    packed_weights = jnp.concatenate([whole_gate_up, whole_down], axis=3)
    made = []
    for at in range(0, hidden_blk.shape[0], most):
        hidden_part, grad_part = hidden_blk[at : at + most], grad_blk[at : at + most]
        made.append(
            experts(
                hidden_part,
                hidden_part.T,
                grad_part,
                grad_part.T,
                gates[at : at + most],
                [(packed_weights, 0, local_experts)],
            )
        )
    out_part = jnp.concatenate([m[0] for m in made], axis=0)
    dx_part = jnp.concatenate([m[1] for m in made], axis=0)
    dg_part = jnp.concatenate([m[2] for m in made], axis=1)
    expert_grads = sum(m[3].astype(F32) for m in made).astype(BF16)
    expert_sums = lax.psum_scatter(expert_grads, PLANE, scatter_dimension=0, tiled=False).astype(F32)
    grad_gate_up = jnp.concatenate([expert_sums[0], expert_sums[1]], axis=2)
    grad_down = expert_sums[2]
    dg_parts = swap(dg_part.reshape(local_experts, blk, count_tok).transpose(1, 2, 0), "blk")
    grad_gates = dg_parts.transpose(1, 0, 2).reshape(count_tok, number)
    dx_sum = sum_scatter(dx_part, "blk")
    output = (mid + sum_scatter(out_part, "blk")).astype(BF16)
    router_probs = lax.dynamic_slice_in_dim(probs_blk, blk_at * count_tok, count_tok)
    chosen = lax.dynamic_slice_in_dim(chosen_blk, blk_at * count_tok, count_tok)
    grad_probs = chosen * grad_gates
    grad_logits = (
        router_probs * (grad_probs - jnp.sum(router_probs * grad_probs, axis=1, keepdims=True))
    ).astype(BF16)
    grad_hidden_two = dx_sum + dot_nt(grad_logits, whole_router)
    grad_router_part = dot_tn(hidden_two, grad_logits)
    grad_gain_ffn = jnp.sum(grad_hidden_two * normed_two, axis=0)
    grad_mid = own_grad.astype(F32) + norm_back(grad_hidden_two * gain_ffn, mid, scale_two)

    branch_grad = lax.all_gather(grad_mid.astype(BF16), ULY, axis=0, tiled=True)
    grad_attn = dot_nt(branch_grad, own_out).astype(BF16)
    grad_attn = to_heads(grad_attn.reshape(rows, local_heads, head_dim).transpose(1, 0, 2))
    grad_out_part = jnp.einsum("htc,td->hcd", attn_rows, branch_grad, preferred_element_type=F32)
    dq, dk, dv = attention_backward(
        q_src, kv_src, cols, grad_attn, attn_f32, lse, seg_q, seg_row, head_dim
    )
    if by_heads:
        dqkv = to_rows_back(jnp.concatenate([dq, dk, dv], axis=2))
        dq, dk, dv = jnp.split(dqkv, 3, axis=2)
    else:
        dk, dv = (lax.psum_scatter(g, "blk", scatter_dimension=1, tiled=True) for g in (dk, dv))
    dq, dk, dv = (g.transpose(1, 0, 2) for g in (dq, dk, dv))
    grad_query_norm = rotate(dq.astype(F32), cos_table, -sin_table)
    grad_key_norm = rotate(dk.astype(F32), cos_table, -sin_table)
    grad_gain_query = jnp.sum(grad_query_norm * (query_raw * query_scale), axis=(0, 1))
    grad_gain_key = jnp.sum(grad_key_norm * (key_raw * key_scale), axis=(0, 1))
    grad_projected = jnp.concatenate(
        [
            norm_back(grad_query_norm * gain_query, query_raw, query_scale)
            .reshape(rows, local_width)
            .astype(BF16),
            norm_back(grad_key_norm * gain_key, key_raw, key_scale)
            .reshape(rows, local_width)
            .astype(BF16),
            dv.reshape(rows, local_width),
        ],
        axis=1,
    )
    grad_hidden_part = dot_nt(grad_projected, own_qkv)
    grad_hidden_one = sum_scatter(grad_hidden_part, ULY)
    grad_gain_attn = jnp.sum(grad_hidden_part * normed_one, axis=0)
    grad_inputs = grad_mid + norm_back(grad_hidden_one * gain_attn, inputs, rms_scale(inputs))

    grad_qkv_part = dot_tn(hidden_one, grad_projected).astype(BF16)
    grad_qkv_rows = lax.psum_scatter(grad_qkv_part, ROWS, scatter_dimension=0, tiled=True)
    grad_qkv_rows = swap(grad_qkv_rows.reshape(uly, shard_rows, 3 * local_width), ULY)
    grad_qkv = (
        grad_qkv_rows.reshape(uly, shard_rows, 3, local_width)
        .transpose(1, 2, 0, 3)
        .reshape(shard_rows, 3 * width)
        .astype(F32)
    )
    grad_out_rows = lax.psum_scatter(
        grad_out_part.reshape(local_width, width).astype(BF16), ROWS, scatter_dimension=0, tiled=True
    )
    grad_out = lax.ppermute(grad_out_rows, ALL, [(b, a) for a, b in to_rows]).astype(F32)
    small = jnp.concatenate([grad_gain_attn[:, None], grad_gain_ffn[:, None], grad_router_part], axis=1)
    small = lax.psum_scatter(small, ALL, scatter_dimension=0, tiled=True)
    grad_qk_gain = lax.psum(jnp.stack([grad_gain_query, grad_gain_key]), ALL)

    clip_gamma = TAU / jnp.maximum(head_max, TAU)
    factor = jnp.repeat(jnp.sqrt(clip_gamma), head_dim)
    column_scale = jnp.concatenate([factor, factor, jnp.ones((width,), F32)])
    clipped = w_qkv.astype(F32) * column_scale[None, :]
    return (
        output[None],
        grad_inputs[None],
        grad_qkv,
        grad_out,
        small[:, 0],
        small[:, 1],
        grad_qk_gain,
        small[:, 2:],
        grad_gate_up,
        grad_down,
        clipped,
    )


def per_device(
    tokens, segments, routes, w_qkv, w_out, attn_gain, ffn_gain, qk_gain, router, w_gate_up, w_down, cotangent
):
    own_tokens = tokens[0]
    own_grad = cotangent[0]
    count_tok, width = own_tokens.shape
    head_dim = qk_gain.shape[1]
    heads = width // head_dim
    batch, blk, uly = lax.axis_size("batch"), lax.axis_size("blk"), spread(ULY)
    total, group = batch * blk * uly, batch * blk
    local_experts = w_down.shape[0]
    if uly != 4 or heads != blk * uly or blk < 2 or batch != 2 or local_experts % 2:
        return per_device_general(
            tokens, segments, routes, w_qkv, w_out, attn_gain, ffn_gain, qk_gain, router, w_gate_up, w_down, cotangent
        )
    blk_at, uly_at = lax.axis_index("blk"), lax.axis_index(ULY)
    rows = count_tok * uly
    seg_row = segments[0]
    length = seg_row.shape[0]
    number = router.shape[1]
    shard_rows = w_qkv.shape[0]

    to_rows = [(u * group + g, g * uly + u) for g in range(group) for u in range(uly)]


    half = local_experts // 2

    def gather_experts(gate_up, down):
        return lax.all_gather(jnp.concatenate([gate_up, down], axis=2), PLANE, axis=0, tiled=False)

    weights_first = gather_experts(w_gate_up[:half], w_down[:half])
    extra = jnp.concatenate([attn_gain[None], ffn_gain[None], router.T], axis=0)
    kept = extra.shape[0]
    extra = jnp.pad(extra, ((0, -kept % 16), (0, -shard_rows % LANES)))
    by_head = w_qkv.reshape(shard_rows, 3, heads, head_dim).transpose(2, 0, 1, 3)
    own_qkv, extras, toks, pair = startup(
        by_head.reshape(heads, shard_rows, 3 * head_dim), extra, own_tokens, w_out, 0
    )
    extras, later_gate_up, later_down = lax.optimization_barrier((extras, w_gate_up[half:], w_down[half:]))
    weights_second = gather_experts(later_gate_up, later_down)
    own_out = lax.all_to_all(
        jnp.broadcast_to(pair[None], (blk, *pair.shape)), "blk", split_axis=0, concat_axis=0, tiled=True
    )
    own_out = own_out.transpose(1, 0, 2, 3).reshape(blk, head_dim, width)
    own_qkv = own_qkv.reshape(width, 3 * head_dim)
    extras = extras.reshape(total, *extra.shape)[:, :kept, :shard_rows]
    extras = extras.transpose(1, 0, 2).reshape(kept, width)
    gain_attn = extras[0].astype(F32)
    gain_ffn = extras[1].astype(F32)
    router_t = extras[2:]

    gains = qk_gain.astype(F32)
    cos, sin = rope_rows(length, head_dim)
    hidden_one, qkv, raw = project(
        toks.reshape(length, width), gain_attn[None], own_qkv, cos, sin, gains
    )
    attn_low, attn_f32, lse, top = attention_forward(
        qkv[None], qkv[None], (0, 1, 2), seg_row, seg_row, head_dim
    )
    (attn_rows,) = exchange([(attn_low.reshape(blk, rows, head_dim), ("blk",), "swap")], 1)
    branch = jnp.einsum("htc,hcd->td", attn_rows, own_out, preferred_element_type=F32)
    branch, grad_blk, routes_blk = exchange(
        [
            (branch.astype(BF16).reshape(uly, count_tok, width), ULY, "pairsum"),
            (own_grad, ("blk",), "line"),
            (routes[0].T, ("blk",), "gather"),
        ],
        2,
    )
    inputs = own_tokens.astype(F32)
    mid = inputs + branch

    scale_two = rms_scale(mid)
    normed_two = mid * scale_two
    hidden_two = (normed_two * gain_ffn).astype(BF16)
    hidden_blk, hidden_t, grad_t = turn_gather(hidden_two, grad_blk, 3)
    tokens_blk = blk * count_tok
    hidden_blk = hidden_blk.reshape(tokens_blk, width)
    grad_blk = grad_blk.reshape(tokens_blk, width)
    probs_blk = jax.nn.softmax(dot_nt(hidden_blk, router_t), axis=1)
    names = jnp.arange(number, dtype=jnp.int32)
    chosen_blk = jnp.any(routes_blk[:, :, :, None] == names, axis=1).astype(F32)
    chosen_blk = chosen_blk.reshape(tokens_blk, number)
    gates = lax.dynamic_slice_in_dim(
        probs_blk * chosen_blk, blk_at * local_experts, local_experts, axis=1
    )
    shared = (hidden_blk, hidden_t, grad_blk, grad_t)
    out_part, dx_part, dg_first, grads_first = experts(
        *shared, gates[:, :half], [(weights_first, 0, half)]
    )
    sums_first = lax.psum_scatter(grads_first, PLANE, scatter_dimension=0, tiled=False)
    out_part, dx_part, dg_others, grads_others = experts(
        *shared, gates[:, half:], [(weights_second, 0, half)], before=(out_part, dx_part)
    )
    sums_others = lax.psum_scatter(grads_others, PLANE, scatter_dimension=0, tiled=False)
    finished = finish_experts(sums_first, 0, local_experts)
    grad_gate_up, grad_down = finish_experts(sums_others, half, local_experts, before=finished)
    dg_part = jnp.concatenate([dg_first, dg_others], axis=0)
    dg_part = dg_part.reshape(local_experts, blk, count_tok)
    dx_parts, dg_parts = exchange(
        [
            (dx_part.reshape(blk, count_tok, width), ("blk",), "swap"),
            (dg_part.transpose(1, 0, 2), ("blk",), "swap"),
        ],
        4,
    )
    out_part = out_part.reshape(blk, count_tok, width)
    out_part, dx_parts = lax.optimization_barrier((out_part, dx_parts))
    out_parts = lax.all_to_all(out_part, "blk", split_axis=0, concat_axis=0, tiled=True)
    output = (mid + jnp.sum(out_parts.astype(F32), axis=0)).astype(BF16)
    router_probs = lax.dynamic_slice_in_dim(probs_blk, blk_at * count_tok, count_tok)
    chosen = lax.dynamic_slice_in_dim(chosen_blk, blk_at * count_tok, count_tok)
    grad_probs = chosen * dg_parts.reshape(number, count_tok).T
    grad_logits = (
        router_probs * (grad_probs - jnp.sum(router_probs * grad_probs, axis=1, keepdims=True))
    ).astype(BF16)
    grad_hidden_two = jnp.sum(dx_parts.astype(F32), axis=0) + dot_nn(grad_logits, router_t)
    grad_router_t = dot_tn(grad_logits, hidden_two)
    grad_gain_ffn = jnp.sum(grad_hidden_two * normed_two, axis=0)
    grad_mid = own_grad.astype(F32) + norm_back(grad_hidden_two * gain_ffn, mid, scale_two)

    (branch_grad,) = exchange([(grad_mid.astype(BF16), ULY, "relay")], 5)
    branch_grad, sent_qkv = lax.optimization_barrier((branch_grad, own_qkv))
    far_qkv = lax.ppermute(sent_qkv, "y", [(0, 1), (1, 0)])
    branch_grad = branch_grad.reshape(rows, width)
    grad_attn = jnp.einsum("td,hcd->htc", branch_grad, own_out, preferred_element_type=F32).astype(BF16)
    grad_out_part = jnp.einsum("htc,td->hcd", attn_rows, branch_grad, preferred_element_type=F32)
    grad_out_part = grad_out_part.astype(BF16).reshape(batch, blk, shard_rows, width)
    batch_at = lax.axis_index("batch")
    (grad_attn,) = exchange([(grad_attn, ("blk",), "swap")], 6, after=[out_parts])
    grad_out_part, grad_attn = lax.optimization_barrier((grad_out_part, grad_attn))
    grad_out_parts = lax.all_to_all(grad_out_part, "blk", split_axis=1, concat_axis=0, tiled=False)
    grad_out_part = jnp.sum(grad_out_parts.astype(F32), axis=0).astype(BF16)
    grad_projected, grad_gains = project_back(
        qkv, grad_attn.reshape(length, head_dim), attn_f32, lse, seg_row, raw, cos, sin, gains
    )
    grad_qkv_part = dot_tn(hidden_one, grad_projected).astype(BF16)
    by_batch = grad_qkv_part.reshape(batch, width // batch, 3 * head_dim)
    projected_blk, got_qkv_part, near_qkv, cross_qkv, got_out_part = exchange(
        [
            (grad_projected.reshape(blk, uly, count_tok, 3 * head_dim), ULY, "swap1"),
            (
                lax.dynamic_index_in_dim(by_batch, 1 - batch_at, 0, keepdims=False),
                ("batch",),
                "trade",
            ),
            (own_qkv, ("core",), "trade"),
            (far_qkv, ("core",), "trade"),
            (
                lax.dynamic_index_in_dim(grad_out_part, 1 - batch_at, 0, keepdims=False),
                ("batch",),
                "trade",
            ),
        ],
        7,
    )
    grad_out_part = lax.dynamic_index_in_dim(grad_out_part, batch_at, 0, keepdims=False) + got_out_part
    grad_out = lax.ppermute(grad_out_part, ALL, [(b, a) for a, b in to_rows]).astype(F32)
    grad_qkv_part = lax.dynamic_index_in_dim(by_batch, batch_at, 0, keepdims=False) + got_qkv_part

    grad_hidden_part, grad_gain_attn = hidden_back(
        projected_blk.reshape(uly, tokens_blk, 3 * head_dim),
        own_qkv,
        near_qkv,
        far_qkv,
        cross_qkv,
        hidden_one.reshape(blk, uly, count_tok, width),
    )
    grad_gain_attn = grad_gain_attn[0] / gain_attn

    small = jnp.concatenate([grad_gain_attn[None], grad_gain_ffn[None], grad_router_t], axis=0)
    beside = LANES // shard_rows
    small = jnp.pad(small, ((0, -kept % beside), (0, 0))).reshape(-1, beside, total, shard_rows)
    small = small.transpose(2, 0, 1, 3).reshape(total, -1, LANES)
    packed_rows = small.shape[1]
    head_row = jnp.where(
        jnp.arange(LANES) == uly_at * blk + blk_at, jnp.max(top) * head_dim**-0.5, NEG
    )
    to_all = jnp.concatenate([grad_gains, head_row[None]], axis=0)
    small = jnp.concatenate([small, jnp.broadcast_to(to_all[None], (total, 3, LANES))], axis=1)
    small = jnp.pad(small, ((0, 0), (0, -small.shape[1] % 8), (0, 0)))
    grad_hidden_parts, small, grad_qkv_parts = exchange(
        [
            (grad_hidden_part, ("blk",), "swap"),
            (small, ALL, "swap"),
            (grad_qkv_part.reshape(total // batch, shard_rows, 3 * head_dim), ("blk", *ULY), "swap"),
        ],
        8,
    )
    grad_qkv = merge_heads(grad_qkv_parts.reshape(blk, uly, shard_rows, 3 * head_dim))
    grad_hidden_one = jnp.sum(grad_hidden_parts.astype(F32), axis=0)
    grad_inputs = grad_mid + norm_back(grad_hidden_one * gain_attn, inputs, rms_scale(inputs))
    sums = jnp.sum(small, axis=0)
    sums, grad_gains = sums[:packed_rows], sums[packed_rows : packed_rows + 2]
    sums = sums.reshape(packed_rows * beside, shard_rows)[:kept]
    head_max = jnp.max(small[:, packed_rows + 2, :heads], axis=0)
    factor = jnp.repeat(jnp.sqrt(TAU / jnp.maximum(head_max, TAU)), head_dim)
    column_scale = jnp.concatenate([factor, factor, jnp.ones((width,), F32)])
    clipped = w_qkv.astype(F32) * column_scale[None, :]
    return (
        output[None],
        grad_inputs[None],
        grad_qkv,
        grad_out,
        sums[0],
        sums[1],
        grad_gains,
        sums[2:].T,
        grad_gate_up,
        grad_down,
        clipped,
    )


def solution(mesh):
    in_specs = (
        P("batch", ("blk", *ULY), None),
        P("batch", None),
        P("batch", ("blk", *ULY), None),
        P(ALL, None),
        P(ALL, None),
        P(ALL),
        P(ALL),
        P(),
        P(ALL, None),
        P("blk", PLANE, None),
        P("blk", PLANE, None),
        P("batch", ("blk", *ULY), None),
    )
    out_specs = (
        P("batch", ("blk", *ULY), None),
        P("batch", ("blk", *ULY), None),
        P(ALL, None),
        P(ALL, None),
        P(ALL),
        P(ALL),
        P(),
        P(ALL, None),
        P("blk", PLANE, None),
        P("blk", PLANE, None),
        P(ALL, None),
    )
    cores = 2 - mesh.shape["uly"] % 2
    mesh = Mesh(
        mesh.devices.reshape(*(mesh.shape[axis] for axis in ROWS), mesh.shape["uly"] // cores, cores), ALL
    )
    return jax.shard_map(
        per_device, mesh=mesh, in_specs=in_specs, out_specs=out_specs, check_vma=False
    )
```

```python
import functools
import math

import jax
import jax.numpy as jnp
from jax import lax
from jax.experimental import pallas as pl
from jax.experimental.pallas import tpu as pltpu
from jax.sharding import Mesh
from jax.sharding import PartitionSpec as P

EPS = 1e-06
THETA = 50000.0
TAU = 4.0
NEG = -1e30
LOG2E = 1.4426950408889634
LANES = 128
MOST_TOKENS = 512
VMEM_LIMIT = 60 * 1024 * 1024

ULY = ("y", "core")
ALL = ("batch", "blk", *ULY)
ROWS = ("batch", "blk")
PLANE = ("batch", *ULY)
CHIPS = ("batch", "y")

MESH = pl.DeviceIdType.MESH
BF16 = jnp.bfloat16
F32 = jnp.float32


def rms_scale(values):
    return lax.rsqrt(jnp.mean(values * values, axis=-1, keepdims=True) + EPS)


def norm_back(grad_normed, values, scale):
    normed = values * scale
    return scale * (grad_normed - normed * jnp.mean(grad_normed * normed, axis=-1, keepdims=True))


def rope_tables(offset, length, head_dim):
    half_dim = head_dim // 2
    frequency = THETA ** (-jnp.arange(half_dim, dtype=F32) * 2.0 / head_dim)
    positions = (offset + jnp.arange(length, dtype=jnp.int32)).astype(F32)
    angles = positions[:, None] * frequency[None, :]
    return (jnp.cos(angles)[:, None, :], jnp.sin(angles)[:, None, :])


def rope_rows(length, head_dim):
    fine = math.gcd(length, LANES)
    frequency = THETA ** (-jnp.arange(head_dim // 2, dtype=F32) * 2.0 / head_dim)
    frequency = jnp.concatenate([frequency, frequency])
    coarse_angle = (jnp.arange(length // fine, dtype=F32) * fine)[:, None, None] * frequency
    fine_angle = jnp.arange(fine, dtype=F32)[None, :, None] * frequency
    cos_a, sin_a, cos_b, sin_b = lax.optimization_barrier(
        (jnp.cos(coarse_angle), jnp.sin(coarse_angle), jnp.cos(fine_angle), jnp.sin(fine_angle))
    )
    sign = jnp.where(jnp.arange(head_dim) < head_dim // 2, -1.0, 1.0)
    cos = cos_a * cos_b - sin_a * sin_b
    sin = (sin_a * cos_b + cos_a * sin_b) * sign
    return cos.reshape(length, head_dim), sin.reshape(length, head_dim)


def rotate(values, cos_table, sin_table):
    half_dim = values.shape[-1] // 2
    first = values[..., :half_dim]
    second = values[..., half_dim:]
    return jnp.concatenate(
        [first * cos_table - second * sin_table, second * cos_table + first * sin_table], axis=-1
    )


def dot_nn(a, b):
    return lax.dot_general(a, b, (((1,), (0,)), ((), ())), preferred_element_type=F32)


def dot_nt(a, b):
    return lax.dot_general(a, b, (((1,), (1,)), ((), ())), preferred_element_type=F32)


def dot_tn(a, b):
    return lax.dot_general(a, b, (((0,), (0,)), ((), ())), preferred_element_type=F32)


def key_chunks(length):
    size = min(512, length)
    return size, length // size


def attn_fwd_kernel(factor, q_ref, k_ref, v_ref, sq_ref, sk_ref, o_ref, of_ref, lse_ref, top_ref, vt_ref):
    length = k_ref.shape[1]
    size, count = key_chunks(length)
    tile, head_dim = q_ref.shape[1:]

    @pl.when(pl.program_id(1) == 0)
    def _():
        vt_ref[...] = v_ref[0].astype(F32).T.astype(BF16)

    q = q_ref[0]
    seg_q = sq_ref[...]

    def step(j, carried):
        total, top, acc = carried
        at = pl.multiple_of(j * size, size)
        scores = dot_nt(k_ref[0, pl.ds(at, size), :], q)
        scores = jnp.where(sk_ref[pl.ds(at, size), :] == seg_q, scores, NEG)
        top = jnp.maximum(top, jnp.max(scores, axis=0, keepdims=True))
        weights = jnp.exp2(scores * factor)
        total = total + jnp.sum(weights, axis=0, keepdims=True)
        acc = acc + dot_nn(vt_ref[:, pl.ds(at, size)], weights.astype(BF16))
        return total, top, acc

    start = (
        jnp.zeros((1, tile), F32),
        jnp.full((1, tile), NEG, F32),
        jnp.zeros((head_dim, tile), F32),
    )
    total, top, acc = lax.fori_loop(0, count, step, start, unroll=count <= 4)
    out = (acc * (1.0 / total)).T
    o_ref[0] = out.astype(BF16)
    of_ref[0] = out
    lse_ref[0] = jnp.log2(total)
    top_ref[0] = top


def attn_bwd_kernel(
    factor, scale, q_ref, k_ref, v_ref, do_ref, of_ref, lse_ref, sq_ref, sk_ref,
    dq_ref, dk_ref, dv_ref, kt_ref, dk_acc, dv_acc,
):
    length = k_ref.shape[1]
    size, count = key_chunks(length)
    tile, head_dim = q_ref.shape[1:]

    @pl.when(pl.program_id(1) == 0)
    def _():
        kt_ref[...] = k_ref[0].astype(F32).T.astype(BF16)
        dk_acc[...] = jnp.zeros_like(dk_acc)
        dv_acc[...] = jnp.zeros_like(dv_acc)

    q = q_ref[0]
    grad = do_ref[0]
    seg_q = sq_ref[...]
    lse = lse_ref[0]
    row_dot = jnp.sum((grad.astype(F32) * of_ref[0]).T, axis=0, keepdims=True)

    def step(j, dq_t):
        at = pl.multiple_of(j * size, size)
        rows = pl.ds(at, size)
        scores = dot_nt(k_ref[0, rows, :], q)
        scores = jnp.where(sk_ref[rows, :] == seg_q, scores, NEG)
        weights = jnp.exp2(scores * factor - lse)
        grad_weights = dot_nt(v_ref[0, rows, :], grad)
        grad_scores = (weights * (grad_weights - row_dot)).astype(BF16)
        dk_acc[rows, :] += dot_nn(grad_scores, q)
        dv_acc[rows, :] += dot_nn(weights.astype(BF16), grad)
        return dq_t + dot_nn(kt_ref[:, rows], grad_scores)

    dq_t = lax.fori_loop(0, count, step, jnp.zeros((head_dim, tile), F32), unroll=count <= 4)
    dq_ref[0] = (dq_t * scale).T.astype(BF16)

    @pl.when(pl.program_id(1) == pl.num_programs(1) - 1)
    def _():
        dk_ref[0] = (dk_acc[...] * scale).astype(BF16)
        dv_ref[0] = dv_acc[...].astype(BF16)


def attention_tile(queries, length):
    return min(queries, 256 if length <= 4096 else 128)


def attention_forward(q_src, kv_src, cols, seg_q, seg_k, head_dim):
    heads, queries = q_src.shape[:2]
    length = kv_src.shape[1]
    tile = attention_tile(queries, length)
    q_col, k_col, v_col = cols
    factor = head_dim**-0.5 * LOG2E
    row = pl.BlockSpec((1, 1, tile), lambda h, i: (h, 0, i))
    block = pl.BlockSpec((1, tile, head_dim), lambda h, i: (h, i, 0))
    return pl.pallas_call(
        functools.partial(attn_fwd_kernel, factor),
        grid=(heads, queries // tile),
        in_specs=[
            pl.BlockSpec((1, tile, head_dim), lambda h, i: (h, i, q_col)),
            pl.BlockSpec((1, length, head_dim), lambda h, i: (h, 0, k_col)),
            pl.BlockSpec((1, length, head_dim), lambda h, i: (h, 0, v_col)),
            pl.BlockSpec((1, tile), lambda h, i: (0, i)),
            pl.BlockSpec((length, 1), lambda h, i: (0, 0)),
        ],
        out_specs=[block, block, row, row],
        out_shape=[
            jax.ShapeDtypeStruct((heads, queries, head_dim), BF16),
            jax.ShapeDtypeStruct((heads, queries, head_dim), F32),
            jax.ShapeDtypeStruct((heads, 1, queries), F32),
            jax.ShapeDtypeStruct((heads, 1, queries), F32),
        ],
        scratch_shapes=[pltpu.VMEM((head_dim, length), BF16)],
        compiler_params=pltpu.CompilerParams(vmem_limit_bytes=VMEM_LIMIT),
        cost_estimate=pl.CostEstimate(
            flops=4 * heads * queries * length * head_dim,
            bytes_accessed=heads * (queries + length) * head_dim * 8,
            transcendentals=heads * queries * length,
        ),
        name="attend",
    )(q_src, kv_src, kv_src, seg_q.reshape(1, -1), seg_k.reshape(-1, 1))


def attention_backward(q_src, kv_src, cols, grad, out_f32, lse, seg_q, seg_k, head_dim):
    heads, queries = q_src.shape[:2]
    length = kv_src.shape[1]
    tile = attention_tile(queries, length)
    q_col, k_col, v_col = cols
    scale = head_dim**-0.5
    row = pl.BlockSpec((1, 1, tile), lambda h, i: (h, 0, i))
    block = pl.BlockSpec((1, tile, head_dim), lambda h, i: (h, i, 0))
    whole = pl.BlockSpec((1, length, head_dim), lambda h, i: (h, 0, 0))
    return pl.pallas_call(
        functools.partial(attn_bwd_kernel, scale * LOG2E, scale),
        grid=(heads, queries // tile),
        in_specs=[
            pl.BlockSpec((1, tile, head_dim), lambda h, i: (h, i, q_col)),
            pl.BlockSpec((1, length, head_dim), lambda h, i: (h, 0, k_col)),
            pl.BlockSpec((1, length, head_dim), lambda h, i: (h, 0, v_col)),
            block,
            block,
            row,
            pl.BlockSpec((1, tile), lambda h, i: (0, i)),
            pl.BlockSpec((length, 1), lambda h, i: (0, 0)),
        ],
        out_specs=[block, whole, whole],
        out_shape=[
            jax.ShapeDtypeStruct((heads, queries, head_dim), BF16),
            jax.ShapeDtypeStruct((heads, length, head_dim), BF16),
            jax.ShapeDtypeStruct((heads, length, head_dim), BF16),
        ],
        scratch_shapes=[
            pltpu.VMEM((head_dim, length), BF16),
            pltpu.VMEM((length, head_dim), F32),
            pltpu.VMEM((length, head_dim), F32),
        ],
        compiler_params=pltpu.CompilerParams(vmem_limit_bytes=VMEM_LIMIT),
        cost_estimate=pl.CostEstimate(
            flops=10 * heads * queries * length * head_dim,
            bytes_accessed=heads * (queries + length) * head_dim * 12,
            transcendentals=heads * queries * length,
        ),
        name="attend_back",
    )(q_src, kv_src, kv_src, grad, out_f32, lse, seg_q.reshape(1, -1), seg_k.reshape(-1, 1))


def expert_step(expert, h_ref, ht_ref, dy_ref, dyt_ref, gate_ref, wg_ref, wu_ref, wd_ref, dg_ref, out_acc, dx_acc):
    width = h_ref.shape[1]
    cols = wg_ref.shape[3]
    w_gate = wg_ref[...].reshape(width, cols)
    w_up = wu_ref[...].reshape(width, cols)
    w_down = wd_ref[...].reshape(width, cols)
    gates = gate_ref[...]
    mine = lax.broadcasted_iota(jnp.int32, gates.shape, 1) == expert
    gate = jnp.sum(jnp.where(mine, gates, 0.0), axis=1, keepdims=True)
    a_gate = dot_nn(h_ref[...], w_gate)
    a_up = dot_nn(h_ref[...], w_up)
    raw = dot_nn(dy_ref[...], w_down)
    sigma = 1.0 / (1.0 + jnp.exp2(a_gate * -LOG2E))
    swish = a_gate * sigma
    act = swish * a_up
    dg_ref[0] += jnp.sum(raw * act, axis=1, keepdims=True)
    gated = (gate * act).astype(BF16)
    d_act = gate * raw
    d_gate = (d_act * a_up * (sigma + swish * (1.0 - sigma))).astype(BF16)
    d_up = (d_act * swish).astype(BF16)
    out_acc[...] += dot_nt(gated, w_down)
    dx_acc[...] += dot_nt(d_gate, w_gate) + dot_nt(d_up, w_up)
    for part, (left, right) in enumerate([(ht_ref, d_gate), (ht_ref, d_up), (dyt_ref, gated)]):
        yield part, dot_nn(left[...], right).astype(BF16)


def expert_kernel(more, counts, *refs):
    h_ref, ht_ref, dy_ref, dyt_ref, gate_ref = refs[:5]
    sources = [refs[5 + 3 * i : 8 + 3 * i] for i in range(len(counts))]
    out_ref, dx_ref, dg_ref, gr_ref, out_acc, dx_acc = refs[-6:]
    step, last = pl.program_id(0), pl.num_programs(0) - 1
    parts, _, part_rows, cols = sources[0][0].shape
    chunks = (last + 1) // sum(counts)

    @pl.when(step == 0)
    def _():
        if more:
            out0_ref, dx0_ref = refs[-8:-6]
            out_acc[...] = out0_ref[...].astype(F32)
            dx_acc[...] = dx0_ref[...].astype(F32)
        else:
            out_acc[...] = jnp.zeros_like(out_acc)
            dx_acc[...] = jnp.zeros_like(dx_acc)

    @pl.when(step % chunks == 0)
    def _():
        dg_ref[...] = jnp.zeros_like(dg_ref)

    begin = 0
    for source, count in zip(sources, counts):
        end = begin + count * chunks

        @pl.when((step >= begin) & (step < end))
        def _(source=source):
            for part, made in expert_step(
                step // chunks, h_ref, ht_ref, dy_ref, dyt_ref, gate_ref, *source, dg_ref, out_acc, dx_acc
            ):
                gr_ref[:, part, 0] = made.reshape(parts, part_rows, cols)

        begin = end

    @pl.when(step == last)
    def _():
        out_ref[...] = out_acc[...].astype(BF16)
        dx_ref[...] = dx_acc[...].astype(BF16)


def experts(hidden, hidden_t, grad, grad_t, gates, sources, before=()):
    tokens, width = hidden.shape
    parts, _, part_rows, units = sources[0][0].shape
    units = units // 3
    counts = [count for _, _, count in sources]
    total = sum(counts)
    cols = min(256, units)
    chunks = units // cols
    once = pl.Buffered(1)
    whole = pl.BlockSpec((tokens, width), lambda s: (0, 0), pipeline_mode=once)
    whole_t = pl.BlockSpec((width, tokens), lambda s: (0, 0), pipeline_mode=once)
    result = pl.BlockSpec((tokens, width), lambda s: (0, 0))

    def weight(source, kind):
        _, first, count = sources[source]
        begin = sum(counts[:source]) * chunks

        def index(step):
            at = jnp.clip(step - begin, 0, count * chunks - 1)
            return (0, first + at // chunks, 0, kind * chunks + at % chunks)

        return pl.BlockSpec((parts, 1, part_rows, cols), index)

    return pl.pallas_call(
        functools.partial(expert_kernel, bool(before), counts),
        grid=(total * chunks,),
        in_specs=[
            whole,
            whole_t,
            whole,
            whole_t,
            pl.BlockSpec(gates.shape, lambda s: (0, 0), pipeline_mode=once),
            *[weight(source, kind) for source in range(len(sources)) for kind in range(3)],
            *[whole for _ in before],
        ],
        out_specs=[
            result,
            result,
            pl.BlockSpec((1, tokens, 1), lambda s: (s // chunks, 0, 0)),
            pl.BlockSpec((parts, 3, 1, part_rows, cols), lambda s: (0, 0, s // chunks, 0, s % chunks)),
        ],
        out_shape=[
            jax.ShapeDtypeStruct((tokens, width), BF16),
            jax.ShapeDtypeStruct((tokens, width), BF16),
            jax.ShapeDtypeStruct((total, tokens, 1), F32),
            jax.ShapeDtypeStruct((parts, 3, total, part_rows, units), BF16),
        ],
        scratch_shapes=[
            pltpu.VMEM((tokens, width), F32),
            pltpu.VMEM((tokens, width), F32),
        ],
        compiler_params=pltpu.CompilerParams(vmem_limit_bytes=VMEM_LIMIT),
        cost_estimate=pl.CostEstimate(
            flops=18 * total * tokens * width * units,
            bytes_accessed=12 * total * width * units,
            transcendentals=total * tokens * units,
        ),
        name="experts",
    )(hidden, hidden_t, grad, grad_t, gates, *[array for array, _, _ in sources for _ in range(3)], *before)


def finish_experts_kernel(sums_ref, *refs):
    gate_up_ref, down_ref = refs[-2:]
    units = down_ref.shape[2]
    gate_up_ref[0, :, :units] = sums_ref[0, 0].astype(F32)
    gate_up_ref[0, :, units:] = sums_ref[1, 0].astype(F32)
    down_ref[0] = sums_ref[2, 0].astype(F32)


def finish_experts(sums, at, total, before=()):
    _, count, rows, units = sums.shape
    tile = min(128, rows)
    return pl.pallas_call(
        finish_experts_kernel,
        grid=(count, rows // tile),
        in_specs=[
            pl.BlockSpec((3, 1, tile, units), lambda e, r: (0, e, r, 0)),
            *[pl.BlockSpec(memory_space=pl.ANY) for _ in before],
        ],
        out_specs=[
            pl.BlockSpec((1, tile, 2 * units), lambda e, r: (at + e, r, 0)),
            pl.BlockSpec((1, tile, units), lambda e, r: (at + e, r, 0)),
        ],
        out_shape=[
            jax.ShapeDtypeStruct((total, rows, 2 * units), F32),
            jax.ShapeDtypeStruct((total, rows, units), F32),
        ],
        input_output_aliases={1 + i: i for i in range(len(before))},
        compiler_params=pltpu.CompilerParams(vmem_limit_bytes=VMEM_LIMIT),
        name="finish_experts",
    )(sums, *before)


def turn(values, cos, sin):
    return values * cos + pltpu.roll(values, values.shape[1] // 2, 1) * sin


def project_kernel(
    tok_ref, gain_ref, w_ref, cos_ref, sin_ref, gains_ref, hidden_ref, qkv_ref, raw_ref
):
    head_dim = cos_ref.shape[1]
    values = tok_ref[...].astype(F32)
    hidden = (values * rms_scale(values) * gain_ref[...]).astype(BF16)
    hidden_ref[...] = hidden
    projected = dot_nn(hidden, w_ref[...])
    raw_ref[...] = projected[:, : 2 * head_dim]
    for part in range(2):
        at = slice(part * head_dim, (part + 1) * head_dim)
        raw = projected[:, at]
        normed = raw * rms_scale(raw) * gains_ref[part : part + 1, :]
        qkv_ref[:, at] = turn(normed, cos_ref[...], sin_ref[...]).astype(BF16)
    qkv_ref[:, 2 * head_dim :] = projected[:, 2 * head_dim :].astype(BF16)


def project(toks, gain, weights, cos, sin, gains):
    length, width = toks.shape
    head_dim = cos.shape[1]
    tile = min(256, length)

    def rows(columns):
        return pl.BlockSpec((tile, columns), lambda i: (i, 0))

    def fixed(shape):
        return pl.BlockSpec(shape, lambda i: (0, 0))

    return pl.pallas_call(
        project_kernel,
        grid=(length // tile,),
        in_specs=[
            rows(width),
            fixed((1, width)),
            fixed(weights.shape),
            rows(head_dim),
            rows(head_dim),
            fixed(gains.shape),
        ],
        out_specs=[rows(width), rows(3 * head_dim), rows(2 * head_dim)],
        out_shape=[
            jax.ShapeDtypeStruct((length, width), BF16),
            jax.ShapeDtypeStruct((length, 3 * head_dim), BF16),
            jax.ShapeDtypeStruct((length, 2 * head_dim), F32),
        ],
        compiler_params=pltpu.CompilerParams(vmem_limit_bytes=VMEM_LIMIT),
        name="project",
    )(toks, gain, weights, cos, sin, gains)


def project_back_kernel(
    factor, scale, q_ref, k_ref, v_ref, do_ref, of_ref, lse_ref, sq_ref, sk_ref,
    raw_q_ref, raw_k_ref, cos_q_ref, sin_q_ref, cos_ref, sin_ref, gains_ref,
    dp_ref, dgain_ref, kt_ref, dk_acc, dv_acc,
):
    length, head_dim = k_ref.shape
    size, count = key_chunks(length)
    tile = q_ref.shape[0]
    step_at = pl.program_id(0)

    @pl.when(step_at == 0)
    def _():
        kt_ref[...] = k_ref[...].astype(F32).T.astype(BF16)
        dk_acc[...] = jnp.zeros_like(dk_acc)
        dv_acc[...] = jnp.zeros_like(dv_acc)
        dgain_ref[...] = jnp.zeros_like(dgain_ref)

    def to_raw(part, grad, raw, cos, sin):
        grad = turn(grad.astype(BF16).astype(F32), cos, -sin)
        raw_scale = rms_scale(raw)
        dgain_ref[part : part + 1, :] += jnp.sum(grad * (raw * raw_scale), axis=0, keepdims=True)
        return norm_back(grad * gains_ref[part : part + 1, :], raw, raw_scale).astype(BF16)

    q = q_ref[...]
    grad = do_ref[...]
    seg_q = sq_ref[...]
    lse = lse_ref[0]
    row_dot = jnp.sum((grad.astype(F32) * of_ref[0]).T, axis=0, keepdims=True)
    dq_t = jnp.zeros((head_dim, tile), F32)
    for j in range(count):
        rows = slice(j * size, (j + 1) * size)
        scores = dot_nt(k_ref[rows, :], q)
        scores = jnp.where(sk_ref[rows, :] == seg_q, scores, NEG)
        weights = jnp.exp2(scores * factor - lse)
        grad_weights = dot_nt(v_ref[rows, :], grad)
        grad_scores = (weights * (grad_weights - row_dot)).astype(BF16)
        dk_acc[rows, :] += dot_nn(grad_scores, q)
        dv_acc[rows, :] += dot_nn(weights.astype(BF16), grad)
        dq_t = dq_t + dot_nn(kt_ref[:, rows], grad_scores)
    own = pl.ds(pl.multiple_of(step_at * tile, tile), tile)
    dp_ref[own, :head_dim] = to_raw(
        0, (dq_t * scale).T, raw_q_ref[...], cos_q_ref[...], sin_q_ref[...]
    )

    @pl.when(step_at == pl.num_programs(0) - 1)
    def _():
        dp_ref[:, head_dim : 2 * head_dim] = to_raw(
            1, dk_acc[...] * scale, raw_k_ref[...], cos_ref[...], sin_ref[...]
        )
        dp_ref[:, 2 * head_dim :] = dv_acc[...].astype(BF16)


def project_back(qkv, grad, out_f32, lse, segments, raw, cos, sin, gains):
    length, head_dim = grad.shape
    tile = min(256, length)

    def rows(column):
        return pl.BlockSpec((tile, head_dim), lambda i: (i, column))

    def whole(column):
        return pl.BlockSpec((length, head_dim), lambda i: (0, column))

    return pl.pallas_call(
        functools.partial(project_back_kernel, head_dim**-0.5 * LOG2E, head_dim**-0.5),
        grid=(length // tile,),
        in_specs=[
            rows(0),
            whole(1),
            whole(2),
            rows(0),
            pl.BlockSpec((1, tile, head_dim), lambda i: (0, i, 0)),
            pl.BlockSpec((1, 1, tile), lambda i: (0, 0, i)),
            pl.BlockSpec((1, tile), lambda i: (0, i)),
            pl.BlockSpec((length, 1), lambda i: (0, 0)),
            rows(0),
            whole(1),
            rows(0),
            rows(0),
            whole(0),
            whole(0),
            pl.BlockSpec(gains.shape, lambda i: (0, 0)),
        ],
        out_specs=[
            pl.BlockSpec((length, 3 * head_dim), lambda i: (0, 0)),
            pl.BlockSpec((2, head_dim), lambda i: (0, 0)),
        ],
        out_shape=[
            jax.ShapeDtypeStruct((length, 3 * head_dim), BF16),
            jax.ShapeDtypeStruct((2, head_dim), F32),
        ],
        scratch_shapes=[
            pltpu.VMEM((head_dim, length), BF16),
            pltpu.VMEM((length, head_dim), F32),
            pltpu.VMEM((length, head_dim), F32),
        ],
        compiler_params=pltpu.CompilerParams(vmem_limit_bytes=VMEM_LIMIT),
        cost_estimate=pl.CostEstimate(
            flops=10 * length * length * head_dim,
            bytes_accessed=length * head_dim * 40,
            transcendentals=length * length,
        ),
        name="project_back",
    )(
        qkv, qkv, qkv, grad, out_f32, lse, segments.reshape(1, -1), segments.reshape(-1, 1),
        raw, raw, cos, sin, cos, sin, gains,
    )


def hidden_back_kernel(grads_ref, own_ref, near_ref, far_ref, cross_ref, hidden_ref, out_ref, gain_ref):
    uly = grads_ref.shape[0]
    u = lax.axis_index(ULY)
    near = u + 1 - 2 * lax.rem(u, 2)
    total = dot_nt(grads_ref[u], own_ref[...])
    total = total + dot_nt(grads_ref[near], near_ref[...])
    total = total + dot_nt(grads_ref[lax.rem(u + 2, uly)], far_ref[...])
    total = total + dot_nt(grads_ref[lax.rem(near + 2, uly)], cross_ref[...])
    out_ref[...] = total.astype(BF16).reshape(out_ref.shape)
    hidden = hidden_ref[...].reshape(total.shape).astype(F32)
    gain_ref[...] = jnp.sum(total * hidden, axis=0, keepdims=True)


def hidden_back(grads, own, near, far, cross, hidden):
    uly, tokens, columns = grads.shape
    blk, _, rows, width = hidden.shape
    tile = min(512, width)
    weights = pl.BlockSpec((tile, columns), lambda n: (n, 0))
    return pl.pallas_call(
        hidden_back_kernel,
        grid=(width // tile,),
        in_specs=[
            pl.BlockSpec(grads.shape, lambda n: (0, 0, 0)),
            *[weights] * 4,
            pl.BlockSpec((blk, 1, rows, tile), lambda n: (0, lax.axis_index(ULY), 0, n)),
        ],
        out_specs=[
            pl.BlockSpec((blk, rows, tile), lambda n: (0, 0, n)),
            pl.BlockSpec((1, tile), lambda n: (0, n)),
        ],
        out_shape=[
            jax.ShapeDtypeStruct((blk, rows, width), BF16),
            jax.ShapeDtypeStruct((1, width), F32),
        ],
        compiler_params=pltpu.CompilerParams(vmem_limit_bytes=VMEM_LIMIT),
        name="hidden_back",
    )(grads, own, near, far, cross, hidden)


def merge_heads_kernel(parts_ref, out_ref):
    blk, uly, _, columns = parts_ref.shape
    head_dim = columns // 3
    heads = blk * uly
    for z in range(blk):
        for u in range(uly):
            head = parts_ref[z, u].astype(F32)
            for part in range(3):
                at = (part * heads + u * blk + z) * head_dim
                out_ref[:, at : at + head_dim] = head[:, part * head_dim : (part + 1) * head_dim]


def merge_heads(parts):
    blk, uly, rows, columns = parts.shape
    return pl.pallas_call(
        merge_heads_kernel,
        out_shape=jax.ShapeDtypeStruct((rows, blk * uly * columns), F32),
        compiler_params=pltpu.CompilerParams(vmem_limit_bytes=VMEM_LIMIT),
        name="merge_heads",
    )(parts)


def swap(values, axis):
    return lax.all_to_all(values, axis, split_axis=0, concat_axis=0, tiled=True)


def sum_scatter(values, axis):
    count = spread(axis) if isinstance(axis, tuple) else lax.axis_size(axis)
    rows, width = values.shape
    parts = swap(values.astype(BF16).reshape(count, rows // count, width), axis)
    return jnp.sum(parts.astype(F32), axis=0)


def place(axes, index):
    found = {}
    for axis in reversed(axes):
        size = lax.axis_size(axis)
        found[axis] = lax.rem(index, size)
        index = index // size
    return found


def spread(axes):
    return math.prod(lax.axis_size(axis) for axis in axes)


def each(count, body):
    if count <= 4:
        for step in range(1, count):
            body(step)
    else:

        def looped(step, carried):
            body(step)
            return carried

        lax.fori_loop(1, count, looped, 0)


def ahead(index, step, size):
    return lax.rem(index + step, size)


def exchange(items, collective_id, after=()):
    count = len(items)
    sizes = [spread(axes) for _, axes, _ in items]
    groups = list(dict.fromkeys(axes for _, axes, _ in items))
    bases = [sum(2 * size for size in sizes[:i]) for i in range(count)]

    def kernel(*refs):
        ins = refs[:count]
        outs = refs[count + len(after) : 2 * count + len(after)]
        send, recv, local = refs[2 * count + len(after) :][:3]
        barrier = pltpu.get_barrier_semaphore()
        for axes in groups:
            size, me = spread(axes), lax.axis_index(axes)

            def greet(step, axes=axes, size=size, me=me):
                pl.semaphore_signal(
                    barrier, inc=1, device_id=place(axes, ahead(me, step, size)), device_id_type=MESH
                )

            each(size, greet)
        pl.semaphore_wait(barrier, sum(spread(axes) - 1 for axes in groups))

        def block(i, peer):
            if items[i][2] == "swap":
                return ins[i].at[peer]
            return ins[i].at[:, peer] if items[i][2] == "swap1" else ins[i]

        def remote(i, step):
            _, axes, kind = items[i]
            me = lax.axis_index(axes)
            if kind == "trade":
                return pltpu.make_async_remote_copy(
                    src_ref=ins[i],
                    dst_ref=outs[i],
                    send_sem=send.at[bases[i] + 1],
                    recv_sem=recv.at[bases[i] + 1],
                    device_id=place(axes, 1 - me),
                    device_id_type=MESH,
                )
            if kind == "relay":
                far, near = lax.rem(me + 2, 4), me + 1 - 2 * lax.rem(me, 2)
                held = far if step == 3 else me
                return pltpu.make_async_remote_copy(
                    src_ref=outs[i].at[far] if step == 3 else ins[i],
                    dst_ref=outs[i].at[held],
                    send_sem=send.at[bases[i] + step],
                    recv_sem=recv.at[bases[i] + step],
                    device_id=place(axes, far if step == 1 else near),
                    device_id_type=MESH,
                )
            peer = ahead(me, step, sizes[i])
            return pltpu.make_async_remote_copy(
                src_ref=block(i, peer),
                dst_ref=outs[i].at[me],
                send_sem=send.at[bases[i] + step],
                recv_sem=recv.at[bases[i] + step],
                device_id=place(axes, peer),
                device_id_type=MESH,
            )

        def own(i):
            _, axes, kind = items[i]
            me = lax.axis_index(axes)
            return pltpu.make_async_copy(
                block(i, me), outs[i].at[me], local.at[i]
            )

        def hop(i, up, hops):
            (axis,) = items[i][1]
            me, size = lax.axis_index(axis), sizes[i]
            way = 1 if up else -1
            held, to = me - way * hops, me + way
            exists = (held >= 0) & (held < size) & (to >= 0) & (to < size)
            held, to = jnp.clip(held, 0, size - 1), jnp.clip(to, 0, size - 1)
            sem = bases[i] + (size if up else 0) + hops
            copy = pltpu.make_async_remote_copy(
                src_ref=outs[i].at[held] if hops else ins[i],
                dst_ref=outs[i].at[held],
                send_sem=send.at[sem],
                recv_sem=recv.at[sem],
                device_id={axis: to},
                device_id_type=MESH,
            )
            return exists, copy

        def arrival(i, up, hops):
            (axis,) = items[i][1]
            me, size = lax.axis_index(axis), sizes[i]
            way = 1 if up else -1
            held, sender = me - way * (hops + 1), me - way
            exists = (held >= 0) & (held < size)
            held, sender = jnp.clip(held, 0, size - 1), jnp.clip(sender, 0, size - 1)
            sem = bases[i] + (size if up else 0) + hops
            copy = pltpu.make_async_remote_copy(
                src_ref=ins[i],
                dst_ref=outs[i].at[held],
                send_sem=send.at[sem],
                recv_sem=recv.at[sem],
                device_id={axis: sender},
                device_id_type=MESH,
            )
            return exists, copy

        def kinds(*names):
            return [i for i in range(count) if items[i][2] in names]

        def when(pair, act):
            exists, copy = pair
            pl.when(exists)(lambda: act(copy))

        def pairsum(i):
            me = lax.axis_index(ULY)
            far, near = lax.rem(me + 2, 4), me + 1 - 2 * lax.rem(me, 2)
            own, out = ins[i], outs[i]
            got_near, got_far, sent = refs[2 * count + len(after) + 3 :]

            def copy(at, src, dst, to):
                return pltpu.make_async_remote_copy(
                    src_ref=src,
                    dst_ref=dst,
                    send_sem=send.at[bases[i] + at],
                    recv_sem=recv.at[bases[i] + at],
                    device_id=place(ULY, to),
                    device_id_type=MESH,
                )

            to_near = [
                copy(0, own.at[near], got_near.at[0], near),
                copy(1, own.at[lax.rem(near + 2, 4)], got_near.at[1], near),
            ]
            to_far = copy(2, sent, got_far, far)

            def first():
                for sending in to_near:
                    sending.start()

            def second():
                for sending in to_near:
                    sending.wait()
                sent[...] = (own[far].astype(F32) + got_near[1].astype(F32)).astype(BF16)
                to_far.start()
                out[...] = own[me].astype(F32) + got_near[0].astype(F32)

            def third():
                to_far.wait()
                out[...] += got_far[...].astype(F32)

            return first, second, third

        def deals(i):
            batch, blk, uly = lax.axis_size("batch"), lax.axis_size("blk"), spread(ULY)
            b, z, u, me = lax.axis_index("batch"), lax.axis_index("blk"), lax.axis_index(ULY), lax.axis_index(ALL)
            shards = batch * blk

            def copy(part, slot, other):
                return other != me, pltpu.make_async_remote_copy(
                    src_ref=ins[i].at[part],
                    dst_ref=outs[i].at[slot],
                    send_sem=send.at[bases[i] + part],
                    recv_sem=recv.at[bases[i] + slot],
                    device_id=place(ALL, other),
                    device_id_type=MESH,
                )

            sent = [copy(part, b, u * shards + part * blk + z) for part in range(batch)]
            keeper, number = me // shards, lax.rem(me, shards)
            got = [
                copy(slot, slot, (slot * blk + lax.rem(number, blk)) * uly + keeper) for slot in range(batch)
            ]
            stays = (keeper == u) & (lax.rem(number, blk) == z)
            kept = pltpu.make_async_copy(ins[i].at[number // blk], outs[i].at[b], local.at[i])
            return sent, got, (stays, kept)

        ways = (True, False)
        dealt = [deals(i) for i in kinds("deal")]
        for sent, _, kept in dealt:
            for pair in (*sent, kept):
                when(pair, lambda copy: copy.start())
        sums = [pairsum(i) for i in kinds("pairsum")]
        for first, _, _ in sums:
            first()
        for i in kinds("line"):
            for up in ways:
                when(hop(i, up, 0), lambda copy: copy.start())
        for i in kinds("gather", "swap", "swap1", "relay", "trade"):
            each(3 if items[i][2] == "relay" else sizes[i], lambda step, i=i: remote(i, step).start())
        for i in kinds("gather", "swap", "swap1", "relay", "line"):
            own(i).start()
        for _, second, _ in sums:
            second()
        for i in kinds("line"):
            for hops in range(1, sizes[i]):
                for up in ways:
                    when(arrival(i, up, hops - 1), lambda copy: copy.wait_recv())
                    if hops < sizes[i] - 1:
                        when(hop(i, up, hops), lambda copy: copy.start())
        for i in kinds("relay"):
            remote(i, 1).wait_recv()
            remote(i, 3).start()
            remote(i, 1).wait_send()
            for step in (2, 3):
                remote(i, step).wait()
        for i in kinds("gather", "swap", "swap1", "trade"):
            each(sizes[i], lambda step, i=i: remote(i, step).wait())
        for i in kinds("line"):
            for hops in range(sizes[i] - 1):
                for up in ways:
                    when(hop(i, up, hops), lambda copy: copy.wait_send())
        for i in kinds("gather", "swap", "swap1", "relay", "line"):
            own(i).wait()
        for sent, got, kept in dealt:
            for pair in got:
                when(pair, lambda copy: copy.wait_recv())
            for pair in sent:
                when(pair, lambda copy: copy.wait_send())
            when(kept, lambda copy: copy.wait())
        for _, _, third in sums:
            third()


    def shape_of(size, array, kind):
        if kind in ("trade", "pairsum", "deal"):
            return array.shape[kind == "pairsum" :]
        dropped = {"swap": 0, "swap1": 1}.get(kind)
        return (size, *(extent for at, extent in enumerate(array.shape) if at != dropped))

    anywhere, close = pl.BlockSpec(memory_space=pl.ANY), pl.BlockSpec(memory_space=pltpu.VMEM)
    specs = [close if kind == "pairsum" else anywhere for _, _, kind in items]
    held = []
    for array, _, kind in items:
        if kind == "pairsum":
            held = [pltpu.VMEM((*more, *array.shape[1:]), BF16) for more in ((2,), (), ())]
    return pl.pallas_call(
        kernel,
        in_specs=specs + [anywhere] * len(after),
        out_specs=specs,
        out_shape=[
            jax.ShapeDtypeStruct(shape_of(size, array, kind), F32 if kind == "pairsum" else array.dtype)
            for size, (array, _, kind) in zip(sizes, items)
        ],
        scratch_shapes=[
            pltpu.SemaphoreType.DMA((2 * sum(sizes),)),
            pltpu.SemaphoreType.DMA((2 * sum(sizes),)),
            pltpu.SemaphoreType.DMA((count,)),
            *held,
        ],
        compiler_params=pltpu.CompilerParams(
            collective_id=collective_id, has_side_effects=True, vmem_limit_bytes=VMEM_LIMIT if held else None
        ),
        name="exchange",
    )(*[item[0] for item in items], *after)


def turn_gather_kernel(
    own_ref, other_ref, all_ref, all_t_ref, other_t_ref, block, turned, send, recv, local
):
    size, me = lax.axis_size("blk"), lax.axis_index("blk")
    rows = own_ref.shape[0]
    barrier = pltpu.get_barrier_semaphore()
    ways = (1, 0)

    def neighbour(up):
        to = me + (1 if up else -1)
        return (to >= 0) & (to < size), jnp.clip(to, 0, size - 1)

    def greet(step):
        pl.semaphore_signal(
            barrier, inc=1, device_id={"blk": ahead(me, step, size)}, device_id_type=MESH
        )

    each(size, greet)
    pl.semaphore_wait(barrier, size - 1)

    def hop(up, hops):
        held = me - (1 if up else -1) * hops
        exists, to = neighbour(up)
        exists = exists & (held >= 0) & (held < size)
        held = jnp.clip(held, 0, size - 1)
        return exists, pltpu.make_async_remote_copy(
            src_ref=all_ref.at[held] if hops else own_ref,
            dst_ref=all_ref.at[held],
            send_sem=send.at[up * size + hops],
            recv_sem=recv.at[up * size + hops],
            device_id={"blk": to},
            device_id_type=MESH,
        )

    def arrival(up, hops):
        held = me - (1 if up else -1) * (hops + 1)
        exists = (held >= 0) & (held < size)
        held = jnp.clip(held, 0, size - 1)
        return exists, held, pltpu.make_async_remote_copy(
            src_ref=own_ref,
            dst_ref=all_ref.at[held],
            send_sem=send.at[up * size + hops],
            recv_sem=recv.at[up * size + hops],
            device_id={"blk": neighbour(1 - up)[1]},
            device_id_type=MESH,
        )

    def when(pair, act):
        exists, copy = pair
        pl.when(exists)(lambda: act(copy))

    def turn(src, dst, at):
        take = pltpu.make_async_copy(src, block, local.at[0])
        take.start()
        take.wait()
        turned[...] = block[...].T
        columns = pl.ds(pl.multiple_of(at * rows, rows), rows)
        give = pltpu.make_async_copy(turned, dst.at[:, columns], local.at[1])
        give.start()
        give.wait()

    for up in ways:
        when(hop(up, 0), lambda copy: copy.start())
    keep = pltpu.make_async_copy(own_ref, all_ref.at[me], local.at[2])
    keep.start()
    turn(own_ref, all_t_ref, me)
    for at in range(size):
        turn(other_ref.at[at], other_t_ref, at)
    for hops in range(1, size):
        for up in ways:
            exists, held, copy = arrival(up, hops - 1)

            @pl.when(exists)
            def _(copy=copy, up=up, hops=hops):
                copy.wait_recv()
                if hops < size - 1:
                    when(hop(up, hops), lambda copy: copy.start())

        for up in ways:
            exists, held, copy = arrival(up, hops - 1)
            pl.when(exists)(lambda held=held: turn(all_ref.at[held], all_t_ref, held))
    for hops in range(size - 1):
        for up in ways:
            when(hop(up, hops), lambda copy: copy.wait_send())
    keep.wait()


def turn_gather(own, other, collective_id, after=()):
    size = lax.axis_size("blk")
    rows, width = own.shape
    anywhere = pl.BlockSpec(memory_space=pl.ANY)

    def kernel(*refs):
        turn_gather_kernel(*refs[:2], *refs[2 + len(after) :])

    return pl.pallas_call(
        kernel,
        in_specs=[anywhere] * (2 + len(after)),
        out_specs=[anywhere] * 3,
        out_shape=[
            jax.ShapeDtypeStruct((size, rows, width), BF16),
            jax.ShapeDtypeStruct((width, size * rows), BF16),
            jax.ShapeDtypeStruct((width, size * rows), BF16),
        ],
        scratch_shapes=[
            pltpu.VMEM((rows, width), BF16),
            pltpu.VMEM((width, rows), BF16),
            pltpu.SemaphoreType.DMA((2 * size,)),
            pltpu.SemaphoreType.DMA((2 * size,)),
            pltpu.SemaphoreType.DMA((3,)),
        ],
        compiler_params=pltpu.CompilerParams(
            collective_id=collective_id, has_side_effects=True, vmem_limit_bytes=VMEM_LIMIT
        ),
        name="turn_gather",
    )(own, other, *after)


def startup_kernel(
    head_ref, extra_ref, tok_ref, heads_ref, extras_ref, toks_ref,
    head_send, head_recv, extra_send, extra_recv, trade_send, trade_recv,
    z_send, z_recv, ay_send, ay_recv, by_send, by_recv, c_send, c_recv, local,
):
    blk, uly = lax.axis_size("blk"), spread(ULY)
    total = spread(ALL)
    z, u, me = lax.axis_index("blk"), lax.axis_index(ULY), lax.axis_index(ALL)
    far = lax.rem(u + 2, uly)
    near = u + 1 - 2 * lax.rem(u, 2)
    half = tok_ref.shape[0] // 2
    parts = (pl.ds(0, half), pl.ds(half, half))

    barrier = pltpu.get_barrier_semaphore()

    def greet(step):
        pl.semaphore_signal(
            barrier, inc=1, device_id=place(ALL, ahead(me, step, total)), device_id_type=MESH
        )

    each(total, greet)
    pl.semaphore_wait(barrier, total - 1)

    def send(src, dst, sent, got, to):
        return pltpu.make_async_remote_copy(
            src_ref=src, dst_ref=dst, send_sem=sent, recv_sem=got, device_id=to, device_id_type=MESH
        )

    def block(step, other, part):
        at = toks_ref.at[ahead(z, step, blk), far if other else u, parts[part]]
        return (tok_ref.at[parts[part]] if step == 0 and not other else at), at

    streams = ((0, 0), (0, 1), (1, 1))

    def hop(stream, up, hops):
        other, part = streams[stream]
        way = 1 if up else -1
        held, to = z - way * hops, z + way
        exists = (held >= 0) & (held < blk) & (to >= 0) & (to < blk)
        held, to = jnp.clip(held, 0, blk - 1), jnp.clip(to, 0, blk - 1)
        at = toks_ref.at[held, far if other else u, parts[part]]
        src = tok_ref.at[parts[part]] if hops == 0 and not other else at
        sem = (2 * stream + up) * blk + hops
        return exists, send(src, at, z_send.at[sem], z_recv.at[sem], {"blk": to})

    def arrival(stream, up, hops):
        other, part = streams[stream]
        way = 1 if up else -1
        held, sender = z - way * (hops + 1), z - way
        exists = (held >= 0) & (held < blk)
        held, sender = jnp.clip(held, 0, blk - 1), jnp.clip(sender, 0, blk - 1)
        at = toks_ref.at[held, far if other else u, parts[part]]
        sem = (2 * stream + up) * blk + hops
        return exists, send(tok_ref.at[parts[part]], at, z_send.at[sem], z_recv.at[sem], {"blk": sender})

    def when(pair, act):
        exists, copy = pair
        pl.when(exists)(lambda: act(copy))

    def a_y(step):
        return send(*block(step, 0, 0), ay_send.at[step], ay_recv.at[step], place(ULY, far))

    def b_y():
        return send(*block(0, 0, 1), by_send.at[0], by_recv.at[0], place(ULY, far))

    def to_near(step, other, part):
        sem = 4 * step + 2 * other + part
        return send(*block(step, other, part), c_send.at[sem], c_recv.at[sem], place(ULY, near))

    group = ("blk", *ULY)
    mine, here, b = lax.axis_index(group), spread(group), lax.axis_index("batch")

    def head(step):
        to = place(group, ahead(mine, step, here))
        src = head_ref.at[(to["y"] * lax.axis_size("core") + to["core"]) * blk + to["blk"]]
        return send(src, heads_ref.at[b, mine], head_send.at[step], head_recv.at[step], to)

    def extra(step):
        to = place(group, ahead(mine, step, here))
        return send(extra_ref, extras_ref.at[b, mine], extra_send.at[step], extra_recv.at[step], to)

    def trade(which):
        ref = (heads_ref, extras_ref)[which].at[b]
        return send(ref, ref, trade_send.at[which], trade_recv.at[which], {"batch": 1 - b})

    own = [
        pltpu.make_async_copy(tok_ref, toks_ref.at[z, u], local.at[0]),
        pltpu.make_async_copy(head_ref.at[u * blk + z], heads_ref.at[b, mine], local.at[1]),
        pltpu.make_async_copy(extra_ref, extras_ref.at[b, mine], local.at[2]),
    ]

    def start_head(step):
        extra(step).start()
        head(step).start()

    each(here, start_head)
    ways = (1, 0)
    b_y().start()
    for stream in range(2):
        for up in ways:
            when(hop(stream, up, 0), lambda copy: copy.start())
    a_y(0).start()
    to_near(0, 0, 0).start()
    to_near(0, 0, 1).start()

    for copy in own:
        copy.start()
    b_y().wait_recv()
    for up in ways:
        when(hop(2, up, 0), lambda copy: copy.start())
    to_near(0, 1, 1).start()
    def wait_head(step):
        extra(step).wait()
        head(step).wait()

    for hops in range(1, blk):
        if hops == min(2, blk - 1):
            each(here, wait_head)
            for copy in own[1:]:
                copy.wait()
            trade(0).start()
            trade(1).start()
        for stream, (other, part) in enumerate(streams):
            for up in ways:
                exists, copy = arrival(stream, up, hops - 1)
                step = blk - hops if up else hops

                @pl.when(exists)
                def _(copy=copy, stream=stream, other=other, part=part, up=up, step=step, hops=hops):
                    copy.wait_recv()
                    if hops < blk - 1:
                        when(hop(stream, up, hops), lambda copy: copy.start())
                    if stream == 0:
                        a_y(step).start()
                    to_near(step, other, part).start()

    for step in [0, *reversed(range(1, blk))]:
        a_y(step).wait_recv()
        to_near(step, 1, 0).start()
    for step in range(blk):
        for other in range(2):
            for part in range(2):
                to_near(step, other, part).wait_recv()

    trade(0).wait()
    trade(1).wait()
    own[0].wait()
    b_y().wait_send()
    for hops in range(blk - 1):
        for stream in range(3):
            for up in ways:
                when(hop(stream, up, hops), lambda copy: copy.wait_send())
    for step in range(blk):
        a_y(step).wait_send()
        for other in range(2):
            for part in range(2):
                to_near(step, other, part).wait_send()


def startup(heads, extra, tok, collective_id):
    batch, blk, uly = lax.axis_size("batch"), lax.axis_size("blk"), spread(ULY)
    anywhere = pl.BlockSpec(memory_space=pl.ANY)
    dma = pltpu.SemaphoreType.DMA
    return pl.pallas_call(
        startup_kernel,
        in_specs=[anywhere] * 3,
        out_specs=[anywhere] * 3,
        out_shape=[
            jax.ShapeDtypeStruct((batch, blk * uly, *heads.shape[1:]), BF16),
            jax.ShapeDtypeStruct((batch, blk * uly, *extra.shape), BF16),
            jax.ShapeDtypeStruct((blk, uly, *tok.shape), BF16),
        ],
        scratch_shapes=[
            *[dma((blk * uly,))] * 4,
            *[dma((2,))] * 2,
            *[dma((6 * blk,))] * 2,
            *[dma((blk,))] * 2,
            *[dma((1,))] * 2,
            *[dma((4 * blk,))] * 2,
            dma((3,)),
        ],
        compiler_params=pltpu.CompilerParams(collective_id=collective_id, has_side_effects=True),
        name="startup",
    )(heads, extra, tok)


def per_device_general(
    tokens, segments, routes, w_qkv, w_out, attn_gain, ffn_gain, qk_gain, router, w_gate_up, w_down, cotangent
):
    own_tokens = tokens[0]
    own_grad = cotangent[0]
    count_tok, width = own_tokens.shape
    head_dim = qk_gain.shape[1]
    heads = width // head_dim
    uly, blk, batch = spread(ULY), lax.axis_size("blk"), lax.axis_size("batch")
    blk_at, uly_at = lax.axis_index("blk"), lax.axis_index(ULY)
    group = batch * blk
    local_heads = heads // uly
    local_width = local_heads * head_dim
    rows = count_tok * uly
    seg_row = segments[0]
    length = seg_row.shape[0]
    number = router.shape[1]
    local_experts, _, units = w_down.shape
    shard_rows = w_qkv.shape[0]

    extra = jnp.concatenate([attn_gain[:, None], ffn_gain[:, None], router], axis=1)
    extra = jnp.pad(extra, ((0, 0), (0, LANES - extra.shape[1])))
    columns = w_qkv.reshape(shard_rows, 3, uly, local_width).transpose(2, 0, 1, 3)
    packed = jnp.concatenate(
        [
            columns.reshape(uly, shard_rows, 3 * local_width),
            jnp.broadcast_to(extra[None], (uly, shard_rows, LANES)),
        ],
        axis=2,
    )
    packed = swap(packed, ULY).reshape(uly * shard_rows, 3 * local_width + LANES)
    packed = lax.all_gather(packed, ROWS, axis=0, tiled=True)
    own_qkv = packed[:, : 3 * local_width]
    gain_attn = packed[:, 3 * local_width].astype(F32)
    gain_ffn = packed[:, 3 * local_width + 1].astype(F32)
    whole_router = packed[:, 3 * local_width + 2 : 3 * local_width + 2 + number]
    tokens_all = lax.all_gather(own_tokens, ULY, axis=0, tiled=True)
    to_rows = [(u * group + g, g * uly + u) for g in range(group) for u in range(uly)]
    own_out = lax.all_gather(lax.ppermute(w_out, ALL, to_rows), ROWS, axis=0, tiled=True)
    whole_gate_up = lax.all_gather(w_gate_up, PLANE, axis=0, tiled=False)
    whole_down = lax.all_gather(w_down, PLANE, axis=0, tiled=False)
    grad_blk = lax.all_gather(own_grad, "blk", axis=0, tiled=True)
    routes_blk = lax.all_gather(routes[0], "blk", axis=0, tiled=True)

    gain_query = qk_gain[0].astype(F32)
    gain_key = qk_gain[1].astype(F32)
    inputs_all = tokens_all.astype(F32)
    normed_one = inputs_all * rms_scale(inputs_all)
    hidden_one = (normed_one * gain_attn).astype(BF16)
    projected = dot_nn(hidden_one, own_qkv)
    query_raw = projected[:, :local_width].reshape(rows, local_heads, head_dim)
    key_raw = projected[:, local_width : 2 * local_width].reshape(rows, local_heads, head_dim)
    value_raw = projected[:, 2 * local_width :].reshape(rows, local_heads, head_dim)
    cos_table, sin_table = rope_tables(blk_at * rows, rows, head_dim)
    query_scale = rms_scale(query_raw)
    key_scale = rms_scale(key_raw)
    qkv = jnp.concatenate(
        [
            rotate(query_raw * query_scale * gain_query, cos_table, sin_table),
            rotate(key_raw * key_scale * gain_key, cos_table, sin_table),
            value_raw,
        ],
        axis=2,
    ).astype(BF16)
    qkv = qkv.transpose(1, 0, 2)

    by_heads = local_heads % blk == 0
    if by_heads:
        per = local_heads // blk

        def to_heads(values):
            columns = values.shape[2]
            moved = swap(values.reshape(blk, per, rows, columns), "blk")
            return moved.transpose(1, 0, 2, 3).reshape(per, length, columns)

        def to_rows_back(values):
            columns = values.shape[2]
            parts = values.reshape(per, blk, rows, columns).transpose(1, 0, 2, 3)
            return swap(parts, "blk").reshape(local_heads, rows, columns)

        q_src = kv_src = to_heads(qkv)
        cols = (0, 1, 2)
        seg_q = seg_row
        first_head = uly_at * local_heads + blk_at * per
    else:

        def to_heads(values):
            return values

        def to_rows_back(values):
            return values

        q_src = qkv
        kv_src = lax.all_gather(qkv[:, :, head_dim:], "blk", axis=1, tiled=True)
        cols = (0, 0, 1)
        seg_q = lax.dynamic_slice_in_dim(seg_row, blk_at * rows, rows)
        first_head = uly_at * local_heads
    attn_low, attn_f32, lse, top = attention_forward(q_src, kv_src, cols, seg_q, seg_row, head_dim)
    head_vector = lax.dynamic_update_slice_in_dim(
        jnp.full((heads,), NEG, F32), jnp.max(top, axis=(1, 2)) * head_dim**-0.5, first_head, 0
    )
    head_max = lax.pmax(head_vector, ALL)
    attn_rows = to_rows_back(attn_low)
    out_heads = own_out.reshape(local_heads, head_dim, width)
    branch = jnp.einsum("htc,hcd->td", attn_rows, out_heads, preferred_element_type=F32)
    inputs = own_tokens.astype(F32)
    mid = inputs + sum_scatter(branch, ULY)

    scale_two = rms_scale(mid)
    normed_two = mid * scale_two
    hidden_two = (normed_two * gain_ffn).astype(BF16)
    hidden_blk = lax.all_gather(hidden_two, "blk", axis=0, tiled=True)
    probs_blk = jax.nn.softmax(dot_nn(hidden_blk, whole_router), axis=1)
    names = jnp.arange(number, dtype=jnp.int32)
    chosen_blk = jnp.any(routes_blk[:, :, None] == names, axis=1).astype(F32)
    own_names = blk_at * local_experts
    gates = lax.dynamic_slice_in_dim(probs_blk * chosen_blk, own_names, local_experts, axis=1)
    most = min(MOST_TOKENS, hidden_blk.shape[0])
    packed_weights = jnp.concatenate([whole_gate_up, whole_down], axis=3)
    made = []
    for at in range(0, hidden_blk.shape[0], most):
        hidden_part, grad_part = hidden_blk[at : at + most], grad_blk[at : at + most]
        made.append(
            experts(
                hidden_part,
                hidden_part.T,
                grad_part,
                grad_part.T,
                gates[at : at + most],
                [(packed_weights, 0, local_experts)],
            )
        )
    out_part = jnp.concatenate([m[0] for m in made], axis=0)
    dx_part = jnp.concatenate([m[1] for m in made], axis=0)
    dg_part = jnp.concatenate([m[2] for m in made], axis=1)
    expert_grads = sum(m[3].astype(F32) for m in made).astype(BF16)
    expert_sums = lax.psum_scatter(expert_grads, PLANE, scatter_dimension=0, tiled=False).astype(F32)
    grad_gate_up = jnp.concatenate([expert_sums[0], expert_sums[1]], axis=2)
    grad_down = expert_sums[2]
    dg_parts = swap(dg_part.reshape(local_experts, blk, count_tok).transpose(1, 2, 0), "blk")
    grad_gates = dg_parts.transpose(1, 0, 2).reshape(count_tok, number)
    dx_sum = sum_scatter(dx_part, "blk")
    output = (mid + sum_scatter(out_part, "blk")).astype(BF16)
    router_probs = lax.dynamic_slice_in_dim(probs_blk, blk_at * count_tok, count_tok)
    chosen = lax.dynamic_slice_in_dim(chosen_blk, blk_at * count_tok, count_tok)
    grad_probs = chosen * grad_gates
    grad_logits = (
        router_probs * (grad_probs - jnp.sum(router_probs * grad_probs, axis=1, keepdims=True))
    ).astype(BF16)
    grad_hidden_two = dx_sum + dot_nt(grad_logits, whole_router)
    grad_router_part = dot_tn(hidden_two, grad_logits)
    grad_gain_ffn = jnp.sum(grad_hidden_two * normed_two, axis=0)
    grad_mid = own_grad.astype(F32) + norm_back(grad_hidden_two * gain_ffn, mid, scale_two)

    branch_grad = lax.all_gather(grad_mid.astype(BF16), ULY, axis=0, tiled=True)
    grad_attn = dot_nt(branch_grad, own_out).astype(BF16)
    grad_attn = to_heads(grad_attn.reshape(rows, local_heads, head_dim).transpose(1, 0, 2))
    grad_out_part = jnp.einsum("htc,td->hcd", attn_rows, branch_grad, preferred_element_type=F32)
    dq, dk, dv = attention_backward(
        q_src, kv_src, cols, grad_attn, attn_f32, lse, seg_q, seg_row, head_dim
    )
    if by_heads:
        dqkv = to_rows_back(jnp.concatenate([dq, dk, dv], axis=2))
        dq, dk, dv = jnp.split(dqkv, 3, axis=2)
    else:
        dk, dv = (lax.psum_scatter(g, "blk", scatter_dimension=1, tiled=True) for g in (dk, dv))
    dq, dk, dv = (g.transpose(1, 0, 2) for g in (dq, dk, dv))
    grad_query_norm = rotate(dq.astype(F32), cos_table, -sin_table)
    grad_key_norm = rotate(dk.astype(F32), cos_table, -sin_table)
    grad_gain_query = jnp.sum(grad_query_norm * (query_raw * query_scale), axis=(0, 1))
    grad_gain_key = jnp.sum(grad_key_norm * (key_raw * key_scale), axis=(0, 1))
    grad_projected = jnp.concatenate(
        [
            norm_back(grad_query_norm * gain_query, query_raw, query_scale)
            .reshape(rows, local_width)
            .astype(BF16),
            norm_back(grad_key_norm * gain_key, key_raw, key_scale)
            .reshape(rows, local_width)
            .astype(BF16),
            dv.reshape(rows, local_width),
        ],
        axis=1,
    )
    grad_hidden_part = dot_nt(grad_projected, own_qkv)
    grad_hidden_one = sum_scatter(grad_hidden_part, ULY)
    grad_gain_attn = jnp.sum(grad_hidden_part * normed_one, axis=0)
    grad_inputs = grad_mid + norm_back(grad_hidden_one * gain_attn, inputs, rms_scale(inputs))

    grad_qkv_part = dot_tn(hidden_one, grad_projected).astype(BF16)
    grad_qkv_rows = lax.psum_scatter(grad_qkv_part, ROWS, scatter_dimension=0, tiled=True)
    grad_qkv_rows = swap(grad_qkv_rows.reshape(uly, shard_rows, 3 * local_width), ULY)
    grad_qkv = (
        grad_qkv_rows.reshape(uly, shard_rows, 3, local_width)
        .transpose(1, 2, 0, 3)
        .reshape(shard_rows, 3 * width)
        .astype(F32)
    )
    grad_out_rows = lax.psum_scatter(
        grad_out_part.reshape(local_width, width).astype(BF16), ROWS, scatter_dimension=0, tiled=True
    )
    grad_out = lax.ppermute(grad_out_rows, ALL, [(b, a) for a, b in to_rows]).astype(F32)
    small = jnp.concatenate([grad_gain_attn[:, None], grad_gain_ffn[:, None], grad_router_part], axis=1)
    small = lax.psum_scatter(small, ALL, scatter_dimension=0, tiled=True)
    grad_qk_gain = lax.psum(jnp.stack([grad_gain_query, grad_gain_key]), ALL)

    clip_gamma = TAU / jnp.maximum(head_max, TAU)
    factor = jnp.repeat(jnp.sqrt(clip_gamma), head_dim)
    column_scale = jnp.concatenate([factor, factor, jnp.ones((width,), F32)])
    clipped = w_qkv.astype(F32) * column_scale[None, :]
    return (
        output[None],
        grad_inputs[None],
        grad_qkv,
        grad_out,
        small[:, 0],
        small[:, 1],
        grad_qk_gain,
        small[:, 2:],
        grad_gate_up,
        grad_down,
        clipped,
    )


def per_device(
    tokens, segments, routes, w_qkv, w_out, attn_gain, ffn_gain, qk_gain, router, w_gate_up, w_down, cotangent
):
    own_tokens = tokens[0]
    own_grad = cotangent[0]
    count_tok, width = own_tokens.shape
    head_dim = qk_gain.shape[1]
    heads = width // head_dim
    batch, blk, uly = lax.axis_size("batch"), lax.axis_size("blk"), spread(ULY)
    total, group = batch * blk * uly, batch * blk
    local_experts = w_down.shape[0]
    if uly != 4 or heads != blk * uly or blk < 2 or batch != 2 or local_experts % 2:
        return per_device_general(
            tokens, segments, routes, w_qkv, w_out, attn_gain, ffn_gain, qk_gain, router, w_gate_up, w_down, cotangent
        )
    blk_at, uly_at = lax.axis_index("blk"), lax.axis_index(ULY)
    rows = count_tok * uly
    seg_row = segments[0]
    length = seg_row.shape[0]
    number = router.shape[1]
    shard_rows = w_qkv.shape[0]

    to_rows = [(u * group + g, g * uly + u) for g in range(group) for u in range(uly)]
    rows_here = lax.ppermute(w_out, ALL, to_rows)
    rows_there = lax.ppermute(w_out, ALL, [(a, (b + total // 2) % total) for a, b in to_rows])


    half = local_experts // 2

    def gather_experts(gate_up, down):
        return lax.all_gather(jnp.concatenate([gate_up, down], axis=2), PLANE, axis=0, tiled=False)

    weights_first = gather_experts(w_gate_up[:half], w_down[:half])
    extra = jnp.concatenate([attn_gain[None], ffn_gain[None], router.T], axis=0)
    kept = extra.shape[0]
    extra = jnp.pad(extra, ((0, -kept % 16), (0, -shard_rows % LANES)))
    by_head = w_qkv.reshape(shard_rows, 3, heads, head_dim).transpose(2, 0, 1, 3)
    own_qkv, extras, toks = startup(
        by_head.reshape(heads, shard_rows, 3 * head_dim), extra, own_tokens, 0
    )
    rows_here, rows_there, extras, later_gate_up, later_down = lax.optimization_barrier(
        (rows_here, rows_there, extras, w_gate_up[half:], w_down[half:])
    )
    weights_second = gather_experts(later_gate_up, later_down)
    is_first = lax.axis_index("batch") == 0
    pair = jnp.stack(
        [jnp.where(is_first, rows_here, rows_there), jnp.where(is_first, rows_there, rows_here)]
    )
    own_out = lax.all_to_all(
        jnp.broadcast_to(pair[None], (blk, *pair.shape)), "blk", split_axis=0, concat_axis=0, tiled=True
    )
    own_out = own_out.transpose(1, 0, 2, 3).reshape(blk, head_dim, width)
    own_qkv = own_qkv.reshape(width, 3 * head_dim)
    extras = extras.reshape(total, *extra.shape)[:, :kept, :shard_rows]
    extras = extras.transpose(1, 0, 2).reshape(kept, width)
    gain_attn = extras[0].astype(F32)
    gain_ffn = extras[1].astype(F32)
    router_t = extras[2:]

    gains = qk_gain.astype(F32)
    cos, sin = rope_rows(length, head_dim)
    hidden_one, qkv, raw = project(
        toks.reshape(length, width), gain_attn[None], own_qkv, cos, sin, gains
    )
    attn_low, attn_f32, lse, top = attention_forward(
        qkv[None], qkv[None], (0, 1, 2), seg_row, seg_row, head_dim
    )
    (attn_rows,) = exchange([(attn_low.reshape(blk, rows, head_dim), ("blk",), "swap")], 1)
    branch = jnp.einsum("htc,hcd->td", attn_rows, own_out, preferred_element_type=F32)
    branch, grad_blk, routes_blk = exchange(
        [
            (branch.astype(BF16).reshape(uly, count_tok, width), ULY, "pairsum"),
            (own_grad, ("blk",), "line"),
            (routes[0].T, ("blk",), "gather"),
        ],
        2,
    )
    inputs = own_tokens.astype(F32)
    mid = inputs + branch

    scale_two = rms_scale(mid)
    normed_two = mid * scale_two
    hidden_two = (normed_two * gain_ffn).astype(BF16)
    hidden_blk, hidden_t, grad_t = turn_gather(hidden_two, grad_blk, 3)
    tokens_blk = blk * count_tok
    hidden_blk = hidden_blk.reshape(tokens_blk, width)
    grad_blk = grad_blk.reshape(tokens_blk, width)
    probs_blk = jax.nn.softmax(dot_nt(hidden_blk, router_t), axis=1)
    names = jnp.arange(number, dtype=jnp.int32)
    chosen_blk = jnp.any(routes_blk[:, :, :, None] == names, axis=1).astype(F32)
    chosen_blk = chosen_blk.reshape(tokens_blk, number)
    gates = lax.dynamic_slice_in_dim(
        probs_blk * chosen_blk, blk_at * local_experts, local_experts, axis=1
    )
    shared = (hidden_blk, hidden_t, grad_blk, grad_t)
    out_part, dx_part, dg_first, grads_first = experts(
        *shared, gates[:, :half], [(weights_first, 0, half)]
    )
    sums_first = lax.psum_scatter(grads_first, PLANE, scatter_dimension=0, tiled=False)
    out_part, dx_part, dg_others, grads_others = experts(
        *shared, gates[:, half:], [(weights_second, 0, half)], before=(out_part, dx_part)
    )
    sums_others = lax.psum_scatter(grads_others, PLANE, scatter_dimension=0, tiled=False)
    finished = finish_experts(sums_first, 0, local_experts)
    grad_gate_up, grad_down = finish_experts(sums_others, half, local_experts, before=finished)
    dg_part = jnp.concatenate([dg_first, dg_others], axis=0)
    dg_part = dg_part.reshape(local_experts, blk, count_tok)
    dx_parts, dg_parts = exchange(
        [
            (dx_part.reshape(blk, count_tok, width), ("blk",), "swap"),
            (dg_part.transpose(1, 0, 2), ("blk",), "swap"),
        ],
        4,
    )
    out_part = out_part.reshape(blk, count_tok, width)
    out_part, dx_parts = lax.optimization_barrier((out_part, dx_parts))
    out_parts = lax.all_to_all(out_part, "blk", split_axis=0, concat_axis=0, tiled=True)
    output = (mid + jnp.sum(out_parts.astype(F32), axis=0)).astype(BF16)
    router_probs = lax.dynamic_slice_in_dim(probs_blk, blk_at * count_tok, count_tok)
    chosen = lax.dynamic_slice_in_dim(chosen_blk, blk_at * count_tok, count_tok)
    grad_probs = chosen * dg_parts.reshape(number, count_tok).T
    grad_logits = (
        router_probs * (grad_probs - jnp.sum(router_probs * grad_probs, axis=1, keepdims=True))
    ).astype(BF16)
    grad_hidden_two = jnp.sum(dx_parts.astype(F32), axis=0) + dot_nn(grad_logits, router_t)
    grad_router_t = dot_tn(grad_logits, hidden_two)
    grad_gain_ffn = jnp.sum(grad_hidden_two * normed_two, axis=0)
    grad_mid = own_grad.astype(F32) + norm_back(grad_hidden_two * gain_ffn, mid, scale_two)

    (branch_grad,) = exchange([(grad_mid.astype(BF16), ULY, "relay")], 5)
    branch_grad, sent_qkv = lax.optimization_barrier((branch_grad, own_qkv))
    far_qkv = lax.ppermute(sent_qkv, "y", [(0, 1), (1, 0)])
    branch_grad = branch_grad.reshape(rows, width)
    grad_attn = jnp.einsum("td,hcd->htc", branch_grad, own_out, preferred_element_type=F32).astype(BF16)
    grad_out_part = jnp.einsum("htc,td->hcd", attn_rows, branch_grad, preferred_element_type=F32)
    grad_out_part = grad_out_part.astype(BF16).reshape(batch, blk, shard_rows, width)
    batch_at = lax.axis_index("batch")
    (grad_attn,) = exchange([(grad_attn, ("blk",), "swap")], 6, after=[out_parts])
    grad_out_part, far_qkv = lax.optimization_barrier((grad_out_part, far_qkv))
    grad_out_parts = lax.all_to_all(grad_out_part, "blk", split_axis=1, concat_axis=0, tiled=False)
    grad_out_part = jnp.sum(grad_out_parts.astype(F32), axis=0).astype(BF16)
    grad_projected, grad_gains = project_back(
        qkv, grad_attn.reshape(length, head_dim), attn_f32, lse, seg_row, raw, cos, sin, gains
    )
    grad_qkv_part = dot_tn(hidden_one, grad_projected).astype(BF16)
    by_batch = grad_qkv_part.reshape(batch, width // batch, 3 * head_dim)
    projected_blk, got_qkv_part, near_qkv, cross_qkv = exchange(
        [
            (grad_projected.reshape(blk, uly, count_tok, 3 * head_dim), ULY, "swap1"),
            (
                lax.dynamic_index_in_dim(by_batch, 1 - batch_at, 0, keepdims=False),
                ("batch",),
                "trade",
            ),
            (own_qkv, ("core",), "trade"),
            (far_qkv, ("core",), "trade"),
        ],
        7,
    )
    grad_qkv_part = lax.dynamic_index_in_dim(by_batch, batch_at, 0, keepdims=False) + got_qkv_part

    grad_hidden_part, grad_gain_attn = hidden_back(
        projected_blk.reshape(uly, tokens_blk, 3 * head_dim),
        own_qkv,
        near_qkv,
        far_qkv,
        cross_qkv,
        hidden_one.reshape(blk, uly, count_tok, width),
    )
    grad_gain_attn = grad_gain_attn[0] / gain_attn

    small = jnp.concatenate([grad_gain_attn[None], grad_gain_ffn[None], grad_router_t], axis=0)
    beside = LANES // shard_rows
    small = jnp.pad(small, ((0, -kept % beside), (0, 0))).reshape(-1, beside, total, shard_rows)
    small = small.transpose(2, 0, 1, 3).reshape(total, -1, LANES)
    packed_rows = small.shape[1]
    head_row = jnp.where(
        jnp.arange(LANES) == uly_at * blk + blk_at, jnp.max(top) * head_dim**-0.5, NEG
    )
    to_all = jnp.concatenate([grad_gains, head_row[None]], axis=0)
    small = jnp.concatenate([small, jnp.broadcast_to(to_all[None], (total, 3, LANES))], axis=1)
    small = jnp.pad(small, ((0, 0), (0, -small.shape[1] % 8), (0, 0)))
    grad_hidden_parts, small, grad_qkv_parts, grad_out = exchange(
        [
            (grad_hidden_part, ("blk",), "swap"),
            (small, ALL, "swap"),
            (grad_qkv_part.reshape(total // batch, shard_rows, 3 * head_dim), ("blk", *ULY), "swap"),
            (grad_out_part, ALL, "deal"),
        ],
        8,
    )
    grad_out = jnp.sum(grad_out.astype(F32), axis=0)
    grad_qkv = merge_heads(grad_qkv_parts.reshape(blk, uly, shard_rows, 3 * head_dim))
    grad_hidden_one = jnp.sum(grad_hidden_parts.astype(F32), axis=0)
    grad_inputs = grad_mid + norm_back(grad_hidden_one * gain_attn, inputs, rms_scale(inputs))
    sums = jnp.sum(small, axis=0)
    sums, grad_gains = sums[:packed_rows], sums[packed_rows : packed_rows + 2]
    sums = sums.reshape(packed_rows * beside, shard_rows)[:kept]
    head_max = jnp.max(small[:, packed_rows + 2, :heads], axis=0)
    factor = jnp.repeat(jnp.sqrt(TAU / jnp.maximum(head_max, TAU)), head_dim)
    column_scale = jnp.concatenate([factor, factor, jnp.ones((width,), F32)])
    clipped = w_qkv.astype(F32) * column_scale[None, :]
    return (
        output[None],
        grad_inputs[None],
        grad_qkv,
        grad_out,
        sums[0],
        sums[1],
        grad_gains,
        sums[2:].T,
        grad_gate_up,
        grad_down,
        clipped,
    )


def solution(mesh):
    in_specs = (
        P("batch", ("blk", *ULY), None),
        P("batch", None),
        P("batch", ("blk", *ULY), None),
        P(ALL, None),
        P(ALL, None),
        P(ALL),
        P(ALL),
        P(),
        P(ALL, None),
        P("blk", PLANE, None),
        P("blk", PLANE, None),
        P("batch", ("blk", *ULY), None),
    )
    out_specs = (
        P("batch", ("blk", *ULY), None),
        P("batch", ("blk", *ULY), None),
        P(ALL, None),
        P(ALL, None),
        P(ALL),
        P(ALL),
        P(),
        P(ALL, None),
        P("blk", PLANE, None),
        P("blk", PLANE, None),
        P(ALL, None),
    )
    cores = 2 - mesh.shape["uly"] % 2
    mesh = Mesh(
        mesh.devices.reshape(*(mesh.shape[axis] for axis in ROWS), mesh.shape["uly"] // cores, cores), ALL
    )
    return jax.shard_map(
        per_device, mesh=mesh, in_specs=in_specs, out_specs=out_specs, check_vma=False
    )
```

```python
import functools
import math

import jax
import jax.numpy as jnp
from jax import lax
from jax.experimental import pallas as pl
from jax.experimental.pallas import tpu as pltpu
from jax.sharding import Mesh
from jax.sharding import PartitionSpec as P

EPS = 1e-06
THETA = 50000.0
TAU = 4.0
NEG = -1e30
LOG2E = 1.4426950408889634
LANES = 128
MOST_TOKENS = 512
VMEM_LIMIT = 60 * 1024 * 1024

ULY = ("y", "core")
ALL = ("batch", "blk", *ULY)
ROWS = ("batch", "blk")
PLANE = ("batch", *ULY)
CHIPS = ("batch", "y")

MESH = pl.DeviceIdType.MESH
BF16 = jnp.bfloat16
F32 = jnp.float32


def rms_scale(values):
    return lax.rsqrt(jnp.mean(values * values, axis=-1, keepdims=True) + EPS)


def norm_back(grad_normed, values, scale):
    normed = values * scale
    return scale * (grad_normed - normed * jnp.mean(grad_normed * normed, axis=-1, keepdims=True))


def rope_tables(offset, length, head_dim):
    half_dim = head_dim // 2
    frequency = THETA ** (-jnp.arange(half_dim, dtype=F32) * 2.0 / head_dim)
    positions = (offset + jnp.arange(length, dtype=jnp.int32)).astype(F32)
    angles = positions[:, None] * frequency[None, :]
    return (jnp.cos(angles)[:, None, :], jnp.sin(angles)[:, None, :])


def rope_rows(length, head_dim):
    fine = math.gcd(length, LANES)
    frequency = THETA ** (-jnp.arange(head_dim // 2, dtype=F32) * 2.0 / head_dim)
    frequency = jnp.concatenate([frequency, frequency])
    coarse_angle = (jnp.arange(length // fine, dtype=F32) * fine)[:, None, None] * frequency
    fine_angle = jnp.arange(fine, dtype=F32)[None, :, None] * frequency
    cos_a, sin_a, cos_b, sin_b = lax.optimization_barrier(
        (jnp.cos(coarse_angle), jnp.sin(coarse_angle), jnp.cos(fine_angle), jnp.sin(fine_angle))
    )
    sign = jnp.where(jnp.arange(head_dim) < head_dim // 2, -1.0, 1.0)
    cos = cos_a * cos_b - sin_a * sin_b
    sin = (sin_a * cos_b + cos_a * sin_b) * sign
    return cos.reshape(length, head_dim), sin.reshape(length, head_dim)


def rotate(values, cos_table, sin_table):
    half_dim = values.shape[-1] // 2
    first = values[..., :half_dim]
    second = values[..., half_dim:]
    return jnp.concatenate(
        [first * cos_table - second * sin_table, second * cos_table + first * sin_table], axis=-1
    )


def dot_nn(a, b):
    return lax.dot_general(a, b, (((1,), (0,)), ((), ())), preferred_element_type=F32)


def dot_nt(a, b):
    return lax.dot_general(a, b, (((1,), (1,)), ((), ())), preferred_element_type=F32)


def dot_tn(a, b):
    return lax.dot_general(a, b, (((0,), (0,)), ((), ())), preferred_element_type=F32)


def key_chunks(length):
    size = min(512, length)
    return size, length // size


def attn_fwd_kernel(factor, q_ref, k_ref, v_ref, sq_ref, sk_ref, o_ref, of_ref, lse_ref, top_ref, vt_ref):
    length = k_ref.shape[1]
    size, count = key_chunks(length)
    tile, head_dim = q_ref.shape[1:]

    @pl.when(pl.program_id(1) == 0)
    def _():
        vt_ref[...] = v_ref[0].astype(F32).T.astype(BF16)

    q = q_ref[0]
    seg_q = sq_ref[...]

    def step(j, carried):
        total, top, acc = carried
        at = pl.multiple_of(j * size, size)
        scores = dot_nt(k_ref[0, pl.ds(at, size), :], q)
        scores = jnp.where(sk_ref[pl.ds(at, size), :] == seg_q, scores, NEG)
        top = jnp.maximum(top, jnp.max(scores, axis=0, keepdims=True))
        weights = jnp.exp2(scores * factor)
        total = total + jnp.sum(weights, axis=0, keepdims=True)
        acc = acc + dot_nn(vt_ref[:, pl.ds(at, size)], weights.astype(BF16))
        return total, top, acc

    start = (
        jnp.zeros((1, tile), F32),
        jnp.full((1, tile), NEG, F32),
        jnp.zeros((head_dim, tile), F32),
    )
    total, top, acc = lax.fori_loop(0, count, step, start, unroll=count <= 4)
    out = (acc * (1.0 / total)).T
    o_ref[0] = out.astype(BF16)
    of_ref[0] = out
    lse_ref[0] = jnp.log2(total)
    top_ref[0] = top


def attn_bwd_kernel(
    factor, scale, q_ref, k_ref, v_ref, do_ref, of_ref, lse_ref, sq_ref, sk_ref,
    dq_ref, dk_ref, dv_ref, kt_ref, dk_acc, dv_acc,
):
    length = k_ref.shape[1]
    size, count = key_chunks(length)
    tile, head_dim = q_ref.shape[1:]

    @pl.when(pl.program_id(1) == 0)
    def _():
        kt_ref[...] = k_ref[0].astype(F32).T.astype(BF16)
        dk_acc[...] = jnp.zeros_like(dk_acc)
        dv_acc[...] = jnp.zeros_like(dv_acc)

    q = q_ref[0]
    grad = do_ref[0]
    seg_q = sq_ref[...]
    lse = lse_ref[0]
    row_dot = jnp.sum((grad.astype(F32) * of_ref[0]).T, axis=0, keepdims=True)

    def step(j, dq_t):
        at = pl.multiple_of(j * size, size)
        rows = pl.ds(at, size)
        scores = dot_nt(k_ref[0, rows, :], q)
        scores = jnp.where(sk_ref[rows, :] == seg_q, scores, NEG)
        weights = jnp.exp2(scores * factor - lse)
        grad_weights = dot_nt(v_ref[0, rows, :], grad)
        grad_scores = (weights * (grad_weights - row_dot)).astype(BF16)
        dk_acc[rows, :] += dot_nn(grad_scores, q)
        dv_acc[rows, :] += dot_nn(weights.astype(BF16), grad)
        return dq_t + dot_nn(kt_ref[:, rows], grad_scores)

    dq_t = lax.fori_loop(0, count, step, jnp.zeros((head_dim, tile), F32), unroll=count <= 4)
    dq_ref[0] = (dq_t * scale).T.astype(BF16)

    @pl.when(pl.program_id(1) == pl.num_programs(1) - 1)
    def _():
        dk_ref[0] = (dk_acc[...] * scale).astype(BF16)
        dv_ref[0] = dv_acc[...].astype(BF16)


def attention_tile(queries, length):
    return min(queries, 256 if length <= 4096 else 128)


def attention_forward(q_src, kv_src, cols, seg_q, seg_k, head_dim):
    heads, queries = q_src.shape[:2]
    length = kv_src.shape[1]
    tile = attention_tile(queries, length)
    q_col, k_col, v_col = cols
    factor = head_dim**-0.5 * LOG2E
    row = pl.BlockSpec((1, 1, tile), lambda h, i: (h, 0, i))
    block = pl.BlockSpec((1, tile, head_dim), lambda h, i: (h, i, 0))
    return pl.pallas_call(
        functools.partial(attn_fwd_kernel, factor),
        grid=(heads, queries // tile),
        in_specs=[
            pl.BlockSpec((1, tile, head_dim), lambda h, i: (h, i, q_col)),
            pl.BlockSpec((1, length, head_dim), lambda h, i: (h, 0, k_col)),
            pl.BlockSpec((1, length, head_dim), lambda h, i: (h, 0, v_col)),
            pl.BlockSpec((1, tile), lambda h, i: (0, i)),
            pl.BlockSpec((length, 1), lambda h, i: (0, 0)),
        ],
        out_specs=[block, block, row, row],
        out_shape=[
            jax.ShapeDtypeStruct((heads, queries, head_dim), BF16),
            jax.ShapeDtypeStruct((heads, queries, head_dim), F32),
            jax.ShapeDtypeStruct((heads, 1, queries), F32),
            jax.ShapeDtypeStruct((heads, 1, queries), F32),
        ],
        scratch_shapes=[pltpu.VMEM((head_dim, length), BF16)],
        compiler_params=pltpu.CompilerParams(vmem_limit_bytes=VMEM_LIMIT),
        cost_estimate=pl.CostEstimate(
            flops=4 * heads * queries * length * head_dim,
            bytes_accessed=heads * (queries + length) * head_dim * 8,
            transcendentals=heads * queries * length,
        ),
        name="attend",
    )(q_src, kv_src, kv_src, seg_q.reshape(1, -1), seg_k.reshape(-1, 1))


def attention_backward(q_src, kv_src, cols, grad, out_f32, lse, seg_q, seg_k, head_dim):
    heads, queries = q_src.shape[:2]
    length = kv_src.shape[1]
    tile = attention_tile(queries, length)
    q_col, k_col, v_col = cols
    scale = head_dim**-0.5
    row = pl.BlockSpec((1, 1, tile), lambda h, i: (h, 0, i))
    block = pl.BlockSpec((1, tile, head_dim), lambda h, i: (h, i, 0))
    whole = pl.BlockSpec((1, length, head_dim), lambda h, i: (h, 0, 0))
    return pl.pallas_call(
        functools.partial(attn_bwd_kernel, scale * LOG2E, scale),
        grid=(heads, queries // tile),
        in_specs=[
            pl.BlockSpec((1, tile, head_dim), lambda h, i: (h, i, q_col)),
            pl.BlockSpec((1, length, head_dim), lambda h, i: (h, 0, k_col)),
            pl.BlockSpec((1, length, head_dim), lambda h, i: (h, 0, v_col)),
            block,
            block,
            row,
            pl.BlockSpec((1, tile), lambda h, i: (0, i)),
            pl.BlockSpec((length, 1), lambda h, i: (0, 0)),
        ],
        out_specs=[block, whole, whole],
        out_shape=[
            jax.ShapeDtypeStruct((heads, queries, head_dim), BF16),
            jax.ShapeDtypeStruct((heads, length, head_dim), BF16),
            jax.ShapeDtypeStruct((heads, length, head_dim), BF16),
        ],
        scratch_shapes=[
            pltpu.VMEM((head_dim, length), BF16),
            pltpu.VMEM((length, head_dim), F32),
            pltpu.VMEM((length, head_dim), F32),
        ],
        compiler_params=pltpu.CompilerParams(vmem_limit_bytes=VMEM_LIMIT),
        cost_estimate=pl.CostEstimate(
            flops=10 * heads * queries * length * head_dim,
            bytes_accessed=heads * (queries + length) * head_dim * 12,
            transcendentals=heads * queries * length,
        ),
        name="attend_back",
    )(q_src, kv_src, kv_src, grad, out_f32, lse, seg_q.reshape(1, -1), seg_k.reshape(-1, 1))


def expert_step(expert, h_ref, ht_ref, dy_ref, dyt_ref, gate_ref, wg_ref, wu_ref, wd_ref, dg_ref, out_acc, dx_acc):
    width = h_ref.shape[1]
    cols = wg_ref.shape[3]
    w_gate = wg_ref[...].reshape(width, cols)
    w_up = wu_ref[...].reshape(width, cols)
    w_down = wd_ref[...].reshape(width, cols)
    gates = gate_ref[...]
    mine = lax.broadcasted_iota(jnp.int32, gates.shape, 1) == expert
    gate = jnp.sum(jnp.where(mine, gates, 0.0), axis=1, keepdims=True)
    a_gate = dot_nn(h_ref[...], w_gate)
    a_up = dot_nn(h_ref[...], w_up)
    raw = dot_nn(dy_ref[...], w_down)
    sigma = 1.0 / (1.0 + jnp.exp2(a_gate * -LOG2E))
    swish = a_gate * sigma
    act = swish * a_up
    dg_ref[0] += jnp.sum(raw * act, axis=1, keepdims=True)
    gated = (gate * act).astype(BF16)
    d_act = gate * raw
    d_gate = (d_act * a_up * (sigma + swish * (1.0 - sigma))).astype(BF16)
    d_up = (d_act * swish).astype(BF16)
    out_acc[...] += dot_nt(gated, w_down)
    dx_acc[...] += dot_nt(d_gate, w_gate) + dot_nt(d_up, w_up)
    for part, (left, right) in enumerate([(ht_ref, d_gate), (ht_ref, d_up), (dyt_ref, gated)]):
        yield part, dot_nn(left[...], right).astype(BF16)


def expert_kernel(more, counts, *refs):
    h_ref, ht_ref, dy_ref, dyt_ref, gate_ref = refs[:5]
    sources = [refs[5 + 3 * i : 8 + 3 * i] for i in range(len(counts))]
    out_ref, dx_ref, dg_ref, gr_ref, out_acc, dx_acc = refs[-6:]
    step, last = pl.program_id(0), pl.num_programs(0) - 1
    parts, _, part_rows, cols = sources[0][0].shape
    chunks = (last + 1) // sum(counts)

    @pl.when(step == 0)
    def _():
        if more:
            out0_ref, dx0_ref = refs[-8:-6]
            out_acc[...] = out0_ref[...].astype(F32)
            dx_acc[...] = dx0_ref[...].astype(F32)
        else:
            out_acc[...] = jnp.zeros_like(out_acc)
            dx_acc[...] = jnp.zeros_like(dx_acc)

    @pl.when(step % chunks == 0)
    def _():
        dg_ref[...] = jnp.zeros_like(dg_ref)

    begin = 0
    for source, count in zip(sources, counts):
        end = begin + count * chunks

        @pl.when((step >= begin) & (step < end))
        def _(source=source):
            for part, made in expert_step(
                step // chunks, h_ref, ht_ref, dy_ref, dyt_ref, gate_ref, *source, dg_ref, out_acc, dx_acc
            ):
                gr_ref[:, part, 0] = made.reshape(parts, part_rows, cols)

        begin = end

    @pl.when(step == last)
    def _():
        out_ref[...] = out_acc[...].astype(BF16)
        dx_ref[...] = dx_acc[...].astype(BF16)


def experts(hidden, hidden_t, grad, grad_t, gates, sources, before=()):
    tokens, width = hidden.shape
    parts, _, part_rows, units = sources[0][0].shape
    units = units // 3
    counts = [count for _, _, count in sources]
    total = sum(counts)
    cols = min(256, units)
    chunks = units // cols
    once = pl.Buffered(1)
    whole = pl.BlockSpec((tokens, width), lambda s: (0, 0), pipeline_mode=once)
    whole_t = pl.BlockSpec((width, tokens), lambda s: (0, 0), pipeline_mode=once)
    result = pl.BlockSpec((tokens, width), lambda s: (0, 0))

    def weight(source, kind):
        _, first, count = sources[source]
        begin = sum(counts[:source]) * chunks

        def index(step):
            at = jnp.clip(step - begin, 0, count * chunks - 1)
            return (0, first + at // chunks, 0, kind * chunks + at % chunks)

        return pl.BlockSpec((parts, 1, part_rows, cols), index)

    return pl.pallas_call(
        functools.partial(expert_kernel, bool(before), counts),
        grid=(total * chunks,),
        in_specs=[
            whole,
            whole_t,
            whole,
            whole_t,
            pl.BlockSpec(gates.shape, lambda s: (0, 0), pipeline_mode=once),
            *[weight(source, kind) for source in range(len(sources)) for kind in range(3)],
            *[whole for _ in before],
        ],
        out_specs=[
            result,
            result,
            pl.BlockSpec((1, tokens, 1), lambda s: (s // chunks, 0, 0)),
            pl.BlockSpec((parts, 3, 1, part_rows, cols), lambda s: (0, 0, s // chunks, 0, s % chunks)),
        ],
        out_shape=[
            jax.ShapeDtypeStruct((tokens, width), BF16),
            jax.ShapeDtypeStruct((tokens, width), BF16),
            jax.ShapeDtypeStruct((total, tokens, 1), F32),
            jax.ShapeDtypeStruct((parts, 3, total, part_rows, units), BF16),
        ],
        scratch_shapes=[
            pltpu.VMEM((tokens, width), F32),
            pltpu.VMEM((tokens, width), F32),
        ],
        compiler_params=pltpu.CompilerParams(vmem_limit_bytes=VMEM_LIMIT),
        cost_estimate=pl.CostEstimate(
            flops=18 * total * tokens * width * units,
            bytes_accessed=12 * total * width * units,
            transcendentals=total * tokens * units,
        ),
        name="experts",
    )(hidden, hidden_t, grad, grad_t, gates, *[array for array, _, _ in sources for _ in range(3)], *before)


def finish_experts_kernel(sums_ref, *refs):
    gate_up_ref, down_ref = refs[-2:]
    units = down_ref.shape[2]
    gate_up_ref[0, :, :units] = sums_ref[0, 0].astype(F32)
    gate_up_ref[0, :, units:] = sums_ref[1, 0].astype(F32)
    down_ref[0] = sums_ref[2, 0].astype(F32)


def finish_experts(sums, at, total, before=()):
    _, count, rows, units = sums.shape
    tile = min(256, rows)
    return pl.pallas_call(
        finish_experts_kernel,
        grid=(count, rows // tile),
        in_specs=[
            pl.BlockSpec((3, 1, tile, units), lambda e, r: (0, e, r, 0)),
            *[pl.BlockSpec(memory_space=pl.ANY) for _ in before],
        ],
        out_specs=[
            pl.BlockSpec((1, tile, 2 * units), lambda e, r: (at + e, r, 0)),
            pl.BlockSpec((1, tile, units), lambda e, r: (at + e, r, 0)),
        ],
        out_shape=[
            jax.ShapeDtypeStruct((total, rows, 2 * units), F32),
            jax.ShapeDtypeStruct((total, rows, units), F32),
        ],
        input_output_aliases={1 + i: i for i in range(len(before))},
        compiler_params=pltpu.CompilerParams(vmem_limit_bytes=VMEM_LIMIT),
        name="finish_experts",
    )(sums, *before)


def turn(values, cos, sin):
    return values * cos + pltpu.roll(values, values.shape[1] // 2, 1) * sin


def project_kernel(
    tok_ref, gain_ref, w_ref, cos_ref, sin_ref, gains_ref, hidden_ref, qkv_ref, raw_ref
):
    head_dim = cos_ref.shape[1]
    values = tok_ref[...].astype(F32)
    hidden = (values * rms_scale(values) * gain_ref[...]).astype(BF16)
    hidden_ref[...] = hidden
    projected = dot_nn(hidden, w_ref[...])
    raw_ref[...] = projected[:, : 2 * head_dim]
    for part in range(2):
        at = slice(part * head_dim, (part + 1) * head_dim)
        raw = projected[:, at]
        normed = raw * rms_scale(raw) * gains_ref[part : part + 1, :]
        qkv_ref[:, at] = turn(normed, cos_ref[...], sin_ref[...]).astype(BF16)
    qkv_ref[:, 2 * head_dim :] = projected[:, 2 * head_dim :].astype(BF16)


def project(toks, gain, weights, cos, sin, gains):
    length, width = toks.shape
    head_dim = cos.shape[1]
    tile = min(256, length)

    def rows(columns):
        return pl.BlockSpec((tile, columns), lambda i: (i, 0))

    def fixed(shape):
        return pl.BlockSpec(shape, lambda i: (0, 0))

    return pl.pallas_call(
        project_kernel,
        grid=(length // tile,),
        in_specs=[
            rows(width),
            fixed((1, width)),
            fixed(weights.shape),
            rows(head_dim),
            rows(head_dim),
            fixed(gains.shape),
        ],
        out_specs=[rows(width), rows(3 * head_dim), rows(2 * head_dim)],
        out_shape=[
            jax.ShapeDtypeStruct((length, width), BF16),
            jax.ShapeDtypeStruct((length, 3 * head_dim), BF16),
            jax.ShapeDtypeStruct((length, 2 * head_dim), F32),
        ],
        compiler_params=pltpu.CompilerParams(vmem_limit_bytes=VMEM_LIMIT),
        name="project",
    )(toks, gain, weights, cos, sin, gains)


def project_back_kernel(
    factor, scale, q_ref, k_ref, v_ref, do_ref, of_ref, lse_ref, sq_ref, sk_ref,
    raw_q_ref, raw_k_ref, cos_q_ref, sin_q_ref, cos_ref, sin_ref, gains_ref,
    dp_ref, dgain_ref, kt_ref, dk_acc, dv_acc,
):
    length, head_dim = k_ref.shape
    size, count = key_chunks(length)
    tile = q_ref.shape[0]
    step_at = pl.program_id(0)

    @pl.when(step_at == 0)
    def _():
        kt_ref[...] = k_ref[...].astype(F32).T.astype(BF16)
        dk_acc[...] = jnp.zeros_like(dk_acc)
        dv_acc[...] = jnp.zeros_like(dv_acc)
        dgain_ref[...] = jnp.zeros_like(dgain_ref)

    def to_raw(part, grad, raw, cos, sin):
        grad = turn(grad.astype(BF16).astype(F32), cos, -sin)
        raw_scale = rms_scale(raw)
        dgain_ref[part : part + 1, :] += jnp.sum(grad * (raw * raw_scale), axis=0, keepdims=True)
        return norm_back(grad * gains_ref[part : part + 1, :], raw, raw_scale).astype(BF16)

    q = q_ref[...]
    grad = do_ref[...]
    seg_q = sq_ref[...]
    lse = lse_ref[0]
    row_dot = jnp.sum((grad.astype(F32) * of_ref[0]).T, axis=0, keepdims=True)
    dq_t = jnp.zeros((head_dim, tile), F32)
    for j in range(count):
        rows = slice(j * size, (j + 1) * size)
        scores = dot_nt(k_ref[rows, :], q)
        scores = jnp.where(sk_ref[rows, :] == seg_q, scores, NEG)
        weights = jnp.exp2(scores * factor - lse)
        grad_weights = dot_nt(v_ref[rows, :], grad)
        grad_scores = (weights * (grad_weights - row_dot)).astype(BF16)
        dk_acc[rows, :] += dot_nn(grad_scores, q)
        dv_acc[rows, :] += dot_nn(weights.astype(BF16), grad)
        dq_t = dq_t + dot_nn(kt_ref[:, rows], grad_scores)
    own = pl.ds(pl.multiple_of(step_at * tile, tile), tile)
    dp_ref[own, :head_dim] = to_raw(
        0, (dq_t * scale).T, raw_q_ref[...], cos_q_ref[...], sin_q_ref[...]
    )

    @pl.when(step_at == pl.num_programs(0) - 1)
    def _():
        dp_ref[:, head_dim : 2 * head_dim] = to_raw(
            1, dk_acc[...] * scale, raw_k_ref[...], cos_ref[...], sin_ref[...]
        )
        dp_ref[:, 2 * head_dim :] = dv_acc[...].astype(BF16)


def project_back(qkv, grad, out_f32, lse, segments, raw, cos, sin, gains):
    length, head_dim = grad.shape
    tile = min(256, length)

    def rows(column):
        return pl.BlockSpec((tile, head_dim), lambda i: (i, column))

    def whole(column):
        return pl.BlockSpec((length, head_dim), lambda i: (0, column))

    return pl.pallas_call(
        functools.partial(project_back_kernel, head_dim**-0.5 * LOG2E, head_dim**-0.5),
        grid=(length // tile,),
        in_specs=[
            rows(0),
            whole(1),
            whole(2),
            rows(0),
            pl.BlockSpec((1, tile, head_dim), lambda i: (0, i, 0)),
            pl.BlockSpec((1, 1, tile), lambda i: (0, 0, i)),
            pl.BlockSpec((1, tile), lambda i: (0, i)),
            pl.BlockSpec((length, 1), lambda i: (0, 0)),
            rows(0),
            whole(1),
            rows(0),
            rows(0),
            whole(0),
            whole(0),
            pl.BlockSpec(gains.shape, lambda i: (0, 0)),
        ],
        out_specs=[
            pl.BlockSpec((length, 3 * head_dim), lambda i: (0, 0)),
            pl.BlockSpec((2, head_dim), lambda i: (0, 0)),
        ],
        out_shape=[
            jax.ShapeDtypeStruct((length, 3 * head_dim), BF16),
            jax.ShapeDtypeStruct((2, head_dim), F32),
        ],
        scratch_shapes=[
            pltpu.VMEM((head_dim, length), BF16),
            pltpu.VMEM((length, head_dim), F32),
            pltpu.VMEM((length, head_dim), F32),
        ],
        compiler_params=pltpu.CompilerParams(vmem_limit_bytes=VMEM_LIMIT),
        cost_estimate=pl.CostEstimate(
            flops=10 * length * length * head_dim,
            bytes_accessed=length * head_dim * 40,
            transcendentals=length * length,
        ),
        name="project_back",
    )(
        qkv, qkv, qkv, grad, out_f32, lse, segments.reshape(1, -1), segments.reshape(-1, 1),
        raw, raw, cos, sin, cos, sin, gains,
    )


def hidden_back_kernel(grads_ref, own_ref, near_ref, far_ref, cross_ref, hidden_ref, out_ref, gain_ref):
    uly = grads_ref.shape[0]
    u = lax.axis_index(ULY)
    near = u + 1 - 2 * lax.rem(u, 2)
    total = dot_nt(grads_ref[u], own_ref[...])
    total = total + dot_nt(grads_ref[near], near_ref[...])
    total = total + dot_nt(grads_ref[lax.rem(u + 2, uly)], far_ref[...])
    total = total + dot_nt(grads_ref[lax.rem(near + 2, uly)], cross_ref[...])
    out_ref[...] = total.astype(BF16).reshape(out_ref.shape)
    hidden = hidden_ref[...].reshape(total.shape).astype(F32)
    gain_ref[...] = jnp.sum(total * hidden, axis=0, keepdims=True)


def hidden_back(grads, own, near, far, cross, hidden):
    uly, tokens, columns = grads.shape
    blk, _, rows, width = hidden.shape
    tile = min(512, width)
    weights = pl.BlockSpec((tile, columns), lambda n: (n, 0))
    return pl.pallas_call(
        hidden_back_kernel,
        grid=(width // tile,),
        in_specs=[
            pl.BlockSpec(grads.shape, lambda n: (0, 0, 0)),
            *[weights] * 4,
            pl.BlockSpec((blk, 1, rows, tile), lambda n: (0, lax.axis_index(ULY), 0, n)),
        ],
        out_specs=[
            pl.BlockSpec((blk, rows, tile), lambda n: (0, 0, n)),
            pl.BlockSpec((1, tile), lambda n: (0, n)),
        ],
        out_shape=[
            jax.ShapeDtypeStruct((blk, rows, width), BF16),
            jax.ShapeDtypeStruct((1, width), F32),
        ],
        compiler_params=pltpu.CompilerParams(vmem_limit_bytes=VMEM_LIMIT),
        name="hidden_back",
    )(grads, own, near, far, cross, hidden)


def merge_heads_kernel(parts_ref, out_ref):
    blk, uly, _, columns = parts_ref.shape
    head_dim = columns // 3
    heads = blk * uly
    for z in range(blk):
        for u in range(uly):
            head = parts_ref[z, u].astype(F32)
            for part in range(3):
                at = (part * heads + u * blk + z) * head_dim
                out_ref[:, at : at + head_dim] = head[:, part * head_dim : (part + 1) * head_dim]


def merge_heads(parts):
    blk, uly, rows, columns = parts.shape
    return pl.pallas_call(
        merge_heads_kernel,
        out_shape=jax.ShapeDtypeStruct((rows, blk * uly * columns), F32),
        compiler_params=pltpu.CompilerParams(vmem_limit_bytes=VMEM_LIMIT),
        name="merge_heads",
    )(parts)


def swap(values, axis):
    return lax.all_to_all(values, axis, split_axis=0, concat_axis=0, tiled=True)


def sum_scatter(values, axis):
    count = spread(axis) if isinstance(axis, tuple) else lax.axis_size(axis)
    rows, width = values.shape
    parts = swap(values.astype(BF16).reshape(count, rows // count, width), axis)
    return jnp.sum(parts.astype(F32), axis=0)


def place(axes, index):
    found = {}
    for axis in reversed(axes):
        size = lax.axis_size(axis)
        found[axis] = lax.rem(index, size)
        index = index // size
    return found


def spread(axes):
    return math.prod(lax.axis_size(axis) for axis in axes)


def each(count, body):
    if count <= 4:
        for step in range(1, count):
            body(step)
    else:

        def looped(step, carried):
            body(step)
            return carried

        lax.fori_loop(1, count, looped, 0)


def ahead(index, step, size):
    return lax.rem(index + step, size)


def exchange(items, collective_id, after=()):
    count = len(items)
    sizes = [spread(axes) for _, axes, _ in items]
    groups = list(dict.fromkeys(axes for _, axes, _ in items))
    bases = [sum(2 * size for size in sizes[:i]) for i in range(count)]

    def kernel(*refs):
        ins = refs[:count]
        outs = refs[count + len(after) : 2 * count + len(after)]
        send, recv, local = refs[2 * count + len(after) :][:3]
        barrier = pltpu.get_barrier_semaphore()
        for axes in groups:
            size, me = spread(axes), lax.axis_index(axes)

            def greet(step, axes=axes, size=size, me=me):
                pl.semaphore_signal(
                    barrier, inc=1, device_id=place(axes, ahead(me, step, size)), device_id_type=MESH
                )

            each(size, greet)
        pl.semaphore_wait(barrier, sum(spread(axes) - 1 for axes in groups))

        def block(i, peer):
            if items[i][2] == "swap":
                return ins[i].at[peer]
            return ins[i].at[:, peer] if items[i][2] == "swap1" else ins[i]

        def remote(i, step):
            _, axes, kind = items[i]
            me = lax.axis_index(axes)
            if kind == "trade":
                return pltpu.make_async_remote_copy(
                    src_ref=ins[i],
                    dst_ref=outs[i],
                    send_sem=send.at[bases[i] + 1],
                    recv_sem=recv.at[bases[i] + 1],
                    device_id=place(axes, 1 - me),
                    device_id_type=MESH,
                )
            if kind == "relay":
                far, near = lax.rem(me + 2, 4), me + 1 - 2 * lax.rem(me, 2)
                held = far if step == 3 else me
                return pltpu.make_async_remote_copy(
                    src_ref=outs[i].at[far] if step == 3 else ins[i],
                    dst_ref=outs[i].at[held],
                    send_sem=send.at[bases[i] + step],
                    recv_sem=recv.at[bases[i] + step],
                    device_id=place(axes, far if step == 1 else near),
                    device_id_type=MESH,
                )
            peer = ahead(me, step, sizes[i])
            return pltpu.make_async_remote_copy(
                src_ref=block(i, peer),
                dst_ref=outs[i].at[me],
                send_sem=send.at[bases[i] + step],
                recv_sem=recv.at[bases[i] + step],
                device_id=place(axes, peer),
                device_id_type=MESH,
            )

        def own(i):
            _, axes, kind = items[i]
            me = lax.axis_index(axes)
            return pltpu.make_async_copy(
                block(i, me), outs[i].at[me], local.at[i]
            )

        def hop(i, up, hops):
            (axis,) = items[i][1]
            me, size = lax.axis_index(axis), sizes[i]
            way = 1 if up else -1
            held, to = me - way * hops, me + way
            exists = (held >= 0) & (held < size) & (to >= 0) & (to < size)
            held, to = jnp.clip(held, 0, size - 1), jnp.clip(to, 0, size - 1)
            sem = bases[i] + (size if up else 0) + hops
            copy = pltpu.make_async_remote_copy(
                src_ref=outs[i].at[held] if hops else ins[i],
                dst_ref=outs[i].at[held],
                send_sem=send.at[sem],
                recv_sem=recv.at[sem],
                device_id={axis: to},
                device_id_type=MESH,
            )
            return exists, copy

        def arrival(i, up, hops):
            (axis,) = items[i][1]
            me, size = lax.axis_index(axis), sizes[i]
            way = 1 if up else -1
            held, sender = me - way * (hops + 1), me - way
            exists = (held >= 0) & (held < size)
            held, sender = jnp.clip(held, 0, size - 1), jnp.clip(sender, 0, size - 1)
            sem = bases[i] + (size if up else 0) + hops
            copy = pltpu.make_async_remote_copy(
                src_ref=ins[i],
                dst_ref=outs[i].at[held],
                send_sem=send.at[sem],
                recv_sem=recv.at[sem],
                device_id={axis: sender},
                device_id_type=MESH,
            )
            return exists, copy

        def kinds(*names):
            return [i for i in range(count) if items[i][2] in names]

        def when(pair, act):
            exists, copy = pair
            pl.when(exists)(lambda: act(copy))

        def pairsum(i):
            me = lax.axis_index(ULY)
            far, near = lax.rem(me + 2, 4), me + 1 - 2 * lax.rem(me, 2)
            own, out = ins[i], outs[i]
            got_near, got_far, sent = refs[2 * count + len(after) + 3 :]

            def copy(at, src, dst, to):
                return pltpu.make_async_remote_copy(
                    src_ref=src,
                    dst_ref=dst,
                    send_sem=send.at[bases[i] + at],
                    recv_sem=recv.at[bases[i] + at],
                    device_id=place(ULY, to),
                    device_id_type=MESH,
                )

            to_near = [
                copy(0, own.at[near], got_near.at[0], near),
                copy(1, own.at[lax.rem(near + 2, 4)], got_near.at[1], near),
            ]
            to_far = copy(2, sent, got_far, far)

            def first():
                for sending in to_near:
                    sending.start()

            def second():
                for sending in to_near:
                    sending.wait()
                sent[...] = (own[far].astype(F32) + got_near[1].astype(F32)).astype(BF16)
                to_far.start()
                out[...] = own[me].astype(F32) + got_near[0].astype(F32)

            def third():
                to_far.wait()
                out[...] += got_far[...].astype(F32)

            return first, second, third

        ways = (True, False)
        sums = [pairsum(i) for i in kinds("pairsum")]
        for first, _, _ in sums:
            first()
        for i in kinds("line"):
            for up in ways:
                when(hop(i, up, 0), lambda copy: copy.start())
        for i in kinds("gather", "swap", "swap1", "relay", "trade"):
            each(3 if items[i][2] == "relay" else sizes[i], lambda step, i=i: remote(i, step).start())
        for i in kinds("gather", "swap", "swap1", "relay", "line"):
            own(i).start()
        for _, second, _ in sums:
            second()
        for i in kinds("line"):
            for hops in range(1, sizes[i]):
                for up in ways:
                    when(arrival(i, up, hops - 1), lambda copy: copy.wait_recv())
                    if hops < sizes[i] - 1:
                        when(hop(i, up, hops), lambda copy: copy.start())
        for i in kinds("relay"):
            remote(i, 1).wait_recv()
            remote(i, 3).start()
            remote(i, 1).wait_send()
            for step in (2, 3):
                remote(i, step).wait()
        for i in kinds("gather", "swap", "swap1", "trade"):
            each(sizes[i], lambda step, i=i: remote(i, step).wait())
        for i in kinds("line"):
            for hops in range(sizes[i] - 1):
                for up in ways:
                    when(hop(i, up, hops), lambda copy: copy.wait_send())
        for i in kinds("gather", "swap", "swap1", "relay", "line"):
            own(i).wait()
        for _, _, third in sums:
            third()


    def shape_of(size, array, kind):
        if kind in ("trade", "pairsum"):
            return array.shape[kind == "pairsum" :]
        dropped = {"swap": 0, "swap1": 1}.get(kind)
        return (size, *(extent for at, extent in enumerate(array.shape) if at != dropped))

    anywhere, close = pl.BlockSpec(memory_space=pl.ANY), pl.BlockSpec(memory_space=pltpu.VMEM)
    specs = [close if kind == "pairsum" else anywhere for _, _, kind in items]
    held = []
    for array, _, kind in items:
        if kind == "pairsum":
            held = [pltpu.VMEM((*more, *array.shape[1:]), BF16) for more in ((2,), (), ())]
    return pl.pallas_call(
        kernel,
        in_specs=specs + [anywhere] * len(after),
        out_specs=specs,
        out_shape=[
            jax.ShapeDtypeStruct(shape_of(size, array, kind), F32 if kind == "pairsum" else array.dtype)
            for size, (array, _, kind) in zip(sizes, items)
        ],
        scratch_shapes=[
            pltpu.SemaphoreType.DMA((2 * sum(sizes),)),
            pltpu.SemaphoreType.DMA((2 * sum(sizes),)),
            pltpu.SemaphoreType.DMA((count,)),
            *held,
        ],
        compiler_params=pltpu.CompilerParams(
            collective_id=collective_id, has_side_effects=True, vmem_limit_bytes=VMEM_LIMIT if held else None
        ),
        name="exchange",
    )(*[item[0] for item in items], *after)


def turn_gather_kernel(
    own_ref, other_ref, all_ref, all_t_ref, other_t_ref, block, turned, send, recv, local
):
    size, me = lax.axis_size("blk"), lax.axis_index("blk")
    rows = own_ref.shape[0]
    barrier = pltpu.get_barrier_semaphore()
    ways = (1, 0)

    def neighbour(up):
        to = me + (1 if up else -1)
        return (to >= 0) & (to < size), jnp.clip(to, 0, size - 1)

    def greet(step):
        pl.semaphore_signal(
            barrier, inc=1, device_id={"blk": ahead(me, step, size)}, device_id_type=MESH
        )

    each(size, greet)
    pl.semaphore_wait(barrier, size - 1)

    def hop(up, hops):
        held = me - (1 if up else -1) * hops
        exists, to = neighbour(up)
        exists = exists & (held >= 0) & (held < size)
        held = jnp.clip(held, 0, size - 1)
        return exists, pltpu.make_async_remote_copy(
            src_ref=all_ref.at[held] if hops else own_ref,
            dst_ref=all_ref.at[held],
            send_sem=send.at[up * size + hops],
            recv_sem=recv.at[up * size + hops],
            device_id={"blk": to},
            device_id_type=MESH,
        )

    def arrival(up, hops):
        held = me - (1 if up else -1) * (hops + 1)
        exists = (held >= 0) & (held < size)
        held = jnp.clip(held, 0, size - 1)
        return exists, held, pltpu.make_async_remote_copy(
            src_ref=own_ref,
            dst_ref=all_ref.at[held],
            send_sem=send.at[up * size + hops],
            recv_sem=recv.at[up * size + hops],
            device_id={"blk": neighbour(1 - up)[1]},
            device_id_type=MESH,
        )

    def when(pair, act):
        exists, copy = pair
        pl.when(exists)(lambda: act(copy))

    def turn(src, dst, at):
        take = pltpu.make_async_copy(src, block, local.at[0])
        take.start()
        take.wait()
        turned[...] = block[...].T
        columns = pl.ds(pl.multiple_of(at * rows, rows), rows)
        give = pltpu.make_async_copy(turned, dst.at[:, columns], local.at[1])
        give.start()
        give.wait()

    for up in ways:
        when(hop(up, 0), lambda copy: copy.start())
    keep = pltpu.make_async_copy(own_ref, all_ref.at[me], local.at[2])
    keep.start()
    turn(own_ref, all_t_ref, me)
    for at in range(size):
        turn(other_ref.at[at], other_t_ref, at)
    for hops in range(1, size):
        for up in ways:
            exists, held, copy = arrival(up, hops - 1)

            @pl.when(exists)
            def _(copy=copy, up=up, hops=hops):
                copy.wait_recv()
                if hops < size - 1:
                    when(hop(up, hops), lambda copy: copy.start())

        for up in ways:
            exists, held, copy = arrival(up, hops - 1)
            pl.when(exists)(lambda held=held: turn(all_ref.at[held], all_t_ref, held))
    for hops in range(size - 1):
        for up in ways:
            when(hop(up, hops), lambda copy: copy.wait_send())
    keep.wait()


def turn_gather(own, other, collective_id, after=()):
    size = lax.axis_size("blk")
    rows, width = own.shape
    anywhere = pl.BlockSpec(memory_space=pl.ANY)

    def kernel(*refs):
        turn_gather_kernel(*refs[:2], *refs[2 + len(after) :])

    return pl.pallas_call(
        kernel,
        in_specs=[anywhere] * (2 + len(after)),
        out_specs=[anywhere] * 3,
        out_shape=[
            jax.ShapeDtypeStruct((size, rows, width), BF16),
            jax.ShapeDtypeStruct((width, size * rows), BF16),
            jax.ShapeDtypeStruct((width, size * rows), BF16),
        ],
        scratch_shapes=[
            pltpu.VMEM((rows, width), BF16),
            pltpu.VMEM((width, rows), BF16),
            pltpu.SemaphoreType.DMA((2 * size,)),
            pltpu.SemaphoreType.DMA((2 * size,)),
            pltpu.SemaphoreType.DMA((3,)),
        ],
        compiler_params=pltpu.CompilerParams(
            collective_id=collective_id, has_side_effects=True, vmem_limit_bytes=VMEM_LIMIT
        ),
        name="turn_gather",
    )(own, other, *after)


def startup_kernel(
    head_ref, extra_ref, tok_ref, heads_ref, extras_ref, toks_ref,
    head_send, head_recv, extra_send, extra_recv, trade_send, trade_recv,
    z_send, z_recv, ay_send, ay_recv, by_send, by_recv, c_send, c_recv, local,
):
    blk, uly = lax.axis_size("blk"), spread(ULY)
    total = spread(ALL)
    z, u, me = lax.axis_index("blk"), lax.axis_index(ULY), lax.axis_index(ALL)
    far = lax.rem(u + 2, uly)
    near = u + 1 - 2 * lax.rem(u, 2)
    rows = tok_ref.shape[0]
    first = rows * 5 // 8 // 16 * 16
    parts = (pl.ds(0, first), pl.ds(first, rows - first))

    barrier = pltpu.get_barrier_semaphore()

    def greet(step):
        pl.semaphore_signal(
            barrier, inc=1, device_id=place(ALL, ahead(me, step, total)), device_id_type=MESH
        )

    each(total, greet)
    pl.semaphore_wait(barrier, total - 1)

    def send(src, dst, sent, got, to):
        return pltpu.make_async_remote_copy(
            src_ref=src, dst_ref=dst, send_sem=sent, recv_sem=got, device_id=to, device_id_type=MESH
        )

    def block(step, other, part):
        at = toks_ref.at[ahead(z, step, blk), far if other else u, parts[part]]
        return (tok_ref.at[parts[part]] if step == 0 and not other else at), at

    streams = ((0, 0), (0, 1), (1, 1))

    def hop(stream, up, hops):
        other, part = streams[stream]
        way = 1 if up else -1
        held, to = z - way * hops, z + way
        exists = (held >= 0) & (held < blk) & (to >= 0) & (to < blk)
        held, to = jnp.clip(held, 0, blk - 1), jnp.clip(to, 0, blk - 1)
        at = toks_ref.at[held, far if other else u, parts[part]]
        src = tok_ref.at[parts[part]] if hops == 0 and not other else at
        sem = (2 * stream + up) * blk + hops
        return exists, send(src, at, z_send.at[sem], z_recv.at[sem], {"blk": to})

    def arrival(stream, up, hops):
        other, part = streams[stream]
        way = 1 if up else -1
        held, sender = z - way * (hops + 1), z - way
        exists = (held >= 0) & (held < blk)
        held, sender = jnp.clip(held, 0, blk - 1), jnp.clip(sender, 0, blk - 1)
        at = toks_ref.at[held, far if other else u, parts[part]]
        sem = (2 * stream + up) * blk + hops
        return exists, send(tok_ref.at[parts[part]], at, z_send.at[sem], z_recv.at[sem], {"blk": sender})

    def when(pair, act):
        exists, copy = pair
        pl.when(exists)(lambda: act(copy))

    def a_y(step):
        return send(*block(step, 0, 0), ay_send.at[step], ay_recv.at[step], place(ULY, far))

    def b_y():
        return send(*block(0, 0, 1), by_send.at[0], by_recv.at[0], place(ULY, far))

    def to_near(step, other, part):
        sem = 4 * step + 2 * other + part
        return send(*block(step, other, part), c_send.at[sem], c_recv.at[sem], place(ULY, near))

    group = ("blk", *ULY)
    mine, here, b = lax.axis_index(group), spread(group), lax.axis_index("batch")

    def head(step):
        to = place(group, ahead(mine, step, here))
        src = head_ref.at[(to["y"] * lax.axis_size("core") + to["core"]) * blk + to["blk"]]
        return send(src, heads_ref.at[b, mine], head_send.at[step], head_recv.at[step], to)

    def extra(step):
        to = place(group, ahead(mine, step, here))
        return send(extra_ref, extras_ref.at[b, mine], extra_send.at[step], extra_recv.at[step], to)

    def trade(which):
        ref = (heads_ref, extras_ref)[which].at[b]
        return send(ref, ref, trade_send.at[which], trade_recv.at[which], {"batch": 1 - b})

    own = [
        pltpu.make_async_copy(tok_ref, toks_ref.at[z, u], local.at[0]),
        pltpu.make_async_copy(head_ref.at[u * blk + z], heads_ref.at[b, mine], local.at[1]),
        pltpu.make_async_copy(extra_ref, extras_ref.at[b, mine], local.at[2]),
    ]

    def start_head(step):
        extra(step).start()
        head(step).start()

    each(here, start_head)
    ways = (1, 0)
    b_y().start()
    for stream in range(2):
        for up in ways:
            when(hop(stream, up, 0), lambda copy: copy.start())
    a_y(0).start()
    to_near(0, 0, 0).start()
    to_near(0, 0, 1).start()

    for copy in own:
        copy.start()
    b_y().wait_recv()
    for up in ways:
        when(hop(2, up, 0), lambda copy: copy.start())
    to_near(0, 1, 1).start()
    def wait_head(step):
        extra(step).wait()
        head(step).wait()

    for hops in range(1, blk):
        if hops == min(2, blk - 1):
            each(here, wait_head)
            for copy in own[1:]:
                copy.wait()
            trade(0).start()
            trade(1).start()
        for stream, (other, part) in enumerate(streams):
            for up in ways:
                exists, copy = arrival(stream, up, hops - 1)
                step = blk - hops if up else hops

                @pl.when(exists)
                def _(copy=copy, stream=stream, other=other, part=part, up=up, step=step, hops=hops):
                    copy.wait_recv()
                    if hops < blk - 1:
                        when(hop(stream, up, hops), lambda copy: copy.start())
                    if stream == 0:
                        a_y(step).start()
                    to_near(step, other, part).start()

    for step in [0, *reversed(range(1, blk))]:
        a_y(step).wait_recv()
        to_near(step, 1, 0).start()
    for step in range(blk):
        for other in range(2):
            for part in range(2):
                to_near(step, other, part).wait_recv()

    trade(0).wait()
    trade(1).wait()
    own[0].wait()
    b_y().wait_send()
    for hops in range(blk - 1):
        for stream in range(3):
            for up in ways:
                when(hop(stream, up, hops), lambda copy: copy.wait_send())
    for step in range(blk):
        a_y(step).wait_send()
        for other in range(2):
            for part in range(2):
                to_near(step, other, part).wait_send()


def startup(heads, extra, tok, collective_id):
    batch, blk, uly = lax.axis_size("batch"), lax.axis_size("blk"), spread(ULY)
    anywhere = pl.BlockSpec(memory_space=pl.ANY)
    dma = pltpu.SemaphoreType.DMA
    return pl.pallas_call(
        startup_kernel,
        in_specs=[anywhere] * 3,
        out_specs=[anywhere] * 3,
        out_shape=[
            jax.ShapeDtypeStruct((batch, blk * uly, *heads.shape[1:]), BF16),
            jax.ShapeDtypeStruct((batch, blk * uly, *extra.shape), BF16),
            jax.ShapeDtypeStruct((blk, uly, *tok.shape), BF16),
        ],
        scratch_shapes=[
            *[dma((blk * uly,))] * 4,
            *[dma((2,))] * 2,
            *[dma((6 * blk,))] * 2,
            *[dma((blk,))] * 2,
            *[dma((1,))] * 2,
            *[dma((4 * blk,))] * 2,
            dma((3,)),
        ],
        compiler_params=pltpu.CompilerParams(collective_id=collective_id, has_side_effects=True),
        name="startup",
    )(heads, extra, tok)


def per_device_general(
    tokens, segments, routes, w_qkv, w_out, attn_gain, ffn_gain, qk_gain, router, w_gate_up, w_down, cotangent
):
    own_tokens = tokens[0]
    own_grad = cotangent[0]
    count_tok, width = own_tokens.shape
    head_dim = qk_gain.shape[1]
    heads = width // head_dim
    uly, blk, batch = spread(ULY), lax.axis_size("blk"), lax.axis_size("batch")
    blk_at, uly_at = lax.axis_index("blk"), lax.axis_index(ULY)
    group = batch * blk
    local_heads = heads // uly
    local_width = local_heads * head_dim
    rows = count_tok * uly
    seg_row = segments[0]
    length = seg_row.shape[0]
    number = router.shape[1]
    local_experts, _, units = w_down.shape
    shard_rows = w_qkv.shape[0]

    extra = jnp.concatenate([attn_gain[:, None], ffn_gain[:, None], router], axis=1)
    extra = jnp.pad(extra, ((0, 0), (0, LANES - extra.shape[1])))
    columns = w_qkv.reshape(shard_rows, 3, uly, local_width).transpose(2, 0, 1, 3)
    packed = jnp.concatenate(
        [
            columns.reshape(uly, shard_rows, 3 * local_width),
            jnp.broadcast_to(extra[None], (uly, shard_rows, LANES)),
        ],
        axis=2,
    )
    packed = swap(packed, ULY).reshape(uly * shard_rows, 3 * local_width + LANES)
    packed = lax.all_gather(packed, ROWS, axis=0, tiled=True)
    own_qkv = packed[:, : 3 * local_width]
    gain_attn = packed[:, 3 * local_width].astype(F32)
    gain_ffn = packed[:, 3 * local_width + 1].astype(F32)
    whole_router = packed[:, 3 * local_width + 2 : 3 * local_width + 2 + number]
    tokens_all = lax.all_gather(own_tokens, ULY, axis=0, tiled=True)
    to_rows = [(u * group + g, g * uly + u) for g in range(group) for u in range(uly)]
    own_out = lax.all_gather(lax.ppermute(w_out, ALL, to_rows), ROWS, axis=0, tiled=True)
    whole_gate_up = lax.all_gather(w_gate_up, PLANE, axis=0, tiled=False)
    whole_down = lax.all_gather(w_down, PLANE, axis=0, tiled=False)
    grad_blk = lax.all_gather(own_grad, "blk", axis=0, tiled=True)
    routes_blk = lax.all_gather(routes[0], "blk", axis=0, tiled=True)

    gain_query = qk_gain[0].astype(F32)
    gain_key = qk_gain[1].astype(F32)
    inputs_all = tokens_all.astype(F32)
    normed_one = inputs_all * rms_scale(inputs_all)
    hidden_one = (normed_one * gain_attn).astype(BF16)
    projected = dot_nn(hidden_one, own_qkv)
    query_raw = projected[:, :local_width].reshape(rows, local_heads, head_dim)
    key_raw = projected[:, local_width : 2 * local_width].reshape(rows, local_heads, head_dim)
    value_raw = projected[:, 2 * local_width :].reshape(rows, local_heads, head_dim)
    cos_table, sin_table = rope_tables(blk_at * rows, rows, head_dim)
    query_scale = rms_scale(query_raw)
    key_scale = rms_scale(key_raw)
    qkv = jnp.concatenate(
        [
            rotate(query_raw * query_scale * gain_query, cos_table, sin_table),
            rotate(key_raw * key_scale * gain_key, cos_table, sin_table),
            value_raw,
        ],
        axis=2,
    ).astype(BF16)
    qkv = qkv.transpose(1, 0, 2)

    by_heads = local_heads % blk == 0
    if by_heads:
        per = local_heads // blk

        def to_heads(values):
            columns = values.shape[2]
            moved = swap(values.reshape(blk, per, rows, columns), "blk")
            return moved.transpose(1, 0, 2, 3).reshape(per, length, columns)

        def to_rows_back(values):
            columns = values.shape[2]
            parts = values.reshape(per, blk, rows, columns).transpose(1, 0, 2, 3)
            return swap(parts, "blk").reshape(local_heads, rows, columns)

        q_src = kv_src = to_heads(qkv)
        cols = (0, 1, 2)
        seg_q = seg_row
        first_head = uly_at * local_heads + blk_at * per
    else:

        def to_heads(values):
            return values

        def to_rows_back(values):
            return values

        q_src = qkv
        kv_src = lax.all_gather(qkv[:, :, head_dim:], "blk", axis=1, tiled=True)
        cols = (0, 0, 1)
        seg_q = lax.dynamic_slice_in_dim(seg_row, blk_at * rows, rows)
        first_head = uly_at * local_heads
    attn_low, attn_f32, lse, top = attention_forward(q_src, kv_src, cols, seg_q, seg_row, head_dim)
    head_vector = lax.dynamic_update_slice_in_dim(
        jnp.full((heads,), NEG, F32), jnp.max(top, axis=(1, 2)) * head_dim**-0.5, first_head, 0
    )
    head_max = lax.pmax(head_vector, ALL)
    attn_rows = to_rows_back(attn_low)
    out_heads = own_out.reshape(local_heads, head_dim, width)
    branch = jnp.einsum("htc,hcd->td", attn_rows, out_heads, preferred_element_type=F32)
    inputs = own_tokens.astype(F32)
    mid = inputs + sum_scatter(branch, ULY)

    scale_two = rms_scale(mid)
    normed_two = mid * scale_two
    hidden_two = (normed_two * gain_ffn).astype(BF16)
    hidden_blk = lax.all_gather(hidden_two, "blk", axis=0, tiled=True)
    probs_blk = jax.nn.softmax(dot_nn(hidden_blk, whole_router), axis=1)
    names = jnp.arange(number, dtype=jnp.int32)
    chosen_blk = jnp.any(routes_blk[:, :, None] == names, axis=1).astype(F32)
    own_names = blk_at * local_experts
    gates = lax.dynamic_slice_in_dim(probs_blk * chosen_blk, own_names, local_experts, axis=1)
    most = min(MOST_TOKENS, hidden_blk.shape[0])
    packed_weights = jnp.concatenate([whole_gate_up, whole_down], axis=3)
    made = []
    for at in range(0, hidden_blk.shape[0], most):
        hidden_part, grad_part = hidden_blk[at : at + most], grad_blk[at : at + most]
        made.append(
            experts(
                hidden_part,
                hidden_part.T,
                grad_part,
                grad_part.T,
                gates[at : at + most],
                [(packed_weights, 0, local_experts)],
            )
        )
    out_part = jnp.concatenate([m[0] for m in made], axis=0)
    dx_part = jnp.concatenate([m[1] for m in made], axis=0)
    dg_part = jnp.concatenate([m[2] for m in made], axis=1)
    expert_grads = sum(m[3].astype(F32) for m in made).astype(BF16)
    expert_sums = lax.psum_scatter(expert_grads, PLANE, scatter_dimension=0, tiled=False).astype(F32)
    grad_gate_up = jnp.concatenate([expert_sums[0], expert_sums[1]], axis=2)
    grad_down = expert_sums[2]
    dg_parts = swap(dg_part.reshape(local_experts, blk, count_tok).transpose(1, 2, 0), "blk")
    grad_gates = dg_parts.transpose(1, 0, 2).reshape(count_tok, number)
    dx_sum = sum_scatter(dx_part, "blk")
    output = (mid + sum_scatter(out_part, "blk")).astype(BF16)
    router_probs = lax.dynamic_slice_in_dim(probs_blk, blk_at * count_tok, count_tok)
    chosen = lax.dynamic_slice_in_dim(chosen_blk, blk_at * count_tok, count_tok)
    grad_probs = chosen * grad_gates
    grad_logits = (
        router_probs * (grad_probs - jnp.sum(router_probs * grad_probs, axis=1, keepdims=True))
    ).astype(BF16)
    grad_hidden_two = dx_sum + dot_nt(grad_logits, whole_router)
    grad_router_part = dot_tn(hidden_two, grad_logits)
    grad_gain_ffn = jnp.sum(grad_hidden_two * normed_two, axis=0)
    grad_mid = own_grad.astype(F32) + norm_back(grad_hidden_two * gain_ffn, mid, scale_two)

    branch_grad = lax.all_gather(grad_mid.astype(BF16), ULY, axis=0, tiled=True)
    grad_attn = dot_nt(branch_grad, own_out).astype(BF16)
    grad_attn = to_heads(grad_attn.reshape(rows, local_heads, head_dim).transpose(1, 0, 2))
    grad_out_part = jnp.einsum("htc,td->hcd", attn_rows, branch_grad, preferred_element_type=F32)
    dq, dk, dv = attention_backward(
        q_src, kv_src, cols, grad_attn, attn_f32, lse, seg_q, seg_row, head_dim
    )
    if by_heads:
        dqkv = to_rows_back(jnp.concatenate([dq, dk, dv], axis=2))
        dq, dk, dv = jnp.split(dqkv, 3, axis=2)
    else:
        dk, dv = (lax.psum_scatter(g, "blk", scatter_dimension=1, tiled=True) for g in (dk, dv))
    dq, dk, dv = (g.transpose(1, 0, 2) for g in (dq, dk, dv))
    grad_query_norm = rotate(dq.astype(F32), cos_table, -sin_table)
    grad_key_norm = rotate(dk.astype(F32), cos_table, -sin_table)
    grad_gain_query = jnp.sum(grad_query_norm * (query_raw * query_scale), axis=(0, 1))
    grad_gain_key = jnp.sum(grad_key_norm * (key_raw * key_scale), axis=(0, 1))
    grad_projected = jnp.concatenate(
        [
            norm_back(grad_query_norm * gain_query, query_raw, query_scale)
            .reshape(rows, local_width)
            .astype(BF16),
            norm_back(grad_key_norm * gain_key, key_raw, key_scale)
            .reshape(rows, local_width)
            .astype(BF16),
            dv.reshape(rows, local_width),
        ],
        axis=1,
    )
    grad_hidden_part = dot_nt(grad_projected, own_qkv)
    grad_hidden_one = sum_scatter(grad_hidden_part, ULY)
    grad_gain_attn = jnp.sum(grad_hidden_part * normed_one, axis=0)
    grad_inputs = grad_mid + norm_back(grad_hidden_one * gain_attn, inputs, rms_scale(inputs))

    grad_qkv_part = dot_tn(hidden_one, grad_projected).astype(BF16)
    grad_qkv_rows = lax.psum_scatter(grad_qkv_part, ROWS, scatter_dimension=0, tiled=True)
    grad_qkv_rows = swap(grad_qkv_rows.reshape(uly, shard_rows, 3 * local_width), ULY)
    grad_qkv = (
        grad_qkv_rows.reshape(uly, shard_rows, 3, local_width)
        .transpose(1, 2, 0, 3)
        .reshape(shard_rows, 3 * width)
        .astype(F32)
    )
    grad_out_rows = lax.psum_scatter(
        grad_out_part.reshape(local_width, width).astype(BF16), ROWS, scatter_dimension=0, tiled=True
    )
    grad_out = lax.ppermute(grad_out_rows, ALL, [(b, a) for a, b in to_rows]).astype(F32)
    small = jnp.concatenate([grad_gain_attn[:, None], grad_gain_ffn[:, None], grad_router_part], axis=1)
    small = lax.psum_scatter(small, ALL, scatter_dimension=0, tiled=True)
    grad_qk_gain = lax.psum(jnp.stack([grad_gain_query, grad_gain_key]), ALL)

    clip_gamma = TAU / jnp.maximum(head_max, TAU)
    factor = jnp.repeat(jnp.sqrt(clip_gamma), head_dim)
    column_scale = jnp.concatenate([factor, factor, jnp.ones((width,), F32)])
    clipped = w_qkv.astype(F32) * column_scale[None, :]
    return (
        output[None],
        grad_inputs[None],
        grad_qkv,
        grad_out,
        small[:, 0],
        small[:, 1],
        grad_qk_gain,
        small[:, 2:],
        grad_gate_up,
        grad_down,
        clipped,
    )


def per_device(
    tokens, segments, routes, w_qkv, w_out, attn_gain, ffn_gain, qk_gain, router, w_gate_up, w_down, cotangent
):
    own_tokens = tokens[0]
    own_grad = cotangent[0]
    count_tok, width = own_tokens.shape
    head_dim = qk_gain.shape[1]
    heads = width // head_dim
    batch, blk, uly = lax.axis_size("batch"), lax.axis_size("blk"), spread(ULY)
    total, group = batch * blk * uly, batch * blk
    local_experts = w_down.shape[0]
    if uly != 4 or heads != blk * uly or blk < 2 or batch != 2 or local_experts % 2:
        return per_device_general(
            tokens, segments, routes, w_qkv, w_out, attn_gain, ffn_gain, qk_gain, router, w_gate_up, w_down, cotangent
        )
    blk_at, uly_at = lax.axis_index("blk"), lax.axis_index(ULY)
    rows = count_tok * uly
    seg_row = segments[0]
    length = seg_row.shape[0]
    number = router.shape[1]
    shard_rows = w_qkv.shape[0]

    to_rows = [(u * group + g, g * uly + u) for g in range(group) for u in range(uly)]
    rows_here = lax.ppermute(w_out, ALL, to_rows)
    rows_there = lax.ppermute(w_out, ALL, [(a, (b + total // 2) % total) for a, b in to_rows])


    half = local_experts // 2

    def gather_experts(gate_up, down):
        return lax.all_gather(jnp.concatenate([gate_up, down], axis=2), PLANE, axis=0, tiled=False)

    weights_first = gather_experts(w_gate_up[:half], w_down[:half])
    extra = jnp.concatenate([attn_gain[None], ffn_gain[None], router.T], axis=0)
    kept = extra.shape[0]
    extra = jnp.pad(extra, ((0, -kept % 16), (0, -shard_rows % LANES)))
    by_head = w_qkv.reshape(shard_rows, 3, heads, head_dim).transpose(2, 0, 1, 3)
    own_qkv, extras, toks = startup(
        by_head.reshape(heads, shard_rows, 3 * head_dim), extra, own_tokens, 0
    )
    rows_here, rows_there, extras, later_gate_up, later_down = lax.optimization_barrier(
        (rows_here, rows_there, extras, w_gate_up[half:], w_down[half:])
    )
    weights_second = gather_experts(later_gate_up, later_down)
    is_first = lax.axis_index("batch") == 0
    pair = jnp.stack(
        [jnp.where(is_first, rows_here, rows_there), jnp.where(is_first, rows_there, rows_here)]
    )
    own_out = lax.all_to_all(
        jnp.broadcast_to(pair[None], (blk, *pair.shape)), "blk", split_axis=0, concat_axis=0, tiled=True
    )
    own_out = own_out.transpose(1, 0, 2, 3).reshape(blk, head_dim, width)
    own_qkv = own_qkv.reshape(width, 3 * head_dim)
    extras = extras.reshape(total, *extra.shape)[:, :kept, :shard_rows]
    extras = extras.transpose(1, 0, 2).reshape(kept, width)
    gain_attn = extras[0].astype(F32)
    gain_ffn = extras[1].astype(F32)
    router_t = extras[2:]

    gains = qk_gain.astype(F32)
    cos, sin = rope_rows(length, head_dim)
    hidden_one, qkv, raw = project(
        toks.reshape(length, width), gain_attn[None], own_qkv, cos, sin, gains
    )
    attn_low, attn_f32, lse, top = attention_forward(
        qkv[None], qkv[None], (0, 1, 2), seg_row, seg_row, head_dim
    )
    (attn_rows,) = exchange([(attn_low.reshape(blk, rows, head_dim), ("blk",), "swap")], 1)
    branch = jnp.einsum("htc,hcd->td", attn_rows, own_out, preferred_element_type=F32)
    branch, grad_blk, routes_blk = exchange(
        [
            (branch.astype(BF16).reshape(uly, count_tok, width), ULY, "pairsum"),
            (own_grad, ("blk",), "line"),
            (routes[0].T, ("blk",), "gather"),
        ],
        2,
    )
    inputs = own_tokens.astype(F32)
    mid = inputs + branch

    scale_two = rms_scale(mid)
    normed_two = mid * scale_two
    hidden_two = (normed_two * gain_ffn).astype(BF16)
    hidden_blk, hidden_t, grad_t = turn_gather(hidden_two, grad_blk, 3)
    tokens_blk = blk * count_tok
    hidden_blk = hidden_blk.reshape(tokens_blk, width)
    grad_blk = grad_blk.reshape(tokens_blk, width)
    probs_blk = jax.nn.softmax(dot_nt(hidden_blk, router_t), axis=1)
    names = jnp.arange(number, dtype=jnp.int32)
    chosen_blk = jnp.any(routes_blk[:, :, :, None] == names, axis=1).astype(F32)
    chosen_blk = chosen_blk.reshape(tokens_blk, number)
    gates = lax.dynamic_slice_in_dim(
        probs_blk * chosen_blk, blk_at * local_experts, local_experts, axis=1
    )
    shared = (hidden_blk, hidden_t, grad_blk, grad_t)
    out_part, dx_part, dg_first, grads_first = experts(
        *shared, gates[:, :half], [(weights_first, 0, half)]
    )
    sums_first = lax.psum_scatter(grads_first, PLANE, scatter_dimension=0, tiled=False)
    out_part, dx_part, dg_others, grads_others = experts(
        *shared, gates[:, half:], [(weights_second, 0, half)], before=(out_part, dx_part)
    )
    sums_others = lax.psum_scatter(grads_others, PLANE, scatter_dimension=0, tiled=False)
    finished = finish_experts(sums_first, 0, local_experts)
    grad_gate_up, grad_down = finish_experts(sums_others, half, local_experts, before=finished)
    dg_part = jnp.concatenate([dg_first, dg_others], axis=0)
    dg_part = dg_part.reshape(local_experts, blk, count_tok)
    dx_parts, dg_parts = exchange(
        [
            (dx_part.reshape(blk, count_tok, width), ("blk",), "swap"),
            (dg_part.transpose(1, 0, 2), ("blk",), "swap"),
        ],
        4,
    )
    out_part = out_part.reshape(blk, count_tok, width)
    out_part, dx_parts = lax.optimization_barrier((out_part, dx_parts))
    out_parts = lax.all_to_all(out_part, "blk", split_axis=0, concat_axis=0, tiled=True)
    output = (mid + jnp.sum(out_parts.astype(F32), axis=0)).astype(BF16)
    router_probs = lax.dynamic_slice_in_dim(probs_blk, blk_at * count_tok, count_tok)
    chosen = lax.dynamic_slice_in_dim(chosen_blk, blk_at * count_tok, count_tok)
    grad_probs = chosen * dg_parts.reshape(number, count_tok).T
    grad_logits = (
        router_probs * (grad_probs - jnp.sum(router_probs * grad_probs, axis=1, keepdims=True))
    ).astype(BF16)
    grad_hidden_two = jnp.sum(dx_parts.astype(F32), axis=0) + dot_nn(grad_logits, router_t)
    grad_router_t = dot_tn(grad_logits, hidden_two)
    grad_gain_ffn = jnp.sum(grad_hidden_two * normed_two, axis=0)
    grad_mid = own_grad.astype(F32) + norm_back(grad_hidden_two * gain_ffn, mid, scale_two)

    (branch_grad,) = exchange([(grad_mid.astype(BF16), ULY, "relay")], 5)
    branch_grad, sent_qkv = lax.optimization_barrier((branch_grad, own_qkv))
    far_qkv = lax.ppermute(sent_qkv, "y", [(0, 1), (1, 0)])
    branch_grad = branch_grad.reshape(rows, width)
    grad_attn = jnp.einsum("td,hcd->htc", branch_grad, own_out, preferred_element_type=F32).astype(BF16)
    grad_out_part = jnp.einsum("htc,td->hcd", attn_rows, branch_grad, preferred_element_type=F32)
    grad_out_part = grad_out_part.astype(BF16).reshape(batch, blk, shard_rows, width)
    batch_at = lax.axis_index("batch")
    grad_attn, got_out_part = exchange(
        [
            (grad_attn, ("blk",), "swap"),
            (
                lax.dynamic_index_in_dim(grad_out_part, 1 - batch_at, 0, keepdims=False),
                ("batch",),
                "trade",
            ),
        ],
        6,
        after=[out_parts],
    )
    grad_out_part = lax.dynamic_index_in_dim(grad_out_part, batch_at, 0, keepdims=False) + got_out_part
    grad_projected, grad_gains = project_back(
        qkv, grad_attn.reshape(length, head_dim), attn_f32, lse, seg_row, raw, cos, sin, gains
    )
    grad_qkv_part = dot_tn(hidden_one, grad_projected).astype(BF16)
    by_batch = grad_qkv_part.reshape(batch, width // batch, 3 * head_dim)
    projected_blk, got_qkv_part, near_qkv, cross_qkv, grad_out_parts = exchange(
        [
            (grad_projected.reshape(blk, uly, count_tok, 3 * head_dim), ULY, "swap1"),
            (
                lax.dynamic_index_in_dim(by_batch, 1 - batch_at, 0, keepdims=False),
                ("batch",),
                "trade",
            ),
            (own_qkv, ("core",), "trade"),
            (far_qkv, ("core",), "trade"),
            (grad_out_part, ("blk",), "swap"),
        ],
        7,
    )
    grad_out = lax.ppermute(
        jnp.sum(grad_out_parts.astype(F32), axis=0).astype(BF16), ALL, [(b, a) for a, b in to_rows]
    ).astype(F32)
    grad_qkv_part = lax.dynamic_index_in_dim(by_batch, batch_at, 0, keepdims=False) + got_qkv_part

    grad_hidden_part, grad_gain_attn = hidden_back(
        projected_blk.reshape(uly, tokens_blk, 3 * head_dim),
        own_qkv,
        near_qkv,
        far_qkv,
        cross_qkv,
        hidden_one.reshape(blk, uly, count_tok, width),
    )
    grad_gain_attn = grad_gain_attn[0] / gain_attn

    small = jnp.concatenate([grad_gain_attn[None], grad_gain_ffn[None], grad_router_t], axis=0)
    beside = LANES // shard_rows
    small = jnp.pad(small, ((0, -kept % beside), (0, 0))).reshape(-1, beside, total, shard_rows)
    small = small.transpose(2, 0, 1, 3).reshape(total, -1, LANES)
    packed_rows = small.shape[1]
    head_row = jnp.where(
        jnp.arange(LANES) == uly_at * blk + blk_at, jnp.max(top) * head_dim**-0.5, NEG
    )
    to_all = jnp.concatenate([grad_gains, head_row[None]], axis=0)
    small = jnp.concatenate([small, jnp.broadcast_to(to_all[None], (total, 3, LANES))], axis=1)
    small = jnp.pad(small, ((0, 0), (0, -small.shape[1] % 8), (0, 0)))
    grad_hidden_parts, small, grad_qkv_parts = exchange(
        [
            (grad_hidden_part, ("blk",), "swap"),
            (small, ALL, "swap"),
            (grad_qkv_part.reshape(total // batch, shard_rows, 3 * head_dim), ("blk", *ULY), "swap"),
        ],
        8,
    )
    grad_qkv = merge_heads(grad_qkv_parts.reshape(blk, uly, shard_rows, 3 * head_dim))
    grad_hidden_one = jnp.sum(grad_hidden_parts.astype(F32), axis=0)
    grad_inputs = grad_mid + norm_back(grad_hidden_one * gain_attn, inputs, rms_scale(inputs))
    sums = jnp.sum(small, axis=0)
    sums, grad_gains = sums[:packed_rows], sums[packed_rows : packed_rows + 2]
    sums = sums.reshape(packed_rows * beside, shard_rows)[:kept]
    head_max = jnp.max(small[:, packed_rows + 2, :heads], axis=0)
    factor = jnp.repeat(jnp.sqrt(TAU / jnp.maximum(head_max, TAU)), head_dim)
    column_scale = jnp.concatenate([factor, factor, jnp.ones((width,), F32)])
    clipped = w_qkv.astype(F32) * column_scale[None, :]
    return (
        output[None],
        grad_inputs[None],
        grad_qkv,
        grad_out,
        sums[0],
        sums[1],
        grad_gains,
        sums[2:].T,
        grad_gate_up,
        grad_down,
        clipped,
    )


def solution(mesh):
    in_specs = (
        P("batch", ("blk", *ULY), None),
        P("batch", None),
        P("batch", ("blk", *ULY), None),
        P(ALL, None),
        P(ALL, None),
        P(ALL),
        P(ALL),
        P(),
        P(ALL, None),
        P("blk", PLANE, None),
        P("blk", PLANE, None),
        P("batch", ("blk", *ULY), None),
    )
    out_specs = (
        P("batch", ("blk", *ULY), None),
        P("batch", ("blk", *ULY), None),
        P(ALL, None),
        P(ALL, None),
        P(ALL),
        P(ALL),
        P(),
        P(ALL, None),
        P("blk", PLANE, None),
        P("blk", PLANE, None),
        P(ALL, None),
    )
    cores = 2 - mesh.shape["uly"] % 2
    mesh = Mesh(
        mesh.devices.reshape(*(mesh.shape[axis] for axis in ROWS), mesh.shape["uly"] // cores, cores), ALL
    )
    return jax.shard_map(
        per_device, mesh=mesh, in_specs=in_specs, out_specs=out_specs, check_vma=False
    )
```

```python
import functools
import math

import jax
import jax.numpy as jnp
from jax import lax
from jax.experimental import pallas as pl
from jax.experimental.pallas import tpu as pltpu
from jax.sharding import Mesh
from jax.sharding import PartitionSpec as P

EPS = 1e-06
THETA = 50000.0
TAU = 4.0
NEG = -1e30
LOG2E = 1.4426950408889634
LANES = 128
MOST_TOKENS = 512
VMEM_LIMIT = 60 * 1024 * 1024

ULY = ("y", "core")
ALL = ("batch", "blk", *ULY)
ROWS = ("batch", "blk")
PLANE = ("batch", *ULY)
CHIPS = ("batch", "y")

MESH = pl.DeviceIdType.MESH
BF16 = jnp.bfloat16
F32 = jnp.float32


def rms_scale(values):
    return lax.rsqrt(jnp.mean(values * values, axis=-1, keepdims=True) + EPS)


def norm_back(grad_normed, values, scale):
    normed = values * scale
    return scale * (grad_normed - normed * jnp.mean(grad_normed * normed, axis=-1, keepdims=True))


def rope_tables(offset, length, head_dim):
    half_dim = head_dim // 2
    frequency = THETA ** (-jnp.arange(half_dim, dtype=F32) * 2.0 / head_dim)
    positions = (offset + jnp.arange(length, dtype=jnp.int32)).astype(F32)
    angles = positions[:, None] * frequency[None, :]
    return (jnp.cos(angles)[:, None, :], jnp.sin(angles)[:, None, :])


def rope_rows(length, head_dim):
    fine = math.gcd(length, LANES)
    frequency = THETA ** (-jnp.arange(head_dim // 2, dtype=F32) * 2.0 / head_dim)
    frequency = jnp.concatenate([frequency, frequency])
    coarse_angle = (jnp.arange(length // fine, dtype=F32) * fine)[:, None, None] * frequency
    fine_angle = jnp.arange(fine, dtype=F32)[None, :, None] * frequency
    cos_a, sin_a, cos_b, sin_b = lax.optimization_barrier(
        (jnp.cos(coarse_angle), jnp.sin(coarse_angle), jnp.cos(fine_angle), jnp.sin(fine_angle))
    )
    sign = jnp.where(jnp.arange(head_dim) < head_dim // 2, -1.0, 1.0)
    cos = cos_a * cos_b - sin_a * sin_b
    sin = (sin_a * cos_b + cos_a * sin_b) * sign
    return cos.reshape(length, head_dim), sin.reshape(length, head_dim)


def rotate(values, cos_table, sin_table):
    half_dim = values.shape[-1] // 2
    first = values[..., :half_dim]
    second = values[..., half_dim:]
    return jnp.concatenate(
        [first * cos_table - second * sin_table, second * cos_table + first * sin_table], axis=-1
    )


def dot_nn(a, b):
    return lax.dot_general(a, b, (((1,), (0,)), ((), ())), preferred_element_type=F32)


def dot_nt(a, b):
    return lax.dot_general(a, b, (((1,), (1,)), ((), ())), preferred_element_type=F32)


def dot_tn(a, b):
    return lax.dot_general(a, b, (((0,), (0,)), ((), ())), preferred_element_type=F32)


def key_chunks(length):
    size = min(512, length)
    return size, length // size


def attn_fwd_kernel(factor, q_ref, k_ref, v_ref, sq_ref, sk_ref, o_ref, of_ref, lse_ref, top_ref, vt_ref):
    length = k_ref.shape[1]
    size, count = key_chunks(length)
    tile, head_dim = q_ref.shape[1:]

    @pl.when(pl.program_id(1) == 0)
    def _():
        vt_ref[...] = v_ref[0].astype(F32).T.astype(BF16)

    q = q_ref[0]
    seg_q = sq_ref[...]

    def step(j, carried):
        total, top, acc = carried
        at = pl.multiple_of(j * size, size)
        scores = dot_nt(k_ref[0, pl.ds(at, size), :], q)
        scores = jnp.where(sk_ref[pl.ds(at, size), :] == seg_q, scores, NEG)
        top = jnp.maximum(top, jnp.max(scores, axis=0, keepdims=True))
        weights = jnp.exp2(scores * factor)
        total = total + jnp.sum(weights, axis=0, keepdims=True)
        acc = acc + dot_nn(vt_ref[:, pl.ds(at, size)], weights.astype(BF16))
        return total, top, acc

    start = (
        jnp.zeros((1, tile), F32),
        jnp.full((1, tile), NEG, F32),
        jnp.zeros((head_dim, tile), F32),
    )
    total, top, acc = lax.fori_loop(0, count, step, start, unroll=count <= 4)
    out = (acc * (1.0 / total)).T
    o_ref[0] = out.astype(BF16)
    of_ref[0] = out
    lse_ref[0] = jnp.log2(total)
    top_ref[0] = top


def attn_bwd_kernel(
    factor, scale, q_ref, k_ref, v_ref, do_ref, of_ref, lse_ref, sq_ref, sk_ref,
    dq_ref, dk_ref, dv_ref, kt_ref, dk_acc, dv_acc,
):
    length = k_ref.shape[1]
    size, count = key_chunks(length)
    tile, head_dim = q_ref.shape[1:]

    @pl.when(pl.program_id(1) == 0)
    def _():
        kt_ref[...] = k_ref[0].astype(F32).T.astype(BF16)
        dk_acc[...] = jnp.zeros_like(dk_acc)
        dv_acc[...] = jnp.zeros_like(dv_acc)

    q = q_ref[0]
    grad = do_ref[0]
    seg_q = sq_ref[...]
    lse = lse_ref[0]
    row_dot = jnp.sum((grad.astype(F32) * of_ref[0]).T, axis=0, keepdims=True)

    def step(j, dq_t):
        at = pl.multiple_of(j * size, size)
        rows = pl.ds(at, size)
        scores = dot_nt(k_ref[0, rows, :], q)
        scores = jnp.where(sk_ref[rows, :] == seg_q, scores, NEG)
        weights = jnp.exp2(scores * factor - lse)
        grad_weights = dot_nt(v_ref[0, rows, :], grad)
        grad_scores = (weights * (grad_weights - row_dot)).astype(BF16)
        dk_acc[rows, :] += dot_nn(grad_scores, q)
        dv_acc[rows, :] += dot_nn(weights.astype(BF16), grad)
        return dq_t + dot_nn(kt_ref[:, rows], grad_scores)

    dq_t = lax.fori_loop(0, count, step, jnp.zeros((head_dim, tile), F32), unroll=count <= 4)
    dq_ref[0] = (dq_t * scale).T.astype(BF16)

    @pl.when(pl.program_id(1) == pl.num_programs(1) - 1)
    def _():
        dk_ref[0] = (dk_acc[...] * scale).astype(BF16)
        dv_ref[0] = dv_acc[...].astype(BF16)


def attention_tile(queries, length):
    return min(queries, 256 if length <= 4096 else 128)


def attention_forward(q_src, kv_src, cols, seg_q, seg_k, head_dim):
    heads, queries = q_src.shape[:2]
    length = kv_src.shape[1]
    tile = attention_tile(queries, length)
    q_col, k_col, v_col = cols
    factor = head_dim**-0.5 * LOG2E
    row = pl.BlockSpec((1, 1, tile), lambda h, i: (h, 0, i))
    block = pl.BlockSpec((1, tile, head_dim), lambda h, i: (h, i, 0))
    return pl.pallas_call(
        functools.partial(attn_fwd_kernel, factor),
        grid=(heads, queries // tile),
        in_specs=[
            pl.BlockSpec((1, tile, head_dim), lambda h, i: (h, i, q_col)),
            pl.BlockSpec((1, length, head_dim), lambda h, i: (h, 0, k_col)),
            pl.BlockSpec((1, length, head_dim), lambda h, i: (h, 0, v_col)),
            pl.BlockSpec((1, tile), lambda h, i: (0, i)),
            pl.BlockSpec((length, 1), lambda h, i: (0, 0)),
        ],
        out_specs=[block, block, row, row],
        out_shape=[
            jax.ShapeDtypeStruct((heads, queries, head_dim), BF16),
            jax.ShapeDtypeStruct((heads, queries, head_dim), F32),
            jax.ShapeDtypeStruct((heads, 1, queries), F32),
            jax.ShapeDtypeStruct((heads, 1, queries), F32),
        ],
        scratch_shapes=[pltpu.VMEM((head_dim, length), BF16)],
        compiler_params=pltpu.CompilerParams(vmem_limit_bytes=VMEM_LIMIT),
        cost_estimate=pl.CostEstimate(
            flops=4 * heads * queries * length * head_dim,
            bytes_accessed=heads * (queries + length) * head_dim * 8,
            transcendentals=heads * queries * length,
        ),
        name="attend",
    )(q_src, kv_src, kv_src, seg_q.reshape(1, -1), seg_k.reshape(-1, 1))


def attention_backward(q_src, kv_src, cols, grad, out_f32, lse, seg_q, seg_k, head_dim):
    heads, queries = q_src.shape[:2]
    length = kv_src.shape[1]
    tile = attention_tile(queries, length)
    q_col, k_col, v_col = cols
    scale = head_dim**-0.5
    row = pl.BlockSpec((1, 1, tile), lambda h, i: (h, 0, i))
    block = pl.BlockSpec((1, tile, head_dim), lambda h, i: (h, i, 0))
    whole = pl.BlockSpec((1, length, head_dim), lambda h, i: (h, 0, 0))
    return pl.pallas_call(
        functools.partial(attn_bwd_kernel, scale * LOG2E, scale),
        grid=(heads, queries // tile),
        in_specs=[
            pl.BlockSpec((1, tile, head_dim), lambda h, i: (h, i, q_col)),
            pl.BlockSpec((1, length, head_dim), lambda h, i: (h, 0, k_col)),
            pl.BlockSpec((1, length, head_dim), lambda h, i: (h, 0, v_col)),
            block,
            block,
            row,
            pl.BlockSpec((1, tile), lambda h, i: (0, i)),
            pl.BlockSpec((length, 1), lambda h, i: (0, 0)),
        ],
        out_specs=[block, whole, whole],
        out_shape=[
            jax.ShapeDtypeStruct((heads, queries, head_dim), BF16),
            jax.ShapeDtypeStruct((heads, length, head_dim), BF16),
            jax.ShapeDtypeStruct((heads, length, head_dim), BF16),
        ],
        scratch_shapes=[
            pltpu.VMEM((head_dim, length), BF16),
            pltpu.VMEM((length, head_dim), F32),
            pltpu.VMEM((length, head_dim), F32),
        ],
        compiler_params=pltpu.CompilerParams(vmem_limit_bytes=VMEM_LIMIT),
        cost_estimate=pl.CostEstimate(
            flops=10 * heads * queries * length * head_dim,
            bytes_accessed=heads * (queries + length) * head_dim * 12,
            transcendentals=heads * queries * length,
        ),
        name="attend_back",
    )(q_src, kv_src, kv_src, grad, out_f32, lse, seg_q.reshape(1, -1), seg_k.reshape(-1, 1))


def expert_step(expert, h_ref, ht_ref, dy_ref, dyt_ref, gate_ref, wg_ref, wu_ref, wd_ref, dg_ref, out_acc, dx_acc):
    width = h_ref.shape[1]
    cols = wg_ref.shape[3]
    w_gate = wg_ref[...].reshape(width, cols)
    w_up = wu_ref[...].reshape(width, cols)
    w_down = wd_ref[...].reshape(width, cols)
    gates = gate_ref[...]
    mine = lax.broadcasted_iota(jnp.int32, gates.shape, 1) == expert
    gate = jnp.sum(jnp.where(mine, gates, 0.0), axis=1, keepdims=True)
    a_gate = dot_nn(h_ref[...], w_gate)
    a_up = dot_nn(h_ref[...], w_up)
    raw = dot_nn(dy_ref[...], w_down)
    sigma = 1.0 / (1.0 + jnp.exp2(a_gate * -LOG2E))
    swish = a_gate * sigma
    act = swish * a_up
    dg_ref[0] += jnp.sum(raw * act, axis=1, keepdims=True)
    gated = (gate * act).astype(BF16)
    d_act = gate * raw
    d_gate = (d_act * a_up * (sigma + swish * (1.0 - sigma))).astype(BF16)
    d_up = (d_act * swish).astype(BF16)
    out_acc[...] += dot_nt(gated, w_down)
    dx_acc[...] += dot_nt(d_gate, w_gate) + dot_nt(d_up, w_up)
    for part, (left, right) in enumerate([(ht_ref, d_gate), (ht_ref, d_up), (dyt_ref, gated)]):
        yield part, dot_nn(left[...], right).astype(BF16)


def expert_kernel(more, counts, *refs):
    h_ref, ht_ref, dy_ref, dyt_ref, gate_ref = refs[:5]
    sources = [refs[5 + 3 * i : 8 + 3 * i] for i in range(len(counts))]
    out_ref, dx_ref, dg_ref, gr_ref, out_acc, dx_acc = refs[-6:]
    step, last = pl.program_id(0), pl.num_programs(0) - 1
    parts, _, part_rows, cols = sources[0][0].shape
    chunks = (last + 1) // sum(counts)

    @pl.when(step == 0)
    def _():
        if more:
            out0_ref, dx0_ref = refs[-8:-6]
            out_acc[...] = out0_ref[...].astype(F32)
            dx_acc[...] = dx0_ref[...].astype(F32)
        else:
            out_acc[...] = jnp.zeros_like(out_acc)
            dx_acc[...] = jnp.zeros_like(dx_acc)

    @pl.when(step % chunks == 0)
    def _():
        dg_ref[...] = jnp.zeros_like(dg_ref)

    begin = 0
    for source, count in zip(sources, counts):
        end = begin + count * chunks

        @pl.when((step >= begin) & (step < end))
        def _(source=source):
            for part, made in expert_step(
                step // chunks, h_ref, ht_ref, dy_ref, dyt_ref, gate_ref, *source, dg_ref, out_acc, dx_acc
            ):
                gr_ref[:, part, 0] = made.reshape(parts, part_rows, cols)

        begin = end

    @pl.when(step == last)
    def _():
        out_ref[...] = out_acc[...].astype(BF16)
        dx_ref[...] = dx_acc[...].astype(BF16)


def experts(hidden, hidden_t, grad, grad_t, gates, sources, before=()):
    tokens, width = hidden.shape
    parts, _, part_rows, units = sources[0][0].shape
    units = units // 3
    counts = [count for _, _, count in sources]
    total = sum(counts)
    cols = min(256, units)
    chunks = units // cols
    once = pl.Buffered(1)
    whole = pl.BlockSpec((tokens, width), lambda s: (0, 0), pipeline_mode=once)
    whole_t = pl.BlockSpec((width, tokens), lambda s: (0, 0), pipeline_mode=once)
    result = pl.BlockSpec((tokens, width), lambda s: (0, 0))

    def weight(source, kind):
        _, first, count = sources[source]
        begin = sum(counts[:source]) * chunks

        def index(step):
            at = jnp.clip(step - begin, 0, count * chunks - 1)
            return (0, first + at // chunks, 0, kind * chunks + at % chunks)

        return pl.BlockSpec((parts, 1, part_rows, cols), index)

    return pl.pallas_call(
        functools.partial(expert_kernel, bool(before), counts),
        grid=(total * chunks,),
        in_specs=[
            whole,
            whole_t,
            whole,
            whole_t,
            pl.BlockSpec(gates.shape, lambda s: (0, 0), pipeline_mode=once),
            *[weight(source, kind) for source in range(len(sources)) for kind in range(3)],
            *[whole for _ in before],
        ],
        out_specs=[
            result,
            result,
            pl.BlockSpec((1, tokens, 1), lambda s: (s // chunks, 0, 0)),
            pl.BlockSpec((parts, 3, 1, part_rows, cols), lambda s: (0, 0, s // chunks, 0, s % chunks)),
        ],
        out_shape=[
            jax.ShapeDtypeStruct((tokens, width), BF16),
            jax.ShapeDtypeStruct((tokens, width), BF16),
            jax.ShapeDtypeStruct((total, tokens, 1), F32),
            jax.ShapeDtypeStruct((parts, 3, total, part_rows, units), BF16),
        ],
        scratch_shapes=[
            pltpu.VMEM((tokens, width), F32),
            pltpu.VMEM((tokens, width), F32),
        ],
        compiler_params=pltpu.CompilerParams(vmem_limit_bytes=VMEM_LIMIT),
        cost_estimate=pl.CostEstimate(
            flops=18 * total * tokens * width * units,
            bytes_accessed=12 * total * width * units,
            transcendentals=total * tokens * units,
        ),
        name="experts",
    )(hidden, hidden_t, grad, grad_t, gates, *[array for array, _, _ in sources for _ in range(3)], *before)


def finish_experts_kernel(sums_ref, *refs):
    gate_up_ref, down_ref = refs[-2:]
    units = down_ref.shape[2]
    gate_up_ref[0, :, :units] = sums_ref[0, 0].astype(F32)
    gate_up_ref[0, :, units:] = sums_ref[1, 0].astype(F32)
    down_ref[0] = sums_ref[2, 0].astype(F32)


def finish_experts(sums, at, total, before=()):
    _, count, rows, units = sums.shape
    tile = min(256, rows)
    return pl.pallas_call(
        finish_experts_kernel,
        grid=(count, rows // tile),
        in_specs=[
            pl.BlockSpec((3, 1, tile, units), lambda e, r: (0, e, r, 0)),
            *[pl.BlockSpec(memory_space=pl.ANY) for _ in before],
        ],
        out_specs=[
            pl.BlockSpec((1, tile, 2 * units), lambda e, r: (at + e, r, 0)),
            pl.BlockSpec((1, tile, units), lambda e, r: (at + e, r, 0)),
        ],
        out_shape=[
            jax.ShapeDtypeStruct((total, rows, 2 * units), F32),
            jax.ShapeDtypeStruct((total, rows, units), F32),
        ],
        input_output_aliases={1 + i: i for i in range(len(before))},
        compiler_params=pltpu.CompilerParams(vmem_limit_bytes=VMEM_LIMIT),
        name="finish_experts",
    )(sums, *before)


def turn(values, cos, sin):
    return values * cos + pltpu.roll(values, values.shape[1] // 2, 1) * sin


def project_kernel(
    tok_ref, gain_ref, w_ref, cos_ref, sin_ref, gains_ref, hidden_ref, qkv_ref, raw_ref
):
    head_dim = cos_ref.shape[1]
    values = tok_ref[...].astype(F32)
    hidden = (values * rms_scale(values) * gain_ref[...]).astype(BF16)
    hidden_ref[...] = hidden
    projected = dot_nn(hidden, w_ref[...])
    raw_ref[...] = projected[:, : 2 * head_dim]
    for part in range(2):
        at = slice(part * head_dim, (part + 1) * head_dim)
        raw = projected[:, at]
        normed = raw * rms_scale(raw) * gains_ref[part : part + 1, :]
        qkv_ref[:, at] = turn(normed, cos_ref[...], sin_ref[...]).astype(BF16)
    qkv_ref[:, 2 * head_dim :] = projected[:, 2 * head_dim :].astype(BF16)


def project(toks, gain, weights, cos, sin, gains):
    length, width = toks.shape
    head_dim = cos.shape[1]
    tile = min(256, length)

    def rows(columns):
        return pl.BlockSpec((tile, columns), lambda i: (i, 0))

    def fixed(shape):
        return pl.BlockSpec(shape, lambda i: (0, 0))

    return pl.pallas_call(
        project_kernel,
        grid=(length // tile,),
        in_specs=[
            rows(width),
            fixed((1, width)),
            fixed(weights.shape),
            rows(head_dim),
            rows(head_dim),
            fixed(gains.shape),
        ],
        out_specs=[rows(width), rows(3 * head_dim), rows(2 * head_dim)],
        out_shape=[
            jax.ShapeDtypeStruct((length, width), BF16),
            jax.ShapeDtypeStruct((length, 3 * head_dim), BF16),
            jax.ShapeDtypeStruct((length, 2 * head_dim), F32),
        ],
        compiler_params=pltpu.CompilerParams(vmem_limit_bytes=VMEM_LIMIT),
        name="project",
    )(toks, gain, weights, cos, sin, gains)


def project_back_kernel(
    factor, scale, q_ref, k_ref, v_ref, do_ref, of_ref, lse_ref, sq_ref, sk_ref,
    raw_q_ref, raw_k_ref, cos_q_ref, sin_q_ref, cos_ref, sin_ref, gains_ref,
    dp_ref, dgain_ref, kt_ref, dk_acc, dv_acc,
):
    length, head_dim = k_ref.shape
    size, count = key_chunks(length)
    tile = q_ref.shape[0]
    step_at = pl.program_id(0)

    @pl.when(step_at == 0)
    def _():
        kt_ref[...] = k_ref[...].astype(F32).T.astype(BF16)
        dk_acc[...] = jnp.zeros_like(dk_acc)
        dv_acc[...] = jnp.zeros_like(dv_acc)
        dgain_ref[...] = jnp.zeros_like(dgain_ref)

    def to_raw(part, grad, raw, cos, sin):
        grad = turn(grad.astype(BF16).astype(F32), cos, -sin)
        raw_scale = rms_scale(raw)
        dgain_ref[part : part + 1, :] += jnp.sum(grad * (raw * raw_scale), axis=0, keepdims=True)
        return norm_back(grad * gains_ref[part : part + 1, :], raw, raw_scale).astype(BF16)

    q = q_ref[...]
    grad = do_ref[...]
    seg_q = sq_ref[...]
    lse = lse_ref[0]
    row_dot = jnp.sum((grad.astype(F32) * of_ref[0]).T, axis=0, keepdims=True)
    dq_t = jnp.zeros((head_dim, tile), F32)
    for j in range(count):
        rows = slice(j * size, (j + 1) * size)
        scores = dot_nt(k_ref[rows, :], q)
        scores = jnp.where(sk_ref[rows, :] == seg_q, scores, NEG)
        weights = jnp.exp2(scores * factor - lse)
        grad_weights = dot_nt(v_ref[rows, :], grad)
        grad_scores = (weights * (grad_weights - row_dot)).astype(BF16)
        dk_acc[rows, :] += dot_nn(grad_scores, q)
        dv_acc[rows, :] += dot_nn(weights.astype(BF16), grad)
        dq_t = dq_t + dot_nn(kt_ref[:, rows], grad_scores)
    own = pl.ds(pl.multiple_of(step_at * tile, tile), tile)
    dp_ref[own, :head_dim] = to_raw(
        0, (dq_t * scale).T, raw_q_ref[...], cos_q_ref[...], sin_q_ref[...]
    )

    @pl.when(step_at == pl.num_programs(0) - 1)
    def _():
        dp_ref[:, head_dim : 2 * head_dim] = to_raw(
            1, dk_acc[...] * scale, raw_k_ref[...], cos_ref[...], sin_ref[...]
        )
        dp_ref[:, 2 * head_dim :] = dv_acc[...].astype(BF16)


def project_back(qkv, grad, out_f32, lse, segments, raw, cos, sin, gains):
    length, head_dim = grad.shape
    tile = min(256, length)

    def rows(column):
        return pl.BlockSpec((tile, head_dim), lambda i: (i, column))

    def whole(column):
        return pl.BlockSpec((length, head_dim), lambda i: (0, column))

    return pl.pallas_call(
        functools.partial(project_back_kernel, head_dim**-0.5 * LOG2E, head_dim**-0.5),
        grid=(length // tile,),
        in_specs=[
            rows(0),
            whole(1),
            whole(2),
            rows(0),
            pl.BlockSpec((1, tile, head_dim), lambda i: (0, i, 0)),
            pl.BlockSpec((1, 1, tile), lambda i: (0, 0, i)),
            pl.BlockSpec((1, tile), lambda i: (0, i)),
            pl.BlockSpec((length, 1), lambda i: (0, 0)),
            rows(0),
            whole(1),
            rows(0),
            rows(0),
            whole(0),
            whole(0),
            pl.BlockSpec(gains.shape, lambda i: (0, 0)),
        ],
        out_specs=[
            pl.BlockSpec((length, 3 * head_dim), lambda i: (0, 0)),
            pl.BlockSpec((2, head_dim), lambda i: (0, 0)),
        ],
        out_shape=[
            jax.ShapeDtypeStruct((length, 3 * head_dim), BF16),
            jax.ShapeDtypeStruct((2, head_dim), F32),
        ],
        scratch_shapes=[
            pltpu.VMEM((head_dim, length), BF16),
            pltpu.VMEM((length, head_dim), F32),
            pltpu.VMEM((length, head_dim), F32),
        ],
        compiler_params=pltpu.CompilerParams(vmem_limit_bytes=VMEM_LIMIT),
        cost_estimate=pl.CostEstimate(
            flops=10 * length * length * head_dim,
            bytes_accessed=length * head_dim * 40,
            transcendentals=length * length,
        ),
        name="project_back",
    )(
        qkv, qkv, qkv, grad, out_f32, lse, segments.reshape(1, -1), segments.reshape(-1, 1),
        raw, raw, cos, sin, cos, sin, gains,
    )


def hidden_back_kernel(grads_ref, own_ref, near_ref, far_ref, cross_ref, hidden_ref, out_ref, gain_ref):
    uly = grads_ref.shape[0]
    u = lax.axis_index(ULY)
    near = u + 1 - 2 * lax.rem(u, 2)
    total = dot_nt(grads_ref[u], own_ref[...])
    total = total + dot_nt(grads_ref[near], near_ref[...])
    total = total + dot_nt(grads_ref[lax.rem(u + 2, uly)], far_ref[...])
    total = total + dot_nt(grads_ref[lax.rem(near + 2, uly)], cross_ref[...])
    out_ref[...] = total.astype(BF16).reshape(out_ref.shape)
    hidden = hidden_ref[...].reshape(total.shape).astype(F32)
    gain_ref[...] = jnp.sum(total * hidden, axis=0, keepdims=True)


def hidden_back(grads, own, near, far, cross, hidden):
    uly, tokens, columns = grads.shape
    blk, _, rows, width = hidden.shape
    tile = min(512, width)
    weights = pl.BlockSpec((tile, columns), lambda n: (n, 0))
    return pl.pallas_call(
        hidden_back_kernel,
        grid=(width // tile,),
        in_specs=[
            pl.BlockSpec(grads.shape, lambda n: (0, 0, 0)),
            *[weights] * 4,
            pl.BlockSpec((blk, 1, rows, tile), lambda n: (0, lax.axis_index(ULY), 0, n)),
        ],
        out_specs=[
            pl.BlockSpec((blk, rows, tile), lambda n: (0, 0, n)),
            pl.BlockSpec((1, tile), lambda n: (0, n)),
        ],
        out_shape=[
            jax.ShapeDtypeStruct((blk, rows, width), BF16),
            jax.ShapeDtypeStruct((1, width), F32),
        ],
        compiler_params=pltpu.CompilerParams(vmem_limit_bytes=VMEM_LIMIT),
        name="hidden_back",
    )(grads, own, near, far, cross, hidden)


def merge_heads_kernel(parts_ref, out_ref):
    blk, uly, _, columns = parts_ref.shape
    head_dim = columns // 3
    heads = blk * uly
    for z in range(blk):
        for u in range(uly):
            head = parts_ref[z, u].astype(F32)
            for part in range(3):
                at = (part * heads + u * blk + z) * head_dim
                out_ref[:, at : at + head_dim] = head[:, part * head_dim : (part + 1) * head_dim]


def merge_heads(parts):
    blk, uly, rows, columns = parts.shape
    return pl.pallas_call(
        merge_heads_kernel,
        out_shape=jax.ShapeDtypeStruct((rows, blk * uly * columns), F32),
        compiler_params=pltpu.CompilerParams(vmem_limit_bytes=VMEM_LIMIT),
        name="merge_heads",
    )(parts)


def swap(values, axis):
    return lax.all_to_all(values, axis, split_axis=0, concat_axis=0, tiled=True)


def sum_scatter(values, axis):
    count = spread(axis) if isinstance(axis, tuple) else lax.axis_size(axis)
    rows, width = values.shape
    parts = swap(values.astype(BF16).reshape(count, rows // count, width), axis)
    return jnp.sum(parts.astype(F32), axis=0)


def place(axes, index):
    found = {}
    for axis in reversed(axes):
        size = lax.axis_size(axis)
        found[axis] = lax.rem(index, size)
        index = index // size
    return found


def spread(axes):
    return math.prod(lax.axis_size(axis) for axis in axes)


def each(count, body):
    if count <= 4:
        for step in range(1, count):
            body(step)
    else:

        def looped(step, carried):
            body(step)
            return carried

        lax.fori_loop(1, count, looped, 0)


def ahead(index, step, size):
    return lax.rem(index + step, size)


def exchange(items, collective_id, after=()):
    count = len(items)
    sizes = [spread(axes) for _, axes, _ in items]
    groups = list(dict.fromkeys(axes for _, axes, _ in items))
    bases = [sum(2 * size for size in sizes[:i]) for i in range(count)]

    def kernel(*refs):
        ins = refs[:count]
        outs = refs[count + len(after) : 2 * count + len(after)]
        send, recv, local = refs[2 * count + len(after) :][:3]
        barrier = pltpu.get_barrier_semaphore()
        for axes in groups:
            size, me = spread(axes), lax.axis_index(axes)

            def greet(step, axes=axes, size=size, me=me):
                pl.semaphore_signal(
                    barrier, inc=1, device_id=place(axes, ahead(me, step, size)), device_id_type=MESH
                )

            each(size, greet)
        pl.semaphore_wait(barrier, sum(spread(axes) - 1 for axes in groups))

        def block(i, peer):
            if items[i][2] == "swap":
                return ins[i].at[peer]
            return ins[i].at[:, peer] if items[i][2] == "swap1" else ins[i]

        def remote(i, step):
            _, axes, kind = items[i]
            me = lax.axis_index(axes)
            if kind == "trade":
                return pltpu.make_async_remote_copy(
                    src_ref=ins[i],
                    dst_ref=outs[i],
                    send_sem=send.at[bases[i] + 1],
                    recv_sem=recv.at[bases[i] + 1],
                    device_id=place(axes, 1 - me),
                    device_id_type=MESH,
                )
            if kind == "relay":
                far, near = lax.rem(me + 2, 4), me + 1 - 2 * lax.rem(me, 2)
                held = far if step == 3 else me
                return pltpu.make_async_remote_copy(
                    src_ref=outs[i].at[far] if step == 3 else ins[i],
                    dst_ref=outs[i].at[held],
                    send_sem=send.at[bases[i] + step],
                    recv_sem=recv.at[bases[i] + step],
                    device_id=place(axes, far if step == 1 else near),
                    device_id_type=MESH,
                )
            peer = ahead(me, step, sizes[i])
            return pltpu.make_async_remote_copy(
                src_ref=block(i, peer),
                dst_ref=outs[i].at[me],
                send_sem=send.at[bases[i] + step],
                recv_sem=recv.at[bases[i] + step],
                device_id=place(axes, peer),
                device_id_type=MESH,
            )

        def own(i):
            _, axes, kind = items[i]
            me = lax.axis_index(axes)
            return pltpu.make_async_copy(
                block(i, me), outs[i].at[me], local.at[i]
            )

        def hop(i, up, hops):
            (axis,) = items[i][1]
            me, size = lax.axis_index(axis), sizes[i]
            way = 1 if up else -1
            held, to = me - way * hops, me + way
            exists = (held >= 0) & (held < size) & (to >= 0) & (to < size)
            held, to = jnp.clip(held, 0, size - 1), jnp.clip(to, 0, size - 1)
            sem = bases[i] + (size if up else 0) + hops
            copy = pltpu.make_async_remote_copy(
                src_ref=outs[i].at[held] if hops else ins[i],
                dst_ref=outs[i].at[held],
                send_sem=send.at[sem],
                recv_sem=recv.at[sem],
                device_id={axis: to},
                device_id_type=MESH,
            )
            return exists, copy

        def arrival(i, up, hops):
            (axis,) = items[i][1]
            me, size = lax.axis_index(axis), sizes[i]
            way = 1 if up else -1
            held, sender = me - way * (hops + 1), me - way
            exists = (held >= 0) & (held < size)
            held, sender = jnp.clip(held, 0, size - 1), jnp.clip(sender, 0, size - 1)
            sem = bases[i] + (size if up else 0) + hops
            copy = pltpu.make_async_remote_copy(
                src_ref=ins[i],
                dst_ref=outs[i].at[held],
                send_sem=send.at[sem],
                recv_sem=recv.at[sem],
                device_id={axis: sender},
                device_id_type=MESH,
            )
            return exists, copy

        def kinds(*names):
            return [i for i in range(count) if items[i][2] in names]

        def when(pair, act):
            exists, copy = pair
            pl.when(exists)(lambda: act(copy))

        def pairsum(i):
            me = lax.axis_index(ULY)
            far, near = lax.rem(me + 2, 4), me + 1 - 2 * lax.rem(me, 2)
            own, out = ins[i], outs[i]
            got_near, got_far, sent = refs[2 * count + len(after) + 3 :]

            def copy(at, src, dst, to):
                return pltpu.make_async_remote_copy(
                    src_ref=src,
                    dst_ref=dst,
                    send_sem=send.at[bases[i] + at],
                    recv_sem=recv.at[bases[i] + at],
                    device_id=place(ULY, to),
                    device_id_type=MESH,
                )

            to_near = [
                copy(0, own.at[near], got_near.at[0], near),
                copy(1, own.at[lax.rem(near + 2, 4)], got_near.at[1], near),
            ]
            to_far = copy(2, sent, got_far, far)

            def first():
                for sending in to_near:
                    sending.start()

            def second():
                for sending in to_near:
                    sending.wait()
                sent[...] = (own[far].astype(F32) + got_near[1].astype(F32)).astype(BF16)
                to_far.start()
                out[...] = own[me].astype(F32) + got_near[0].astype(F32)

            def third():
                to_far.wait()
                out[...] += got_far[...].astype(F32)

            return first, second, third

        ways = (True, False)
        sums = [pairsum(i) for i in kinds("pairsum")]
        for first, _, _ in sums:
            first()
        for i in kinds("line"):
            for up in ways:
                when(hop(i, up, 0), lambda copy: copy.start())
        for i in kinds("gather", "swap", "swap1", "relay", "trade"):
            each(3 if items[i][2] == "relay" else sizes[i], lambda step, i=i: remote(i, step).start())
        for i in kinds("gather", "swap", "swap1", "relay", "line"):
            own(i).start()
        for _, second, _ in sums:
            second()
        for i in kinds("line"):
            for hops in range(1, sizes[i]):
                for up in ways:
                    when(arrival(i, up, hops - 1), lambda copy: copy.wait_recv())
                    if hops < sizes[i] - 1:
                        when(hop(i, up, hops), lambda copy: copy.start())
        for i in kinds("relay"):
            remote(i, 1).wait_recv()
            remote(i, 3).start()
            remote(i, 1).wait_send()
            for step in (2, 3):
                remote(i, step).wait()
        for i in kinds("gather", "swap", "swap1", "trade"):
            each(sizes[i], lambda step, i=i: remote(i, step).wait())
        for i in kinds("line"):
            for hops in range(sizes[i] - 1):
                for up in ways:
                    when(hop(i, up, hops), lambda copy: copy.wait_send())
        for i in kinds("gather", "swap", "swap1", "relay", "line"):
            own(i).wait()
        for _, _, third in sums:
            third()


    def shape_of(size, array, kind):
        if kind in ("trade", "pairsum"):
            return array.shape[kind == "pairsum" :]
        dropped = {"swap": 0, "swap1": 1}.get(kind)
        return (size, *(extent for at, extent in enumerate(array.shape) if at != dropped))

    anywhere, close = pl.BlockSpec(memory_space=pl.ANY), pl.BlockSpec(memory_space=pltpu.VMEM)
    specs = [close if kind == "pairsum" else anywhere for _, _, kind in items]
    held = []
    for array, _, kind in items:
        if kind == "pairsum":
            held = [pltpu.VMEM((*more, *array.shape[1:]), BF16) for more in ((2,), (), ())]
    return pl.pallas_call(
        kernel,
        in_specs=specs + [anywhere] * len(after),
        out_specs=specs,
        out_shape=[
            jax.ShapeDtypeStruct(shape_of(size, array, kind), F32 if kind == "pairsum" else array.dtype)
            for size, (array, _, kind) in zip(sizes, items)
        ],
        scratch_shapes=[
            pltpu.SemaphoreType.DMA((2 * sum(sizes),)),
            pltpu.SemaphoreType.DMA((2 * sum(sizes),)),
            pltpu.SemaphoreType.DMA((count,)),
            *held,
        ],
        compiler_params=pltpu.CompilerParams(
            collective_id=collective_id, has_side_effects=True, vmem_limit_bytes=VMEM_LIMIT if held else None
        ),
        name="exchange",
    )(*[item[0] for item in items], *after)


def turn_gather_kernel(
    own_ref, other_ref, all_ref, all_t_ref, other_t_ref, block, turned, send, recv, local
):
    size, me = lax.axis_size("blk"), lax.axis_index("blk")
    rows = own_ref.shape[0]
    barrier = pltpu.get_barrier_semaphore()
    ways = (1, 0)

    def neighbour(up):
        to = me + (1 if up else -1)
        return (to >= 0) & (to < size), jnp.clip(to, 0, size - 1)

    def greet(step):
        pl.semaphore_signal(
            barrier, inc=1, device_id={"blk": ahead(me, step, size)}, device_id_type=MESH
        )

    each(size, greet)
    pl.semaphore_wait(barrier, size - 1)

    def hop(up, hops):
        held = me - (1 if up else -1) * hops
        exists, to = neighbour(up)
        exists = exists & (held >= 0) & (held < size)
        held = jnp.clip(held, 0, size - 1)
        return exists, pltpu.make_async_remote_copy(
            src_ref=all_ref.at[held] if hops else own_ref,
            dst_ref=all_ref.at[held],
            send_sem=send.at[up * size + hops],
            recv_sem=recv.at[up * size + hops],
            device_id={"blk": to},
            device_id_type=MESH,
        )

    def arrival(up, hops):
        held = me - (1 if up else -1) * (hops + 1)
        exists = (held >= 0) & (held < size)
        held = jnp.clip(held, 0, size - 1)
        return exists, held, pltpu.make_async_remote_copy(
            src_ref=own_ref,
            dst_ref=all_ref.at[held],
            send_sem=send.at[up * size + hops],
            recv_sem=recv.at[up * size + hops],
            device_id={"blk": neighbour(1 - up)[1]},
            device_id_type=MESH,
        )

    def when(pair, act):
        exists, copy = pair
        pl.when(exists)(lambda: act(copy))

    def turn(src, dst, at):
        take = pltpu.make_async_copy(src, block, local.at[0])
        take.start()
        take.wait()
        turned[...] = block[...].T
        columns = pl.ds(pl.multiple_of(at * rows, rows), rows)
        give = pltpu.make_async_copy(turned, dst.at[:, columns], local.at[1])
        give.start()
        give.wait()

    for up in ways:
        when(hop(up, 0), lambda copy: copy.start())
    keep = pltpu.make_async_copy(own_ref, all_ref.at[me], local.at[2])
    keep.start()
    turn(own_ref, all_t_ref, me)
    for at in range(size):
        turn(other_ref.at[at], other_t_ref, at)
    for hops in range(1, size):
        for up in ways:
            exists, held, copy = arrival(up, hops - 1)

            @pl.when(exists)
            def _(copy=copy, up=up, hops=hops):
                copy.wait_recv()
                if hops < size - 1:
                    when(hop(up, hops), lambda copy: copy.start())

        for up in ways:
            exists, held, copy = arrival(up, hops - 1)
            pl.when(exists)(lambda held=held: turn(all_ref.at[held], all_t_ref, held))
    for hops in range(size - 1):
        for up in ways:
            when(hop(up, hops), lambda copy: copy.wait_send())
    keep.wait()


def turn_gather(own, other, collective_id, after=()):
    size = lax.axis_size("blk")
    rows, width = own.shape
    anywhere = pl.BlockSpec(memory_space=pl.ANY)

    def kernel(*refs):
        turn_gather_kernel(*refs[:2], *refs[2 + len(after) :])

    return pl.pallas_call(
        kernel,
        in_specs=[anywhere] * (2 + len(after)),
        out_specs=[anywhere] * 3,
        out_shape=[
            jax.ShapeDtypeStruct((size, rows, width), BF16),
            jax.ShapeDtypeStruct((width, size * rows), BF16),
            jax.ShapeDtypeStruct((width, size * rows), BF16),
        ],
        scratch_shapes=[
            pltpu.VMEM((rows, width), BF16),
            pltpu.VMEM((width, rows), BF16),
            pltpu.SemaphoreType.DMA((2 * size,)),
            pltpu.SemaphoreType.DMA((2 * size,)),
            pltpu.SemaphoreType.DMA((3,)),
        ],
        compiler_params=pltpu.CompilerParams(
            collective_id=collective_id, has_side_effects=True, vmem_limit_bytes=VMEM_LIMIT
        ),
        name="turn_gather",
    )(own, other, *after)


def startup_kernel(
    head_ref, extra_ref, tok_ref, heads_ref, extras_ref, toks_ref,
    head_send, head_recv, extra_send, extra_recv, trade_send, trade_recv,
    z_send, z_recv, ay_send, ay_recv, by_send, by_recv, c_send, c_recv, local,
):
    blk, uly = lax.axis_size("blk"), spread(ULY)
    total = spread(ALL)
    z, u, me = lax.axis_index("blk"), lax.axis_index(ULY), lax.axis_index(ALL)
    far = lax.rem(u + 2, uly)
    near = u + 1 - 2 * lax.rem(u, 2)
    half = tok_ref.shape[0] // 2
    parts = (pl.ds(0, half), pl.ds(half, half))

    barrier = pltpu.get_barrier_semaphore()

    def greet(step):
        pl.semaphore_signal(
            barrier, inc=1, device_id=place(ALL, ahead(me, step, total)), device_id_type=MESH
        )

    each(total, greet)
    pl.semaphore_wait(barrier, total - 1)

    def send(src, dst, sent, got, to):
        return pltpu.make_async_remote_copy(
            src_ref=src, dst_ref=dst, send_sem=sent, recv_sem=got, device_id=to, device_id_type=MESH
        )

    def block(step, other, part):
        at = toks_ref.at[ahead(z, step, blk), far if other else u, parts[part]]
        return (tok_ref.at[parts[part]] if step == 0 and not other else at), at

    streams = ((0, 0), (0, 1), (1, 1))

    def hop(stream, up, hops):
        other, part = streams[stream]
        way = 1 if up else -1
        held, to = z - way * hops, z + way
        exists = (held >= 0) & (held < blk) & (to >= 0) & (to < blk)
        held, to = jnp.clip(held, 0, blk - 1), jnp.clip(to, 0, blk - 1)
        at = toks_ref.at[held, far if other else u, parts[part]]
        src = tok_ref.at[parts[part]] if hops == 0 and not other else at
        sem = (2 * stream + up) * blk + hops
        return exists, send(src, at, z_send.at[sem], z_recv.at[sem], {"blk": to})

    def arrival(stream, up, hops):
        other, part = streams[stream]
        way = 1 if up else -1
        held, sender = z - way * (hops + 1), z - way
        exists = (held >= 0) & (held < blk)
        held, sender = jnp.clip(held, 0, blk - 1), jnp.clip(sender, 0, blk - 1)
        at = toks_ref.at[held, far if other else u, parts[part]]
        sem = (2 * stream + up) * blk + hops
        return exists, send(tok_ref.at[parts[part]], at, z_send.at[sem], z_recv.at[sem], {"blk": sender})

    def when(pair, act):
        exists, copy = pair
        pl.when(exists)(lambda: act(copy))

    def a_y(step):
        return send(*block(step, 0, 0), ay_send.at[step], ay_recv.at[step], place(ULY, far))

    def b_y():
        return send(*block(0, 0, 1), by_send.at[0], by_recv.at[0], place(ULY, far))

    def to_near(step, other, part):
        sem = 4 * step + 2 * other + part
        return send(*block(step, other, part), c_send.at[sem], c_recv.at[sem], place(ULY, near))

    group = ("blk", *ULY)
    mine, here, b = lax.axis_index(group), spread(group), lax.axis_index("batch")

    def head(step):
        to = place(group, ahead(mine, step, here))
        src = head_ref.at[(to["y"] * lax.axis_size("core") + to["core"]) * blk + to["blk"]]
        return send(src, heads_ref.at[b, mine], head_send.at[step], head_recv.at[step], to)

    def extra(step):
        to = place(group, ahead(mine, step, here))
        return send(extra_ref, extras_ref.at[b, mine], extra_send.at[step], extra_recv.at[step], to)

    def trade(which):
        ref = (heads_ref, extras_ref)[which].at[b]
        return send(ref, ref, trade_send.at[which], trade_recv.at[which], {"batch": 1 - b})

    own = [
        pltpu.make_async_copy(tok_ref, toks_ref.at[z, u], local.at[0]),
        pltpu.make_async_copy(head_ref.at[u * blk + z], heads_ref.at[b, mine], local.at[1]),
        pltpu.make_async_copy(extra_ref, extras_ref.at[b, mine], local.at[2]),
    ]

    def start_head(step):
        extra(step).start()
        head(step).start()

    ways = (1, 0)
    b_y().start()
    for stream in range(2):
        for up in ways:
            when(hop(stream, up, 0), lambda copy: copy.start())
    a_y(0).start()
    to_near(0, 0, 0).start()
    to_near(0, 0, 1).start()

    each(here, start_head)
    for copy in own:
        copy.start()
    b_y().wait_recv()
    for up in ways:
        when(hop(2, up, 0), lambda copy: copy.start())
    to_near(0, 1, 1).start()
    def wait_head(step):
        extra(step).wait()
        head(step).wait()

    for hops in range(1, blk):
        if hops == min(2, blk - 1):
            each(here, wait_head)
            for copy in own[1:]:
                copy.wait()
            trade(0).start()
            trade(1).start()
        for stream, (other, part) in enumerate(streams):
            for up in ways:
                exists, copy = arrival(stream, up, hops - 1)
                step = blk - hops if up else hops

                @pl.when(exists)
                def _(copy=copy, stream=stream, other=other, part=part, up=up, step=step, hops=hops):
                    copy.wait_recv()
                    if hops < blk - 1:
                        when(hop(stream, up, hops), lambda copy: copy.start())
                    if stream == 0:
                        a_y(step).start()
                    to_near(step, other, part).start()

    for step in [0, *reversed(range(1, blk))]:
        a_y(step).wait_recv()
        to_near(step, 1, 0).start()
    for step in range(blk):
        for other in range(2):
            for part in range(2):
                to_near(step, other, part).wait_recv()

    trade(0).wait()
    trade(1).wait()
    own[0].wait()
    b_y().wait_send()
    for hops in range(blk - 1):
        for stream in range(3):
            for up in ways:
                when(hop(stream, up, hops), lambda copy: copy.wait_send())
    for step in range(blk):
        a_y(step).wait_send()
        for other in range(2):
            for part in range(2):
                to_near(step, other, part).wait_send()


def startup(heads, extra, tok, collective_id):
    batch, blk, uly = lax.axis_size("batch"), lax.axis_size("blk"), spread(ULY)
    anywhere = pl.BlockSpec(memory_space=pl.ANY)
    dma = pltpu.SemaphoreType.DMA
    return pl.pallas_call(
        startup_kernel,
        in_specs=[anywhere] * 3,
        out_specs=[anywhere] * 3,
        out_shape=[
            jax.ShapeDtypeStruct((batch, blk * uly, *heads.shape[1:]), BF16),
            jax.ShapeDtypeStruct((batch, blk * uly, *extra.shape), BF16),
            jax.ShapeDtypeStruct((blk, uly, *tok.shape), BF16),
        ],
        scratch_shapes=[
            *[dma((blk * uly,))] * 4,
            *[dma((2,))] * 2,
            *[dma((6 * blk,))] * 2,
            *[dma((blk,))] * 2,
            *[dma((1,))] * 2,
            *[dma((4 * blk,))] * 2,
            dma((3,)),
        ],
        compiler_params=pltpu.CompilerParams(collective_id=collective_id, has_side_effects=True),
        name="startup",
    )(heads, extra, tok)


def per_device_general(
    tokens, segments, routes, w_qkv, w_out, attn_gain, ffn_gain, qk_gain, router, w_gate_up, w_down, cotangent
):
    own_tokens = tokens[0]
    own_grad = cotangent[0]
    count_tok, width = own_tokens.shape
    head_dim = qk_gain.shape[1]
    heads = width // head_dim
    uly, blk, batch = spread(ULY), lax.axis_size("blk"), lax.axis_size("batch")
    blk_at, uly_at = lax.axis_index("blk"), lax.axis_index(ULY)
    group = batch * blk
    local_heads = heads // uly
    local_width = local_heads * head_dim
    rows = count_tok * uly
    seg_row = segments[0]
    length = seg_row.shape[0]
    number = router.shape[1]
    local_experts, _, units = w_down.shape
    shard_rows = w_qkv.shape[0]

    extra = jnp.concatenate([attn_gain[:, None], ffn_gain[:, None], router], axis=1)
    extra = jnp.pad(extra, ((0, 0), (0, LANES - extra.shape[1])))
    columns = w_qkv.reshape(shard_rows, 3, uly, local_width).transpose(2, 0, 1, 3)
    packed = jnp.concatenate(
        [
            columns.reshape(uly, shard_rows, 3 * local_width),
            jnp.broadcast_to(extra[None], (uly, shard_rows, LANES)),
        ],
        axis=2,
    )
    packed = swap(packed, ULY).reshape(uly * shard_rows, 3 * local_width + LANES)
    packed = lax.all_gather(packed, ROWS, axis=0, tiled=True)
    own_qkv = packed[:, : 3 * local_width]
    gain_attn = packed[:, 3 * local_width].astype(F32)
    gain_ffn = packed[:, 3 * local_width + 1].astype(F32)
    whole_router = packed[:, 3 * local_width + 2 : 3 * local_width + 2 + number]
    tokens_all = lax.all_gather(own_tokens, ULY, axis=0, tiled=True)
    to_rows = [(u * group + g, g * uly + u) for g in range(group) for u in range(uly)]
    own_out = lax.all_gather(lax.ppermute(w_out, ALL, to_rows), ROWS, axis=0, tiled=True)
    whole_gate_up = lax.all_gather(w_gate_up, PLANE, axis=0, tiled=False)
    whole_down = lax.all_gather(w_down, PLANE, axis=0, tiled=False)
    grad_blk = lax.all_gather(own_grad, "blk", axis=0, tiled=True)
    routes_blk = lax.all_gather(routes[0], "blk", axis=0, tiled=True)

    gain_query = qk_gain[0].astype(F32)
    gain_key = qk_gain[1].astype(F32)
    inputs_all = tokens_all.astype(F32)
    normed_one = inputs_all * rms_scale(inputs_all)
    hidden_one = (normed_one * gain_attn).astype(BF16)
    projected = dot_nn(hidden_one, own_qkv)
    query_raw = projected[:, :local_width].reshape(rows, local_heads, head_dim)
    key_raw = projected[:, local_width : 2 * local_width].reshape(rows, local_heads, head_dim)
    value_raw = projected[:, 2 * local_width :].reshape(rows, local_heads, head_dim)
    cos_table, sin_table = rope_tables(blk_at * rows, rows, head_dim)
    query_scale = rms_scale(query_raw)
    key_scale = rms_scale(key_raw)
    qkv = jnp.concatenate(
        [
            rotate(query_raw * query_scale * gain_query, cos_table, sin_table),
            rotate(key_raw * key_scale * gain_key, cos_table, sin_table),
            value_raw,
        ],
        axis=2,
    ).astype(BF16)
    qkv = qkv.transpose(1, 0, 2)

    by_heads = local_heads % blk == 0
    if by_heads:
        per = local_heads // blk

        def to_heads(values):
            columns = values.shape[2]
            moved = swap(values.reshape(blk, per, rows, columns), "blk")
            return moved.transpose(1, 0, 2, 3).reshape(per, length, columns)

        def to_rows_back(values):
            columns = values.shape[2]
            parts = values.reshape(per, blk, rows, columns).transpose(1, 0, 2, 3)
            return swap(parts, "blk").reshape(local_heads, rows, columns)

        q_src = kv_src = to_heads(qkv)
        cols = (0, 1, 2)
        seg_q = seg_row
        first_head = uly_at * local_heads + blk_at * per
    else:

        def to_heads(values):
            return values

        def to_rows_back(values):
            return values

        q_src = qkv
        kv_src = lax.all_gather(qkv[:, :, head_dim:], "blk", axis=1, tiled=True)
        cols = (0, 0, 1)
        seg_q = lax.dynamic_slice_in_dim(seg_row, blk_at * rows, rows)
        first_head = uly_at * local_heads
    attn_low, attn_f32, lse, top = attention_forward(q_src, kv_src, cols, seg_q, seg_row, head_dim)
    head_vector = lax.dynamic_update_slice_in_dim(
        jnp.full((heads,), NEG, F32), jnp.max(top, axis=(1, 2)) * head_dim**-0.5, first_head, 0
    )
    head_max = lax.pmax(head_vector, ALL)
    attn_rows = to_rows_back(attn_low)
    out_heads = own_out.reshape(local_heads, head_dim, width)
    branch = jnp.einsum("htc,hcd->td", attn_rows, out_heads, preferred_element_type=F32)
    inputs = own_tokens.astype(F32)
    mid = inputs + sum_scatter(branch, ULY)

    scale_two = rms_scale(mid)
    normed_two = mid * scale_two
    hidden_two = (normed_two * gain_ffn).astype(BF16)
    hidden_blk = lax.all_gather(hidden_two, "blk", axis=0, tiled=True)
    probs_blk = jax.nn.softmax(dot_nn(hidden_blk, whole_router), axis=1)
    names = jnp.arange(number, dtype=jnp.int32)
    chosen_blk = jnp.any(routes_blk[:, :, None] == names, axis=1).astype(F32)
    own_names = blk_at * local_experts
    gates = lax.dynamic_slice_in_dim(probs_blk * chosen_blk, own_names, local_experts, axis=1)
    most = min(MOST_TOKENS, hidden_blk.shape[0])
    packed_weights = jnp.concatenate([whole_gate_up, whole_down], axis=3)
    made = []
    for at in range(0, hidden_blk.shape[0], most):
        hidden_part, grad_part = hidden_blk[at : at + most], grad_blk[at : at + most]
        made.append(
            experts(
                hidden_part,
                hidden_part.T,
                grad_part,
                grad_part.T,
                gates[at : at + most],
                [(packed_weights, 0, local_experts)],
            )
        )
    out_part = jnp.concatenate([m[0] for m in made], axis=0)
    dx_part = jnp.concatenate([m[1] for m in made], axis=0)
    dg_part = jnp.concatenate([m[2] for m in made], axis=1)
    expert_grads = sum(m[3].astype(F32) for m in made).astype(BF16)
    expert_sums = lax.psum_scatter(expert_grads, PLANE, scatter_dimension=0, tiled=False).astype(F32)
    grad_gate_up = jnp.concatenate([expert_sums[0], expert_sums[1]], axis=2)
    grad_down = expert_sums[2]
    dg_parts = swap(dg_part.reshape(local_experts, blk, count_tok).transpose(1, 2, 0), "blk")
    grad_gates = dg_parts.transpose(1, 0, 2).reshape(count_tok, number)
    dx_sum = sum_scatter(dx_part, "blk")
    output = (mid + sum_scatter(out_part, "blk")).astype(BF16)
    router_probs = lax.dynamic_slice_in_dim(probs_blk, blk_at * count_tok, count_tok)
    chosen = lax.dynamic_slice_in_dim(chosen_blk, blk_at * count_tok, count_tok)
    grad_probs = chosen * grad_gates
    grad_logits = (
        router_probs * (grad_probs - jnp.sum(router_probs * grad_probs, axis=1, keepdims=True))
    ).astype(BF16)
    grad_hidden_two = dx_sum + dot_nt(grad_logits, whole_router)
    grad_router_part = dot_tn(hidden_two, grad_logits)
    grad_gain_ffn = jnp.sum(grad_hidden_two * normed_two, axis=0)
    grad_mid = own_grad.astype(F32) + norm_back(grad_hidden_two * gain_ffn, mid, scale_two)

    branch_grad = lax.all_gather(grad_mid.astype(BF16), ULY, axis=0, tiled=True)
    grad_attn = dot_nt(branch_grad, own_out).astype(BF16)
    grad_attn = to_heads(grad_attn.reshape(rows, local_heads, head_dim).transpose(1, 0, 2))
    grad_out_part = jnp.einsum("htc,td->hcd", attn_rows, branch_grad, preferred_element_type=F32)
    dq, dk, dv = attention_backward(
        q_src, kv_src, cols, grad_attn, attn_f32, lse, seg_q, seg_row, head_dim
    )
    if by_heads:
        dqkv = to_rows_back(jnp.concatenate([dq, dk, dv], axis=2))
        dq, dk, dv = jnp.split(dqkv, 3, axis=2)
    else:
        dk, dv = (lax.psum_scatter(g, "blk", scatter_dimension=1, tiled=True) for g in (dk, dv))
    dq, dk, dv = (g.transpose(1, 0, 2) for g in (dq, dk, dv))
    grad_query_norm = rotate(dq.astype(F32), cos_table, -sin_table)
    grad_key_norm = rotate(dk.astype(F32), cos_table, -sin_table)
    grad_gain_query = jnp.sum(grad_query_norm * (query_raw * query_scale), axis=(0, 1))
    grad_gain_key = jnp.sum(grad_key_norm * (key_raw * key_scale), axis=(0, 1))
    grad_projected = jnp.concatenate(
        [
            norm_back(grad_query_norm * gain_query, query_raw, query_scale)
            .reshape(rows, local_width)
            .astype(BF16),
            norm_back(grad_key_norm * gain_key, key_raw, key_scale)
            .reshape(rows, local_width)
            .astype(BF16),
            dv.reshape(rows, local_width),
        ],
        axis=1,
    )
    grad_hidden_part = dot_nt(grad_projected, own_qkv)
    grad_hidden_one = sum_scatter(grad_hidden_part, ULY)
    grad_gain_attn = jnp.sum(grad_hidden_part * normed_one, axis=0)
    grad_inputs = grad_mid + norm_back(grad_hidden_one * gain_attn, inputs, rms_scale(inputs))

    grad_qkv_part = dot_tn(hidden_one, grad_projected).astype(BF16)
    grad_qkv_rows = lax.psum_scatter(grad_qkv_part, ROWS, scatter_dimension=0, tiled=True)
    grad_qkv_rows = swap(grad_qkv_rows.reshape(uly, shard_rows, 3 * local_width), ULY)
    grad_qkv = (
        grad_qkv_rows.reshape(uly, shard_rows, 3, local_width)
        .transpose(1, 2, 0, 3)
        .reshape(shard_rows, 3 * width)
        .astype(F32)
    )
    grad_out_rows = lax.psum_scatter(
        grad_out_part.reshape(local_width, width).astype(BF16), ROWS, scatter_dimension=0, tiled=True
    )
    grad_out = lax.ppermute(grad_out_rows, ALL, [(b, a) for a, b in to_rows]).astype(F32)
    small = jnp.concatenate([grad_gain_attn[:, None], grad_gain_ffn[:, None], grad_router_part], axis=1)
    small = lax.psum_scatter(small, ALL, scatter_dimension=0, tiled=True)
    grad_qk_gain = lax.psum(jnp.stack([grad_gain_query, grad_gain_key]), ALL)

    clip_gamma = TAU / jnp.maximum(head_max, TAU)
    factor = jnp.repeat(jnp.sqrt(clip_gamma), head_dim)
    column_scale = jnp.concatenate([factor, factor, jnp.ones((width,), F32)])
    clipped = w_qkv.astype(F32) * column_scale[None, :]
    return (
        output[None],
        grad_inputs[None],
        grad_qkv,
        grad_out,
        small[:, 0],
        small[:, 1],
        grad_qk_gain,
        small[:, 2:],
        grad_gate_up,
        grad_down,
        clipped,
    )


def per_device(
    tokens, segments, routes, w_qkv, w_out, attn_gain, ffn_gain, qk_gain, router, w_gate_up, w_down, cotangent
):
    own_tokens = tokens[0]
    own_grad = cotangent[0]
    count_tok, width = own_tokens.shape
    head_dim = qk_gain.shape[1]
    heads = width // head_dim
    batch, blk, uly = lax.axis_size("batch"), lax.axis_size("blk"), spread(ULY)
    total, group = batch * blk * uly, batch * blk
    local_experts = w_down.shape[0]
    if uly != 4 or heads != blk * uly or blk < 2 or batch != 2 or local_experts % 2:
        return per_device_general(
            tokens, segments, routes, w_qkv, w_out, attn_gain, ffn_gain, qk_gain, router, w_gate_up, w_down, cotangent
        )
    blk_at, uly_at = lax.axis_index("blk"), lax.axis_index(ULY)
    rows = count_tok * uly
    seg_row = segments[0]
    length = seg_row.shape[0]
    number = router.shape[1]
    shard_rows = w_qkv.shape[0]

    to_rows = [(u * group + g, g * uly + u) for g in range(group) for u in range(uly)]
    rows_here = lax.ppermute(w_out, ALL, to_rows)
    rows_there = lax.ppermute(w_out, ALL, [(a, (b + total // 2) % total) for a, b in to_rows])


    half = local_experts // 2

    def gather_experts(gate_up, down):
        return lax.all_gather(jnp.concatenate([gate_up, down], axis=2), PLANE, axis=0, tiled=False)

    weights_first = gather_experts(w_gate_up[:half], w_down[:half])
    extra = jnp.concatenate([attn_gain[None], ffn_gain[None], router.T], axis=0)
    kept = extra.shape[0]
    extra = jnp.pad(extra, ((0, -kept % 16), (0, -shard_rows % LANES)))
    by_head = w_qkv.reshape(shard_rows, 3, heads, head_dim).transpose(2, 0, 1, 3)
    own_qkv, extras, toks = startup(
        by_head.reshape(heads, shard_rows, 3 * head_dim), extra, own_tokens, 0
    )
    rows_here, rows_there, extras, later_gate_up, later_down = lax.optimization_barrier(
        (rows_here, rows_there, extras, w_gate_up[half:], w_down[half:])
    )
    weights_second = gather_experts(later_gate_up, later_down)
    is_first = lax.axis_index("batch") == 0
    pair = jnp.stack(
        [jnp.where(is_first, rows_here, rows_there), jnp.where(is_first, rows_there, rows_here)]
    )
    own_out = lax.all_to_all(
        jnp.broadcast_to(pair[None], (blk, *pair.shape)), "blk", split_axis=0, concat_axis=0, tiled=True
    )
    own_out = own_out.transpose(1, 0, 2, 3).reshape(blk, head_dim, width)
    own_qkv = own_qkv.reshape(width, 3 * head_dim)
    extras = extras.reshape(total, *extra.shape)[:, :kept, :shard_rows]
    extras = extras.transpose(1, 0, 2).reshape(kept, width)
    gain_attn = extras[0].astype(F32)
    gain_ffn = extras[1].astype(F32)
    router_t = extras[2:]

    gains = qk_gain.astype(F32)
    cos, sin = rope_rows(length, head_dim)
    hidden_one, qkv, raw = project(
        toks.reshape(length, width), gain_attn[None], own_qkv, cos, sin, gains
    )
    attn_low, attn_f32, lse, top = attention_forward(
        qkv[None], qkv[None], (0, 1, 2), seg_row, seg_row, head_dim
    )
    (attn_rows,) = exchange([(attn_low.reshape(blk, rows, head_dim), ("blk",), "swap")], 1)
    branch = jnp.einsum("htc,hcd->td", attn_rows, own_out, preferred_element_type=F32)
    branch, grad_blk, routes_blk = exchange(
        [
            (branch.astype(BF16).reshape(uly, count_tok, width), ULY, "pairsum"),
            (own_grad, ("blk",), "line"),
            (routes[0].T, ("blk",), "gather"),
        ],
        2,
    )
    inputs = own_tokens.astype(F32)
    mid = inputs + branch

    scale_two = rms_scale(mid)
    normed_two = mid * scale_two
    hidden_two = (normed_two * gain_ffn).astype(BF16)
    hidden_blk, hidden_t, grad_t = turn_gather(hidden_two, grad_blk, 3)
    tokens_blk = blk * count_tok
    hidden_blk = hidden_blk.reshape(tokens_blk, width)
    grad_blk = grad_blk.reshape(tokens_blk, width)
    probs_blk = jax.nn.softmax(dot_nt(hidden_blk, router_t), axis=1)
    names = jnp.arange(number, dtype=jnp.int32)
    chosen_blk = jnp.any(routes_blk[:, :, :, None] == names, axis=1).astype(F32)
    chosen_blk = chosen_blk.reshape(tokens_blk, number)
    gates = lax.dynamic_slice_in_dim(
        probs_blk * chosen_blk, blk_at * local_experts, local_experts, axis=1
    )
    shared = (hidden_blk, hidden_t, grad_blk, grad_t)
    out_part, dx_part, dg_first, grads_first = experts(
        *shared, gates[:, :half], [(weights_first, 0, half)]
    )
    sums_first = lax.psum_scatter(grads_first, PLANE, scatter_dimension=0, tiled=False)
    out_part, dx_part, dg_others, grads_others = experts(
        *shared, gates[:, half:], [(weights_second, 0, half)], before=(out_part, dx_part)
    )
    sums_others = lax.psum_scatter(grads_others, PLANE, scatter_dimension=0, tiled=False)
    finished = finish_experts(sums_first, 0, local_experts)
    grad_gate_up, grad_down = finish_experts(sums_others, half, local_experts, before=finished)
    dg_part = jnp.concatenate([dg_first, dg_others], axis=0)
    dg_part = dg_part.reshape(local_experts, blk, count_tok)
    dx_parts, dg_parts = exchange(
        [
            (dx_part.reshape(blk, count_tok, width), ("blk",), "swap"),
            (dg_part.transpose(1, 0, 2), ("blk",), "swap"),
        ],
        4,
    )
    out_part = out_part.reshape(blk, count_tok, width)
    out_part, dx_parts = lax.optimization_barrier((out_part, dx_parts))
    out_parts = lax.all_to_all(out_part, "blk", split_axis=0, concat_axis=0, tiled=True)
    output = (mid + jnp.sum(out_parts.astype(F32), axis=0)).astype(BF16)
    router_probs = lax.dynamic_slice_in_dim(probs_blk, blk_at * count_tok, count_tok)
    chosen = lax.dynamic_slice_in_dim(chosen_blk, blk_at * count_tok, count_tok)
    grad_probs = chosen * dg_parts.reshape(number, count_tok).T
    grad_logits = (
        router_probs * (grad_probs - jnp.sum(router_probs * grad_probs, axis=1, keepdims=True))
    ).astype(BF16)
    grad_hidden_two = jnp.sum(dx_parts.astype(F32), axis=0) + dot_nn(grad_logits, router_t)
    grad_router_t = dot_tn(grad_logits, hidden_two)
    grad_gain_ffn = jnp.sum(grad_hidden_two * normed_two, axis=0)
    grad_mid = own_grad.astype(F32) + norm_back(grad_hidden_two * gain_ffn, mid, scale_two)

    (branch_grad,) = exchange([(grad_mid.astype(BF16), ULY, "relay")], 5)
    branch_grad, sent_qkv = lax.optimization_barrier((branch_grad, own_qkv))
    far_qkv = lax.ppermute(sent_qkv, "y", [(0, 1), (1, 0)])
    branch_grad = branch_grad.reshape(rows, width)
    grad_attn = jnp.einsum("td,hcd->htc", branch_grad, own_out, preferred_element_type=F32).astype(BF16)
    grad_out_part = jnp.einsum("htc,td->hcd", attn_rows, branch_grad, preferred_element_type=F32)
    grad_out_part = grad_out_part.astype(BF16).reshape(batch, blk, shard_rows, width)
    batch_at = lax.axis_index("batch")
    grad_attn, got_out_part = exchange(
        [
            (grad_attn, ("blk",), "swap"),
            (
                lax.dynamic_index_in_dim(grad_out_part, 1 - batch_at, 0, keepdims=False),
                ("batch",),
                "trade",
            ),
        ],
        6,
        after=[out_parts],
    )
    grad_out_part = lax.dynamic_index_in_dim(grad_out_part, batch_at, 0, keepdims=False) + got_out_part
    grad_projected, grad_gains = project_back(
        qkv, grad_attn.reshape(length, head_dim), attn_f32, lse, seg_row, raw, cos, sin, gains
    )
    grad_qkv_part = dot_tn(hidden_one, grad_projected).astype(BF16)
    by_batch = grad_qkv_part.reshape(batch, width // batch, 3 * head_dim)
    projected_blk, got_qkv_part, near_qkv, cross_qkv, grad_out_parts = exchange(
        [
            (grad_projected.reshape(blk, uly, count_tok, 3 * head_dim), ULY, "swap1"),
            (
                lax.dynamic_index_in_dim(by_batch, 1 - batch_at, 0, keepdims=False),
                ("batch",),
                "trade",
            ),
            (own_qkv, ("core",), "trade"),
            (far_qkv, ("core",), "trade"),
            (grad_out_part, ("blk",), "swap"),
        ],
        7,
    )
    grad_out = lax.ppermute(
        jnp.sum(grad_out_parts.astype(F32), axis=0).astype(BF16), ALL, [(b, a) for a, b in to_rows]
    ).astype(F32)
    grad_qkv_part = lax.dynamic_index_in_dim(by_batch, batch_at, 0, keepdims=False) + got_qkv_part

    grad_hidden_part, grad_gain_attn = hidden_back(
        projected_blk.reshape(uly, tokens_blk, 3 * head_dim),
        own_qkv,
        near_qkv,
        far_qkv,
        cross_qkv,
        hidden_one.reshape(blk, uly, count_tok, width),
    )
    grad_gain_attn = grad_gain_attn[0] / gain_attn

    small = jnp.concatenate([grad_gain_attn[None], grad_gain_ffn[None], grad_router_t], axis=0)
    beside = LANES // shard_rows
    small = jnp.pad(small, ((0, -kept % beside), (0, 0))).reshape(-1, beside, total, shard_rows)
    small = small.transpose(2, 0, 1, 3).reshape(total, -1, LANES)
    packed_rows = small.shape[1]
    head_row = jnp.where(
        jnp.arange(LANES) == uly_at * blk + blk_at, jnp.max(top) * head_dim**-0.5, NEG
    )
    to_all = jnp.concatenate([grad_gains, head_row[None]], axis=0)
    small = jnp.concatenate([small, jnp.broadcast_to(to_all[None], (total, 3, LANES))], axis=1)
    small = jnp.pad(small, ((0, 0), (0, -small.shape[1] % 8), (0, 0)))
    grad_hidden_parts, small, grad_qkv_parts = exchange(
        [
            (grad_hidden_part, ("blk",), "swap"),
            (small, ALL, "swap"),
            (grad_qkv_part.reshape(total // batch, shard_rows, 3 * head_dim), ("blk", *ULY), "swap"),
        ],
        8,
    )
    grad_qkv = merge_heads(grad_qkv_parts.reshape(blk, uly, shard_rows, 3 * head_dim))
    grad_hidden_one = jnp.sum(grad_hidden_parts.astype(F32), axis=0)
    grad_inputs = grad_mid + norm_back(grad_hidden_one * gain_attn, inputs, rms_scale(inputs))
    sums = jnp.sum(small, axis=0)
    sums, grad_gains = sums[:packed_rows], sums[packed_rows : packed_rows + 2]
    sums = sums.reshape(packed_rows * beside, shard_rows)[:kept]
    head_max = jnp.max(small[:, packed_rows + 2, :heads], axis=0)
    factor = jnp.repeat(jnp.sqrt(TAU / jnp.maximum(head_max, TAU)), head_dim)
    column_scale = jnp.concatenate([factor, factor, jnp.ones((width,), F32)])
    clipped = w_qkv.astype(F32) * column_scale[None, :]
    return (
        output[None],
        grad_inputs[None],
        grad_qkv,
        grad_out,
        sums[0],
        sums[1],
        grad_gains,
        sums[2:].T,
        grad_gate_up,
        grad_down,
        clipped,
    )


def solution(mesh):
    in_specs = (
        P("batch", ("blk", *ULY), None),
        P("batch", None),
        P("batch", ("blk", *ULY), None),
        P(ALL, None),
        P(ALL, None),
        P(ALL),
        P(ALL),
        P(),
        P(ALL, None),
        P("blk", PLANE, None),
        P("blk", PLANE, None),
        P("batch", ("blk", *ULY), None),
    )
    out_specs = (
        P("batch", ("blk", *ULY), None),
        P("batch", ("blk", *ULY), None),
        P(ALL, None),
        P(ALL, None),
        P(ALL),
        P(ALL),
        P(),
        P(ALL, None),
        P("blk", PLANE, None),
        P("blk", PLANE, None),
        P(ALL, None),
    )
    cores = 2 - mesh.shape["uly"] % 2
    mesh = Mesh(
        mesh.devices.reshape(*(mesh.shape[axis] for axis in ROWS), mesh.shape["uly"] // cores, cores), ALL
    )
    return jax.shard_map(
        per_device, mesh=mesh, in_specs=in_specs, out_specs=out_specs, check_vma=False
    )
```
